32 devices in a mesh: section: 2 (over core), gx: 4 (over z), gy: 4 (over y, x).
Axes of the slice: x: 2, y: 2, z: 4, core: 2. Of those that a mesh axis runs over, the one named last changes fastest.
Arguments:
- rhs: float32 [4, 20, 20, 160], P('section', 'gx', 'gy'), may hold values from -6 to 6
- guess: float32 [4, 20, 20, 160], P('section', 'gx', 'gy'), may hold values from -6 to 6
- kappa: float32 [20, 20, 160], P('gx', 'gy'), may hold values from 0.1 to 10
- bc_flags: int32 [6, 4, 4, 32], P(None, 'gx', 'gy'), may hold values from 0 to 1
Outputs:
- solution: float32 [4, 20, 20, 160], P('section', 'gx', 'gy')
- residual: float32 [4, 20, 20, 160], P('section', 'gx', 'gy')
- arnoldi: float32 [3], replicated
The draws below stay inside these ranges and needn't reach their ends.
Inputs may be any that keep to these rules, and one draw needn't show every extreme that they name: `bc_flags`: 1 selects the upwind flux, 0 the central flux, on that face of that element.
All inputs are finite; a program needn't handle non-finite values.
Results may differ from the reference program's by a relative error of at most 0.0003.
Values sent between devices are 32-bit elements; how exact they have to be, the bound alone decides.
No kernel may reach another device: no remote copies, remote signals or barrier semaphores. Data moves between devices by JAX's collectives and lax.ppermute only.
A program may use at most 64 MiB of HBM per device.

```python
import math
from functools import partial
import jax
import jax.numpy as jnp
import numpy as np
from jax import lax

SECTIONS = 4
NP = 5
EZ = 32
NEX = 4
NEY = 4


def with_ends(values, rng, least, high):
    longest = values.shape.index(max(values.shape))
    spots = []
    for shift in (0, 1):
        where = [jax.random.randint(jax.random.fold_in(rng, axis), (), 0, length) for axis, length in enumerate(values.shape)]
        where[longest] = (where[longest] + shift) % values.shape[longest]
        spots.append(tuple(where))
    return values.at[spots[0]].set(least).at[spots[1]].set(high)


def shard_levels(stream_key, dims, cuts, low, high):
    level = 1.0
    for position, parts in cuts:
        steps = jax.random.uniform(jax.random.fold_in(jax.random.fold_in(stream_key, 6), position), (parts,), jnp.float32, low / len(cuts), high / len(cuts))
        level = level * jnp.repeat(jnp.exp(steps), dims[position] // parts).reshape((-1,) + (1,) * (len(dims) - 1 - position))
    return level


def bell_draw(stream_key, dims, deviation, bound, cuts=(), held_as=jnp.bfloat16):
    values = jax.random.normal(stream_key, dims, jnp.float32) * deviation
    if len(cuts) > 0:
        values = shard_levels(stream_key, dims, cuts, -0.22, 0.18) * values
    return jnp.clip(values, min=-bound, max=bound).astype(held_as)


def setup_inputs(seed: int = 0) -> dict:
    streams_of = jax.random.split(jax.random.key(seed), 5)
    return {
        "rhs": bell_draw(streams_of[0], (SECTIONS, NEX * NP, NEY * NP, EZ * NP), 1.0, 6.0, ((0, 2), (1, 4), (2, 4)), jnp.float32),
        "guess": bell_draw(streams_of[1], (SECTIONS, NEX * NP, NEY * NP, EZ * NP), 0.5, 6.0, ((0, 2), (1, 4), (2, 4)), jnp.float32),
        "kappa": jnp.clip(jnp.exp(math.log(10.0) - 4.6051702 * jax.random.uniform(streams_of[2], (NEX * NP, NEY * NP, EZ * NP), jnp.float32) ** shard_levels(streams_of[2], (NEX * NP, NEY * NP, EZ * NP), ((0, 4), (1, 4)), -0.2, 0.2)), 0.1, 10.0),
        "bc_flags": with_ends(jax.random.randint(streams_of[3], (6, NEX, NEY, EZ), 0, 2), jax.random.fold_in(streams_of[3], 1), 0, 1).astype(jnp.int32),
    }


ADVECT = (1.0, 0.7, 0.5)
DIFFUSE = 0.05
STEP_SIZE = 0.2
JACOBI_SCALE = 0.25
CHEB_LOW = 0.25
CHEB_HIGH = 2.0
LETTERS = 'abcdef'

def lobatto(count):
    if count == 5:
        inner = math.sqrt(3.0 / 7.0)
        return (np.array([-1.0, -inner, 0.0, inner, 1.0]), np.array([0.1, 49.0 / 90.0, 32.0 / 45.0, 49.0 / 90.0, 0.1]))
    if count == 3:
        return (np.array([-1.0, 0.0, 1.0]), np.array([1.0 / 3.0, 4.0 / 3.0, 1.0 / 3.0]))
    return (np.array([-1.0, 1.0]), np.array([1.0, 1.0]))

def lagrange_table(nodes, points):
    table = np.ones((len(points), len(nodes)))
    for column in range(len(nodes)):
        for other in range(len(nodes)):
            if other != column:
                table[:, column] *= (points - nodes[other]) / (nodes[column] - nodes[other])
    return table

def slope_table(nodes):
    total = len(nodes)
    factor = np.array([np.prod([nodes[i] - nodes[k] for k in range(total) if k != i]) for i in range(total)])
    table = np.zeros((total, total))
    for row in range(total):
        for column in range(total):
            if row != column:
                table[row, column] = factor[row] / factor[column] / (nodes[row] - nodes[column])
        table[row, row] = -np.sum(table[row])
    return table

def element_matrix(count, direction):
    nodes, weights = lobatto(count)
    slopes = slope_table(nodes)
    stiffness = (1.0 / weights)[:, None] * (slopes.T @ (weights[:, None] * slopes))
    return ADVECT[direction] * slopes + DIFFUSE * stiffness

def legendre_pair(point, order):
    values = [1.0, point]
    slopes = [0.0, 1.0]
    for index in range(1, order):
        values.append(((2 * index + 1) * point * values[index] - index * values[index - 1]) / (index + 1))
        slopes.append(slopes[index - 1] + (2 * index + 1) * values[index])
    return (values, slopes)

def radau_nodes():
    starts = [0.0885879595127039, 0.4094668644407347, 0.7876594617608471]
    found = []
    for start in starts:
        point = start
        for sweep in range(30):
            values, slopes = legendre_pair(2.0 * point - 1.0, 4)
            change = (values[4] - values[3]) / (2.0 * (slopes[4] - slopes[3]))
            point = point - change
        found.append(point)
    found.append(1.0)
    return found

def poly_times(coefs, root):
    result = [0.0] * (len(coefs) + 1)
    for index in range(len(coefs)):
        result[index + 1] += coefs[index]
        result[index] -= root * coefs[index]
    return result

def radau_matrix():
    order = 4
    nodes = radau_nodes()
    matrix = np.zeros((order, order))
    for column in range(order):
        coefs = [1.0]
        denominator = 1.0
        for other in range(order):
            if other != column:
                coefs = poly_times(coefs, nodes[other])
                denominator *= nodes[column] - nodes[other]
        for row in range(order):
            upper_end = nodes[row]
            integral = 0.0
            for index in range(len(coefs)):
                integral += coefs[index] * upper_end ** (index + 1) / (index + 1)
            matrix[row, column] = integral / denominator
    return matrix

def node_einsum(table, field, axis):
    labels = LETTERS[:field.ndim]
    source = labels[:axis + 1] + 'j' + labels[axis + 2:]
    target = labels[:axis + 1] + 'i' + labels[axis + 2:]
    return jnp.einsum('ij,' + source + '->' + target, jnp.asarray(table, jnp.float32), field, precision=lax.Precision.HIGHEST)

def apply_along(field, axis, count, table):
    shape = field.shape
    split = shape[:axis] + (shape[axis] // count, count) + shape[axis + 1:]
    mapped = node_einsum(table, field.reshape(split), axis)
    return mapped.reshape(shape[:axis] + (mapped.shape[axis] * mapped.shape[axis + 1],) + shape[axis + 1:])

def line_part(field, axis, count, table, left_gain, right_gain, left_edge, right_edge):
    shape = field.shape
    elements = shape[axis] // count
    split = field.reshape(shape[:axis] + (elements, count) + shape[axis + 1:])
    linear = node_einsum(table, split, axis)
    first = lax.index_in_dim(split, 0, axis + 1, keepdims=False)
    last = lax.index_in_dim(split, count - 1, axis + 1, keepdims=False)
    before = jnp.concatenate([jnp.expand_dims(left_edge, axis), lax.slice_in_dim(last, 0, elements - 1, axis=axis)], axis)
    after = jnp.concatenate([lax.slice_in_dim(first, 1, elements, axis=axis), jnp.expand_dims(right_edge, axis)], axis)
    front = jnp.expand_dims(left_gain * (first - before), axis + 1)
    back = jnp.expand_dims(right_gain * (last - after), axis + 1)
    if count > 2:
        middle_shape = list(front.shape)
        middle_shape[axis + 1] = count - 2
        pieces = [front, jnp.zeros(middle_shape, jnp.float32), back]
    else:
        pieces = [front, back]
    return (linear + jnp.concatenate(pieces, axis + 1)).reshape(shape)

def diag_along(shape, axis, count, table, left_gain, right_gain):
    elements = shape[axis] // count
    split = shape[:axis] + (elements, count) + shape[axis + 1:]
    profile = [1] * len(split)
    profile[axis + 1] = count
    diagonal_entries = np.array([table[index, index] for index in range(count)])
    base = jnp.broadcast_to(jnp.asarray(diagonal_entries, jnp.float32).reshape(profile), split)
    front = jnp.expand_dims(left_gain, axis + 1)
    back = jnp.expand_dims(right_gain, axis + 1)
    if count > 2:
        middle_shape = list(front.shape)
        middle_shape[axis + 1] = count - 2
        pieces = [front, jnp.zeros(middle_shape, jnp.float32), back]
    else:
        pieces = [front, back]
    return (base + jnp.concatenate(pieces, axis + 1)).reshape(shape)

def level_kappa(kappa, count):
    if count == 5:
        return kappa
    picks = np.array([0, 2, 4]) if count == 3 else np.array([0, 4])
    extents = [extent // 5 for extent in kappa.shape]
    grouped = kappa.reshape(extents[0], 5, extents[1], 5, extents[2], 5)
    for axis in (1, 3, 5):
        grouped = jnp.take(grouped, picks, axis=axis)
    return grouped.reshape(extents[0] * count, extents[1] * count, extents[2] * count)

def face_plane(face, direction, count):
    plane = face.astype(jnp.float32)
    for axis in range(3):
        if axis != direction:
            plane = jnp.repeat(plane, count, axis=axis)
    return plane

def build_level(kappa, flags, count):
    nodes, weights = lobatto(count)
    kappa_level = level_kappa(kappa, count)
    tables, lefts, rights = ([], [], [])
    diagonal = kappa_level
    for direction in range(3):
        table = element_matrix(count, direction)
        lower = face_plane(flags[2 * direction], direction, count)
        upper = face_plane(flags[2 * direction + 1], direction, count)
        left_gain = (ADVECT[direction] * (1.0 + lower) / 2.0 + DIFFUSE * count * count) / float(weights[0])
        right_gain = (DIFFUSE * count * count - ADVECT[direction] * (1.0 - upper) / 2.0) / float(weights[-1])
        tables.append(table)
        lefts.append(left_gain)
        rights.append(right_gain)
        diagonal = diagonal + diag_along(kappa_level.shape, direction, count, table, left_gain, right_gain)
    scale = 1.0 / (1.0 + STEP_SIZE * JACOBI_SCALE * diagonal)
    return (count, tables, lefts, rights, kappa_level, scale)

def restrict(field, fine_count, coarse_count):
    fine_nodes, fine_weights = lobatto(fine_count)
    coarse_nodes, coarse_weights = lobatto(coarse_count)
    table = (1.0 / coarse_weights)[:, None] * lagrange_table(coarse_nodes, fine_nodes).T * fine_weights[None, :]
    for axis in range(field.ndim - 3, field.ndim):
        field = apply_along(field, axis, fine_count, table)
    return field

def prolong(field, coarse_count, fine_count):
    fine_nodes, fine_weights = lobatto(fine_count)
    coarse_nodes, coarse_weights = lobatto(coarse_count)
    table = lagrange_table(coarse_nodes, fine_nodes)
    for axis in range(field.ndim - 3, field.ndim):
        field = apply_along(field, axis, coarse_count, table)
    return field

def chebyshev(rhs, start, level, operator):
    centre = (CHEB_HIGH + CHEB_LOW) / 2.0
    radius = (CHEB_HIGH - CHEB_LOW) / 2.0
    ratio = centre / radius
    first_rho = 1.0 / ratio
    second_rho = 1.0 / (2.0 * ratio - first_rho)
    scale = level[5]
    if start is None:
        remain = rhs
    else:
        remain = rhs - operator(start, level)
    step = scale * remain / centre
    guess = step if start is None else start + step
    remain = remain - operator(step, level)
    step = second_rho * first_rho * step + 2.0 * second_rho / radius * scale * remain
    return guess + step

def vcycle(rhs, levels, operator):
    fine, middle, coarse = levels
    fine_x = chebyshev(rhs, None, fine, operator)
    middle_rhs = restrict(rhs - operator(fine_x, fine), 5, 3)
    middle_x = chebyshev(middle_rhs, None, middle, operator)
    coarse_rhs = restrict(middle_rhs - operator(middle_x, middle), 3, 2)
    coarse_x = chebyshev(coarse_rhs, None, coarse, operator)
    middle_x = chebyshev(middle_rhs, middle_x + prolong(coarse_x, 2, 3), middle, operator)
    return chebyshev(rhs, fine_x + prolong(middle_x, 3, 5), fine, operator)

def spatial_one(field, level):
    count, tables, lefts, rights, kappa_level, scale = level
    total = kappa_level * field
    for direction in range(3):
        extent = field.shape[direction]
        total = total + line_part(field, direction, count, tables[direction], lefts[direction], rights[direction], lax.index_in_dim(field, extent - 1, direction, keepdims=False), lax.index_in_dim(field, 0, direction, keepdims=False))
    return total

def apply_system(field, level):
    image = lax.map(partial(spatial_one, level=level), field)
    butcher = jnp.asarray(radau_matrix(), jnp.float32)
    mixed = jnp.einsum('ij,jabc->iabc', butcher, image, precision=lax.Precision.HIGHEST)
    return field + STEP_SIZE * mixed

def reference(rhs, guess, kappa, bc_flags):
    levels = [build_level(kappa, bc_flags, count) for count in (5, 3, 2)]
    start_residual = rhs - apply_system(guess, levels[0])
    beta = jnp.sqrt(jnp.sum(start_residual * start_residual))
    basis = start_residual / beta
    precond = vcycle(basis, levels, apply_system)
    image = apply_system(precond, levels[0])
    upper = jnp.sum(image * basis)
    remainder = image - upper * basis
    lower = jnp.sqrt(jnp.sum(remainder * remainder))
    weight = beta * upper / (upper * upper + lower * lower)
    solution = guess + weight * precond
    residual = start_residual - weight * image
    arnoldi = jnp.stack([beta / math.sqrt(float(rhs.size)), upper, lower]).astype(jnp.float32)
    return (solution, residual, arnoldi)
```

```python
from functools import partial
import math

import jax
import jax.numpy as jnp
import numpy as np
from jax import lax
from jax.experimental import pallas as pl
from jax.experimental.pallas import tpu as pltpu
from jax.sharding import PartitionSpec as P

ADVECT = (1.0, 0.7, 0.5)
DIFFUSE = 0.05
STEP_SIZE = 0.2
JACOBI_SCALE = 0.25
CHEB_LOW = 0.25
CHEB_HIGH = 2.0
LETTERS = "abcdef"


def extended(x, sides, width):
    for axis, dim in sides:
        peers, length = (lax.axis_size(axis), x.shape[dim])
        up = [(i, (i + 1) % peers) for i in range(peers)]
        down = [(j, i) for i, j in up]
        last = lax.slice_in_dim(x, length - width, length, axis=dim)
        leading = lax.slice_in_dim(x, 0, width, axis=dim)
        before = lax.ppermute(last, axis, up)
        after = lax.ppermute(leading, axis, down)
        x = jnp.concatenate([before, x, after], axis=dim)
    return x


def lobatto(count):
    if count == 5:
        inner = math.sqrt(3.0 / 7.0)
        return (
            np.array([-1.0, -inner, 0.0, inner, 1.0]),
            np.array([0.1, 49.0 / 90.0, 32.0 / 45.0, 49.0 / 90.0, 0.1]),
        )
    if count == 3:
        return (np.array([-1.0, 0.0, 1.0]), np.array([1.0 / 3.0, 4.0 / 3.0, 1.0 / 3.0]))
    return (np.array([-1.0, 1.0]), np.array([1.0, 1.0]))


def lagrange_table(nodes, points):
    table = np.ones((len(points), len(nodes)))
    for column in range(len(nodes)):
        for other in range(len(nodes)):
            if other != column:
                table[:, column] *= (points - nodes[other]) / (nodes[column] - nodes[other])
    return table


def slope_table(nodes):
    total = len(nodes)
    factor = np.array(
        [np.prod([nodes[i] - nodes[k] for k in range(total) if k != i]) for i in range(total)]
    )
    table = np.zeros((total, total))
    for row in range(total):
        for column in range(total):
            if row != column:
                table[row, column] = factor[row] / factor[column] / (nodes[row] - nodes[column])
        table[row, row] = -np.sum(table[row])
    return table


def element_matrix(count, direction):
    nodes, weights = lobatto(count)
    slopes = slope_table(nodes)
    stiffness = (1.0 / weights)[:, None] * (slopes.T @ (weights[:, None] * slopes))
    return ADVECT[direction] * slopes + DIFFUSE * stiffness


def legendre_pair(point, order):
    values = [1.0, point]
    slopes = [0.0, 1.0]
    for index in range(1, order):
        values.append(
            ((2 * index + 1) * point * values[index] - index * values[index - 1]) / (index + 1)
        )
        slopes.append(slopes[index - 1] + (2 * index + 1) * values[index])
    return (values, slopes)


def radau_nodes():
    starts = [0.0885879595127039, 0.4094668644407347, 0.7876594617608471]
    found = []
    for start in starts:
        point = start
        for sweep in range(30):
            values, slopes = legendre_pair(2.0 * point - 1.0, 4)
            change = (values[4] - values[3]) / (2.0 * (slopes[4] - slopes[3]))
            point = point - change
        found.append(point)
    found.append(1.0)
    return found


def poly_times(coefs, root):
    result = [0.0] * (len(coefs) + 1)
    for index in range(len(coefs)):
        result[index + 1] += coefs[index]
        result[index] -= root * coefs[index]
    return result


def radau_matrix():
    order = 4
    nodes = radau_nodes()
    matrix = np.zeros((order, order))
    for column in range(order):
        coefs = [1.0]
        denominator = 1.0
        for other in range(order):
            if other != column:
                coefs = poly_times(coefs, nodes[other])
                denominator *= nodes[column] - nodes[other]
        for row in range(order):
            upper_end = nodes[row]
            integral = 0.0
            for index in range(len(coefs)):
                integral += coefs[index] * upper_end ** (index + 1) / (index + 1)
            matrix[row, column] = integral / denominator
    return matrix


def node_einsum(table, field, axis):
    labels = LETTERS[: field.ndim]
    source = labels[: axis + 1] + "j" + labels[axis + 2 :]
    target = labels[: axis + 1] + "i" + labels[axis + 2 :]
    return jnp.einsum(
        "ij," + source + "->" + target,
        jnp.asarray(table, jnp.float32),
        field,
        precision=lax.Precision.HIGHEST,
    )


def apply_along(field, axis, count, table):
    shape = field.shape
    split = shape[:axis] + (shape[axis] // count, count) + shape[axis + 1 :]
    mapped = node_einsum(table, field.reshape(split), axis)
    return mapped.reshape(
        shape[:axis] + (mapped.shape[axis] * mapped.shape[axis + 1],) + shape[axis + 1 :]
    )


def line_part(field, axis, count, table, left_gain, right_gain, left_edge, right_edge):
    shape = field.shape
    elements = shape[axis] // count
    split = field.reshape(shape[:axis] + (elements, count) + shape[axis + 1 :])
    linear = node_einsum(table, split, axis)
    first = lax.index_in_dim(split, 0, axis + 1, keepdims=False)
    last = lax.index_in_dim(split, count - 1, axis + 1, keepdims=False)
    before = jnp.concatenate(
        [jnp.expand_dims(left_edge, axis), lax.slice_in_dim(last, 0, elements - 1, axis=axis)], axis
    )
    after = jnp.concatenate(
        [lax.slice_in_dim(first, 1, elements, axis=axis), jnp.expand_dims(right_edge, axis)], axis
    )
    front = jnp.expand_dims(left_gain * (first - before), axis + 1)
    back = jnp.expand_dims(right_gain * (last - after), axis + 1)
    if count > 2:
        middle_shape = list(front.shape)
        middle_shape[axis + 1] = count - 2
        pieces = [front, jnp.zeros(middle_shape, jnp.float32), back]
    else:
        pieces = [front, back]
    return (linear + jnp.concatenate(pieces, axis + 1)).reshape(shape)


def diag_along(shape, axis, count, table, left_gain, right_gain):
    elements = shape[axis] // count
    split = shape[:axis] + (elements, count) + shape[axis + 1 :]
    profile = [1] * len(split)
    profile[axis + 1] = count
    diagonal_entries = np.array([table[index, index] for index in range(count)])
    base = jnp.broadcast_to(jnp.asarray(diagonal_entries, jnp.float32).reshape(profile), split)
    front = jnp.expand_dims(left_gain, axis + 1)
    back = jnp.expand_dims(right_gain, axis + 1)
    if count > 2:
        middle_shape = list(front.shape)
        middle_shape[axis + 1] = count - 2
        pieces = [front, jnp.zeros(middle_shape, jnp.float32), back]
    else:
        pieces = [front, back]
    return (base + jnp.concatenate(pieces, axis + 1)).reshape(shape)


def level_kappa(kappa, count):
    if count == 5:
        return kappa
    picks = np.array([0, 2, 4]) if count == 3 else np.array([0, 4])
    extents = [extent // 5 for extent in kappa.shape]
    grouped = kappa.reshape(extents[0], 5, extents[1], 5, extents[2], 5)
    for axis in (1, 3, 5):
        grouped = jnp.take(grouped, picks, axis=axis)
    return grouped.reshape(extents[0] * count, extents[1] * count, extents[2] * count)


def face_plane(face, direction, count):
    plane = face.astype(jnp.float32)
    for axis in range(3):
        if axis != direction:
            plane = jnp.repeat(plane, count, axis=axis)
    return plane


def build_level(kappa, flags, count):
    nodes, weights = lobatto(count)
    kappa_level = level_kappa(kappa, count)
    tables, lefts, rights = ([], [], [])
    diagonal = kappa_level
    for direction in range(3):
        table = element_matrix(count, direction)
        lower = face_plane(flags[2 * direction], direction, count)
        upper = face_plane(flags[2 * direction + 1], direction, count)
        left_gain = (ADVECT[direction] * (1.0 + lower) / 2.0 + DIFFUSE * count * count) / float(
            weights[0]
        )
        right_gain = (DIFFUSE * count * count - ADVECT[direction] * (1.0 - upper) / 2.0) / float(
            weights[-1]
        )
        tables.append(table)
        lefts.append(left_gain)
        rights.append(right_gain)
        diagonal = diagonal + diag_along(
            kappa_level.shape, direction, count, table, left_gain, right_gain
        )
    scale = 1.0 / (1.0 + STEP_SIZE * JACOBI_SCALE * diagonal)
    return (count, tables, lefts, rights, kappa_level, scale)


def restrict(field, fine_count, coarse_count):
    fine_nodes, fine_weights = lobatto(fine_count)
    coarse_nodes, coarse_weights = lobatto(coarse_count)
    table = (
        (1.0 / coarse_weights)[:, None]
        * lagrange_table(coarse_nodes, fine_nodes).T
        * fine_weights[None, :]
    )
    for axis in range(field.ndim - 3, field.ndim):
        field = apply_along(field, axis, fine_count, table)
    return field


def prolong(field, coarse_count, fine_count):
    fine_nodes, fine_weights = lobatto(fine_count)
    coarse_nodes, coarse_weights = lobatto(coarse_count)
    table = lagrange_table(coarse_nodes, fine_nodes)
    for axis in range(field.ndim - 3, field.ndim):
        field = apply_along(field, axis, coarse_count, table)
    return field


def chebyshev(rhs, start, level, operator):
    centre = (CHEB_HIGH + CHEB_LOW) / 2.0
    radius = (CHEB_HIGH - CHEB_LOW) / 2.0
    ratio = centre / radius
    first_rho = 1.0 / ratio
    second_rho = 1.0 / (2.0 * ratio - first_rho)
    scale = level[5]
    if start is None:
        remain = rhs
    else:
        remain = rhs - operator(start, level)
    step = scale * remain / centre
    guess = step if start is None else start + step
    remain = remain - operator(step, level)
    step = second_rho * first_rho * step + 2.0 * second_rho / radius * scale * remain
    return guess + step


def vcycle(rhs, levels, operator):
    fine, middle, coarse = levels
    fine_x = chebyshev(rhs, None, fine, operator)
    middle_rhs = restrict(rhs - operator(fine_x, fine), 5, 3)
    middle_x = chebyshev(middle_rhs, None, middle, operator)
    coarse_rhs = restrict(middle_rhs - operator(middle_x, middle), 3, 2)
    coarse_x = chebyshev(coarse_rhs, None, coarse, operator)
    middle_x = chebyshev(middle_rhs, middle_x + prolong(coarse_x, 2, 3), middle, operator)
    return chebyshev(rhs, fine_x + prolong(middle_x, 3, 5), fine, operator)


def spatial(field, level):
    count, tables, lefts, rights, kappa_level, scale = level
    padded = extended(field, (("gx", 1), ("gy", 2)), 1)
    total = kappa_level * field
    total = total + line_part(
        field,
        1,
        count,
        tables[0],
        lefts[0],
        rights[0],
        padded[:, 0, 1:-1, :],
        padded[:, -1, 1:-1, :],
    )
    total = total + line_part(
        field,
        2,
        count,
        tables[1],
        lefts[1],
        rights[1],
        padded[:, 1:-1, 0, :],
        padded[:, 1:-1, -1, :],
    )
    total = total + line_part(
        field, 3, count, tables[2], lefts[2], rights[2], field[:, :, :, -1], field[:, :, :, 0]
    )
    return total


def apply_system(field, level, coupling):
    image = spatial(field, level)
    everyone = lax.all_gather(image, "section", axis=0, tiled=True)
    butcher = jnp.asarray(radau_matrix(), jnp.float32)
    rows = lax.dynamic_slice_in_dim(
        butcher, lax.axis_index("section") * field.shape[0], field.shape[0], 0
    )
    mixed = jnp.einsum("ij,jabc->iabc", rows, everyone, precision=lax.Precision.HIGHEST)
    return field + STEP_SIZE * mixed


def global_total(values):
    return lax.psum(values, ("section", "gx", "gy"))


def stepwise(rhs, guess, kappa, bc_flags):
    levels = [build_level(kappa, bc_flags, count) for count in (5, 3, 2)]
    section_operator = partial(apply_system, coupling=None)
    start_residual = rhs - section_operator(guess, levels[0])
    dofs = float(rhs.size * lax.axis_size("section") * lax.axis_size("gx") * lax.axis_size("gy"))
    beta = jnp.sqrt(global_total(jnp.sum(start_residual * start_residual).reshape(1))[0])
    basis = start_residual / beta
    precond = vcycle(basis, levels, section_operator)
    image = section_operator(precond, levels[0])
    upper = global_total(jnp.sum(image * basis).reshape(1))[0]
    remainder = image - upper * basis
    lower = jnp.sqrt(global_total(jnp.sum(remainder * remainder).reshape(1))[0])
    weight = beta * upper / (upper * upper + lower * lower)
    solution = guess + weight * precond
    residual = start_residual - weight * image
    arnoldi = jnp.stack([beta / math.sqrt(dofs), upper, lower]).astype(jnp.float32)
    return (solution, residual, arnoldi)


SECS = 4
EZ = 32
COLS = 16
HALF = 64
PIECE = 80
F32 = jnp.float32


def iota(shape, dim):
    return lax.broadcasted_iota(jnp.int32, shape, dim)


def exact_dot(a, b):
    return lax.dot_general(
        a, b, (((1,), (0,)), ((), ())), precision=lax.Precision.HIGHEST, preferred_element_type=F32
    )


def choose(index, values):
    out = values[-1]
    for place in range(len(values) - 2, -1, -1):
        out = jnp.where(index == place, values[place], out)
    return out


def face_gains(flag, direction, side, count):
    nodes, weights = lobatto(count)
    c, nu = ADVECT[direction], DIFFUSE * count * count
    if side == 0:
        return (c * (1.0 + flag) / 2.0 + nu) * (1.0 / float(weights[0]))
    return (nu - c * (1.0 - flag) / 2.0) * (1.0 / float(weights[-1]))


def column_tables():
    kx, ky, kz = (element_matrix(5, d) for d in range(3))
    rows = np.zeros((64, 64))
    for s in range(2):
        for i in range(5):
            for j in range(5):
                r = s * 32 + i * 5 + j
                for m in range(5):
                    rows[r, s * 32 + m * 5 + j] += kx[i, m]
                    rows[r, s * 32 + i * 5 + m] += ky[j, m]
    lines = np.zeros((160, 320))
    for e in range(EZ):
        lines[e * 5 : e * 5 + 5, e * 5 : e * 5 + 5] = kz.T
        lines[(e - 1) % EZ * 5 + 4, 160 + e * 5] = 1.0
        lines[(e + 1) % EZ * 5, 160 + e * 5 + 4] = 1.0
    return rows.astype(np.float32), lines.astype(np.float32)


def residual_kernel(
    rhs, guess, kappa, flags, xb, xa, yb, ya, rows_t, lines_t, mine, theirs, x, nbx, nby, kap, stack, packed, krep
):
    sec = lax.axis_index("section")
    x[...] = jnp.zeros_like(x)
    nbx[...] = jnp.zeros_like(nbx)
    nby[...] = jnp.zeros_like(nby)
    kap[...] = jnp.zeros_like(kap)
    stack[...] = jnp.zeros_like(stack)
    for i in range(5):
        kap[5 * i : 5 * i + 5, :] = kappa[i]
    for s in range(2):
        for i in range(5):
            r = s * 32 + 5 * i
            x[r : r + 5, :] = guess[s, i]
            stack[r : r + 5, :] = rhs[s, i] - guess[s, i]
            nby[r : r + 1, :] = yb[s, i, 4:5, :]
            nby[r + 4 : r + 5, :] = ya[s, i, 0:1, :]
        nbx[s * 32 : s * 32 + 5, :] = xb[s, 4]
        nbx[s * 32 + 20 : s * 32 + 25, :] = xa[s, 0]
    flag = flags[:, 0, 0, :].astype(F32)
    spread = (iota((EZ, 160), 1) // 5 == iota((EZ, 160), 0)).astype(F32)
    wide = exact_dot(flag, spread)
    gains = [face_gains(wide[d : d + 1, :], d // 2, d % 2, 5) for d in range(6)]
    row = iota((32, 160), 0)
    lane = iota((32, 160), 1) % 5
    none = jnp.zeros((32, 160), F32)
    gx = jnp.where(row < 5, gains[0], jnp.where((row >= 20) & (row < 25), gains[1], none))
    gy = jnp.where(row % 5 == 0, gains[2], jnp.where(row % 5 == 4, gains[3], none))
    gz = jnp.where(lane == 0, gains[4], jnp.where(lane == 4, gains[5], none))
    field = x[...]
    along = exact_dot(rows_t[...], field)
    across = exact_dot(field, lines_t[...])
    own = kap[...] + gx + gy + gz
    for s in range(2):
        r = slice(s * 32, s * 32 + 32)
        image = own * field[r] + along[r] + across[r, :160]
        image = image - gz * across[r, 160:] - gx * nbx[r, :] - gy * nby[r, :]
        stack[64 + s * 32 : 96 + s * 32, :] = image
    butcher = radau_matrix()
    group = iota((32, 128), 1) // EZ
    factors = [
        jnp.where(
            sec == 0,
            choose(group, [float(-STEP_SIZE * butcher[g, s]) for g in range(SECS)]),
            choose(group, [float(-STEP_SIZE * butcher[g, 2 + s]) for g in range(SECS)]),
        )
        for s in range(2)
    ]
    packed[...] = jnp.zeros_like(packed)
    krep[...] = jnp.zeros_like(krep)
    source = stack[...]
    coefs = kap[...]
    for k in range(5):
        pick = (iota((160, 128), 0) == 5 * (iota((160, 128), 1) % EZ) + k).astype(F32)
        parts = exact_dot(source, pick)
        total = jnp.zeros((32, 128), F32)
        for s in range(2):
            total = total + jnp.where(group == 2 * sec + s, parts[s * 32 : s * 32 + 32], 0.0)
            total = total + factors[s] * parts[64 + s * 32 : 96 + s * 32]
        packed[25 * k : 25 * k + 25, :] = total[:25]
        krep[25 * k : 25 * k + 25, :] = exact_dot(coefs, pick)[:25]
    repeat = (iota((EZ, 128), 1) % EZ == iota((EZ, 128), 0)).astype(F32)
    shown = exact_dot(flag, repeat)
    lanes = group[:1]
    keep = (sec == 1).astype(F32)
    packed[125:126, :] = keep * choose(lanes, [shown[d : d + 1] for d in range(4)])
    packed[126:127, :] = keep * choose(lanes, [shown[4:5], shown[5:6]])
    low, high = packed[:HALF, :], packed[HALF:, :]
    mine[:HALF, :] = jnp.where(sec == 0, low, high)
    theirs[:HALF, :] = jnp.where(sec == 0, high, low)
    group16 = group[:16]
    first = choose(group16, [krep[32 * q : 32 * q + 16, :] for q in range(4)])
    second = choose(group16, [krep[32 * q + 16 : 32 * q + 32, :] for q in range(4)])
    mine[HALF:, :] = jnp.where(sec == 0, first, second)
    theirs[HALF:, :] = jnp.zeros((16, 128), F32)


def column_residual(rhs, guess, kappa, flags, halos):
    rows_t, lines_t = column_tables()
    whole = pl.BlockSpec(memory_space=pltpu.VMEM)
    return pl.pallas_call(
        residual_kernel,
        out_shape=[jax.ShapeDtypeStruct((PIECE, 128), F32)] * 2,
        in_specs=[whole] * 10,
        out_specs=[whole] * 2,
        scratch_shapes=[
            pltpu.VMEM((64, 160), F32),
            pltpu.VMEM((64, 160), F32),
            pltpu.VMEM((64, 160), F32),
            pltpu.VMEM((32, 160), F32),
            pltpu.VMEM((128, 160), F32),
            pltpu.VMEM((128, 128), F32),
            pltpu.VMEM((128, 128), F32),
        ],
        compiler_params=pltpu.CompilerParams(vmem_limit_bytes=16 * 2**20),
        name="column_residual",
    )(rhs, guess, kappa, flags, *halos, jnp.asarray(rows_t), jnp.asarray(lines_t))


class Level:
    def __init__(self, count, refs):
        self.count = count
        self.f, self.diag, self.jac, self.x, self.dir, self.res, self.edge = refs
        self.tables = [element_matrix(count, d) for d in range(3)]
        self.gains = None


def tile(index):
    return pl.ds(pl.multiple_of(index * 8, 8), 8)


def whole_kernel(gathered, guess, sol, res_out, arnoldi, *scratch):
    sec = lax.axis_index("section")
    column = lax.axis_index("gx") * 4 + lax.axis_index("gy")
    levels = [Level(n, scratch[7 * p : 7 * p + 7]) for p, n in enumerate((5, 3, 2))]
    kap, half, image, gain_ref, cols, outs = scratch[21:27]
    fine, middle, coarse = levels
    lane = iota((8, 128), 1)
    sub = iota((8, 128), 0)
    group = lane // EZ
    element = lane % EZ
    place = sub % 4
    low_half = sub < 4
    butcher = radau_matrix()
    mixers = [
        choose(group, [float(STEP_SIZE * butcher[g, (g - m) % SECS]) for g in range(SECS)])
        for m in range(SECS)
    ]
    centre = (CHEB_HIGH + CHEB_LOW) / 2.0
    radius = (CHEB_HIGH - CHEB_LOW) / 2.0
    first_rho = radius / centre
    second_rho = 1.0 / (2.0 * centre / radius - first_rho)
    keep = 1.0 + second_rho * first_rho
    push = 2.0 * second_rho / radius * centre

    for s, many in ((0, 64), (1, 61)):
        def place_rows(step, carry, s=s):
            for h in range(2):
                got = gathered[pl.ds((s * COLS + 8 * h) * PIECE + step, 8, stride=PIECE), :]
                fine.f[tile((s * 64 + step) * 2 + h), :] = got
            return carry
        lax.fori_loop(0, many, place_rows, 0, unroll=4 if s == 0 else 1)

    def expand(source):
        turned = [source] + [pltpu.roll(source, 32 * m, 1) for m in range(1, 4)]
        return [choose(group, [turned[(g - q) % 4] for g in range(4)]) for q in range(4)]

    for s in range(2):
        def place_kappa(step, carry, s=s):
            for h in range(2):
                got = gathered[pl.ds((s * COLS + 8 * h) * PIECE + HALF + step, 8, stride=PIECE), :]
                for q, part in enumerate(expand(got)):
                    kap[tile((q * 32 + s * 16 + step) * 2 + h), :] = part
            return carry
        lax.fori_loop(0, 16, place_kappa, 0)

    for h in range(2):
        got = [gathered[pl.ds((COLS + 8 * h) * PIECE + 61 + r, 8, stride=PIECE), :] for r in range(2)]
        shown = expand(got[0]) + expand(got[1])[:2]
        for p, level in enumerate(levels):
            for d in range(6):
                gain_ref[tile((p * 6 + d) * 2 + h), :] = face_gains(shown[d], d // 2, d % 2, level.count)

    def gain(p, d, h):
        return gain_ref[tile((p * 6 + d) * 2 + h), :]

    for p, level in enumerate(levels):
        n = level.count
        picks = {5: (0, 1, 2, 3, 4), 3: (0, 2, 4), 2: (0, 4)}[n]

        def diagonals(h, carry, p=p, level=level, n=n, picks=picks):
            terms = []
            for d in range(3):
                row = []
                for m in range(n):
                    value = float(level.tables[d][m, m])
                    if m == 0:
                        row.append(gain(p, 2 * d, h) + value)
                    elif m == n - 1:
                        row.append(gain(p, 2 * d + 1, h) + value)
                    else:
                        row.append(jnp.full((8, 128), value, F32))
                terms.append(row)
            for k in range(n):
                for i in range(n):
                    both = terms[2][k] + terms[0][i]
                    for j in range(n):
                        source = (picks[k] * 5 + picks[i]) * 5 + picks[j]
                        value = kap[tile(source * 2 + h), :] + (both + terms[1][j])
                        where = tile(((k * n + i) * n + j) * 2 + h)
                        level.diag[where, :] = value
                        scale = 1.0 / (1.0 + STEP_SIZE * JACOBI_SCALE * value)
                        level.jac[where, :] = scale * (1.0 / centre)
            return carry
        lax.fori_loop(0, 2, diagonals, 0)
        level.edge[...] = jnp.zeros_like(level.edge)

    def apply(p, source, finish, carry):
        level = levels[p]
        n = level.count
        kx, ky, kz = level.tables

        def faces(h, unused):
            before, after = gain(p, 2, h), gain(p, 3, h)
            for r in range(n * n):
                v = source[tile((r * n + n - 1) * 2 + h), :]
                moved = jnp.where(place == 0, pltpu.roll(v, 5, 0), pltpu.roll(v, 1, 0))
                level.edge[tile(r * n * 2 + h), :] = before * moved
                v = source[tile(r * n * 2 + h), :]
                moved = jnp.where(place == 3, pltpu.roll(v, 3, 0), pltpu.roll(v, 7, 0))
                level.edge[tile((r * n + n - 1) * 2 + h), :] = after * moved
            return unused
        lax.fori_loop(0, 2, faces, 0)

        def plane(t, carry):
            j, h = t // 2, t % 2
            other = 2 * j + 1 - h
            gains = [gain(p, d, h) for d in (0, 1, 4, 5)]
            sides = []
            for m in range(1, n):
                coef = choose(j, [float(ky[a, (a + m) % n]) for a in range(n)])
                far = jnp.where(j + m >= n, j + m - n, j + m)
                sides.append((coef, 2 * far + h))
            v = [[source[tile((k * n + i) * n * 2 + t), :] for i in range(n)] for k in range(n)]
            for k in range(n):
                left = pltpu.roll(v[k][n - 1], 4, 0)
                left_far = pltpu.roll(source[tile((k * n + n - 1) * n * 2 + other), :], 4, 0)
                right = pltpu.roll(v[k][0], 4, 0)
                right_far = pltpu.roll(source[tile(k * n * n * 2 + other), :], 4, 0)
                for i in range(n):
                    base = (k * n + i) * n * 2
                    total = level.diag[tile(base + t), :] * v[k][i] - level.edge[tile(base + t), :]
                    for m in range(n):
                        if m != i:
                            total = total + float(kx[i, m]) * v[k][m]
                    for m in range(n):
                        if m != k:
                            total = total + float(kz[k, m]) * v[m][i]
                    for coef, where in sides:
                        total = total + coef * source[tile(base + where), :]
                    if i == 0:
                        total = total - gains[0] * jnp.where(low_half, left_far, left)
                    if i == n - 1:
                        total = total - gains[1] * jnp.where(low_half, right, right_far)
                    if k == 0:
                        u = v[n - 1][i]
                        moved = jnp.where(element == 0, pltpu.roll(u, 97, 1), pltpu.roll(u, 1, 1))
                        total = total - gains[2] * moved
                    if k == n - 1:
                        u = v[0][i]
                        moved = jnp.where(element == EZ - 1, pltpu.roll(u, 31, 1), pltpu.roll(u, 127, 1))
                        total = total - gains[3] * moved
                    out = v[k][i] + mixers[0] * total
                    for m in range(1, SECS):
                        out = out + mixers[m] * pltpu.roll(total, 32 * m, 1)
                    carry = finish(tile(base + t), v[k][i], out, carry)
            return carry
        return lax.fori_loop(0, 2 * n, plane, carry)

    def smooth_first(p):
        level = levels[p]
        n = level.count
        rows = n * n * 16
        def start(step, carry):
            where = pl.ds(pl.multiple_of(step * rows, 8), rows)
            level.dir[where, :] = level.jac[where, :] * level.f[where, :]
            return carry
        lax.fori_loop(0, n, start, 0)
        def finish(where, v, av, carry):
            level.x[where, :] = keep * v + push * level.jac[where, :] * (level.f[where, :] - av)
            return carry
        apply(p, level.dir, finish, 0)

    def defect(p):
        level = levels[p]
        def finish(where, v, av, carry):
            level.res[where, :] = level.f[where, :] - av
            return carry
        apply(p, level.x, finish, 0)

    def smooth_again(p):
        level = levels[p]
        def middle_step(where, v, av, carry):
            left = level.f[where, :] - av
            level.res[where, :] = left
            level.dir[where, :] = level.jac[where, :] * left
            return carry
        apply(p, level.x, middle_step, 0)
        def finish(where, v, av, carry):
            step = push * level.jac[where, :] * (level.res[where, :] - av)
            level.x[where, :] = level.x[where, :] + keep * v + step
            return carry
        apply(p, level.dir, finish, 0)

    def combine(weights, parts):
        total = None
        for weight, part in zip(weights, parts):
            if abs(weight) > 1e-14:
                term = part if abs(weight - 1.0) < 1e-14 else float(weight) * part
                total = term if total is None else total + term
        return total

    def change(table, source, target, add):
        m, n = table.shape
        def outer(step, carry):
            where = [pl.ds(pl.multiple_of((k * n * n * 2 + step * 2 * n) * 8, 8), 16 * n) for k in range(n)]
            parts = [source[w, :] for w in where]
            for k in range(m):
                out = combine(table[k], parts)
                half[pl.ds(pl.multiple_of((k * n * n * 2 + step * 2 * n) * 8, 8), 16 * n), :] = out
            return carry
        lax.fori_loop(0, n, outer, 0)
        def inner(k, carry):
            parts = [
                half[pl.ds(pl.multiple_of((k * n * n * 2 + i * 2 * n) * 8, 8), 16 * n), :] for i in range(n)
            ]
            for i in range(m):
                line = combine(table[i], parts)
                points = [line[16 * j : 16 * j + 16] for j in range(n)]
                for j in range(m):
                    value = combine(table[j], points)
                    where = pl.ds(pl.multiple_of(((k * m + i) * m + j) * 16, 8), 16)
                    target[where, :] = target[where, :] + value if add else value
            return carry
        lax.fori_loop(0, m, inner, 0)

    def down(n, m):
        fine_nodes, fine_weights = lobatto(n)
        coarse_nodes, coarse_weights = lobatto(m)
        table = lagrange_table(coarse_nodes, fine_nodes)
        return (1.0 / coarse_weights)[:, None] * table.T * fine_weights[None, :]

    def up(m, n):
        return lagrange_table(lobatto(m)[0], lobatto(n)[0])

    smooth_first(0)
    defect(0)
    change(down(5, 3), fine.res, middle.f, False)
    smooth_first(1)
    defect(1)
    change(down(3, 2), middle.res, coarse.f, False)
    smooth_first(2)
    change(up(2, 3), coarse.x, middle.x, True)
    smooth_again(1)
    change(up(3, 5), middle.x, fine.x, True)
    smooth_again(0)

    def last(where, v, av, carry):
        image[where, :] = av
        f = fine.f[where, :]
        return carry[0] + av * f, carry[1] + f * f
    nothing = jnp.zeros((8, 128), F32)
    cross, size = apply(0, fine.x, last, (nothing, nothing))
    cross = jnp.sum(cross, keepdims=True)
    size = jnp.sum(size, keepdims=True)
    upper = cross / size

    def remainder(step, carry):
        for m in range(10):
            where = tile(step * 10 + m)
            left = image[where, :] - upper * fine.f[where, :]
            carry = carry + left * left
        return carry
    rest = jnp.sum(lax.fori_loop(0, 25, remainder, nothing), keepdims=True)
    beta = jnp.sqrt(size)
    lower = jnp.sqrt(rest) / beta
    weight = upper / (upper * upper + lower * lower)
    for place_out, value in enumerate((beta * (1.0 / math.sqrt(125.0 * EZ * COLS * SECS)), upper, lower)):
        arnoldi[place_out] = value[0, 0]

    cols[...] = jnp.zeros_like(cols)
    total = [jnp.zeros((64, 160), F32) for s in range(2)]
    for k in range(5):
        where = pl.ds(k * 400 + column, 25, stride=16)
        cols[0:25, :] = weight * fine.x[where, :]
        cols[32:57, :] = fine.f[where, :] - weight * image[where, :]
        block = cols[...]
        for s in range(2):
            lanes = iota((128, 160), 0)
            hit = (iota((128, 160), 1) == 5 * (lanes % EZ) + k) & (lanes // EZ == 2 * sec + s)
            total[s] = total[s] + exact_dot(block, hit.astype(F32))
    for s in range(2):
        outs[...] = total[s]
        for i in range(5):
            sol[s, i] = guess[s, i] + outs[5 * i : 5 * i + 5, :]
            res_out[s, i] = outs[32 + 5 * i : 37 + 5 * i, :]


def whole_step(gathered, guess):
    whole = pl.BlockSpec(memory_space=pltpu.VMEM)
    scratch = []
    for n in (5, 3, 2):
        scratch += [pltpu.VMEM((n**3 * 16, 128), F32)] * 7
    scratch += [
        pltpu.VMEM((128 * 16, 128), F32),
        pltpu.VMEM((125 * 16, 128), F32),
        pltpu.VMEM((125 * 16, 128), F32),
        pltpu.VMEM((36 * 8, 128), F32),
        pltpu.VMEM((64, 128), F32),
        pltpu.VMEM((64, 160), F32),
    ]
    return pl.pallas_call(
        whole_kernel,
        out_shape=[
            jax.ShapeDtypeStruct(guess.shape, F32),
            jax.ShapeDtypeStruct(guess.shape, F32),
            jax.ShapeDtypeStruct((3,), F32),
        ],
        in_specs=[whole] * 2,
        out_specs=[whole, whole, pl.BlockSpec(memory_space=pltpu.SMEM)],
        scratch_shapes=scratch,
        compiler_params=pltpu.CompilerParams(vmem_limit_bytes=32 * 2**20),
        name="whole_step",
    )(gathered, guess)


def gathered_body(rhs, guess, kappa, bc_flags):
    up = [(i, (i + 1) % 4) for i in range(4)]
    down = [(j, i) for i, j in up]
    halos = [
        lax.ppermute(guess, "gx", up),
        lax.ppermute(guess, "gx", down),
        lax.ppermute(guess, "gy", up),
        lax.ppermute(guess, "gy", down),
    ]
    mine, theirs = column_residual(rhs, guess, kappa, bc_flags, halos)
    piece = mine + lax.ppermute(theirs, "section", [(0, 1), (1, 0)])
    across = lax.all_gather(piece, ("gx", "gy"))
    both = lax.all_gather(across, "section")
    return tuple(whole_step(both.reshape(2 * COLS * PIECE, 128), guess))


def solution(mesh):
    placed = (
        P("section", "gx", "gy", None),
        P("section", "gx", "gy", None),
        P("gx", "gy", None),
        P(None, "gx", "gy", None),
    )
    sizes = (mesh.shape["section"], mesh.shape["gx"], mesh.shape["gy"])

    def step(rhs, guess, kappa, bc_flags):
        fits = sizes == (2, 4, 4) and rhs.shape == (4, 20, 20, 160)
        return jax.shard_map(
            gathered_body if fits else stepwise,
            mesh=mesh,
            in_specs=placed,
            out_specs=(P("section", "gx", "gy", None), P("section", "gx", "gy", None), P()),
            check_vma=False,
        )(rhs, guess, kappa, bc_flags)

    return step
```

```python
from functools import partial
import math

import jax
import jax.numpy as jnp
import numpy as np
from jax import lax
from jax.experimental import pallas as pl
from jax.experimental.pallas import tpu as pltpu
from jax.sharding import PartitionSpec as P

ADVECT = (1.0, 0.7, 0.5)
DIFFUSE = 0.05
STEP_SIZE = 0.2
JACOBI_SCALE = 0.25
CHEB_LOW = 0.25
CHEB_HIGH = 2.0
LETTERS = "abcdef"


def extended(x, sides, width):
    for axis, dim in sides:
        peers, length = (lax.axis_size(axis), x.shape[dim])
        up = [(i, (i + 1) % peers) for i in range(peers)]
        down = [(j, i) for i, j in up]
        last = lax.slice_in_dim(x, length - width, length, axis=dim)
        leading = lax.slice_in_dim(x, 0, width, axis=dim)
        before = lax.ppermute(last, axis, up)
        after = lax.ppermute(leading, axis, down)
        x = jnp.concatenate([before, x, after], axis=dim)
    return x


def lobatto(count):
    if count == 5:
        inner = math.sqrt(3.0 / 7.0)
        return (
            np.array([-1.0, -inner, 0.0, inner, 1.0]),
            np.array([0.1, 49.0 / 90.0, 32.0 / 45.0, 49.0 / 90.0, 0.1]),
        )
    if count == 3:
        return (np.array([-1.0, 0.0, 1.0]), np.array([1.0 / 3.0, 4.0 / 3.0, 1.0 / 3.0]))
    return (np.array([-1.0, 1.0]), np.array([1.0, 1.0]))


def lagrange_table(nodes, points):
    table = np.ones((len(points), len(nodes)))
    for column in range(len(nodes)):
        for other in range(len(nodes)):
            if other != column:
                table[:, column] *= (points - nodes[other]) / (nodes[column] - nodes[other])
    return table


def slope_table(nodes):
    total = len(nodes)
    factor = np.array(
        [np.prod([nodes[i] - nodes[k] for k in range(total) if k != i]) for i in range(total)]
    )
    table = np.zeros((total, total))
    for row in range(total):
        for column in range(total):
            if row != column:
                table[row, column] = factor[row] / factor[column] / (nodes[row] - nodes[column])
        table[row, row] = -np.sum(table[row])
    return table


def element_matrix(count, direction):
    nodes, weights = lobatto(count)
    slopes = slope_table(nodes)
    stiffness = (1.0 / weights)[:, None] * (slopes.T @ (weights[:, None] * slopes))
    return ADVECT[direction] * slopes + DIFFUSE * stiffness


def legendre_pair(point, order):
    values = [1.0, point]
    slopes = [0.0, 1.0]
    for index in range(1, order):
        values.append(
            ((2 * index + 1) * point * values[index] - index * values[index - 1]) / (index + 1)
        )
        slopes.append(slopes[index - 1] + (2 * index + 1) * values[index])
    return (values, slopes)


def radau_nodes():
    starts = [0.0885879595127039, 0.4094668644407347, 0.7876594617608471]
    found = []
    for start in starts:
        point = start
        for sweep in range(30):
            values, slopes = legendre_pair(2.0 * point - 1.0, 4)
            change = (values[4] - values[3]) / (2.0 * (slopes[4] - slopes[3]))
            point = point - change
        found.append(point)
    found.append(1.0)
    return found


def poly_times(coefs, root):
    result = [0.0] * (len(coefs) + 1)
    for index in range(len(coefs)):
        result[index + 1] += coefs[index]
        result[index] -= root * coefs[index]
    return result


def radau_matrix():
    order = 4
    nodes = radau_nodes()
    matrix = np.zeros((order, order))
    for column in range(order):
        coefs = [1.0]
        denominator = 1.0
        for other in range(order):
            if other != column:
                coefs = poly_times(coefs, nodes[other])
                denominator *= nodes[column] - nodes[other]
        for row in range(order):
            upper_end = nodes[row]
            integral = 0.0
            for index in range(len(coefs)):
                integral += coefs[index] * upper_end ** (index + 1) / (index + 1)
            matrix[row, column] = integral / denominator
    return matrix


def node_einsum(table, field, axis):
    labels = LETTERS[: field.ndim]
    source = labels[: axis + 1] + "j" + labels[axis + 2 :]
    target = labels[: axis + 1] + "i" + labels[axis + 2 :]
    return jnp.einsum(
        "ij," + source + "->" + target,
        jnp.asarray(table, jnp.float32),
        field,
        precision=lax.Precision.HIGHEST,
    )


def apply_along(field, axis, count, table):
    shape = field.shape
    split = shape[:axis] + (shape[axis] // count, count) + shape[axis + 1 :]
    mapped = node_einsum(table, field.reshape(split), axis)
    return mapped.reshape(
        shape[:axis] + (mapped.shape[axis] * mapped.shape[axis + 1],) + shape[axis + 1 :]
    )


def line_part(field, axis, count, table, left_gain, right_gain, left_edge, right_edge):
    shape = field.shape
    elements = shape[axis] // count
    split = field.reshape(shape[:axis] + (elements, count) + shape[axis + 1 :])
    linear = node_einsum(table, split, axis)
    first = lax.index_in_dim(split, 0, axis + 1, keepdims=False)
    last = lax.index_in_dim(split, count - 1, axis + 1, keepdims=False)
    before = jnp.concatenate(
        [jnp.expand_dims(left_edge, axis), lax.slice_in_dim(last, 0, elements - 1, axis=axis)], axis
    )
    after = jnp.concatenate(
        [lax.slice_in_dim(first, 1, elements, axis=axis), jnp.expand_dims(right_edge, axis)], axis
    )
    front = jnp.expand_dims(left_gain * (first - before), axis + 1)
    back = jnp.expand_dims(right_gain * (last - after), axis + 1)
    if count > 2:
        middle_shape = list(front.shape)
        middle_shape[axis + 1] = count - 2
        pieces = [front, jnp.zeros(middle_shape, jnp.float32), back]
    else:
        pieces = [front, back]
    return (linear + jnp.concatenate(pieces, axis + 1)).reshape(shape)


def diag_along(shape, axis, count, table, left_gain, right_gain):
    elements = shape[axis] // count
    split = shape[:axis] + (elements, count) + shape[axis + 1 :]
    profile = [1] * len(split)
    profile[axis + 1] = count
    diagonal_entries = np.array([table[index, index] for index in range(count)])
    base = jnp.broadcast_to(jnp.asarray(diagonal_entries, jnp.float32).reshape(profile), split)
    front = jnp.expand_dims(left_gain, axis + 1)
    back = jnp.expand_dims(right_gain, axis + 1)
    if count > 2:
        middle_shape = list(front.shape)
        middle_shape[axis + 1] = count - 2
        pieces = [front, jnp.zeros(middle_shape, jnp.float32), back]
    else:
        pieces = [front, back]
    return (base + jnp.concatenate(pieces, axis + 1)).reshape(shape)


def level_kappa(kappa, count):
    if count == 5:
        return kappa
    picks = np.array([0, 2, 4]) if count == 3 else np.array([0, 4])
    extents = [extent // 5 for extent in kappa.shape]
    grouped = kappa.reshape(extents[0], 5, extents[1], 5, extents[2], 5)
    for axis in (1, 3, 5):
        grouped = jnp.take(grouped, picks, axis=axis)
    return grouped.reshape(extents[0] * count, extents[1] * count, extents[2] * count)


def face_plane(face, direction, count):
    plane = face.astype(jnp.float32)
    for axis in range(3):
        if axis != direction:
            plane = jnp.repeat(plane, count, axis=axis)
    return plane


def build_level(kappa, flags, count):
    nodes, weights = lobatto(count)
    kappa_level = level_kappa(kappa, count)
    tables, lefts, rights = ([], [], [])
    diagonal = kappa_level
    for direction in range(3):
        table = element_matrix(count, direction)
        lower = face_plane(flags[2 * direction], direction, count)
        upper = face_plane(flags[2 * direction + 1], direction, count)
        left_gain = (ADVECT[direction] * (1.0 + lower) / 2.0 + DIFFUSE * count * count) / float(
            weights[0]
        )
        right_gain = (DIFFUSE * count * count - ADVECT[direction] * (1.0 - upper) / 2.0) / float(
            weights[-1]
        )
        tables.append(table)
        lefts.append(left_gain)
        rights.append(right_gain)
        diagonal = diagonal + diag_along(
            kappa_level.shape, direction, count, table, left_gain, right_gain
        )
    scale = 1.0 / (1.0 + STEP_SIZE * JACOBI_SCALE * diagonal)
    return (count, tables, lefts, rights, kappa_level, scale)


def restrict(field, fine_count, coarse_count):
    fine_nodes, fine_weights = lobatto(fine_count)
    coarse_nodes, coarse_weights = lobatto(coarse_count)
    table = (
        (1.0 / coarse_weights)[:, None]
        * lagrange_table(coarse_nodes, fine_nodes).T
        * fine_weights[None, :]
    )
    for axis in range(field.ndim - 3, field.ndim):
        field = apply_along(field, axis, fine_count, table)
    return field


def prolong(field, coarse_count, fine_count):
    fine_nodes, fine_weights = lobatto(fine_count)
    coarse_nodes, coarse_weights = lobatto(coarse_count)
    table = lagrange_table(coarse_nodes, fine_nodes)
    for axis in range(field.ndim - 3, field.ndim):
        field = apply_along(field, axis, coarse_count, table)
    return field


def chebyshev(rhs, start, level, operator):
    centre = (CHEB_HIGH + CHEB_LOW) / 2.0
    radius = (CHEB_HIGH - CHEB_LOW) / 2.0
    ratio = centre / radius
    first_rho = 1.0 / ratio
    second_rho = 1.0 / (2.0 * ratio - first_rho)
    scale = level[5]
    if start is None:
        remain = rhs
    else:
        remain = rhs - operator(start, level)
    step = scale * remain / centre
    guess = step if start is None else start + step
    remain = remain - operator(step, level)
    step = second_rho * first_rho * step + 2.0 * second_rho / radius * scale * remain
    return guess + step


def vcycle(rhs, levels, operator):
    fine, middle, coarse = levels
    fine_x = chebyshev(rhs, None, fine, operator)
    middle_rhs = restrict(rhs - operator(fine_x, fine), 5, 3)
    middle_x = chebyshev(middle_rhs, None, middle, operator)
    coarse_rhs = restrict(middle_rhs - operator(middle_x, middle), 3, 2)
    coarse_x = chebyshev(coarse_rhs, None, coarse, operator)
    middle_x = chebyshev(middle_rhs, middle_x + prolong(coarse_x, 2, 3), middle, operator)
    return chebyshev(rhs, fine_x + prolong(middle_x, 3, 5), fine, operator)


def spatial(field, level):
    count, tables, lefts, rights, kappa_level, scale = level
    padded = extended(field, (("gx", 1), ("gy", 2)), 1)
    total = kappa_level * field
    total = total + line_part(
        field,
        1,
        count,
        tables[0],
        lefts[0],
        rights[0],
        padded[:, 0, 1:-1, :],
        padded[:, -1, 1:-1, :],
    )
    total = total + line_part(
        field,
        2,
        count,
        tables[1],
        lefts[1],
        rights[1],
        padded[:, 1:-1, 0, :],
        padded[:, 1:-1, -1, :],
    )
    total = total + line_part(
        field, 3, count, tables[2], lefts[2], rights[2], field[:, :, :, -1], field[:, :, :, 0]
    )
    return total


def apply_system(field, level, coupling):
    image = spatial(field, level)
    everyone = lax.all_gather(image, "section", axis=0, tiled=True)
    butcher = jnp.asarray(radau_matrix(), jnp.float32)
    rows = lax.dynamic_slice_in_dim(
        butcher, lax.axis_index("section") * field.shape[0], field.shape[0], 0
    )
    mixed = jnp.einsum("ij,jabc->iabc", rows, everyone, precision=lax.Precision.HIGHEST)
    return field + STEP_SIZE * mixed


def global_total(values):
    return lax.psum(values, ("section", "gx", "gy"))


def stepwise(rhs, guess, kappa, bc_flags):
    levels = [build_level(kappa, bc_flags, count) for count in (5, 3, 2)]
    section_operator = partial(apply_system, coupling=None)
    start_residual = rhs - section_operator(guess, levels[0])
    dofs = float(rhs.size * lax.axis_size("section") * lax.axis_size("gx") * lax.axis_size("gy"))
    beta = jnp.sqrt(global_total(jnp.sum(start_residual * start_residual).reshape(1))[0])
    basis = start_residual / beta
    precond = vcycle(basis, levels, section_operator)
    image = section_operator(precond, levels[0])
    upper = global_total(jnp.sum(image * basis).reshape(1))[0]
    remainder = image - upper * basis
    lower = jnp.sqrt(global_total(jnp.sum(remainder * remainder).reshape(1))[0])
    weight = beta * upper / (upper * upper + lower * lower)
    solution = guess + weight * precond
    residual = start_residual - weight * image
    arnoldi = jnp.stack([beta / math.sqrt(dofs), upper, lower]).astype(jnp.float32)
    return (solution, residual, arnoldi)


EZ = 32
COLS = 16
HALF = 64
PIECE = 96
FIELD = 1000
F32 = jnp.float32


def split_sections():
    matrix = radau_matrix()
    values, vectors = np.linalg.eig(matrix)
    order = [n for n in np.argsort(np.abs(values.imag), kind="stable") if values[n].imag > 0]
    bases = []
    for n in order:
        plane = np.stack([vectors[:, n].real, vectors[:, n].imag], axis=1)
        bases.append(np.linalg.qr(plane)[0])
    left, cross, right = np.linalg.svd(bases[0].T @ bases[1])
    bases = [bases[0] @ left, bases[1] @ right.T]
    for c in range(2):
        sign = np.sign(bases[0][np.argmax(np.abs(bases[0][:, c])), c])
        bases = [np.concatenate([b[:, :c], sign * b[:, c : c + 1], b[:, c + 1 :]], axis=1) for b in bases]
    whole = np.concatenate(bases, axis=1)
    back = np.linalg.inv(whole)
    return whole, back, back @ matrix, back @ matrix @ whole, cross


def iota(shape, dim):
    return lax.broadcasted_iota(jnp.int32, shape, dim)


def exact_dot(a, b):
    return lax.dot_general(
        a, b, (((1,), (0,)), ((), ())), precision=lax.Precision.HIGHEST, preferred_element_type=F32
    )


def choose(index, values):
    out = values[-1]
    for place in range(len(values) - 2, -1, -1):
        out = jnp.where(index == place, values[place], out)
    return out


def face_gains(flag, direction, side, count):
    nodes, weights = lobatto(count)
    c, nu = ADVECT[direction], DIFFUSE * count * count
    if side == 0:
        return (c * (1.0 + flag) / 2.0 + nu) * (1.0 / float(weights[0]))
    return (nu - c * (1.0 - flag) / 2.0) * (1.0 / float(weights[-1]))


def column_tables():
    kx, ky, kz = (element_matrix(5, d) for d in range(3))
    rows = np.zeros((64, 64))
    for s in range(2):
        for i in range(5):
            for j in range(5):
                r = s * 32 + i * 5 + j
                for m in range(5):
                    rows[r, s * 32 + m * 5 + j] += kx[i, m]
                    rows[r, s * 32 + i * 5 + m] += ky[j, m]
    lines = np.zeros((160, 320))
    for e in range(EZ):
        lines[e * 5 : e * 5 + 5, e * 5 : e * 5 + 5] = kz.T
        lines[(e - 1) % EZ * 5 + 4, 160 + e * 5] = 1.0
        lines[(e + 1) % EZ * 5, 160 + e * 5 + 4] = 1.0
    return rows.astype(np.float32), lines.astype(np.float32)


def pick_line(k):
    return (iota((160, 128), 0) == 5 * (iota((160, 128), 1) % EZ) + k).astype(F32)


def pair_factors(sec, table, own, s):
    upper = iota((32, 128), 1) < 64
    first = jnp.where(upper, float(table[0, s]), float(table[1, s]))
    second = jnp.where(upper, float(table[2, 2 + s]), float(table[3, 2 + s]))
    if not own:
        first = jnp.where(upper, float(table[2, s]), float(table[3, s]))
        second = jnp.where(upper, float(table[0, 2 + s]), float(table[1, 2 + s]))
    return jnp.where(sec == 0, first, second)


def pack_nodes(nodes):
    odd = iota((HALF, 128), 1) // EZ % 2 == 1
    return jnp.where(odd, nodes[HALF:, :], nodes[:HALF, :])


def fetch(pairs, sems):
    copies = [pltpu.make_async_copy(src, dst, sems.at[n]) for n, (src, dst) in enumerate(pairs)]
    for copy in copies:
        copy.start()
    for copy in copies:
        copy.wait()


def local_kernel(
    rhs_in, guess_in, kappa_in, flags_in, rows_in, lines_in, mine, theirs, faces,
    rhs, guess, kappa, flags, rows_t, lines_t, sems, x, kap, stack, own_nodes, other_nodes, krep,
):
    sec = lax.axis_index("section")
    fetch(
        [(rhs_in, rhs), (guess_in, guess), (kappa_in, kappa), (flags_in, flags), (rows_in, rows_t), (lines_in, lines_t)],
        sems,
    )
    x[...] = jnp.zeros_like(x)
    kap[...] = jnp.zeros_like(kap)
    stack[...] = jnp.zeros_like(stack)
    for i in range(5):
        kap[5 * i : 5 * i + 5, :] = kappa[i]
        for j in range(5):
            r = 5 * i + j
            value = guess[i, j]
            left = rhs[i, j] - value
            for s in range(2):
                x[s * 32 + r : s * 32 + r + 1, :] = value[s : s + 1]
                stack[s * 32 + r : s * 32 + r + 1, :] = left[s : s + 1]
    flag = flags[:, 0, 0, :].astype(F32)
    spread = (iota((EZ, 160), 1) // 5 == iota((EZ, 160), 0)).astype(F32)
    wide = exact_dot(flag, spread)
    gains = [face_gains(wide[d : d + 1, :], d // 2, d % 2, 5) for d in range(6)]
    row = iota((32, 160), 0)
    lane = iota((32, 160), 1) % 5
    none = jnp.zeros((32, 160), F32)
    gx = jnp.where(row < 5, gains[0], jnp.where((row >= 20) & (row < 25), gains[1], none))
    gy = jnp.where(row % 5 == 0, gains[2], jnp.where(row % 5 == 4, gains[3], none))
    gz = jnp.where(lane == 0, gains[4], jnp.where(lane == 4, gains[5], none))
    faces[0:32, :] = gx
    faces[32:64, :] = jnp.where(row < 25, gy, none)
    field = x[...]
    along = exact_dot(rows_t[...], field)
    across = exact_dot(field, lines_t[...])
    own = kap[...] + gx + gy + gz
    for s in range(2):
        r = slice(s * 32, s * 32 + 32)
        image = own * field[r] + along[r] + across[r, :160] - gz * across[r, 160:]
        stack[64 + s * 32 : 96 + s * 32, :] = image
    whole, back, back_matrix, blocks, cross = split_sections()
    own_nodes[...] = jnp.zeros_like(own_nodes)
    other_nodes[...] = jnp.zeros_like(other_nodes)
    krep[...] = jnp.zeros_like(krep)
    source = stack[...]
    coefs = kap[...]
    for k in range(5):
        pick = pick_line(k)
        parts = exact_dot(source, pick)
        for target, mark in ((own_nodes, True), (other_nodes, False)):
            total = jnp.zeros((32, 128), F32)
            for s in range(2):
                total = total + pair_factors(sec, back, mark, s) * parts[s * 32 : s * 32 + 32]
                factor = pair_factors(sec, -STEP_SIZE * back_matrix, mark, s)
                total = total + factor * parts[64 + s * 32 : 96 + s * 32]
            target[25 * k : 25 * k + 25, :] = total[:25]
        krep[25 * k : 25 * k + 25, :] = exact_dot(coefs, pick)[:25]
    repeat = (iota((EZ, 128), 1) % EZ == iota((EZ, 128), 0)).astype(F32)
    shown = exact_dot(flag, repeat)
    upper = iota((1, 128), 1) < 64
    for r in range(3):
        own_nodes[125 + r : 126 + r, :] = jnp.where(upper, shown[2 * r : 2 * r + 1], shown[2 * r + 1 : 2 * r + 2])
    mine[:HALF, :] = pack_nodes(own_nodes)
    theirs[...] = pack_nodes(other_nodes)
    mine[HALF:, :] = choose(iota((32, 128), 1) // EZ, [krep[32 * q : 32 * q + 32, :] for q in range(4)])


def halo_kernel(base_mine, base_theirs, faces, xb, xa, yb, ya, mine, theirs, nbx, nby, own_nodes, other_nodes):
    sec = lax.axis_index("section")
    for ref in (nbx, nby, own_nodes, other_nodes):
        ref[...] = jnp.zeros_like(ref)
    for m in range(5):
        for s in range(2):
            r = s * 32
            nbx[r + m : r + m + 1, :] = xb[4, m, s : s + 1, :]
            nbx[r + 20 + m : r + 21 + m, :] = xa[0, m, s : s + 1, :]
            nby[r + 5 * m : r + 5 * m + 1, :] = yb[m, 4, s : s + 1, :]
            nby[r + 5 * m + 4 : r + 5 * m + 5, :] = ya[m, 0, s : s + 1, :]
    gx, gy = faces[0:32, :], faces[32:64, :]
    for s in range(2):
        r = slice(s * 32, s * 32 + 32)
        nbx[r, :] = gx * nbx[r, :] + gy * nby[r, :]
    source = nbx[...]
    back_matrix = split_sections()[2]
    for k in range(5):
        parts = exact_dot(source, pick_line(k))
        for target, mark in ((own_nodes, True), (other_nodes, False)):
            total = jnp.zeros((32, 128), F32)
            for s in range(2):
                factor = pair_factors(sec, STEP_SIZE * back_matrix, mark, s)
                total = total + factor * parts[s * 32 : s * 32 + 32]
            target[25 * k : 25 * k + 25, :] = total[:25]
    mine[:HALF, :] = base_mine[:HALF, :] + pack_nodes(own_nodes)
    mine[HALF:, :] = base_mine[HALF:, :]
    theirs[...] = base_theirs[...] + pack_nodes(other_nodes)


VMEM = pl.BlockSpec(memory_space=pltpu.VMEM)
HBM = pl.BlockSpec(memory_space=pltpu.HBM)


def limit(mib):
    return pltpu.CompilerParams(vmem_limit_bytes=mib * 2**20)


def local_part(rhs, guess, kappa, flags):
    rows_t, lines_t = column_tables()
    operands = (rhs, guess, kappa, flags, jnp.asarray(rows_t), jnp.asarray(lines_t))
    return pl.pallas_call(
        local_kernel,
        out_shape=[
            jax.ShapeDtypeStruct((PIECE, 128), F32),
            jax.ShapeDtypeStruct((HALF, 128), F32),
            jax.ShapeDtypeStruct((64, 160), F32),
        ],
        in_specs=[HBM] * 6,
        out_specs=[VMEM] * 3,
        scratch_shapes=[pltpu.VMEM(o.shape, o.dtype) for o in operands]
        + [
            pltpu.SemaphoreType.DMA((6,)),
            pltpu.VMEM((64, 160), F32),
            pltpu.VMEM((32, 160), F32),
            pltpu.VMEM((128, 160), F32),
            pltpu.VMEM((128, 128), F32),
            pltpu.VMEM((128, 128), F32),
            pltpu.VMEM((128, 128), F32),
        ],
        compiler_params=limit(16),
        name="local_part",
    )(*operands)


def halo_part(base_mine, base_theirs, faces, halos):
    return pl.pallas_call(
        halo_kernel,
        out_shape=[
            jax.ShapeDtypeStruct((PIECE, 128), F32),
            jax.ShapeDtypeStruct((HALF, 128), F32),
        ],
        in_specs=[VMEM] * 7,
        out_specs=[VMEM] * 2,
        scratch_shapes=[pltpu.VMEM((64, 160), F32)] * 2 + [pltpu.VMEM((128, 128), F32)] * 2,
        compiler_params=limit(16),
        name="halo_part",
    )(base_mine, base_theirs, faces, *halos)


class Level:
    def __init__(self, count, refs):
        self.count = count
        self.f, self.diag, self.jac, self.x, self.dir, self.res, self.edge = refs
        self.tables = [element_matrix(count, d) for d in range(3)]
        self.gains = None


def tile(index):
    return pl.ds(index * 8, 8)


def cycle_kernel(block0, block1, block2, block3, fields, *scratch):
    sec = lax.axis_index("section")
    my_gx, my_gy = lax.axis_index("gx"), lax.axis_index("gy")
    levels = [Level(n, scratch[7 * p : 7 * p + 7]) for p, n in enumerate((5, 3, 2))]
    pieces, kap, half = scratch[21:24]
    fine, middle, coarse = levels
    lane = iota((8, 128), 1)
    sub = iota((8, 128), 0)
    group = lane // EZ
    odd = group % 2 == 1
    element = lane % EZ
    place = sub % 4
    low_half = sub < 4
    blocks = split_sections()[3]

    def lanes_of(upper, lower):
        return jnp.where(lane < 64, jnp.where(sec == 0, upper[0], upper[1]), jnp.where(sec == 0, lower[0], lower[1]))

    entry = [[[float(STEP_SIZE * blocks[2 * p + a, 2 * p + b]) for p in range(2)] for b in range(2)] for a in range(2)]
    same = lanes_of(entry[0][0], entry[1][1])
    swap = lanes_of(entry[0][1], entry[1][0])
    centre = (CHEB_HIGH + CHEB_LOW) / 2.0
    radius = (CHEB_HIGH - CHEB_LOW) / 2.0
    first_rho = radius / centre
    second_rho = 1.0 / (2.0 * centre / radius - first_rho)
    keep = 1.0 + second_rho * first_rho
    push = 2.0 * second_rho / radius * centre

    for b, block in enumerate((block0, block1, block2, block3)):
        gy = lax.rem(my_gy + 4 - b, 4)
        for a in range(4):
            column = lax.rem(my_gx + 4 - a, 4) * 4 + gy
            start = pl.multiple_of(column * PIECE, 8)
            pieces[pl.ds(start, PIECE), :] = block[a * PIECE : a * PIECE + PIECE, :]

    def rows_of(r, h):
        return pieces[pl.ds(8 * h * PIECE + r, 8, stride=PIECE), :]

    def place_nodes(r, last):
        low, high = rows_of(r, 0), rows_of(r, 1)
        fine.f[tile(r), :] = jnp.where(odd, pltpu.roll(high, 32, 1), low)
        if not last:
            fine.f[tile(64 + r), :] = jnp.where(odd, high, pltpu.roll(low, 96, 1))
        return low, high

    for r in range(61):
        place_nodes(r, False)
    flags = []
    for r in range(3):
        low, high = place_nodes(61 + r, True)
        turned = [[pltpu.roll(v, 32 * m, 1) if m else v for m in range(4)] for v in (low, high)]
        flags.append(choose(group, [turned[0][3], turned[1][0], turned[0][1], turned[1][2]]))
        flags.append(choose(group, [turned[0][1], turned[1][2], turned[0][3], turned[1][0]]))
    for r in range(32):
        turned = []
        for h in range(2):
            got = rows_of(HALF + r, h)
            turned.append([pltpu.roll(got, 32 * m, 1) if m else got for m in range(4)])
        for q in range(4):
            if q * 32 + r < 125:
                kap[tile(q * 32 + r), :] = choose(group, [turned[g % 2][(g - q) % 4] for g in range(4)])

    for level in levels:
        n = level.count
        picks = {5: (0, 1, 2, 3, 4), 3: (0, 2, 4), 2: (0, 4)}[n]
        level.gains = [face_gains(flags[d], d // 2, d % 2, n) for d in range(6)]
        terms = []
        for d in range(3):
            row = []
            for m in range(n):
                value = float(level.tables[d][m, m])
                if m == 0:
                    row.append(level.gains[2 * d] + value)
                elif m == n - 1:
                    row.append(level.gains[2 * d + 1] + value)
                else:
                    row.append(value)
            terms.append(row)
        for k in range(n):
            for i in range(n):
                both = terms[2][k] + terms[0][i]
                for j in range(n):
                    source = (picks[k] * 5 + picks[i]) * 5 + picks[j]
                    value = kap[tile(source), :] + (both + terms[1][j])
                    where = tile((k * n + i) * n + j)
                    level.diag[where, :] = value
                    scale = 1.0 / (1.0 + STEP_SIZE * JACOBI_SCALE * value)
                    level.jac[where, :] = scale * (1.0 / centre)
        level.edge[...] = jnp.zeros_like(level.edge)

    def apply(p, source, finish, carry):
        level = levels[p]
        n = level.count
        kx, ky, kz = level.tables
        for r in range(n * n):
            v = source[tile(r * n + n - 1), :]
            moved = jnp.where(place == 0, pltpu.roll(v, 5, 0), pltpu.roll(v, 1, 0))
            level.edge[tile(r * n), :] = level.gains[2] * moved
            v = source[tile(r * n), :]
            moved = jnp.where(place == 3, pltpu.roll(v, 3, 0), pltpu.roll(v, 7, 0))
            level.edge[tile(r * n + n - 1), :] = level.gains[3] * moved

        def at(r, j):
            return pl.ds(pl.multiple_of(j * 8, 8) + r * n * 8, 8)

        def plane(j, carry):
            sides = []
            for m in range(1, n):
                coef = choose(j, [float(ky[a, (a + m) % n]) for a in range(n)])
                sides.append((coef, jnp.where(j + m >= n, j + m - n, j + m)))
            v = [[source[at(k * n + i, j), :] for i in range(n)] for k in range(n)]

            def around(u):
                turned = pltpu.roll(u, 4, 0)
                return turned, jnp.where(odd, pltpu.roll(turned, 32, 1), pltpu.roll(turned, 96, 1))

            for k in range(n):
                left, left_far = around(v[k][n - 1])
                right, right_far = around(v[k][0])
                for i in range(n):
                    r = k * n + i
                    total = level.diag[at(r, j), :] * v[k][i] - level.edge[at(r, j), :]
                    for m in range(n):
                        if m != i:
                            total = total + float(kx[i, m]) * v[k][m]
                    for m in range(n):
                        if m != k:
                            total = total + float(kz[k, m]) * v[m][i]
                    for coef, far in sides:
                        total = total + coef * source[at(r, far), :]
                    if i == 0:
                        total = total - level.gains[0] * jnp.where(low_half, left_far, left)
                    if i == n - 1:
                        total = total - level.gains[1] * jnp.where(low_half, right, right_far)
                    if k == 0:
                        u = v[n - 1][i]
                        moved = jnp.where(element == 0, pltpu.roll(u, 97, 1), pltpu.roll(u, 1, 1))
                        total = total - level.gains[4] * moved
                    if k == n - 1:
                        u = v[0][i]
                        moved = jnp.where(element == EZ - 1, pltpu.roll(u, 31, 1), pltpu.roll(u, 127, 1))
                        total = total - level.gains[5] * moved
                    out = v[k][i] + (same * total + swap * pltpu.roll(total, 64, 1))
                    carry = finish(at(r, j), v[k][i], out, carry)
            return carry
        return lax.fori_loop(0, n, plane, carry)

    def smooth_first(p):
        level = levels[p]
        level.dir[...] = level.jac[...] * level.f[...]
        def finish(where, v, av, carry):
            level.x[where, :] = keep * v + push * level.jac[where, :] * (level.f[where, :] - av)
            return carry
        apply(p, level.dir, finish, 0)

    def defect(p):
        level = levels[p]
        def finish(where, v, av, carry):
            level.res[where, :] = level.f[where, :] - av
            return carry
        apply(p, level.x, finish, 0)

    def smooth_again(p):
        level = levels[p]
        def middle_step(where, v, av, carry):
            left = level.f[where, :] - av
            level.res[where, :] = left
            level.dir[where, :] = level.jac[where, :] * left
            return carry
        apply(p, level.x, middle_step, 0)
        def finish(where, v, av, carry):
            step = push * level.jac[where, :] * (level.res[where, :] - av)
            level.x[where, :] = level.x[where, :] + keep * v + step
            return carry
        apply(p, level.dir, finish, 0)

    def combine(weights, parts):
        total = None
        for weight, part in zip(weights, parts):
            if abs(weight) > 1e-14:
                term = part if abs(weight - 1.0) < 1e-14 else float(weight) * part
                total = term if total is None else total + term
        return total

    def change(table, source, target, add):
        m, n = table.shape
        for i in range(n):
            parts = [source[pl.ds((k * n + i) * n * 8, 8 * n), :] for k in range(n)]
            for k in range(m):
                half[pl.ds((k * n + i) * n * 8, 8 * n), :] = combine(table[k], parts)
        for k in range(m):
            parts = [half[pl.ds((k * n + i) * n * 8, 8 * n), :] for i in range(n)]
            for i in range(m):
                line = combine(table[i], parts)
                points = [line[8 * j : 8 * j + 8] for j in range(n)]
                for j in range(m):
                    value = combine(table[j], points)
                    where = tile((k * m + i) * m + j)
                    target[where, :] = target[where, :] + value if add else value

    def down(n, m):
        fine_nodes, fine_weights = lobatto(n)
        coarse_nodes, coarse_weights = lobatto(m)
        table = lagrange_table(coarse_nodes, fine_nodes)
        return (1.0 / coarse_weights)[:, None] * table.T * fine_weights[None, :]

    def up(m, n):
        return lagrange_table(lobatto(m)[0], lobatto(n)[0])

    smooth_first(0)
    defect(0)
    change(down(5, 3), fine.res, middle.f, False)
    smooth_first(1)
    defect(1)
    change(down(3, 2), middle.res, coarse.f, False)
    smooth_first(2)
    change(up(2, 3), coarse.x, middle.x, True)
    smooth_again(1)
    change(up(3, 5), middle.x, fine.x, True)
    smooth_again(0)

    def last(where, v, av, carry):
        fields[where, :] = av
        return carry
    apply(0, fine.x, last, 0)
    fields[FIELD : 2 * FIELD, :] = fine.f[...]
    column = (my_gx % 2) * 4 + my_gy
    fields[2 * FIELD : 2 * FIELD + 125, :] = fine.x[pl.ds(column, 125, stride=8), :]
    fields[2 * FIELD + 125 : 2 * FIELD + 128, :] = jnp.zeros((3, 128), F32)


def finish_kernel(own, other, guess, sol, res_out, arnoldi, cols, outs):
    sec = lax.axis_index("section")
    my_gx, my_gy = lax.axis_index("gx"), lax.axis_index("gy")
    whole, back, back_matrix, blocks, cross = split_sections()
    weights = jnp.where(iota((8, 128), 1) < 64, float(cross[0]), float(cross[1]))
    nothing = jnp.zeros((8, 128), F32)

    def product(a, b, c, d):
        return a * c + b * d + weights * (a * d + b * c)

    def sums(step, carry):
        uppers, sizes = carry
        for m in range(5):
            r = pl.multiple_of(step * 40, 8) + m * 8
            a, b = own[pl.ds(r, 8), :], other[pl.ds(r, 8), :]
            c, d = own[pl.ds(FIELD + r, 8), :], other[pl.ds(FIELD + r, 8), :]
            uppers = uppers + product(a, b, c, d)
            sizes = sizes + product(c, d, c, d)
        return uppers, sizes
    uppers, sizes = lax.fori_loop(0, 25, sums, (nothing, nothing))
    size = jnp.sum(sizes, keepdims=True)
    upper = jnp.sum(uppers, keepdims=True) / size

    def remainder(step, carry):
        for m in range(5):
            r = pl.multiple_of(step * 40, 8) + m * 8
            a = own[pl.ds(r, 8), :] - upper * own[pl.ds(FIELD + r, 8), :]
            b = other[pl.ds(r, 8), :] - upper * other[pl.ds(FIELD + r, 8), :]
            carry = carry + product(a, b, a, b)
        return carry
    rest = jnp.sum(lax.fori_loop(0, 25, remainder, nothing), keepdims=True)
    beta = jnp.sqrt(size)
    lower = jnp.sqrt(rest) / beta
    weight = upper / (upper * upper + lower * lower)
    entries = float(125 * EZ * COLS * 4)
    for place_out, value in enumerate((beta * (1.0 / math.sqrt(entries)), upper, lower)):
        arnoldi[place_out] = value[0, 0]

    lane = iota((32, 128), 1)
    here = lane // EZ % 2 == my_gx // 2
    factors = []
    for s in range(2):
        row = []
        for p in range(2):
            parts = []
            for mine in range(2):
                t = whole[2 * mine + s]
                pairs = [jnp.where(lane < 64, float(t[2 * q]), float(t[2 * q + 1])) for q in range(2)]
                parts.append(pairs[mine] if p == 0 else pairs[1 - mine])
            row.append(jnp.where(here, jnp.where(sec == 0, parts[0], parts[1]), 0.0))
        factors.append(row)
    column = (my_gx % 2) * 4 + my_gy
    cols[...] = jnp.zeros_like(cols)
    total = jnp.zeros((128, 160), F32)
    for k in range(5):
        for p, source in enumerate((own, other)):
            image = source[pl.ds(k * 200 + column, 25, stride=8), :]
            start = source[pl.ds(FIELD + k * 200 + column, 25, stride=8), :]
            for s in range(2):
                factor = factors[s][p][:25]
                z = weight * (factor * source[2 * FIELD + k * 25 : 2 * FIELD + k * 25 + 25, :])
                r = factor * (start - weight * image)
                if p == 0:
                    cols[s * 32 : s * 32 + 25, :] = z
                    cols[64 + s * 32 : 64 + s * 32 + 25, :] = r
                else:
                    cols[s * 32 : s * 32 + 25, :] += z
                    cols[64 + s * 32 : 64 + s * 32 + 25, :] += r
        hit = (iota((128, 160), 1) == 5 * (iota((128, 160), 0) % EZ) + k).astype(F32)
        total = total + exact_dot(cols[...], hit)
    outs[...] = total
    for i in range(5):
        for j in range(5):
            r = 5 * i + j
            for s in range(2):
                sol[i, j, s : s + 1, :] = guess[i, j, s : s + 1, :] + outs[s * 32 + r : s * 32 + r + 1, :]
                res_out[i, j, s : s + 1, :] = outs[64 + s * 32 + r : 64 + s * 32 + r + 1, :]


def cycle(blocks):
    scratch = []
    for n in (5, 3, 2):
        scratch += [pltpu.VMEM((n**3 * 8, 128), F32)] * 7
    scratch += [
        pltpu.VMEM((COLS * PIECE, 128), F32),
        pltpu.VMEM((FIELD, 128), F32),
        pltpu.VMEM((FIELD, 128), F32),
    ]
    return pl.pallas_call(
        cycle_kernel,
        out_shape=jax.ShapeDtypeStruct((2 * FIELD + 128, 128), F32),
        in_specs=[VMEM] * 4,
        out_specs=VMEM,
        scratch_shapes=scratch,
        compiler_params=limit(24),
        name="cycle",
    )(*blocks)


def finish(own, other, guess):
    return pl.pallas_call(
        finish_kernel,
        out_shape=[
            jax.ShapeDtypeStruct(guess.shape, F32),
            jax.ShapeDtypeStruct(guess.shape, F32),
            jax.ShapeDtypeStruct((3,), F32),
        ],
        in_specs=[VMEM] * 3,
        out_specs=[VMEM, VMEM, pl.BlockSpec(memory_space=pltpu.SMEM)],
        scratch_shapes=[pltpu.VMEM((128, 128), F32), pltpu.VMEM((128, 160), F32)],
        compiler_params=limit(24),
        name="finish",
    )(own, other, guess)


def turn(x, axis, offset):
    return lax.ppermute(x, axis, [(n, (n + offset) % 4) for n in range(4)])


def swap_cores(x):
    return lax.ppermute(x, "section", [(0, 1), (1, 0)])


def gathered_body(rhs, guess, kappa, bc_flags):
    rhs, guess = (jnp.transpose(v, (1, 2, 0, 3)) for v in (rhs, guess))
    halos = [turn(guess, axis, offset) for axis in ("gx", "gy") for offset in (1, 3)]
    base = local_part(rhs, guess, kappa, bc_flags)
    mine, theirs = halo_part(*base, halos)
    got = swap_cores(theirs)
    piece = jnp.concatenate([mine[:HALF] + got, mine[HALF:]])
    line = jnp.concatenate([piece] + [turn(piece, "gx", offset) for offset in (1, 2, 3)])
    blocks = [line] + [turn(line, "gy", offset) for offset in (1, 2, 3)]
    own = cycle(blocks)
    sol, res, arnoldi = finish(own, swap_cores(own), guess)
    sol, res = (jnp.transpose(v, (2, 0, 1, 3)) for v in (sol, res))
    return sol, res, arnoldi


def solution(mesh):
    placed = (
        P("section", "gx", "gy", None),
        P("section", "gx", "gy", None),
        P("gx", "gy", None),
        P(None, "gx", "gy", None),
    )
    sizes = (mesh.shape["section"], mesh.shape["gx"], mesh.shape["gy"])

    def step(rhs, guess, kappa, bc_flags):
        fits = sizes == (2, 4, 4) and rhs.shape == (4, 20, 20, 160)
        return jax.shard_map(
            gathered_body if fits else stepwise,
            mesh=mesh,
            in_specs=placed,
            out_specs=(P("section", "gx", "gy", None), P("section", "gx", "gy", None), P()),
            check_vma=False,
        )(rhs, guess, kappa, bc_flags)

    return step
```

```python
from functools import partial
import math

import jax
import jax.numpy as jnp
import numpy as np
from jax import lax
from jax.experimental import pallas as pl
from jax.experimental.pallas import tpu as pltpu
from jax.sharding import PartitionSpec as P

ADVECT = (1.0, 0.7, 0.5)
DIFFUSE = 0.05
STEP_SIZE = 0.2
JACOBI_SCALE = 0.25
CHEB_LOW = 0.25
CHEB_HIGH = 2.0
LETTERS = "abcdef"


def extended(x, sides, width):
    for axis, dim in sides:
        peers, length = (lax.axis_size(axis), x.shape[dim])
        up = [(i, (i + 1) % peers) for i in range(peers)]
        down = [(j, i) for i, j in up]
        last = lax.slice_in_dim(x, length - width, length, axis=dim)
        leading = lax.slice_in_dim(x, 0, width, axis=dim)
        before = lax.ppermute(last, axis, up)
        after = lax.ppermute(leading, axis, down)
        x = jnp.concatenate([before, x, after], axis=dim)
    return x


def lobatto(count):
    if count == 5:
        inner = math.sqrt(3.0 / 7.0)
        return (
            np.array([-1.0, -inner, 0.0, inner, 1.0]),
            np.array([0.1, 49.0 / 90.0, 32.0 / 45.0, 49.0 / 90.0, 0.1]),
        )
    if count == 3:
        return (np.array([-1.0, 0.0, 1.0]), np.array([1.0 / 3.0, 4.0 / 3.0, 1.0 / 3.0]))
    return (np.array([-1.0, 1.0]), np.array([1.0, 1.0]))


def lagrange_table(nodes, points):
    table = np.ones((len(points), len(nodes)))
    for column in range(len(nodes)):
        for other in range(len(nodes)):
            if other != column:
                table[:, column] *= (points - nodes[other]) / (nodes[column] - nodes[other])
    return table


def slope_table(nodes):
    total = len(nodes)
    factor = np.array(
        [np.prod([nodes[i] - nodes[k] for k in range(total) if k != i]) for i in range(total)]
    )
    table = np.zeros((total, total))
    for row in range(total):
        for column in range(total):
            if row != column:
                table[row, column] = factor[row] / factor[column] / (nodes[row] - nodes[column])
        table[row, row] = -np.sum(table[row])
    return table


def element_matrix(count, direction):
    nodes, weights = lobatto(count)
    slopes = slope_table(nodes)
    stiffness = (1.0 / weights)[:, None] * (slopes.T @ (weights[:, None] * slopes))
    return ADVECT[direction] * slopes + DIFFUSE * stiffness


def legendre_pair(point, order):
    values = [1.0, point]
    slopes = [0.0, 1.0]
    for index in range(1, order):
        values.append(
            ((2 * index + 1) * point * values[index] - index * values[index - 1]) / (index + 1)
        )
        slopes.append(slopes[index - 1] + (2 * index + 1) * values[index])
    return (values, slopes)


def radau_nodes():
    starts = [0.0885879595127039, 0.4094668644407347, 0.7876594617608471]
    found = []
    for start in starts:
        point = start
        for sweep in range(30):
            values, slopes = legendre_pair(2.0 * point - 1.0, 4)
            change = (values[4] - values[3]) / (2.0 * (slopes[4] - slopes[3]))
            point = point - change
        found.append(point)
    found.append(1.0)
    return found


def poly_times(coefs, root):
    result = [0.0] * (len(coefs) + 1)
    for index in range(len(coefs)):
        result[index + 1] += coefs[index]
        result[index] -= root * coefs[index]
    return result


def radau_matrix():
    order = 4
    nodes = radau_nodes()
    matrix = np.zeros((order, order))
    for column in range(order):
        coefs = [1.0]
        denominator = 1.0
        for other in range(order):
            if other != column:
                coefs = poly_times(coefs, nodes[other])
                denominator *= nodes[column] - nodes[other]
        for row in range(order):
            upper_end = nodes[row]
            integral = 0.0
            for index in range(len(coefs)):
                integral += coefs[index] * upper_end ** (index + 1) / (index + 1)
            matrix[row, column] = integral / denominator
    return matrix


def node_einsum(table, field, axis):
    labels = LETTERS[: field.ndim]
    source = labels[: axis + 1] + "j" + labels[axis + 2 :]
    target = labels[: axis + 1] + "i" + labels[axis + 2 :]
    return jnp.einsum(
        "ij," + source + "->" + target,
        jnp.asarray(table, jnp.float32),
        field,
        precision=lax.Precision.HIGHEST,
    )


def apply_along(field, axis, count, table):
    shape = field.shape
    split = shape[:axis] + (shape[axis] // count, count) + shape[axis + 1 :]
    mapped = node_einsum(table, field.reshape(split), axis)
    return mapped.reshape(
        shape[:axis] + (mapped.shape[axis] * mapped.shape[axis + 1],) + shape[axis + 1 :]
    )


def line_part(field, axis, count, table, left_gain, right_gain, left_edge, right_edge):
    shape = field.shape
    elements = shape[axis] // count
    split = field.reshape(shape[:axis] + (elements, count) + shape[axis + 1 :])
    linear = node_einsum(table, split, axis)
    first = lax.index_in_dim(split, 0, axis + 1, keepdims=False)
    last = lax.index_in_dim(split, count - 1, axis + 1, keepdims=False)
    before = jnp.concatenate(
        [jnp.expand_dims(left_edge, axis), lax.slice_in_dim(last, 0, elements - 1, axis=axis)], axis
    )
    after = jnp.concatenate(
        [lax.slice_in_dim(first, 1, elements, axis=axis), jnp.expand_dims(right_edge, axis)], axis
    )
    front = jnp.expand_dims(left_gain * (first - before), axis + 1)
    back = jnp.expand_dims(right_gain * (last - after), axis + 1)
    if count > 2:
        middle_shape = list(front.shape)
        middle_shape[axis + 1] = count - 2
        pieces = [front, jnp.zeros(middle_shape, jnp.float32), back]
    else:
        pieces = [front, back]
    return (linear + jnp.concatenate(pieces, axis + 1)).reshape(shape)


def diag_along(shape, axis, count, table, left_gain, right_gain):
    elements = shape[axis] // count
    split = shape[:axis] + (elements, count) + shape[axis + 1 :]
    profile = [1] * len(split)
    profile[axis + 1] = count
    diagonal_entries = np.array([table[index, index] for index in range(count)])
    base = jnp.broadcast_to(jnp.asarray(diagonal_entries, jnp.float32).reshape(profile), split)
    front = jnp.expand_dims(left_gain, axis + 1)
    back = jnp.expand_dims(right_gain, axis + 1)
    if count > 2:
        middle_shape = list(front.shape)
        middle_shape[axis + 1] = count - 2
        pieces = [front, jnp.zeros(middle_shape, jnp.float32), back]
    else:
        pieces = [front, back]
    return (base + jnp.concatenate(pieces, axis + 1)).reshape(shape)


def level_kappa(kappa, count):
    if count == 5:
        return kappa
    picks = np.array([0, 2, 4]) if count == 3 else np.array([0, 4])
    extents = [extent // 5 for extent in kappa.shape]
    grouped = kappa.reshape(extents[0], 5, extents[1], 5, extents[2], 5)
    for axis in (1, 3, 5):
        grouped = jnp.take(grouped, picks, axis=axis)
    return grouped.reshape(extents[0] * count, extents[1] * count, extents[2] * count)


def face_plane(face, direction, count):
    plane = face.astype(jnp.float32)
    for axis in range(3):
        if axis != direction:
            plane = jnp.repeat(plane, count, axis=axis)
    return plane


def build_level(kappa, flags, count):
    nodes, weights = lobatto(count)
    kappa_level = level_kappa(kappa, count)
    tables, lefts, rights = ([], [], [])
    diagonal = kappa_level
    for direction in range(3):
        table = element_matrix(count, direction)
        lower = face_plane(flags[2 * direction], direction, count)
        upper = face_plane(flags[2 * direction + 1], direction, count)
        left_gain = (ADVECT[direction] * (1.0 + lower) / 2.0 + DIFFUSE * count * count) / float(
            weights[0]
        )
        right_gain = (DIFFUSE * count * count - ADVECT[direction] * (1.0 - upper) / 2.0) / float(
            weights[-1]
        )
        tables.append(table)
        lefts.append(left_gain)
        rights.append(right_gain)
        diagonal = diagonal + diag_along(
            kappa_level.shape, direction, count, table, left_gain, right_gain
        )
    scale = 1.0 / (1.0 + STEP_SIZE * JACOBI_SCALE * diagonal)
    return (count, tables, lefts, rights, kappa_level, scale)


def restrict(field, fine_count, coarse_count):
    fine_nodes, fine_weights = lobatto(fine_count)
    coarse_nodes, coarse_weights = lobatto(coarse_count)
    table = (
        (1.0 / coarse_weights)[:, None]
        * lagrange_table(coarse_nodes, fine_nodes).T
        * fine_weights[None, :]
    )
    for axis in range(field.ndim - 3, field.ndim):
        field = apply_along(field, axis, fine_count, table)
    return field


def prolong(field, coarse_count, fine_count):
    fine_nodes, fine_weights = lobatto(fine_count)
    coarse_nodes, coarse_weights = lobatto(coarse_count)
    table = lagrange_table(coarse_nodes, fine_nodes)
    for axis in range(field.ndim - 3, field.ndim):
        field = apply_along(field, axis, coarse_count, table)
    return field


def chebyshev(rhs, start, level, operator):
    centre = (CHEB_HIGH + CHEB_LOW) / 2.0
    radius = (CHEB_HIGH - CHEB_LOW) / 2.0
    ratio = centre / radius
    first_rho = 1.0 / ratio
    second_rho = 1.0 / (2.0 * ratio - first_rho)
    scale = level[5]
    if start is None:
        remain = rhs
    else:
        remain = rhs - operator(start, level)
    step = scale * remain / centre
    guess = step if start is None else start + step
    remain = remain - operator(step, level)
    step = second_rho * first_rho * step + 2.0 * second_rho / radius * scale * remain
    return guess + step


def vcycle(rhs, levels, operator):
    fine, middle, coarse = levels
    fine_x = chebyshev(rhs, None, fine, operator)
    middle_rhs = restrict(rhs - operator(fine_x, fine), 5, 3)
    middle_x = chebyshev(middle_rhs, None, middle, operator)
    coarse_rhs = restrict(middle_rhs - operator(middle_x, middle), 3, 2)
    coarse_x = chebyshev(coarse_rhs, None, coarse, operator)
    middle_x = chebyshev(middle_rhs, middle_x + prolong(coarse_x, 2, 3), middle, operator)
    return chebyshev(rhs, fine_x + prolong(middle_x, 3, 5), fine, operator)


def spatial(field, level):
    count, tables, lefts, rights, kappa_level, scale = level
    padded = extended(field, (("gx", 1), ("gy", 2)), 1)
    total = kappa_level * field
    total = total + line_part(
        field,
        1,
        count,
        tables[0],
        lefts[0],
        rights[0],
        padded[:, 0, 1:-1, :],
        padded[:, -1, 1:-1, :],
    )
    total = total + line_part(
        field,
        2,
        count,
        tables[1],
        lefts[1],
        rights[1],
        padded[:, 1:-1, 0, :],
        padded[:, 1:-1, -1, :],
    )
    total = total + line_part(
        field, 3, count, tables[2], lefts[2], rights[2], field[:, :, :, -1], field[:, :, :, 0]
    )
    return total


def apply_system(field, level, coupling):
    image = spatial(field, level)
    everyone = lax.all_gather(image, "section", axis=0, tiled=True)
    butcher = jnp.asarray(radau_matrix(), jnp.float32)
    rows = lax.dynamic_slice_in_dim(
        butcher, lax.axis_index("section") * field.shape[0], field.shape[0], 0
    )
    mixed = jnp.einsum("ij,jabc->iabc", rows, everyone, precision=lax.Precision.HIGHEST)
    return field + STEP_SIZE * mixed


def global_total(values):
    return lax.psum(values, ("section", "gx", "gy"))


def stepwise(rhs, guess, kappa, bc_flags):
    levels = [build_level(kappa, bc_flags, count) for count in (5, 3, 2)]
    section_operator = partial(apply_system, coupling=None)
    start_residual = rhs - section_operator(guess, levels[0])
    dofs = float(rhs.size * lax.axis_size("section") * lax.axis_size("gx") * lax.axis_size("gy"))
    beta = jnp.sqrt(global_total(jnp.sum(start_residual * start_residual).reshape(1))[0])
    basis = start_residual / beta
    precond = vcycle(basis, levels, section_operator)
    image = section_operator(precond, levels[0])
    upper = global_total(jnp.sum(image * basis).reshape(1))[0]
    remainder = image - upper * basis
    lower = jnp.sqrt(global_total(jnp.sum(remainder * remainder).reshape(1))[0])
    weight = beta * upper / (upper * upper + lower * lower)
    solution = guess + weight * precond
    residual = start_residual - weight * image
    arnoldi = jnp.stack([beta / math.sqrt(dofs), upper, lower]).astype(jnp.float32)
    return (solution, residual, arnoldi)


EZ = 32
COLS = 16
HALF = 64
PIECE = 96
FIELD = 1000
F32 = jnp.float32


def split_sections():
    matrix = radau_matrix()
    values, vectors = np.linalg.eig(matrix)
    order = [n for n in np.argsort(np.abs(values.imag), kind="stable") if values[n].imag > 0]
    bases = []
    for n in order:
        plane = np.stack([vectors[:, n].real, vectors[:, n].imag], axis=1)
        bases.append(np.linalg.qr(plane)[0])
    left, cross, right = np.linalg.svd(bases[0].T @ bases[1])
    bases = [bases[0] @ left, bases[1] @ right.T]
    for c in range(2):
        sign = np.sign(bases[0][np.argmax(np.abs(bases[0][:, c])), c])
        bases = [np.concatenate([b[:, :c], sign * b[:, c : c + 1], b[:, c + 1 :]], axis=1) for b in bases]
    whole = np.concatenate(bases, axis=1)
    back = np.linalg.inv(whole)
    return whole, back, back @ matrix, back @ matrix @ whole, cross


def iota(shape, dim):
    return lax.broadcasted_iota(jnp.int32, shape, dim)


def exact_dot(a, b):
    return lax.dot_general(
        a, b, (((1,), (0,)), ((), ())), precision=lax.Precision.HIGHEST, preferred_element_type=F32
    )


def choose(index, values):
    out = values[-1]
    for place in range(len(values) - 2, -1, -1):
        out = jnp.where(index == place, values[place], out)
    return out


def face_gains(flag, direction, side, count):
    nodes, weights = lobatto(count)
    c, nu = ADVECT[direction], DIFFUSE * count * count
    if side == 0:
        return (c * (1.0 + flag) / 2.0 + nu) * (1.0 / float(weights[0]))
    return (nu - c * (1.0 - flag) / 2.0) * (1.0 / float(weights[-1]))


def column_tables():
    kx, ky, kz = (element_matrix(5, d) for d in range(3))
    rows = np.zeros((64, 64))
    for s in range(2):
        for i in range(5):
            for j in range(5):
                r = s * 32 + i * 5 + j
                for m in range(5):
                    rows[r, s * 32 + m * 5 + j] += kx[i, m]
                    rows[r, s * 32 + i * 5 + m] += ky[j, m]
    lines = np.zeros((160, 320))
    for e in range(EZ):
        lines[e * 5 : e * 5 + 5, e * 5 : e * 5 + 5] = kz.T
        lines[(e - 1) % EZ * 5 + 4, 160 + e * 5] = 1.0
        lines[(e + 1) % EZ * 5, 160 + e * 5 + 4] = 1.0
    return rows.astype(np.float32), lines.astype(np.float32)


def pick_line(k):
    return (iota((160, 128), 0) == 5 * (iota((160, 128), 1) % EZ) + k).astype(F32)


def pair_factors(sec, table, own, s):
    upper = iota((32, 128), 1) < 64
    first = jnp.where(upper, float(table[0, s]), float(table[1, s]))
    second = jnp.where(upper, float(table[2, 2 + s]), float(table[3, 2 + s]))
    if not own:
        first = jnp.where(upper, float(table[2, s]), float(table[3, s]))
        second = jnp.where(upper, float(table[0, 2 + s]), float(table[1, 2 + s]))
    return jnp.where(sec == 0, first, second)


def pack_nodes(nodes):
    odd = iota((HALF, 128), 1) // EZ % 2 == 1
    return jnp.where(odd, nodes[HALF:, :], nodes[:HALF, :])


def fetch(pairs, sems):
    copies = [pltpu.make_async_copy(src, dst, sems.at[n]) for n, (src, dst) in enumerate(pairs)]
    for copy in copies:
        copy.start()
    for copy in copies:
        copy.wait()


def local_kernel(
    rhs_in, guess_in, kappa_in, flags_in, rows_in, lines_in, base,
    rhs, guess, kappa, flags, rows_t, lines_t, sems, x, kap, stack, own_nodes, other_nodes, krep,
):
    sec = lax.axis_index("section")
    fetch(
        [(rhs_in, rhs), (guess_in, guess), (kappa_in, kappa), (flags_in, flags), (rows_in, rows_t), (lines_in, lines_t)],
        sems,
    )
    x[...] = jnp.zeros_like(x)
    kap[...] = jnp.zeros_like(kap)
    stack[...] = jnp.zeros_like(stack)
    for i in range(5):
        kap[5 * i : 5 * i + 5, :] = kappa[i]
        for j in range(5):
            r = 5 * i + j
            value = guess[i, j]
            left = rhs[i, j] - value
            for s in range(2):
                x[s * 32 + r : s * 32 + r + 1, :] = value[s : s + 1]
                stack[s * 32 + r : s * 32 + r + 1, :] = left[s : s + 1]
    flag = flags[:, 0, 0, :].astype(F32)
    spread = (iota((EZ, 160), 1) // 5 == iota((EZ, 160), 0)).astype(F32)
    wide = exact_dot(flag, spread)
    gains = [face_gains(wide[d : d + 1, :], d // 2, d % 2, 5) for d in range(6)]
    row = iota((32, 160), 0)
    lane = iota((32, 160), 1) % 5
    none = jnp.zeros((32, 160), F32)
    gx = jnp.where(row < 5, gains[0], jnp.where((row >= 20) & (row < 25), gains[1], none))
    gy = jnp.where(row % 5 == 0, gains[2], jnp.where(row % 5 == 4, gains[3], none))
    gz = jnp.where(lane == 0, gains[4], jnp.where(lane == 4, gains[5], none))
    gy = jnp.where(row < 25, gy, none)
    for place, gain in ((160, gx), (192, gy)):
        base[place : place + 32, :] = gain[:, :128]
        base[64 + place : 96 + place, :EZ] = gain[:, 128:]
    field = x[...]
    along = exact_dot(rows_t[...], field)
    across = exact_dot(field, lines_t[...])
    own = kap[...] + gx + gy + gz
    for s in range(2):
        r = slice(s * 32, s * 32 + 32)
        image = own * field[r] + along[r] + across[r, :160] - gz * across[r, 160:]
        stack[64 + s * 32 : 96 + s * 32, :] = image
    whole, back, back_matrix, blocks, cross = split_sections()
    own_nodes[...] = jnp.zeros_like(own_nodes)
    other_nodes[...] = jnp.zeros_like(other_nodes)
    krep[...] = jnp.zeros_like(krep)
    source = stack[...]
    coefs = kap[...]
    for k in range(5):
        pick = pick_line(k)
        parts = exact_dot(source, pick)
        for target, mark in ((own_nodes, True), (other_nodes, False)):
            total = jnp.zeros((32, 128), F32)
            for s in range(2):
                total = total + pair_factors(sec, back, mark, s) * parts[s * 32 : s * 32 + 32]
                factor = pair_factors(sec, -STEP_SIZE * back_matrix, mark, s)
                total = total + factor * parts[64 + s * 32 : 96 + s * 32]
            target[25 * k : 25 * k + 25, :] = total[:25]
        krep[25 * k : 25 * k + 25, :] = exact_dot(coefs, pick)[:25]
    repeat = (iota((EZ, 128), 1) % EZ == iota((EZ, 128), 0)).astype(F32)
    shown = exact_dot(flag, repeat)
    upper = iota((1, 128), 1) < 64
    for r in range(3):
        own_nodes[125 + r : 126 + r, :] = jnp.where(upper, shown[2 * r : 2 * r + 1], shown[2 * r + 1 : 2 * r + 2])
    base[:HALF, :] = pack_nodes(own_nodes)
    base[PIECE : PIECE + HALF, :] = pack_nodes(other_nodes)
    base[HALF:PIECE, :] = choose(iota((32, 128), 1) // EZ, [krep[32 * q : 32 * q + 32, :] for q in range(4)])


def halo_kernel(base, x1, x3, y1, y3, mine, theirs, near, own_nodes, other_nodes):
    sec = lax.axis_index("section")
    even_x = lax.axis_index("gx") % 2 == 0
    even_y = lax.axis_index("gy") % 2 == 0
    for ref in (near, own_nodes, other_nodes):
        ref[...] = jnp.zeros_like(ref)
    for m in range(5):
        for s in range(2):
            r = s * 32
            one = slice(s, s + 1)
            near[r + m : r + m + 1, :] = jnp.where(even_x, x3[4, m, one, :], x1[4, m, one, :])
            near[r + 20 + m : r + 21 + m, :] = jnp.where(even_x, x1[0, m, one, :], x3[0, m, one, :])
            r += 64
            near[r + 5 * m : r + 5 * m + 1, :] = jnp.where(even_y, y3[m, 4, one, :], y1[m, 4, one, :])
            near[r + 5 * m + 4 : r + 5 * m + 5, :] = jnp.where(even_y, y1[m, 0, one, :], y3[m, 0, one, :])
    gx, gy = (
        jnp.concatenate([base[r : r + 32, :], base[64 + r : 96 + r, :EZ]], axis=1) for r in (160, 192)
    )
    parts_in = []
    for s in range(2):
        r = s * 32
        parts_in.append(gx * near[r : r + 32, :] + gy * near[64 + r : 96 + r, :])
    source = jnp.concatenate(parts_in, axis=0)
    back_matrix = split_sections()[2]
    for k in range(5):
        parts = exact_dot(source, pick_line(k))
        for target, mark in ((own_nodes, True), (other_nodes, False)):
            total = jnp.zeros((32, 128), F32)
            for s in range(2):
                factor = pair_factors(sec, STEP_SIZE * back_matrix, mark, s)
                total = total + factor * parts[s * 32 : s * 32 + 32]
            target[25 * k : 25 * k + 25, :] = total[:25]
    mine[:HALF, :] = base[:HALF, :] + pack_nodes(own_nodes)
    mine[HALF:, :] = base[HALF:PIECE, :]
    theirs[...] = base[PIECE : PIECE + HALF, :] + pack_nodes(other_nodes)


VMEM = pl.BlockSpec(memory_space=pltpu.VMEM)
HBM = pl.BlockSpec(memory_space=pltpu.HBM)


def limit(mib):
    return pltpu.CompilerParams(vmem_limit_bytes=mib * 2**20)


def local_part(rhs, guess, kappa, flags):
    rows_t, lines_t = column_tables()
    operands = (rhs, guess, kappa, flags, jnp.asarray(rows_t), jnp.asarray(lines_t))
    return pl.pallas_call(
        local_kernel,
        out_shape=jax.ShapeDtypeStruct((288, 128), F32),
        in_specs=[HBM] * 6,
        out_specs=VMEM,
        scratch_shapes=[pltpu.VMEM(o.shape, o.dtype) for o in operands]
        + [
            pltpu.SemaphoreType.DMA((6,)),
            pltpu.VMEM((64, 160), F32),
            pltpu.VMEM((32, 160), F32),
            pltpu.VMEM((128, 160), F32),
            pltpu.VMEM((128, 128), F32),
            pltpu.VMEM((128, 128), F32),
            pltpu.VMEM((128, 128), F32),
        ],
        compiler_params=limit(60),
        name="local_part",
    )(*operands)


def halo_part(base, halos):
    return pl.pallas_call(
        halo_kernel,
        out_shape=[
            jax.ShapeDtypeStruct((PIECE, 128), F32),
            jax.ShapeDtypeStruct((HALF, 128), F32),
        ],
        in_specs=[VMEM] * 5,
        out_specs=[VMEM] * 2,
        scratch_shapes=[pltpu.VMEM((128, 160), F32)] + [pltpu.VMEM((128, 128), F32)] * 2,
        compiler_params=limit(16),
        name="halo_part",
    )(base, *halos)


class Level:
    def __init__(self, count, refs):
        self.count = count
        self.diag, self.jac, self.x, self.dir, self.res, self.f = refs
        self.tables = [element_matrix(count, d) for d in range(3)]
        self.gains = None


def tile(index):
    return pl.ds(index * 8, 8)


def rows_of(pieces, size, r, h):
    return pieces[pl.ds(8 * h * size + r, 8, stride=size), :]


def place_pieces(blocks, pieces, first, size):
    my_gx, my_gy = lax.axis_index("gx"), lax.axis_index("gy")
    for b, block in enumerate(blocks):
        for a in range(4):
            column = (my_gx ^ a) * 4 + (my_gy ^ b)
            start = pl.multiple_of(column * size, 8)
            pieces[pl.ds(start, size), :] = block[a * PIECE + first : a * PIECE + first + size, :]


def assemble_kernel(block0, block1, block2, block3, field, pieces):
    place_pieces((block0, block1, block2, block3), pieces, 0, HALF)
    odd = iota((8, 128), 1) // EZ % 2 == 1
    for r in range(HALF):
        low, high = rows_of(pieces, HALF, r, 0), rows_of(pieces, HALF, r, 1)
        field[tile(r), :] = jnp.where(odd, pltpu.roll(high, 32, 1), low)
        field[tile(HALF + r), :] = jnp.where(odd, high, pltpu.roll(low, 96, 1))


def cycle_kernel(block0, block1, block2, block3, assembled, fields, *scratch):
    sec = lax.axis_index("section")
    my_gx, my_gy = lax.axis_index("gx"), lax.axis_index("gy")
    levels = [Level(n, scratch[6 * p : 6 * p + 6]) for p, n in enumerate((5, 3, 2))]
    pieces, kap, half = scratch[18:21]
    fine, middle, coarse = levels
    fine.f = assembled
    lane = iota((8, 128), 1)
    sub = iota((8, 128), 0)
    group = lane // EZ
    odd = group % 2 == 1
    element = lane % EZ
    place = sub % 4
    low_half = sub < 4
    blocks = split_sections()[3]

    def lanes_of(upper, lower):
        return jnp.where(lane < 64, jnp.where(sec == 0, upper[0], upper[1]), jnp.where(sec == 0, lower[0], lower[1]))

    entry = [[[float(STEP_SIZE * blocks[2 * p + a, 2 * p + b]) for p in range(2)] for b in range(2)] for a in range(2)]
    same = lanes_of(entry[0][0], entry[1][1])
    swap = lanes_of(entry[0][1], entry[1][0])
    centre = (CHEB_HIGH + CHEB_LOW) / 2.0
    radius = (CHEB_HIGH - CHEB_LOW) / 2.0
    first_rho = radius / centre
    second_rho = 1.0 / (2.0 * centre / radius - first_rho)
    keep = 1.0 + second_rho * first_rho
    push = 2.0 * second_rho / radius * centre

    flags = []
    for r in range(3):
        got = assembled[tile(125 + r), :]
        across = pltpu.roll(got, 64, 1)
        flags += [jnp.where(lane < 64, got, across), jnp.where(lane < 64, across, got)]
    place_pieces((block0, block1, block2, block3), pieces, HALF, 32)
    for r in range(32):
        turned = []
        for h in range(2):
            got = rows_of(pieces, 32, r, h)
            turned.append([pltpu.roll(got, 32 * m, 1) if m else got for m in range(4)])
        for q in range(4):
            if q * 32 + r < 125:
                kap[tile(q * 32 + r), :] = choose(group, [turned[g % 2][(g - q) % 4] for g in range(4)])

    for level in levels:
        n = level.count
        picks = {5: (0, 1, 2, 3, 4), 3: (0, 2, 4), 2: (0, 4)}[n]
        level.gains = [face_gains(flags[d], d // 2, d % 2, n) for d in range(6)]
        terms = []
        for d in range(3):
            row = []
            for m in range(n):
                value = float(level.tables[d][m, m])
                if m == 0:
                    row.append(level.gains[2 * d] + value)
                elif m == n - 1:
                    row.append(level.gains[2 * d + 1] + value)
                else:
                    row.append(value)
            terms.append(row)
        for k in range(n):
            for i in range(n):
                both = terms[2][k] + terms[0][i]
                for j in range(n):
                    source = (picks[k] * 5 + picks[i]) * 5 + picks[j]
                    value = kap[tile(source), :] + (both + terms[1][j])
                    where = tile((k * n + i) * n + j)
                    level.diag[where, :] = value
                    scale = 1.0 / (1.0 + STEP_SIZE * JACOBI_SCALE * value)
                    level.jac[where, :] = scale * (1.0 / centre)

    def apply(p, source, finish, carry):
        level = levels[p]
        n = level.count
        kx, ky, kz = level.tables

        def around(u):
            turned = pltpu.roll(u, 4, 0)
            return turned, jnp.where(odd, pltpu.roll(turned, 32, 1), pltpu.roll(turned, 96, 1))

        for j in range(n):
            v = [[source[tile((k * n + i) * n + j), :] for i in range(n)] for k in range(n)]
            for k in range(n):
                left, left_far = around(v[k][n - 1])
                right, right_far = around(v[k][0])
                for i in range(n):
                    base = (k * n + i) * n
                    total = level.diag[tile(base + j), :] * v[k][i]
                    for m in range(n):
                        if m != i:
                            total = total + float(kx[i, m]) * v[k][m]
                    for m in range(n):
                        if m != k:
                            total = total + float(kz[k, m]) * v[m][i]
                    for m in range(n):
                        if m != j:
                            total = total + float(ky[j, m]) * source[tile(base + m), :]
                    if i == 0:
                        total = total - level.gains[0] * jnp.where(low_half, left_far, left)
                    if i == n - 1:
                        total = total - level.gains[1] * jnp.where(low_half, right, right_far)
                    if j == 0:
                        u = source[tile(base + n - 1), :]
                        moved = jnp.where(place == 0, pltpu.roll(u, 5, 0), pltpu.roll(u, 1, 0))
                        total = total - level.gains[2] * moved
                    if j == n - 1:
                        u = source[tile(base), :]
                        moved = jnp.where(place == 3, pltpu.roll(u, 3, 0), pltpu.roll(u, 7, 0))
                        total = total - level.gains[3] * moved
                    if k == 0:
                        u = v[n - 1][i]
                        moved = jnp.where(element == 0, pltpu.roll(u, 97, 1), pltpu.roll(u, 1, 1))
                        total = total - level.gains[4] * moved
                    if k == n - 1:
                        u = v[0][i]
                        moved = jnp.where(element == EZ - 1, pltpu.roll(u, 31, 1), pltpu.roll(u, 127, 1))
                        total = total - level.gains[5] * moved
                    out = v[k][i] + (same * total + swap * pltpu.roll(total, 64, 1))
                    carry = finish(tile(base + j), v[k][i], out, carry)
        return carry

    def smooth_first(p):
        level = levels[p]
        rows = 8 * level.count**3
        level.dir[...] = level.jac[...] * level.f[:rows, :]
        def finish(where, v, av, carry):
            level.x[where, :] = keep * v + push * level.jac[where, :] * (level.f[where, :] - av)
            return carry
        apply(p, level.dir, finish, 0)

    def defect(p):
        level = levels[p]
        def finish(where, v, av, carry):
            level.res[where, :] = level.f[where, :] - av
            return carry
        apply(p, level.x, finish, 0)

    def smooth_again(p):
        level = levels[p]
        def middle_step(where, v, av, carry):
            left = level.f[where, :] - av
            level.res[where, :] = left
            level.dir[where, :] = level.jac[where, :] * left
            return carry
        apply(p, level.x, middle_step, 0)
        def finish(where, v, av, carry):
            step = push * level.jac[where, :] * (level.res[where, :] - av)
            level.x[where, :] = level.x[where, :] + keep * v + step
            return carry
        apply(p, level.dir, finish, 0)

    def combine(weights, parts):
        total = None
        for weight, part in zip(weights, parts):
            if abs(weight) > 1e-14:
                term = part if abs(weight - 1.0) < 1e-14 else float(weight) * part
                total = term if total is None else total + term
        return total

    def change(table, source, target, add):
        m, n = table.shape
        for i in range(n):
            parts = [source[pl.ds((k * n + i) * n * 8, 8 * n), :] for k in range(n)]
            for k in range(m):
                half[pl.ds((k * n + i) * n * 8, 8 * n), :] = combine(table[k], parts)
        for k in range(m):
            parts = [half[pl.ds((k * n + i) * n * 8, 8 * n), :] for i in range(n)]
            for i in range(m):
                line = combine(table[i], parts)
                points = [line[8 * j : 8 * j + 8] for j in range(n)]
                for j in range(m):
                    value = combine(table[j], points)
                    where = tile((k * m + i) * m + j)
                    target[where, :] = target[where, :] + value if add else value

    def down(n, m):
        fine_nodes, fine_weights = lobatto(n)
        coarse_nodes, coarse_weights = lobatto(m)
        table = lagrange_table(coarse_nodes, fine_nodes)
        return (1.0 / coarse_weights)[:, None] * table.T * fine_weights[None, :]

    def up(m, n):
        return lagrange_table(lobatto(m)[0], lobatto(n)[0])

    smooth_first(0)
    defect(0)
    change(down(5, 3), fine.res, middle.f, False)
    smooth_first(1)
    defect(1)
    change(down(3, 2), middle.res, coarse.f, False)
    smooth_first(2)
    change(up(2, 3), coarse.x, middle.x, True)
    smooth_again(1)
    change(up(3, 5), middle.x, fine.x, True)
    smooth_again(0)

    def last(where, v, av, carry):
        fields[where, :] = av
        return carry
    apply(0, fine.x, last, 0)
    column = (my_gx % 2) * 4 + my_gy
    fields[FIELD : FIELD + 125, :] = fine.x[pl.ds(column, 125, stride=8), :]
    fields[FIELD + 125 : FIELD + 128, :] = jnp.zeros((3, 128), F32)


def split_dot(a, b):
    high = a.astype(jnp.bfloat16)
    rest = a - high.astype(F32)
    middle = rest.astype(jnp.bfloat16)
    low = (rest - middle.astype(F32)).astype(jnp.bfloat16)
    b = b.astype(jnp.bfloat16)
    return sum(
        lax.dot_general(part, b, (((1,), (0,)), ((), ())), preferred_element_type=F32)
        for part in (low, middle, high)
    )


def finish_kernel(own, other, own_start, other_start, guess, sol, res_out, arnoldi, cols, outs):
    sec = lax.axis_index("section")
    my_gx, my_gy = lax.axis_index("gx"), lax.axis_index("gy")
    whole, back, back_matrix, blocks, cross = split_sections()
    weights = jnp.where(iota((8, 128), 1) < 64, float(cross[0]), float(cross[1]))
    nothing = jnp.zeros((8, 128), F32)

    lane = iota((32, 128), 1)
    here = lane // EZ % 2 == my_gx // 2
    factors = []
    for s in range(2):
        row = []
        for p in range(2):
            parts = []
            for mine in range(2):
                t = whole[2 * mine + s]
                pairs = [jnp.where(lane < 64, float(t[2 * q]), float(t[2 * q + 1])) for q in range(2)]
                parts.append(pairs[mine] if p == 0 else pairs[1 - mine])
            row.append(jnp.where(here, jnp.where(sec == 0, parts[0], parts[1]), 0.0)[:25])
        factors.append(row)
    column = (my_gx % 2) * 4 + my_gy
    cols[...] = jnp.zeros_like(cols)
    total = jnp.zeros((192, 160), F32)
    for k in range(5):
        where = pl.ds(k * 200 + column, 25, stride=8)
        shown = [[ref[FIELD + k * 25 : FIELD + k * 25 + 25, :] for ref in (own, other)]]
        shown.append([ref[where, :] for ref in (own_start, other_start)])
        shown.append([ref[where, :] for ref in (own, other)])
        for f, (a, b) in enumerate(shown):
            for s in range(2):
                r = f * 64 + s * 32
                cols[r : r + 25, :] = factors[s][0] * a + factors[s][1] * b
        hit = (iota((128, 160), 1) == 5 * (iota((128, 160), 0) % EZ) + k).astype(F32)
        total = total + split_dot(cols[...], hit)

    def product(a, b, c, d):
        return (a * c + b * d) + weights * (a * d + b * c)

    uppers, sizes = [nothing] * 5, [nothing] * 5
    for r in range(125):
        a, b, c, d = (ref[tile(r), :] for ref in (own, other, own_start, other_start))
        uppers[r % 5] = uppers[r % 5] + product(a, b, c, d)
        sizes[r % 5] = sizes[r % 5] + product(c, d, c, d)
    size = jnp.sum(sum(sizes), keepdims=True)
    upper = jnp.sum(sum(uppers), keepdims=True) / size
    rests = [nothing] * 5
    for r in range(125):
        a, b, c, d = (ref[tile(r), :] for ref in (own, other, own_start, other_start))
        a, b = a - upper * c, b - upper * d
        rests[r % 5] = rests[r % 5] + product(a, b, a, b)
    rest = jnp.sum(sum(rests), keepdims=True)
    beta = jnp.sqrt(size)
    lower = jnp.sqrt(rest) / beta
    weight = upper / (upper * upper + lower * lower)
    entries = float(125 * EZ * COLS * 4)
    for place_out, value in enumerate((beta * (1.0 / math.sqrt(entries)), upper, lower)):
        arnoldi[place_out] = value[0, 0]
    outs[:64, :] = weight * total[:64]
    outs[64:, :] = total[64:128] - weight * total[128:]
    for i in range(5):
        for j in range(5):
            r = 5 * i + j
            for s in range(2):
                sol[i, j, s : s + 1, :] = guess[i, j, s : s + 1, :] + outs[s * 32 + r : s * 32 + r + 1, :]
                res_out[i, j, s : s + 1, :] = outs[64 + s * 32 + r : 64 + s * 32 + r + 1, :]


def assemble(blocks):
    return pl.pallas_call(
        assemble_kernel,
        out_shape=jax.ShapeDtypeStruct((128 * 8, 128), F32),
        in_specs=[VMEM] * 4,
        out_specs=VMEM,
        scratch_shapes=[pltpu.VMEM((COLS * HALF, 128), F32)],
        compiler_params=limit(16),
        name="assemble",
    )(*blocks)


def cycle(blocks, assembled):
    scratch = []
    for n in (5, 3, 2):
        scratch += [pltpu.VMEM((n**3 * 8, 128), F32)] * 6
    scratch += [
        pltpu.VMEM((COLS * 32, 128), F32),
        pltpu.VMEM((FIELD, 128), F32),
        pltpu.VMEM((FIELD, 128), F32),
    ]
    return pl.pallas_call(
        cycle_kernel,
        out_shape=jax.ShapeDtypeStruct((FIELD + 128, 128), F32),
        in_specs=[VMEM] * 5,
        out_specs=VMEM,
        scratch_shapes=scratch,
        compiler_params=limit(24),
        name="cycle",
    )(*blocks, assembled)


def finish(own, other, own_start, other_start, guess):
    return pl.pallas_call(
        finish_kernel,
        out_shape=[
            jax.ShapeDtypeStruct(guess.shape, F32),
            jax.ShapeDtypeStruct(guess.shape, F32),
            jax.ShapeDtypeStruct((3,), F32),
        ],
        in_specs=[VMEM] * 5,
        out_specs=[VMEM, VMEM, pl.BlockSpec(memory_space=pltpu.SMEM)],
        scratch_shapes=[pltpu.VMEM((192, 128), F32), pltpu.VMEM((128, 160), F32)],
        compiler_params=limit(24),
        name="finish",
    )(own, other, own_start, other_start, guess)


def exchange(x, axis, bits):
    return lax.ppermute(x, axis, [(n, n ^ bits) for n in range(lax.axis_size(axis))])


def gathered_body(rhs, guess, kappa, bc_flags):
    rhs, guess = (jnp.transpose(v, (1, 2, 0, 3)) for v in (rhs, guess))
    halos = [exchange(guess, axis, bits) for axis in ("gx", "gy") for bits in (1, 3)]
    base = local_part(rhs, guess, kappa, bc_flags)
    mine, theirs = halo_part(base, halos)
    got = exchange(theirs, "section", 1)
    piece = jnp.concatenate([mine[:HALF] + got, mine[HALF:]])
    line = jnp.concatenate([piece] + [exchange(piece, "gx", bits) for bits in (1, 2, 3)])
    blocks = [line] + [exchange(line, "gy", bits) for bits in (1, 2, 3)]
    start = assemble(blocks)
    other_start = exchange(start, "section", 1)
    own = cycle(blocks, start)
    sol, res, arnoldi = finish(own, exchange(own, "section", 1), start, other_start, guess)
    sol, res = (jnp.transpose(v, (2, 0, 1, 3)) for v in (sol, res))
    return sol, res, arnoldi


def solution(mesh):
    placed = (
        P("section", "gx", "gy", None),
        P("section", "gx", "gy", None),
        P("gx", "gy", None),
        P(None, "gx", "gy", None),
    )
    sizes = (mesh.shape["section"], mesh.shape["gx"], mesh.shape["gy"])

    def step(rhs, guess, kappa, bc_flags):
        fits = sizes == (2, 4, 4) and rhs.shape == (4, 20, 20, 160)
        return jax.shard_map(
            gathered_body if fits else stepwise,
            mesh=mesh,
            in_specs=placed,
            out_specs=(P("section", "gx", "gy", None), P("section", "gx", "gy", None), P()),
            check_vma=False,
        )(rhs, guess, kappa, bc_flags)

    return step
```

```python
from functools import partial
import math

import jax
import jax.numpy as jnp
import numpy as np
from jax import lax
from jax.experimental import pallas as pl
from jax.experimental.pallas import tpu as pltpu
from jax.sharding import PartitionSpec as P

ADVECT = (1.0, 0.7, 0.5)
DIFFUSE = 0.05
STEP_SIZE = 0.2
JACOBI_SCALE = 0.25
CHEB_LOW = 0.25
CHEB_HIGH = 2.0
LETTERS = "abcdef"


def extended(x, sides, width):
    for axis, dim in sides:
        peers, length = (lax.axis_size(axis), x.shape[dim])
        up = [(i, (i + 1) % peers) for i in range(peers)]
        down = [(j, i) for i, j in up]
        last = lax.slice_in_dim(x, length - width, length, axis=dim)
        leading = lax.slice_in_dim(x, 0, width, axis=dim)
        before = lax.ppermute(last, axis, up)
        after = lax.ppermute(leading, axis, down)
        x = jnp.concatenate([before, x, after], axis=dim)
    return x


def lobatto(count):
    if count == 5:
        inner = math.sqrt(3.0 / 7.0)
        return (
            np.array([-1.0, -inner, 0.0, inner, 1.0]),
            np.array([0.1, 49.0 / 90.0, 32.0 / 45.0, 49.0 / 90.0, 0.1]),
        )
    if count == 3:
        return (np.array([-1.0, 0.0, 1.0]), np.array([1.0 / 3.0, 4.0 / 3.0, 1.0 / 3.0]))
    return (np.array([-1.0, 1.0]), np.array([1.0, 1.0]))


def lagrange_table(nodes, points):
    table = np.ones((len(points), len(nodes)))
    for column in range(len(nodes)):
        for other in range(len(nodes)):
            if other != column:
                table[:, column] *= (points - nodes[other]) / (nodes[column] - nodes[other])
    return table


def slope_table(nodes):
    total = len(nodes)
    factor = np.array(
        [np.prod([nodes[i] - nodes[k] for k in range(total) if k != i]) for i in range(total)]
    )
    table = np.zeros((total, total))
    for row in range(total):
        for column in range(total):
            if row != column:
                table[row, column] = factor[row] / factor[column] / (nodes[row] - nodes[column])
        table[row, row] = -np.sum(table[row])
    return table


def element_matrix(count, direction):
    nodes, weights = lobatto(count)
    slopes = slope_table(nodes)
    stiffness = (1.0 / weights)[:, None] * (slopes.T @ (weights[:, None] * slopes))
    return ADVECT[direction] * slopes + DIFFUSE * stiffness


def legendre_pair(point, order):
    values = [1.0, point]
    slopes = [0.0, 1.0]
    for index in range(1, order):
        values.append(
            ((2 * index + 1) * point * values[index] - index * values[index - 1]) / (index + 1)
        )
        slopes.append(slopes[index - 1] + (2 * index + 1) * values[index])
    return (values, slopes)


def radau_nodes():
    starts = [0.0885879595127039, 0.4094668644407347, 0.7876594617608471]
    found = []
    for start in starts:
        point = start
        for sweep in range(30):
            values, slopes = legendre_pair(2.0 * point - 1.0, 4)
            change = (values[4] - values[3]) / (2.0 * (slopes[4] - slopes[3]))
            point = point - change
        found.append(point)
    found.append(1.0)
    return found


def poly_times(coefs, root):
    result = [0.0] * (len(coefs) + 1)
    for index in range(len(coefs)):
        result[index + 1] += coefs[index]
        result[index] -= root * coefs[index]
    return result


def radau_matrix():
    order = 4
    nodes = radau_nodes()
    matrix = np.zeros((order, order))
    for column in range(order):
        coefs = [1.0]
        denominator = 1.0
        for other in range(order):
            if other != column:
                coefs = poly_times(coefs, nodes[other])
                denominator *= nodes[column] - nodes[other]
        for row in range(order):
            upper_end = nodes[row]
            integral = 0.0
            for index in range(len(coefs)):
                integral += coefs[index] * upper_end ** (index + 1) / (index + 1)
            matrix[row, column] = integral / denominator
    return matrix


def node_einsum(table, field, axis):
    labels = LETTERS[: field.ndim]
    source = labels[: axis + 1] + "j" + labels[axis + 2 :]
    target = labels[: axis + 1] + "i" + labels[axis + 2 :]
    return jnp.einsum(
        "ij," + source + "->" + target,
        jnp.asarray(table, jnp.float32),
        field,
        precision=lax.Precision.HIGHEST,
    )


def apply_along(field, axis, count, table):
    shape = field.shape
    split = shape[:axis] + (shape[axis] // count, count) + shape[axis + 1 :]
    mapped = node_einsum(table, field.reshape(split), axis)
    return mapped.reshape(
        shape[:axis] + (mapped.shape[axis] * mapped.shape[axis + 1],) + shape[axis + 1 :]
    )


def line_part(field, axis, count, table, left_gain, right_gain, left_edge, right_edge):
    shape = field.shape
    elements = shape[axis] // count
    split = field.reshape(shape[:axis] + (elements, count) + shape[axis + 1 :])
    linear = node_einsum(table, split, axis)
    first = lax.index_in_dim(split, 0, axis + 1, keepdims=False)
    last = lax.index_in_dim(split, count - 1, axis + 1, keepdims=False)
    before = jnp.concatenate(
        [jnp.expand_dims(left_edge, axis), lax.slice_in_dim(last, 0, elements - 1, axis=axis)], axis
    )
    after = jnp.concatenate(
        [lax.slice_in_dim(first, 1, elements, axis=axis), jnp.expand_dims(right_edge, axis)], axis
    )
    front = jnp.expand_dims(left_gain * (first - before), axis + 1)
    back = jnp.expand_dims(right_gain * (last - after), axis + 1)
    if count > 2:
        middle_shape = list(front.shape)
        middle_shape[axis + 1] = count - 2
        pieces = [front, jnp.zeros(middle_shape, jnp.float32), back]
    else:
        pieces = [front, back]
    return (linear + jnp.concatenate(pieces, axis + 1)).reshape(shape)


def diag_along(shape, axis, count, table, left_gain, right_gain):
    elements = shape[axis] // count
    split = shape[:axis] + (elements, count) + shape[axis + 1 :]
    profile = [1] * len(split)
    profile[axis + 1] = count
    diagonal_entries = np.array([table[index, index] for index in range(count)])
    base = jnp.broadcast_to(jnp.asarray(diagonal_entries, jnp.float32).reshape(profile), split)
    front = jnp.expand_dims(left_gain, axis + 1)
    back = jnp.expand_dims(right_gain, axis + 1)
    if count > 2:
        middle_shape = list(front.shape)
        middle_shape[axis + 1] = count - 2
        pieces = [front, jnp.zeros(middle_shape, jnp.float32), back]
    else:
        pieces = [front, back]
    return (base + jnp.concatenate(pieces, axis + 1)).reshape(shape)


def level_kappa(kappa, count):
    if count == 5:
        return kappa
    picks = np.array([0, 2, 4]) if count == 3 else np.array([0, 4])
    extents = [extent // 5 for extent in kappa.shape]
    grouped = kappa.reshape(extents[0], 5, extents[1], 5, extents[2], 5)
    for axis in (1, 3, 5):
        grouped = jnp.take(grouped, picks, axis=axis)
    return grouped.reshape(extents[0] * count, extents[1] * count, extents[2] * count)


def face_plane(face, direction, count):
    plane = face.astype(jnp.float32)
    for axis in range(3):
        if axis != direction:
            plane = jnp.repeat(plane, count, axis=axis)
    return plane


def build_level(kappa, flags, count):
    nodes, weights = lobatto(count)
    kappa_level = level_kappa(kappa, count)
    tables, lefts, rights = ([], [], [])
    diagonal = kappa_level
    for direction in range(3):
        table = element_matrix(count, direction)
        lower = face_plane(flags[2 * direction], direction, count)
        upper = face_plane(flags[2 * direction + 1], direction, count)
        left_gain = (ADVECT[direction] * (1.0 + lower) / 2.0 + DIFFUSE * count * count) / float(
            weights[0]
        )
        right_gain = (DIFFUSE * count * count - ADVECT[direction] * (1.0 - upper) / 2.0) / float(
            weights[-1]
        )
        tables.append(table)
        lefts.append(left_gain)
        rights.append(right_gain)
        diagonal = diagonal + diag_along(
            kappa_level.shape, direction, count, table, left_gain, right_gain
        )
    scale = 1.0 / (1.0 + STEP_SIZE * JACOBI_SCALE * diagonal)
    return (count, tables, lefts, rights, kappa_level, scale)


def restrict(field, fine_count, coarse_count):
    fine_nodes, fine_weights = lobatto(fine_count)
    coarse_nodes, coarse_weights = lobatto(coarse_count)
    table = (
        (1.0 / coarse_weights)[:, None]
        * lagrange_table(coarse_nodes, fine_nodes).T
        * fine_weights[None, :]
    )
    for axis in range(field.ndim - 3, field.ndim):
        field = apply_along(field, axis, fine_count, table)
    return field


def prolong(field, coarse_count, fine_count):
    fine_nodes, fine_weights = lobatto(fine_count)
    coarse_nodes, coarse_weights = lobatto(coarse_count)
    table = lagrange_table(coarse_nodes, fine_nodes)
    for axis in range(field.ndim - 3, field.ndim):
        field = apply_along(field, axis, coarse_count, table)
    return field


def chebyshev(rhs, start, level, operator):
    centre = (CHEB_HIGH + CHEB_LOW) / 2.0
    radius = (CHEB_HIGH - CHEB_LOW) / 2.0
    ratio = centre / radius
    first_rho = 1.0 / ratio
    second_rho = 1.0 / (2.0 * ratio - first_rho)
    scale = level[5]
    if start is None:
        remain = rhs
    else:
        remain = rhs - operator(start, level)
    step = scale * remain / centre
    guess = step if start is None else start + step
    remain = remain - operator(step, level)
    step = second_rho * first_rho * step + 2.0 * second_rho / radius * scale * remain
    return guess + step


def vcycle(rhs, levels, operator):
    fine, middle, coarse = levels
    fine_x = chebyshev(rhs, None, fine, operator)
    middle_rhs = restrict(rhs - operator(fine_x, fine), 5, 3)
    middle_x = chebyshev(middle_rhs, None, middle, operator)
    coarse_rhs = restrict(middle_rhs - operator(middle_x, middle), 3, 2)
    coarse_x = chebyshev(coarse_rhs, None, coarse, operator)
    middle_x = chebyshev(middle_rhs, middle_x + prolong(coarse_x, 2, 3), middle, operator)
    return chebyshev(rhs, fine_x + prolong(middle_x, 3, 5), fine, operator)


def spatial(field, level):
    count, tables, lefts, rights, kappa_level, scale = level
    padded = extended(field, (("gx", 1), ("gy", 2)), 1)
    total = kappa_level * field
    total = total + line_part(
        field,
        1,
        count,
        tables[0],
        lefts[0],
        rights[0],
        padded[:, 0, 1:-1, :],
        padded[:, -1, 1:-1, :],
    )
    total = total + line_part(
        field,
        2,
        count,
        tables[1],
        lefts[1],
        rights[1],
        padded[:, 1:-1, 0, :],
        padded[:, 1:-1, -1, :],
    )
    total = total + line_part(
        field, 3, count, tables[2], lefts[2], rights[2], field[:, :, :, -1], field[:, :, :, 0]
    )
    return total


def apply_system(field, level, coupling):
    image = spatial(field, level)
    everyone = lax.all_gather(image, "section", axis=0, tiled=True)
    butcher = jnp.asarray(radau_matrix(), jnp.float32)
    rows = lax.dynamic_slice_in_dim(
        butcher, lax.axis_index("section") * field.shape[0], field.shape[0], 0
    )
    mixed = jnp.einsum("ij,jabc->iabc", rows, everyone, precision=lax.Precision.HIGHEST)
    return field + STEP_SIZE * mixed


def global_total(values):
    return lax.psum(values, ("section", "gx", "gy"))


def stepwise(rhs, guess, kappa, bc_flags):
    levels = [build_level(kappa, bc_flags, count) for count in (5, 3, 2)]
    section_operator = partial(apply_system, coupling=None)
    start_residual = rhs - section_operator(guess, levels[0])
    dofs = float(rhs.size * lax.axis_size("section") * lax.axis_size("gx") * lax.axis_size("gy"))
    beta = jnp.sqrt(global_total(jnp.sum(start_residual * start_residual).reshape(1))[0])
    basis = start_residual / beta
    precond = vcycle(basis, levels, section_operator)
    image = section_operator(precond, levels[0])
    upper = global_total(jnp.sum(image * basis).reshape(1))[0]
    remainder = image - upper * basis
    lower = jnp.sqrt(global_total(jnp.sum(remainder * remainder).reshape(1))[0])
    weight = beta * upper / (upper * upper + lower * lower)
    solution = guess + weight * precond
    residual = start_residual - weight * image
    arnoldi = jnp.stack([beta / math.sqrt(dofs), upper, lower]).astype(jnp.float32)
    return (solution, residual, arnoldi)


EZ = 32
COLS = 16
HALF = 64
PIECE = 96
FIELD = 1000
F32 = jnp.float32


def split_sections():
    matrix = radau_matrix()
    values, vectors = np.linalg.eig(matrix)
    order = [n for n in np.argsort(np.abs(values.imag), kind="stable") if values[n].imag > 0]
    bases = []
    for n in order:
        plane = np.stack([vectors[:, n].real, vectors[:, n].imag], axis=1)
        bases.append(np.linalg.qr(plane)[0])
    left, cross, right = np.linalg.svd(bases[0].T @ bases[1])
    bases = [bases[0] @ left, bases[1] @ right.T]
    for c in range(2):
        sign = np.sign(bases[0][np.argmax(np.abs(bases[0][:, c])), c])
        bases = [np.concatenate([b[:, :c], sign * b[:, c : c + 1], b[:, c + 1 :]], axis=1) for b in bases]
    whole = np.concatenate(bases, axis=1)
    back = np.linalg.inv(whole)
    return whole, back, back @ matrix, back @ matrix @ whole, cross


def iota(shape, dim):
    return lax.broadcasted_iota(jnp.int32, shape, dim)


def exact_dot(a, b):
    return lax.dot_general(
        a, b, (((1,), (0,)), ((), ())), precision=lax.Precision.HIGHEST, preferred_element_type=F32
    )


def choose(index, values):
    out = values[-1]
    for place in range(len(values) - 2, -1, -1):
        out = jnp.where(index == place, values[place], out)
    return out


def face_gains(flag, direction, side, count):
    nodes, weights = lobatto(count)
    c, nu = ADVECT[direction], DIFFUSE * count * count
    if side == 0:
        return (c * (1.0 + flag) / 2.0 + nu) * (1.0 / float(weights[0]))
    return (nu - c * (1.0 - flag) / 2.0) * (1.0 / float(weights[-1]))


def column_tables():
    kx, ky, kz = (element_matrix(5, d) for d in range(3))
    rows = np.zeros((64, 64))
    for s in range(2):
        for i in range(5):
            for j in range(5):
                r = s * 32 + i * 5 + j
                for m in range(5):
                    rows[r, s * 32 + m * 5 + j] += kx[i, m]
                    rows[r, s * 32 + i * 5 + m] += ky[j, m]
    lines = np.zeros((160, 320))
    for e in range(EZ):
        lines[e * 5 : e * 5 + 5, e * 5 : e * 5 + 5] = kz.T
        lines[(e - 1) % EZ * 5 + 4, 160 + e * 5] = 1.0
        lines[(e + 1) % EZ * 5, 160 + e * 5 + 4] = 1.0
    return rows.astype(np.float32), lines.astype(np.float32)


def pick_line(k):
    return (iota((160, 128), 0) == 5 * (iota((160, 128), 1) % EZ) + k).astype(F32)


def pair_factors(sec, table, own, s):
    upper = iota((32, 128), 1) < 64
    first = jnp.where(upper, float(table[0, s]), float(table[1, s]))
    second = jnp.where(upper, float(table[2, 2 + s]), float(table[3, 2 + s]))
    if not own:
        first = jnp.where(upper, float(table[2, s]), float(table[3, s]))
        second = jnp.where(upper, float(table[0, 2 + s]), float(table[1, 2 + s]))
    return jnp.where(sec == 0, first, second)


def pack_nodes(nodes):
    odd = iota((HALF, 128), 1) // EZ % 2 == 1
    return jnp.where(odd, nodes[HALF:, :], nodes[:HALF, :])


def fetch(pairs, sems):
    copies = [pltpu.make_async_copy(src, dst, sems.at[n]) for n, (src, dst) in enumerate(pairs)]
    for copy in copies:
        copy.start()
    for copy in copies:
        copy.wait()


def local_kernel(
    rhs_in, guess_in, kappa_in, flags_in, rows_in, lines_in, base,
    rhs, guess, kappa, flags, rows_t, lines_t, sems, x, kap, stack, own_nodes, other_nodes, krep,
):
    sec = lax.axis_index("section")
    fetch(
        [(rhs_in, rhs), (guess_in, guess), (kappa_in, kappa), (flags_in, flags), (rows_in, rows_t), (lines_in, lines_t)],
        sems,
    )
    x[...] = jnp.zeros_like(x)
    kap[...] = jnp.zeros_like(kap)
    stack[...] = jnp.zeros_like(stack)
    for i in range(5):
        kap[5 * i : 5 * i + 5, :] = kappa[i]
        for j in range(5):
            r = 5 * i + j
            value = guess[i, j]
            left = rhs[i, j] - value
            for s in range(2):
                x[s * 32 + r : s * 32 + r + 1, :] = value[s : s + 1]
                stack[s * 32 + r : s * 32 + r + 1, :] = left[s : s + 1]
    flag = flags[:, 0, 0, :].astype(F32)
    spread = (iota((EZ, 160), 1) // 5 == iota((EZ, 160), 0)).astype(F32)
    wide = exact_dot(flag, spread)
    gains = [face_gains(wide[d : d + 1, :], d // 2, d % 2, 5) for d in range(6)]
    row = iota((32, 160), 0)
    lane = iota((32, 160), 1) % 5
    none = jnp.zeros((32, 160), F32)
    gx = jnp.where(row < 5, gains[0], jnp.where((row >= 20) & (row < 25), gains[1], none))
    gy = jnp.where(row % 5 == 0, gains[2], jnp.where(row % 5 == 4, gains[3], none))
    gz = jnp.where(lane == 0, gains[4], jnp.where(lane == 4, gains[5], none))
    gy = jnp.where(row < 25, gy, none)
    for place, gain in ((160, gx), (192, gy)):
        base[place : place + 32, :] = gain[:, :128]
        base[64 + place : 96 + place, :EZ] = gain[:, 128:]
    field = x[...]
    along = exact_dot(rows_t[...], field)
    across = exact_dot(field, lines_t[...])
    own = kap[...] + gx + gy + gz
    for s in range(2):
        r = slice(s * 32, s * 32 + 32)
        image = own * field[r] + along[r] + across[r, :160] - gz * across[r, 160:]
        stack[64 + s * 32 : 96 + s * 32, :] = image
    whole, back, back_matrix, blocks, cross = split_sections()
    own_nodes[...] = jnp.zeros_like(own_nodes)
    other_nodes[...] = jnp.zeros_like(other_nodes)
    krep[...] = jnp.zeros_like(krep)
    source = stack[...]
    coefs = kap[...]
    for k in range(5):
        pick = pick_line(k)
        parts = exact_dot(source, pick)
        for target, mark in ((own_nodes, True), (other_nodes, False)):
            total = jnp.zeros((32, 128), F32)
            for s in range(2):
                total = total + pair_factors(sec, back, mark, s) * parts[s * 32 : s * 32 + 32]
                factor = pair_factors(sec, -STEP_SIZE * back_matrix, mark, s)
                total = total + factor * parts[64 + s * 32 : 96 + s * 32]
            target[25 * k : 25 * k + 25, :] = total[:25]
        krep[25 * k : 25 * k + 25, :] = exact_dot(coefs, pick)[:25]
    repeat = (iota((EZ, 128), 1) % EZ == iota((EZ, 128), 0)).astype(F32)
    shown = exact_dot(flag, repeat)
    upper = iota((1, 128), 1) < 64
    for r in range(3):
        own_nodes[125 + r : 126 + r, :] = jnp.where(upper, shown[2 * r : 2 * r + 1], shown[2 * r + 1 : 2 * r + 2])
    base[:HALF, :] = pack_nodes(own_nodes)
    base[PIECE : PIECE + HALF, :] = pack_nodes(other_nodes)
    base[HALF:PIECE, :] = choose(iota((32, 128), 1) // EZ, [krep[32 * q : 32 * q + 32, :] for q in range(4)])


def halo_kernel(base, x1, x3, y1, y3, mine, theirs, near, own_nodes, other_nodes):
    sec = lax.axis_index("section")
    even_x = lax.axis_index("gx") % 2 == 0
    even_y = lax.axis_index("gy") % 2 == 0
    for ref in (near, own_nodes, other_nodes):
        ref[...] = jnp.zeros_like(ref)
    for m in range(5):
        for s in range(2):
            r = s * 32
            one = slice(s, s + 1)
            near[r + m : r + m + 1, :] = jnp.where(even_x, x3[4, m, one, :], x1[4, m, one, :])
            near[r + 20 + m : r + 21 + m, :] = jnp.where(even_x, x1[0, m, one, :], x3[0, m, one, :])
            r += 64
            near[r + 5 * m : r + 5 * m + 1, :] = jnp.where(even_y, y3[m, 4, one, :], y1[m, 4, one, :])
            near[r + 5 * m + 4 : r + 5 * m + 5, :] = jnp.where(even_y, y1[m, 0, one, :], y3[m, 0, one, :])
    gx, gy = (
        jnp.concatenate([base[r : r + 32, :], base[64 + r : 96 + r, :EZ]], axis=1) for r in (160, 192)
    )
    parts_in = []
    for s in range(2):
        r = s * 32
        parts_in.append(gx * near[r : r + 32, :] + gy * near[64 + r : 96 + r, :])
    source = jnp.concatenate(parts_in, axis=0)
    back_matrix = split_sections()[2]
    for k in range(5):
        parts = exact_dot(source, pick_line(k))
        for target, mark in ((own_nodes, True), (other_nodes, False)):
            total = jnp.zeros((32, 128), F32)
            for s in range(2):
                factor = pair_factors(sec, STEP_SIZE * back_matrix, mark, s)
                total = total + factor * parts[s * 32 : s * 32 + 32]
            target[25 * k : 25 * k + 25, :] = total[:25]
    mine[:HALF, :] = base[:HALF, :] + pack_nodes(own_nodes)
    mine[HALF:, :] = base[HALF:PIECE, :]
    theirs[...] = base[PIECE : PIECE + HALF, :] + pack_nodes(other_nodes)


VMEM = pl.BlockSpec(memory_space=pltpu.VMEM)
HBM = pl.BlockSpec(memory_space=pltpu.HBM)


def limit(mib):
    return pltpu.CompilerParams(vmem_limit_bytes=mib * 2**20)


def local_part(rhs, guess, kappa, flags):
    rows_t, lines_t = column_tables()
    operands = (rhs, guess, kappa, flags, jnp.asarray(rows_t), jnp.asarray(lines_t))
    return pl.pallas_call(
        local_kernel,
        out_shape=jax.ShapeDtypeStruct((288, 128), F32),
        in_specs=[HBM] * 6,
        out_specs=VMEM,
        scratch_shapes=[pltpu.VMEM(o.shape, o.dtype) for o in operands]
        + [
            pltpu.SemaphoreType.DMA((6,)),
            pltpu.VMEM((64, 160), F32),
            pltpu.VMEM((32, 160), F32),
            pltpu.VMEM((128, 160), F32),
            pltpu.VMEM((128, 128), F32),
            pltpu.VMEM((128, 128), F32),
            pltpu.VMEM((128, 128), F32),
        ],
        compiler_params=limit(60),
        name="local_part",
    )(*operands)


def halo_part(base, halos):
    return pl.pallas_call(
        halo_kernel,
        out_shape=[
            jax.ShapeDtypeStruct((PIECE, 128), F32),
            jax.ShapeDtypeStruct((HALF, 128), F32),
        ],
        in_specs=[VMEM] * 5,
        out_specs=[VMEM] * 2,
        scratch_shapes=[pltpu.VMEM((128, 160), F32)] + [pltpu.VMEM((128, 128), F32)] * 2,
        compiler_params=limit(16),
        name="halo_part",
    )(base, *halos)


class Level:
    def __init__(self, count, refs):
        self.count = count
        self.size = 8 * count**3
        self.diag, self.jac, self.held, self.edge = refs
        self.tables = [element_matrix(count, d) for d in range(3)]
        self.gains = None


def tile(index):
    return pl.ds(index * 8, 8)


def rows_of(pieces, size, r, h):
    return pieces[pl.ds(8 * h * size + r, 8, stride=size), :]


def place_pieces(blocks, pieces, first, size):
    my_gx, my_gy = lax.axis_index("gx"), lax.axis_index("gy")
    for b, block in enumerate(blocks):
        for a in range(4):
            column = (my_gx ^ a) * 4 + (my_gy ^ b)
            start = pl.multiple_of(column * size, 8)
            pieces[pl.ds(start, size), :] = block[a * PIECE + first : a * PIECE + first + size, :]


def assemble_kernel(block0, block1, block2, block3, field, pieces):
    place_pieces((block0, block1, block2, block3), pieces, 0, HALF)
    odd = iota((8, 128), 1) // EZ % 2 == 1
    for r in range(HALF):
        low, high = rows_of(pieces, HALF, r, 0), rows_of(pieces, HALF, r, 1)
        field[tile(r), :] = jnp.where(odd, pltpu.roll(high, 32, 1), low)
        field[tile(HALF + r), :] = jnp.where(odd, high, pltpu.roll(low, 96, 1))


def at(offset, static):
    return pl.ds(pl.multiple_of(offset, 8) + static, 8)


def cycle_kernel(block0, block1, block2, block3, assembled, fields, *scratch):
    sec = lax.axis_index("section")
    my_gx, my_gy = lax.axis_index("gx"), lax.axis_index("gy")
    levels = [Level(n, scratch[4 * p : 4 * p + 4]) for p, n in enumerate((5, 3, 2))]
    pieces, kap, half, terms = scratch[12:16]
    lane = iota((8, 128), 1)
    sub = iota((8, 128), 0)
    group = lane // EZ
    odd = group % 2 == 1
    element = lane % EZ
    place = sub % 4
    low_half = sub < 4
    blocks = split_sections()[3]

    def lanes_of(upper, lower):
        return jnp.where(lane < 64, jnp.where(sec == 0, upper[0], upper[1]), jnp.where(sec == 0, lower[0], lower[1]))

    entry = [[[float(STEP_SIZE * blocks[2 * p + a, 2 * p + b]) for p in range(2)] for b in range(2)] for a in range(2)]
    same = lanes_of(entry[0][0], entry[1][1])
    swap = lanes_of(entry[0][1], entry[1][0])
    centre = (CHEB_HIGH + CHEB_LOW) / 2.0
    radius = (CHEB_HIGH - CHEB_LOW) / 2.0
    first_rho = radius / centre
    second_rho = 1.0 / (2.0 * centre / radius - first_rho)
    keep = 1.0 + second_rho * first_rho
    push = 2.0 * second_rho / radius * centre

    flags = []
    for r in range(3):
        got = assembled[tile(125 + r), :]
        across = pltpu.roll(got, 64, 1)
        flags += [jnp.where(lane < 64, got, across), jnp.where(lane < 64, across, got)]
    place_pieces((block0, block1, block2, block3), pieces, HALF, 32)

    def place_kappa(r, carry):
        turned = []
        for h in range(2):
            got = rows_of(pieces, 32, r, h)
            turned.append([pltpu.roll(got, 32 * m, 1) if m else got for m in range(4)])
        for q in range(4):
            kap[at(r * 8, q * 256), :] = choose(group, [turned[g % 2][(g - q) % 4] for g in range(4)])
        return carry
    lax.fori_loop(0, 32, place_kappa, 0, unroll=2)

    for level in levels:
        n = level.count
        stride = 4 // (n - 1)
        level.gains = [face_gains(flags[d], d // 2, d % 2, n) for d in range(6)]
        for d in range(3):
            for m in range(n):
                value = jnp.full((8, 128), float(level.tables[d][m, m]), F32)
                if m == 0:
                    value = value + level.gains[2 * d]
                if m == n - 1:
                    value = value + level.gains[2 * d + 1]
                terms[tile(5 * d + m), :] = value

        def diagonals(r, carry, level=level, n=n, stride=stride):
            k = r // n
            i = r - k * n
            both = terms[at(i * 8, 0), :] + terms[at(k * 8, 80), :]
            for j in range(n):
                source = at((k * 25 + i * 5) * 8 * stride, j * stride * 8)
                value = kap[source, :] + (both + terms[tile(5 + j), :])
                level.diag[at(r * n * 8, j * 8), :] = value
                scale = 1.0 / (1.0 + STEP_SIZE * JACOBI_SCALE * value)
                level.jac[at(r * n * 8, j * 8), :] = scale * (1.0 / centre)
            return carry
        lax.fori_loop(0, n * n, diagonals, 0)
        level.edge[...] = jnp.zeros_like(level.edge)

    def begin(level, source):
        n = level.count

        def start(r, carry):
            for j in range(n):
                where = at(r * n * 8, j * 8)
                f = source[where, :]
                level.held[where, :] = f
                level.held[at(r * n * 8, level.size + j * 8), :] = f
                level.held[at(r * n * 8, 2 * level.size + j * 8), :] = jnp.zeros_like(f)
                level.held[at(r * n * 8, 3 * level.size + j * 8), :] = level.jac[where, :] * f
            return carry
        lax.fori_loop(0, n * n, start, 0)

    def apply(level, smooth):
        n, size, held = level.count, level.size, level.held
        kx, ky, kz = level.tables
        source = jnp.where(smooth, 3 * size, 2 * size)
        right_side = jnp.where(smooth, size, 0)
        first_out = jnp.where(smooth, 2 * size, size)
        second_out = jnp.where(smooth, 4 * size, 3 * size)

        def faces(r, carry):
            v = held[at(source + r * n * 8, (n - 1) * 8), :]
            moved = jnp.where(place == 0, pltpu.roll(v, 5, 0), pltpu.roll(v, 1, 0))
            level.edge[at(r * n * 8, 0), :] = level.gains[2] * moved
            v = held[at(source + r * n * 8, 0), :]
            moved = jnp.where(place == 3, pltpu.roll(v, 3, 0), pltpu.roll(v, 7, 0))
            level.edge[at(r * n * 8, (n - 1) * 8), :] = level.gains[3] * moved
            return carry
        lax.fori_loop(0, n * n, faces, 0, unroll=n)

        def around(u):
            turned = pltpu.roll(u, 4, 0)
            return turned, jnp.where(odd, pltpu.roll(turned, 32, 1), pltpu.roll(turned, 96, 1))

        def plane(j, carry):
            sides = []
            for m in range(1, n):
                coef = choose(j, [float(ky[a, (a + m) % n]) for a in range(n)])
                far = jnp.where(j + m >= n, j + m - n, j + m)
                sides.append((coef, source + far * 8))
            here = source + j * 8
            v = [[held[at(here, (k * n + i) * n * 8), :] for i in range(n)] for k in range(n)]
            for k in range(n):
                left, left_far = around(v[k][n - 1])
                right, right_far = around(v[k][0])
                for i in range(n):
                    base = (k * n + i) * n * 8
                    total = level.diag[at(j * 8, base), :] * v[k][i] - level.edge[at(j * 8, base), :]
                    for m in range(n):
                        if m != i:
                            total = total + float(kx[i, m]) * v[k][m]
                    for m in range(n):
                        if m != k:
                            total = total + float(kz[k, m]) * v[m][i]
                    for coef, far in sides:
                        total = total + coef * held[at(far, base), :]
                    if i == 0:
                        total = total - level.gains[0] * jnp.where(low_half, left_far, left)
                    if i == n - 1:
                        total = total - level.gains[1] * jnp.where(low_half, right, right_far)
                    if k == 0:
                        u = v[n - 1][i]
                        moved = jnp.where(element == 0, pltpu.roll(u, 97, 1), pltpu.roll(u, 1, 1))
                        total = total - level.gains[4] * moved
                    if k == n - 1:
                        u = v[0][i]
                        moved = jnp.where(element == EZ - 1, pltpu.roll(u, 31, 1), pltpu.roll(u, 127, 1))
                        total = total - level.gains[5] * moved
                    image = v[k][i] + (same * total + swap * pltpu.roll(total, 64, 1))
                    left_over = held[at(right_side + j * 8, base), :] - image
                    scaled = level.jac[at(j * 8, base), :] * left_over
                    x = held[at(j * 8, 2 * size + base), :]
                    first = jnp.where(smooth, x + keep * v[k][i] + push * scaled, left_over)
                    held[at(first_out + j * 8, base), :] = first
                    held[at(second_out + j * 8, base), :] = scaled
            return carry
        lax.fori_loop(0, n, plane, 0)

    def combine(weights, parts):
        total = None
        for weight, part in zip(weights, parts):
            if abs(weight) > 1e-14:
                term = part if abs(weight - 1.0) < 1e-14 else float(weight) * part
                total = term if total is None else total + term
        return total

    def change(table, source, source_base, target, target_base, add):
        m, n = table.shape

        def outer(i, carry):
            parts = [
                source[pl.ds(pl.multiple_of(i * n * 8, 8) + source_base + k * n * n * 8, 8 * n), :] for k in range(n)
            ]
            for k in range(m):
                half[pl.ds(pl.multiple_of(i * n * 8, 8) + k * n * n * 8, 8 * n), :] = combine(table[k], parts)
            return carry
        lax.fori_loop(0, n, outer, 0)

        def inner(k, carry):
            parts = [half[pl.ds(pl.multiple_of(k * n * n * 8, 8) + i * n * 8, 8 * n), :] for i in range(n)]
            for i in range(m):
                line = combine(table[i], parts)
                points = [line[8 * j : 8 * j + 8] for j in range(n)]
                for j in range(m):
                    value = combine(table[j], points)
                    where = at(k * m * m * 8, target_base + (i * m + j) * 8)
                    target[where, :] = target[where, :] + value if add else value
            return carry
        lax.fori_loop(0, m, inner, 0)

    def down(n, m):
        fine_nodes, fine_weights = lobatto(n)
        coarse_nodes, coarse_weights = lobatto(m)
        table = lagrange_table(coarse_nodes, fine_nodes)
        return (1.0 / coarse_weights)[:, None] * table.T * fine_weights[None, :]

    def up(m, n):
        return lagrange_table(lobatto(m)[0], lobatto(n)[0])

    def solve(p):
        level = levels[p]
        if p == 2:
            apply(level, True)
            return
        below = levels[p + 1]

        def step(t, carry):
            apply(level, (t == 0) | (t == 3))

            @pl.when(t == 1)
            def _():
                n, m = level.count, below.count
                change(down(n, m), level.held, level.size, below.held, 0, False)
                begin(below, below.held)
                solve(p + 1)
                change(up(m, n), below.held, 2 * below.size, level.held, 2 * level.size, True)
            return carry
        lax.fori_loop(0, 5 if p == 0 else 4, step, 0)

    begin(levels[0], assembled)
    solve(0)
    fine = levels[0]

    def give(r, carry):
        for m in range(5):
            fields[at(r * 40, m * 8), :] = fine.held[at(r * 40, fine.size + m * 8), :]
        return carry
    lax.fori_loop(0, 25, give, 0)
    column = (my_gx % 2) * 4 + my_gy
    fields[FIELD : FIELD + 125, :] = fine.held[pl.ds(2 * fine.size + column, 125, stride=8), :]
    fields[FIELD + 125 : FIELD + 128, :] = jnp.zeros((3, 128), F32)


def split_dot(a, b):
    high = a.astype(jnp.bfloat16)
    rest = a - high.astype(F32)
    middle = rest.astype(jnp.bfloat16)
    low = (rest - middle.astype(F32)).astype(jnp.bfloat16)
    b = b.astype(jnp.bfloat16)
    return sum(
        lax.dot_general(part, b, (((1,), (0,)), ((), ())), preferred_element_type=F32)
        for part in (low, middle, high)
    )


def finish_kernel(own, other, own_start, other_start, guess, sol, res_out, arnoldi, cols, outs):
    sec = lax.axis_index("section")
    my_gx, my_gy = lax.axis_index("gx"), lax.axis_index("gy")
    whole, back, back_matrix, blocks, cross = split_sections()
    weights = jnp.where(iota((8, 128), 1) < 64, float(cross[0]), float(cross[1]))
    nothing = jnp.zeros((8, 128), F32)

    lane = iota((32, 128), 1)
    here = lane // EZ % 2 == my_gx // 2
    factors = []
    for s in range(2):
        row = []
        for p in range(2):
            parts = []
            for mine in range(2):
                t = whole[2 * mine + s]
                pairs = [jnp.where(lane < 64, float(t[2 * q]), float(t[2 * q + 1])) for q in range(2)]
                parts.append(pairs[mine] if p == 0 else pairs[1 - mine])
            row.append(jnp.where(here, jnp.where(sec == 0, parts[0], parts[1]), 0.0)[:25])
        factors.append(row)
    column = (my_gx % 2) * 4 + my_gy
    cols[...] = jnp.zeros_like(cols)
    total = jnp.zeros((192, 160), F32)
    for k in range(5):
        where = pl.ds(k * 200 + column, 25, stride=8)
        shown = [[ref[FIELD + k * 25 : FIELD + k * 25 + 25, :] for ref in (own, other)]]
        shown.append([ref[where, :] for ref in (own_start, other_start)])
        shown.append([b[where, :] - a[where, :] for a, b in ((own, own_start), (other, other_start))])
        for f, (a, b) in enumerate(shown):
            for s in range(2):
                r = f * 64 + s * 32
                cols[r : r + 25, :] = factors[s][0] * a + factors[s][1] * b
        hit = (iota((128, 160), 1) == 5 * (iota((128, 160), 0) % EZ) + k).astype(F32)
        total = total + split_dot(cols[...], hit)

    def product(a, b, c, d):
        return (a * c + b * d) + weights * (a * d + b * c)

    uppers, sizes = [nothing] * 5, [nothing] * 5
    for r in range(125):
        a, b, c, d = (ref[tile(r), :] for ref in (own, other, own_start, other_start))
        a, b = c - a, d - b
        uppers[r % 5] = uppers[r % 5] + product(a, b, c, d)
        sizes[r % 5] = sizes[r % 5] + product(c, d, c, d)
    size = jnp.sum(sum(sizes), keepdims=True)
    upper = jnp.sum(sum(uppers), keepdims=True) / size
    rests = [nothing] * 5
    for r in range(125):
        a, b, c, d = (ref[tile(r), :] for ref in (own, other, own_start, other_start))
        a, b = c - a, d - b
        a, b = a - upper * c, b - upper * d
        rests[r % 5] = rests[r % 5] + product(a, b, a, b)
    rest = jnp.sum(sum(rests), keepdims=True)
    beta = jnp.sqrt(size)
    lower = jnp.sqrt(rest) / beta
    weight = upper / (upper * upper + lower * lower)
    entries = float(125 * EZ * COLS * 4)
    for place_out, value in enumerate((beta * (1.0 / math.sqrt(entries)), upper, lower)):
        arnoldi[place_out] = value[0, 0]
    outs[:64, :] = weight * total[:64]
    outs[64:, :] = total[64:128] - weight * total[128:]
    for i in range(5):
        for j in range(5):
            r = 5 * i + j
            for s in range(2):
                sol[i, j, s : s + 1, :] = guess[i, j, s : s + 1, :] + outs[s * 32 + r : s * 32 + r + 1, :]
                res_out[i, j, s : s + 1, :] = outs[64 + s * 32 + r : 64 + s * 32 + r + 1, :]


def assemble(blocks):
    return pl.pallas_call(
        assemble_kernel,
        out_shape=jax.ShapeDtypeStruct((128 * 8, 128), F32),
        in_specs=[VMEM] * 4,
        out_specs=VMEM,
        scratch_shapes=[pltpu.VMEM((COLS * HALF, 128), F32)],
        compiler_params=limit(16),
        name="assemble",
    )(*blocks)


def cycle(blocks, assembled):
    scratch = []
    for n in (5, 3, 2):
        scratch += [pltpu.VMEM((n**3 * 8 * copies, 128), F32) for copies in (1, 1, 5, 1)]
    scratch += [
        pltpu.VMEM((COLS * 32, 128), F32),
        pltpu.VMEM((128 * 8, 128), F32),
        pltpu.VMEM((FIELD, 128), F32),
        pltpu.VMEM((15 * 8, 128), F32),
    ]
    return pl.pallas_call(
        cycle_kernel,
        out_shape=jax.ShapeDtypeStruct((FIELD + 128, 128), F32),
        in_specs=[VMEM] * 5,
        out_specs=VMEM,
        scratch_shapes=scratch,
        compiler_params=limit(24),
        cost_estimate=pl.CostEstimate(flops=40_000_000, bytes_accessed=30_000_000, transcendentals=0),
        name="cycle",
    )(*blocks, assembled)


def finish(own, other, own_start, other_start, guess):
    return pl.pallas_call(
        finish_kernel,
        out_shape=[
            jax.ShapeDtypeStruct(guess.shape, F32),
            jax.ShapeDtypeStruct(guess.shape, F32),
            jax.ShapeDtypeStruct((3,), F32),
        ],
        in_specs=[VMEM] * 5,
        out_specs=[VMEM, VMEM, pl.BlockSpec(memory_space=pltpu.SMEM)],
        scratch_shapes=[pltpu.VMEM((192, 128), F32), pltpu.VMEM((128, 160), F32)],
        compiler_params=limit(24),
        name="finish",
    )(own, other, own_start, other_start, guess)


def exchange(x, axis, bits):
    return lax.ppermute(x, axis, [(n, n ^ bits) for n in range(lax.axis_size(axis))])


def gathered_body(rhs, guess, kappa, bc_flags):
    rhs, guess = (jnp.transpose(v, (1, 2, 0, 3)) for v in (rhs, guess))
    halos = [exchange(guess, axis, bits) for axis in ("gx", "gy") for bits in (1, 3)]
    base = local_part(rhs, guess, kappa, bc_flags)
    mine, theirs = halo_part(base, halos)
    got = exchange(theirs, "section", 1)
    piece = jnp.concatenate([mine[:HALF] + got, mine[HALF:]])
    line = jnp.concatenate([piece] + [exchange(piece, "gx", bits) for bits in (1, 2, 3)])
    blocks = [line] + [exchange(line, "gy", bits) for bits in (1, 2, 3)]
    start = assemble(blocks)
    other_start = exchange(start, "section", 1)
    own, other_start = lax.optimization_barrier((cycle(blocks, start), other_start))
    sol, res, arnoldi = finish(own, exchange(own, "section", 1), start, other_start, guess)
    sol, res = (jnp.transpose(v, (2, 0, 1, 3)) for v in (sol, res))
    return sol, res, arnoldi


def solution(mesh):
    placed = (
        P("section", "gx", "gy", None),
        P("section", "gx", "gy", None),
        P("gx", "gy", None),
        P(None, "gx", "gy", None),
    )
    sizes = (mesh.shape["section"], mesh.shape["gx"], mesh.shape["gy"])

    def step(rhs, guess, kappa, bc_flags):
        fits = sizes == (2, 4, 4) and rhs.shape == (4, 20, 20, 160)
        return jax.shard_map(
            gathered_body if fits else stepwise,
            mesh=mesh,
            in_specs=placed,
            out_specs=(P("section", "gx", "gy", None), P("section", "gx", "gy", None), P()),
            check_vma=False,
        )(rhs, guess, kappa, bc_flags)

    return step
```

```python
from functools import partial
import math

import jax
import jax.numpy as jnp
import numpy as np
from jax import lax
from jax.experimental import pallas as pl
from jax.experimental.pallas import tpu as pltpu
from jax.sharding import PartitionSpec as P

ADVECT = (1.0, 0.7, 0.5)
DIFFUSE = 0.05
STEP_SIZE = 0.2
JACOBI_SCALE = 0.25
CHEB_LOW = 0.25
CHEB_HIGH = 2.0
LETTERS = "abcdef"


def extended(x, sides, width):
    for axis, dim in sides:
        peers, length = (lax.axis_size(axis), x.shape[dim])
        up = [(i, (i + 1) % peers) for i in range(peers)]
        down = [(j, i) for i, j in up]
        last = lax.slice_in_dim(x, length - width, length, axis=dim)
        leading = lax.slice_in_dim(x, 0, width, axis=dim)
        before = lax.ppermute(last, axis, up)
        after = lax.ppermute(leading, axis, down)
        x = jnp.concatenate([before, x, after], axis=dim)
    return x


def lobatto(count):
    if count == 5:
        inner = math.sqrt(3.0 / 7.0)
        return (
            np.array([-1.0, -inner, 0.0, inner, 1.0]),
            np.array([0.1, 49.0 / 90.0, 32.0 / 45.0, 49.0 / 90.0, 0.1]),
        )
    if count == 3:
        return (np.array([-1.0, 0.0, 1.0]), np.array([1.0 / 3.0, 4.0 / 3.0, 1.0 / 3.0]))
    return (np.array([-1.0, 1.0]), np.array([1.0, 1.0]))


def lagrange_table(nodes, points):
    table = np.ones((len(points), len(nodes)))
    for column in range(len(nodes)):
        for other in range(len(nodes)):
            if other != column:
                table[:, column] *= (points - nodes[other]) / (nodes[column] - nodes[other])
    return table


def slope_table(nodes):
    total = len(nodes)
    factor = np.array(
        [np.prod([nodes[i] - nodes[k] for k in range(total) if k != i]) for i in range(total)]
    )
    table = np.zeros((total, total))
    for row in range(total):
        for column in range(total):
            if row != column:
                table[row, column] = factor[row] / factor[column] / (nodes[row] - nodes[column])
        table[row, row] = -np.sum(table[row])
    return table


def element_matrix(count, direction):
    nodes, weights = lobatto(count)
    slopes = slope_table(nodes)
    stiffness = (1.0 / weights)[:, None] * (slopes.T @ (weights[:, None] * slopes))
    return ADVECT[direction] * slopes + DIFFUSE * stiffness


def legendre_pair(point, order):
    values = [1.0, point]
    slopes = [0.0, 1.0]
    for index in range(1, order):
        values.append(
            ((2 * index + 1) * point * values[index] - index * values[index - 1]) / (index + 1)
        )
        slopes.append(slopes[index - 1] + (2 * index + 1) * values[index])
    return (values, slopes)


def radau_nodes():
    starts = [0.0885879595127039, 0.4094668644407347, 0.7876594617608471]
    found = []
    for start in starts:
        point = start
        for sweep in range(30):
            values, slopes = legendre_pair(2.0 * point - 1.0, 4)
            change = (values[4] - values[3]) / (2.0 * (slopes[4] - slopes[3]))
            point = point - change
        found.append(point)
    found.append(1.0)
    return found


def poly_times(coefs, root):
    result = [0.0] * (len(coefs) + 1)
    for index in range(len(coefs)):
        result[index + 1] += coefs[index]
        result[index] -= root * coefs[index]
    return result


def radau_matrix():
    order = 4
    nodes = radau_nodes()
    matrix = np.zeros((order, order))
    for column in range(order):
        coefs = [1.0]
        denominator = 1.0
        for other in range(order):
            if other != column:
                coefs = poly_times(coefs, nodes[other])
                denominator *= nodes[column] - nodes[other]
        for row in range(order):
            upper_end = nodes[row]
            integral = 0.0
            for index in range(len(coefs)):
                integral += coefs[index] * upper_end ** (index + 1) / (index + 1)
            matrix[row, column] = integral / denominator
    return matrix


def node_einsum(table, field, axis):
    labels = LETTERS[: field.ndim]
    source = labels[: axis + 1] + "j" + labels[axis + 2 :]
    target = labels[: axis + 1] + "i" + labels[axis + 2 :]
    return jnp.einsum(
        "ij," + source + "->" + target,
        jnp.asarray(table, jnp.float32),
        field,
        precision=lax.Precision.HIGHEST,
    )


def apply_along(field, axis, count, table):
    shape = field.shape
    split = shape[:axis] + (shape[axis] // count, count) + shape[axis + 1 :]
    mapped = node_einsum(table, field.reshape(split), axis)
    return mapped.reshape(
        shape[:axis] + (mapped.shape[axis] * mapped.shape[axis + 1],) + shape[axis + 1 :]
    )


def line_part(field, axis, count, table, left_gain, right_gain, left_edge, right_edge):
    shape = field.shape
    elements = shape[axis] // count
    split = field.reshape(shape[:axis] + (elements, count) + shape[axis + 1 :])
    linear = node_einsum(table, split, axis)
    first = lax.index_in_dim(split, 0, axis + 1, keepdims=False)
    last = lax.index_in_dim(split, count - 1, axis + 1, keepdims=False)
    before = jnp.concatenate(
        [jnp.expand_dims(left_edge, axis), lax.slice_in_dim(last, 0, elements - 1, axis=axis)], axis
    )
    after = jnp.concatenate(
        [lax.slice_in_dim(first, 1, elements, axis=axis), jnp.expand_dims(right_edge, axis)], axis
    )
    front = jnp.expand_dims(left_gain * (first - before), axis + 1)
    back = jnp.expand_dims(right_gain * (last - after), axis + 1)
    if count > 2:
        middle_shape = list(front.shape)
        middle_shape[axis + 1] = count - 2
        pieces = [front, jnp.zeros(middle_shape, jnp.float32), back]
    else:
        pieces = [front, back]
    return (linear + jnp.concatenate(pieces, axis + 1)).reshape(shape)


def diag_along(shape, axis, count, table, left_gain, right_gain):
    elements = shape[axis] // count
    split = shape[:axis] + (elements, count) + shape[axis + 1 :]
    profile = [1] * len(split)
    profile[axis + 1] = count
    diagonal_entries = np.array([table[index, index] for index in range(count)])
    base = jnp.broadcast_to(jnp.asarray(diagonal_entries, jnp.float32).reshape(profile), split)
    front = jnp.expand_dims(left_gain, axis + 1)
    back = jnp.expand_dims(right_gain, axis + 1)
    if count > 2:
        middle_shape = list(front.shape)
        middle_shape[axis + 1] = count - 2
        pieces = [front, jnp.zeros(middle_shape, jnp.float32), back]
    else:
        pieces = [front, back]
    return (base + jnp.concatenate(pieces, axis + 1)).reshape(shape)


def level_kappa(kappa, count):
    if count == 5:
        return kappa
    picks = np.array([0, 2, 4]) if count == 3 else np.array([0, 4])
    extents = [extent // 5 for extent in kappa.shape]
    grouped = kappa.reshape(extents[0], 5, extents[1], 5, extents[2], 5)
    for axis in (1, 3, 5):
        grouped = jnp.take(grouped, picks, axis=axis)
    return grouped.reshape(extents[0] * count, extents[1] * count, extents[2] * count)


def face_plane(face, direction, count):
    plane = face.astype(jnp.float32)
    for axis in range(3):
        if axis != direction:
            plane = jnp.repeat(plane, count, axis=axis)
    return plane


def build_level(kappa, flags, count):
    nodes, weights = lobatto(count)
    kappa_level = level_kappa(kappa, count)
    tables, lefts, rights = ([], [], [])
    diagonal = kappa_level
    for direction in range(3):
        table = element_matrix(count, direction)
        lower = face_plane(flags[2 * direction], direction, count)
        upper = face_plane(flags[2 * direction + 1], direction, count)
        left_gain = (ADVECT[direction] * (1.0 + lower) / 2.0 + DIFFUSE * count * count) / float(
            weights[0]
        )
        right_gain = (DIFFUSE * count * count - ADVECT[direction] * (1.0 - upper) / 2.0) / float(
            weights[-1]
        )
        tables.append(table)
        lefts.append(left_gain)
        rights.append(right_gain)
        diagonal = diagonal + diag_along(
            kappa_level.shape, direction, count, table, left_gain, right_gain
        )
    scale = 1.0 / (1.0 + STEP_SIZE * JACOBI_SCALE * diagonal)
    return (count, tables, lefts, rights, kappa_level, scale)


def restrict(field, fine_count, coarse_count):
    fine_nodes, fine_weights = lobatto(fine_count)
    coarse_nodes, coarse_weights = lobatto(coarse_count)
    table = (
        (1.0 / coarse_weights)[:, None]
        * lagrange_table(coarse_nodes, fine_nodes).T
        * fine_weights[None, :]
    )
    for axis in range(field.ndim - 3, field.ndim):
        field = apply_along(field, axis, fine_count, table)
    return field


def prolong(field, coarse_count, fine_count):
    fine_nodes, fine_weights = lobatto(fine_count)
    coarse_nodes, coarse_weights = lobatto(coarse_count)
    table = lagrange_table(coarse_nodes, fine_nodes)
    for axis in range(field.ndim - 3, field.ndim):
        field = apply_along(field, axis, coarse_count, table)
    return field


def chebyshev(rhs, start, level, operator):
    centre = (CHEB_HIGH + CHEB_LOW) / 2.0
    radius = (CHEB_HIGH - CHEB_LOW) / 2.0
    ratio = centre / radius
    first_rho = 1.0 / ratio
    second_rho = 1.0 / (2.0 * ratio - first_rho)
    scale = level[5]
    if start is None:
        remain = rhs
    else:
        remain = rhs - operator(start, level)
    step = scale * remain / centre
    guess = step if start is None else start + step
    remain = remain - operator(step, level)
    step = second_rho * first_rho * step + 2.0 * second_rho / radius * scale * remain
    return guess + step


def vcycle(rhs, levels, operator):
    fine, middle, coarse = levels
    fine_x = chebyshev(rhs, None, fine, operator)
    middle_rhs = restrict(rhs - operator(fine_x, fine), 5, 3)
    middle_x = chebyshev(middle_rhs, None, middle, operator)
    coarse_rhs = restrict(middle_rhs - operator(middle_x, middle), 3, 2)
    coarse_x = chebyshev(coarse_rhs, None, coarse, operator)
    middle_x = chebyshev(middle_rhs, middle_x + prolong(coarse_x, 2, 3), middle, operator)
    return chebyshev(rhs, fine_x + prolong(middle_x, 3, 5), fine, operator)


def spatial(field, level):
    count, tables, lefts, rights, kappa_level, scale = level
    padded = extended(field, (("gx", 1), ("gy", 2)), 1)
    total = kappa_level * field
    total = total + line_part(
        field,
        1,
        count,
        tables[0],
        lefts[0],
        rights[0],
        padded[:, 0, 1:-1, :],
        padded[:, -1, 1:-1, :],
    )
    total = total + line_part(
        field,
        2,
        count,
        tables[1],
        lefts[1],
        rights[1],
        padded[:, 1:-1, 0, :],
        padded[:, 1:-1, -1, :],
    )
    total = total + line_part(
        field, 3, count, tables[2], lefts[2], rights[2], field[:, :, :, -1], field[:, :, :, 0]
    )
    return total


def apply_system(field, level, coupling):
    image = spatial(field, level)
    everyone = lax.all_gather(image, "section", axis=0, tiled=True)
    butcher = jnp.asarray(radau_matrix(), jnp.float32)
    rows = lax.dynamic_slice_in_dim(
        butcher, lax.axis_index("section") * field.shape[0], field.shape[0], 0
    )
    mixed = jnp.einsum("ij,jabc->iabc", rows, everyone, precision=lax.Precision.HIGHEST)
    return field + STEP_SIZE * mixed


def global_total(values):
    return lax.psum(values, ("section", "gx", "gy"))


def stepwise(rhs, guess, kappa, bc_flags):
    levels = [build_level(kappa, bc_flags, count) for count in (5, 3, 2)]
    section_operator = partial(apply_system, coupling=None)
    start_residual = rhs - section_operator(guess, levels[0])
    dofs = float(rhs.size * lax.axis_size("section") * lax.axis_size("gx") * lax.axis_size("gy"))
    beta = jnp.sqrt(global_total(jnp.sum(start_residual * start_residual).reshape(1))[0])
    basis = start_residual / beta
    precond = vcycle(basis, levels, section_operator)
    image = section_operator(precond, levels[0])
    upper = global_total(jnp.sum(image * basis).reshape(1))[0]
    remainder = image - upper * basis
    lower = jnp.sqrt(global_total(jnp.sum(remainder * remainder).reshape(1))[0])
    weight = beta * upper / (upper * upper + lower * lower)
    solution = guess + weight * precond
    residual = start_residual - weight * image
    arnoldi = jnp.stack([beta / math.sqrt(dofs), upper, lower]).astype(jnp.float32)
    return (solution, residual, arnoldi)


EZ = 32
COLS = 16
HALF = 64
PIECE = 96
FIELD = 1000
F32 = jnp.float32


def split_sections():
    matrix = radau_matrix()
    values, vectors = np.linalg.eig(matrix)
    order = [n for n in np.argsort(np.abs(values.imag), kind="stable") if values[n].imag > 0]
    bases = []
    for n in order:
        plane = np.stack([vectors[:, n].real, vectors[:, n].imag], axis=1)
        bases.append(np.linalg.qr(plane)[0])
    left, cross, right = np.linalg.svd(bases[0].T @ bases[1])
    bases = [bases[0] @ left, bases[1] @ right.T]
    for c in range(2):
        sign = np.sign(bases[0][np.argmax(np.abs(bases[0][:, c])), c])
        bases = [np.concatenate([b[:, :c], sign * b[:, c : c + 1], b[:, c + 1 :]], axis=1) for b in bases]
    whole = np.concatenate(bases, axis=1)
    back = np.linalg.inv(whole)
    return whole, back, back @ matrix, back @ matrix @ whole, cross


def iota(shape, dim):
    return lax.broadcasted_iota(jnp.int32, shape, dim)


def exact_dot(a, b):
    return lax.dot_general(
        a, b, (((1,), (0,)), ((), ())), precision=lax.Precision.HIGHEST, preferred_element_type=F32
    )


def choose(index, values):
    out = values[-1]
    for place in range(len(values) - 2, -1, -1):
        out = jnp.where(index == place, values[place], out)
    return out


def face_gains(flag, direction, side, count):
    nodes, weights = lobatto(count)
    c, nu = ADVECT[direction], DIFFUSE * count * count
    if side == 0:
        return (c * (1.0 + flag) / 2.0 + nu) * (1.0 / float(weights[0]))
    return (nu - c * (1.0 - flag) / 2.0) * (1.0 / float(weights[-1]))


def column_tables():
    kx, ky, kz = (element_matrix(5, d) for d in range(3))
    rows = np.zeros((64, 64))
    for s in range(2):
        for i in range(5):
            for j in range(5):
                r = s * 32 + i * 5 + j
                for m in range(5):
                    rows[r, s * 32 + m * 5 + j] += kx[i, m]
                    rows[r, s * 32 + i * 5 + m] += ky[j, m]
    lines = np.zeros((160, 320))
    for e in range(EZ):
        lines[e * 5 : e * 5 + 5, e * 5 : e * 5 + 5] = kz.T
        lines[(e - 1) % EZ * 5 + 4, 160 + e * 5] = 1.0
        lines[(e + 1) % EZ * 5, 160 + e * 5 + 4] = 1.0
    return rows.astype(np.float32), lines.astype(np.float32)


def pick_line(k):
    return (iota((160, 128), 0) == 5 * (iota((160, 128), 1) % EZ) + k).astype(F32)


def pair_factors(sec, table, own, s):
    upper = iota((32, 128), 1) < 64
    first = jnp.where(upper, float(table[0, s]), float(table[1, s]))
    second = jnp.where(upper, float(table[2, 2 + s]), float(table[3, 2 + s]))
    if not own:
        first = jnp.where(upper, float(table[2, s]), float(table[3, s]))
        second = jnp.where(upper, float(table[0, 2 + s]), float(table[1, 2 + s]))
    return jnp.where(sec == 0, first, second)


def pack_nodes(nodes):
    odd = iota((HALF, 128), 1) // EZ % 2 == 1
    return jnp.where(odd, nodes[HALF:, :], nodes[:HALF, :])


def fetch(pairs, sems):
    copies = [pltpu.make_async_copy(src, dst, sems.at[n]) for n, (src, dst) in enumerate(pairs)]
    for copy in copies:
        copy.start()
    for copy in copies:
        copy.wait()


def local_kernel(
    rhs_in, guess_in, kappa_in, flags_in, rows_in, lines_in, base,
    rhs, guess, kappa, flags, rows_t, lines_t, sems, x, kap, stack, own_nodes, other_nodes, krep,
):
    sec = lax.axis_index("section")
    fetch(
        [(rhs_in, rhs), (guess_in, guess), (kappa_in, kappa), (flags_in, flags), (rows_in, rows_t), (lines_in, lines_t)],
        sems,
    )
    x[...] = jnp.zeros_like(x)
    kap[...] = jnp.zeros_like(kap)
    stack[...] = jnp.zeros_like(stack)
    for i in range(5):
        kap[5 * i : 5 * i + 5, :] = kappa[i]
        for j in range(5):
            r = 5 * i + j
            value = guess[i, j]
            left = rhs[i, j] - value
            for s in range(2):
                x[s * 32 + r : s * 32 + r + 1, :] = value[s : s + 1]
                stack[s * 32 + r : s * 32 + r + 1, :] = left[s : s + 1]
    flag = flags[:, 0, 0, :].astype(F32)
    spread = (iota((EZ, 160), 1) // 5 == iota((EZ, 160), 0)).astype(F32)
    wide = exact_dot(flag, spread)
    gains = [face_gains(wide[d : d + 1, :], d // 2, d % 2, 5) for d in range(6)]
    row = iota((32, 160), 0)
    lane = iota((32, 160), 1) % 5
    none = jnp.zeros((32, 160), F32)
    gx = jnp.where(row < 5, gains[0], jnp.where((row >= 20) & (row < 25), gains[1], none))
    gy = jnp.where(row % 5 == 0, gains[2], jnp.where(row % 5 == 4, gains[3], none))
    gz = jnp.where(lane == 0, gains[4], jnp.where(lane == 4, gains[5], none))
    gy = jnp.where(row < 25, gy, none)
    for place, gain in ((160, gx), (192, gy)):
        base[place : place + 32, :] = gain[:, :128]
        base[64 + place : 96 + place, :EZ] = gain[:, 128:]
    field = x[...]
    along = exact_dot(rows_t[...], field)
    across = exact_dot(field, lines_t[...])
    own = kap[...] + gx + gy + gz
    for s in range(2):
        r = slice(s * 32, s * 32 + 32)
        image = own * field[r] + along[r] + across[r, :160] - gz * across[r, 160:]
        stack[64 + s * 32 : 96 + s * 32, :] = image
    whole, back, back_matrix, blocks, cross = split_sections()
    own_nodes[...] = jnp.zeros_like(own_nodes)
    other_nodes[...] = jnp.zeros_like(other_nodes)
    krep[...] = jnp.zeros_like(krep)
    source = stack[...]
    coefs = kap[...]
    for k in range(5):
        pick = pick_line(k)
        parts = exact_dot(source, pick)
        for target, mark in ((own_nodes, True), (other_nodes, False)):
            total = jnp.zeros((32, 128), F32)
            for s in range(2):
                total = total + pair_factors(sec, back, mark, s) * parts[s * 32 : s * 32 + 32]
                factor = pair_factors(sec, -STEP_SIZE * back_matrix, mark, s)
                total = total + factor * parts[64 + s * 32 : 96 + s * 32]
            target[25 * k : 25 * k + 25, :] = total[:25]
        krep[25 * k : 25 * k + 25, :] = exact_dot(coefs, pick)[:25]
    repeat = (iota((EZ, 128), 1) % EZ == iota((EZ, 128), 0)).astype(F32)
    shown = exact_dot(flag, repeat)
    upper = iota((1, 128), 1) < 64
    for r in range(3):
        own_nodes[125 + r : 126 + r, :] = jnp.where(upper, shown[2 * r : 2 * r + 1], shown[2 * r + 1 : 2 * r + 2])
    base[:HALF, :] = pack_nodes(own_nodes)
    base[PIECE : PIECE + HALF, :] = pack_nodes(other_nodes)
    base[HALF:PIECE, :] = choose(iota((32, 128), 1) // EZ, [krep[32 * q : 32 * q + 32, :] for q in range(4)])


def halo_kernel(base, x1, x3, y1, y3, mine, theirs, near, own_nodes, other_nodes):
    sec = lax.axis_index("section")
    even_x = lax.axis_index("gx") % 2 == 0
    even_y = lax.axis_index("gy") % 2 == 0
    for ref in (near, own_nodes, other_nodes):
        ref[...] = jnp.zeros_like(ref)
    for m in range(5):
        for s in range(2):
            r = s * 32
            one = slice(s, s + 1)
            near[r + m : r + m + 1, :] = jnp.where(even_x, x3[4, m, one, :], x1[4, m, one, :])
            near[r + 20 + m : r + 21 + m, :] = jnp.where(even_x, x1[0, m, one, :], x3[0, m, one, :])
            r += 64
            near[r + 5 * m : r + 5 * m + 1, :] = jnp.where(even_y, y3[m, 4, one, :], y1[m, 4, one, :])
            near[r + 5 * m + 4 : r + 5 * m + 5, :] = jnp.where(even_y, y1[m, 0, one, :], y3[m, 0, one, :])
    gx, gy = (
        jnp.concatenate([base[r : r + 32, :], base[64 + r : 96 + r, :EZ]], axis=1) for r in (160, 192)
    )
    parts_in = []
    for s in range(2):
        r = s * 32
        parts_in.append(gx * near[r : r + 32, :] + gy * near[64 + r : 96 + r, :])
    source = jnp.concatenate(parts_in, axis=0)
    back_matrix = split_sections()[2]
    for k in range(5):
        parts = exact_dot(source, pick_line(k))
        for target, mark in ((own_nodes, True), (other_nodes, False)):
            total = jnp.zeros((32, 128), F32)
            for s in range(2):
                factor = pair_factors(sec, STEP_SIZE * back_matrix, mark, s)
                total = total + factor * parts[s * 32 : s * 32 + 32]
            target[25 * k : 25 * k + 25, :] = total[:25]
    mine[:HALF, :] = base[:HALF, :] + pack_nodes(own_nodes)
    mine[HALF:, :] = base[HALF:PIECE, :]
    theirs[...] = base[PIECE : PIECE + HALF, :] + pack_nodes(other_nodes)


VMEM = pl.BlockSpec(memory_space=pltpu.VMEM)
HBM = pl.BlockSpec(memory_space=pltpu.HBM)


def limit(mib):
    return pltpu.CompilerParams(vmem_limit_bytes=mib * 2**20)


def local_part(rhs, guess, kappa, flags):
    rows_t, lines_t = column_tables()
    operands = (rhs, guess, kappa, flags, jnp.asarray(rows_t), jnp.asarray(lines_t))
    return pl.pallas_call(
        local_kernel,
        out_shape=jax.ShapeDtypeStruct((288, 128), F32),
        in_specs=[HBM] * 6,
        out_specs=VMEM,
        scratch_shapes=[pltpu.VMEM(o.shape, o.dtype) for o in operands]
        + [
            pltpu.SemaphoreType.DMA((6,)),
            pltpu.VMEM((64, 160), F32),
            pltpu.VMEM((32, 160), F32),
            pltpu.VMEM((128, 160), F32),
            pltpu.VMEM((128, 128), F32),
            pltpu.VMEM((128, 128), F32),
            pltpu.VMEM((128, 128), F32),
        ],
        compiler_params=limit(60),
        name="local_part",
    )(*operands)


def halo_part(base, halos):
    return pl.pallas_call(
        halo_kernel,
        out_shape=[
            jax.ShapeDtypeStruct((PIECE, 128), F32),
            jax.ShapeDtypeStruct((HALF, 128), F32),
        ],
        in_specs=[VMEM] * 5,
        out_specs=[VMEM] * 2,
        scratch_shapes=[pltpu.VMEM((128, 160), F32)] + [pltpu.VMEM((128, 128), F32)] * 2,
        compiler_params=limit(16),
        name="halo_part",
    )(base, *halos)


class Level:
    def __init__(self, count, refs):
        self.count = count
        self.diag, self.jac, self.x, self.dir, self.res, self.edge, self.f = refs
        self.tables = [element_matrix(count, d) for d in range(3)]
        self.gains = None


def tile(index):
    return pl.ds(index * 8, 8)


def rows_of(pieces, size, r, h):
    return pieces[pl.ds(8 * h * size + r, 8, stride=size), :]


def place_pieces(blocks, pieces, first, size):
    my_gx, my_gy = lax.axis_index("gx"), lax.axis_index("gy")
    for b, block in enumerate(blocks):
        for a in range(4):
            column = (my_gx ^ a) * 4 + (my_gy ^ b)
            start = pl.multiple_of(column * size, 8)
            pieces[pl.ds(start, size), :] = block[a * PIECE + first : a * PIECE + first + size, :]


def assemble_kernel(block0, block1, block2, block3, field, pieces):
    place_pieces((block0, block1, block2, block3), pieces, 0, HALF)
    odd = iota((8, 128), 1) // EZ % 2 == 1
    for r in range(HALF):
        low, high = rows_of(pieces, HALF, r, 0), rows_of(pieces, HALF, r, 1)
        field[tile(r), :] = jnp.where(odd, pltpu.roll(high, 32, 1), low)
        field[tile(HALF + r), :] = jnp.where(odd, high, pltpu.roll(low, 96, 1))


def load(ref, first, count):
    start = first * 8 if isinstance(first, int) else pl.multiple_of(first * 8, 8)
    return ref[pl.ds(start, count * 8), :].reshape(count, 8, 128)


def store(ref, first, value):
    start = first * 8 if isinstance(first, int) else pl.multiple_of(first * 8, 8)
    ref[pl.ds(start, value.shape[0] * 8), :] = value.reshape(value.shape[0] * 8, 128)


def cycle_kernel(block0, block1, block2, block3, assembled, fields, *scratch):
    sec = lax.axis_index("section")
    my_gx, my_gy = lax.axis_index("gx"), lax.axis_index("gy")
    levels = [Level(n, scratch[7 * p : 7 * p + 7]) for p, n in enumerate((5, 3, 2))]
    pieces, kap, half, terms = scratch[21:25]
    lane = iota((8, 128), 1)
    sub = iota((8, 128), 0)
    group = lane // EZ
    odd = group % 2 == 1
    element = lane % EZ
    place = sub % 4
    low_half = sub < 4
    blocks = split_sections()[3]

    def lanes_of(upper, lower):
        return jnp.where(lane < 64, jnp.where(sec == 0, upper[0], upper[1]), jnp.where(sec == 0, lower[0], lower[1]))

    entry = [[[float(STEP_SIZE * blocks[2 * p + a, 2 * p + b]) for p in range(2)] for b in range(2)] for a in range(2)]
    same = lanes_of(entry[0][0], entry[1][1])
    swap = lanes_of(entry[0][1], entry[1][0])
    centre = (CHEB_HIGH + CHEB_LOW) / 2.0
    radius = (CHEB_HIGH - CHEB_LOW) / 2.0
    first_rho = radius / centre
    second_rho = 1.0 / (2.0 * centre / radius - first_rho)
    keep = 1.0 + second_rho * first_rho
    push = 2.0 * second_rho / radius * centre

    flags = []
    for r in range(3):
        got = assembled[tile(125 + r), :]
        across = pltpu.roll(got, 64, 1)
        flags += [jnp.where(lane < 64, got, across), jnp.where(lane < 64, across, got)]
    place_pieces((block0, block1, block2, block3), pieces, HALF, 32)

    for r in range(32):
        turned = []
        for h in range(2):
            got = rows_of(pieces, 32, r, h)
            turned.append([pltpu.roll(got, 32 * m, 1) if m else got for m in range(4)])
        for q in range(4):
            kap[tile(q * 32 + r), :] = choose(group, [turned[g % 2][(g - q) % 4] for g in range(4)])

    for level in levels:
        n = level.count
        stride = 4 // (n - 1)
        level.gains = [face_gains(flags[d], d // 2, d % 2, n) for d in range(6)]
        rows = []
        for d in range(3):
            row = [jnp.full((8, 128), float(level.tables[d][m, m]), F32) for m in range(n)]
            row[0] = row[0] + level.gains[2 * d]
            row[n - 1] = row[n - 1] + level.gains[2 * d + 1]
            rows.append(row)
        for m in range(n):
            terms[tile(m), :] = rows[2][m]

        def diagonals(k, carry, level=level, n=n, stride=stride, rows=rows):
            along = jnp.stack(rows[1])
            for i in range(n):
                line = load(kap, k * 25 * stride + i * stride * 5, 5)
                line = jnp.stack([line[j * stride] for j in range(n)])
                value = line + (along + (load(terms, k, 1) + rows[0][i]))
                scale = 1.0 / (1.0 + STEP_SIZE * JACOBI_SCALE * value)
                store(level.diag, (k * n + i) * n, value)
                store(level.jac, (k * n + i) * n, scale * (1.0 / centre))
            return carry
        lax.fori_loop(0, n, diagonals, 0)
        level.edge[...] = jnp.zeros_like(level.edge)

    def begin(level, source):
        n = level.count

        def start(k, carry):
            first = k * n * n
            f = load(source, first, n * n)
            store(level.dir, first, load(level.jac, first, n * n) * f)
            store(level.res, first, f)
            store(level.x, first, jnp.zeros_like(f))
            return carry
        lax.fori_loop(0, n, start, 0)

    def apply(level, smooth):
        n = level.count
        kx, ky, kz = level.tables
        source = level.dir if smooth else level.x
        for i in range(n):
            v = load(source, ((n - 1) * n + i) * n, n)
            moved = jnp.where(element == 0, pltpu.roll(v, 97, 2), pltpu.roll(v, 1, 2))
            store(level.edge, i * n, level.gains[4] * moved)
            v = load(source, i * n, n)
            moved = jnp.where(element == EZ - 1, pltpu.roll(v, 31, 2), pltpu.roll(v, 127, 2))
            store(level.edge, ((n - 1) * n + i) * n, level.gains[5] * moved)

        def around(u):
            turned = pltpu.roll(u, 4, 1)
            return turned, jnp.where(odd, pltpu.roll(turned, 32, 2), pltpu.roll(turned, 96, 2))

        def plane(k, carry):
            sides = []
            for m in range(1, n):
                coef = choose(k, [float(kz[a, (a + m) % n]) for a in range(n)])
                sides.append((coef, jnp.where(k + m >= n, k + m - n, k + m) * (n * n)))
            here = k * (n * n)
            v = [load(source, here + i * n, n) for i in range(n)]
            left, left_far = around(v[n - 1])
            right, right_far = around(v[0])
            waiting = []
            for i in range(n):
                first = here + i * n
                total = load(level.diag, first, n) * v[i] - load(level.edge, first, n)
                for m in range(n):
                    if m != i:
                        total = total + float(kx[i, m]) * v[m]
                for coef, far in sides:
                    total = total + coef * load(source, far + i * n, n)
                lines = []
                for j in range(n):
                    line = None
                    for m in range(n):
                        if m != j:
                            term = float(ky[j, m]) * v[i][m]
                            line = term if line is None else line + term
                    if j == 0:
                        u = v[i][n - 1]
                        moved = jnp.where(place == 0, pltpu.roll(u, 5, 0), pltpu.roll(u, 1, 0))
                        line = line - level.gains[2] * moved
                    if j == n - 1:
                        u = v[i][0]
                        moved = jnp.where(place == 3, pltpu.roll(u, 3, 0), pltpu.roll(u, 7, 0))
                        line = line - level.gains[3] * moved
                    lines.append(line)
                total = total + jnp.stack(lines)
                if i == 0:
                    total = total - level.gains[0] * jnp.where(low_half, left_far, left)
                if i == n - 1:
                    total = total - level.gains[1] * jnp.where(low_half, right, right_far)
                image = v[i] + (same * total + swap * pltpu.roll(total, 64, 2))
                if smooth:
                    scaled = load(level.jac, first, n) * (load(level.res, first, n) - image)
                    waiting.append((level.x, first, load(level.x, first, n) + keep * v[i] + push * scaled))
                else:
                    rest = load(level.f, first, n) - image
                    waiting.append((level.res, first, rest))
                    waiting.append((level.dir, first, load(level.jac, first, n) * rest))
                if i % 2 == 1 or i == n - 1:
                    for place_out in waiting:
                        store(*place_out)
                    waiting = []
            return carry
        lax.fori_loop(0, n, plane, 0)

    def combine(weights, parts):
        total = None
        for weight, part in zip(weights, parts):
            if abs(weight) > 1e-14:
                term = part if abs(weight - 1.0) < 1e-14 else float(weight) * part
                total = term if total is None else total + term
        return total

    def change(table, source, target, add):
        m, n = table.shape

        def outer(i, carry):
            parts = [load(source, i * n + k * n * n, n) for k in range(n)]
            for k in range(m):
                store(half, i * n + k * n * n, combine(table[k], parts))
            return carry
        lax.fori_loop(0, n, outer, 0)

        def inner(k, carry):
            parts = [load(half, k * n * n + i * n, n) for i in range(n)]
            for i in range(m):
                line = combine(table[i], parts)
                value = jnp.stack([combine(table[j], [line[a] for a in range(n)]) for j in range(m)])
                first = k * m * m + i * m
                store(target, first, load(target, first, m) + value if add else value)
            return carry
        lax.fori_loop(0, m, inner, 0)

    def down(n, m):
        fine_nodes, fine_weights = lobatto(n)
        coarse_nodes, coarse_weights = lobatto(m)
        table = lagrange_table(coarse_nodes, fine_nodes)
        return (1.0 / coarse_weights)[:, None] * table.T * fine_weights[None, :]

    def up(m, n):
        return lagrange_table(lobatto(m)[0], lobatto(n)[0])

    def solve(p):
        level = levels[p]
        if p == 2:
            apply(level, True)
            return
        below = levels[p + 1]

        def step(t, carry):
            @pl.when(t != 1)
            def _():
                apply(level, True)

            @pl.when((t != 2) | (p == 0))
            def _():
                apply(level, False)

            @pl.when(t == 0)
            def _():
                n, m = level.count, below.count
                change(down(n, m), level.res, below.f, False)
                begin(below, below.f)
                solve(p + 1)
                change(up(m, n), below.x, level.x, True)
            return carry
        lax.fori_loop(0, 3, step, 0)

    fine = levels[0]
    fine.f = assembled
    begin(fine, assembled)
    solve(0)

    def give(k, carry):
        store(fields, k * 25, load(fine.res, k * 25, 25))
        return carry
    lax.fori_loop(0, 5, give, 0)
    column = (my_gx % 2) * 4 + my_gy
    fields[FIELD : FIELD + 125, :] = fine.x[pl.ds(column, 125, stride=8), :]
    fields[FIELD + 125 : FIELD + 128, :] = jnp.zeros((3, 128), F32)


def split_dot(a, b):
    high = a.astype(jnp.bfloat16)
    rest = a - high.astype(F32)
    middle = rest.astype(jnp.bfloat16)
    low = (rest - middle.astype(F32)).astype(jnp.bfloat16)
    b = b.astype(jnp.bfloat16)
    return sum(
        lax.dot_general(part, b, (((1,), (0,)), ((), ())), preferred_element_type=F32)
        for part in (low, middle, high)
    )


def finish_kernel(own, other, own_start, other_start, guess, sol, res_out, arnoldi, cols, outs):
    sec = lax.axis_index("section")
    my_gx, my_gy = lax.axis_index("gx"), lax.axis_index("gy")
    whole, back, back_matrix, blocks, cross = split_sections()
    weights = jnp.where(iota((8, 128), 1) < 64, float(cross[0]), float(cross[1]))
    nothing = jnp.zeros((8, 128), F32)

    lane = iota((32, 128), 1)
    here = lane // EZ % 2 == my_gx // 2
    factors = []
    for s in range(2):
        row = []
        for p in range(2):
            parts = []
            for mine in range(2):
                t = whole[2 * mine + s]
                pairs = [jnp.where(lane < 64, float(t[2 * q]), float(t[2 * q + 1])) for q in range(2)]
                parts.append(pairs[mine] if p == 0 else pairs[1 - mine])
            row.append(jnp.where(here, jnp.where(sec == 0, parts[0], parts[1]), 0.0)[:25])
        factors.append(row)
    column = (my_gx % 2) * 4 + my_gy
    cols[...] = jnp.zeros_like(cols)
    total = jnp.zeros((192, 160), F32)
    for k in range(5):
        where = pl.ds(k * 200 + column, 25, stride=8)
        shown = [[ref[FIELD + k * 25 : FIELD + k * 25 + 25, :] for ref in (own, other)]]
        shown.append([ref[where, :] for ref in (own_start, other_start)])
        shown.append([b[where, :] - a[where, :] for a, b in ((own, own_start), (other, other_start))])
        for f, (a, b) in enumerate(shown):
            for s in range(2):
                r = f * 64 + s * 32
                cols[r : r + 25, :] = factors[s][0] * a + factors[s][1] * b
        hit = (iota((128, 160), 1) == 5 * (iota((128, 160), 0) % EZ) + k).astype(F32)
        total = total + split_dot(cols[...], hit)

    def product(a, b, c, d):
        return (a * c + b * d) + weights * (a * d + b * c)

    uppers, sizes = [nothing] * 5, [nothing] * 5
    for r in range(125):
        a, b, c, d = (ref[tile(r), :] for ref in (own, other, own_start, other_start))
        a, b = c - a, d - b
        uppers[r % 5] = uppers[r % 5] + product(a, b, c, d)
        sizes[r % 5] = sizes[r % 5] + product(c, d, c, d)
    size = jnp.sum(sum(sizes), keepdims=True)
    upper = jnp.sum(sum(uppers), keepdims=True) / size
    rests = [nothing] * 5
    for r in range(125):
        a, b, c, d = (ref[tile(r), :] for ref in (own, other, own_start, other_start))
        a, b = c - a, d - b
        a, b = a - upper * c, b - upper * d
        rests[r % 5] = rests[r % 5] + product(a, b, a, b)
    rest = jnp.sum(sum(rests), keepdims=True)
    beta = jnp.sqrt(size)
    lower = jnp.sqrt(rest) / beta
    weight = upper / (upper * upper + lower * lower)
    entries = float(125 * EZ * COLS * 4)
    for place_out, value in enumerate((beta * (1.0 / math.sqrt(entries)), upper, lower)):
        arnoldi[place_out] = value[0, 0]
    outs[:64, :] = weight * total[:64]
    outs[64:, :] = total[64:128] - weight * total[128:]
    for i in range(5):
        for j in range(5):
            r = 5 * i + j
            for s in range(2):
                sol[i, j, s : s + 1, :] = guess[i, j, s : s + 1, :] + outs[s * 32 + r : s * 32 + r + 1, :]
                res_out[i, j, s : s + 1, :] = outs[64 + s * 32 + r : 64 + s * 32 + r + 1, :]


def assemble(blocks):
    return pl.pallas_call(
        assemble_kernel,
        out_shape=jax.ShapeDtypeStruct((128 * 8, 128), F32),
        in_specs=[VMEM] * 4,
        out_specs=VMEM,
        scratch_shapes=[pltpu.VMEM((COLS * HALF, 128), F32)],
        compiler_params=limit(16),
        name="assemble",
    )(*blocks)


def cycle(blocks, assembled):
    scratch = []
    for n in (5, 3, 2):
        scratch += [pltpu.VMEM((n**3 * 8, 128), F32)] * 7
    scratch += [
        pltpu.VMEM((COLS * 32, 128), F32),
        pltpu.VMEM((128 * 8, 128), F32),
        pltpu.VMEM((FIELD, 128), F32),
        pltpu.VMEM((15 * 8, 128), F32),
    ]
    return pl.pallas_call(
        cycle_kernel,
        out_shape=jax.ShapeDtypeStruct((FIELD + 128, 128), F32),
        in_specs=[VMEM] * 5,
        out_specs=VMEM,
        scratch_shapes=scratch,
        compiler_params=limit(24),
        cost_estimate=pl.CostEstimate(flops=40_000_000, bytes_accessed=30_000_000, transcendentals=0),
        name="cycle",
    )(*blocks, assembled)


def finish(own, other, own_start, other_start, guess):
    return pl.pallas_call(
        finish_kernel,
        out_shape=[
            jax.ShapeDtypeStruct(guess.shape, F32),
            jax.ShapeDtypeStruct(guess.shape, F32),
            jax.ShapeDtypeStruct((3,), F32),
        ],
        in_specs=[VMEM] * 5,
        out_specs=[VMEM, VMEM, pl.BlockSpec(memory_space=pltpu.SMEM)],
        scratch_shapes=[pltpu.VMEM((192, 128), F32), pltpu.VMEM((128, 160), F32)],
        compiler_params=limit(24),
        name="finish",
    )(own, other, own_start, other_start, guess)


def exchange(x, axis, bits):
    return lax.ppermute(x, axis, [(n, n ^ bits) for n in range(lax.axis_size(axis))])


def gathered_body(rhs, guess, kappa, bc_flags):
    rhs, guess = (jnp.transpose(v, (1, 2, 0, 3)) for v in (rhs, guess))
    halos = [exchange(guess, axis, bits) for axis in ("gx", "gy") for bits in (1, 3)]
    base = local_part(rhs, guess, kappa, bc_flags)
    mine, theirs = halo_part(base, halos)
    got = exchange(theirs, "section", 1)
    piece = jnp.concatenate([mine[:HALF] + got, mine[HALF:]])
    line = jnp.concatenate([piece] + [exchange(piece, "gx", bits) for bits in (1, 2, 3)])
    blocks = [line] + [exchange(line, "gy", bits) for bits in (1, 2, 3)]
    start = assemble(blocks)
    other_start = exchange(start, "section", 1)
    own, other_start = lax.optimization_barrier((cycle(blocks, start), other_start))
    sol, res, arnoldi = finish(own, exchange(own, "section", 1), start, other_start, guess)
    sol, res = (jnp.transpose(v, (2, 0, 1, 3)) for v in (sol, res))
    return sol, res, arnoldi


def solution(mesh):
    placed = (
        P("section", "gx", "gy", None),
        P("section", "gx", "gy", None),
        P("gx", "gy", None),
        P(None, "gx", "gy", None),
    )
    sizes = (mesh.shape["section"], mesh.shape["gx"], mesh.shape["gy"])

    def step(rhs, guess, kappa, bc_flags):
        fits = sizes == (2, 4, 4) and rhs.shape == (4, 20, 20, 160)
        return jax.shard_map(
            gathered_body if fits else stepwise,
            mesh=mesh,
            in_specs=placed,
            out_specs=(P("section", "gx", "gy", None), P("section", "gx", "gy", None), P()),
            check_vma=False,
        )(rhs, guess, kappa, bc_flags)

    return step
```

```python
from functools import partial
import math

import jax
import jax.numpy as jnp
import numpy as np
from jax import lax
from jax.experimental import pallas as pl
from jax.experimental.pallas import tpu as pltpu
from jax.sharding import PartitionSpec as P

ADVECT = (1.0, 0.7, 0.5)
DIFFUSE = 0.05
STEP_SIZE = 0.2
JACOBI_SCALE = 0.25
CHEB_LOW = 0.25
CHEB_HIGH = 2.0
LETTERS = "abcdef"


def extended(x, sides, width):
    for axis, dim in sides:
        peers, length = (lax.axis_size(axis), x.shape[dim])
        up = [(i, (i + 1) % peers) for i in range(peers)]
        down = [(j, i) for i, j in up]
        last = lax.slice_in_dim(x, length - width, length, axis=dim)
        leading = lax.slice_in_dim(x, 0, width, axis=dim)
        before = lax.ppermute(last, axis, up)
        after = lax.ppermute(leading, axis, down)
        x = jnp.concatenate([before, x, after], axis=dim)
    return x


def lobatto(count):
    if count == 5:
        inner = math.sqrt(3.0 / 7.0)
        return (
            np.array([-1.0, -inner, 0.0, inner, 1.0]),
            np.array([0.1, 49.0 / 90.0, 32.0 / 45.0, 49.0 / 90.0, 0.1]),
        )
    if count == 3:
        return (np.array([-1.0, 0.0, 1.0]), np.array([1.0 / 3.0, 4.0 / 3.0, 1.0 / 3.0]))
    return (np.array([-1.0, 1.0]), np.array([1.0, 1.0]))


def lagrange_table(nodes, points):
    table = np.ones((len(points), len(nodes)))
    for column in range(len(nodes)):
        for other in range(len(nodes)):
            if other != column:
                table[:, column] *= (points - nodes[other]) / (nodes[column] - nodes[other])
    return table


def slope_table(nodes):
    total = len(nodes)
    factor = np.array(
        [np.prod([nodes[i] - nodes[k] for k in range(total) if k != i]) for i in range(total)]
    )
    table = np.zeros((total, total))
    for row in range(total):
        for column in range(total):
            if row != column:
                table[row, column] = factor[row] / factor[column] / (nodes[row] - nodes[column])
        table[row, row] = -np.sum(table[row])
    return table


def element_matrix(count, direction):
    nodes, weights = lobatto(count)
    slopes = slope_table(nodes)
    stiffness = (1.0 / weights)[:, None] * (slopes.T @ (weights[:, None] * slopes))
    return ADVECT[direction] * slopes + DIFFUSE * stiffness


def legendre_pair(point, order):
    values = [1.0, point]
    slopes = [0.0, 1.0]
    for index in range(1, order):
        values.append(
            ((2 * index + 1) * point * values[index] - index * values[index - 1]) / (index + 1)
        )
        slopes.append(slopes[index - 1] + (2 * index + 1) * values[index])
    return (values, slopes)


def radau_nodes():
    starts = [0.0885879595127039, 0.4094668644407347, 0.7876594617608471]
    found = []
    for start in starts:
        point = start
        for sweep in range(30):
            values, slopes = legendre_pair(2.0 * point - 1.0, 4)
            change = (values[4] - values[3]) / (2.0 * (slopes[4] - slopes[3]))
            point = point - change
        found.append(point)
    found.append(1.0)
    return found


def poly_times(coefs, root):
    result = [0.0] * (len(coefs) + 1)
    for index in range(len(coefs)):
        result[index + 1] += coefs[index]
        result[index] -= root * coefs[index]
    return result


def radau_matrix():
    order = 4
    nodes = radau_nodes()
    matrix = np.zeros((order, order))
    for column in range(order):
        coefs = [1.0]
        denominator = 1.0
        for other in range(order):
            if other != column:
                coefs = poly_times(coefs, nodes[other])
                denominator *= nodes[column] - nodes[other]
        for row in range(order):
            upper_end = nodes[row]
            integral = 0.0
            for index in range(len(coefs)):
                integral += coefs[index] * upper_end ** (index + 1) / (index + 1)
            matrix[row, column] = integral / denominator
    return matrix


def node_einsum(table, field, axis):
    labels = LETTERS[: field.ndim]
    source = labels[: axis + 1] + "j" + labels[axis + 2 :]
    target = labels[: axis + 1] + "i" + labels[axis + 2 :]
    return jnp.einsum(
        "ij," + source + "->" + target,
        jnp.asarray(table, jnp.float32),
        field,
        precision=lax.Precision.HIGHEST,
    )


def apply_along(field, axis, count, table):
    shape = field.shape
    split = shape[:axis] + (shape[axis] // count, count) + shape[axis + 1 :]
    mapped = node_einsum(table, field.reshape(split), axis)
    return mapped.reshape(
        shape[:axis] + (mapped.shape[axis] * mapped.shape[axis + 1],) + shape[axis + 1 :]
    )


def line_part(field, axis, count, table, left_gain, right_gain, left_edge, right_edge):
    shape = field.shape
    elements = shape[axis] // count
    split = field.reshape(shape[:axis] + (elements, count) + shape[axis + 1 :])
    linear = node_einsum(table, split, axis)
    first = lax.index_in_dim(split, 0, axis + 1, keepdims=False)
    last = lax.index_in_dim(split, count - 1, axis + 1, keepdims=False)
    before = jnp.concatenate(
        [jnp.expand_dims(left_edge, axis), lax.slice_in_dim(last, 0, elements - 1, axis=axis)], axis
    )
    after = jnp.concatenate(
        [lax.slice_in_dim(first, 1, elements, axis=axis), jnp.expand_dims(right_edge, axis)], axis
    )
    front = jnp.expand_dims(left_gain * (first - before), axis + 1)
    back = jnp.expand_dims(right_gain * (last - after), axis + 1)
    if count > 2:
        middle_shape = list(front.shape)
        middle_shape[axis + 1] = count - 2
        pieces = [front, jnp.zeros(middle_shape, jnp.float32), back]
    else:
        pieces = [front, back]
    return (linear + jnp.concatenate(pieces, axis + 1)).reshape(shape)


def diag_along(shape, axis, count, table, left_gain, right_gain):
    elements = shape[axis] // count
    split = shape[:axis] + (elements, count) + shape[axis + 1 :]
    profile = [1] * len(split)
    profile[axis + 1] = count
    diagonal_entries = np.array([table[index, index] for index in range(count)])
    base = jnp.broadcast_to(jnp.asarray(diagonal_entries, jnp.float32).reshape(profile), split)
    front = jnp.expand_dims(left_gain, axis + 1)
    back = jnp.expand_dims(right_gain, axis + 1)
    if count > 2:
        middle_shape = list(front.shape)
        middle_shape[axis + 1] = count - 2
        pieces = [front, jnp.zeros(middle_shape, jnp.float32), back]
    else:
        pieces = [front, back]
    return (base + jnp.concatenate(pieces, axis + 1)).reshape(shape)


def level_kappa(kappa, count):
    if count == 5:
        return kappa
    picks = np.array([0, 2, 4]) if count == 3 else np.array([0, 4])
    extents = [extent // 5 for extent in kappa.shape]
    grouped = kappa.reshape(extents[0], 5, extents[1], 5, extents[2], 5)
    for axis in (1, 3, 5):
        grouped = jnp.take(grouped, picks, axis=axis)
    return grouped.reshape(extents[0] * count, extents[1] * count, extents[2] * count)


def face_plane(face, direction, count):
    plane = face.astype(jnp.float32)
    for axis in range(3):
        if axis != direction:
            plane = jnp.repeat(plane, count, axis=axis)
    return plane


def build_level(kappa, flags, count):
    nodes, weights = lobatto(count)
    kappa_level = level_kappa(kappa, count)
    tables, lefts, rights = ([], [], [])
    diagonal = kappa_level
    for direction in range(3):
        table = element_matrix(count, direction)
        lower = face_plane(flags[2 * direction], direction, count)
        upper = face_plane(flags[2 * direction + 1], direction, count)
        left_gain = (ADVECT[direction] * (1.0 + lower) / 2.0 + DIFFUSE * count * count) / float(
            weights[0]
        )
        right_gain = (DIFFUSE * count * count - ADVECT[direction] * (1.0 - upper) / 2.0) / float(
            weights[-1]
        )
        tables.append(table)
        lefts.append(left_gain)
        rights.append(right_gain)
        diagonal = diagonal + diag_along(
            kappa_level.shape, direction, count, table, left_gain, right_gain
        )
    scale = 1.0 / (1.0 + STEP_SIZE * JACOBI_SCALE * diagonal)
    return (count, tables, lefts, rights, kappa_level, scale)


def restrict(field, fine_count, coarse_count):
    fine_nodes, fine_weights = lobatto(fine_count)
    coarse_nodes, coarse_weights = lobatto(coarse_count)
    table = (
        (1.0 / coarse_weights)[:, None]
        * lagrange_table(coarse_nodes, fine_nodes).T
        * fine_weights[None, :]
    )
    for axis in range(field.ndim - 3, field.ndim):
        field = apply_along(field, axis, fine_count, table)
    return field


def prolong(field, coarse_count, fine_count):
    fine_nodes, fine_weights = lobatto(fine_count)
    coarse_nodes, coarse_weights = lobatto(coarse_count)
    table = lagrange_table(coarse_nodes, fine_nodes)
    for axis in range(field.ndim - 3, field.ndim):
        field = apply_along(field, axis, coarse_count, table)
    return field


def chebyshev(rhs, start, level, operator):
    centre = (CHEB_HIGH + CHEB_LOW) / 2.0
    radius = (CHEB_HIGH - CHEB_LOW) / 2.0
    ratio = centre / radius
    first_rho = 1.0 / ratio
    second_rho = 1.0 / (2.0 * ratio - first_rho)
    scale = level[5]
    if start is None:
        remain = rhs
    else:
        remain = rhs - operator(start, level)
    step = scale * remain / centre
    guess = step if start is None else start + step
    remain = remain - operator(step, level)
    step = second_rho * first_rho * step + 2.0 * second_rho / radius * scale * remain
    return guess + step


def vcycle(rhs, levels, operator):
    fine, middle, coarse = levels
    fine_x = chebyshev(rhs, None, fine, operator)
    middle_rhs = restrict(rhs - operator(fine_x, fine), 5, 3)
    middle_x = chebyshev(middle_rhs, None, middle, operator)
    coarse_rhs = restrict(middle_rhs - operator(middle_x, middle), 3, 2)
    coarse_x = chebyshev(coarse_rhs, None, coarse, operator)
    middle_x = chebyshev(middle_rhs, middle_x + prolong(coarse_x, 2, 3), middle, operator)
    return chebyshev(rhs, fine_x + prolong(middle_x, 3, 5), fine, operator)


def spatial(field, level):
    count, tables, lefts, rights, kappa_level, scale = level
    padded = extended(field, (("gx", 1), ("gy", 2)), 1)
    total = kappa_level * field
    total = total + line_part(
        field,
        1,
        count,
        tables[0],
        lefts[0],
        rights[0],
        padded[:, 0, 1:-1, :],
        padded[:, -1, 1:-1, :],
    )
    total = total + line_part(
        field,
        2,
        count,
        tables[1],
        lefts[1],
        rights[1],
        padded[:, 1:-1, 0, :],
        padded[:, 1:-1, -1, :],
    )
    total = total + line_part(
        field, 3, count, tables[2], lefts[2], rights[2], field[:, :, :, -1], field[:, :, :, 0]
    )
    return total


def apply_system(field, level, coupling):
    image = spatial(field, level)
    everyone = lax.all_gather(image, "section", axis=0, tiled=True)
    butcher = jnp.asarray(radau_matrix(), jnp.float32)
    rows = lax.dynamic_slice_in_dim(
        butcher, lax.axis_index("section") * field.shape[0], field.shape[0], 0
    )
    mixed = jnp.einsum("ij,jabc->iabc", rows, everyone, precision=lax.Precision.HIGHEST)
    return field + STEP_SIZE * mixed


def global_total(values):
    return lax.psum(values, ("section", "gx", "gy"))


def stepwise(rhs, guess, kappa, bc_flags):
    levels = [build_level(kappa, bc_flags, count) for count in (5, 3, 2)]
    section_operator = partial(apply_system, coupling=None)
    start_residual = rhs - section_operator(guess, levels[0])
    dofs = float(rhs.size * lax.axis_size("section") * lax.axis_size("gx") * lax.axis_size("gy"))
    beta = jnp.sqrt(global_total(jnp.sum(start_residual * start_residual).reshape(1))[0])
    basis = start_residual / beta
    precond = vcycle(basis, levels, section_operator)
    image = section_operator(precond, levels[0])
    upper = global_total(jnp.sum(image * basis).reshape(1))[0]
    remainder = image - upper * basis
    lower = jnp.sqrt(global_total(jnp.sum(remainder * remainder).reshape(1))[0])
    weight = beta * upper / (upper * upper + lower * lower)
    solution = guess + weight * precond
    residual = start_residual - weight * image
    arnoldi = jnp.stack([beta / math.sqrt(dofs), upper, lower]).astype(jnp.float32)
    return (solution, residual, arnoldi)


EZ = 32
COLS = 16
HALF = 64
PIECE = 96
FIELD = 1000
F32 = jnp.float32


def split_sections():
    matrix = radau_matrix()
    values, vectors = np.linalg.eig(matrix)
    order = [n for n in np.argsort(np.abs(values.imag), kind="stable") if values[n].imag > 0]
    bases = []
    for n in order:
        plane = np.stack([vectors[:, n].real, vectors[:, n].imag], axis=1)
        bases.append(np.linalg.qr(plane)[0])
    left, cross, right = np.linalg.svd(bases[0].T @ bases[1])
    bases = [bases[0] @ left, bases[1] @ right.T]
    for c in range(2):
        sign = np.sign(bases[0][np.argmax(np.abs(bases[0][:, c])), c])
        bases = [np.concatenate([b[:, :c], sign * b[:, c : c + 1], b[:, c + 1 :]], axis=1) for b in bases]
    whole = np.concatenate(bases, axis=1)
    back = np.linalg.inv(whole)
    return whole, back, back @ matrix, back @ matrix @ whole, cross


def iota(shape, dim):
    return lax.broadcasted_iota(jnp.int32, shape, dim)


def exact_dot(a, b):
    return lax.dot_general(
        a, b, (((1,), (0,)), ((), ())), precision=lax.Precision.HIGHEST, preferred_element_type=F32
    )


def split_dot(a, b):
    high = a.astype(jnp.bfloat16)
    rest = a - high.astype(F32)
    middle = rest.astype(jnp.bfloat16)
    low = (rest - middle.astype(F32)).astype(jnp.bfloat16)
    b = b.astype(jnp.bfloat16)
    return sum(
        lax.dot_general(part, b, (((1,), (0,)), ((), ())), preferred_element_type=F32)
        for part in (low, middle, high)
    )


def choose(index, values):
    out = values[-1]
    for place in range(len(values) - 2, -1, -1):
        out = jnp.where(index == place, values[place], out)
    return out


def face_gains(flag, direction, side, count):
    nodes, weights = lobatto(count)
    c, nu = ADVECT[direction], DIFFUSE * count * count
    if side == 0:
        return (c * (1.0 + flag) / 2.0 + nu) * (1.0 / float(weights[0]))
    return (nu - c * (1.0 - flag) / 2.0) * (1.0 / float(weights[-1]))


def column_tables():
    kx, ky, kz = (element_matrix(5, d) for d in range(3))
    rows = np.zeros((64, 64))
    for s in range(2):
        for i in range(5):
            for j in range(5):
                r = s * 32 + i * 5 + j
                for m in range(5):
                    rows[r, s * 32 + m * 5 + j] += kx[i, m]
                    rows[r, s * 32 + i * 5 + m] += ky[j, m]
    lines = np.zeros((160, 320))
    for e in range(EZ):
        lines[e * 5 : e * 5 + 5, e * 5 : e * 5 + 5] = kz.T
        lines[(e - 1) % EZ * 5 + 4, 160 + e * 5] = 1.0
        lines[(e + 1) % EZ * 5, 160 + e * 5 + 4] = 1.0
    return rows.astype(np.float32), lines.astype(np.float32)


def pick_line(k):
    return (iota((160, 128), 0) == 5 * (iota((160, 128), 1) % EZ) + k).astype(F32)


def pair_factors(sec, table, own, s):
    upper = iota((32, 128), 1) < 64
    first = jnp.where(upper, float(table[0, s]), float(table[1, s]))
    second = jnp.where(upper, float(table[2, 2 + s]), float(table[3, 2 + s]))
    if not own:
        first = jnp.where(upper, float(table[2, s]), float(table[3, s]))
        second = jnp.where(upper, float(table[0, 2 + s]), float(table[1, 2 + s]))
    return jnp.where(sec == 0, first, second)


def pack_nodes(nodes):
    odd = iota((HALF, 128), 1) // EZ % 2 == 1
    return jnp.where(odd, nodes[HALF:, :], nodes[:HALF, :])


def fetch(pairs, sems):
    copies = [pltpu.make_async_copy(src, dst, sems.at[n]) for n, (src, dst) in enumerate(pairs)]
    for copy in copies:
        copy.start()
    for copy in copies:
        copy.wait()


def local_kernel(
    rhs_in, guess_in, kappa_in, flags_in, rows_in, lines_in, base,
    rhs, guess, kappa, flags, rows_t, lines_t, sems, x, kap, stack, own_nodes, other_nodes, krep,
):
    sec = lax.axis_index("section")
    fetch(
        [(rhs_in, rhs), (guess_in, guess), (kappa_in, kappa), (flags_in, flags), (rows_in, rows_t), (lines_in, lines_t)],
        sems,
    )
    x[...] = jnp.zeros_like(x)
    kap[...] = jnp.zeros_like(kap)
    stack[...] = jnp.zeros_like(stack)
    for i in range(5):
        kap[5 * i : 5 * i + 5, :] = kappa[i]
        for j in range(5):
            r = 5 * i + j
            value = guess[i, j]
            left = rhs[i, j] - value
            for s in range(2):
                x[s * 32 + r : s * 32 + r + 1, :] = value[s : s + 1]
                stack[s * 32 + r : s * 32 + r + 1, :] = left[s : s + 1]
    flag = flags[:, 0, 0, :].astype(F32)
    spread = (iota((EZ, 160), 1) // 5 == iota((EZ, 160), 0)).astype(F32)
    wide = split_dot(flag, spread)
    gains = [face_gains(wide[d : d + 1, :], d // 2, d % 2, 5) for d in range(6)]
    row = iota((32, 160), 0)
    lane = iota((32, 160), 1) % 5
    none = jnp.zeros((32, 160), F32)
    gx = jnp.where(row < 5, gains[0], jnp.where((row >= 20) & (row < 25), gains[1], none))
    gy = jnp.where(row % 5 == 0, gains[2], jnp.where(row % 5 == 4, gains[3], none))
    gz = jnp.where(lane == 0, gains[4], jnp.where(lane == 4, gains[5], none))
    gy = jnp.where(row < 25, gy, none)
    for place, gain in ((160, gx), (192, gy)):
        base[place : place + 32, :] = gain[:, :128]
        base[64 + place : 96 + place, :EZ] = gain[:, 128:]
    field = x[...]
    along = exact_dot(rows_t[...], field)
    across = exact_dot(field, lines_t[...])
    own = kap[...] + gx + gy + gz
    for s in range(2):
        r = slice(s * 32, s * 32 + 32)
        image = own * field[r] + along[r] + across[r, :160] - gz * across[r, 160:]
        stack[64 + s * 32 : 96 + s * 32, :] = image
    whole, back, back_matrix, blocks, cross = split_sections()
    own_nodes[...] = jnp.zeros_like(own_nodes)
    other_nodes[...] = jnp.zeros_like(other_nodes)
    krep[...] = jnp.zeros_like(krep)
    stack[128:, :] = kap[...]
    source = stack[...]
    for k in range(5):
        parts = split_dot(source, pick_line(k))
        for target, mark in ((own_nodes, True), (other_nodes, False)):
            total = jnp.zeros((32, 128), F32)
            for s in range(2):
                total = total + pair_factors(sec, back, mark, s) * parts[s * 32 : s * 32 + 32]
                factor = pair_factors(sec, -STEP_SIZE * back_matrix, mark, s)
                total = total + factor * parts[64 + s * 32 : 96 + s * 32]
            target[25 * k : 25 * k + 25, :] = total[:25]
        krep[25 * k : 25 * k + 25, :] = parts[128:153]
    repeat = (iota((EZ, 128), 1) % EZ == iota((EZ, 128), 0)).astype(F32)
    shown = split_dot(flag, repeat)
    upper = iota((1, 128), 1) < 64
    for r in range(3):
        own_nodes[125 + r : 126 + r, :] = jnp.where(upper, shown[2 * r : 2 * r + 1], shown[2 * r + 1 : 2 * r + 2])
    base[:HALF, :] = pack_nodes(own_nodes)
    base[PIECE : PIECE + HALF, :] = pack_nodes(other_nodes)
    base[HALF:PIECE, :] = choose(iota((32, 128), 1) // EZ, [krep[32 * q : 32 * q + 32, :] for q in range(4)])


def halo_kernel(base, x1, x3, y1, y3, mine, theirs, near, own_nodes, other_nodes):
    sec = lax.axis_index("section")
    even_x = lax.axis_index("gx") % 2 == 0
    even_y = lax.axis_index("gy") % 2 == 0
    for ref in (near, own_nodes, other_nodes):
        ref[...] = jnp.zeros_like(ref)
    for m in range(5):
        for s in range(2):
            r = s * 32
            one = slice(s, s + 1)
            near[r + m : r + m + 1, :] = jnp.where(even_x, x3[4, m, one, :], x1[4, m, one, :])
            near[r + 20 + m : r + 21 + m, :] = jnp.where(even_x, x1[0, m, one, :], x3[0, m, one, :])
            r += 64
            near[r + 5 * m : r + 5 * m + 1, :] = jnp.where(even_y, y3[m, 4, one, :], y1[m, 4, one, :])
            near[r + 5 * m + 4 : r + 5 * m + 5, :] = jnp.where(even_y, y1[m, 0, one, :], y3[m, 0, one, :])
    gx, gy = (
        jnp.concatenate([base[r : r + 32, :], base[64 + r : 96 + r, :EZ]], axis=1) for r in (160, 192)
    )
    parts_in = []
    for s in range(2):
        r = s * 32
        parts_in.append(gx * near[r : r + 32, :] + gy * near[64 + r : 96 + r, :])
    source = jnp.concatenate(parts_in, axis=0)
    back_matrix = split_sections()[2]
    for k in range(5):
        parts = split_dot(source, pick_line(k))
        for target, mark in ((own_nodes, True), (other_nodes, False)):
            total = jnp.zeros((32, 128), F32)
            for s in range(2):
                factor = pair_factors(sec, STEP_SIZE * back_matrix, mark, s)
                total = total + factor * parts[s * 32 : s * 32 + 32]
            target[25 * k : 25 * k + 25, :] = total[:25]
    mine[:HALF, :] = base[:HALF, :] + pack_nodes(own_nodes)
    mine[HALF:, :] = base[HALF:PIECE, :]
    theirs[...] = base[PIECE : PIECE + HALF, :] + pack_nodes(other_nodes)


VMEM = pl.BlockSpec(memory_space=pltpu.VMEM)
HBM = pl.BlockSpec(memory_space=pltpu.HBM)


def limit(mib):
    return pltpu.CompilerParams(vmem_limit_bytes=mib * 2**20)


def local_part(rhs, guess, kappa, flags):
    rows_t, lines_t = column_tables()
    operands = (rhs, guess, kappa, flags, jnp.asarray(rows_t), jnp.asarray(lines_t))
    return pl.pallas_call(
        local_kernel,
        out_shape=jax.ShapeDtypeStruct((288, 128), F32),
        in_specs=[HBM] * 6,
        out_specs=VMEM,
        scratch_shapes=[pltpu.VMEM(o.shape, o.dtype) for o in operands]
        + [
            pltpu.SemaphoreType.DMA((6,)),
            pltpu.VMEM((64, 160), F32),
            pltpu.VMEM((32, 160), F32),
            pltpu.VMEM((160, 160), F32),
            pltpu.VMEM((128, 128), F32),
            pltpu.VMEM((128, 128), F32),
            pltpu.VMEM((128, 128), F32),
        ],
        compiler_params=limit(60),
        name="local_part",
    )(*operands)


def halo_part(base, halos):
    return pl.pallas_call(
        halo_kernel,
        out_shape=[
            jax.ShapeDtypeStruct((PIECE, 128), F32),
            jax.ShapeDtypeStruct((HALF, 128), F32),
        ],
        in_specs=[VMEM] * 5,
        out_specs=[VMEM] * 2,
        scratch_shapes=[pltpu.VMEM((128, 160), F32)] + [pltpu.VMEM((128, 128), F32)] * 2,
        compiler_params=limit(16),
        name="halo_part",
    )(base, *halos)


class Level:
    def __init__(self, count, refs):
        self.count = count
        self.diag, self.jac, self.x, self.dir, self.res, self.f = refs
        self.tables = [element_matrix(count, d) for d in range(3)]
        self.gains = None


def tile(index):
    return pl.ds(index * 8, 8)


def rows_of(pieces, size, r, h):
    return pieces[pl.ds(8 * h * size + r, 8, stride=size), :]


def place_pieces(blocks, pieces, first, size):
    my_gx, my_gy = lax.axis_index("gx"), lax.axis_index("gy")
    for b, block in enumerate(blocks):
        for a in range(4):
            column = (my_gx ^ a) * 4 + (my_gy ^ b)
            start = pl.multiple_of(column * size, 8)
            pieces[pl.ds(start, size), :] = block[a * PIECE + first : a * PIECE + first + size, :]


def assemble_kernel(block0, block1, block2, block3, field, pieces):
    place_pieces((block0, block1, block2, block3), pieces, 0, HALF)
    odd = iota((8, 128), 1) // EZ % 2 == 1
    for r in range(HALF):
        low, high = rows_of(pieces, HALF, r, 0), rows_of(pieces, HALF, r, 1)
        field[tile(r), :] = jnp.where(odd, pltpu.roll(high, 32, 1), low)
        field[tile(HALF + r), :] = jnp.where(odd, high, pltpu.roll(low, 96, 1))


def load(ref, first, count):
    start = first * 8 if isinstance(first, int) else pl.multiple_of(first * 8, 8)
    return ref[pl.ds(start, count * 8), :].reshape(count, 8, 128)


def store(ref, first, value):
    start = first * 8 if isinstance(first, int) else pl.multiple_of(first * 8, 8)
    ref[pl.ds(start, value.shape[0] * 8), :] = value.reshape(value.shape[0] * 8, 128)


def cycle_kernel(block0, block1, block2, block3, assembled, fields, *scratch):
    sec = lax.axis_index("section")
    my_gx, my_gy = lax.axis_index("gx"), lax.axis_index("gy")
    levels = [Level(n, scratch[6 * p : 6 * p + 6]) for p, n in enumerate((5, 3, 2))]
    pieces, kap, half, terms = scratch[18:22]
    lane = iota((8, 128), 1)
    sub = iota((8, 128), 0)
    group = lane // EZ
    odd = group % 2 == 1
    element = lane % EZ
    place = sub % 4
    low_half = sub < 4
    blocks = split_sections()[3]

    def lanes_of(upper, lower):
        return jnp.where(lane < 64, jnp.where(sec == 0, upper[0], upper[1]), jnp.where(sec == 0, lower[0], lower[1]))

    entry = [[[float(STEP_SIZE * blocks[2 * p + a, 2 * p + b]) for p in range(2)] for b in range(2)] for a in range(2)]
    same = lanes_of(entry[0][0], entry[1][1])
    swap = lanes_of(entry[0][1], entry[1][0])
    centre = (CHEB_HIGH + CHEB_LOW) / 2.0
    radius = (CHEB_HIGH - CHEB_LOW) / 2.0
    first_rho = radius / centre
    second_rho = 1.0 / (2.0 * centre / radius - first_rho)
    keep = 1.0 + second_rho * first_rho
    push = 2.0 * second_rho / radius * centre

    flags = []
    for r in range(3):
        got = assembled[tile(125 + r), :]
        across = pltpu.roll(got, 64, 1)
        flags += [jnp.where(lane < 64, got, across), jnp.where(lane < 64, across, got)]
    place_pieces((block0, block1, block2, block3), pieces, HALF, 32)

    for r in range(32):
        turned = []
        for h in range(2):
            got = rows_of(pieces, 32, r, h)
            turned.append([pltpu.roll(got, 32 * m, 1) if m else got for m in range(4)])
        for q in range(4):
            kap[tile(q * 32 + r), :] = choose(group, [turned[g % 2][(g - q) % 4] for g in range(4)])

    for level in levels:
        n = level.count
        stride = 4 // (n - 1)
        level.gains = [face_gains(flags[d], d // 2, d % 2, n) for d in range(6)]
        rows = []
        for d in range(3):
            row = [jnp.full((8, 128), float(level.tables[d][m, m]), F32) for m in range(n)]
            row[0] = row[0] + level.gains[2 * d]
            row[n - 1] = row[n - 1] + level.gains[2 * d + 1]
            rows.append(row)
        for m in range(n):
            terms[tile(m), :] = rows[2][m]

        def diagonals(k, carry, level=level, n=n, stride=stride, rows=rows):
            along = jnp.stack(rows[1])
            for i in range(n):
                line = load(kap, k * 25 * stride + i * stride * 5, 5)
                line = jnp.stack([line[j * stride] for j in range(n)])
                value = line + (along + (load(terms, k, 1) + rows[0][i]))
                scale = 1.0 / (1.0 + STEP_SIZE * JACOBI_SCALE * value)
                store(level.diag, (k * n + i) * n, value)
                store(level.jac, (k * n + i) * n, scale * (1.0 / centre))
            return carry
        lax.fori_loop(0, n, diagonals, 0)

    def begin(level, source):
        n = level.count

        def start(k, carry):
            first = k * n * n
            f = load(source, first, n * n)
            store(level.dir, first, load(level.jac, first, n * n) * f)
            store(level.res, first, f)
            store(level.x, first, jnp.zeros_like(f))
            return carry
        lax.fori_loop(0, n, start, 0)

    def apply(level, smooth):
        n = level.count
        kx, ky, kz = level.tables
        source = level.dir if smooth else level.x

        def around(u):
            turned = pltpu.roll(u, 4, 1)
            return turned, jnp.where(odd, pltpu.roll(turned, 32, 2), pltpu.roll(turned, 96, 2))

        for k in range(n):
            here = k * n * n
            v = [load(source, here + i * n, n) for i in range(n)]
            left, left_far = around(v[n - 1])
            right, right_far = around(v[0])
            waiting = []
            for i in range(n):
                first = here + i * n
                total = load(level.diag, first, n) * v[i]
                for m in range(n):
                    if m != i:
                        total = total + float(kx[i, m]) * v[m]
                for m in range(n):
                    if m != k:
                        total = total + float(kz[k, m]) * load(source, (m * n + i) * n, n)
                lines = []
                for j in range(n):
                    line = None
                    for m in range(n):
                        if m != j:
                            term = float(ky[j, m]) * v[i][m]
                            line = term if line is None else line + term
                    if j == 0:
                        u = v[i][n - 1]
                        moved = jnp.where(place == 0, pltpu.roll(u, 5, 0), pltpu.roll(u, 1, 0))
                        line = line - level.gains[2] * moved
                    if j == n - 1:
                        u = v[i][0]
                        moved = jnp.where(place == 3, pltpu.roll(u, 3, 0), pltpu.roll(u, 7, 0))
                        line = line - level.gains[3] * moved
                    lines.append(line)
                total = total + jnp.stack(lines)
                if i == 0:
                    total = total - level.gains[0] * jnp.where(low_half, left_far, left)
                if i == n - 1:
                    total = total - level.gains[1] * jnp.where(low_half, right, right_far)
                if k == 0:
                    u = load(source, ((n - 1) * n + i) * n, n)
                    moved = jnp.where(element == 0, pltpu.roll(u, 97, 2), pltpu.roll(u, 1, 2))
                    total = total - level.gains[4] * moved
                if k == n - 1:
                    u = load(source, i * n, n)
                    moved = jnp.where(element == EZ - 1, pltpu.roll(u, 31, 2), pltpu.roll(u, 127, 2))
                    total = total - level.gains[5] * moved
                image = v[i] + (same * total + swap * pltpu.roll(total, 64, 2))
                if smooth:
                    scaled = load(level.jac, first, n) * (load(level.res, first, n) - image)
                    waiting.append((level.x, first, load(level.x, first, n) + keep * v[i] + push * scaled))
                else:
                    rest = load(level.f, first, n) - image
                    waiting.append((level.res, first, rest))
                    waiting.append((level.dir, first, load(level.jac, first, n) * rest))
                if i % 2 == 1 or i == n - 1:
                    for place_out in waiting:
                        store(*place_out)
                    waiting = []

    def combine(weights, parts):
        total = None
        for weight, part in zip(weights, parts):
            if abs(weight) > 1e-14:
                term = part if abs(weight - 1.0) < 1e-14 else float(weight) * part
                total = term if total is None else total + term
        return total

    def change(table, source, target, add):
        m, n = table.shape

        def outer(i, carry):
            parts = [load(source, i * n + k * n * n, n) for k in range(n)]
            for k in range(m):
                store(half, i * n + k * n * n, combine(table[k], parts))
            return carry
        lax.fori_loop(0, n, outer, 0)

        def inner(k, carry):
            parts = [load(half, k * n * n + i * n, n) for i in range(n)]
            for i in range(m):
                line = combine(table[i], parts)
                value = jnp.stack([combine(table[j], [line[a] for a in range(n)]) for j in range(m)])
                first = k * m * m + i * m
                store(target, first, load(target, first, m) + value if add else value)
            return carry
        lax.fori_loop(0, m, inner, 0)

    def down(n, m):
        fine_nodes, fine_weights = lobatto(n)
        coarse_nodes, coarse_weights = lobatto(m)
        table = lagrange_table(coarse_nodes, fine_nodes)
        return (1.0 / coarse_weights)[:, None] * table.T * fine_weights[None, :]

    def up(m, n):
        return lagrange_table(lobatto(m)[0], lobatto(n)[0])

    def solve(p):
        level = levels[p]
        if p == 2:
            apply(level, True)
            return
        below = levels[p + 1]

        def step(t, carry):
            @pl.when(t != 1)
            def _():
                apply(level, True)

            @pl.when((t != 2) | (p == 0))
            def _():
                apply(level, False)

            @pl.when(t == 0)
            def _():
                n, m = level.count, below.count
                change(down(n, m), level.res, below.f, False)
                begin(below, below.f)
                solve(p + 1)
                change(up(m, n), below.x, level.x, True)
            return carry
        lax.fori_loop(0, 3, step, 0)

    fine = levels[0]
    fine.f = assembled
    begin(fine, assembled)
    solve(0)

    def give(k, carry):
        store(fields, k * 25, load(fine.res, k * 25, 25))
        return carry
    lax.fori_loop(0, 5, give, 0)
    column = (my_gx % 2) * 4 + my_gy
    fields[FIELD : FIELD + 125, :] = fine.x[pl.ds(column, 125, stride=8), :]
    fields[FIELD + 125 : FIELD + 128, :] = jnp.zeros((3, 128), F32)


def finish_kernel(own, other, own_start, other_start, guess, sol, res_out, arnoldi, cols, outs):
    sec = lax.axis_index("section")
    my_gx, my_gy = lax.axis_index("gx"), lax.axis_index("gy")
    whole, back, back_matrix, blocks, cross = split_sections()
    weights = jnp.where(iota((8, 128), 1) < 64, float(cross[0]), float(cross[1]))
    nothing = jnp.zeros((8, 128), F32)

    lane = iota((32, 128), 1)
    here = lane // EZ % 2 == my_gx // 2
    factors = []
    for s in range(2):
        row = []
        for p in range(2):
            parts = []
            for mine in range(2):
                t = whole[2 * mine + s]
                pairs = [jnp.where(lane < 64, float(t[2 * q]), float(t[2 * q + 1])) for q in range(2)]
                parts.append(pairs[mine] if p == 0 else pairs[1 - mine])
            row.append(jnp.where(here, jnp.where(sec == 0, parts[0], parts[1]), 0.0)[:25])
        factors.append(row)
    column = (my_gx % 2) * 4 + my_gy
    cols[...] = jnp.zeros_like(cols)
    total = jnp.zeros((192, 160), F32)
    for k in range(5):
        where = pl.ds(k * 200 + column, 25, stride=8)
        shown = [[ref[FIELD + k * 25 : FIELD + k * 25 + 25, :] for ref in (own, other)]]
        shown.append([ref[where, :] for ref in (own_start, other_start)])
        shown.append([b[where, :] - a[where, :] for a, b in ((own, own_start), (other, other_start))])
        for f, (a, b) in enumerate(shown):
            for s in range(2):
                r = f * 64 + s * 32
                cols[r : r + 25, :] = factors[s][0] * a + factors[s][1] * b
        hit = (iota((128, 160), 1) == 5 * (iota((128, 160), 0) % EZ) + k).astype(F32)
        total = total + split_dot(cols[...], hit)

    def product(a, b, c, d):
        return (a * c + b * d) + weights * (a * d + b * c)

    uppers, sizes = [nothing] * 5, [nothing] * 5
    for r in range(125):
        a, b, c, d = (ref[tile(r), :] for ref in (own, other, own_start, other_start))
        a, b = c - a, d - b
        uppers[r % 5] = uppers[r % 5] + product(a, b, c, d)
        sizes[r % 5] = sizes[r % 5] + product(c, d, c, d)
    size = jnp.sum(sum(sizes), keepdims=True)
    upper = jnp.sum(sum(uppers), keepdims=True) / size
    rests = [nothing] * 5
    for r in range(125):
        a, b, c, d = (ref[tile(r), :] for ref in (own, other, own_start, other_start))
        a, b = c - a, d - b
        a, b = a - upper * c, b - upper * d
        rests[r % 5] = rests[r % 5] + product(a, b, a, b)
    rest = jnp.sum(sum(rests), keepdims=True)
    beta = jnp.sqrt(size)
    lower = jnp.sqrt(rest) / beta
    weight = upper / (upper * upper + lower * lower)
    entries = float(125 * EZ * COLS * 4)
    for place_out, value in enumerate((beta * (1.0 / math.sqrt(entries)), upper, lower)):
        arnoldi[place_out] = value[0, 0]
    outs[:64, :] = weight * total[:64]
    outs[64:, :] = total[64:128] - weight * total[128:]
    for i in range(5):
        for j in range(5):
            r = 5 * i + j
            for s in range(2):
                sol[i, j, s : s + 1, :] = guess[i, j, s : s + 1, :] + outs[s * 32 + r : s * 32 + r + 1, :]
                res_out[i, j, s : s + 1, :] = outs[64 + s * 32 + r : 64 + s * 32 + r + 1, :]


def assemble(blocks):
    return pl.pallas_call(
        assemble_kernel,
        out_shape=jax.ShapeDtypeStruct((128 * 8, 128), F32),
        in_specs=[VMEM] * 4,
        out_specs=VMEM,
        scratch_shapes=[pltpu.VMEM((COLS * HALF, 128), F32)],
        compiler_params=limit(16),
        name="assemble",
    )(*blocks)


def cycle(blocks, assembled):
    scratch = []
    for n in (5, 3, 2):
        scratch += [pltpu.VMEM((n**3 * 8, 128), F32)] * 6
    scratch += [
        pltpu.VMEM((COLS * 32, 128), F32),
        pltpu.VMEM((128 * 8, 128), F32),
        pltpu.VMEM((FIELD, 128), F32),
        pltpu.VMEM((15 * 8, 128), F32),
    ]
    return pl.pallas_call(
        cycle_kernel,
        out_shape=jax.ShapeDtypeStruct((FIELD + 128, 128), F32),
        in_specs=[VMEM] * 5,
        out_specs=VMEM,
        scratch_shapes=scratch,
        compiler_params=limit(24),
        cost_estimate=pl.CostEstimate(flops=40_000_000, bytes_accessed=30_000_000, transcendentals=0),
        name="cycle",
    )(*blocks, assembled)


def finish(own, other, own_start, other_start, guess):
    return pl.pallas_call(
        finish_kernel,
        out_shape=[
            jax.ShapeDtypeStruct(guess.shape, F32),
            jax.ShapeDtypeStruct(guess.shape, F32),
            jax.ShapeDtypeStruct((3,), F32),
        ],
        in_specs=[VMEM] * 5,
        out_specs=[VMEM, VMEM, pl.BlockSpec(memory_space=pltpu.SMEM)],
        scratch_shapes=[pltpu.VMEM((192, 128), F32), pltpu.VMEM((128, 160), F32)],
        compiler_params=limit(24),
        name="finish",
    )(own, other, own_start, other_start, guess)


def exchange(x, axis, bits):
    return lax.ppermute(x, axis, [(n, n ^ bits) for n in range(lax.axis_size(axis))])


def gathered_body(rhs, guess, kappa, bc_flags):
    rhs, guess = (jnp.transpose(v, (1, 2, 0, 3)) for v in (rhs, guess))
    halos = [exchange(guess, axis, bits) for axis in ("gx", "gy") for bits in (1, 3)]
    base = local_part(rhs, guess, kappa, bc_flags)
    mine, theirs = halo_part(base, halos)
    got = exchange(theirs, "section", 1)
    piece = jnp.concatenate([mine[:HALF] + got, mine[HALF:]])
    line = jnp.concatenate([piece] + [exchange(piece, "gx", bits) for bits in (1, 2, 3)])
    blocks = [line] + [exchange(line, "gy", bits) for bits in (1, 2, 3)]
    start = assemble(blocks)
    other_start = exchange(start, "section", 1)
    own, other_start = lax.optimization_barrier((cycle(blocks, start), other_start))
    sol, res, arnoldi = finish(own, exchange(own, "section", 1), start, other_start, guess)
    sol, res = (jnp.transpose(v, (2, 0, 1, 3)) for v in (sol, res))
    return sol, res, arnoldi


def solution(mesh):
    placed = (
        P("section", "gx", "gy", None),
        P("section", "gx", "gy", None),
        P("gx", "gy", None),
        P(None, "gx", "gy", None),
    )
    sizes = (mesh.shape["section"], mesh.shape["gx"], mesh.shape["gy"])

    def step(rhs, guess, kappa, bc_flags):
        fits = sizes == (2, 4, 4) and rhs.shape == (4, 20, 20, 160)
        return jax.shard_map(
            gathered_body if fits else stepwise,
            mesh=mesh,
            in_specs=placed,
            out_specs=(P("section", "gx", "gy", None), P("section", "gx", "gy", None), P()),
            check_vma=False,
        )(rhs, guess, kappa, bc_flags)

    return step
```

```python
from functools import partial
import math

import jax
import jax.numpy as jnp
import numpy as np
from jax import lax
from jax.experimental import pallas as pl
from jax.experimental.pallas import tpu as pltpu
from jax.sharding import PartitionSpec as P

ADVECT = (1.0, 0.7, 0.5)
DIFFUSE = 0.05
STEP_SIZE = 0.2
JACOBI_SCALE = 0.25
CHEB_LOW = 0.25
CHEB_HIGH = 2.0
LETTERS = "abcdef"


def extended(x, sides, width):
    for axis, dim in sides:
        peers, length = (lax.axis_size(axis), x.shape[dim])
        up = [(i, (i + 1) % peers) for i in range(peers)]
        down = [(j, i) for i, j in up]
        last = lax.slice_in_dim(x, length - width, length, axis=dim)
        leading = lax.slice_in_dim(x, 0, width, axis=dim)
        before = lax.ppermute(last, axis, up)
        after = lax.ppermute(leading, axis, down)
        x = jnp.concatenate([before, x, after], axis=dim)
    return x


def lobatto(count):
    if count == 5:
        inner = math.sqrt(3.0 / 7.0)
        return (
            np.array([-1.0, -inner, 0.0, inner, 1.0]),
            np.array([0.1, 49.0 / 90.0, 32.0 / 45.0, 49.0 / 90.0, 0.1]),
        )
    if count == 3:
        return (np.array([-1.0, 0.0, 1.0]), np.array([1.0 / 3.0, 4.0 / 3.0, 1.0 / 3.0]))
    return (np.array([-1.0, 1.0]), np.array([1.0, 1.0]))


def lagrange_table(nodes, points):
    table = np.ones((len(points), len(nodes)))
    for column in range(len(nodes)):
        for other in range(len(nodes)):
            if other != column:
                table[:, column] *= (points - nodes[other]) / (nodes[column] - nodes[other])
    return table


def slope_table(nodes):
    total = len(nodes)
    factor = np.array(
        [np.prod([nodes[i] - nodes[k] for k in range(total) if k != i]) for i in range(total)]
    )
    table = np.zeros((total, total))
    for row in range(total):
        for column in range(total):
            if row != column:
                table[row, column] = factor[row] / factor[column] / (nodes[row] - nodes[column])
        table[row, row] = -np.sum(table[row])
    return table


def element_matrix(count, direction):
    nodes, weights = lobatto(count)
    slopes = slope_table(nodes)
    stiffness = (1.0 / weights)[:, None] * (slopes.T @ (weights[:, None] * slopes))
    return ADVECT[direction] * slopes + DIFFUSE * stiffness


def legendre_pair(point, order):
    values = [1.0, point]
    slopes = [0.0, 1.0]
    for index in range(1, order):
        values.append(
            ((2 * index + 1) * point * values[index] - index * values[index - 1]) / (index + 1)
        )
        slopes.append(slopes[index - 1] + (2 * index + 1) * values[index])
    return (values, slopes)


def radau_nodes():
    starts = [0.0885879595127039, 0.4094668644407347, 0.7876594617608471]
    found = []
    for start in starts:
        point = start
        for sweep in range(30):
            values, slopes = legendre_pair(2.0 * point - 1.0, 4)
            change = (values[4] - values[3]) / (2.0 * (slopes[4] - slopes[3]))
            point = point - change
        found.append(point)
    found.append(1.0)
    return found


def poly_times(coefs, root):
    result = [0.0] * (len(coefs) + 1)
    for index in range(len(coefs)):
        result[index + 1] += coefs[index]
        result[index] -= root * coefs[index]
    return result


def radau_matrix():
    order = 4
    nodes = radau_nodes()
    matrix = np.zeros((order, order))
    for column in range(order):
        coefs = [1.0]
        denominator = 1.0
        for other in range(order):
            if other != column:
                coefs = poly_times(coefs, nodes[other])
                denominator *= nodes[column] - nodes[other]
        for row in range(order):
            upper_end = nodes[row]
            integral = 0.0
            for index in range(len(coefs)):
                integral += coefs[index] * upper_end ** (index + 1) / (index + 1)
            matrix[row, column] = integral / denominator
    return matrix


def node_einsum(table, field, axis):
    labels = LETTERS[: field.ndim]
    source = labels[: axis + 1] + "j" + labels[axis + 2 :]
    target = labels[: axis + 1] + "i" + labels[axis + 2 :]
    return jnp.einsum(
        "ij," + source + "->" + target,
        jnp.asarray(table, jnp.float32),
        field,
        precision=lax.Precision.HIGHEST,
    )


def apply_along(field, axis, count, table):
    shape = field.shape
    split = shape[:axis] + (shape[axis] // count, count) + shape[axis + 1 :]
    mapped = node_einsum(table, field.reshape(split), axis)
    return mapped.reshape(
        shape[:axis] + (mapped.shape[axis] * mapped.shape[axis + 1],) + shape[axis + 1 :]
    )


def line_part(field, axis, count, table, left_gain, right_gain, left_edge, right_edge):
    shape = field.shape
    elements = shape[axis] // count
    split = field.reshape(shape[:axis] + (elements, count) + shape[axis + 1 :])
    linear = node_einsum(table, split, axis)
    first = lax.index_in_dim(split, 0, axis + 1, keepdims=False)
    last = lax.index_in_dim(split, count - 1, axis + 1, keepdims=False)
    before = jnp.concatenate(
        [jnp.expand_dims(left_edge, axis), lax.slice_in_dim(last, 0, elements - 1, axis=axis)], axis
    )
    after = jnp.concatenate(
        [lax.slice_in_dim(first, 1, elements, axis=axis), jnp.expand_dims(right_edge, axis)], axis
    )
    front = jnp.expand_dims(left_gain * (first - before), axis + 1)
    back = jnp.expand_dims(right_gain * (last - after), axis + 1)
    if count > 2:
        middle_shape = list(front.shape)
        middle_shape[axis + 1] = count - 2
        pieces = [front, jnp.zeros(middle_shape, jnp.float32), back]
    else:
        pieces = [front, back]
    return (linear + jnp.concatenate(pieces, axis + 1)).reshape(shape)


def diag_along(shape, axis, count, table, left_gain, right_gain):
    elements = shape[axis] // count
    split = shape[:axis] + (elements, count) + shape[axis + 1 :]
    profile = [1] * len(split)
    profile[axis + 1] = count
    diagonal_entries = np.array([table[index, index] for index in range(count)])
    base = jnp.broadcast_to(jnp.asarray(diagonal_entries, jnp.float32).reshape(profile), split)
    front = jnp.expand_dims(left_gain, axis + 1)
    back = jnp.expand_dims(right_gain, axis + 1)
    if count > 2:
        middle_shape = list(front.shape)
        middle_shape[axis + 1] = count - 2
        pieces = [front, jnp.zeros(middle_shape, jnp.float32), back]
    else:
        pieces = [front, back]
    return (base + jnp.concatenate(pieces, axis + 1)).reshape(shape)


def level_kappa(kappa, count):
    if count == 5:
        return kappa
    picks = np.array([0, 2, 4]) if count == 3 else np.array([0, 4])
    extents = [extent // 5 for extent in kappa.shape]
    grouped = kappa.reshape(extents[0], 5, extents[1], 5, extents[2], 5)
    for axis in (1, 3, 5):
        grouped = jnp.take(grouped, picks, axis=axis)
    return grouped.reshape(extents[0] * count, extents[1] * count, extents[2] * count)


def face_plane(face, direction, count):
    plane = face.astype(jnp.float32)
    for axis in range(3):
        if axis != direction:
            plane = jnp.repeat(plane, count, axis=axis)
    return plane


def build_level(kappa, flags, count):
    nodes, weights = lobatto(count)
    kappa_level = level_kappa(kappa, count)
    tables, lefts, rights = ([], [], [])
    diagonal = kappa_level
    for direction in range(3):
        table = element_matrix(count, direction)
        lower = face_plane(flags[2 * direction], direction, count)
        upper = face_plane(flags[2 * direction + 1], direction, count)
        left_gain = (ADVECT[direction] * (1.0 + lower) / 2.0 + DIFFUSE * count * count) / float(
            weights[0]
        )
        right_gain = (DIFFUSE * count * count - ADVECT[direction] * (1.0 - upper) / 2.0) / float(
            weights[-1]
        )
        tables.append(table)
        lefts.append(left_gain)
        rights.append(right_gain)
        diagonal = diagonal + diag_along(
            kappa_level.shape, direction, count, table, left_gain, right_gain
        )
    scale = 1.0 / (1.0 + STEP_SIZE * JACOBI_SCALE * diagonal)
    return (count, tables, lefts, rights, kappa_level, scale)


def restrict(field, fine_count, coarse_count):
    fine_nodes, fine_weights = lobatto(fine_count)
    coarse_nodes, coarse_weights = lobatto(coarse_count)
    table = (
        (1.0 / coarse_weights)[:, None]
        * lagrange_table(coarse_nodes, fine_nodes).T
        * fine_weights[None, :]
    )
    for axis in range(field.ndim - 3, field.ndim):
        field = apply_along(field, axis, fine_count, table)
    return field


def prolong(field, coarse_count, fine_count):
    fine_nodes, fine_weights = lobatto(fine_count)
    coarse_nodes, coarse_weights = lobatto(coarse_count)
    table = lagrange_table(coarse_nodes, fine_nodes)
    for axis in range(field.ndim - 3, field.ndim):
        field = apply_along(field, axis, coarse_count, table)
    return field


def chebyshev(rhs, start, level, operator):
    centre = (CHEB_HIGH + CHEB_LOW) / 2.0
    radius = (CHEB_HIGH - CHEB_LOW) / 2.0
    ratio = centre / radius
    first_rho = 1.0 / ratio
    second_rho = 1.0 / (2.0 * ratio - first_rho)
    scale = level[5]
    if start is None:
        remain = rhs
    else:
        remain = rhs - operator(start, level)
    step = scale * remain / centre
    guess = step if start is None else start + step
    remain = remain - operator(step, level)
    step = second_rho * first_rho * step + 2.0 * second_rho / radius * scale * remain
    return guess + step


def vcycle(rhs, levels, operator):
    fine, middle, coarse = levels
    fine_x = chebyshev(rhs, None, fine, operator)
    middle_rhs = restrict(rhs - operator(fine_x, fine), 5, 3)
    middle_x = chebyshev(middle_rhs, None, middle, operator)
    coarse_rhs = restrict(middle_rhs - operator(middle_x, middle), 3, 2)
    coarse_x = chebyshev(coarse_rhs, None, coarse, operator)
    middle_x = chebyshev(middle_rhs, middle_x + prolong(coarse_x, 2, 3), middle, operator)
    return chebyshev(rhs, fine_x + prolong(middle_x, 3, 5), fine, operator)


def spatial(field, level):
    count, tables, lefts, rights, kappa_level, scale = level
    padded = extended(field, (("gx", 1), ("gy", 2)), 1)
    total = kappa_level * field
    total = total + line_part(
        field,
        1,
        count,
        tables[0],
        lefts[0],
        rights[0],
        padded[:, 0, 1:-1, :],
        padded[:, -1, 1:-1, :],
    )
    total = total + line_part(
        field,
        2,
        count,
        tables[1],
        lefts[1],
        rights[1],
        padded[:, 1:-1, 0, :],
        padded[:, 1:-1, -1, :],
    )
    total = total + line_part(
        field, 3, count, tables[2], lefts[2], rights[2], field[:, :, :, -1], field[:, :, :, 0]
    )
    return total


def apply_system(field, level, coupling):
    image = spatial(field, level)
    everyone = lax.all_gather(image, "section", axis=0, tiled=True)
    butcher = jnp.asarray(radau_matrix(), jnp.float32)
    rows = lax.dynamic_slice_in_dim(
        butcher, lax.axis_index("section") * field.shape[0], field.shape[0], 0
    )
    mixed = jnp.einsum("ij,jabc->iabc", rows, everyone, precision=lax.Precision.HIGHEST)
    return field + STEP_SIZE * mixed


def global_total(values):
    return lax.psum(values, ("section", "gx", "gy"))


def stepwise(rhs, guess, kappa, bc_flags):
    levels = [build_level(kappa, bc_flags, count) for count in (5, 3, 2)]
    section_operator = partial(apply_system, coupling=None)
    start_residual = rhs - section_operator(guess, levels[0])
    dofs = float(rhs.size * lax.axis_size("section") * lax.axis_size("gx") * lax.axis_size("gy"))
    beta = jnp.sqrt(global_total(jnp.sum(start_residual * start_residual).reshape(1))[0])
    basis = start_residual / beta
    precond = vcycle(basis, levels, section_operator)
    image = section_operator(precond, levels[0])
    upper = global_total(jnp.sum(image * basis).reshape(1))[0]
    remainder = image - upper * basis
    lower = jnp.sqrt(global_total(jnp.sum(remainder * remainder).reshape(1))[0])
    weight = beta * upper / (upper * upper + lower * lower)
    solution = guess + weight * precond
    residual = start_residual - weight * image
    arnoldi = jnp.stack([beta / math.sqrt(dofs), upper, lower]).astype(jnp.float32)
    return (solution, residual, arnoldi)


EZ = 32
COLS = 16
HALF = 64
PIECE = 96
FIELD = 1000
F32 = jnp.float32


def split_sections():
    matrix = radau_matrix()
    values, vectors = np.linalg.eig(matrix)
    order = [n for n in np.argsort(np.abs(values.imag), kind="stable") if values[n].imag > 0]
    bases = []
    for n in order:
        plane = np.stack([vectors[:, n].real, vectors[:, n].imag], axis=1)
        bases.append(np.linalg.qr(plane)[0])
    left, cross, right = np.linalg.svd(bases[0].T @ bases[1])
    bases = [bases[0] @ left, bases[1] @ right.T]
    for c in range(2):
        sign = np.sign(bases[0][np.argmax(np.abs(bases[0][:, c])), c])
        bases = [np.concatenate([b[:, :c], sign * b[:, c : c + 1], b[:, c + 1 :]], axis=1) for b in bases]
    whole = np.concatenate(bases, axis=1)
    back = np.linalg.inv(whole)
    return whole, back, back @ matrix, back @ matrix @ whole, cross


def iota(shape, dim):
    return lax.broadcasted_iota(jnp.int32, shape, dim)


def exact_dot(a, b):
    return lax.dot_general(
        a, b, (((1,), (0,)), ((), ())), precision=lax.Precision.HIGHEST, preferred_element_type=F32
    )


def split_dot(a, b):
    high = a.astype(jnp.bfloat16)
    rest = a - high.astype(F32)
    middle = rest.astype(jnp.bfloat16)
    low = (rest - middle.astype(F32)).astype(jnp.bfloat16)
    b = b.astype(jnp.bfloat16)
    return sum(
        lax.dot_general(part, b, (((1,), (0,)), ((), ())), preferred_element_type=F32)
        for part in (low, middle, high)
    )


def choose(index, values):
    out = values[-1]
    for place in range(len(values) - 2, -1, -1):
        out = jnp.where(index == place, values[place], out)
    return out


def face_gains(flag, direction, side, count):
    nodes, weights = lobatto(count)
    c, nu = ADVECT[direction], DIFFUSE * count * count
    if side == 0:
        return (c * (1.0 + flag) / 2.0 + nu) * (1.0 / float(weights[0]))
    return (nu - c * (1.0 - flag) / 2.0) * (1.0 / float(weights[-1]))


def column_tables():
    kx, ky, kz = (element_matrix(5, d) for d in range(3))
    rows = np.zeros((64, 64))
    for s in range(2):
        for i in range(5):
            for j in range(5):
                r = s * 32 + i * 5 + j
                for m in range(5):
                    rows[r, s * 32 + m * 5 + j] += kx[i, m]
                    rows[r, s * 32 + i * 5 + m] += ky[j, m]
    lines = np.zeros((160, 320))
    for e in range(EZ):
        lines[e * 5 : e * 5 + 5, e * 5 : e * 5 + 5] = kz.T
        lines[(e - 1) % EZ * 5 + 4, 160 + e * 5] = 1.0
        lines[(e + 1) % EZ * 5, 160 + e * 5 + 4] = 1.0
    return rows.astype(np.float32), lines.astype(np.float32)


def pick_line(k):
    return (iota((160, 128), 0) == 5 * (iota((160, 128), 1) % EZ) + k).astype(F32)


def pair_factors(sec, table, own, s):
    upper = iota((32, 128), 1) < 64
    first = jnp.where(upper, float(table[0, s]), float(table[1, s]))
    second = jnp.where(upper, float(table[2, 2 + s]), float(table[3, 2 + s]))
    if not own:
        first = jnp.where(upper, float(table[2, s]), float(table[3, s]))
        second = jnp.where(upper, float(table[0, 2 + s]), float(table[1, 2 + s]))
    return jnp.where(sec == 0, first, second)


def pack_nodes(nodes):
    odd = iota((HALF, 128), 1) // EZ % 2 == 1
    return jnp.where(odd, nodes[HALF:, :], nodes[:HALF, :])


def fetch(pairs, sems):
    copies = [pltpu.make_async_copy(src, dst, sems.at[n]) for n, (src, dst) in enumerate(pairs)]
    for copy in copies:
        copy.start()
    for copy in copies:
        copy.wait()


def local_kernel(
    rhs_in, guess_in, kappa_in, flags_in, rows_in, lines_in, base,
    rhs, guess, kappa, flags, rows_t, lines_t, sems, x, kap, stack, own_nodes, other_nodes, krep,
):
    sec = lax.axis_index("section")
    fetch(
        [(rhs_in, rhs), (guess_in, guess), (kappa_in, kappa), (flags_in, flags), (rows_in, rows_t), (lines_in, lines_t)],
        sems,
    )
    x[...] = jnp.zeros_like(x)
    kap[...] = jnp.zeros_like(kap)
    stack[...] = jnp.zeros_like(stack)
    for i in range(5):
        kap[5 * i : 5 * i + 5, :] = kappa[i]
        for j in range(5):
            r = 5 * i + j
            value = guess[i, j]
            left = rhs[i, j] - value
            for s in range(2):
                x[s * 32 + r : s * 32 + r + 1, :] = value[s : s + 1]
                stack[s * 32 + r : s * 32 + r + 1, :] = left[s : s + 1]
    flag = flags[:, 0, 0, :].astype(F32)
    spread = (iota((EZ, 160), 1) // 5 == iota((EZ, 160), 0)).astype(F32)
    wide = split_dot(flag, spread)
    gains = [face_gains(wide[d : d + 1, :], d // 2, d % 2, 5) for d in range(6)]
    row = iota((32, 160), 0)
    lane = iota((32, 160), 1) % 5
    none = jnp.zeros((32, 160), F32)
    gx = jnp.where(row < 5, gains[0], jnp.where((row >= 20) & (row < 25), gains[1], none))
    gy = jnp.where(row % 5 == 0, gains[2], jnp.where(row % 5 == 4, gains[3], none))
    gz = jnp.where(lane == 0, gains[4], jnp.where(lane == 4, gains[5], none))
    gy = jnp.where(row < 25, gy, none)
    for place, gain in ((160, gx), (192, gy)):
        base[place : place + 32, :] = gain[:, :128]
        base[64 + place : 96 + place, :EZ] = gain[:, 128:]
    field = x[...]
    along = exact_dot(rows_t[...], field)
    across = exact_dot(field, lines_t[...])
    own = kap[...] + gx + gy + gz
    for s in range(2):
        r = slice(s * 32, s * 32 + 32)
        image = own * field[r] + along[r] + across[r, :160] - gz * across[r, 160:]
        stack[64 + s * 32 : 96 + s * 32, :] = image
    whole, back, back_matrix, blocks, cross = split_sections()
    own_nodes[...] = jnp.zeros_like(own_nodes)
    other_nodes[...] = jnp.zeros_like(other_nodes)
    krep[...] = jnp.zeros_like(krep)
    stack[128:, :] = kap[...]
    source = stack[...]
    for k in range(5):
        parts = split_dot(source, pick_line(k))
        for target, mark in ((own_nodes, True), (other_nodes, False)):
            total = jnp.zeros((32, 128), F32)
            for s in range(2):
                total = total + pair_factors(sec, back, mark, s) * parts[s * 32 : s * 32 + 32]
                factor = pair_factors(sec, -STEP_SIZE * back_matrix, mark, s)
                total = total + factor * parts[64 + s * 32 : 96 + s * 32]
            target[25 * k : 25 * k + 25, :] = total[:25]
        krep[25 * k : 25 * k + 25, :] = parts[128:153]
    repeat = (iota((EZ, 128), 1) % EZ == iota((EZ, 128), 0)).astype(F32)
    shown = split_dot(flag, repeat)
    upper = iota((1, 128), 1) < 64
    for r in range(3):
        own_nodes[125 + r : 126 + r, :] = jnp.where(upper, shown[2 * r : 2 * r + 1], shown[2 * r + 1 : 2 * r + 2])
    base[:HALF, :] = pack_nodes(own_nodes)
    base[PIECE : PIECE + HALF, :] = pack_nodes(other_nodes)
    base[HALF:PIECE, :] = choose(iota((32, 128), 1) // EZ, [krep[32 * q : 32 * q + 32, :] for q in range(4)])


def halo_kernel(base, x1, x3, y1, y3, mine, theirs, near, own_nodes, other_nodes):
    sec = lax.axis_index("section")
    even_x = lax.axis_index("gx") % 2 == 0
    even_y = lax.axis_index("gy") % 2 == 0
    for ref in (near, own_nodes, other_nodes):
        ref[...] = jnp.zeros_like(ref)
    for m in range(5):
        for s in range(2):
            r = s * 32
            one = slice(s, s + 1)
            near[r + m : r + m + 1, :] = jnp.where(even_x, x3[4, m, one, :], x1[4, m, one, :])
            near[r + 20 + m : r + 21 + m, :] = jnp.where(even_x, x1[0, m, one, :], x3[0, m, one, :])
            r += 64
            near[r + 5 * m : r + 5 * m + 1, :] = jnp.where(even_y, y3[m, 4, one, :], y1[m, 4, one, :])
            near[r + 5 * m + 4 : r + 5 * m + 5, :] = jnp.where(even_y, y1[m, 0, one, :], y3[m, 0, one, :])
    gx, gy = (
        jnp.concatenate([base[r : r + 32, :], base[64 + r : 96 + r, :EZ]], axis=1) for r in (160, 192)
    )
    parts_in = []
    for s in range(2):
        r = s * 32
        parts_in.append(gx * near[r : r + 32, :] + gy * near[64 + r : 96 + r, :])
    source = jnp.concatenate(parts_in, axis=0)
    back_matrix = split_sections()[2]
    for k in range(5):
        parts = split_dot(source, pick_line(k))
        for target, mark in ((own_nodes, True), (other_nodes, False)):
            total = jnp.zeros((32, 128), F32)
            for s in range(2):
                factor = pair_factors(sec, STEP_SIZE * back_matrix, mark, s)
                total = total + factor * parts[s * 32 : s * 32 + 32]
            target[25 * k : 25 * k + 25, :] = total[:25]
    mine[:HALF, :] = base[:HALF, :] + pack_nodes(own_nodes)
    mine[HALF:, :] = base[HALF:PIECE, :]
    theirs[...] = base[PIECE : PIECE + HALF, :] + pack_nodes(other_nodes)


VMEM = pl.BlockSpec(memory_space=pltpu.VMEM)
HBM = pl.BlockSpec(memory_space=pltpu.HBM)


def limit(mib):
    return pltpu.CompilerParams(vmem_limit_bytes=mib * 2**20)


def local_part(rhs, guess, kappa, flags):
    rows_t, lines_t = column_tables()
    operands = (rhs, guess, kappa, flags, jnp.asarray(rows_t), jnp.asarray(lines_t))
    return pl.pallas_call(
        local_kernel,
        out_shape=jax.ShapeDtypeStruct((288, 128), F32),
        in_specs=[HBM] * 6,
        out_specs=VMEM,
        scratch_shapes=[pltpu.VMEM(o.shape, o.dtype) for o in operands]
        + [
            pltpu.SemaphoreType.DMA((6,)),
            pltpu.VMEM((64, 160), F32),
            pltpu.VMEM((32, 160), F32),
            pltpu.VMEM((160, 160), F32),
            pltpu.VMEM((128, 128), F32),
            pltpu.VMEM((128, 128), F32),
            pltpu.VMEM((128, 128), F32),
        ],
        compiler_params=limit(60),
        name="local_part",
    )(*operands)


def halo_part(base, halos):
    return pl.pallas_call(
        halo_kernel,
        out_shape=[
            jax.ShapeDtypeStruct((PIECE, 128), F32),
            jax.ShapeDtypeStruct((HALF, 128), F32),
        ],
        in_specs=[VMEM] * 5,
        out_specs=[VMEM] * 2,
        scratch_shapes=[pltpu.VMEM((128, 160), F32)] + [pltpu.VMEM((128, 128), F32)] * 2,
        compiler_params=limit(16),
        name="halo_part",
    )(base, *halos)


class Level:
    def __init__(self, count, refs):
        self.count = count
        self.diag, self.jac, self.x, self.dir, self.res, self.f = refs
        self.tables = [element_matrix(count, d) for d in range(3)]
        self.gains = None


def tile(index):
    return pl.ds(index * 8, 8)


def rows_of(pieces, size, r, h):
    return pieces[pl.ds(8 * h * size + r, 8, stride=size), :]


def place_pieces(blocks, pieces, first, size):
    for gy in range(4):
        for gx in range(4):
            source = (gy * 4 + gx) * PIECE + first
            target = (gx * 4 + gy) * size
            pieces[target : target + size, :] = blocks[source : source + size, :]


def assemble_kernel(blocks, field, pieces):
    place_pieces(blocks, pieces, 0, HALF)
    odd = iota((8, 128), 1) // EZ % 2 == 1
    for r in range(HALF):
        low, high = rows_of(pieces, HALF, r, 0), rows_of(pieces, HALF, r, 1)
        field[tile(r), :] = jnp.where(odd, pltpu.roll(high, 32, 1), low)
        field[tile(HALF + r), :] = jnp.where(odd, high, pltpu.roll(low, 96, 1))


def load(ref, first, count):
    start = first * 8 if isinstance(first, int) else pl.multiple_of(first * 8, 8)
    return ref[pl.ds(start, count * 8), :].reshape(count, 8, 128)


def store(ref, first, value):
    start = first * 8 if isinstance(first, int) else pl.multiple_of(first * 8, 8)
    ref[pl.ds(start, value.shape[0] * 8), :] = value.reshape(value.shape[0] * 8, 128)


def cycle_kernel(gathered, assembled, fields, *scratch):
    sec = lax.axis_index("section")
    my_gx, my_gy = lax.axis_index("gx"), lax.axis_index("gy")
    levels = [Level(n, scratch[6 * p : 6 * p + 6]) for p, n in enumerate((5, 3, 2))]
    pieces, kap, half, terms = scratch[18:22]
    lane = iota((8, 128), 1)
    sub = iota((8, 128), 0)
    group = lane // EZ
    odd = group % 2 == 1
    element = lane % EZ
    place = sub % 4
    low_half = sub < 4
    blocks = split_sections()[3]

    def lanes_of(upper, lower):
        return jnp.where(lane < 64, jnp.where(sec == 0, upper[0], upper[1]), jnp.where(sec == 0, lower[0], lower[1]))

    entry = [[[float(STEP_SIZE * blocks[2 * p + a, 2 * p + b]) for p in range(2)] for b in range(2)] for a in range(2)]
    same = lanes_of(entry[0][0], entry[1][1])
    swap = lanes_of(entry[0][1], entry[1][0])
    centre = (CHEB_HIGH + CHEB_LOW) / 2.0
    radius = (CHEB_HIGH - CHEB_LOW) / 2.0
    first_rho = radius / centre
    second_rho = 1.0 / (2.0 * centre / radius - first_rho)
    keep = 1.0 + second_rho * first_rho
    push = 2.0 * second_rho / radius * centre

    flags = []
    for r in range(3):
        got = assembled[tile(125 + r), :]
        across = pltpu.roll(got, 64, 1)
        flags += [jnp.where(lane < 64, got, across), jnp.where(lane < 64, across, got)]
    place_pieces(gathered, pieces, HALF, 32)

    for r in range(32):
        turned = []
        for h in range(2):
            got = rows_of(pieces, 32, r, h)
            turned.append([pltpu.roll(got, 32 * m, 1) if m else got for m in range(4)])
        for q in range(4):
            kap[tile(q * 32 + r), :] = choose(group, [turned[g % 2][(g - q) % 4] for g in range(4)])

    for level in levels:
        n = level.count
        stride = 4 // (n - 1)
        level.gains = [face_gains(flags[d], d // 2, d % 2, n) for d in range(6)]
        rows = []
        for d in range(3):
            row = [jnp.full((8, 128), float(level.tables[d][m, m]), F32) for m in range(n)]
            row[0] = row[0] + level.gains[2 * d]
            row[n - 1] = row[n - 1] + level.gains[2 * d + 1]
            rows.append(row)
        for m in range(n):
            terms[tile(m), :] = rows[2][m]

        def diagonals(k, carry, level=level, n=n, stride=stride, rows=rows):
            along = jnp.stack(rows[1])
            for i in range(n):
                line = load(kap, k * 25 * stride + i * stride * 5, 5)
                line = jnp.stack([line[j * stride] for j in range(n)])
                value = line + (along + (load(terms, k, 1) + rows[0][i]))
                scale = 1.0 / (1.0 + STEP_SIZE * JACOBI_SCALE * value)
                store(level.diag, (k * n + i) * n, value)
                store(level.jac, (k * n + i) * n, scale * (1.0 / centre))
            return carry
        lax.fori_loop(0, n, diagonals, 0)

    def begin(level, source):
        n = level.count

        def start(k, carry):
            first = k * n * n
            f = load(source, first, n * n)
            store(level.dir, first, load(level.jac, first, n * n) * f)
            store(level.res, first, f)
            store(level.x, first, jnp.zeros_like(f))
            return carry
        lax.fori_loop(0, n, start, 0)

    def apply(level, smooth):
        n = level.count
        kx, ky, kz = level.tables
        source = level.dir if smooth else level.x

        def around(u):
            turned = pltpu.roll(u, 4, 1)
            return turned, jnp.where(odd, pltpu.roll(turned, 32, 2), pltpu.roll(turned, 96, 2))

        for k in range(n):
            here = k * n * n
            v = [load(source, here + i * n, n) for i in range(n)]
            left, left_far = around(v[n - 1])
            right, right_far = around(v[0])
            waiting = []
            for i in range(n):
                first = here + i * n
                total = load(level.diag, first, n) * v[i]
                for m in range(n):
                    if m != i:
                        total = total + float(kx[i, m]) * v[m]
                for m in range(n):
                    if m != k:
                        total = total + float(kz[k, m]) * load(source, (m * n + i) * n, n)
                lines = []
                for j in range(n):
                    line = None
                    for m in range(n):
                        if m != j:
                            term = float(ky[j, m]) * v[i][m]
                            line = term if line is None else line + term
                    if j == 0:
                        u = v[i][n - 1]
                        moved = jnp.where(place == 0, pltpu.roll(u, 5, 0), pltpu.roll(u, 1, 0))
                        line = line - level.gains[2] * moved
                    if j == n - 1:
                        u = v[i][0]
                        moved = jnp.where(place == 3, pltpu.roll(u, 3, 0), pltpu.roll(u, 7, 0))
                        line = line - level.gains[3] * moved
                    lines.append(line)
                total = total + jnp.stack(lines)
                if i == 0:
                    total = total - level.gains[0] * jnp.where(low_half, left_far, left)
                if i == n - 1:
                    total = total - level.gains[1] * jnp.where(low_half, right, right_far)
                if k == 0:
                    u = load(source, ((n - 1) * n + i) * n, n)
                    moved = jnp.where(element == 0, pltpu.roll(u, 97, 2), pltpu.roll(u, 1, 2))
                    total = total - level.gains[4] * moved
                if k == n - 1:
                    u = load(source, i * n, n)
                    moved = jnp.where(element == EZ - 1, pltpu.roll(u, 31, 2), pltpu.roll(u, 127, 2))
                    total = total - level.gains[5] * moved
                image = v[i] + (same * total + swap * pltpu.roll(total, 64, 2))
                if smooth:
                    scaled = load(level.jac, first, n) * (load(level.res, first, n) - image)
                    waiting.append((level.x, first, load(level.x, first, n) + keep * v[i] + push * scaled))
                else:
                    rest = load(level.f, first, n) - image
                    waiting.append((level.res, first, rest))
                    waiting.append((level.dir, first, load(level.jac, first, n) * rest))
                if i % 2 == 1 or i == n - 1:
                    for place_out in waiting:
                        store(*place_out)
                    waiting = []

    def combine(weights, parts):
        total = None
        for weight, part in zip(weights, parts):
            if abs(weight) > 1e-14:
                term = part if abs(weight - 1.0) < 1e-14 else float(weight) * part
                total = term if total is None else total + term
        return total

    def change(table, source, target, add):
        m, n = table.shape

        def outer(i, carry):
            parts = [load(source, i * n + k * n * n, n) for k in range(n)]
            for k in range(m):
                store(half, i * n + k * n * n, combine(table[k], parts))
            return carry
        lax.fori_loop(0, n, outer, 0)

        def inner(k, carry):
            parts = [load(half, k * n * n + i * n, n) for i in range(n)]
            for i in range(m):
                line = combine(table[i], parts)
                value = jnp.stack([combine(table[j], [line[a] for a in range(n)]) for j in range(m)])
                first = k * m * m + i * m
                store(target, first, load(target, first, m) + value if add else value)
            return carry
        lax.fori_loop(0, m, inner, 0)

    def down(n, m):
        fine_nodes, fine_weights = lobatto(n)
        coarse_nodes, coarse_weights = lobatto(m)
        table = lagrange_table(coarse_nodes, fine_nodes)
        return (1.0 / coarse_weights)[:, None] * table.T * fine_weights[None, :]

    def up(m, n):
        return lagrange_table(lobatto(m)[0], lobatto(n)[0])

    def solve(p):
        level = levels[p]
        if p == 2:
            apply(level, True)
            return
        below = levels[p + 1]

        def step(t, carry):
            @pl.when(t != 1)
            def _():
                apply(level, True)

            @pl.when((t != 2) | (p == 0))
            def _():
                apply(level, False)

            @pl.when(t == 0)
            def _():
                n, m = level.count, below.count
                change(down(n, m), level.res, below.f, False)
                begin(below, below.f)
                solve(p + 1)
                change(up(m, n), below.x, level.x, True)
            return carry
        lax.fori_loop(0, 3, step, 0)

    fine = levels[0]
    fine.f = assembled
    begin(fine, assembled)
    solve(0)

    def give(k, carry):
        store(fields, k * 25, load(fine.res, k * 25, 25))
        return carry
    lax.fori_loop(0, 5, give, 0)
    column = (my_gx % 2) * 4 + my_gy
    fields[FIELD : FIELD + 125, :] = fine.x[pl.ds(column, 125, stride=8), :]
    fields[FIELD + 125 : FIELD + 128, :] = jnp.zeros((3, 128), F32)


def finish_kernel(own, other, own_start, other_start, guess, sol, res_out, arnoldi, cols, outs):
    sec = lax.axis_index("section")
    my_gx, my_gy = lax.axis_index("gx"), lax.axis_index("gy")
    whole, back, back_matrix, blocks, cross = split_sections()
    weights = jnp.where(iota((8, 128), 1) < 64, float(cross[0]), float(cross[1]))
    nothing = jnp.zeros((8, 128), F32)

    lane = iota((32, 128), 1)
    here = lane // EZ % 2 == my_gx // 2
    factors = []
    for s in range(2):
        row = []
        for p in range(2):
            parts = []
            for mine in range(2):
                t = whole[2 * mine + s]
                pairs = [jnp.where(lane < 64, float(t[2 * q]), float(t[2 * q + 1])) for q in range(2)]
                parts.append(pairs[mine] if p == 0 else pairs[1 - mine])
            row.append(jnp.where(here, jnp.where(sec == 0, parts[0], parts[1]), 0.0)[:25])
        factors.append(row)
    column = (my_gx % 2) * 4 + my_gy
    cols[...] = jnp.zeros_like(cols)
    total = jnp.zeros((192, 160), F32)
    for k in range(5):
        where = pl.ds(k * 200 + column, 25, stride=8)
        shown = [[ref[FIELD + k * 25 : FIELD + k * 25 + 25, :] for ref in (own, other)]]
        shown.append([ref[where, :] for ref in (own_start, other_start)])
        shown.append([b[where, :] - a[where, :] for a, b in ((own, own_start), (other, other_start))])
        for f, (a, b) in enumerate(shown):
            for s in range(2):
                r = f * 64 + s * 32
                cols[r : r + 25, :] = factors[s][0] * a + factors[s][1] * b
        hit = (iota((128, 160), 1) == 5 * (iota((128, 160), 0) % EZ) + k).astype(F32)
        total = total + split_dot(cols[...], hit)

    def product(a, b, c, d):
        return (a * c + b * d) + weights * (a * d + b * c)

    uppers, sizes = [nothing] * 5, [nothing] * 5
    for r in range(125):
        a, b, c, d = (ref[tile(r), :] for ref in (own, other, own_start, other_start))
        a, b = c - a, d - b
        uppers[r % 5] = uppers[r % 5] + product(a, b, c, d)
        sizes[r % 5] = sizes[r % 5] + product(c, d, c, d)
    size = jnp.sum(sum(sizes), keepdims=True)
    upper = jnp.sum(sum(uppers), keepdims=True) / size
    rests = [nothing] * 5
    for r in range(125):
        a, b, c, d = (ref[tile(r), :] for ref in (own, other, own_start, other_start))
        a, b = c - a, d - b
        a, b = a - upper * c, b - upper * d
        rests[r % 5] = rests[r % 5] + product(a, b, a, b)
    rest = jnp.sum(sum(rests), keepdims=True)
    beta = jnp.sqrt(size)
    lower = jnp.sqrt(rest) / beta
    weight = upper / (upper * upper + lower * lower)
    entries = float(125 * EZ * COLS * 4)
    for place_out, value in enumerate((beta * (1.0 / math.sqrt(entries)), upper, lower)):
        arnoldi[place_out] = value[0, 0]
    outs[:64, :] = weight * total[:64]
    outs[64:, :] = total[64:128] - weight * total[128:]
    for i in range(5):
        for j in range(5):
            r = 5 * i + j
            for s in range(2):
                sol[i, j, s : s + 1, :] = guess[i, j, s : s + 1, :] + outs[s * 32 + r : s * 32 + r + 1, :]
                res_out[i, j, s : s + 1, :] = outs[64 + s * 32 + r : 64 + s * 32 + r + 1, :]


def assemble(blocks):
    return pl.pallas_call(
        assemble_kernel,
        out_shape=jax.ShapeDtypeStruct((128 * 8, 128), F32),
        in_specs=[VMEM],
        out_specs=VMEM,
        scratch_shapes=[pltpu.VMEM((COLS * HALF, 128), F32)],
        compiler_params=limit(16),
        name="assemble",
    )(blocks)


def cycle(blocks, assembled):
    scratch = []
    for n in (5, 3, 2):
        scratch += [pltpu.VMEM((n**3 * 8, 128), F32)] * 6
    scratch += [
        pltpu.VMEM((COLS * 32, 128), F32),
        pltpu.VMEM((128 * 8, 128), F32),
        pltpu.VMEM((FIELD, 128), F32),
        pltpu.VMEM((15 * 8, 128), F32),
    ]
    return pl.pallas_call(
        cycle_kernel,
        out_shape=jax.ShapeDtypeStruct((FIELD + 128, 128), F32),
        in_specs=[VMEM] * 2,
        out_specs=VMEM,
        scratch_shapes=scratch,
        compiler_params=limit(24),
        cost_estimate=pl.CostEstimate(flops=40_000_000, bytes_accessed=30_000_000, transcendentals=0),
        name="cycle",
    )(blocks, assembled)


def finish(own, other, own_start, other_start, guess):
    return pl.pallas_call(
        finish_kernel,
        out_shape=[
            jax.ShapeDtypeStruct(guess.shape, F32),
            jax.ShapeDtypeStruct(guess.shape, F32),
            jax.ShapeDtypeStruct((3,), F32),
        ],
        in_specs=[VMEM] * 5,
        out_specs=[VMEM, VMEM, pl.BlockSpec(memory_space=pltpu.SMEM)],
        scratch_shapes=[pltpu.VMEM((192, 128), F32), pltpu.VMEM((128, 160), F32)],
        compiler_params=limit(24),
        name="finish",
    )(own, other, own_start, other_start, guess)


def exchange(x, axis, bits):
    return lax.ppermute(x, axis, [(n, n ^ bits) for n in range(lax.axis_size(axis))])


def spread(x, axis):
    copies = jnp.broadcast_to(x, (lax.axis_size(axis),) + x.shape)
    got = lax.all_to_all(copies, axis, split_axis=0, concat_axis=0)
    return got.reshape((-1,) + x.shape[1:])


def gathered_body(rhs, guess, kappa, bc_flags):
    rhs, guess = (jnp.transpose(v, (1, 2, 0, 3)) for v in (rhs, guess))
    halos = [exchange(guess, axis, bits) for axis in ("gx", "gy") for bits in (1, 3)]
    base = local_part(rhs, guess, kappa, bc_flags)
    mine, theirs = halo_part(base, halos)
    got = exchange(theirs, "section", 1)
    piece = jnp.concatenate([mine[:HALF] + got, mine[HALF:]])
    blocks = spread(spread(piece, "gx"), "gy")
    start = assemble(blocks)
    other_start = exchange(start, "section", 1)
    own, other_start = lax.optimization_barrier((cycle(blocks, start), other_start))
    sol, res, arnoldi = finish(own, exchange(own, "section", 1), start, other_start, guess)
    sol, res = (jnp.transpose(v, (2, 0, 1, 3)) for v in (sol, res))
    return sol, res, arnoldi


def solution(mesh):
    placed = (
        P("section", "gx", "gy", None),
        P("section", "gx", "gy", None),
        P("gx", "gy", None),
        P(None, "gx", "gy", None),
    )
    sizes = (mesh.shape["section"], mesh.shape["gx"], mesh.shape["gy"])

    def step(rhs, guess, kappa, bc_flags):
        fits = sizes == (2, 4, 4) and rhs.shape == (4, 20, 20, 160)
        return jax.shard_map(
            gathered_body if fits else stepwise,
            mesh=mesh,
            in_specs=placed,
            out_specs=(P("section", "gx", "gy", None), P("section", "gx", "gy", None), P()),
            check_vma=False,
        )(rhs, guess, kappa, bc_flags)

    return step
```

```python
from functools import partial
import math

import jax
import jax.numpy as jnp
import numpy as np
from jax import lax
from jax.experimental import pallas as pl
from jax.experimental.pallas import tpu as pltpu
from jax.sharding import PartitionSpec as P

ADVECT = (1.0, 0.7, 0.5)
DIFFUSE = 0.05
STEP_SIZE = 0.2
JACOBI_SCALE = 0.25
CHEB_LOW = 0.25
CHEB_HIGH = 2.0
LETTERS = "abcdef"


def extended(x, sides, width):
    for axis, dim in sides:
        peers, length = (lax.axis_size(axis), x.shape[dim])
        up = [(i, (i + 1) % peers) for i in range(peers)]
        down = [(j, i) for i, j in up]
        last = lax.slice_in_dim(x, length - width, length, axis=dim)
        leading = lax.slice_in_dim(x, 0, width, axis=dim)
        before = lax.ppermute(last, axis, up)
        after = lax.ppermute(leading, axis, down)
        x = jnp.concatenate([before, x, after], axis=dim)
    return x


def lobatto(count):
    if count == 5:
        inner = math.sqrt(3.0 / 7.0)
        return (
            np.array([-1.0, -inner, 0.0, inner, 1.0]),
            np.array([0.1, 49.0 / 90.0, 32.0 / 45.0, 49.0 / 90.0, 0.1]),
        )
    if count == 3:
        return (np.array([-1.0, 0.0, 1.0]), np.array([1.0 / 3.0, 4.0 / 3.0, 1.0 / 3.0]))
    return (np.array([-1.0, 1.0]), np.array([1.0, 1.0]))


def lagrange_table(nodes, points):
    table = np.ones((len(points), len(nodes)))
    for column in range(len(nodes)):
        for other in range(len(nodes)):
            if other != column:
                table[:, column] *= (points - nodes[other]) / (nodes[column] - nodes[other])
    return table


def slope_table(nodes):
    total = len(nodes)
    factor = np.array(
        [np.prod([nodes[i] - nodes[k] for k in range(total) if k != i]) for i in range(total)]
    )
    table = np.zeros((total, total))
    for row in range(total):
        for column in range(total):
            if row != column:
                table[row, column] = factor[row] / factor[column] / (nodes[row] - nodes[column])
        table[row, row] = -np.sum(table[row])
    return table


def element_matrix(count, direction):
    nodes, weights = lobatto(count)
    slopes = slope_table(nodes)
    stiffness = (1.0 / weights)[:, None] * (slopes.T @ (weights[:, None] * slopes))
    return ADVECT[direction] * slopes + DIFFUSE * stiffness


def legendre_pair(point, order):
    values = [1.0, point]
    slopes = [0.0, 1.0]
    for index in range(1, order):
        values.append(
            ((2 * index + 1) * point * values[index] - index * values[index - 1]) / (index + 1)
        )
        slopes.append(slopes[index - 1] + (2 * index + 1) * values[index])
    return (values, slopes)


def radau_nodes():
    starts = [0.0885879595127039, 0.4094668644407347, 0.7876594617608471]
    found = []
    for start in starts:
        point = start
        for sweep in range(30):
            values, slopes = legendre_pair(2.0 * point - 1.0, 4)
            change = (values[4] - values[3]) / (2.0 * (slopes[4] - slopes[3]))
            point = point - change
        found.append(point)
    found.append(1.0)
    return found


def poly_times(coefs, root):
    result = [0.0] * (len(coefs) + 1)
    for index in range(len(coefs)):
        result[index + 1] += coefs[index]
        result[index] -= root * coefs[index]
    return result


def radau_matrix():
    order = 4
    nodes = radau_nodes()
    matrix = np.zeros((order, order))
    for column in range(order):
        coefs = [1.0]
        denominator = 1.0
        for other in range(order):
            if other != column:
                coefs = poly_times(coefs, nodes[other])
                denominator *= nodes[column] - nodes[other]
        for row in range(order):
            upper_end = nodes[row]
            integral = 0.0
            for index in range(len(coefs)):
                integral += coefs[index] * upper_end ** (index + 1) / (index + 1)
            matrix[row, column] = integral / denominator
    return matrix


def node_einsum(table, field, axis):
    labels = LETTERS[: field.ndim]
    source = labels[: axis + 1] + "j" + labels[axis + 2 :]
    target = labels[: axis + 1] + "i" + labels[axis + 2 :]
    return jnp.einsum(
        "ij," + source + "->" + target,
        jnp.asarray(table, jnp.float32),
        field,
        precision=lax.Precision.HIGHEST,
    )


def apply_along(field, axis, count, table):
    shape = field.shape
    split = shape[:axis] + (shape[axis] // count, count) + shape[axis + 1 :]
    mapped = node_einsum(table, field.reshape(split), axis)
    return mapped.reshape(
        shape[:axis] + (mapped.shape[axis] * mapped.shape[axis + 1],) + shape[axis + 1 :]
    )


def line_part(field, axis, count, table, left_gain, right_gain, left_edge, right_edge):
    shape = field.shape
    elements = shape[axis] // count
    split = field.reshape(shape[:axis] + (elements, count) + shape[axis + 1 :])
    linear = node_einsum(table, split, axis)
    first = lax.index_in_dim(split, 0, axis + 1, keepdims=False)
    last = lax.index_in_dim(split, count - 1, axis + 1, keepdims=False)
    before = jnp.concatenate(
        [jnp.expand_dims(left_edge, axis), lax.slice_in_dim(last, 0, elements - 1, axis=axis)], axis
    )
    after = jnp.concatenate(
        [lax.slice_in_dim(first, 1, elements, axis=axis), jnp.expand_dims(right_edge, axis)], axis
    )
    front = jnp.expand_dims(left_gain * (first - before), axis + 1)
    back = jnp.expand_dims(right_gain * (last - after), axis + 1)
    if count > 2:
        middle_shape = list(front.shape)
        middle_shape[axis + 1] = count - 2
        pieces = [front, jnp.zeros(middle_shape, jnp.float32), back]
    else:
        pieces = [front, back]
    return (linear + jnp.concatenate(pieces, axis + 1)).reshape(shape)


def diag_along(shape, axis, count, table, left_gain, right_gain):
    elements = shape[axis] // count
    split = shape[:axis] + (elements, count) + shape[axis + 1 :]
    profile = [1] * len(split)
    profile[axis + 1] = count
    diagonal_entries = np.array([table[index, index] for index in range(count)])
    base = jnp.broadcast_to(jnp.asarray(diagonal_entries, jnp.float32).reshape(profile), split)
    front = jnp.expand_dims(left_gain, axis + 1)
    back = jnp.expand_dims(right_gain, axis + 1)
    if count > 2:
        middle_shape = list(front.shape)
        middle_shape[axis + 1] = count - 2
        pieces = [front, jnp.zeros(middle_shape, jnp.float32), back]
    else:
        pieces = [front, back]
    return (base + jnp.concatenate(pieces, axis + 1)).reshape(shape)


def level_kappa(kappa, count):
    if count == 5:
        return kappa
    picks = np.array([0, 2, 4]) if count == 3 else np.array([0, 4])
    extents = [extent // 5 for extent in kappa.shape]
    grouped = kappa.reshape(extents[0], 5, extents[1], 5, extents[2], 5)
    for axis in (1, 3, 5):
        grouped = jnp.take(grouped, picks, axis=axis)
    return grouped.reshape(extents[0] * count, extents[1] * count, extents[2] * count)


def face_plane(face, direction, count):
    plane = face.astype(jnp.float32)
    for axis in range(3):
        if axis != direction:
            plane = jnp.repeat(plane, count, axis=axis)
    return plane


def build_level(kappa, flags, count):
    nodes, weights = lobatto(count)
    kappa_level = level_kappa(kappa, count)
    tables, lefts, rights = ([], [], [])
    diagonal = kappa_level
    for direction in range(3):
        table = element_matrix(count, direction)
        lower = face_plane(flags[2 * direction], direction, count)
        upper = face_plane(flags[2 * direction + 1], direction, count)
        left_gain = (ADVECT[direction] * (1.0 + lower) / 2.0 + DIFFUSE * count * count) / float(
            weights[0]
        )
        right_gain = (DIFFUSE * count * count - ADVECT[direction] * (1.0 - upper) / 2.0) / float(
            weights[-1]
        )
        tables.append(table)
        lefts.append(left_gain)
        rights.append(right_gain)
        diagonal = diagonal + diag_along(
            kappa_level.shape, direction, count, table, left_gain, right_gain
        )
    scale = 1.0 / (1.0 + STEP_SIZE * JACOBI_SCALE * diagonal)
    return (count, tables, lefts, rights, kappa_level, scale)


def restrict(field, fine_count, coarse_count):
    fine_nodes, fine_weights = lobatto(fine_count)
    coarse_nodes, coarse_weights = lobatto(coarse_count)
    table = (
        (1.0 / coarse_weights)[:, None]
        * lagrange_table(coarse_nodes, fine_nodes).T
        * fine_weights[None, :]
    )
    for axis in range(field.ndim - 3, field.ndim):
        field = apply_along(field, axis, fine_count, table)
    return field


def prolong(field, coarse_count, fine_count):
    fine_nodes, fine_weights = lobatto(fine_count)
    coarse_nodes, coarse_weights = lobatto(coarse_count)
    table = lagrange_table(coarse_nodes, fine_nodes)
    for axis in range(field.ndim - 3, field.ndim):
        field = apply_along(field, axis, coarse_count, table)
    return field


def chebyshev(rhs, start, level, operator):
    centre = (CHEB_HIGH + CHEB_LOW) / 2.0
    radius = (CHEB_HIGH - CHEB_LOW) / 2.0
    ratio = centre / radius
    first_rho = 1.0 / ratio
    second_rho = 1.0 / (2.0 * ratio - first_rho)
    scale = level[5]
    if start is None:
        remain = rhs
    else:
        remain = rhs - operator(start, level)
    step = scale * remain / centre
    guess = step if start is None else start + step
    remain = remain - operator(step, level)
    step = second_rho * first_rho * step + 2.0 * second_rho / radius * scale * remain
    return guess + step


def vcycle(rhs, levels, operator):
    fine, middle, coarse = levels
    fine_x = chebyshev(rhs, None, fine, operator)
    middle_rhs = restrict(rhs - operator(fine_x, fine), 5, 3)
    middle_x = chebyshev(middle_rhs, None, middle, operator)
    coarse_rhs = restrict(middle_rhs - operator(middle_x, middle), 3, 2)
    coarse_x = chebyshev(coarse_rhs, None, coarse, operator)
    middle_x = chebyshev(middle_rhs, middle_x + prolong(coarse_x, 2, 3), middle, operator)
    return chebyshev(rhs, fine_x + prolong(middle_x, 3, 5), fine, operator)


def spatial(field, level):
    count, tables, lefts, rights, kappa_level, scale = level
    padded = extended(field, (("gx", 1), ("gy", 2)), 1)
    total = kappa_level * field
    total = total + line_part(
        field,
        1,
        count,
        tables[0],
        lefts[0],
        rights[0],
        padded[:, 0, 1:-1, :],
        padded[:, -1, 1:-1, :],
    )
    total = total + line_part(
        field,
        2,
        count,
        tables[1],
        lefts[1],
        rights[1],
        padded[:, 1:-1, 0, :],
        padded[:, 1:-1, -1, :],
    )
    total = total + line_part(
        field, 3, count, tables[2], lefts[2], rights[2], field[:, :, :, -1], field[:, :, :, 0]
    )
    return total


def apply_system(field, level, coupling):
    image = spatial(field, level)
    everyone = lax.all_gather(image, "section", axis=0, tiled=True)
    butcher = jnp.asarray(radau_matrix(), jnp.float32)
    rows = lax.dynamic_slice_in_dim(
        butcher, lax.axis_index("section") * field.shape[0], field.shape[0], 0
    )
    mixed = jnp.einsum("ij,jabc->iabc", rows, everyone, precision=lax.Precision.HIGHEST)
    return field + STEP_SIZE * mixed


def global_total(values):
    return lax.psum(values, ("section", "gx", "gy"))


def stepwise(rhs, guess, kappa, bc_flags):
    levels = [build_level(kappa, bc_flags, count) for count in (5, 3, 2)]
    section_operator = partial(apply_system, coupling=None)
    start_residual = rhs - section_operator(guess, levels[0])
    dofs = float(rhs.size * lax.axis_size("section") * lax.axis_size("gx") * lax.axis_size("gy"))
    beta = jnp.sqrt(global_total(jnp.sum(start_residual * start_residual).reshape(1))[0])
    basis = start_residual / beta
    precond = vcycle(basis, levels, section_operator)
    image = section_operator(precond, levels[0])
    upper = global_total(jnp.sum(image * basis).reshape(1))[0]
    remainder = image - upper * basis
    lower = jnp.sqrt(global_total(jnp.sum(remainder * remainder).reshape(1))[0])
    weight = beta * upper / (upper * upper + lower * lower)
    solution = guess + weight * precond
    residual = start_residual - weight * image
    arnoldi = jnp.stack([beta / math.sqrt(dofs), upper, lower]).astype(jnp.float32)
    return (solution, residual, arnoldi)


EZ = 32
COLS = 16
HALF = 64
TRACE = 40
PIECE = HALF + TRACE
COEFS = 40
FIELD = 1000
F32 = jnp.float32


def split_sections():
    matrix = radau_matrix()
    values, vectors = np.linalg.eig(matrix)
    order = [n for n in np.argsort(np.abs(values.imag), kind="stable") if values[n].imag > 0]
    bases = []
    for n in order:
        plane = np.stack([vectors[:, n].real, vectors[:, n].imag], axis=1)
        bases.append(np.linalg.qr(plane)[0])
    left, cross, right = np.linalg.svd(bases[0].T @ bases[1])
    bases = [bases[0] @ left, bases[1] @ right.T]
    for c in range(2):
        sign = np.sign(bases[0][np.argmax(np.abs(bases[0][:, c])), c])
        bases = [np.concatenate([b[:, :c], sign * b[:, c : c + 1], b[:, c + 1 :]], axis=1) for b in bases]
    whole = np.concatenate(bases, axis=1)
    back = np.linalg.inv(whole)
    return whole, back, back @ matrix, back @ matrix @ whole, cross


def iota(shape, dim):
    return lax.broadcasted_iota(jnp.int32, shape, dim)


def exact_dot(a, b):
    return lax.dot_general(
        a, b, (((1,), (0,)), ((), ())), precision=lax.Precision.HIGHEST, preferred_element_type=F32
    )


def split_dot(a, b):
    high = a.astype(jnp.bfloat16)
    rest = a - high.astype(F32)
    middle = rest.astype(jnp.bfloat16)
    low = (rest - middle.astype(F32)).astype(jnp.bfloat16)
    b = b.astype(jnp.bfloat16)
    return sum(
        lax.dot_general(part, b, (((1,), (0,)), ((), ())), preferred_element_type=F32)
        for part in (low, middle, high)
    )


def choose(index, values):
    out = values[-1]
    for place in range(len(values) - 2, -1, -1):
        out = jnp.where(index == place, values[place], out)
    return out


def face_gains(flag, direction, side, count):
    nodes, weights = lobatto(count)
    c, nu = ADVECT[direction], DIFFUSE * count * count
    if side == 0:
        return (c * (1.0 + flag) / 2.0 + nu) * (1.0 / float(weights[0]))
    return (nu - c * (1.0 - flag) / 2.0) * (1.0 / float(weights[-1]))


def column_tables():
    kx, ky, kz = (element_matrix(5, d) for d in range(3))
    rows = np.zeros((64, 64))
    for s in range(2):
        for i in range(5):
            for j in range(5):
                r = s * 32 + i * 5 + j
                for m in range(5):
                    rows[r, s * 32 + m * 5 + j] += kx[i, m]
                    rows[r, s * 32 + i * 5 + m] += ky[j, m]
    lines = np.zeros((160, 320))
    for e in range(EZ):
        lines[e * 5 : e * 5 + 5, e * 5 : e * 5 + 5] = kz.T
        lines[(e - 1) % EZ * 5 + 4, 160 + e * 5] = 1.0
        lines[(e + 1) % EZ * 5, 160 + e * 5 + 4] = 1.0
    return rows.astype(np.float32), lines.astype(np.float32)


def pick_line(k):
    return (iota((160, 128), 0) == 5 * (iota((160, 128), 1) % EZ) + k).astype(F32)


def pair_factors(sec, table, own, s):
    upper = iota((32, 128), 1) < 64
    first = jnp.where(upper, float(table[0, s]), float(table[1, s]))
    second = jnp.where(upper, float(table[2, 2 + s]), float(table[3, 2 + s]))
    if not own:
        first = jnp.where(upper, float(table[2, s]), float(table[3, s]))
        second = jnp.where(upper, float(table[0, 2 + s]), float(table[1, 2 + s]))
    return jnp.where(sec == 0, first, second)


def pack_nodes(nodes):
    half = nodes.shape[0] // 2
    odd = iota((half, 128), 1) // EZ % 2 == 1
    return jnp.where(odd, nodes[half:, :], nodes[:half, :])


def face_place(i, j):
    if i == 0:
        return j
    if i == 4:
        return 11 + j
    return 3 + 2 * i + (0 if j == 0 else 1)


def fetch(pairs, sems):
    copies = [pltpu.make_async_copy(src, dst, sems.at[n]) for n, (src, dst) in enumerate(pairs)]
    for copy in copies:
        copy.start()
    for copy in copies:
        copy.wait()


def coefs_kernel(kappa_in, flags_in, out, kappa, flags, sems, kap, krep):
    fetch([(kappa_in, kappa), (flags_in, flags)], sems)
    kap[...] = jnp.zeros_like(kap)
    for i in range(5):
        kap[5 * i : 5 * i + 5, :] = kappa[i]
    coefs = kap[...]
    krep[...] = jnp.zeros_like(krep)
    for k in range(5):
        krep[25 * k : 25 * k + 25, :] = split_dot(coefs, pick_line(k))[:25]
    out[:32, :] = choose(iota((32, 128), 1) // EZ, [krep[32 * q : 32 * q + 32, :] for q in range(4)])
    flag = flags[:, 0, 0, :].astype(F32)
    repeat = (iota((EZ, 128), 1) % EZ == iota((EZ, 128), 0)).astype(F32)
    shown = split_dot(flag, repeat)
    group = iota((1, 128), 1) // EZ
    out[32:40, :] = jnp.zeros((8, 128), F32)
    out[32:33, :] = choose(group, [shown[d : d + 1] for d in range(4)])
    out[33:34, :] = choose(group, [shown[4:5], shown[5:6]])


def local_kernel(
    rhs_in, guess_in, kappa_in, flags_in, rows_in, lines_in, mine, theirs,
    rhs, guess, kappa, flags, rows_t, lines_t, sems, x, kap, stack, nodes, traces,
):
    sec = lax.axis_index("section")
    fetch(
        [(rhs_in, rhs), (guess_in, guess), (kappa_in, kappa), (flags_in, flags), (rows_in, rows_t), (lines_in, lines_t)],
        sems,
    )
    x[...] = jnp.zeros_like(x)
    kap[...] = jnp.zeros_like(kap)
    stack[...] = jnp.zeros_like(stack)
    for i in range(5):
        kap[5 * i : 5 * i + 5, :] = kappa[i]
        for j in range(5):
            r = 5 * i + j
            value = guess[i, j]
            left = rhs[i, j] - value
            for s in range(2):
                x[s * 32 + r : s * 32 + r + 1, :] = value[s : s + 1]
                stack[s * 32 + r : s * 32 + r + 1, :] = left[s : s + 1]
    flag = flags[:, 0, 0, :].astype(F32)
    spread = (iota((EZ, 160), 1) // 5 == iota((EZ, 160), 0)).astype(F32)
    wide = split_dot(flag, spread)
    gains = [face_gains(wide[d : d + 1, :], d // 2, d % 2, 5) for d in range(6)]
    row = iota((32, 160), 0)
    lane = iota((32, 160), 1) % 5
    none = jnp.zeros((32, 160), F32)
    gx = jnp.where(row < 5, gains[0], jnp.where((row >= 20) & (row < 25), gains[1], none))
    gy = jnp.where(row % 5 == 0, gains[2], jnp.where(row % 5 == 4, gains[3], none))
    gz = jnp.where(lane == 0, gains[4], jnp.where(lane == 4, gains[5], none))
    field = x[...]
    along = exact_dot(rows_t[...], field)
    across = exact_dot(field, lines_t[...])
    own = kap[...] + gx + gy + gz
    for s in range(2):
        r = slice(s * 32, s * 32 + 32)
        image = own * field[r] + along[r] + across[r, :160] - gz * across[r, 160:]
        stack[64 + s * 32 : 96 + s * 32, :] = image
    stack[128:, :] = field
    source = stack[...]
    back, back_matrix = split_sections()[1:3]
    nodes[...] = jnp.zeros_like(nodes)
    for k in range(5):
        parts = split_dot(source, pick_line(k))
        for p, mark in enumerate((True, False)):
            total = jnp.zeros((32, 128), F32)
            trace = jnp.zeros((32, 128), F32)
            for s in range(2):
                total = total + pair_factors(sec, back, mark, s) * parts[s * 32 : s * 32 + 32]
                factor = pair_factors(sec, STEP_SIZE * back_matrix, mark, s)
                total = total - factor * parts[64 + s * 32 : 96 + s * 32]
                trace = trace + factor * parts[128 + s * 32 : 160 + s * 32]
            nodes[128 * p + 25 * k : 128 * p + 25 * k + 25, :] = total[:25]
            start = 80 * p + 16 * k
            traces[start : start + 5, :] = trace[:5]
            for i in range(1, 4):
                for j in (0, 4):
                    r = start + face_place(i, j)
                    traces[r : r + 1, :] = trace[5 * i + j : 5 * i + j + 1]
            traces[start + 11 : start + 16, :] = trace[20:25]
    for p, out in enumerate((mine, theirs)):
        out[:HALF, :] = pack_nodes(nodes[128 * p : 128 * p + 128, :])
        out[HALF:, :] = pack_nodes(traces[80 * p : 80 * p + 80, :])


VMEM = pl.BlockSpec(memory_space=pltpu.VMEM)
HBM = pl.BlockSpec(memory_space=pltpu.HBM)


def limit(mib):
    return pltpu.CompilerParams(vmem_limit_bytes=mib * 2**20)


def coefs_part(kappa, flags):
    operands = (kappa, flags)
    return pl.pallas_call(
        coefs_kernel,
        out_shape=jax.ShapeDtypeStruct((COEFS, 128), F32),
        in_specs=[HBM] * 2,
        out_specs=VMEM,
        scratch_shapes=[pltpu.VMEM(o.shape, o.dtype) for o in operands]
        + [pltpu.SemaphoreType.DMA((2,)), pltpu.VMEM((32, 160), F32), pltpu.VMEM((128, 128), F32)],
        compiler_params=limit(60),
        name="coefs_part",
    )(*operands)


def local_part(rhs, guess, kappa, flags):
    rows_t, lines_t = column_tables()
    operands = (rhs, guess, kappa, flags, jnp.asarray(rows_t), jnp.asarray(lines_t))
    return pl.pallas_call(
        local_kernel,
        out_shape=[jax.ShapeDtypeStruct((PIECE, 128), F32)] * 2,
        in_specs=[HBM] * 6,
        out_specs=[VMEM] * 2,
        scratch_shapes=[pltpu.VMEM(o.shape, o.dtype) for o in operands]
        + [
            pltpu.SemaphoreType.DMA((6,)),
            pltpu.VMEM((64, 160), F32),
            pltpu.VMEM((32, 160), F32),
            pltpu.VMEM((192, 160), F32),
            pltpu.VMEM((256, 128), F32),
            pltpu.VMEM((160, 128), F32),
        ],
        compiler_params=limit(60),
        cost_estimate=pl.CostEstimate(flops=20_000_000, bytes_accessed=8_000_000, transcendentals=0),
        name="local_part",
    )(*operands)


class Level:
    def __init__(self, count, refs):
        self.count = count
        self.x, self.dir, self.res, self.f = refs
        self.tables = [element_matrix(count, d) for d in range(3)]
        self.gains = self.diag = self.jac = None


def tile(index):
    return pl.ds(index * 8, 8)


def rows_of(pieces, size, r, h):
    return pieces[pl.ds(8 * h * size + r, 8, stride=size), :]


def place_pieces(blocks, stride, pieces, first, size):
    my_gx, my_gy = lax.axis_index("gx"), lax.axis_index("gy")
    for b, block in enumerate(blocks):
        for a in range(4):
            column = (my_gx ^ a) * 4 + (my_gy ^ b)
            start = pl.multiple_of(column * size, 8)
            pieces[pl.ds(start, size), :] = block[a * stride + first : a * stride + first + size, :]


class Lanes:
    def __init__(self):
        self.lane = iota((8, 128), 1)
        sub = iota((8, 128), 0)
        self.group = self.lane // EZ
        self.odd = self.group % 2 == 1
        self.element = self.lane % EZ
        self.place = sub % 4
        self.low_half = sub < 4

    def around(self, u):
        turned = pltpu.roll(u, 4, u.ndim - 2)
        far = jnp.where(self.odd, pltpu.roll(turned, 32, u.ndim - 1), pltpu.roll(turned, 96, u.ndim - 1))
        return turned, far

    def x_before(self, u):
        turned, far = self.around(u)
        return jnp.where(self.low_half, far, turned)

    def x_after(self, u):
        turned, far = self.around(u)
        return jnp.where(self.low_half, turned, far)

    def y_before(self, u):
        return jnp.where(self.place == 0, pltpu.roll(u, 5, 0), pltpu.roll(u, 1, 0))

    def y_after(self, u):
        return jnp.where(self.place == 3, pltpu.roll(u, 3, 0), pltpu.roll(u, 7, 0))

    def z_before(self, u):
        return jnp.where(self.element == 0, pltpu.roll(u, 97, u.ndim - 1), pltpu.roll(u, 1, u.ndim - 1))

    def z_after(self, u):
        last = self.element == EZ - 1
        return jnp.where(last, pltpu.roll(u, 31, u.ndim - 1), pltpu.roll(u, 127, u.ndim - 1))


def assemble_kernel(block0, block1, block2, block3, coefs, field, pieces, edges, traces):
    blocks = (block0, block1, block2, block3)
    place_pieces(blocks, PIECE, pieces, 0, HALF)
    place_pieces(blocks, PIECE, edges, HALF, TRACE)
    lanes = Lanes()

    def widen(source, size, target):
        for r in range(size):
            low, high = rows_of(source, size, r, 0), rows_of(source, size, r, 1)
            target[tile(r), :] = jnp.where(lanes.odd, pltpu.roll(high, 32, 1), low)
            target[tile(size + r), :] = jnp.where(lanes.odd, high, pltpu.roll(low, 96, 1))

    widen(edges, TRACE, traces)
    widen(pieces, HALF, field)
    gains = [coefs[tile(GAINS[0] + d), :] for d in range(4)]
    for k in range(5):
        def trace(i, j, k=k):
            return traces[tile(k * 16 + face_place(i, j)), :]

        for m in range(5):
            for where, term in (
                (m, gains[0] * lanes.x_before(trace(4, m))),
                (20 + m, gains[1] * lanes.x_after(trace(0, m))),
                (5 * m, gains[2] * lanes.y_before(trace(m, 4))),
                (5 * m + 4, gains[3] * lanes.y_after(trace(m, 0))),
            ):
                field[tile(k * 25 + where), :] = field[tile(k * 25 + where), :] + term


def load(ref, first, count):
    start = first * 8 if isinstance(first, int) else pl.multiple_of(first * 8, 8)
    return ref[pl.ds(start, count * 8), :].reshape(count, 8, 128)


def store(ref, first, value):
    start = first * 8 if isinstance(first, int) else pl.multiple_of(first * 8, 8)
    ref[pl.ds(start, value.shape[0] * 8), :] = value.reshape(value.shape[0] * 8, 128)


DIAGS = (0, 250, 304)
GAINS = (320, 326, 332)
REGISTERS = 338
CENTRE = (CHEB_HIGH + CHEB_LOW) / 2.0
RADIUS = (CHEB_HIGH - CHEB_LOW) / 2.0


def setup_kernel(block0, block1, block2, block3, coefs, pieces, kap):
    place_pieces((block0, block1, block2, block3), COEFS, pieces, 0, COEFS)
    lanes = Lanes()
    group = lanes.group

    def widen(r):
        turned = []
        for h in range(2):
            got = rows_of(pieces, COEFS, r, h)
            turned.append([pltpu.roll(got, 32 * m, 1) if m else got for m in range(4)])
        return [choose(group, [turned[g % 2][(g - q) % 4] for g in range(4)]) for q in range(4)]

    for r in range(32):
        for q, part in enumerate(widen(r)):
            kap[tile(q * 32 + r), :] = part
    flags = widen(32) + widen(33)[:2]
    for p, n in enumerate((5, 3, 2)):
        stride = 4 // (n - 1)
        gains = [face_gains(flags[d], d // 2, d % 2, n) for d in range(6)]
        rows = []
        for d in range(3):
            coefs[tile(GAINS[p] + 2 * d), :] = gains[2 * d]
            coefs[tile(GAINS[p] + 2 * d + 1), :] = gains[2 * d + 1]
            table = element_matrix(n, d)
            row = [jnp.full((8, 128), float(table[m, m]), F32) for m in range(n)]
            row[0] = row[0] + gains[2 * d]
            row[n - 1] = row[n - 1] + gains[2 * d + 1]
            rows.append(row)
        along = jnp.stack(rows[1])
        for k in range(n):
            for i in range(n):
                line = load(kap, k * 25 * stride + i * stride * 5, 5)
                line = jnp.stack([line[j * stride] for j in range(n)])
                value = line + (along + (rows[2][k] + rows[0][i]))
                scale = 1.0 / (1.0 + STEP_SIZE * JACOBI_SCALE * value)
                store(coefs, DIAGS[p] + (k * n + i) * n, value)
                store(coefs, DIAGS[p] + n**3 + (k * n + i) * n, scale * (1.0 / CENTRE))


def cycle_kernel(coefs, assembled, fields, *scratch):
    sec = lax.axis_index("section")
    my_gx, my_gy = lax.axis_index("gx"), lax.axis_index("gy")
    levels = [Level(n, scratch[4 * p : 4 * p + 4]) for p, n in enumerate((5, 3, 2))]
    half = scratch[12]
    lanes = Lanes()
    lane = lanes.lane
    blocks = split_sections()[3]

    def lanes_of(upper, lower):
        return jnp.where(lane < 64, jnp.where(sec == 0, upper[0], upper[1]), jnp.where(sec == 0, lower[0], lower[1]))

    entry = [[[float(STEP_SIZE * blocks[2 * p + a, 2 * p + b]) for p in range(2)] for b in range(2)] for a in range(2)]
    same = lanes_of(entry[0][0], entry[1][1])
    swap = lanes_of(entry[0][1], entry[1][0])
    first_rho = RADIUS / CENTRE
    second_rho = 1.0 / (2.0 * CENTRE / RADIUS - first_rho)
    keep = 1.0 + second_rho * first_rho
    push = 2.0 * second_rho / RADIUS * CENTRE
    for p, level in enumerate(levels):
        size = level.count**3
        level.gains = [coefs[tile(GAINS[p] + d), :] for d in range(6)]
        level.diag = lambda first, count, p=p: load(coefs, DIAGS[p] + first, count)
        level.jac = lambda first, count, p=p, size=size: load(coefs, DIAGS[p] + size + first, count)

    def begin(level, source):
        n = level.count
        for first in range(0, n**3, n):
            f = load(source, first, n)
            store(level.dir, first, level.jac(first, n) * f)
            store(level.res, first, f)
            store(level.x, first, jnp.zeros_like(f))

    def apply(level, smooth):
        n = level.count
        kx, ky, kz = level.tables
        gains = level.gains
        source = level.dir if smooth else level.x
        for k in range(n):
            here = k * n * n
            v = [load(source, here + i * n, n) for i in range(n)]
            waiting = []
            for i in range(n):
                first = here + i * n
                total = level.diag(first, n) * v[i]
                for m in range(n):
                    if m != i:
                        total = total + float(kx[i, m]) * v[m]
                for m in range(n):
                    if m != k:
                        total = total + float(kz[k, m]) * load(source, (m * n + i) * n, n)
                lines = []
                for j in range(n):
                    line = None
                    for m in range(n):
                        if m != j:
                            term = float(ky[j, m]) * v[i][m]
                            line = term if line is None else line + term
                    if j == 0:
                        line = line - gains[2] * lanes.y_before(v[i][n - 1])
                    if j == n - 1:
                        line = line - gains[3] * lanes.y_after(v[i][0])
                    lines.append(line)
                total = total + jnp.stack(lines)
                if i == 0:
                    total = total - gains[0] * lanes.x_before(v[n - 1])
                if i == n - 1:
                    total = total - gains[1] * lanes.x_after(v[0])
                if k == 0:
                    total = total - gains[4] * lanes.z_before(load(source, ((n - 1) * n + i) * n, n))
                if k == n - 1:
                    total = total - gains[5] * lanes.z_after(load(source, i * n, n))
                image = v[i] + (same * total + swap * pltpu.roll(total, 64, 2))
                if smooth:
                    scaled = level.jac(first, n) * (load(level.res, first, n) - image)
                    waiting.append((level.x, first, load(level.x, first, n) + keep * v[i] + push * scaled))
                else:
                    rest = load(level.f, first, n) - image
                    waiting.append((level.res, first, rest))
                    waiting.append((level.dir, first, level.jac(first, n) * rest))
                if i % 2 == 1 or i == n - 1:
                    for place_out in waiting:
                        store(*place_out)
                    waiting = []

    def combine(weights, parts):
        total = None
        for weight, part in zip(weights, parts):
            if abs(weight) > 1e-14:
                term = part if abs(weight - 1.0) < 1e-14 else float(weight) * part
                total = term if total is None else total + term
        return total

    def change(table, source, target, add):
        m, n = table.shape
        for i in range(n):
            parts = [load(source, i * n + k * n * n, n) for k in range(n)]
            for k in range(m):
                store(half, i * n + k * n * n, combine(table[k], parts))
        for k in range(m):
            parts = [load(half, k * n * n + i * n, n) for i in range(n)]
            for i in range(m):
                line = combine(table[i], parts)
                value = jnp.stack([combine(table[j], [line[a] for a in range(n)]) for j in range(m)])
                first = k * m * m + i * m
                store(target, first, load(target, first, m) + value if add else value)

    def down(n, m):
        fine_nodes, fine_weights = lobatto(n)
        coarse_nodes, coarse_weights = lobatto(m)
        table = lagrange_table(coarse_nodes, fine_nodes)
        return (1.0 / coarse_weights)[:, None] * table.T * fine_weights[None, :]

    def up(m, n):
        return lagrange_table(lobatto(m)[0], lobatto(n)[0])

    def solve(p):
        level = levels[p]
        if p == 2:
            apply(level, True)
            return
        below = levels[p + 1]

        def step(t, carry):
            @pl.when(t != 1)
            def _():
                apply(level, True)

            @pl.when((t != 2) | (p == 0))
            def _():
                apply(level, False)

            @pl.when(t == 0)
            def _():
                n, m = level.count, below.count
                change(down(n, m), level.res, below.f, False)
                begin(below, below.f)
                solve(p + 1)
                change(up(m, n), below.x, level.x, True)
            return carry
        lax.fori_loop(0, 3, step, 0)

    fine = levels[0]
    fine.f = assembled
    begin(fine, assembled)
    solve(0)

    for first in range(0, 125, 5):
        store(fields, first, load(fine.res, first, 5))
    column = (my_gx % 2) * 4 + my_gy
    fields[FIELD : FIELD + 125, :] = fine.x[pl.ds(column, 125, stride=8), :]
    fields[FIELD + 125 : FIELD + 128, :] = jnp.zeros((3, 128), F32)


def finish_kernel(own, other, own_start, other_start, guess, sol, res_out, arnoldi, cols, outs):
    sec = lax.axis_index("section")
    my_gx, my_gy = lax.axis_index("gx"), lax.axis_index("gy")
    whole, back, back_matrix, blocks, cross = split_sections()
    weights = jnp.where(iota((8, 128), 1) < 64, float(cross[0]), float(cross[1]))
    nothing = jnp.zeros((8, 128), F32)

    lane = iota((32, 128), 1)
    here = lane // EZ % 2 == my_gx // 2
    factors = []
    for s in range(2):
        row = []
        for p in range(2):
            parts = []
            for mine in range(2):
                t = whole[2 * mine + s]
                pairs = [jnp.where(lane < 64, float(t[2 * q]), float(t[2 * q + 1])) for q in range(2)]
                parts.append(pairs[mine] if p == 0 else pairs[1 - mine])
            row.append(jnp.where(here, jnp.where(sec == 0, parts[0], parts[1]), 0.0)[:25])
        factors.append(row)
    column = (my_gx % 2) * 4 + my_gy
    cols[...] = jnp.zeros_like(cols)
    total = jnp.zeros((192, 160), F32)
    for k in range(5):
        where = pl.ds(k * 200 + column, 25, stride=8)
        shown = [[ref[FIELD + k * 25 : FIELD + k * 25 + 25, :] for ref in (own, other)]]
        shown.append([ref[where, :] for ref in (own_start, other_start)])
        shown.append([b[where, :] - a[where, :] for a, b in ((own, own_start), (other, other_start))])
        for f, (a, b) in enumerate(shown):
            for s in range(2):
                r = f * 64 + s * 32
                cols[r : r + 25, :] = factors[s][0] * a + factors[s][1] * b
        hit = (iota((128, 160), 1) == 5 * (iota((128, 160), 0) % EZ) + k).astype(F32)
        total = total + split_dot(cols[...], hit)

    def product(a, b, c, d):
        return (a * c + b * d) + weights * (a * d + b * c)

    uppers, sizes = [nothing] * 5, [nothing] * 5
    for r in range(125):
        a, b, c, d = (ref[tile(r), :] for ref in (own, other, own_start, other_start))
        a, b = c - a, d - b
        uppers[r % 5] = uppers[r % 5] + product(a, b, c, d)
        sizes[r % 5] = sizes[r % 5] + product(c, d, c, d)
    size = jnp.sum(sum(sizes), keepdims=True)
    upper = jnp.sum(sum(uppers), keepdims=True) / size
    rests = [nothing] * 5
    for r in range(125):
        a, b, c, d = (ref[tile(r), :] for ref in (own, other, own_start, other_start))
        a, b = c - a, d - b
        a, b = a - upper * c, b - upper * d
        rests[r % 5] = rests[r % 5] + product(a, b, a, b)
    rest = jnp.sum(sum(rests), keepdims=True)
    beta = jnp.sqrt(size)
    lower = jnp.sqrt(rest) / beta
    weight = upper / (upper * upper + lower * lower)
    entries = float(125 * EZ * COLS * 4)
    for place_out, value in enumerate((beta * (1.0 / math.sqrt(entries)), upper, lower)):
        arnoldi[place_out] = value[0, 0]
    outs[:64, :] = weight * total[:64]
    outs[64:, :] = total[64:128] - weight * total[128:]
    for i in range(5):
        for j in range(5):
            r = 5 * i + j
            for s in range(2):
                sol[i, j, s : s + 1, :] = guess[i, j, s : s + 1, :] + outs[s * 32 + r : s * 32 + r + 1, :]
                res_out[i, j, s : s + 1, :] = outs[64 + s * 32 + r : 64 + s * 32 + r + 1, :]


def setup(blocks):
    return pl.pallas_call(
        setup_kernel,
        out_shape=jax.ShapeDtypeStruct((REGISTERS * 8, 128), F32),
        in_specs=[VMEM] * 4,
        out_specs=VMEM,
        scratch_shapes=[pltpu.VMEM((COLS * COEFS, 128), F32), pltpu.VMEM((128 * 8, 128), F32)],
        compiler_params=limit(16),
        cost_estimate=pl.CostEstimate(flops=4_000_000, bytes_accessed=4_000_000, transcendentals=0),
        name="setup",
    )(*blocks)


def assemble(blocks, coefs):
    return pl.pallas_call(
        assemble_kernel,
        out_shape=jax.ShapeDtypeStruct((128 * 8, 128), F32),
        in_specs=[VMEM] * 5,
        out_specs=VMEM,
        scratch_shapes=[
            pltpu.VMEM((COLS * HALF, 128), F32),
            pltpu.VMEM((COLS * TRACE, 128), F32),
            pltpu.VMEM((80 * 8, 128), F32),
        ],
        compiler_params=limit(16),
        name="assemble",
    )(*blocks, coefs)


def cycle(coefs, assembled):
    scratch = []
    for n in (5, 3, 2):
        scratch += [pltpu.VMEM((n**3 * 8, 128), F32)] * 4
    scratch += [pltpu.VMEM((FIELD, 128), F32)]
    return pl.pallas_call(
        cycle_kernel,
        out_shape=jax.ShapeDtypeStruct((FIELD + 128, 128), F32),
        in_specs=[VMEM] * 2,
        out_specs=VMEM,
        scratch_shapes=scratch,
        compiler_params=limit(24),
        cost_estimate=pl.CostEstimate(flops=40_000_000, bytes_accessed=30_000_000, transcendentals=0),
        name="cycle",
    )(coefs, assembled)


def finish(own, other, own_start, other_start, guess):
    return pl.pallas_call(
        finish_kernel,
        out_shape=[
            jax.ShapeDtypeStruct(guess.shape, F32),
            jax.ShapeDtypeStruct(guess.shape, F32),
            jax.ShapeDtypeStruct((3,), F32),
        ],
        in_specs=[VMEM] * 5,
        out_specs=[VMEM, VMEM, pl.BlockSpec(memory_space=pltpu.SMEM)],
        scratch_shapes=[pltpu.VMEM((192, 128), F32), pltpu.VMEM((128, 160), F32)],
        compiler_params=limit(24),
        name="finish",
    )(own, other, own_start, other_start, guess)


def exchange(x, axis, bits):
    return lax.ppermute(x, axis, [(n, n ^ bits) for n in range(lax.axis_size(axis))])


def gathered_body(rhs, guess, kappa, bc_flags):
    rhs, guess = (jnp.transpose(v, (1, 2, 0, 3)) for v in (rhs, guess))
    coefs = coefs_part(kappa, bc_flags)
    coefs_line = jnp.concatenate([coefs] + [exchange(coefs, "gx", bits) for bits in (1, 2, 3)])
    mine, theirs = local_part(rhs, guess, kappa, bc_flags)
    piece = mine + exchange(theirs, "section", 1)
    piece, coefs_line = lax.optimization_barrier((piece, coefs_line))
    parts = [exchange(piece, "gx", bits) for bits in (1, 2, 3)]
    others = [exchange(coefs_line, "gy", bits) for bits in (1, 2, 3)]
    parts, others = lax.optimization_barrier((parts, others))
    coefs_blocks = [coefs_line] + others
    line = jnp.concatenate([piece] + parts)
    blocks = [line] + [exchange(line, "gy", bits) for bits in (1, 2, 3)]
    all_coefs = setup(coefs_blocks)
    start = assemble(blocks, all_coefs)
    other_start = exchange(start, "section", 1)
    own, other_start = lax.optimization_barrier((cycle(all_coefs, start), other_start))
    sol, res, arnoldi = finish(own, exchange(own, "section", 1), start, other_start, guess)
    sol, res = (jnp.transpose(v, (2, 0, 1, 3)) for v in (sol, res))
    return sol, res, arnoldi


def solution(mesh):
    placed = (
        P("section", "gx", "gy", None),
        P("section", "gx", "gy", None),
        P("gx", "gy", None),
        P(None, "gx", "gy", None),
    )
    sizes = (mesh.shape["section"], mesh.shape["gx"], mesh.shape["gy"])

    def step(rhs, guess, kappa, bc_flags):
        fits = sizes == (2, 4, 4) and rhs.shape == (4, 20, 20, 160)
        return jax.shard_map(
            gathered_body if fits else stepwise,
            mesh=mesh,
            in_specs=placed,
            out_specs=(P("section", "gx", "gy", None), P("section", "gx", "gy", None), P()),
            check_vma=False,
        )(rhs, guess, kappa, bc_flags)

    return step
```

```python
from functools import partial
import math

import jax
import jax.numpy as jnp
import numpy as np
from jax import lax
from jax.experimental import pallas as pl
from jax.experimental.pallas import tpu as pltpu
from jax.sharding import PartitionSpec as P

ADVECT = (1.0, 0.7, 0.5)
DIFFUSE = 0.05
STEP_SIZE = 0.2
JACOBI_SCALE = 0.25
CHEB_LOW = 0.25
CHEB_HIGH = 2.0
LETTERS = "abcdef"


def extended(x, sides, width):
    for axis, dim in sides:
        peers, length = (lax.axis_size(axis), x.shape[dim])
        up = [(i, (i + 1) % peers) for i in range(peers)]
        down = [(j, i) for i, j in up]
        last = lax.slice_in_dim(x, length - width, length, axis=dim)
        leading = lax.slice_in_dim(x, 0, width, axis=dim)
        before = lax.ppermute(last, axis, up)
        after = lax.ppermute(leading, axis, down)
        x = jnp.concatenate([before, x, after], axis=dim)
    return x


def lobatto(count):
    if count == 5:
        inner = math.sqrt(3.0 / 7.0)
        return (
            np.array([-1.0, -inner, 0.0, inner, 1.0]),
            np.array([0.1, 49.0 / 90.0, 32.0 / 45.0, 49.0 / 90.0, 0.1]),
        )
    if count == 3:
        return (np.array([-1.0, 0.0, 1.0]), np.array([1.0 / 3.0, 4.0 / 3.0, 1.0 / 3.0]))
    return (np.array([-1.0, 1.0]), np.array([1.0, 1.0]))


def lagrange_table(nodes, points):
    table = np.ones((len(points), len(nodes)))
    for column in range(len(nodes)):
        for other in range(len(nodes)):
            if other != column:
                table[:, column] *= (points - nodes[other]) / (nodes[column] - nodes[other])
    return table


def slope_table(nodes):
    total = len(nodes)
    factor = np.array(
        [np.prod([nodes[i] - nodes[k] for k in range(total) if k != i]) for i in range(total)]
    )
    table = np.zeros((total, total))
    for row in range(total):
        for column in range(total):
            if row != column:
                table[row, column] = factor[row] / factor[column] / (nodes[row] - nodes[column])
        table[row, row] = -np.sum(table[row])
    return table


def element_matrix(count, direction):
    nodes, weights = lobatto(count)
    slopes = slope_table(nodes)
    stiffness = (1.0 / weights)[:, None] * (slopes.T @ (weights[:, None] * slopes))
    return ADVECT[direction] * slopes + DIFFUSE * stiffness


def legendre_pair(point, order):
    values = [1.0, point]
    slopes = [0.0, 1.0]
    for index in range(1, order):
        values.append(
            ((2 * index + 1) * point * values[index] - index * values[index - 1]) / (index + 1)
        )
        slopes.append(slopes[index - 1] + (2 * index + 1) * values[index])
    return (values, slopes)


def radau_nodes():
    starts = [0.0885879595127039, 0.4094668644407347, 0.7876594617608471]
    found = []
    for start in starts:
        point = start
        for sweep in range(30):
            values, slopes = legendre_pair(2.0 * point - 1.0, 4)
            change = (values[4] - values[3]) / (2.0 * (slopes[4] - slopes[3]))
            point = point - change
        found.append(point)
    found.append(1.0)
    return found


def poly_times(coefs, root):
    result = [0.0] * (len(coefs) + 1)
    for index in range(len(coefs)):
        result[index + 1] += coefs[index]
        result[index] -= root * coefs[index]
    return result


def radau_matrix():
    order = 4
    nodes = radau_nodes()
    matrix = np.zeros((order, order))
    for column in range(order):
        coefs = [1.0]
        denominator = 1.0
        for other in range(order):
            if other != column:
                coefs = poly_times(coefs, nodes[other])
                denominator *= nodes[column] - nodes[other]
        for row in range(order):
            upper_end = nodes[row]
            integral = 0.0
            for index in range(len(coefs)):
                integral += coefs[index] * upper_end ** (index + 1) / (index + 1)
            matrix[row, column] = integral / denominator
    return matrix


def node_einsum(table, field, axis):
    labels = LETTERS[: field.ndim]
    source = labels[: axis + 1] + "j" + labels[axis + 2 :]
    target = labels[: axis + 1] + "i" + labels[axis + 2 :]
    return jnp.einsum(
        "ij," + source + "->" + target,
        jnp.asarray(table, jnp.float32),
        field,
        precision=lax.Precision.HIGHEST,
    )


def apply_along(field, axis, count, table):
    shape = field.shape
    split = shape[:axis] + (shape[axis] // count, count) + shape[axis + 1 :]
    mapped = node_einsum(table, field.reshape(split), axis)
    return mapped.reshape(
        shape[:axis] + (mapped.shape[axis] * mapped.shape[axis + 1],) + shape[axis + 1 :]
    )


def line_part(field, axis, count, table, left_gain, right_gain, left_edge, right_edge):
    shape = field.shape
    elements = shape[axis] // count
    split = field.reshape(shape[:axis] + (elements, count) + shape[axis + 1 :])
    linear = node_einsum(table, split, axis)
    first = lax.index_in_dim(split, 0, axis + 1, keepdims=False)
    last = lax.index_in_dim(split, count - 1, axis + 1, keepdims=False)
    before = jnp.concatenate(
        [jnp.expand_dims(left_edge, axis), lax.slice_in_dim(last, 0, elements - 1, axis=axis)], axis
    )
    after = jnp.concatenate(
        [lax.slice_in_dim(first, 1, elements, axis=axis), jnp.expand_dims(right_edge, axis)], axis
    )
    front = jnp.expand_dims(left_gain * (first - before), axis + 1)
    back = jnp.expand_dims(right_gain * (last - after), axis + 1)
    if count > 2:
        middle_shape = list(front.shape)
        middle_shape[axis + 1] = count - 2
        pieces = [front, jnp.zeros(middle_shape, jnp.float32), back]
    else:
        pieces = [front, back]
    return (linear + jnp.concatenate(pieces, axis + 1)).reshape(shape)


def diag_along(shape, axis, count, table, left_gain, right_gain):
    elements = shape[axis] // count
    split = shape[:axis] + (elements, count) + shape[axis + 1 :]
    profile = [1] * len(split)
    profile[axis + 1] = count
    diagonal_entries = np.array([table[index, index] for index in range(count)])
    base = jnp.broadcast_to(jnp.asarray(diagonal_entries, jnp.float32).reshape(profile), split)
    front = jnp.expand_dims(left_gain, axis + 1)
    back = jnp.expand_dims(right_gain, axis + 1)
    if count > 2:
        middle_shape = list(front.shape)
        middle_shape[axis + 1] = count - 2
        pieces = [front, jnp.zeros(middle_shape, jnp.float32), back]
    else:
        pieces = [front, back]
    return (base + jnp.concatenate(pieces, axis + 1)).reshape(shape)


def level_kappa(kappa, count):
    if count == 5:
        return kappa
    picks = np.array([0, 2, 4]) if count == 3 else np.array([0, 4])
    extents = [extent // 5 for extent in kappa.shape]
    grouped = kappa.reshape(extents[0], 5, extents[1], 5, extents[2], 5)
    for axis in (1, 3, 5):
        grouped = jnp.take(grouped, picks, axis=axis)
    return grouped.reshape(extents[0] * count, extents[1] * count, extents[2] * count)


def face_plane(face, direction, count):
    plane = face.astype(jnp.float32)
    for axis in range(3):
        if axis != direction:
            plane = jnp.repeat(plane, count, axis=axis)
    return plane


def build_level(kappa, flags, count):
    nodes, weights = lobatto(count)
    kappa_level = level_kappa(kappa, count)
    tables, lefts, rights = ([], [], [])
    diagonal = kappa_level
    for direction in range(3):
        table = element_matrix(count, direction)
        lower = face_plane(flags[2 * direction], direction, count)
        upper = face_plane(flags[2 * direction + 1], direction, count)
        left_gain = (ADVECT[direction] * (1.0 + lower) / 2.0 + DIFFUSE * count * count) / float(
            weights[0]
        )
        right_gain = (DIFFUSE * count * count - ADVECT[direction] * (1.0 - upper) / 2.0) / float(
            weights[-1]
        )
        tables.append(table)
        lefts.append(left_gain)
        rights.append(right_gain)
        diagonal = diagonal + diag_along(
            kappa_level.shape, direction, count, table, left_gain, right_gain
        )
    scale = 1.0 / (1.0 + STEP_SIZE * JACOBI_SCALE * diagonal)
    return (count, tables, lefts, rights, kappa_level, scale)


def restrict(field, fine_count, coarse_count):
    fine_nodes, fine_weights = lobatto(fine_count)
    coarse_nodes, coarse_weights = lobatto(coarse_count)
    table = (
        (1.0 / coarse_weights)[:, None]
        * lagrange_table(coarse_nodes, fine_nodes).T
        * fine_weights[None, :]
    )
    for axis in range(field.ndim - 3, field.ndim):
        field = apply_along(field, axis, fine_count, table)
    return field


def prolong(field, coarse_count, fine_count):
    fine_nodes, fine_weights = lobatto(fine_count)
    coarse_nodes, coarse_weights = lobatto(coarse_count)
    table = lagrange_table(coarse_nodes, fine_nodes)
    for axis in range(field.ndim - 3, field.ndim):
        field = apply_along(field, axis, coarse_count, table)
    return field


def chebyshev(rhs, start, level, operator):
    centre = (CHEB_HIGH + CHEB_LOW) / 2.0
    radius = (CHEB_HIGH - CHEB_LOW) / 2.0
    ratio = centre / radius
    first_rho = 1.0 / ratio
    second_rho = 1.0 / (2.0 * ratio - first_rho)
    scale = level[5]
    if start is None:
        remain = rhs
    else:
        remain = rhs - operator(start, level)
    step = scale * remain / centre
    guess = step if start is None else start + step
    remain = remain - operator(step, level)
    step = second_rho * first_rho * step + 2.0 * second_rho / radius * scale * remain
    return guess + step


def vcycle(rhs, levels, operator):
    fine, middle, coarse = levels
    fine_x = chebyshev(rhs, None, fine, operator)
    middle_rhs = restrict(rhs - operator(fine_x, fine), 5, 3)
    middle_x = chebyshev(middle_rhs, None, middle, operator)
    coarse_rhs = restrict(middle_rhs - operator(middle_x, middle), 3, 2)
    coarse_x = chebyshev(coarse_rhs, None, coarse, operator)
    middle_x = chebyshev(middle_rhs, middle_x + prolong(coarse_x, 2, 3), middle, operator)
    return chebyshev(rhs, fine_x + prolong(middle_x, 3, 5), fine, operator)


def spatial(field, level):
    count, tables, lefts, rights, kappa_level, scale = level
    padded = extended(field, (("gx", 1), ("gy", 2)), 1)
    total = kappa_level * field
    total = total + line_part(
        field,
        1,
        count,
        tables[0],
        lefts[0],
        rights[0],
        padded[:, 0, 1:-1, :],
        padded[:, -1, 1:-1, :],
    )
    total = total + line_part(
        field,
        2,
        count,
        tables[1],
        lefts[1],
        rights[1],
        padded[:, 1:-1, 0, :],
        padded[:, 1:-1, -1, :],
    )
    total = total + line_part(
        field, 3, count, tables[2], lefts[2], rights[2], field[:, :, :, -1], field[:, :, :, 0]
    )
    return total


def apply_system(field, level, coupling):
    image = spatial(field, level)
    everyone = lax.all_gather(image, "section", axis=0, tiled=True)
    butcher = jnp.asarray(radau_matrix(), jnp.float32)
    rows = lax.dynamic_slice_in_dim(
        butcher, lax.axis_index("section") * field.shape[0], field.shape[0], 0
    )
    mixed = jnp.einsum("ij,jabc->iabc", rows, everyone, precision=lax.Precision.HIGHEST)
    return field + STEP_SIZE * mixed


def global_total(values):
    return lax.psum(values, ("section", "gx", "gy"))


def stepwise(rhs, guess, kappa, bc_flags):
    levels = [build_level(kappa, bc_flags, count) for count in (5, 3, 2)]
    section_operator = partial(apply_system, coupling=None)
    start_residual = rhs - section_operator(guess, levels[0])
    dofs = float(rhs.size * lax.axis_size("section") * lax.axis_size("gx") * lax.axis_size("gy"))
    beta = jnp.sqrt(global_total(jnp.sum(start_residual * start_residual).reshape(1))[0])
    basis = start_residual / beta
    precond = vcycle(basis, levels, section_operator)
    image = section_operator(precond, levels[0])
    upper = global_total(jnp.sum(image * basis).reshape(1))[0]
    remainder = image - upper * basis
    lower = jnp.sqrt(global_total(jnp.sum(remainder * remainder).reshape(1))[0])
    weight = beta * upper / (upper * upper + lower * lower)
    solution = guess + weight * precond
    residual = start_residual - weight * image
    arnoldi = jnp.stack([beta / math.sqrt(dofs), upper, lower]).astype(jnp.float32)
    return (solution, residual, arnoldi)


EZ = 32
COLS = 16
HALF = 64
TRACE = 40
KAPPA = HALF + TRACE
PIECE = KAPPA + 32
FIELD = 1000
F32 = jnp.float32


def split_sections():
    matrix = radau_matrix()
    values, vectors = np.linalg.eig(matrix)
    order = [n for n in np.argsort(np.abs(values.imag), kind="stable") if values[n].imag > 0]
    bases = []
    for n in order:
        plane = np.stack([vectors[:, n].real, vectors[:, n].imag], axis=1)
        bases.append(np.linalg.qr(plane)[0])
    left, cross, right = np.linalg.svd(bases[0].T @ bases[1])
    bases = [bases[0] @ left, bases[1] @ right.T]
    for c in range(2):
        sign = np.sign(bases[0][np.argmax(np.abs(bases[0][:, c])), c])
        bases = [np.concatenate([b[:, :c], sign * b[:, c : c + 1], b[:, c + 1 :]], axis=1) for b in bases]
    whole = np.concatenate(bases, axis=1)
    back = np.linalg.inv(whole)
    return whole, back, back @ matrix, back @ matrix @ whole, cross


def iota(shape, dim):
    return lax.broadcasted_iota(jnp.int32, shape, dim)


def exact_dot(a, b):
    return lax.dot_general(
        a, b, (((1,), (0,)), ((), ())), precision=lax.Precision.HIGHEST, preferred_element_type=F32
    )


def split_dot(a, b):
    high = a.astype(jnp.bfloat16)
    rest = a - high.astype(F32)
    middle = rest.astype(jnp.bfloat16)
    low = (rest - middle.astype(F32)).astype(jnp.bfloat16)
    b = b.astype(jnp.bfloat16)
    return sum(
        lax.dot_general(part, b, (((1,), (0,)), ((), ())), preferred_element_type=F32)
        for part in (low, middle, high)
    )


def choose(index, values):
    out = values[-1]
    for place in range(len(values) - 2, -1, -1):
        out = jnp.where(index == place, values[place], out)
    return out


def face_gains(flag, direction, side, count):
    nodes, weights = lobatto(count)
    c, nu = ADVECT[direction], DIFFUSE * count * count
    if side == 0:
        return (c * (1.0 + flag) / 2.0 + nu) * (1.0 / float(weights[0]))
    return (nu - c * (1.0 - flag) / 2.0) * (1.0 / float(weights[-1]))


def column_tables():
    kx, ky, kz = (element_matrix(5, d) for d in range(3))
    rows = np.zeros((64, 64))
    for s in range(2):
        for i in range(5):
            for j in range(5):
                r = s * 32 + i * 5 + j
                for m in range(5):
                    rows[r, s * 32 + m * 5 + j] += kx[i, m]
                    rows[r, s * 32 + i * 5 + m] += ky[j, m]
    lines = np.zeros((160, 320))
    for e in range(EZ):
        lines[e * 5 : e * 5 + 5, e * 5 : e * 5 + 5] = kz.T
        lines[(e - 1) % EZ * 5 + 4, 160 + e * 5] = 1.0
        lines[(e + 1) % EZ * 5, 160 + e * 5 + 4] = 1.0
    return rows.astype(np.float32), lines.astype(np.float32)


def pick_line(k):
    return (iota((160, 128), 0) == 5 * (iota((160, 128), 1) % EZ) + k).astype(F32)


def pair_factors(sec, table, own, s):
    upper = iota((32, 128), 1) < 64
    first = jnp.where(upper, float(table[0, s]), float(table[1, s]))
    second = jnp.where(upper, float(table[2, 2 + s]), float(table[3, 2 + s]))
    if not own:
        first = jnp.where(upper, float(table[2, s]), float(table[3, s]))
        second = jnp.where(upper, float(table[0, 2 + s]), float(table[1, 2 + s]))
    return jnp.where(sec == 0, first, second)


def pack_nodes(nodes):
    half = nodes.shape[0] // 2
    odd = iota((half, 128), 1) // EZ % 2 == 1
    return jnp.where(odd, nodes[half:, :], nodes[:half, :])


def face_place(i, j):
    if i == 0:
        return j
    if i == 4:
        return 11 + j
    return 3 + 2 * i + (0 if j == 0 else 1)


def fetch(pairs, sems):
    copies = [pltpu.make_async_copy(src, dst, sems.at[n]) for n, (src, dst) in enumerate(pairs)]
    for copy in copies:
        copy.start()
    for copy in copies:
        copy.wait()


def local_kernel(
    rhs_in, guess_in, kappa_in, flags_in, rows_in, lines_in, mine, theirs,
    rhs, guess, kappa, flags, rows_t, lines_t, sems, x, kap, stack, nodes, traces, krep,
):
    sec = lax.axis_index("section")
    fetch(
        [(rhs_in, rhs), (guess_in, guess), (kappa_in, kappa), (flags_in, flags), (rows_in, rows_t), (lines_in, lines_t)],
        sems,
    )
    x[...] = jnp.zeros_like(x)
    kap[...] = jnp.zeros_like(kap)
    stack[...] = jnp.zeros_like(stack)
    for i in range(5):
        kap[5 * i : 5 * i + 5, :] = kappa[i]
        for j in range(5):
            r = 5 * i + j
            value = guess[i, j]
            left = rhs[i, j] - value
            for s in range(2):
                x[s * 32 + r : s * 32 + r + 1, :] = value[s : s + 1]
                stack[s * 32 + r : s * 32 + r + 1, :] = left[s : s + 1]
    flag = flags[:, 0, 0, :].astype(F32)
    spread = (iota((EZ, 160), 1) // 5 == iota((EZ, 160), 0)).astype(F32)
    wide = split_dot(flag, spread)
    gains = [face_gains(wide[d : d + 1, :], d // 2, d % 2, 5) for d in range(6)]
    row = iota((32, 160), 0)
    lane = iota((32, 160), 1) % 5
    none = jnp.zeros((32, 160), F32)
    gx = jnp.where(row < 5, gains[0], jnp.where((row >= 20) & (row < 25), gains[1], none))
    gy = jnp.where(row % 5 == 0, gains[2], jnp.where(row % 5 == 4, gains[3], none))
    gz = jnp.where(lane == 0, gains[4], jnp.where(lane == 4, gains[5], none))
    field = x[...]
    along = exact_dot(rows_t[...], field)
    across = exact_dot(field, lines_t[...])
    own = kap[...] + gx + gy + gz
    for s in range(2):
        r = slice(s * 32, s * 32 + 32)
        image = own * field[r] + along[r] + across[r, :160] - gz * across[r, 160:]
        stack[64 + s * 32 : 96 + s * 32, :] = image
    stack[128:192, :] = field
    stack[192:, :] = kap[...]
    source = stack[...]
    back, back_matrix = split_sections()[1:3]
    nodes[...] = jnp.zeros_like(nodes)
    krep[...] = jnp.zeros_like(krep)
    for k in range(5):
        parts = split_dot(source, pick_line(k))
        for p, mark in enumerate((True, False)):
            total = jnp.zeros((32, 128), F32)
            trace = jnp.zeros((32, 128), F32)
            for s in range(2):
                total = total + pair_factors(sec, back, mark, s) * parts[s * 32 : s * 32 + 32]
                factor = pair_factors(sec, STEP_SIZE * back_matrix, mark, s)
                total = total - factor * parts[64 + s * 32 : 96 + s * 32]
                trace = trace + factor * parts[128 + s * 32 : 160 + s * 32]
            nodes[128 * p + 25 * k : 128 * p + 25 * k + 25, :] = total[:25]
            start = 80 * p + 16 * k
            traces[start : start + 5, :] = trace[:5]
            for i in range(1, 4):
                for j in (0, 4):
                    r = start + face_place(i, j)
                    traces[r : r + 1, :] = trace[5 * i + j : 5 * i + j + 1]
            traces[start + 11 : start + 16, :] = trace[20:25]
        krep[25 * k : 25 * k + 25, :] = parts[192:217]
    repeat = (iota((EZ, 128), 1) % EZ == iota((EZ, 128), 0)).astype(F32)
    shown = split_dot(flag, repeat)
    upper = iota((1, 128), 1) < 64
    for r in range(3):
        nodes[125 + r : 126 + r, :] = jnp.where(upper, shown[2 * r : 2 * r + 1], shown[2 * r + 1 : 2 * r + 2])
    for p, out in enumerate((mine, theirs)):
        out[:HALF, :] = pack_nodes(nodes[128 * p : 128 * p + 128, :])
        out[HALF:KAPPA, :] = pack_nodes(traces[80 * p : 80 * p + 80, :])
    mine[KAPPA:, :] = choose(iota((32, 128), 1) // EZ, [krep[32 * q : 32 * q + 32, :] for q in range(4)])
    theirs[KAPPA:, :] = jnp.zeros((32, 128), F32)


VMEM = pl.BlockSpec(memory_space=pltpu.VMEM)
HBM = pl.BlockSpec(memory_space=pltpu.HBM)


def limit(mib):
    return pltpu.CompilerParams(vmem_limit_bytes=mib * 2**20)


def local_part(rhs, guess, kappa, flags):
    rows_t, lines_t = column_tables()
    operands = (rhs, guess, kappa, flags, jnp.asarray(rows_t), jnp.asarray(lines_t))
    return pl.pallas_call(
        local_kernel,
        out_shape=[jax.ShapeDtypeStruct((PIECE, 128), F32)] * 2,
        in_specs=[HBM] * 6,
        out_specs=[VMEM] * 2,
        scratch_shapes=[pltpu.VMEM(o.shape, o.dtype) for o in operands]
        + [
            pltpu.SemaphoreType.DMA((6,)),
            pltpu.VMEM((64, 160), F32),
            pltpu.VMEM((32, 160), F32),
            pltpu.VMEM((224, 160), F32),
            pltpu.VMEM((256, 128), F32),
            pltpu.VMEM((160, 128), F32),
            pltpu.VMEM((128, 128), F32),
        ],
        compiler_params=limit(60),
        cost_estimate=pl.CostEstimate(flops=20_000_000, bytes_accessed=8_000_000, transcendentals=0),
        name="local_part",
    )(*operands)


class Level:
    def __init__(self, count, refs):
        self.count = count
        self.x, self.dir, self.res, self.f = refs
        self.tables = [element_matrix(count, d) for d in range(3)]
        self.gains = self.diag = self.jac = None


def tile(index):
    return pl.ds(index * 8, 8)


def rows_of(pieces, size, r, h):
    return pieces[pl.ds(8 * h * size + r, 8, stride=size), :]


def place_pieces(blocks, stride, pieces, first, size):
    my_gx, my_gy = lax.axis_index("gx"), lax.axis_index("gy")
    for b, block in enumerate(blocks):
        for a in range(4):
            column = (my_gx ^ a) * 4 + (my_gy ^ b)
            start = pl.multiple_of(column * size, 8)
            pieces[pl.ds(start, size), :] = block[a * stride + first : a * stride + first + size, :]


class Lanes:
    def __init__(self):
        self.lane = iota((8, 128), 1)
        sub = iota((8, 128), 0)
        self.group = self.lane // EZ
        self.odd = self.group % 2 == 1
        self.element = self.lane % EZ
        self.place = sub % 4
        self.low_half = sub < 4

    def around(self, u):
        turned = pltpu.roll(u, 4, u.ndim - 2)
        far = jnp.where(self.odd, pltpu.roll(turned, 32, u.ndim - 1), pltpu.roll(turned, 96, u.ndim - 1))
        return turned, far

    def x_before(self, u):
        turned, far = self.around(u)
        return jnp.where(self.low_half, far, turned)

    def x_after(self, u):
        turned, far = self.around(u)
        return jnp.where(self.low_half, turned, far)

    def y_before(self, u):
        return jnp.where(self.place == 0, pltpu.roll(u, 5, 0), pltpu.roll(u, 1, 0))

    def y_after(self, u):
        return jnp.where(self.place == 3, pltpu.roll(u, 3, 0), pltpu.roll(u, 7, 0))

    def z_before(self, u):
        return jnp.where(self.element == 0, pltpu.roll(u, 97, u.ndim - 1), pltpu.roll(u, 1, u.ndim - 1))

    def z_after(self, u):
        last = self.element == EZ - 1
        return jnp.where(last, pltpu.roll(u, 31, u.ndim - 1), pltpu.roll(u, 127, u.ndim - 1))


def load(ref, first, count):
    return ref[pl.ds(first * 8, count * 8), :].reshape(count, 8, 128)


def store(ref, first, value):
    ref[pl.ds(first * 8, value.shape[0] * 8), :] = value.reshape(value.shape[0] * 8, 128)


DIAGS = (0, 250, 304)
GAINS = (320, 326, 332)
REGISTERS = 338
CENTRE = (CHEB_HIGH + CHEB_LOW) / 2.0
RADIUS = (CHEB_HIGH - CHEB_LOW) / 2.0


def assemble_kernel(block0, block1, block2, block3, field, coefs, pieces, edges, kappas, traces, kap):
    blocks = (block0, block1, block2, block3)
    place_pieces(blocks, PIECE, pieces, 0, HALF)
    place_pieces(blocks, PIECE, edges, HALF, TRACE)
    place_pieces(blocks, PIECE, kappas, KAPPA, 32)
    lanes = Lanes()
    group, lane = lanes.group, lanes.lane

    def widen(source, size, target):
        for r in range(size):
            low, high = rows_of(source, size, r, 0), rows_of(source, size, r, 1)
            target[tile(r), :] = jnp.where(lanes.odd, pltpu.roll(high, 32, 1), low)
            target[tile(size + r), :] = jnp.where(lanes.odd, high, pltpu.roll(low, 96, 1))

    widen(edges, TRACE, traces)
    widen(pieces, HALF, field)
    flags = []
    for r in range(3):
        got = field[tile(125 + r), :]
        across = pltpu.roll(got, 64, 1)
        flags += [jnp.where(lane < 64, got, across), jnp.where(lane < 64, across, got)]
    for r in range(32):
        turned = []
        for h in range(2):
            got = rows_of(kappas, 32, r, h)
            turned.append([pltpu.roll(got, 32 * m, 1) if m else got for m in range(4)])
        for q in range(4):
            kap[tile(q * 32 + r), :] = choose(group, [turned[g % 2][(g - q) % 4] for g in range(4)])
    for p, n in enumerate((5, 3, 2)):
        stride = 4 // (n - 1)
        gains = [face_gains(flags[d], d // 2, d % 2, n) for d in range(6)]
        if p == 0:
            for k in range(5):
                def trace(i, j, k=k):
                    return traces[tile(k * 16 + face_place(i, j)), :]

                for m in range(5):
                    for where, term in (
                        (m, gains[0] * lanes.x_before(trace(4, m))),
                        (20 + m, gains[1] * lanes.x_after(trace(0, m))),
                        (5 * m, gains[2] * lanes.y_before(trace(m, 4))),
                        (5 * m + 4, gains[3] * lanes.y_after(trace(m, 0))),
                    ):
                        field[tile(k * 25 + where), :] = field[tile(k * 25 + where), :] + term
        rows = []
        for d in range(3):
            coefs[tile(GAINS[p] + 2 * d), :] = gains[2 * d]
            coefs[tile(GAINS[p] + 2 * d + 1), :] = gains[2 * d + 1]
            table = element_matrix(n, d)
            row = [jnp.full((8, 128), float(table[m, m]), F32) for m in range(n)]
            row[0] = row[0] + gains[2 * d]
            row[n - 1] = row[n - 1] + gains[2 * d + 1]
            rows.append(row)
        along = jnp.stack(rows[1])
        for k in range(n):
            for i in range(n):
                line = load(kap, k * 25 * stride + i * stride * 5, 5)
                line = jnp.stack([line[j * stride] for j in range(n)])
                value = line + (along + (rows[2][k] + rows[0][i]))
                scale = 1.0 / (1.0 + STEP_SIZE * JACOBI_SCALE * value)
                store(coefs, DIAGS[p] + (k * n + i) * n, value)
                store(coefs, DIAGS[p] + n**3 + (k * n + i) * n, scale * (1.0 / CENTRE))


def cycle_kernel(coefs, assembled, fields, *scratch):
    sec = lax.axis_index("section")
    my_gx, my_gy = lax.axis_index("gx"), lax.axis_index("gy")
    levels = [Level(n, scratch[4 * p : 4 * p + 4]) for p, n in enumerate((5, 3, 2))]
    half = scratch[12]
    lanes = Lanes()
    lane = lanes.lane
    blocks = split_sections()[3]

    def lanes_of(upper, lower):
        return jnp.where(lane < 64, jnp.where(sec == 0, upper[0], upper[1]), jnp.where(sec == 0, lower[0], lower[1]))

    entry = [[[float(STEP_SIZE * blocks[2 * p + a, 2 * p + b]) for p in range(2)] for b in range(2)] for a in range(2)]
    same = lanes_of(entry[0][0], entry[1][1])
    swap = lanes_of(entry[0][1], entry[1][0])
    first_rho = RADIUS / CENTRE
    second_rho = 1.0 / (2.0 * CENTRE / RADIUS - first_rho)
    keep = 1.0 + second_rho * first_rho
    push = 2.0 * second_rho / RADIUS * CENTRE
    for p, level in enumerate(levels):
        size = level.count**3
        level.gains = [coefs[tile(GAINS[p] + d), :] for d in range(6)]
        level.diag = lambda first, count, p=p: load(coefs, DIAGS[p] + first, count)
        level.jac = lambda first, count, p=p, size=size: load(coefs, DIAGS[p] + size + first, count)

    def begin(level, source):
        n = level.count
        for first in range(0, n**3, n):
            f = load(source, first, n)
            store(level.dir, first, level.jac(first, n) * f)
            store(level.res, first, f)
            store(level.x, first, jnp.zeros_like(f))

    def apply(level, smooth):
        n = level.count
        kx, ky, kz = level.tables
        gains = level.gains
        source = level.dir if smooth else level.x
        for k in range(n):
            def line_at(i, k=k):
                return load(source, (k * n + i) * n, n)

            for i in range(n):
                first = (k * n + i) * n
                v = line_at(i)
                total = level.diag(first, n) * v
                for m in range(n):
                    if m != i:
                        total = total + float(kx[i, m]) * line_at(m)
                for m in range(n):
                    if m != k:
                        total = total + float(kz[k, m]) * load(source, (m * n + i) * n, n)
                lines = []
                for j in range(n):
                    line = None
                    for m in range(n):
                        if m != j:
                            term = float(ky[j, m]) * v[m]
                            line = term if line is None else line + term
                    if j == 0:
                        line = line - gains[2] * lanes.y_before(v[n - 1])
                    if j == n - 1:
                        line = line - gains[3] * lanes.y_after(v[0])
                    lines.append(line)
                total = total + jnp.stack(lines)
                if i == 0:
                    total = total - gains[0] * lanes.x_before(line_at(n - 1))
                if i == n - 1:
                    total = total - gains[1] * lanes.x_after(line_at(0))
                if k == 0:
                    total = total - gains[4] * lanes.z_before(load(source, ((n - 1) * n + i) * n, n))
                if k == n - 1:
                    total = total - gains[5] * lanes.z_after(load(source, i * n, n))
                image = v + (same * total + swap * pltpu.roll(total, 64, 2))
                if smooth:
                    scaled = level.jac(first, n) * (load(level.res, first, n) - image)
                    store(level.x, first, load(level.x, first, n) + keep * v + push * scaled)
                else:
                    rest = load(level.f, first, n) - image
                    store(level.res, first, rest)
                    store(level.dir, first, level.jac(first, n) * rest)

    def combine(weights, parts):
        total = None
        for weight, part in zip(weights, parts):
            if abs(weight) > 1e-14:
                term = part if abs(weight - 1.0) < 1e-14 else float(weight) * part
                total = term if total is None else total + term
        return total

    def change(table, source, target, add):
        m, n = table.shape
        for i in range(n):
            parts = [load(source, i * n + k * n * n, n) for k in range(n)]
            for k in range(m):
                store(half, i * n + k * n * n, combine(table[k], parts))
        for k in range(m):
            parts = [load(half, k * n * n + i * n, n) for i in range(n)]
            for i in range(m):
                line = combine(table[i], parts)
                value = jnp.stack([combine(table[j], [line[a] for a in range(n)]) for j in range(m)])
                first = k * m * m + i * m
                store(target, first, load(target, first, m) + value if add else value)

    def down(n, m):
        fine_nodes, fine_weights = lobatto(n)
        coarse_nodes, coarse_weights = lobatto(m)
        table = lagrange_table(coarse_nodes, fine_nodes)
        return (1.0 / coarse_weights)[:, None] * table.T * fine_weights[None, :]

    def up(m, n):
        return lagrange_table(lobatto(m)[0], lobatto(n)[0])

    def solve(p):
        level = levels[p]
        if p == 2:
            apply(level, True)
            return
        below = levels[p + 1]

        def step(t, carry):
            @pl.when(t != 1)
            def _():
                apply(level, True)

            @pl.when((t != 2) | (p == 0))
            def _():
                apply(level, False)

            @pl.when(t == 0)
            def _():
                n, m = level.count, below.count
                change(down(n, m), level.res, below.f, False)
                begin(below, below.f)
                solve(p + 1)
                change(up(m, n), below.x, level.x, True)
            return carry
        lax.fori_loop(0, 3, step, 0)

    fine = levels[0]
    fine.f = assembled
    begin(fine, assembled)
    solve(0)

    for first in range(0, 125, 5):
        store(fields, first, load(fine.res, first, 5))
    column = (my_gx % 2) * 4 + my_gy
    fields[FIELD : FIELD + 125, :] = fine.x[pl.ds(column, 125, stride=8), :]
    fields[FIELD + 125 : FIELD + 128, :] = jnp.zeros((3, 128), F32)


def pair_weights():
    cross = split_sections()[4]
    return jnp.where(iota((8, 128), 1) < 64, float(cross[0]), float(cross[1]))


def column_factors(p):
    sec = lax.axis_index("section")
    whole = split_sections()[0]
    lane = iota((25, 128), 1)
    here = lane // EZ % 2 == lax.axis_index("gx") // 2
    factors = []
    for s in range(2):
        parts = []
        for mine in range(2):
            t = whole[2 * mine + s]
            q = mine if p == 0 else 1 - mine
            parts.append(jnp.where(lane < 64, float(t[2 * q]), float(t[2 * q + 1])))
        factors.append(jnp.where(here, jnp.where(sec == 0, parts[0], parts[1]), 0.0))
    return factors


def column_rows(k):
    column = (lax.axis_index("gx") % 2) * 4 + lax.axis_index("gy")
    return pl.ds(k * 200 + column, 25, stride=8)


def raw_order(k):
    return (iota((128, 160), 1) == 5 * (iota((128, 160), 0) % EZ) + k).astype(F32)


def early_kernel(own, own_start, other_start, sums, column_out, cols):
    weights = pair_weights()
    cols[...] = jnp.zeros_like(cols)
    total = jnp.zeros((192, 160), F32)
    own_factors, other_factors = column_factors(0), column_factors(1)
    for k in range(5):
        where = column_rows(k)
        z = own[FIELD + k * 25 : FIELD + k * 25 + 25, :]
        start, other = own_start[where, :], other_start[where, :]
        w = start - own[where, :]
        for s in range(2):
            cols[s * 32 : s * 32 + 25, :] = own_factors[s] * z
            cols[64 + s * 32 : 64 + s * 32 + 25, :] = own_factors[s] * start + other_factors[s] * other
            cols[128 + s * 32 : 128 + s * 32 + 25, :] = own_factors[s] * w
        total = total + split_dot(cols[...], raw_order(k))
    column_out[...] = total
    nothing = jnp.zeros((8, 128), F32)
    uppers, sizes = [nothing] * 5, [nothing] * 5
    for r in range(125):
        c, d = own_start[tile(r), :], other_start[tile(r), :]
        a = c - own[tile(r), :]
        uppers[r % 5] = uppers[r % 5] + a * (c + weights * d)
        sizes[r % 5] = sizes[r % 5] + ((c * c + d * d) + 2.0 * (weights * (c * d)))
    sums[0:8, :] = sum(uppers)
    sums[8:16, :] = sum(sizes)


def finish_kernel(own, other, own_start, other_start, sums, column, guess, sol, res_out, arnoldi, cols, outs):
    sec = lax.axis_index("section")
    weights = pair_weights()
    cols[...] = jnp.zeros_like(cols)
    total = jnp.zeros((128, 160), F32)
    factors = column_factors(1)
    for k in range(5):
        where = column_rows(k)
        z = other[FIELD + k * 25 : FIELD + k * 25 + 25, :]
        w = other_start[where, :] - other[where, :]
        for s in range(2):
            cols[s * 32 : s * 32 + 25, :] = factors[s] * z
            cols[64 + s * 32 : 64 + s * 32 + 25, :] = factors[s] * w
        total = total + split_dot(cols[...], raw_order(k))
    nothing = jnp.zeros((8, 128), F32)
    uppers = [nothing] * 5
    for r in range(125):
        c, d = own_start[tile(r), :], other_start[tile(r), :]
        b = d - other[tile(r), :]
        uppers[r % 5] = uppers[r % 5] + b * (d + weights * c)

    mine, theirs = sums[0:8, :], sum(uppers)
    size = jnp.sum(sums[8:16, :], keepdims=True)
    upper = jnp.sum(mine + theirs, keepdims=True) / size
    rests = [nothing] * 5
    for r in range(125):
        c, d = own_start[tile(r), :], other_start[tile(r), :]
        a = (c - own[tile(r), :]) - upper * c
        b = (d - other[tile(r), :]) - upper * d
        rests[r % 5] = rests[r % 5] + ((a * a + b * b) + 2.0 * (weights * (a * b)))
    rest = jnp.sum(sum(rests), keepdims=True)
    beta = jnp.sqrt(size)
    lower = jnp.sqrt(rest) / beta
    weight = upper / (upper * upper + lower * lower)
    entries = float(125 * EZ * COLS * 4)
    for place_out, value in enumerate((beta * (1.0 / math.sqrt(entries)), upper, lower)):
        arnoldi[place_out] = value[0, 0]
    outs[:64, :] = weight * (column[:64, :] + total[:64])
    outs[64:, :] = column[64:128, :] - weight * (column[128:, :] + total[64:])
    for i in range(5):
        for j in range(5):
            r = 5 * i + j
            for s in range(2):
                sol[i, j, s : s + 1, :] = guess[i, j, s : s + 1, :] + outs[s * 32 + r : s * 32 + r + 1, :]
                res_out[i, j, s : s + 1, :] = outs[64 + s * 32 + r : 64 + s * 32 + r + 1, :]


def assemble(blocks):
    return pl.pallas_call(
        assemble_kernel,
        out_shape=[
            jax.ShapeDtypeStruct((128 * 8, 128), F32),
            jax.ShapeDtypeStruct((REGISTERS * 8, 128), F32),
        ],
        in_specs=[VMEM] * 4,
        out_specs=[VMEM] * 2,
        scratch_shapes=[
            pltpu.VMEM((COLS * HALF, 128), F32),
            pltpu.VMEM((COLS * TRACE, 128), F32),
            pltpu.VMEM((COLS * 32, 128), F32),
            pltpu.VMEM((80 * 8, 128), F32),
            pltpu.VMEM((128 * 8, 128), F32),
        ],
        compiler_params=limit(16),
        name="assemble",
    )(*blocks)


def cycle(coefs, assembled):
    scratch = []
    for n in (5, 3, 2):
        scratch += [pltpu.VMEM((n**3 * 8, 128), F32)] * 4
    scratch += [pltpu.VMEM((FIELD, 128), F32)]
    return pl.pallas_call(
        cycle_kernel,
        out_shape=jax.ShapeDtypeStruct((FIELD + 128, 128), F32),
        in_specs=[VMEM] * 2,
        out_specs=VMEM,
        scratch_shapes=scratch,
        compiler_params=limit(24),
        cost_estimate=pl.CostEstimate(flops=40_000_000, bytes_accessed=30_000_000, transcendentals=0),
        name="cycle",
    )(coefs, assembled)


def early(own, own_start, other_start):
    return pl.pallas_call(
        early_kernel,
        out_shape=[jax.ShapeDtypeStruct((16, 128), F32), jax.ShapeDtypeStruct((192, 160), F32)],
        in_specs=[VMEM] * 3,
        out_specs=[VMEM] * 2,
        scratch_shapes=[pltpu.VMEM((192, 128), F32)],
        compiler_params=limit(16),
        cost_estimate=pl.CostEstimate(flops=4_000_000, bytes_accessed=4_000_000, transcendentals=0),
        name="early",
    )(own, own_start, other_start)


def finish(own, other, own_start, other_start, sums, column, guess):
    return pl.pallas_call(
        finish_kernel,
        out_shape=[
            jax.ShapeDtypeStruct(guess.shape, F32),
            jax.ShapeDtypeStruct(guess.shape, F32),
            jax.ShapeDtypeStruct((3,), F32),
        ],
        in_specs=[VMEM] * 7,
        out_specs=[VMEM, VMEM, pl.BlockSpec(memory_space=pltpu.SMEM)],
        scratch_shapes=[pltpu.VMEM((128, 128), F32), pltpu.VMEM((128, 160), F32)],
        compiler_params=limit(24),
        name="finish",
    )(own, other, own_start, other_start, sums, column, guess)


def exchange(x, axis, bits):
    return lax.ppermute(x, axis, [(n, n ^ bits) for n in range(lax.axis_size(axis))])


def gathered_body(rhs, guess, kappa, bc_flags):
    rhs, guess = (jnp.transpose(v, (1, 2, 0, 3)) for v in (rhs, guess))
    mine, theirs = local_part(rhs, guess, kappa, bc_flags)
    piece = mine + exchange(theirs, "section", 1)
    line = jnp.concatenate([piece] + [exchange(piece, "gx", bits) for bits in (1, 2, 3)])
    blocks = [line] + [exchange(line, "gy", bits) for bits in (1, 2, 3)]
    start, coefs = assemble(blocks)
    other_start = exchange(start, "section", 1)
    own, other_start = lax.optimization_barrier((cycle(coefs, start), other_start))
    sums, column = early(own, start, other_start)
    sol, res, arnoldi = finish(own, exchange(own, "section", 1), start, other_start, sums, column, guess)
    sol, res = (jnp.transpose(v, (2, 0, 1, 3)) for v in (sol, res))
    return sol, res, arnoldi


def solution(mesh):
    placed = (
        P("section", "gx", "gy", None),
        P("section", "gx", "gy", None),
        P("gx", "gy", None),
        P(None, "gx", "gy", None),
    )
    sizes = (mesh.shape["section"], mesh.shape["gx"], mesh.shape["gy"])

    def step(rhs, guess, kappa, bc_flags):
        fits = sizes == (2, 4, 4) and rhs.shape == (4, 20, 20, 160)
        return jax.shard_map(
            gathered_body if fits else stepwise,
            mesh=mesh,
            in_specs=placed,
            out_specs=(P("section", "gx", "gy", None), P("section", "gx", "gy", None), P()),
            check_vma=False,
        )(rhs, guess, kappa, bc_flags)

    return step
```

```python
from functools import partial
import math

import jax
import jax.numpy as jnp
import numpy as np
from jax import lax
from jax.experimental import pallas as pl
from jax.experimental.pallas import tpu as pltpu
from jax.sharding import PartitionSpec as P

ADVECT = (1.0, 0.7, 0.5)
DIFFUSE = 0.05
STEP_SIZE = 0.2
JACOBI_SCALE = 0.25
CHEB_LOW = 0.25
CHEB_HIGH = 2.0
LETTERS = "abcdef"


def extended(x, sides, width):
    for axis, dim in sides:
        peers, length = (lax.axis_size(axis), x.shape[dim])
        up = [(i, (i + 1) % peers) for i in range(peers)]
        down = [(j, i) for i, j in up]
        last = lax.slice_in_dim(x, length - width, length, axis=dim)
        leading = lax.slice_in_dim(x, 0, width, axis=dim)
        before = lax.ppermute(last, axis, up)
        after = lax.ppermute(leading, axis, down)
        x = jnp.concatenate([before, x, after], axis=dim)
    return x


def lobatto(count):
    if count == 5:
        inner = math.sqrt(3.0 / 7.0)
        return (
            np.array([-1.0, -inner, 0.0, inner, 1.0]),
            np.array([0.1, 49.0 / 90.0, 32.0 / 45.0, 49.0 / 90.0, 0.1]),
        )
    if count == 3:
        return (np.array([-1.0, 0.0, 1.0]), np.array([1.0 / 3.0, 4.0 / 3.0, 1.0 / 3.0]))
    return (np.array([-1.0, 1.0]), np.array([1.0, 1.0]))


def lagrange_table(nodes, points):
    table = np.ones((len(points), len(nodes)))
    for column in range(len(nodes)):
        for other in range(len(nodes)):
            if other != column:
                table[:, column] *= (points - nodes[other]) / (nodes[column] - nodes[other])
    return table


def slope_table(nodes):
    total = len(nodes)
    factor = np.array(
        [np.prod([nodes[i] - nodes[k] for k in range(total) if k != i]) for i in range(total)]
    )
    table = np.zeros((total, total))
    for row in range(total):
        for column in range(total):
            if row != column:
                table[row, column] = factor[row] / factor[column] / (nodes[row] - nodes[column])
        table[row, row] = -np.sum(table[row])
    return table


def element_matrix(count, direction):
    nodes, weights = lobatto(count)
    slopes = slope_table(nodes)
    stiffness = (1.0 / weights)[:, None] * (slopes.T @ (weights[:, None] * slopes))
    return ADVECT[direction] * slopes + DIFFUSE * stiffness


def legendre_pair(point, order):
    values = [1.0, point]
    slopes = [0.0, 1.0]
    for index in range(1, order):
        values.append(
            ((2 * index + 1) * point * values[index] - index * values[index - 1]) / (index + 1)
        )
        slopes.append(slopes[index - 1] + (2 * index + 1) * values[index])
    return (values, slopes)


def radau_nodes():
    starts = [0.0885879595127039, 0.4094668644407347, 0.7876594617608471]
    found = []
    for start in starts:
        point = start
        for sweep in range(30):
            values, slopes = legendre_pair(2.0 * point - 1.0, 4)
            change = (values[4] - values[3]) / (2.0 * (slopes[4] - slopes[3]))
            point = point - change
        found.append(point)
    found.append(1.0)
    return found


def poly_times(coefs, root):
    result = [0.0] * (len(coefs) + 1)
    for index in range(len(coefs)):
        result[index + 1] += coefs[index]
        result[index] -= root * coefs[index]
    return result


def radau_matrix():
    order = 4
    nodes = radau_nodes()
    matrix = np.zeros((order, order))
    for column in range(order):
        coefs = [1.0]
        denominator = 1.0
        for other in range(order):
            if other != column:
                coefs = poly_times(coefs, nodes[other])
                denominator *= nodes[column] - nodes[other]
        for row in range(order):
            upper_end = nodes[row]
            integral = 0.0
            for index in range(len(coefs)):
                integral += coefs[index] * upper_end ** (index + 1) / (index + 1)
            matrix[row, column] = integral / denominator
    return matrix


def node_einsum(table, field, axis):
    labels = LETTERS[: field.ndim]
    source = labels[: axis + 1] + "j" + labels[axis + 2 :]
    target = labels[: axis + 1] + "i" + labels[axis + 2 :]
    return jnp.einsum(
        "ij," + source + "->" + target,
        jnp.asarray(table, jnp.float32),
        field,
        precision=lax.Precision.HIGHEST,
    )


def apply_along(field, axis, count, table):
    shape = field.shape
    split = shape[:axis] + (shape[axis] // count, count) + shape[axis + 1 :]
    mapped = node_einsum(table, field.reshape(split), axis)
    return mapped.reshape(
        shape[:axis] + (mapped.shape[axis] * mapped.shape[axis + 1],) + shape[axis + 1 :]
    )


def line_part(field, axis, count, table, left_gain, right_gain, left_edge, right_edge):
    shape = field.shape
    elements = shape[axis] // count
    split = field.reshape(shape[:axis] + (elements, count) + shape[axis + 1 :])
    linear = node_einsum(table, split, axis)
    first = lax.index_in_dim(split, 0, axis + 1, keepdims=False)
    last = lax.index_in_dim(split, count - 1, axis + 1, keepdims=False)
    before = jnp.concatenate(
        [jnp.expand_dims(left_edge, axis), lax.slice_in_dim(last, 0, elements - 1, axis=axis)], axis
    )
    after = jnp.concatenate(
        [lax.slice_in_dim(first, 1, elements, axis=axis), jnp.expand_dims(right_edge, axis)], axis
    )
    front = jnp.expand_dims(left_gain * (first - before), axis + 1)
    back = jnp.expand_dims(right_gain * (last - after), axis + 1)
    if count > 2:
        middle_shape = list(front.shape)
        middle_shape[axis + 1] = count - 2
        pieces = [front, jnp.zeros(middle_shape, jnp.float32), back]
    else:
        pieces = [front, back]
    return (linear + jnp.concatenate(pieces, axis + 1)).reshape(shape)


def diag_along(shape, axis, count, table, left_gain, right_gain):
    elements = shape[axis] // count
    split = shape[:axis] + (elements, count) + shape[axis + 1 :]
    profile = [1] * len(split)
    profile[axis + 1] = count
    diagonal_entries = np.array([table[index, index] for index in range(count)])
    base = jnp.broadcast_to(jnp.asarray(diagonal_entries, jnp.float32).reshape(profile), split)
    front = jnp.expand_dims(left_gain, axis + 1)
    back = jnp.expand_dims(right_gain, axis + 1)
    if count > 2:
        middle_shape = list(front.shape)
        middle_shape[axis + 1] = count - 2
        pieces = [front, jnp.zeros(middle_shape, jnp.float32), back]
    else:
        pieces = [front, back]
    return (base + jnp.concatenate(pieces, axis + 1)).reshape(shape)


def level_kappa(kappa, count):
    if count == 5:
        return kappa
    picks = np.array([0, 2, 4]) if count == 3 else np.array([0, 4])
    extents = [extent // 5 for extent in kappa.shape]
    grouped = kappa.reshape(extents[0], 5, extents[1], 5, extents[2], 5)
    for axis in (1, 3, 5):
        grouped = jnp.take(grouped, picks, axis=axis)
    return grouped.reshape(extents[0] * count, extents[1] * count, extents[2] * count)


def face_plane(face, direction, count):
    plane = face.astype(jnp.float32)
    for axis in range(3):
        if axis != direction:
            plane = jnp.repeat(plane, count, axis=axis)
    return plane


def build_level(kappa, flags, count):
    nodes, weights = lobatto(count)
    kappa_level = level_kappa(kappa, count)
    tables, lefts, rights = ([], [], [])
    diagonal = kappa_level
    for direction in range(3):
        table = element_matrix(count, direction)
        lower = face_plane(flags[2 * direction], direction, count)
        upper = face_plane(flags[2 * direction + 1], direction, count)
        left_gain = (ADVECT[direction] * (1.0 + lower) / 2.0 + DIFFUSE * count * count) / float(
            weights[0]
        )
        right_gain = (DIFFUSE * count * count - ADVECT[direction] * (1.0 - upper) / 2.0) / float(
            weights[-1]
        )
        tables.append(table)
        lefts.append(left_gain)
        rights.append(right_gain)
        diagonal = diagonal + diag_along(
            kappa_level.shape, direction, count, table, left_gain, right_gain
        )
    scale = 1.0 / (1.0 + STEP_SIZE * JACOBI_SCALE * diagonal)
    return (count, tables, lefts, rights, kappa_level, scale)


def restrict(field, fine_count, coarse_count):
    fine_nodes, fine_weights = lobatto(fine_count)
    coarse_nodes, coarse_weights = lobatto(coarse_count)
    table = (
        (1.0 / coarse_weights)[:, None]
        * lagrange_table(coarse_nodes, fine_nodes).T
        * fine_weights[None, :]
    )
    for axis in range(field.ndim - 3, field.ndim):
        field = apply_along(field, axis, fine_count, table)
    return field


def prolong(field, coarse_count, fine_count):
    fine_nodes, fine_weights = lobatto(fine_count)
    coarse_nodes, coarse_weights = lobatto(coarse_count)
    table = lagrange_table(coarse_nodes, fine_nodes)
    for axis in range(field.ndim - 3, field.ndim):
        field = apply_along(field, axis, coarse_count, table)
    return field


def chebyshev(rhs, start, level, operator):
    centre = (CHEB_HIGH + CHEB_LOW) / 2.0
    radius = (CHEB_HIGH - CHEB_LOW) / 2.0
    ratio = centre / radius
    first_rho = 1.0 / ratio
    second_rho = 1.0 / (2.0 * ratio - first_rho)
    scale = level[5]
    if start is None:
        remain = rhs
    else:
        remain = rhs - operator(start, level)
    step = scale * remain / centre
    guess = step if start is None else start + step
    remain = remain - operator(step, level)
    step = second_rho * first_rho * step + 2.0 * second_rho / radius * scale * remain
    return guess + step


def vcycle(rhs, levels, operator):
    fine, middle, coarse = levels
    fine_x = chebyshev(rhs, None, fine, operator)
    middle_rhs = restrict(rhs - operator(fine_x, fine), 5, 3)
    middle_x = chebyshev(middle_rhs, None, middle, operator)
    coarse_rhs = restrict(middle_rhs - operator(middle_x, middle), 3, 2)
    coarse_x = chebyshev(coarse_rhs, None, coarse, operator)
    middle_x = chebyshev(middle_rhs, middle_x + prolong(coarse_x, 2, 3), middle, operator)
    return chebyshev(rhs, fine_x + prolong(middle_x, 3, 5), fine, operator)


def spatial(field, level):
    count, tables, lefts, rights, kappa_level, scale = level
    padded = extended(field, (("gx", 1), ("gy", 2)), 1)
    total = kappa_level * field
    total = total + line_part(
        field,
        1,
        count,
        tables[0],
        lefts[0],
        rights[0],
        padded[:, 0, 1:-1, :],
        padded[:, -1, 1:-1, :],
    )
    total = total + line_part(
        field,
        2,
        count,
        tables[1],
        lefts[1],
        rights[1],
        padded[:, 1:-1, 0, :],
        padded[:, 1:-1, -1, :],
    )
    total = total + line_part(
        field, 3, count, tables[2], lefts[2], rights[2], field[:, :, :, -1], field[:, :, :, 0]
    )
    return total


def apply_system(field, level, coupling):
    image = spatial(field, level)
    everyone = lax.all_gather(image, "section", axis=0, tiled=True)
    butcher = jnp.asarray(radau_matrix(), jnp.float32)
    rows = lax.dynamic_slice_in_dim(
        butcher, lax.axis_index("section") * field.shape[0], field.shape[0], 0
    )
    mixed = jnp.einsum("ij,jabc->iabc", rows, everyone, precision=lax.Precision.HIGHEST)
    return field + STEP_SIZE * mixed


def global_total(values):
    return lax.psum(values, ("section", "gx", "gy"))


def stepwise(rhs, guess, kappa, bc_flags):
    levels = [build_level(kappa, bc_flags, count) for count in (5, 3, 2)]
    section_operator = partial(apply_system, coupling=None)
    start_residual = rhs - section_operator(guess, levels[0])
    dofs = float(rhs.size * lax.axis_size("section") * lax.axis_size("gx") * lax.axis_size("gy"))
    beta = jnp.sqrt(global_total(jnp.sum(start_residual * start_residual).reshape(1))[0])
    basis = start_residual / beta
    precond = vcycle(basis, levels, section_operator)
    image = section_operator(precond, levels[0])
    upper = global_total(jnp.sum(image * basis).reshape(1))[0]
    remainder = image - upper * basis
    lower = jnp.sqrt(global_total(jnp.sum(remainder * remainder).reshape(1))[0])
    weight = beta * upper / (upper * upper + lower * lower)
    solution = guess + weight * precond
    residual = start_residual - weight * image
    arnoldi = jnp.stack([beta / math.sqrt(dofs), upper, lower]).astype(jnp.float32)
    return (solution, residual, arnoldi)


EZ = 32
COLS = 16
HALF = 64
TRACE = 40
PIECE = HALF + TRACE
FIELD = 1000
F32 = jnp.float32


def split_sections():
    matrix = radau_matrix()
    values, vectors = np.linalg.eig(matrix)
    order = [n for n in np.argsort(np.abs(values.imag), kind="stable") if values[n].imag > 0]
    bases = []
    for n in order:
        plane = np.stack([vectors[:, n].real, vectors[:, n].imag], axis=1)
        bases.append(np.linalg.qr(plane)[0])
    left, cross, right = np.linalg.svd(bases[0].T @ bases[1])
    bases = [bases[0] @ left, bases[1] @ right.T]
    for c in range(2):
        sign = np.sign(bases[0][np.argmax(np.abs(bases[0][:, c])), c])
        bases = [np.concatenate([b[:, :c], sign * b[:, c : c + 1], b[:, c + 1 :]], axis=1) for b in bases]
    whole = np.concatenate(bases, axis=1)
    back = np.linalg.inv(whole)
    return whole, back, back @ matrix, back @ matrix @ whole, cross


def iota(shape, dim):
    return lax.broadcasted_iota(jnp.int32, shape, dim)


def exact_dot(a, b):
    return lax.dot_general(
        a, b, (((1,), (0,)), ((), ())), precision=lax.Precision.HIGHEST, preferred_element_type=F32
    )


def split_dot(a, b):
    high = a.astype(jnp.bfloat16)
    rest = a - high.astype(F32)
    middle = rest.astype(jnp.bfloat16)
    low = (rest - middle.astype(F32)).astype(jnp.bfloat16)
    b = b.astype(jnp.bfloat16)
    return sum(
        lax.dot_general(part, b, (((1,), (0,)), ((), ())), preferred_element_type=F32)
        for part in (low, middle, high)
    )


def choose(index, values):
    out = values[-1]
    for place in range(len(values) - 2, -1, -1):
        out = jnp.where(index == place, values[place], out)
    return out


def face_gains(flag, direction, side, count):
    nodes, weights = lobatto(count)
    c, nu = ADVECT[direction], DIFFUSE * count * count
    if side == 0:
        return (c * (1.0 + flag) / 2.0 + nu) * (1.0 / float(weights[0]))
    return (nu - c * (1.0 - flag) / 2.0) * (1.0 / float(weights[-1]))


def row_table():
    kx, ky = (element_matrix(5, d) for d in range(2))
    rows = np.zeros((64, 64))
    for s in range(2):
        for i in range(5):
            for j in range(5):
                r = s * 32 + i * 5 + j
                for m in range(5):
                    rows[r, s * 32 + m * 5 + j] += kx[i, m]
                    rows[r, s * 32 + i * 5 + m] += ky[j, m]
    return rows.astype(np.float32)


def pick_line(k):
    return (iota((160, 128), 0) == 5 * (iota((160, 128), 1) % EZ) + k).astype(F32)


def pair_factors(sec, table, own, s):
    upper = iota((32, 128), 1) < 64
    first = jnp.where(upper, float(table[0, s]), float(table[1, s]))
    second = jnp.where(upper, float(table[2, 2 + s]), float(table[3, 2 + s]))
    if not own:
        first = jnp.where(upper, float(table[2, s]), float(table[3, s]))
        second = jnp.where(upper, float(table[0, 2 + s]), float(table[1, 2 + s]))
    return jnp.where(sec == 0, first, second)


def pack_nodes(nodes):
    half = nodes.shape[0] // 2
    odd = iota((half, 128), 1) // EZ % 2 == 1
    return jnp.where(odd, nodes[half:, :], nodes[:half, :])


def face_place(i, j):
    if i == 0:
        return j
    if i == 4:
        return 11 + j
    return 3 + 2 * i + (0 if j == 0 else 1)


def fetch(pairs, sems):
    copies = [pltpu.make_async_copy(src, dst, sems.at[n]) for n, (src, dst) in enumerate(pairs)]
    for copy in copies:
        copy.start()
    for copy in copies:
        copy.wait()


def local_kernel(
    rhs_in, guess_in, kappa_in, flags_in, rows_in, mine, theirs,
    rhs, guess, kappa, flags, rows_t, sems, stack, lines, nodes, traces,
):
    sec = lax.axis_index("section")
    fetch([(rhs_in, rhs), (guess_in, guess), (kappa_in, kappa), (flags_in, flags), (rows_in, rows_t)], sems)
    stack[...] = jnp.zeros_like(stack)
    for i in range(5):
        stack[192 + 5 * i : 197 + 5 * i, :] = kappa[i]
        for j in range(5):
            r = 5 * i + j
            value = guess[i, j]
            left = rhs[i, j] - value
            for s in range(2):
                stack[s * 32 + r : s * 32 + r + 1, :] = left[s : s + 1]
                stack[128 + s * 32 + r : 128 + s * 32 + r + 1, :] = value[s : s + 1]
    stack[64:128, :] = exact_dot(rows_t[...], stack[128:192, :])
    source = stack[...]
    for k in range(5):
        lines[224 * k : 224 * k + 224, :] = split_dot(source, pick_line(k))

    def part(k, first):
        return lines[224 * k + first : 224 * k + first + 32, :]

    repeat = (iota((EZ, 128), 1) % EZ == iota((EZ, 128), 0)).astype(F32)
    shown = split_dot(flags[:, 0, 0, :].astype(F32), repeat)
    gains = [face_gains(shown[d : d + 1, :], d // 2, d % 2, 5) for d in range(6)]
    row = iota((32, 128), 0)
    none = jnp.zeros((32, 128), F32)
    own = jnp.where(row < 5, gains[0], jnp.where((row >= 20) & (row < 25), gains[1], none))
    own = own + jnp.where(row % 5 == 0, gains[2], jnp.where(row % 5 == 4, gains[3], none))
    kz = element_matrix(5, 2)
    back, back_matrix = split_sections()[1:3]
    nodes[...] = jnp.zeros_like(nodes)
    for k in range(5):
        diagonal = part(k, 192) + own
        if k == 0:
            diagonal = diagonal + gains[4]
        if k == 4:
            diagonal = diagonal + gains[5]
        images = []
        for s in range(2):
            first = 128 + 32 * s
            image = diagonal * part(k, first) + part(k, 64 + 32 * s)
            for m in range(5):
                image = image + float(kz[k, m]) * part(m, first)
            if k == 0:
                image = image - gains[4] * pltpu.roll(part(4, first), 1, 1)
            if k == 4:
                image = image - gains[5] * pltpu.roll(part(0, first), 127, 1)
            images.append(image)
        for p, mark in enumerate((True, False)):
            total = jnp.zeros((32, 128), F32)
            trace = jnp.zeros((32, 128), F32)
            for s in range(2):
                total = total + pair_factors(sec, back, mark, s) * part(k, 32 * s)
                factor = pair_factors(sec, STEP_SIZE * back_matrix, mark, s)
                total = total - factor * images[s]
                trace = trace + factor * part(k, 128 + 32 * s)
            nodes[128 * p + 25 * k : 128 * p + 25 * k + 25, :] = total[:25]
            start = 80 * p + 16 * k
            traces[start : start + 5, :] = trace[:5]
            for i in range(1, 4):
                for j in (0, 4):
                    r = start + face_place(i, j)
                    traces[r : r + 1, :] = trace[5 * i + j : 5 * i + j + 1]
            traces[start + 11 : start + 16, :] = trace[20:25]
    upper = iota((1, 128), 1) < 64
    for r in range(3):
        nodes[125 + r : 126 + r, :] = jnp.where(upper, shown[2 * r : 2 * r + 1], shown[2 * r + 1 : 2 * r + 2])
    for p, out in enumerate((mine, theirs)):
        out[:HALF, :] = pack_nodes(nodes[128 * p : 128 * p + 128, :])
        out[HALF:PIECE, :] = pack_nodes(traces[80 * p : 80 * p + 80, :])
    for k in range(5):
        nodes[25 * k : 25 * k + 25, :] = part(k, 192)[:25]
    mine[PIECE:, :] = choose(iota((32, 128), 1) // EZ, [nodes[32 * q : 32 * q + 32, :] for q in range(4)])


def part_kernel(source, piece, kappa):
    piece[...] = source[:PIECE, :]
    kappa[...] = source[PIECE:, :]


VMEM = pl.BlockSpec(memory_space=pltpu.VMEM)
HBM = pl.BlockSpec(memory_space=pltpu.HBM)


def limit(mib):
    return pltpu.CompilerParams(vmem_limit_bytes=mib * 2**20)


def local_part(rhs, guess, kappa, flags):
    operands = (rhs, guess, kappa, flags, jnp.asarray(row_table()))
    return pl.pallas_call(
        local_kernel,
        out_shape=[jax.ShapeDtypeStruct((rows, 128), F32) for rows in (PIECE + 32, PIECE)],
        in_specs=[HBM] * 5,
        out_specs=[VMEM] * 2,
        scratch_shapes=[pltpu.VMEM(o.shape, o.dtype) for o in operands]
        + [
            pltpu.SemaphoreType.DMA((5,)),
            pltpu.VMEM((224, 160), F32),
            pltpu.VMEM((5 * 224, 128), F32),
            pltpu.VMEM((256, 128), F32),
            pltpu.VMEM((160, 128), F32),
        ],
        compiler_params=limit(60),
        cost_estimate=pl.CostEstimate(flops=20_000_000, bytes_accessed=8_000_000, transcendentals=0),
        name="local_part",
    )(*operands)


def part(x):
    return pl.pallas_call(
        part_kernel,
        out_shape=[jax.ShapeDtypeStruct((rows, 128), F32) for rows in (PIECE, 32)],
        in_specs=[VMEM],
        out_specs=[VMEM] * 2,
        compiler_params=limit(16),
        name="part",
    )(x)


class Level:
    def __init__(self, count, refs):
        self.count = count
        self.x, self.dir, self.res, self.f = refs
        self.tables = [element_matrix(count, d) for d in range(3)]
        self.gains = self.diag = self.jac = None


def tile(index):
    return pl.ds(index * 8, 8)


def rows_of(pieces, size, r, h):
    return pieces[pl.ds(8 * h * size + r, 8, stride=size), :]


def place_pieces(blocks, stride, pieces, first, size, outer="gy"):
    my_gx, my_gy = lax.axis_index("gx"), lax.axis_index("gy")
    for b, block in enumerate(blocks):
        for a in range(4):
            column = (my_gx ^ a) * 4 + (my_gy ^ b) if outer == "gy" else (my_gx ^ b) * 4 + (my_gy ^ a)
            start = pl.multiple_of(column * size, 8)
            pieces[pl.ds(start, size), :] = block[a * stride + first : a * stride + first + size, :]


class Lanes:
    def __init__(self):
        self.lane = iota((8, 128), 1)
        sub = iota((8, 128), 0)
        self.group = self.lane // EZ
        self.odd = self.group % 2 == 1
        self.element = self.lane % EZ
        self.place = sub % 4
        self.low_half = sub < 4

    def around(self, u):
        turned = pltpu.roll(u, 4, u.ndim - 2)
        far = jnp.where(self.odd, pltpu.roll(turned, 32, u.ndim - 1), pltpu.roll(turned, 96, u.ndim - 1))
        return turned, far

    def x_before(self, u):
        turned, far = self.around(u)
        return jnp.where(self.low_half, far, turned)

    def x_after(self, u):
        turned, far = self.around(u)
        return jnp.where(self.low_half, turned, far)

    def y_before(self, u):
        return jnp.where(self.place == 0, pltpu.roll(u, 5, 0), pltpu.roll(u, 1, 0))

    def y_after(self, u):
        return jnp.where(self.place == 3, pltpu.roll(u, 3, 0), pltpu.roll(u, 7, 0))

    def z_before(self, u):
        return jnp.where(self.element == 0, pltpu.roll(u, 97, u.ndim - 1), pltpu.roll(u, 1, u.ndim - 1))

    def z_after(self, u):
        last = self.element == EZ - 1
        return jnp.where(last, pltpu.roll(u, 31, u.ndim - 1), pltpu.roll(u, 127, u.ndim - 1))


def load(ref, first, count):
    return ref[pl.ds(first * 8, count * 8), :].reshape(count, 8, 128)


def store(ref, first, value):
    ref[pl.ds(first * 8, value.shape[0] * 8), :] = value.reshape(value.shape[0] * 8, 128)


DIAGS = (0, 250, 304)
GAINS = (320, 326, 332)
REGISTERS = 338
CENTRE = (CHEB_HIGH + CHEB_LOW) / 2.0
RADIUS = (CHEB_HIGH - CHEB_LOW) / 2.0


def assemble_kernel(block0, block1, block2, block3, kappa0, kappa1, kappa2, kappa3, field, coefs, pieces, edges, kappas, traces, kap):
    blocks = (block0, block1, block2, block3)
    place_pieces(blocks, PIECE, pieces, 0, HALF)
    place_pieces(blocks, PIECE, edges, HALF, TRACE)
    place_pieces((kappa0, kappa1, kappa2, kappa3), 32, kappas, 0, 32, outer="gx")
    lanes = Lanes()
    group, lane = lanes.group, lanes.lane

    def widen(source, size, target):
        for r in range(size):
            low, high = rows_of(source, size, r, 0), rows_of(source, size, r, 1)
            target[tile(r), :] = jnp.where(lanes.odd, pltpu.roll(high, 32, 1), low)
            target[tile(size + r), :] = jnp.where(lanes.odd, high, pltpu.roll(low, 96, 1))

    widen(edges, TRACE, traces)
    widen(pieces, HALF, field)
    flags = []
    for r in range(3):
        got = field[tile(125 + r), :]
        across = pltpu.roll(got, 64, 1)
        flags += [jnp.where(lane < 64, got, across), jnp.where(lane < 64, across, got)]
    for r in range(32):
        turned = []
        for h in range(2):
            got = rows_of(kappas, 32, r, h)
            turned.append([pltpu.roll(got, 32 * m, 1) if m else got for m in range(4)])
        for q in range(4):
            kap[tile(q * 32 + r), :] = choose(group, [turned[g % 2][(g - q) % 4] for g in range(4)])
    for p, n in enumerate((5, 3, 2)):
        stride = 4 // (n - 1)
        gains = [face_gains(flags[d], d // 2, d % 2, n) for d in range(6)]
        if p == 0:
            for k in range(5):
                def trace(i, j, k=k):
                    return traces[tile(k * 16 + face_place(i, j)), :]

                for m in range(5):
                    for where, term in (
                        (m, gains[0] * lanes.x_before(trace(4, m))),
                        (20 + m, gains[1] * lanes.x_after(trace(0, m))),
                        (5 * m, gains[2] * lanes.y_before(trace(m, 4))),
                        (5 * m + 4, gains[3] * lanes.y_after(trace(m, 0))),
                    ):
                        field[tile(k * 25 + where), :] = field[tile(k * 25 + where), :] + term
        rows = []
        for d in range(3):
            coefs[tile(GAINS[p] + 2 * d), :] = gains[2 * d]
            coefs[tile(GAINS[p] + 2 * d + 1), :] = gains[2 * d + 1]
            table = element_matrix(n, d)
            row = [jnp.full((8, 128), float(table[m, m]), F32) for m in range(n)]
            row[0] = row[0] + gains[2 * d]
            row[n - 1] = row[n - 1] + gains[2 * d + 1]
            rows.append(row)
        along = jnp.stack(rows[1])
        for k in range(n):
            for i in range(n):
                line = load(kap, k * 25 * stride + i * stride * 5, 5)
                line = jnp.stack([line[j * stride] for j in range(n)])
                value = line + (along + (rows[2][k] + rows[0][i]))
                scale = 1.0 / (1.0 + STEP_SIZE * JACOBI_SCALE * value)
                store(coefs, DIAGS[p] + (k * n + i) * n, value)
                store(coefs, DIAGS[p] + n**3 + (k * n + i) * n, scale * (1.0 / CENTRE))


def cycle_kernel(coefs, assembled, fields, *scratch):
    sec = lax.axis_index("section")
    my_gx, my_gy = lax.axis_index("gx"), lax.axis_index("gy")
    levels = [Level(n, scratch[4 * p : 4 * p + 4]) for p, n in enumerate((5, 3, 2))]
    half = scratch[12]
    lanes = Lanes()
    lane = lanes.lane
    blocks = split_sections()[3]

    def lanes_of(upper, lower):
        return jnp.where(lane < 64, jnp.where(sec == 0, upper[0], upper[1]), jnp.where(sec == 0, lower[0], lower[1]))

    entry = [[[float(STEP_SIZE * blocks[2 * p + a, 2 * p + b]) for p in range(2)] for b in range(2)] for a in range(2)]
    same = lanes_of(entry[0][0], entry[1][1])
    swap = lanes_of(entry[0][1], entry[1][0])
    first_rho = RADIUS / CENTRE
    second_rho = 1.0 / (2.0 * CENTRE / RADIUS - first_rho)
    keep = 1.0 + second_rho * first_rho
    push = 2.0 * second_rho / RADIUS * CENTRE
    for p, level in enumerate(levels):
        size = level.count**3
        level.gains = [coefs[tile(GAINS[p] + d), :] for d in range(6)]
        level.diag = lambda first, count, p=p: load(coefs, DIAGS[p] + first, count)
        level.jac = lambda first, count, p=p, size=size: load(coefs, DIAGS[p] + size + first, count)

    def begin(level, source):
        n = level.count
        for first in range(0, n**3, n):
            f = load(source, first, n)
            store(level.dir, first, level.jac(first, n) * f)
            store(level.res, first, f)
            store(level.x, first, jnp.zeros_like(f))

    def apply(level, smooth):
        n = level.count
        kx, ky, kz = level.tables
        gains = level.gains
        source = level.dir if smooth else level.x
        for k in range(n):
            def line_at(i, k=k):
                return load(source, (k * n + i) * n, n)

            for i in range(n):
                first = (k * n + i) * n
                v = line_at(i)
                total = level.diag(first, n) * v
                for m in range(n):
                    if m != i:
                        total = total + float(kx[i, m]) * line_at(m)
                for m in range(n):
                    if m != k:
                        total = total + float(kz[k, m]) * load(source, (m * n + i) * n, n)
                lines = []
                for j in range(n):
                    line = None
                    for m in range(n):
                        if m != j:
                            term = float(ky[j, m]) * v[m]
                            line = term if line is None else line + term
                    if j == 0:
                        line = line - gains[2] * lanes.y_before(v[n - 1])
                    if j == n - 1:
                        line = line - gains[3] * lanes.y_after(v[0])
                    lines.append(line)
                total = total + jnp.stack(lines)
                if i == 0:
                    total = total - gains[0] * lanes.x_before(line_at(n - 1))
                if i == n - 1:
                    total = total - gains[1] * lanes.x_after(line_at(0))
                if k == 0:
                    total = total - gains[4] * lanes.z_before(load(source, ((n - 1) * n + i) * n, n))
                if k == n - 1:
                    total = total - gains[5] * lanes.z_after(load(source, i * n, n))
                image = v + (same * total + swap * pltpu.roll(total, 64, 2))
                if smooth:
                    scaled = level.jac(first, n) * (load(level.res, first, n) - image)
                    store(level.x, first, load(level.x, first, n) + keep * v + push * scaled)
                else:
                    rest = load(level.f, first, n) - image
                    store(level.res, first, rest)
                    store(level.dir, first, level.jac(first, n) * rest)

    def combine(weights, parts):
        total = None
        for weight, part in zip(weights, parts):
            if abs(weight) > 1e-14:
                term = part if abs(weight - 1.0) < 1e-14 else float(weight) * part
                total = term if total is None else total + term
        return total

    def change(table, source, target, add):
        m, n = table.shape
        for i in range(n):
            parts = [load(source, i * n + k * n * n, n) for k in range(n)]
            for k in range(m):
                store(half, i * n + k * n * n, combine(table[k], parts))
        for k in range(m):
            parts = [load(half, k * n * n + i * n, n) for i in range(n)]
            for i in range(m):
                line = combine(table[i], parts)
                value = jnp.stack([combine(table[j], [line[a] for a in range(n)]) for j in range(m)])
                first = k * m * m + i * m
                store(target, first, load(target, first, m) + value if add else value)

    def down(n, m):
        fine_nodes, fine_weights = lobatto(n)
        coarse_nodes, coarse_weights = lobatto(m)
        table = lagrange_table(coarse_nodes, fine_nodes)
        return (1.0 / coarse_weights)[:, None] * table.T * fine_weights[None, :]

    def up(m, n):
        return lagrange_table(lobatto(m)[0], lobatto(n)[0])

    def solve(p):
        level = levels[p]
        if p == 2:
            apply(level, True)
            return
        below = levels[p + 1]

        def step(t, carry):
            @pl.when(t != 1)
            def _():
                apply(level, True)

            @pl.when((t != 2) | (p == 0))
            def _():
                apply(level, False)

            @pl.when(t == 0)
            def _():
                n, m = level.count, below.count
                change(down(n, m), level.res, below.f, False)
                begin(below, below.f)
                solve(p + 1)
                change(up(m, n), below.x, level.x, True)
            return carry
        lax.fori_loop(0, 3, step, 0)

    fine = levels[0]
    fine.f = assembled
    begin(fine, assembled)
    solve(0)

    for first in range(0, 125, 5):
        store(fields, first, load(fine.res, first, 5))
    column = (my_gx % 2) * 4 + my_gy
    fields[FIELD : FIELD + 125, :] = fine.x[pl.ds(column, 125, stride=8), :]
    fields[FIELD + 125 : FIELD + 128, :] = jnp.zeros((3, 128), F32)


def pair_weights():
    cross = split_sections()[4]
    return jnp.where(iota((8, 128), 1) < 64, float(cross[0]), float(cross[1]))


def column_factors(p):
    sec = lax.axis_index("section")
    whole = split_sections()[0]
    lane = iota((25, 128), 1)
    here = lane // EZ % 2 == lax.axis_index("gx") // 2
    factors = []
    for s in range(2):
        parts = []
        for mine in range(2):
            t = whole[2 * mine + s]
            q = mine if p == 0 else 1 - mine
            parts.append(jnp.where(lane < 64, float(t[2 * q]), float(t[2 * q + 1])))
        factors.append(jnp.where(here, jnp.where(sec == 0, parts[0], parts[1]), 0.0))
    return factors


def column_rows(k):
    column = (lax.axis_index("gx") % 2) * 4 + lax.axis_index("gy")
    return pl.ds(k * 200 + column, 25, stride=8)


def raw_order(k):
    return (iota((128, 160), 1) == 5 * (iota((128, 160), 0) % EZ) + k).astype(F32)


def early_kernel(own, own_start, other_start, sums, column_out, cols):
    weights = pair_weights()
    cols[...] = jnp.zeros_like(cols)
    total = jnp.zeros((192, 160), F32)
    own_factors, other_factors = column_factors(0), column_factors(1)
    for k in range(5):
        where = column_rows(k)
        z = own[FIELD + k * 25 : FIELD + k * 25 + 25, :]
        start, other = own_start[where, :], other_start[where, :]
        w = start - own[where, :]
        for s in range(2):
            cols[s * 32 : s * 32 + 25, :] = own_factors[s] * z
            cols[64 + s * 32 : 64 + s * 32 + 25, :] = own_factors[s] * start + other_factors[s] * other
            cols[128 + s * 32 : 128 + s * 32 + 25, :] = own_factors[s] * w
        total = total + split_dot(cols[...], raw_order(k))
    column_out[...] = total
    nothing = jnp.zeros((8, 128), F32)
    uppers, sizes = [nothing] * 5, [nothing] * 5
    for r in range(125):
        c, d = own_start[tile(r), :], other_start[tile(r), :]
        a = c - own[tile(r), :]
        uppers[r % 5] = uppers[r % 5] + a * (c + weights * d)
        sizes[r % 5] = sizes[r % 5] + ((c * c + d * d) + 2.0 * (weights * (c * d)))
    sums[0:8, :] = sum(uppers)
    sums[8:16, :] = sum(sizes)


def finish_kernel(own, other, own_start, other_start, sums, column, guess, sol, res_out, arnoldi, cols, outs):
    sec = lax.axis_index("section")
    weights = pair_weights()
    cols[...] = jnp.zeros_like(cols)
    total = jnp.zeros((128, 160), F32)
    factors = column_factors(1)
    for k in range(5):
        where = column_rows(k)
        z = other[FIELD + k * 25 : FIELD + k * 25 + 25, :]
        w = other_start[where, :] - other[where, :]
        for s in range(2):
            cols[s * 32 : s * 32 + 25, :] = factors[s] * z
            cols[64 + s * 32 : 64 + s * 32 + 25, :] = factors[s] * w
        total = total + split_dot(cols[...], raw_order(k))
    nothing = jnp.zeros((8, 128), F32)
    uppers = [nothing] * 5
    for r in range(125):
        c, d = own_start[tile(r), :], other_start[tile(r), :]
        b = d - other[tile(r), :]
        uppers[r % 5] = uppers[r % 5] + b * (d + weights * c)

    mine, theirs = sums[0:8, :], sum(uppers)
    size = jnp.sum(sums[8:16, :], keepdims=True)
    upper = jnp.sum(mine + theirs, keepdims=True) / size
    rests = [nothing] * 5
    for r in range(125):
        c, d = own_start[tile(r), :], other_start[tile(r), :]
        a = (c - own[tile(r), :]) - upper * c
        b = (d - other[tile(r), :]) - upper * d
        rests[r % 5] = rests[r % 5] + ((a * a + b * b) + 2.0 * (weights * (a * b)))
    rest = jnp.sum(sum(rests), keepdims=True)
    beta = jnp.sqrt(size)
    lower = jnp.sqrt(rest) / beta
    weight = upper / (upper * upper + lower * lower)
    entries = float(125 * EZ * COLS * 4)
    for place_out, value in enumerate((beta * (1.0 / math.sqrt(entries)), upper, lower)):
        arnoldi[place_out] = value[0, 0]
    outs[:64, :] = weight * (column[:64, :] + total[:64])
    outs[64:, :] = column[64:128, :] - weight * (column[128:, :] + total[64:])
    for i in range(5):
        for j in range(5):
            r = 5 * i + j
            for s in range(2):
                sol[i, j, s : s + 1, :] = guess[i, j, s : s + 1, :] + outs[s * 32 + r : s * 32 + r + 1, :]
                res_out[i, j, s : s + 1, :] = outs[64 + s * 32 + r : 64 + s * 32 + r + 1, :]


def assemble(blocks, kappas):
    return pl.pallas_call(
        assemble_kernel,
        out_shape=[
            jax.ShapeDtypeStruct((128 * 8, 128), F32),
            jax.ShapeDtypeStruct((REGISTERS * 8, 128), F32),
        ],
        in_specs=[VMEM] * 8,
        out_specs=[VMEM] * 2,
        scratch_shapes=[
            pltpu.VMEM((COLS * HALF, 128), F32),
            pltpu.VMEM((COLS * TRACE, 128), F32),
            pltpu.VMEM((COLS * 32, 128), F32),
            pltpu.VMEM((80 * 8, 128), F32),
            pltpu.VMEM((128 * 8, 128), F32),
        ],
        compiler_params=limit(16),
        name="assemble",
    )(*blocks, *kappas)


def cycle(coefs, assembled):
    scratch = []
    for n in (5, 3, 2):
        scratch += [pltpu.VMEM((n**3 * 8, 128), F32)] * 4
    scratch += [pltpu.VMEM((FIELD, 128), F32)]
    return pl.pallas_call(
        cycle_kernel,
        out_shape=jax.ShapeDtypeStruct((FIELD + 128, 128), F32),
        in_specs=[VMEM] * 2,
        out_specs=VMEM,
        scratch_shapes=scratch,
        compiler_params=limit(24),
        cost_estimate=pl.CostEstimate(flops=40_000_000, bytes_accessed=30_000_000, transcendentals=0),
        name="cycle",
    )(coefs, assembled)


def early(own, own_start, other_start):
    return pl.pallas_call(
        early_kernel,
        out_shape=[jax.ShapeDtypeStruct((16, 128), F32), jax.ShapeDtypeStruct((192, 160), F32)],
        in_specs=[VMEM] * 3,
        out_specs=[VMEM] * 2,
        scratch_shapes=[pltpu.VMEM((192, 128), F32)],
        compiler_params=limit(16),
        cost_estimate=pl.CostEstimate(flops=4_000_000, bytes_accessed=4_000_000, transcendentals=0),
        name="early",
    )(own, own_start, other_start)


def finish(own, other, own_start, other_start, sums, column, guess):
    return pl.pallas_call(
        finish_kernel,
        out_shape=[
            jax.ShapeDtypeStruct(guess.shape, F32),
            jax.ShapeDtypeStruct(guess.shape, F32),
            jax.ShapeDtypeStruct((3,), F32),
        ],
        in_specs=[VMEM] * 7,
        out_specs=[VMEM, VMEM, pl.BlockSpec(memory_space=pltpu.SMEM)],
        scratch_shapes=[pltpu.VMEM((128, 128), F32), pltpu.VMEM((128, 160), F32)],
        compiler_params=limit(24),
        name="finish",
    )(own, other, own_start, other_start, sums, column, guess)


def exchange(x, axis, bits):
    return lax.ppermute(x, axis, [(n, n ^ bits) for n in range(lax.axis_size(axis))])


def gathered_body(rhs, guess, kappa, bc_flags):
    rhs, guess = (jnp.transpose(v, (1, 2, 0, 3)) for v in (rhs, guess))
    mine, theirs = local_part(rhs, guess, kappa, bc_flags)
    got, mine, kappa_piece = lax.optimization_barrier((exchange(theirs, "section", 1), *part(mine)))
    piece = mine + got
    parts = [exchange(piece, "gx", bits) for bits in (1, 2, 3)]
    parts[0], kappa_piece = lax.optimization_barrier((parts[0], kappa_piece))
    others = [exchange(kappa_piece, "gy", bits) for bits in (1, 2, 3)]
    parts, others = lax.optimization_barrier((parts, others))
    line = jnp.concatenate([piece] + parts)
    across = jnp.concatenate([kappa_piece] + others)
    blocks = [line] + [exchange(line, "gy", bits) for bits in (1, 2, 3)]
    kappas = [across] + [exchange(across, "gx", bits) for bits in (1, 2, 3)]
    start, coefs = assemble(blocks, kappas)
    other_start = exchange(start, "section", 1)
    own, other_start = lax.optimization_barrier((cycle(coefs, start), other_start))
    sums, column = early(own, start, other_start)
    sol, res, arnoldi = finish(own, exchange(own, "section", 1), start, other_start, sums, column, guess)
    sol, res = (jnp.transpose(v, (2, 0, 1, 3)) for v in (sol, res))
    return sol, res, arnoldi


def solution(mesh):
    placed = (
        P("section", "gx", "gy", None),
        P("section", "gx", "gy", None),
        P("gx", "gy", None),
        P(None, "gx", "gy", None),
    )
    sizes = (mesh.shape["section"], mesh.shape["gx"], mesh.shape["gy"])

    def step(rhs, guess, kappa, bc_flags):
        fits = sizes == (2, 4, 4) and rhs.shape == (4, 20, 20, 160)
        return jax.shard_map(
            gathered_body if fits else stepwise,
            mesh=mesh,
            in_specs=placed,
            out_specs=(P("section", "gx", "gy", None), P("section", "gx", "gy", None), P()),
            check_vma=False,
        )(rhs, guess, kappa, bc_flags)

    return step
```

```python
from functools import partial
import math

import jax
import jax.numpy as jnp
import numpy as np
from jax import lax
from jax.experimental import pallas as pl
from jax.experimental.pallas import tpu as pltpu
from jax.sharding import PartitionSpec as P

ADVECT = (1.0, 0.7, 0.5)
DIFFUSE = 0.05
STEP_SIZE = 0.2
JACOBI_SCALE = 0.25
CHEB_LOW = 0.25
CHEB_HIGH = 2.0
LETTERS = "abcdef"


def extended(x, sides, width):
    for axis, dim in sides:
        peers, length = (lax.axis_size(axis), x.shape[dim])
        up = [(i, (i + 1) % peers) for i in range(peers)]
        down = [(j, i) for i, j in up]
        last = lax.slice_in_dim(x, length - width, length, axis=dim)
        leading = lax.slice_in_dim(x, 0, width, axis=dim)
        before = lax.ppermute(last, axis, up)
        after = lax.ppermute(leading, axis, down)
        x = jnp.concatenate([before, x, after], axis=dim)
    return x


def lobatto(count):
    if count == 5:
        inner = math.sqrt(3.0 / 7.0)
        return (
            np.array([-1.0, -inner, 0.0, inner, 1.0]),
            np.array([0.1, 49.0 / 90.0, 32.0 / 45.0, 49.0 / 90.0, 0.1]),
        )
    if count == 3:
        return (np.array([-1.0, 0.0, 1.0]), np.array([1.0 / 3.0, 4.0 / 3.0, 1.0 / 3.0]))
    return (np.array([-1.0, 1.0]), np.array([1.0, 1.0]))


def lagrange_table(nodes, points):
    table = np.ones((len(points), len(nodes)))
    for column in range(len(nodes)):
        for other in range(len(nodes)):
            if other != column:
                table[:, column] *= (points - nodes[other]) / (nodes[column] - nodes[other])
    return table


def slope_table(nodes):
    total = len(nodes)
    factor = np.array(
        [np.prod([nodes[i] - nodes[k] for k in range(total) if k != i]) for i in range(total)]
    )
    table = np.zeros((total, total))
    for row in range(total):
        for column in range(total):
            if row != column:
                table[row, column] = factor[row] / factor[column] / (nodes[row] - nodes[column])
        table[row, row] = -np.sum(table[row])
    return table


def element_matrix(count, direction):
    nodes, weights = lobatto(count)
    slopes = slope_table(nodes)
    stiffness = (1.0 / weights)[:, None] * (slopes.T @ (weights[:, None] * slopes))
    return ADVECT[direction] * slopes + DIFFUSE * stiffness


def legendre_pair(point, order):
    values = [1.0, point]
    slopes = [0.0, 1.0]
    for index in range(1, order):
        values.append(
            ((2 * index + 1) * point * values[index] - index * values[index - 1]) / (index + 1)
        )
        slopes.append(slopes[index - 1] + (2 * index + 1) * values[index])
    return (values, slopes)


def radau_nodes():
    starts = [0.0885879595127039, 0.4094668644407347, 0.7876594617608471]
    found = []
    for start in starts:
        point = start
        for sweep in range(30):
            values, slopes = legendre_pair(2.0 * point - 1.0, 4)
            change = (values[4] - values[3]) / (2.0 * (slopes[4] - slopes[3]))
            point = point - change
        found.append(point)
    found.append(1.0)
    return found


def poly_times(coefs, root):
    result = [0.0] * (len(coefs) + 1)
    for index in range(len(coefs)):
        result[index + 1] += coefs[index]
        result[index] -= root * coefs[index]
    return result


def radau_matrix():
    order = 4
    nodes = radau_nodes()
    matrix = np.zeros((order, order))
    for column in range(order):
        coefs = [1.0]
        denominator = 1.0
        for other in range(order):
            if other != column:
                coefs = poly_times(coefs, nodes[other])
                denominator *= nodes[column] - nodes[other]
        for row in range(order):
            upper_end = nodes[row]
            integral = 0.0
            for index in range(len(coefs)):
                integral += coefs[index] * upper_end ** (index + 1) / (index + 1)
            matrix[row, column] = integral / denominator
    return matrix


def node_einsum(table, field, axis):
    labels = LETTERS[: field.ndim]
    source = labels[: axis + 1] + "j" + labels[axis + 2 :]
    target = labels[: axis + 1] + "i" + labels[axis + 2 :]
    return jnp.einsum(
        "ij," + source + "->" + target,
        jnp.asarray(table, jnp.float32),
        field,
        precision=lax.Precision.HIGHEST,
    )


def apply_along(field, axis, count, table):
    shape = field.shape
    split = shape[:axis] + (shape[axis] // count, count) + shape[axis + 1 :]
    mapped = node_einsum(table, field.reshape(split), axis)
    return mapped.reshape(
        shape[:axis] + (mapped.shape[axis] * mapped.shape[axis + 1],) + shape[axis + 1 :]
    )


def line_part(field, axis, count, table, left_gain, right_gain, left_edge, right_edge):
    shape = field.shape
    elements = shape[axis] // count
    split = field.reshape(shape[:axis] + (elements, count) + shape[axis + 1 :])
    linear = node_einsum(table, split, axis)
    first = lax.index_in_dim(split, 0, axis + 1, keepdims=False)
    last = lax.index_in_dim(split, count - 1, axis + 1, keepdims=False)
    before = jnp.concatenate(
        [jnp.expand_dims(left_edge, axis), lax.slice_in_dim(last, 0, elements - 1, axis=axis)], axis
    )
    after = jnp.concatenate(
        [lax.slice_in_dim(first, 1, elements, axis=axis), jnp.expand_dims(right_edge, axis)], axis
    )
    front = jnp.expand_dims(left_gain * (first - before), axis + 1)
    back = jnp.expand_dims(right_gain * (last - after), axis + 1)
    if count > 2:
        middle_shape = list(front.shape)
        middle_shape[axis + 1] = count - 2
        pieces = [front, jnp.zeros(middle_shape, jnp.float32), back]
    else:
        pieces = [front, back]
    return (linear + jnp.concatenate(pieces, axis + 1)).reshape(shape)


def diag_along(shape, axis, count, table, left_gain, right_gain):
    elements = shape[axis] // count
    split = shape[:axis] + (elements, count) + shape[axis + 1 :]
    profile = [1] * len(split)
    profile[axis + 1] = count
    diagonal_entries = np.array([table[index, index] for index in range(count)])
    base = jnp.broadcast_to(jnp.asarray(diagonal_entries, jnp.float32).reshape(profile), split)
    front = jnp.expand_dims(left_gain, axis + 1)
    back = jnp.expand_dims(right_gain, axis + 1)
    if count > 2:
        middle_shape = list(front.shape)
        middle_shape[axis + 1] = count - 2
        pieces = [front, jnp.zeros(middle_shape, jnp.float32), back]
    else:
        pieces = [front, back]
    return (base + jnp.concatenate(pieces, axis + 1)).reshape(shape)


def level_kappa(kappa, count):
    if count == 5:
        return kappa
    picks = np.array([0, 2, 4]) if count == 3 else np.array([0, 4])
    extents = [extent // 5 for extent in kappa.shape]
    grouped = kappa.reshape(extents[0], 5, extents[1], 5, extents[2], 5)
    for axis in (1, 3, 5):
        grouped = jnp.take(grouped, picks, axis=axis)
    return grouped.reshape(extents[0] * count, extents[1] * count, extents[2] * count)


def face_plane(face, direction, count):
    plane = face.astype(jnp.float32)
    for axis in range(3):
        if axis != direction:
            plane = jnp.repeat(plane, count, axis=axis)
    return plane


def build_level(kappa, flags, count):
    nodes, weights = lobatto(count)
    kappa_level = level_kappa(kappa, count)
    tables, lefts, rights = ([], [], [])
    diagonal = kappa_level
    for direction in range(3):
        table = element_matrix(count, direction)
        lower = face_plane(flags[2 * direction], direction, count)
        upper = face_plane(flags[2 * direction + 1], direction, count)
        left_gain = (ADVECT[direction] * (1.0 + lower) / 2.0 + DIFFUSE * count * count) / float(
            weights[0]
        )
        right_gain = (DIFFUSE * count * count - ADVECT[direction] * (1.0 - upper) / 2.0) / float(
            weights[-1]
        )
        tables.append(table)
        lefts.append(left_gain)
        rights.append(right_gain)
        diagonal = diagonal + diag_along(
            kappa_level.shape, direction, count, table, left_gain, right_gain
        )
    scale = 1.0 / (1.0 + STEP_SIZE * JACOBI_SCALE * diagonal)
    return (count, tables, lefts, rights, kappa_level, scale)


def restrict(field, fine_count, coarse_count):
    fine_nodes, fine_weights = lobatto(fine_count)
    coarse_nodes, coarse_weights = lobatto(coarse_count)
    table = (
        (1.0 / coarse_weights)[:, None]
        * lagrange_table(coarse_nodes, fine_nodes).T
        * fine_weights[None, :]
    )
    for axis in range(field.ndim - 3, field.ndim):
        field = apply_along(field, axis, fine_count, table)
    return field


def prolong(field, coarse_count, fine_count):
    fine_nodes, fine_weights = lobatto(fine_count)
    coarse_nodes, coarse_weights = lobatto(coarse_count)
    table = lagrange_table(coarse_nodes, fine_nodes)
    for axis in range(field.ndim - 3, field.ndim):
        field = apply_along(field, axis, coarse_count, table)
    return field


def chebyshev(rhs, start, level, operator):
    centre = (CHEB_HIGH + CHEB_LOW) / 2.0
    radius = (CHEB_HIGH - CHEB_LOW) / 2.0
    ratio = centre / radius
    first_rho = 1.0 / ratio
    second_rho = 1.0 / (2.0 * ratio - first_rho)
    scale = level[5]
    if start is None:
        remain = rhs
    else:
        remain = rhs - operator(start, level)
    step = scale * remain / centre
    guess = step if start is None else start + step
    remain = remain - operator(step, level)
    step = second_rho * first_rho * step + 2.0 * second_rho / radius * scale * remain
    return guess + step


def vcycle(rhs, levels, operator):
    fine, middle, coarse = levels
    fine_x = chebyshev(rhs, None, fine, operator)
    middle_rhs = restrict(rhs - operator(fine_x, fine), 5, 3)
    middle_x = chebyshev(middle_rhs, None, middle, operator)
    coarse_rhs = restrict(middle_rhs - operator(middle_x, middle), 3, 2)
    coarse_x = chebyshev(coarse_rhs, None, coarse, operator)
    middle_x = chebyshev(middle_rhs, middle_x + prolong(coarse_x, 2, 3), middle, operator)
    return chebyshev(rhs, fine_x + prolong(middle_x, 3, 5), fine, operator)


def spatial(field, level):
    count, tables, lefts, rights, kappa_level, scale = level
    padded = extended(field, (("gx", 1), ("gy", 2)), 1)
    total = kappa_level * field
    total = total + line_part(
        field,
        1,
        count,
        tables[0],
        lefts[0],
        rights[0],
        padded[:, 0, 1:-1, :],
        padded[:, -1, 1:-1, :],
    )
    total = total + line_part(
        field,
        2,
        count,
        tables[1],
        lefts[1],
        rights[1],
        padded[:, 1:-1, 0, :],
        padded[:, 1:-1, -1, :],
    )
    total = total + line_part(
        field, 3, count, tables[2], lefts[2], rights[2], field[:, :, :, -1], field[:, :, :, 0]
    )
    return total


def apply_system(field, level, coupling):
    image = spatial(field, level)
    everyone = lax.all_gather(image, "section", axis=0, tiled=True)
    butcher = jnp.asarray(radau_matrix(), jnp.float32)
    rows = lax.dynamic_slice_in_dim(
        butcher, lax.axis_index("section") * field.shape[0], field.shape[0], 0
    )
    mixed = jnp.einsum("ij,jabc->iabc", rows, everyone, precision=lax.Precision.HIGHEST)
    return field + STEP_SIZE * mixed


def global_total(values):
    return lax.psum(values, ("section", "gx", "gy"))


def stepwise(rhs, guess, kappa, bc_flags):
    levels = [build_level(kappa, bc_flags, count) for count in (5, 3, 2)]
    section_operator = partial(apply_system, coupling=None)
    start_residual = rhs - section_operator(guess, levels[0])
    dofs = float(rhs.size * lax.axis_size("section") * lax.axis_size("gx") * lax.axis_size("gy"))
    beta = jnp.sqrt(global_total(jnp.sum(start_residual * start_residual).reshape(1))[0])
    basis = start_residual / beta
    precond = vcycle(basis, levels, section_operator)
    image = section_operator(precond, levels[0])
    upper = global_total(jnp.sum(image * basis).reshape(1))[0]
    remainder = image - upper * basis
    lower = jnp.sqrt(global_total(jnp.sum(remainder * remainder).reshape(1))[0])
    weight = beta * upper / (upper * upper + lower * lower)
    solution = guess + weight * precond
    residual = start_residual - weight * image
    arnoldi = jnp.stack([beta / math.sqrt(dofs), upper, lower]).astype(jnp.float32)
    return (solution, residual, arnoldi)


EZ = 32
COLS = 16
HALF = 64
TRACE = 40
KAPPA = HALF + TRACE
PIECE = KAPPA + 32
FIELD = 1000
F32 = jnp.float32


def split_sections():
    matrix = radau_matrix()
    values, vectors = np.linalg.eig(matrix)
    order = [n for n in np.argsort(np.abs(values.imag), kind="stable") if values[n].imag > 0]
    bases = []
    for n in order:
        plane = np.stack([vectors[:, n].real, vectors[:, n].imag], axis=1)
        bases.append(np.linalg.qr(plane)[0])
    left, cross, right = np.linalg.svd(bases[0].T @ bases[1])
    bases = [bases[0] @ left, bases[1] @ right.T]
    for c in range(2):
        sign = np.sign(bases[0][np.argmax(np.abs(bases[0][:, c])), c])
        bases = [np.concatenate([b[:, :c], sign * b[:, c : c + 1], b[:, c + 1 :]], axis=1) for b in bases]
    whole = np.concatenate(bases, axis=1)
    back = np.linalg.inv(whole)
    return whole, back, back @ matrix, back @ matrix @ whole, cross


def iota(shape, dim):
    return lax.broadcasted_iota(jnp.int32, shape, dim)


def exact_dot(a, b):
    return lax.dot_general(
        a, b, (((1,), (0,)), ((), ())), precision=lax.Precision.HIGHEST, preferred_element_type=F32
    )


def split_dot(a, b):
    high = a.astype(jnp.bfloat16)
    rest = a - high.astype(F32)
    middle = rest.astype(jnp.bfloat16)
    low = (rest - middle.astype(F32)).astype(jnp.bfloat16)
    b = b.astype(jnp.bfloat16)
    return sum(
        lax.dot_general(part, b, (((1,), (0,)), ((), ())), preferred_element_type=F32)
        for part in (low, middle, high)
    )


def choose(index, values):
    out = values[-1]
    for place in range(len(values) - 2, -1, -1):
        out = jnp.where(index == place, values[place], out)
    return out


def face_gains(flag, direction, side, count):
    nodes, weights = lobatto(count)
    c, nu = ADVECT[direction], DIFFUSE * count * count
    if side == 0:
        return (c * (1.0 + flag) / 2.0 + nu) * (1.0 / float(weights[0]))
    return (nu - c * (1.0 - flag) / 2.0) * (1.0 / float(weights[-1]))


def row_table():
    kx, ky = (element_matrix(5, d) for d in range(2))
    rows = np.zeros((64, 64))
    for s in range(2):
        for i in range(5):
            for j in range(5):
                r = s * 32 + i * 5 + j
                for m in range(5):
                    rows[r, s * 32 + m * 5 + j] += kx[i, m]
                    rows[r, s * 32 + i * 5 + m] += ky[j, m]
    return rows.astype(np.float32)


def pick_line(k):
    return (iota((160, 128), 0) == 5 * (iota((160, 128), 1) % EZ) + k).astype(F32)


def pair_factors(sec, table, own, s):
    upper = iota((32, 128), 1) < 64
    first = jnp.where(upper, float(table[0, s]), float(table[1, s]))
    second = jnp.where(upper, float(table[2, 2 + s]), float(table[3, 2 + s]))
    if not own:
        first = jnp.where(upper, float(table[2, s]), float(table[3, s]))
        second = jnp.where(upper, float(table[0, 2 + s]), float(table[1, 2 + s]))
    return jnp.where(sec == 0, first, second)


def pack_nodes(nodes):
    half = nodes.shape[0] // 2
    odd = iota((half, 128), 1) // EZ % 2 == 1
    return jnp.where(odd, nodes[half:, :], nodes[:half, :])


def face_place(i, j):
    if i == 0:
        return j
    if i == 4:
        return 11 + j
    return 3 + 2 * i + (0 if j == 0 else 1)


def fetch(pairs, sems):
    copies = [pltpu.make_async_copy(src, dst, sems.at[n]) for n, (src, dst) in enumerate(pairs)]
    for copy in copies:
        copy.start()
    for copy in copies:
        copy.wait()


def local_kernel(
    rhs_in, guess_in, kappa_in, flags_in, rows_in, mine, theirs,
    rhs, guess, kappa, flags, rows_t, sems, stack, lines, nodes, traces,
):
    sec = lax.axis_index("section")
    fetch([(rhs_in, rhs), (guess_in, guess), (kappa_in, kappa), (flags_in, flags), (rows_in, rows_t)], sems)
    stack[...] = jnp.zeros_like(stack)
    for i in range(5):
        stack[192 + 5 * i : 197 + 5 * i, :] = kappa[i]
        for j in range(5):
            r = 5 * i + j
            value = guess[i, j]
            left = rhs[i, j] - value
            for s in range(2):
                stack[s * 32 + r : s * 32 + r + 1, :] = left[s : s + 1]
                stack[128 + s * 32 + r : 128 + s * 32 + r + 1, :] = value[s : s + 1]
    stack[64:128, :] = exact_dot(rows_t[...], stack[128:192, :])
    source = stack[...]
    for k in range(5):
        lines[224 * k : 224 * k + 224, :] = split_dot(source, pick_line(k))

    def part(k, first):
        return lines[224 * k + first : 224 * k + first + 32, :]

    repeat = (iota((EZ, 128), 1) % EZ == iota((EZ, 128), 0)).astype(F32)
    shown = split_dot(flags[:, 0, 0, :].astype(F32), repeat)
    gains = [face_gains(shown[d : d + 1, :], d // 2, d % 2, 5) for d in range(6)]
    row = iota((32, 128), 0)
    none = jnp.zeros((32, 128), F32)
    own = jnp.where(row < 5, gains[0], jnp.where((row >= 20) & (row < 25), gains[1], none))
    own = own + jnp.where(row % 5 == 0, gains[2], jnp.where(row % 5 == 4, gains[3], none))
    kz = element_matrix(5, 2)
    back, back_matrix = split_sections()[1:3]
    nodes[...] = jnp.zeros_like(nodes)
    for k in range(5):
        diagonal = part(k, 192) + own
        if k == 0:
            diagonal = diagonal + gains[4]
        if k == 4:
            diagonal = diagonal + gains[5]
        images = []
        for s in range(2):
            first = 128 + 32 * s
            image = diagonal * part(k, first) + part(k, 64 + 32 * s)
            for m in range(5):
                image = image + float(kz[k, m]) * part(m, first)
            if k == 0:
                image = image - gains[4] * pltpu.roll(part(4, first), 1, 1)
            if k == 4:
                image = image - gains[5] * pltpu.roll(part(0, first), 127, 1)
            images.append(image)
        for p, mark in enumerate((True, False)):
            total = jnp.zeros((32, 128), F32)
            trace = jnp.zeros((32, 128), F32)
            for s in range(2):
                total = total + pair_factors(sec, back, mark, s) * part(k, 32 * s)
                factor = pair_factors(sec, STEP_SIZE * back_matrix, mark, s)
                total = total - factor * images[s]
                trace = trace + factor * part(k, 128 + 32 * s)
            nodes[128 * p + 25 * k : 128 * p + 25 * k + 25, :] = total[:25]
            start = 80 * p + 16 * k
            traces[start : start + 5, :] = trace[:5]
            for i in range(1, 4):
                for j in (0, 4):
                    r = start + face_place(i, j)
                    traces[r : r + 1, :] = trace[5 * i + j : 5 * i + j + 1]
            traces[start + 11 : start + 16, :] = trace[20:25]
    upper = iota((1, 128), 1) < 64
    for r in range(3):
        nodes[125 + r : 126 + r, :] = jnp.where(upper, shown[2 * r : 2 * r + 1], shown[2 * r + 1 : 2 * r + 2])
    for p, out in enumerate((mine, theirs)):
        out[:HALF, :] = pack_nodes(nodes[128 * p : 128 * p + 128, :])
        out[HALF:KAPPA, :] = pack_nodes(traces[80 * p : 80 * p + 80, :])
    for k in range(5):
        nodes[25 * k : 25 * k + 25, :] = part(k, 192)[:25]
    mine[KAPPA:, :] = choose(iota((32, 128), 1) // EZ, [nodes[32 * q : 32 * q + 32, :] for q in range(4)])


def part_kernel(source, piece, kappa):
    piece[...] = source[:KAPPA, :]
    kappa[...] = source[KAPPA:, :]


VMEM = pl.BlockSpec(memory_space=pltpu.VMEM)
HBM = pl.BlockSpec(memory_space=pltpu.HBM)


def limit(mib):
    return pltpu.CompilerParams(vmem_limit_bytes=mib * 2**20)


def local_part(rhs, guess, kappa, flags):
    operands = (rhs, guess, kappa, flags, jnp.asarray(row_table()))
    return pl.pallas_call(
        local_kernel,
        out_shape=[jax.ShapeDtypeStruct((rows, 128), F32) for rows in (PIECE, KAPPA)],
        in_specs=[HBM] * 5,
        out_specs=[VMEM] * 2,
        scratch_shapes=[pltpu.VMEM(o.shape, o.dtype) for o in operands]
        + [
            pltpu.SemaphoreType.DMA((5,)),
            pltpu.VMEM((224, 160), F32),
            pltpu.VMEM((5 * 224, 128), F32),
            pltpu.VMEM((256, 128), F32),
            pltpu.VMEM((160, 128), F32),
        ],
        compiler_params=limit(60),
        cost_estimate=pl.CostEstimate(flops=20_000_000, bytes_accessed=8_000_000, transcendentals=0),
        name="local_part",
    )(*operands)


def part(x):
    return pl.pallas_call(
        part_kernel,
        out_shape=[jax.ShapeDtypeStruct((rows, 128), F32) for rows in (KAPPA, 32)],
        in_specs=[VMEM],
        out_specs=[VMEM] * 2,
        compiler_params=limit(16),
        name="part",
    )(x)


class Level:
    def __init__(self, count, refs):
        self.count = count
        self.x, self.dir, self.res, self.f = refs
        self.tables = [element_matrix(count, d) for d in range(3)]
        self.gains = self.diag = self.jac = None


def tile(index):
    return pl.ds(index * 8, 8)


def rows_of(pieces, size, r, h):
    return pieces[pl.ds(8 * h * size + r, 8, stride=size), :]


def place_pieces(blocks, stride, pieces, first, size):
    my_gx, my_gy = lax.axis_index("gx"), lax.axis_index("gy")
    for b, block in enumerate(blocks):
        for a in range(4):
            column = (my_gx ^ a) * 4 + (my_gy ^ b)
            start = pl.multiple_of(column * size, 8)
            pieces[pl.ds(start, size), :] = block[a * stride + first : a * stride + first + size, :]


class Lanes:
    def __init__(self):
        self.lane = iota((8, 128), 1)
        sub = iota((8, 128), 0)
        self.group = self.lane // EZ
        self.odd = self.group % 2 == 1
        self.element = self.lane % EZ
        self.place = sub % 4
        self.low_half = sub < 4

    def around(self, u):
        turned = pltpu.roll(u, 4, u.ndim - 2)
        far = jnp.where(self.odd, pltpu.roll(turned, 32, u.ndim - 1), pltpu.roll(turned, 96, u.ndim - 1))
        return turned, far

    def x_before(self, u):
        turned, far = self.around(u)
        return jnp.where(self.low_half, far, turned)

    def x_after(self, u):
        turned, far = self.around(u)
        return jnp.where(self.low_half, turned, far)

    def y_before(self, u):
        return jnp.where(self.place == 0, pltpu.roll(u, 5, 0), pltpu.roll(u, 1, 0))

    def y_after(self, u):
        return jnp.where(self.place == 3, pltpu.roll(u, 3, 0), pltpu.roll(u, 7, 0))

    def z_before(self, u):
        return jnp.where(self.element == 0, pltpu.roll(u, 97, u.ndim - 1), pltpu.roll(u, 1, u.ndim - 1))

    def z_after(self, u):
        last = self.element == EZ - 1
        return jnp.where(last, pltpu.roll(u, 31, u.ndim - 1), pltpu.roll(u, 127, u.ndim - 1))


def load(ref, first, count):
    return ref[pl.ds(first * 8, count * 8), :].reshape(count, 8, 128)


def store(ref, first, value):
    ref[pl.ds(first * 8, value.shape[0] * 8), :] = value.reshape(value.shape[0] * 8, 128)


DIAGS = (0, 250, 304)
GAINS = (320, 326, 332)
REGISTERS = 338
CENTRE = (CHEB_HIGH + CHEB_LOW) / 2.0
RADIUS = (CHEB_HIGH - CHEB_LOW) / 2.0


def assemble_kernel(block0, block1, block2, block3, field, coefs, pieces, edges, kappas, traces, kap):
    blocks = (block0, block1, block2, block3)
    place_pieces(blocks, PIECE, pieces, 0, HALF)
    place_pieces(blocks, PIECE, edges, HALF, TRACE)
    place_pieces(blocks, PIECE, kappas, KAPPA, 32)
    lanes = Lanes()
    group, lane = lanes.group, lanes.lane

    def widen(source, size, target):
        for r in range(size):
            low, high = rows_of(source, size, r, 0), rows_of(source, size, r, 1)
            target[tile(r), :] = jnp.where(lanes.odd, pltpu.roll(high, 32, 1), low)
            target[tile(size + r), :] = jnp.where(lanes.odd, high, pltpu.roll(low, 96, 1))

    widen(edges, TRACE, traces)
    widen(pieces, HALF, field)
    flags = []
    for r in range(3):
        got = field[tile(125 + r), :]
        across = pltpu.roll(got, 64, 1)
        flags += [jnp.where(lane < 64, got, across), jnp.where(lane < 64, across, got)]
    for r in range(32):
        turned = []
        for h in range(2):
            got = rows_of(kappas, 32, r, h)
            turned.append([pltpu.roll(got, 32 * m, 1) if m else got for m in range(4)])
        for q in range(4):
            kap[tile(q * 32 + r), :] = choose(group, [turned[g % 2][(g - q) % 4] for g in range(4)])
    for p, n in enumerate((5, 3, 2)):
        stride = 4 // (n - 1)
        gains = [face_gains(flags[d], d // 2, d % 2, n) for d in range(6)]
        if p == 0:
            for k in range(5):
                def trace(i, j, k=k):
                    return traces[tile(k * 16 + face_place(i, j)), :]

                for m in range(5):
                    for where, term in (
                        (m, gains[0] * lanes.x_before(trace(4, m))),
                        (20 + m, gains[1] * lanes.x_after(trace(0, m))),
                        (5 * m, gains[2] * lanes.y_before(trace(m, 4))),
                        (5 * m + 4, gains[3] * lanes.y_after(trace(m, 0))),
                    ):
                        field[tile(k * 25 + where), :] = field[tile(k * 25 + where), :] + term
        rows = []
        for d in range(3):
            coefs[tile(GAINS[p] + 2 * d), :] = gains[2 * d]
            coefs[tile(GAINS[p] + 2 * d + 1), :] = gains[2 * d + 1]
            table = element_matrix(n, d)
            row = [jnp.full((8, 128), float(table[m, m]), F32) for m in range(n)]
            row[0] = row[0] + gains[2 * d]
            row[n - 1] = row[n - 1] + gains[2 * d + 1]
            rows.append(row)
        along = jnp.stack(rows[1])
        for k in range(n):
            for i in range(n):
                line = load(kap, k * 25 * stride + i * stride * 5, 5)
                line = jnp.stack([line[j * stride] for j in range(n)])
                value = line + (along + (rows[2][k] + rows[0][i]))
                scale = 1.0 / (1.0 + STEP_SIZE * JACOBI_SCALE * value)
                store(coefs, DIAGS[p] + (k * n + i) * n, value)
                store(coefs, DIAGS[p] + n**3 + (k * n + i) * n, scale * (1.0 / CENTRE))


def cycle_kernel(coefs, assembled, fields, *scratch):
    sec = lax.axis_index("section")
    my_gx, my_gy = lax.axis_index("gx"), lax.axis_index("gy")
    levels = [Level(n, scratch[4 * p : 4 * p + 4]) for p, n in enumerate((5, 3, 2))]
    half = scratch[12]
    lanes = Lanes()
    lane = lanes.lane
    blocks = split_sections()[3]

    def lanes_of(upper, lower):
        return jnp.where(lane < 64, jnp.where(sec == 0, upper[0], upper[1]), jnp.where(sec == 0, lower[0], lower[1]))

    entry = [[[float(STEP_SIZE * blocks[2 * p + a, 2 * p + b]) for p in range(2)] for b in range(2)] for a in range(2)]
    same = lanes_of(entry[0][0], entry[1][1])
    swap = lanes_of(entry[0][1], entry[1][0])
    first_rho = RADIUS / CENTRE
    second_rho = 1.0 / (2.0 * CENTRE / RADIUS - first_rho)
    keep = 1.0 + second_rho * first_rho
    push = 2.0 * second_rho / RADIUS * CENTRE
    for p, level in enumerate(levels):
        size = level.count**3
        level.gains = [coefs[tile(GAINS[p] + d), :] for d in range(6)]
        level.diag = lambda first, count, p=p: load(coefs, DIAGS[p] + first, count)
        level.jac = lambda first, count, p=p, size=size: load(coefs, DIAGS[p] + size + first, count)

    def begin(level, source):
        n = level.count
        for first in range(0, n**3, n):
            f = load(source, first, n)
            store(level.dir, first, level.jac(first, n) * f)
            store(level.res, first, f)
            store(level.x, first, jnp.zeros_like(f))

    def apply(level, smooth, always):
        n = level.count
        kx, ky, kz = level.tables
        gains = level.gains
        source = level.dir if smooth else level.x
        def plane(k):
            def line_at(i):
                return load(source, (k * n + i) * n, n)

            for i in range(n):
                first = (k * n + i) * n
                v = line_at(i)
                total = level.diag(first, n) * v
                for m in range(n):
                    if m != i:
                        total = total + float(kx[i, m]) * line_at(m)
                for m in range(n):
                    if m != k:
                        total = total + float(kz[k, m]) * load(source, (m * n + i) * n, n)
                lines = []
                for j in range(n):
                    line = None
                    for m in range(n):
                        if m != j:
                            term = float(ky[j, m]) * v[m]
                            line = term if line is None else line + term
                    if j == 0:
                        line = line - gains[2] * lanes.y_before(v[n - 1])
                    if j == n - 1:
                        line = line - gains[3] * lanes.y_after(v[0])
                    lines.append(line)
                total = total + jnp.stack(lines)
                if i == 0:
                    total = total - gains[0] * lanes.x_before(line_at(n - 1))
                if i == n - 1:
                    total = total - gains[1] * lanes.x_after(line_at(0))
                if k == 0:
                    total = total - gains[4] * lanes.z_before(load(source, ((n - 1) * n + i) * n, n))
                if k == n - 1:
                    total = total - gains[5] * lanes.z_after(load(source, i * n, n))
                image = v + (same * total + swap * pltpu.roll(total, 64, 2))
                if smooth:
                    scaled = level.jac(first, n) * (load(level.res, first, n) - image)
                    store(level.x, first, load(level.x, first, n) + keep * v + push * scaled)
                else:
                    rest = load(level.f, first, n) - image
                    store(level.res, first, rest)
                    store(level.dir, first, level.jac(first, n) * rest)

        for k in range(n):
            @pl.when(always)
            def _(k=k):
                plane(k)

    def combine(weights, parts):
        total = None
        for weight, part in zip(weights, parts):
            if abs(weight) > 1e-14:
                term = part if abs(weight - 1.0) < 1e-14 else float(weight) * part
                total = term if total is None else total + term
        return total

    def change(table, source, target, add):
        m, n = table.shape
        for i in range(n):
            parts = [load(source, i * n + k * n * n, n) for k in range(n)]
            for k in range(m):
                store(half, i * n + k * n * n, combine(table[k], parts))
        for k in range(m):
            parts = [load(half, k * n * n + i * n, n) for i in range(n)]
            for i in range(m):
                line = combine(table[i], parts)
                value = jnp.stack([combine(table[j], [line[a] for a in range(n)]) for j in range(m)])
                first = k * m * m + i * m
                store(target, first, load(target, first, m) + value if add else value)

    def down(n, m):
        fine_nodes, fine_weights = lobatto(n)
        coarse_nodes, coarse_weights = lobatto(m)
        table = lagrange_table(coarse_nodes, fine_nodes)
        return (1.0 / coarse_weights)[:, None] * table.T * fine_weights[None, :]

    def up(m, n):
        return lagrange_table(lobatto(m)[0], lobatto(n)[0])

    def solve(p, always=None):
        level = levels[p]
        if p == 2:
            apply(level, True, always)
            return
        below = levels[p + 1]

        def step(t, carry):
            @pl.when(t != 1)
            def _():
                apply(level, True, t >= 0)

            @pl.when((t != 2) | (p == 0))
            def _():
                apply(level, False, t >= 0)

            @pl.when(t == 0)
            def _():
                n, m = level.count, below.count
                change(down(n, m), level.res, below.f, False)
                begin(below, below.f)
                solve(p + 1, t >= 0)
                change(up(m, n), below.x, level.x, True)
            return carry
        lax.fori_loop(0, 3, step, 0)

    fine = levels[0]
    fine.f = assembled
    begin(fine, assembled)
    solve(0)

    for first in range(0, 125, 5):
        store(fields, first, load(fine.res, first, 5))
    column = (my_gx % 2) * 4 + my_gy
    fields[FIELD : FIELD + 125, :] = fine.x[pl.ds(column, 125, stride=8), :]
    fields[FIELD + 125 : FIELD + 128, :] = jnp.zeros((3, 128), F32)


def pair_weights():
    cross = split_sections()[4]
    return jnp.where(iota((8, 128), 1) < 64, float(cross[0]), float(cross[1]))


def column_factors(p):
    sec = lax.axis_index("section")
    whole = split_sections()[0]
    lane = iota((25, 128), 1)
    here = lane // EZ % 2 == lax.axis_index("gx") // 2
    factors = []
    for s in range(2):
        parts = []
        for mine in range(2):
            t = whole[2 * mine + s]
            q = mine if p == 0 else 1 - mine
            parts.append(jnp.where(lane < 64, float(t[2 * q]), float(t[2 * q + 1])))
        factors.append(jnp.where(here, jnp.where(sec == 0, parts[0], parts[1]), 0.0))
    return factors


def column_rows(k):
    column = (lax.axis_index("gx") % 2) * 4 + lax.axis_index("gy")
    return pl.ds(k * 200 + column, 25, stride=8)


def raw_order(k):
    return (iota((128, 160), 1) == 5 * (iota((128, 160), 0) % EZ) + k).astype(F32)


def early_kernel(own, own_start, other_start, sums, column_out, cols):
    weights = pair_weights()
    cols[...] = jnp.zeros_like(cols)
    total = jnp.zeros((192, 160), F32)
    own_factors, other_factors = column_factors(0), column_factors(1)
    for k in range(5):
        where = column_rows(k)
        z = own[FIELD + k * 25 : FIELD + k * 25 + 25, :]
        start, other = own_start[where, :], other_start[where, :]
        w = start - own[where, :]
        for s in range(2):
            cols[s * 32 : s * 32 + 25, :] = own_factors[s] * z
            cols[64 + s * 32 : 64 + s * 32 + 25, :] = own_factors[s] * start + other_factors[s] * other
            cols[128 + s * 32 : 128 + s * 32 + 25, :] = own_factors[s] * w
        total = total + split_dot(cols[...], raw_order(k))
    column_out[...] = total
    nothing = jnp.zeros((8, 128), F32)
    uppers, sizes = [nothing] * 5, [nothing] * 5
    for r in range(125):
        c, d = own_start[tile(r), :], other_start[tile(r), :]
        a = c - own[tile(r), :]
        uppers[r % 5] = uppers[r % 5] + a * (c + weights * d)
        sizes[r % 5] = sizes[r % 5] + ((c * c + d * d) + 2.0 * (weights * (c * d)))
    sums[0:8, :] = sum(uppers)
    sums[8:16, :] = sum(sizes)


def finish_kernel(own, other, own_start, other_start, sums, column, guess, sol, res_out, arnoldi, cols, outs):
    sec = lax.axis_index("section")
    weights = pair_weights()
    cols[...] = jnp.zeros_like(cols)
    total = jnp.zeros((128, 160), F32)
    factors = column_factors(1)
    for k in range(5):
        where = column_rows(k)
        z = other[FIELD + k * 25 : FIELD + k * 25 + 25, :]
        w = other_start[where, :] - other[where, :]
        for s in range(2):
            cols[s * 32 : s * 32 + 25, :] = factors[s] * z
            cols[64 + s * 32 : 64 + s * 32 + 25, :] = factors[s] * w
        total = total + split_dot(cols[...], raw_order(k))
    nothing = jnp.zeros((8, 128), F32)
    uppers = [nothing] * 5
    for r in range(125):
        c, d = own_start[tile(r), :], other_start[tile(r), :]
        b = d - other[tile(r), :]
        uppers[r % 5] = uppers[r % 5] + b * (d + weights * c)

    mine, theirs = sums[0:8, :], sum(uppers)
    size = jnp.sum(sums[8:16, :], keepdims=True)
    upper = jnp.sum(mine + theirs, keepdims=True) / size
    rests = [nothing] * 5
    for r in range(125):
        c, d = own_start[tile(r), :], other_start[tile(r), :]
        a = (c - own[tile(r), :]) - upper * c
        b = (d - other[tile(r), :]) - upper * d
        rests[r % 5] = rests[r % 5] + ((a * a + b * b) + 2.0 * (weights * (a * b)))
    rest = jnp.sum(sum(rests), keepdims=True)
    beta = jnp.sqrt(size)
    lower = jnp.sqrt(rest) / beta
    weight = upper / (upper * upper + lower * lower)
    entries = float(125 * EZ * COLS * 4)
    for place_out, value in enumerate((beta * (1.0 / math.sqrt(entries)), upper, lower)):
        arnoldi[place_out] = value[0, 0]
    outs[:64, :] = weight * (column[:64, :] + total[:64])
    outs[64:, :] = column[64:128, :] - weight * (column[128:, :] + total[64:])
    for i in range(5):
        for j in range(5):
            r = 5 * i + j
            for s in range(2):
                sol[i, j, s : s + 1, :] = guess[i, j, s : s + 1, :] + outs[s * 32 + r : s * 32 + r + 1, :]
                res_out[i, j, s : s + 1, :] = outs[64 + s * 32 + r : 64 + s * 32 + r + 1, :]


def assemble(blocks):
    return pl.pallas_call(
        assemble_kernel,
        out_shape=[
            jax.ShapeDtypeStruct((128 * 8, 128), F32),
            jax.ShapeDtypeStruct((REGISTERS * 8, 128), F32),
        ],
        in_specs=[VMEM] * 4,
        out_specs=[VMEM] * 2,
        scratch_shapes=[
            pltpu.VMEM((COLS * HALF, 128), F32),
            pltpu.VMEM((COLS * TRACE, 128), F32),
            pltpu.VMEM((COLS * 32, 128), F32),
            pltpu.VMEM((80 * 8, 128), F32),
            pltpu.VMEM((128 * 8, 128), F32),
        ],
        compiler_params=limit(16),
        name="assemble",
    )(*blocks)


def cycle(coefs, assembled):
    scratch = []
    for n in (5, 3, 2):
        scratch += [pltpu.VMEM((n**3 * 8, 128), F32)] * 4
    scratch += [pltpu.VMEM((FIELD, 128), F32)]
    return pl.pallas_call(
        cycle_kernel,
        out_shape=jax.ShapeDtypeStruct((FIELD + 128, 128), F32),
        in_specs=[VMEM] * 2,
        out_specs=VMEM,
        scratch_shapes=scratch,
        compiler_params=limit(24),
        cost_estimate=pl.CostEstimate(flops=40_000_000, bytes_accessed=30_000_000, transcendentals=0),
        name="cycle",
    )(coefs, assembled)


def early(own, own_start, other_start):
    return pl.pallas_call(
        early_kernel,
        out_shape=[jax.ShapeDtypeStruct((16, 128), F32), jax.ShapeDtypeStruct((192, 160), F32)],
        in_specs=[VMEM] * 3,
        out_specs=[VMEM] * 2,
        scratch_shapes=[pltpu.VMEM((192, 128), F32)],
        compiler_params=limit(16),
        cost_estimate=pl.CostEstimate(flops=4_000_000, bytes_accessed=4_000_000, transcendentals=0),
        name="early",
    )(own, own_start, other_start)


def finish(own, other, own_start, other_start, sums, column, guess):
    return pl.pallas_call(
        finish_kernel,
        out_shape=[
            jax.ShapeDtypeStruct(guess.shape, F32),
            jax.ShapeDtypeStruct(guess.shape, F32),
            jax.ShapeDtypeStruct((3,), F32),
        ],
        in_specs=[VMEM] * 7,
        out_specs=[VMEM, VMEM, pl.BlockSpec(memory_space=pltpu.SMEM)],
        scratch_shapes=[pltpu.VMEM((128, 128), F32), pltpu.VMEM((128, 160), F32)],
        compiler_params=limit(24),
        name="finish",
    )(own, other, own_start, other_start, sums, column, guess)


def exchange(x, axis, bits):
    return lax.ppermute(x, axis, [(n, n ^ bits) for n in range(lax.axis_size(axis))])


def gathered_body(rhs, guess, kappa, bc_flags):
    rhs, guess = (jnp.transpose(v, (1, 2, 0, 3)) for v in (rhs, guess))
    mine, theirs = local_part(rhs, guess, kappa, bc_flags)
    got, mine, kappa_piece = lax.optimization_barrier((exchange(theirs, "section", 1), *part(mine)))
    piece = jnp.concatenate([mine + got, kappa_piece])
    line = jnp.concatenate([piece] + [exchange(piece, "gx", bits) for bits in (1, 2, 3)])
    blocks = [line] + [exchange(line, "gy", bits) for bits in (1, 2, 3)]
    start, coefs = assemble(blocks)
    other_start = exchange(start, "section", 1)
    own, other_start = lax.optimization_barrier((cycle(coefs, start), other_start))
    sums, column = early(own, start, other_start)
    sol, res, arnoldi = finish(own, exchange(own, "section", 1), start, other_start, sums, column, guess)
    sol, res = (jnp.transpose(v, (2, 0, 1, 3)) for v in (sol, res))
    return sol, res, arnoldi


def solution(mesh):
    placed = (
        P("section", "gx", "gy", None),
        P("section", "gx", "gy", None),
        P("gx", "gy", None),
        P(None, "gx", "gy", None),
    )
    sizes = (mesh.shape["section"], mesh.shape["gx"], mesh.shape["gy"])

    def step(rhs, guess, kappa, bc_flags):
        fits = sizes == (2, 4, 4) and rhs.shape == (4, 20, 20, 160)
        return jax.shard_map(
            gathered_body if fits else stepwise,
            mesh=mesh,
            in_specs=placed,
            out_specs=(P("section", "gx", "gy", None), P("section", "gx", "gy", None), P()),
            check_vma=False,
        )(rhs, guess, kappa, bc_flags)

    return step
```

```python
from functools import partial
import math

import jax
import jax.numpy as jnp
import numpy as np
from jax import lax
from jax.experimental import pallas as pl
from jax.experimental.pallas import tpu as pltpu
from jax.sharding import PartitionSpec as P

ADVECT = (1.0, 0.7, 0.5)
DIFFUSE = 0.05
STEP_SIZE = 0.2
JACOBI_SCALE = 0.25
CHEB_LOW = 0.25
CHEB_HIGH = 2.0
LETTERS = "abcdef"


def extended(x, sides, width):
    for axis, dim in sides:
        peers, length = (lax.axis_size(axis), x.shape[dim])
        up = [(i, (i + 1) % peers) for i in range(peers)]
        down = [(j, i) for i, j in up]
        last = lax.slice_in_dim(x, length - width, length, axis=dim)
        leading = lax.slice_in_dim(x, 0, width, axis=dim)
        before = lax.ppermute(last, axis, up)
        after = lax.ppermute(leading, axis, down)
        x = jnp.concatenate([before, x, after], axis=dim)
    return x


def lobatto(count):
    if count == 5:
        inner = math.sqrt(3.0 / 7.0)
        return (
            np.array([-1.0, -inner, 0.0, inner, 1.0]),
            np.array([0.1, 49.0 / 90.0, 32.0 / 45.0, 49.0 / 90.0, 0.1]),
        )
    if count == 3:
        return (np.array([-1.0, 0.0, 1.0]), np.array([1.0 / 3.0, 4.0 / 3.0, 1.0 / 3.0]))
    return (np.array([-1.0, 1.0]), np.array([1.0, 1.0]))


def lagrange_table(nodes, points):
    table = np.ones((len(points), len(nodes)))
    for column in range(len(nodes)):
        for other in range(len(nodes)):
            if other != column:
                table[:, column] *= (points - nodes[other]) / (nodes[column] - nodes[other])
    return table


def slope_table(nodes):
    total = len(nodes)
    factor = np.array(
        [np.prod([nodes[i] - nodes[k] for k in range(total) if k != i]) for i in range(total)]
    )
    table = np.zeros((total, total))
    for row in range(total):
        for column in range(total):
            if row != column:
                table[row, column] = factor[row] / factor[column] / (nodes[row] - nodes[column])
        table[row, row] = -np.sum(table[row])
    return table


def element_matrix(count, direction):
    nodes, weights = lobatto(count)
    slopes = slope_table(nodes)
    stiffness = (1.0 / weights)[:, None] * (slopes.T @ (weights[:, None] * slopes))
    return ADVECT[direction] * slopes + DIFFUSE * stiffness


def legendre_pair(point, order):
    values = [1.0, point]
    slopes = [0.0, 1.0]
    for index in range(1, order):
        values.append(
            ((2 * index + 1) * point * values[index] - index * values[index - 1]) / (index + 1)
        )
        slopes.append(slopes[index - 1] + (2 * index + 1) * values[index])
    return (values, slopes)


def radau_nodes():
    starts = [0.0885879595127039, 0.4094668644407347, 0.7876594617608471]
    found = []
    for start in starts:
        point = start
        for sweep in range(30):
            values, slopes = legendre_pair(2.0 * point - 1.0, 4)
            change = (values[4] - values[3]) / (2.0 * (slopes[4] - slopes[3]))
            point = point - change
        found.append(point)
    found.append(1.0)
    return found


def poly_times(coefs, root):
    result = [0.0] * (len(coefs) + 1)
    for index in range(len(coefs)):
        result[index + 1] += coefs[index]
        result[index] -= root * coefs[index]
    return result


def radau_matrix():
    order = 4
    nodes = radau_nodes()
    matrix = np.zeros((order, order))
    for column in range(order):
        coefs = [1.0]
        denominator = 1.0
        for other in range(order):
            if other != column:
                coefs = poly_times(coefs, nodes[other])
                denominator *= nodes[column] - nodes[other]
        for row in range(order):
            upper_end = nodes[row]
            integral = 0.0
            for index in range(len(coefs)):
                integral += coefs[index] * upper_end ** (index + 1) / (index + 1)
            matrix[row, column] = integral / denominator
    return matrix


def node_einsum(table, field, axis):
    labels = LETTERS[: field.ndim]
    source = labels[: axis + 1] + "j" + labels[axis + 2 :]
    target = labels[: axis + 1] + "i" + labels[axis + 2 :]
    return jnp.einsum(
        "ij," + source + "->" + target,
        jnp.asarray(table, jnp.float32),
        field,
        precision=lax.Precision.HIGHEST,
    )


def apply_along(field, axis, count, table):
    shape = field.shape
    split = shape[:axis] + (shape[axis] // count, count) + shape[axis + 1 :]
    mapped = node_einsum(table, field.reshape(split), axis)
    return mapped.reshape(
        shape[:axis] + (mapped.shape[axis] * mapped.shape[axis + 1],) + shape[axis + 1 :]
    )


def line_part(field, axis, count, table, left_gain, right_gain, left_edge, right_edge):
    shape = field.shape
    elements = shape[axis] // count
    split = field.reshape(shape[:axis] + (elements, count) + shape[axis + 1 :])
    linear = node_einsum(table, split, axis)
    first = lax.index_in_dim(split, 0, axis + 1, keepdims=False)
    last = lax.index_in_dim(split, count - 1, axis + 1, keepdims=False)
    before = jnp.concatenate(
        [jnp.expand_dims(left_edge, axis), lax.slice_in_dim(last, 0, elements - 1, axis=axis)], axis
    )
    after = jnp.concatenate(
        [lax.slice_in_dim(first, 1, elements, axis=axis), jnp.expand_dims(right_edge, axis)], axis
    )
    front = jnp.expand_dims(left_gain * (first - before), axis + 1)
    back = jnp.expand_dims(right_gain * (last - after), axis + 1)
    if count > 2:
        middle_shape = list(front.shape)
        middle_shape[axis + 1] = count - 2
        pieces = [front, jnp.zeros(middle_shape, jnp.float32), back]
    else:
        pieces = [front, back]
    return (linear + jnp.concatenate(pieces, axis + 1)).reshape(shape)


def diag_along(shape, axis, count, table, left_gain, right_gain):
    elements = shape[axis] // count
    split = shape[:axis] + (elements, count) + shape[axis + 1 :]
    profile = [1] * len(split)
    profile[axis + 1] = count
    diagonal_entries = np.array([table[index, index] for index in range(count)])
    base = jnp.broadcast_to(jnp.asarray(diagonal_entries, jnp.float32).reshape(profile), split)
    front = jnp.expand_dims(left_gain, axis + 1)
    back = jnp.expand_dims(right_gain, axis + 1)
    if count > 2:
        middle_shape = list(front.shape)
        middle_shape[axis + 1] = count - 2
        pieces = [front, jnp.zeros(middle_shape, jnp.float32), back]
    else:
        pieces = [front, back]
    return (base + jnp.concatenate(pieces, axis + 1)).reshape(shape)


def level_kappa(kappa, count):
    if count == 5:
        return kappa
    picks = np.array([0, 2, 4]) if count == 3 else np.array([0, 4])
    extents = [extent // 5 for extent in kappa.shape]
    grouped = kappa.reshape(extents[0], 5, extents[1], 5, extents[2], 5)
    for axis in (1, 3, 5):
        grouped = jnp.take(grouped, picks, axis=axis)
    return grouped.reshape(extents[0] * count, extents[1] * count, extents[2] * count)


def face_plane(face, direction, count):
    plane = face.astype(jnp.float32)
    for axis in range(3):
        if axis != direction:
            plane = jnp.repeat(plane, count, axis=axis)
    return plane


def build_level(kappa, flags, count):
    nodes, weights = lobatto(count)
    kappa_level = level_kappa(kappa, count)
    tables, lefts, rights = ([], [], [])
    diagonal = kappa_level
    for direction in range(3):
        table = element_matrix(count, direction)
        lower = face_plane(flags[2 * direction], direction, count)
        upper = face_plane(flags[2 * direction + 1], direction, count)
        left_gain = (ADVECT[direction] * (1.0 + lower) / 2.0 + DIFFUSE * count * count) / float(
            weights[0]
        )
        right_gain = (DIFFUSE * count * count - ADVECT[direction] * (1.0 - upper) / 2.0) / float(
            weights[-1]
        )
        tables.append(table)
        lefts.append(left_gain)
        rights.append(right_gain)
        diagonal = diagonal + diag_along(
            kappa_level.shape, direction, count, table, left_gain, right_gain
        )
    scale = 1.0 / (1.0 + STEP_SIZE * JACOBI_SCALE * diagonal)
    return (count, tables, lefts, rights, kappa_level, scale)


def restrict(field, fine_count, coarse_count):
    fine_nodes, fine_weights = lobatto(fine_count)
    coarse_nodes, coarse_weights = lobatto(coarse_count)
    table = (
        (1.0 / coarse_weights)[:, None]
        * lagrange_table(coarse_nodes, fine_nodes).T
        * fine_weights[None, :]
    )
    for axis in range(field.ndim - 3, field.ndim):
        field = apply_along(field, axis, fine_count, table)
    return field


def prolong(field, coarse_count, fine_count):
    fine_nodes, fine_weights = lobatto(fine_count)
    coarse_nodes, coarse_weights = lobatto(coarse_count)
    table = lagrange_table(coarse_nodes, fine_nodes)
    for axis in range(field.ndim - 3, field.ndim):
        field = apply_along(field, axis, coarse_count, table)
    return field


def chebyshev(rhs, start, level, operator):
    centre = (CHEB_HIGH + CHEB_LOW) / 2.0
    radius = (CHEB_HIGH - CHEB_LOW) / 2.0
    ratio = centre / radius
    first_rho = 1.0 / ratio
    second_rho = 1.0 / (2.0 * ratio - first_rho)
    scale = level[5]
    if start is None:
        remain = rhs
    else:
        remain = rhs - operator(start, level)
    step = scale * remain / centre
    guess = step if start is None else start + step
    remain = remain - operator(step, level)
    step = second_rho * first_rho * step + 2.0 * second_rho / radius * scale * remain
    return guess + step


def vcycle(rhs, levels, operator):
    fine, middle, coarse = levels
    fine_x = chebyshev(rhs, None, fine, operator)
    middle_rhs = restrict(rhs - operator(fine_x, fine), 5, 3)
    middle_x = chebyshev(middle_rhs, None, middle, operator)
    coarse_rhs = restrict(middle_rhs - operator(middle_x, middle), 3, 2)
    coarse_x = chebyshev(coarse_rhs, None, coarse, operator)
    middle_x = chebyshev(middle_rhs, middle_x + prolong(coarse_x, 2, 3), middle, operator)
    return chebyshev(rhs, fine_x + prolong(middle_x, 3, 5), fine, operator)


def spatial(field, level):
    count, tables, lefts, rights, kappa_level, scale = level
    padded = extended(field, (("gx", 1), ("gy", 2)), 1)
    total = kappa_level * field
    total = total + line_part(
        field,
        1,
        count,
        tables[0],
        lefts[0],
        rights[0],
        padded[:, 0, 1:-1, :],
        padded[:, -1, 1:-1, :],
    )
    total = total + line_part(
        field,
        2,
        count,
        tables[1],
        lefts[1],
        rights[1],
        padded[:, 1:-1, 0, :],
        padded[:, 1:-1, -1, :],
    )
    total = total + line_part(
        field, 3, count, tables[2], lefts[2], rights[2], field[:, :, :, -1], field[:, :, :, 0]
    )
    return total


def apply_system(field, level, coupling):
    image = spatial(field, level)
    everyone = lax.all_gather(image, "section", axis=0, tiled=True)
    butcher = jnp.asarray(radau_matrix(), jnp.float32)
    rows = lax.dynamic_slice_in_dim(
        butcher, lax.axis_index("section") * field.shape[0], field.shape[0], 0
    )
    mixed = jnp.einsum("ij,jabc->iabc", rows, everyone, precision=lax.Precision.HIGHEST)
    return field + STEP_SIZE * mixed


def global_total(values):
    return lax.psum(values, ("section", "gx", "gy"))


def stepwise(rhs, guess, kappa, bc_flags):
    levels = [build_level(kappa, bc_flags, count) for count in (5, 3, 2)]
    section_operator = partial(apply_system, coupling=None)
    start_residual = rhs - section_operator(guess, levels[0])
    dofs = float(rhs.size * lax.axis_size("section") * lax.axis_size("gx") * lax.axis_size("gy"))
    beta = jnp.sqrt(global_total(jnp.sum(start_residual * start_residual).reshape(1))[0])
    basis = start_residual / beta
    precond = vcycle(basis, levels, section_operator)
    image = section_operator(precond, levels[0])
    upper = global_total(jnp.sum(image * basis).reshape(1))[0]
    remainder = image - upper * basis
    lower = jnp.sqrt(global_total(jnp.sum(remainder * remainder).reshape(1))[0])
    weight = beta * upper / (upper * upper + lower * lower)
    solution = guess + weight * precond
    residual = start_residual - weight * image
    arnoldi = jnp.stack([beta / math.sqrt(dofs), upper, lower]).astype(jnp.float32)
    return (solution, residual, arnoldi)


EZ = 32
COLS = 16
HALF = 64
FACE_X = HALF + 25
KAPPA = FACE_X + 15
PIECE = KAPPA + 16
LINE_KAPPA = 4 * HALF
LINE_Y = LINE_KAPPA + 4 * 16
LINE = LINE_Y + 104
FIELD = 1000
F32 = jnp.float32


def split_sections():
    matrix = radau_matrix()
    values, vectors = np.linalg.eig(matrix)
    order = [n for n in np.argsort(np.abs(values.imag), kind="stable") if values[n].imag > 0]
    bases = []
    for n in order:
        plane = np.stack([vectors[:, n].real, vectors[:, n].imag], axis=1)
        bases.append(np.linalg.qr(plane)[0])
    left, cross, right = np.linalg.svd(bases[0].T @ bases[1])
    bases = [bases[0] @ left, bases[1] @ right.T]
    for c in range(2):
        sign = np.sign(bases[0][np.argmax(np.abs(bases[0][:, c])), c])
        bases = [np.concatenate([b[:, :c], sign * b[:, c : c + 1], b[:, c + 1 :]], axis=1) for b in bases]
    whole = np.concatenate(bases, axis=1)
    back = np.linalg.inv(whole)
    return whole, back, back @ matrix, back @ matrix @ whole, cross


def iota(shape, dim):
    return lax.broadcasted_iota(jnp.int32, shape, dim)


def exact_dot(a, b):
    return lax.dot_general(
        a, b, (((1,), (0,)), ((), ())), precision=lax.Precision.HIGHEST, preferred_element_type=F32
    )


def split_dot(a, b):
    high = a.astype(jnp.bfloat16)
    rest = a - high.astype(F32)
    middle = rest.astype(jnp.bfloat16)
    low = (rest - middle.astype(F32)).astype(jnp.bfloat16)
    b = b.astype(jnp.bfloat16)
    return sum(
        lax.dot_general(part, b, (((1,), (0,)), ((), ())), preferred_element_type=F32)
        for part in (low, middle, high)
    )


def choose(index, values):
    out = values[-1]
    for place in range(len(values) - 2, -1, -1):
        out = jnp.where(index == place, values[place], out)
    return out


def face_gains(flag, direction, side, count):
    nodes, weights = lobatto(count)
    c, nu = ADVECT[direction], DIFFUSE * count * count
    if side == 0:
        return (c * (1.0 + flag) / 2.0 + nu) * (1.0 / float(weights[0]))
    return (nu - c * (1.0 - flag) / 2.0) * (1.0 / float(weights[-1]))


def row_table():
    kx, ky = (element_matrix(5, d) for d in range(2))
    rows = np.zeros((64, 64))
    for s in range(2):
        for i in range(5):
            for j in range(5):
                r = s * 32 + i * 5 + j
                for m in range(5):
                    rows[r, s * 32 + m * 5 + j] += kx[i, m]
                    rows[r, s * 32 + i * 5 + m] += ky[j, m]
    return rows.astype(np.float32)


def pick_line(k):
    return (iota((160, 128), 0) == 5 * (iota((160, 128), 1) % EZ) + k).astype(F32)


def pair_factors(sec, table, own, s):
    upper = iota((32, 128), 1) < 64
    first = jnp.where(upper, float(table[0, s]), float(table[1, s]))
    second = jnp.where(upper, float(table[2, 2 + s]), float(table[3, 2 + s]))
    if not own:
        first = jnp.where(upper, float(table[2, s]), float(table[3, s]))
        second = jnp.where(upper, float(table[0, 2 + s]), float(table[1, 2 + s]))
    return jnp.where(sec == 0, first, second)


def pack_nodes(nodes):
    half = nodes.shape[0] // 2
    odd = iota((half, 128), 1) // EZ % 2 == 1
    return jnp.where(odd, nodes[half:, :], nodes[:half, :])


def fetch(pairs, sems):
    copies = [pltpu.make_async_copy(src, dst, sems.at[n]) for n, (src, dst) in enumerate(pairs)]
    for copy in copies:
        copy.start()
    for copy in copies:
        copy.wait()


def local_kernel(
    rhs_in, guess_in, kappa_in, flags_in, rows_in, mine, theirs,
    rhs, guess, kappa, flags, rows_t, sems, stack, lines, nodes, y_faces, x_faces,
):
    sec = lax.axis_index("section")
    fetch([(rhs_in, rhs), (guess_in, guess), (kappa_in, kappa), (flags_in, flags), (rows_in, rows_t)], sems)
    stack[...] = jnp.zeros_like(stack)
    for i in range(5):
        stack[192 + 5 * i : 197 + 5 * i, :] = kappa[i]
        for j in range(5):
            r = 5 * i + j
            value = guess[i, j]
            left = rhs[i, j] - value
            for s in range(2):
                stack[s * 32 + r : s * 32 + r + 1, :] = left[s : s + 1]
                stack[128 + s * 32 + r : 128 + s * 32 + r + 1, :] = value[s : s + 1]
    stack[64:128, :] = exact_dot(rows_t[...], stack[128:192, :])
    source = stack[...]
    for k in range(5):
        lines[224 * k : 224 * k + 224, :] = split_dot(source, pick_line(k))

    def part(k, first):
        return lines[224 * k + first : 224 * k + first + 32, :]

    repeat = (iota((EZ, 128), 1) % EZ == iota((EZ, 128), 0)).astype(F32)
    shown = split_dot(flags[:, 0, 0, :].astype(F32), repeat)
    gains = [face_gains(shown[d : d + 1, :], d // 2, d % 2, 5) for d in range(6)]
    row = iota((32, 128), 0)
    none = jnp.zeros((32, 128), F32)
    own = jnp.where(row < 5, gains[0], jnp.where((row >= 20) & (row < 25), gains[1], none))
    own = own + jnp.where(row % 5 == 0, gains[2], jnp.where(row % 5 == 4, gains[3], none))
    kz = element_matrix(5, 2)
    back, back_matrix = split_sections()[1:3]
    for ref in (nodes, y_faces, x_faces):
        ref[...] = jnp.zeros_like(ref)
    for k in range(5):
        diagonal = part(k, 192) + own
        if k == 0:
            diagonal = diagonal + gains[4]
        if k == 4:
            diagonal = diagonal + gains[5]
        images = []
        for s in range(2):
            first = 128 + 32 * s
            image = diagonal * part(k, first) + part(k, 64 + 32 * s)
            for m in range(5):
                image = image + float(kz[k, m]) * part(m, first)
            if k == 0:
                image = image - gains[4] * pltpu.roll(part(4, first), 1, 1)
            if k == 4:
                image = image - gains[5] * pltpu.roll(part(0, first), 127, 1)
            images.append(image)
        for p, mark in enumerate((True, False)):
            total = jnp.zeros((32, 128), F32)
            trace = jnp.zeros((32, 128), F32)
            for s in range(2):
                total = total + pair_factors(sec, back, mark, s) * part(k, 32 * s)
                factor = pair_factors(sec, STEP_SIZE * back_matrix, mark, s)
                total = total - factor * images[s]
                trace = trace + factor * part(k, 128 + 32 * s)
            nodes[128 * p + 25 * k : 128 * p + 25 * k + 25, :] = total[:25]
            for i in range(5):
                for f in range(2):
                    r = 64 * p + 32 * f + 5 * k + i
                    y_faces[r : r + 1, :] = trace[5 * i + 4 * f : 5 * i + 4 * f + 1]
            for f in range(2):
                r = 32 * p + 16 * f + 3 * k
                x_faces[r : r + 3, :] = trace[20 * f + 1 : 20 * f + 4]
    upper = iota((1, 128), 1) < 64
    for r in range(3):
        nodes[125 + r : 126 + r, :] = jnp.where(upper, shown[2 * r : 2 * r + 1], shown[2 * r + 1 : 2 * r + 2])
    for p, out in enumerate((mine, theirs)):
        out[:HALF, :] = pack_nodes(nodes[128 * p : 128 * p + 128, :])
        out[HALF:FACE_X, :] = pack_nodes(y_faces[64 * p : 64 * p + 64, :])[:25]
        out[FACE_X:KAPPA, :] = pack_nodes(x_faces[32 * p : 32 * p + 32, :])[:15]
    for k in range(5):
        nodes[25 * k : 25 * k + 25, :] = part(k, 192)[:25]
    kappas = choose(iota((32, 128), 1) // EZ, [nodes[32 * q : 32 * q + 32, :] for q in range(4)])
    mine[KAPPA:, :] = jnp.where(sec == 0, kappas[:16], kappas[16:])


def part_kernel(source, piece, kappa):
    piece[...] = source[:KAPPA, :]
    kappa[...] = source[KAPPA:, :]


VMEM = pl.BlockSpec(memory_space=pltpu.VMEM)
HBM = pl.BlockSpec(memory_space=pltpu.HBM)


def limit(mib):
    return pltpu.CompilerParams(vmem_limit_bytes=mib * 2**20)


def local_part(rhs, guess, kappa, flags):
    operands = (rhs, guess, kappa, flags, jnp.asarray(row_table()))
    return pl.pallas_call(
        local_kernel,
        out_shape=[jax.ShapeDtypeStruct((rows, 128), F32) for rows in (PIECE, KAPPA)],
        in_specs=[HBM] * 5,
        out_specs=[VMEM] * 2,
        scratch_shapes=[pltpu.VMEM(o.shape, o.dtype) for o in operands]
        + [
            pltpu.SemaphoreType.DMA((5,)),
            pltpu.VMEM((224, 160), F32),
            pltpu.VMEM((5 * 224, 128), F32),
            pltpu.VMEM((256, 128), F32),
            pltpu.VMEM((128, 128), F32),
            pltpu.VMEM((64, 128), F32),
        ],
        compiler_params=limit(60),
        cost_estimate=pl.CostEstimate(flops=20_000_000, bytes_accessed=8_000_000, transcendentals=0),
        name="local_part",
    )(*operands)


def part(x):
    return pl.pallas_call(
        part_kernel,
        out_shape=[jax.ShapeDtypeStruct((rows, 128), F32) for rows in (KAPPA, 16)],
        in_specs=[VMEM],
        out_specs=[VMEM] * 2,
        compiler_params=limit(16),
        name="part",
    )(x)


class Level:
    def __init__(self, count, refs):
        self.count = count
        self.x, self.dir, self.res, self.f = refs
        self.tables = [element_matrix(count, d) for d in range(3)]
        self.gains = self.diag = self.jac = None


def tile(index):
    return pl.ds(index * 8, 8)


def rows_of(pieces, size, r, h):
    return pieces[pl.ds(8 * h * size + r, 8, stride=size), :]


def place_pieces(blocks, pieces, first, size, room):
    my_gx, my_gy = lax.axis_index("gx"), lax.axis_index("gy")
    for b, block in enumerate(blocks):
        for a in range(4):
            column = (my_gx ^ a) * 4 + (my_gy ^ b)
            start = pl.multiple_of(column * room, 8)
            pieces[pl.ds(start, size), :] = block[first + a * size : first + a * size + size, :]


class Lanes:
    def __init__(self):
        self.lane = iota((8, 128), 1)
        sub = iota((8, 128), 0)
        self.group = self.lane // EZ
        self.odd = self.group % 2 == 1
        self.element = self.lane % EZ
        self.place = sub % 4
        self.low_half = sub < 4

    def around(self, u):
        turned = pltpu.roll(u, 4, u.ndim - 2)
        far = jnp.where(self.odd, pltpu.roll(turned, 32, u.ndim - 1), pltpu.roll(turned, 96, u.ndim - 1))
        return turned, far

    def x_before(self, u):
        turned, far = self.around(u)
        return jnp.where(self.low_half, far, turned)

    def x_after(self, u):
        turned, far = self.around(u)
        return jnp.where(self.low_half, turned, far)

    def y_before(self, u):
        return jnp.where(self.place == 0, pltpu.roll(u, 5, 0), pltpu.roll(u, 1, 0))

    def y_after(self, u):
        return jnp.where(self.place == 3, pltpu.roll(u, 3, 0), pltpu.roll(u, 7, 0))

    def z_before(self, u):
        return jnp.where(self.element == 0, pltpu.roll(u, 97, u.ndim - 1), pltpu.roll(u, 1, u.ndim - 1))

    def z_after(self, u):
        last = self.element == EZ - 1
        return jnp.where(last, pltpu.roll(u, 31, u.ndim - 1), pltpu.roll(u, 127, u.ndim - 1))


def load(ref, first, count):
    return ref[pl.ds(first * 8, count * 8), :].reshape(count, 8, 128)


def store(ref, first, value):
    ref[pl.ds(first * 8, value.shape[0] * 8), :] = value.reshape(value.shape[0] * 8, 128)


DIAGS = (0, 250, 304)
GAINS = (320, 326, 332)
REGISTERS = 338
CENTRE = (CHEB_HIGH + CHEB_LOW) / 2.0
RADIUS = (CHEB_HIGH - CHEB_LOW) / 2.0


def flag_lanes(row, slot):
    turned = [row] + [pltpu.roll(row, 32 * m, 1) for m in range(1, 4)]
    return choose(iota(row.shape, 1) // EZ, [turned[(g - 2 * slot - 1) % 4] for g in range(4)])


def line_kernel(piece0, piece1, piece2, piece3, line, faces):
    pieces = (piece0, piece1, piece2, piece3)
    even = lax.axis_index("gx") % 2 == 0
    odd = iota((8, 128), 1) // EZ % 2 == 1
    faces[...] = jnp.zeros_like(faces)

    def both(rows, f):
        side = odd[:1] if f else jnp.logical_not(odd[:1])
        return jnp.where(side, rows, pltpu.roll(rows, 96 if f else 32, 1))

    for a, piece in enumerate(pieces):
        for f in range(2):
            base = 64 * a + 32 * f
            inner = both(piece[FACE_X:KAPPA, :], f)
            ends = [both(piece[HALF:FACE_X, :], g) for g in range(2)]
            for k in range(5):
                r = base + 5 * k
                node = 5 * k + 4 * f
                faces[r : r + 1, :] = ends[0][node : node + 1]
                faces[r + 1 : r + 4, :] = inner[3 * k : 3 * k + 3]
                faces[r + 4 : r + 5, :] = ends[1][node : node + 1]
    for a, piece in enumerate(pieces):
        line[HALF * a : HALF * a + HALF, :] = piece[:HALF, :]
        line[LINE_KAPPA + 16 * a : LINE_KAPPA + 16 * a + 16, :] = piece[KAPPA:, :]
        line[LINE_Y + 25 * a : LINE_Y + 25 * a + 25, :] = piece[HALF:FACE_X, :]
        flags = [flag_lanes(piece[61:62, :], slot) for slot in range(2)]
        gains = [face_gains(flags[d], 0, d, 5) for d in range(2)]
        next_first = even if a % 2 == 0 else jnp.logical_not(even)
        for f in range(2):
            one = faces[64 * (a ^ 1) + 32 * (1 - f) : 64 * (a ^ 1) + 32 * (1 - f) + 32, :]
            three = faces[64 * (a ^ 3) + 32 * (1 - f) : 64 * (a ^ 3) + 32 * (1 - f) + 32, :]
            near = jnp.where(next_first, one, three) if f else jnp.where(next_first, three, one)
            term = gains[f] * near
            for k in range(5):
                node = 25 * k + 20 * f
                side = odd[:5] if node >= HALF else jnp.logical_not(odd[:5])
                r = HALF * a + node % HALF
                line[r : r + 5, :] = line[r : r + 5, :] + jnp.where(side, term[5 * k : 5 * k + 5], 0.0)
    line[LINE_Y + 100 :, :] = jnp.zeros((4, 128), F32)


def halves_kernel(block0, block1, block2, block3, out):
    place_pieces((block0, block1, block2, block3), out, LINE_KAPPA, 16, 16)


def widen(low, high, odd):
    return jnp.where(odd, pltpu.roll(high, 32, 1), low), jnp.where(odd, high, pltpu.roll(low, 96, 1))


def assemble_kernel(block0, block1, block2, block3, field, pieces, edges, traces):
    blocks = (block0, block1, block2, block3)
    place_pieces(blocks, pieces, 0, HALF, HALF)
    place_pieces(blocks, edges, LINE_Y, 25, 32)
    lanes = Lanes()
    for source, size, rows, target, apart in ((edges, 32, 25, traces, 25), (pieces, HALF, HALF, field, HALF)):
        for r in range(rows):
            first, second = widen(rows_of(source, size, r, 0), rows_of(source, size, r, 1), lanes.odd)
            target[tile(r), :] = first
            target[tile(apart + r), :] = second
    got = field[tile(126), :]
    across = pltpu.roll(got, 64, 1)
    gains = [
        face_gains(jnp.where(lanes.lane < 64, got, across), 1, 0, 5),
        face_gains(jnp.where(lanes.lane < 64, across, got), 1, 1, 5),
    ]
    for k in range(5):
        for i in range(5):
            lower, upper = traces[tile(5 * k + i), :], traces[tile(25 + 5 * k + i), :]
            node = 25 * k + 5 * i
            field[tile(node), :] = field[tile(node), :] + gains[0] * lanes.y_before(upper)
            field[tile(node + 4), :] = field[tile(node + 4), :] + gains[1] * lanes.y_after(lower)


def setup_kernel(field, own_halves, other_halves, coefs, kap):
    sec = lax.axis_index("section")
    lanes = Lanes()
    group, lane = lanes.group, lanes.lane
    flags = []
    for r in range(3):
        got = field[tile(125 + r), :]
        across = pltpu.roll(got, 64, 1)
        flags += [jnp.where(lane < 64, got, across), jnp.where(lane < 64, across, got)]
    for r in range(16):
        pairs = [[rows_of(ref, 16, r, h) for h in range(2)] for ref in (own_halves, other_halves)]
        for half in range(2):
            turned = []
            for h in range(2):
                got = jnp.where(sec == half, pairs[0][h], pairs[1][h])
                turned.append([pltpu.roll(got, 32 * m, 1) if m else got for m in range(4)])
            for q in range(4):
                value = choose(group, [turned[g % 2][(g - q) % 4] for g in range(4)])
                kap[tile(q * 32 + half * 16 + r), :] = value
    for p, n in enumerate((5, 3, 2)):
        stride = 4 // (n - 1)
        gains = [face_gains(flags[d], d // 2, d % 2, n) for d in range(6)]
        rows = []
        for d in range(3):
            coefs[tile(GAINS[p] + 2 * d), :] = gains[2 * d]
            coefs[tile(GAINS[p] + 2 * d + 1), :] = gains[2 * d + 1]
            table = element_matrix(n, d)
            row = [jnp.full((8, 128), float(table[m, m]), F32) for m in range(n)]
            row[0] = row[0] + gains[2 * d]
            row[n - 1] = row[n - 1] + gains[2 * d + 1]
            rows.append(row)
        along = jnp.stack(rows[1])
        for k in range(n):
            for i in range(n):
                line = load(kap, k * 25 * stride + i * stride * 5, 5)
                line = jnp.stack([line[j * stride] for j in range(n)])
                value = line + (along + (rows[2][k] + rows[0][i]))
                scale = 1.0 / (1.0 + STEP_SIZE * JACOBI_SCALE * value)
                store(coefs, DIAGS[p] + (k * n + i) * n, value)
                store(coefs, DIAGS[p] + n**3 + (k * n + i) * n, scale * (1.0 / CENTRE))


def cycle_kernel(coefs, assembled, fields, *scratch):
    sec = lax.axis_index("section")
    my_gx, my_gy = lax.axis_index("gx"), lax.axis_index("gy")
    levels = [Level(n, scratch[4 * p : 4 * p + 4]) for p, n in enumerate((5, 3, 2))]
    half = scratch[12]
    lanes = Lanes()
    lane = lanes.lane
    blocks = split_sections()[3]

    def lanes_of(upper, lower):
        return jnp.where(lane < 64, jnp.where(sec == 0, upper[0], upper[1]), jnp.where(sec == 0, lower[0], lower[1]))

    entry = [[[float(STEP_SIZE * blocks[2 * p + a, 2 * p + b]) for p in range(2)] for b in range(2)] for a in range(2)]
    same = lanes_of(entry[0][0], entry[1][1])
    swap = lanes_of(entry[0][1], entry[1][0])
    first_rho = RADIUS / CENTRE
    second_rho = 1.0 / (2.0 * CENTRE / RADIUS - first_rho)
    keep = 1.0 + second_rho * first_rho
    push = 2.0 * second_rho / RADIUS * CENTRE
    for p, level in enumerate(levels):
        size = level.count**3
        level.gains = [coefs[tile(GAINS[p] + d), :] for d in range(6)]
        level.diag = lambda first, count, p=p: load(coefs, DIAGS[p] + first, count)
        level.jac = lambda first, count, p=p, size=size: load(coefs, DIAGS[p] + size + first, count)

    def begin(level, source):
        n = level.count
        for first in range(0, n**3, n):
            f = load(source, first, n)
            store(level.dir, first, level.jac(first, n) * f)
            store(level.res, first, f)
            store(level.x, first, jnp.zeros_like(f))

    def apply(level, smooth, always):
        n = level.count
        kx, ky, kz = level.tables
        gains = level.gains
        source = level.dir if smooth else level.x
        def plane(k):
            def line_at(i):
                return load(source, (k * n + i) * n, n)

            for i in range(n):
                first = (k * n + i) * n
                v = line_at(i)
                total = level.diag(first, n) * v
                for m in range(n):
                    if m != i:
                        total = total + float(kx[i, m]) * line_at(m)
                for m in range(n):
                    if m != k:
                        total = total + float(kz[k, m]) * load(source, (m * n + i) * n, n)
                lines = []
                for j in range(n):
                    line = None
                    for m in range(n):
                        if m != j:
                            term = float(ky[j, m]) * v[m]
                            line = term if line is None else line + term
                    if j == 0:
                        line = line - gains[2] * lanes.y_before(v[n - 1])
                    if j == n - 1:
                        line = line - gains[3] * lanes.y_after(v[0])
                    lines.append(line)
                total = total + jnp.stack(lines)
                if i == 0:
                    total = total - gains[0] * lanes.x_before(line_at(n - 1))
                if i == n - 1:
                    total = total - gains[1] * lanes.x_after(line_at(0))
                if k == 0:
                    total = total - gains[4] * lanes.z_before(load(source, ((n - 1) * n + i) * n, n))
                if k == n - 1:
                    total = total - gains[5] * lanes.z_after(load(source, i * n, n))
                image = v + (same * total + swap * pltpu.roll(total, 64, 2))
                if smooth:
                    scaled = level.jac(first, n) * (load(level.res, first, n) - image)
                    store(level.x, first, load(level.x, first, n) + keep * v + push * scaled)
                else:
                    rest = load(level.f, first, n) - image
                    store(level.res, first, rest)
                    store(level.dir, first, level.jac(first, n) * rest)

        for k in range(n):
            @pl.when(always)
            def _(k=k):
                plane(k)

    def combine(weights, parts):
        total = None
        for weight, part in zip(weights, parts):
            if abs(weight) > 1e-14:
                term = part if abs(weight - 1.0) < 1e-14 else float(weight) * part
                total = term if total is None else total + term
        return total

    def change(table, source, target, add):
        m, n = table.shape
        for i in range(n):
            parts = [load(source, i * n + k * n * n, n) for k in range(n)]
            for k in range(m):
                store(half, i * n + k * n * n, combine(table[k], parts))
        for k in range(m):
            parts = [load(half, k * n * n + i * n, n) for i in range(n)]
            for i in range(m):
                line = combine(table[i], parts)
                value = jnp.stack([combine(table[j], [line[a] for a in range(n)]) for j in range(m)])
                first = k * m * m + i * m
                store(target, first, load(target, first, m) + value if add else value)

    def down(n, m):
        fine_nodes, fine_weights = lobatto(n)
        coarse_nodes, coarse_weights = lobatto(m)
        table = lagrange_table(coarse_nodes, fine_nodes)
        return (1.0 / coarse_weights)[:, None] * table.T * fine_weights[None, :]

    def up(m, n):
        return lagrange_table(lobatto(m)[0], lobatto(n)[0])

    def solve(p, always=None):
        level = levels[p]
        if p == 2:
            apply(level, True, always)
            return
        below = levels[p + 1]

        def step(t, carry):
            @pl.when(t != 1)
            def _():
                apply(level, True, t >= 0)

            @pl.when((t != 2) | (p == 0))
            def _():
                apply(level, False, t >= 0)

            @pl.when(t == 0)
            def _():
                n, m = level.count, below.count
                change(down(n, m), level.res, below.f, False)
                begin(below, below.f)
                solve(p + 1, t >= 0)
                change(up(m, n), below.x, level.x, True)
            return carry
        lax.fori_loop(0, 3, step, 0)

    fine = levels[0]
    fine.f = assembled
    begin(fine, assembled)
    solve(0)

    for first in range(0, 125, 5):
        store(fields, first, load(fine.res, first, 5))
    column = (my_gx % 2) * 4 + my_gy
    fields[FIELD : FIELD + 125, :] = fine.x[pl.ds(column, 125, stride=8), :]
    fields[FIELD + 125 : FIELD + 128, :] = jnp.zeros((3, 128), F32)


def pair_weights():
    cross = split_sections()[4]
    return jnp.where(iota((8, 128), 1) < 64, float(cross[0]), float(cross[1]))


def column_factors(p):
    sec = lax.axis_index("section")
    whole = split_sections()[0]
    lane = iota((25, 128), 1)
    here = lane // EZ % 2 == lax.axis_index("gx") // 2
    factors = []
    for s in range(2):
        parts = []
        for mine in range(2):
            t = whole[2 * mine + s]
            q = mine if p == 0 else 1 - mine
            parts.append(jnp.where(lane < 64, float(t[2 * q]), float(t[2 * q + 1])))
        factors.append(jnp.where(here, jnp.where(sec == 0, parts[0], parts[1]), 0.0))
    return factors


def column_rows(k):
    column = (lax.axis_index("gx") % 2) * 4 + lax.axis_index("gy")
    return pl.ds(k * 200 + column, 25, stride=8)


def raw_order(k):
    return (iota((128, 160), 1) == 5 * (iota((128, 160), 0) % EZ) + k).astype(F32)


def early_kernel(own, own_start, other_start, sums, column_out, cols):
    weights = pair_weights()
    cols[...] = jnp.zeros_like(cols)
    total = jnp.zeros((192, 160), F32)
    own_factors, other_factors = column_factors(0), column_factors(1)
    for k in range(5):
        where = column_rows(k)
        z = own[FIELD + k * 25 : FIELD + k * 25 + 25, :]
        start, other = own_start[where, :], other_start[where, :]
        w = start - own[where, :]
        for s in range(2):
            cols[s * 32 : s * 32 + 25, :] = own_factors[s] * z
            cols[64 + s * 32 : 64 + s * 32 + 25, :] = own_factors[s] * start + other_factors[s] * other
            cols[128 + s * 32 : 128 + s * 32 + 25, :] = own_factors[s] * w
        total = total + split_dot(cols[...], raw_order(k))
    column_out[...] = total
    nothing = jnp.zeros((8, 128), F32)
    uppers, sizes = [nothing] * 5, [nothing] * 5
    for r in range(125):
        c, d = own_start[tile(r), :], other_start[tile(r), :]
        a = c - own[tile(r), :]
        uppers[r % 5] = uppers[r % 5] + a * (c + weights * d)
        sizes[r % 5] = sizes[r % 5] + ((c * c + d * d) + 2.0 * (weights * (c * d)))
    sums[0:8, :] = sum(uppers)
    sums[8:16, :] = sum(sizes)


def finish_kernel(own, other, own_start, other_start, sums, column, guess, sol, res_out, arnoldi, cols, outs):
    sec = lax.axis_index("section")
    weights = pair_weights()
    cols[...] = jnp.zeros_like(cols)
    total = jnp.zeros((128, 160), F32)
    factors = column_factors(1)
    for k in range(5):
        where = column_rows(k)
        z = other[FIELD + k * 25 : FIELD + k * 25 + 25, :]
        w = other_start[where, :] - other[where, :]
        for s in range(2):
            cols[s * 32 : s * 32 + 25, :] = factors[s] * z
            cols[64 + s * 32 : 64 + s * 32 + 25, :] = factors[s] * w
        total = total + split_dot(cols[...], raw_order(k))
    nothing = jnp.zeros((8, 128), F32)
    uppers = [nothing] * 5
    for r in range(125):
        c, d = own_start[tile(r), :], other_start[tile(r), :]
        b = d - other[tile(r), :]
        uppers[r % 5] = uppers[r % 5] + b * (d + weights * c)

    mine, theirs = sums[0:8, :], sum(uppers)
    size = jnp.sum(sums[8:16, :], keepdims=True)
    upper = jnp.sum(mine + theirs, keepdims=True) / size
    rests = [nothing] * 5
    for r in range(125):
        c, d = own_start[tile(r), :], other_start[tile(r), :]
        a = (c - own[tile(r), :]) - upper * c
        b = (d - other[tile(r), :]) - upper * d
        rests[r % 5] = rests[r % 5] + ((a * a + b * b) + 2.0 * (weights * (a * b)))
    rest = jnp.sum(sum(rests), keepdims=True)
    beta = jnp.sqrt(size)
    lower = jnp.sqrt(rest) / beta
    weight = upper / (upper * upper + lower * lower)
    entries = float(125 * EZ * COLS * 4)
    for place_out, value in enumerate((beta * (1.0 / math.sqrt(entries)), upper, lower)):
        arnoldi[place_out] = value[0, 0]
    outs[:64, :] = weight * (column[:64, :] + total[:64])
    outs[64:, :] = column[64:128, :] - weight * (column[128:, :] + total[64:])
    for i in range(5):
        for j in range(5):
            r = 5 * i + j
            for s in range(2):
                sol[i, j, s : s + 1, :] = guess[i, j, s : s + 1, :] + outs[s * 32 + r : s * 32 + r + 1, :]
                res_out[i, j, s : s + 1, :] = outs[64 + s * 32 + r : 64 + s * 32 + r + 1, :]


def plain_call(kernel, name, rows, scratch, operands, cost=1_000_000):
    return pl.pallas_call(
        kernel,
        out_shape=jax.ShapeDtypeStruct((rows, 128), F32),
        in_specs=[VMEM] * len(operands),
        out_specs=VMEM,
        scratch_shapes=[pltpu.VMEM((r, 128), F32) for r in scratch],
        compiler_params=limit(16),
        cost_estimate=pl.CostEstimate(flops=cost, bytes_accessed=cost, transcendentals=0),
        name=name,
    )(*operands)


def cycle(coefs, assembled):
    scratch = []
    for n in (5, 3, 2):
        scratch += [pltpu.VMEM((n**3 * 8, 128), F32)] * 4
    scratch += [pltpu.VMEM((FIELD, 128), F32)]
    return pl.pallas_call(
        cycle_kernel,
        out_shape=jax.ShapeDtypeStruct((FIELD + 128, 128), F32),
        in_specs=[VMEM] * 2,
        out_specs=VMEM,
        scratch_shapes=scratch,
        compiler_params=limit(24),
        cost_estimate=pl.CostEstimate(flops=40_000_000, bytes_accessed=30_000_000, transcendentals=0),
        name="cycle",
    )(coefs, assembled)


def early(own, own_start, other_start):
    return pl.pallas_call(
        early_kernel,
        out_shape=[jax.ShapeDtypeStruct((16, 128), F32), jax.ShapeDtypeStruct((192, 160), F32)],
        in_specs=[VMEM] * 3,
        out_specs=[VMEM] * 2,
        scratch_shapes=[pltpu.VMEM((192, 128), F32)],
        compiler_params=limit(16),
        cost_estimate=pl.CostEstimate(flops=4_000_000, bytes_accessed=4_000_000, transcendentals=0),
        name="early",
    )(own, own_start, other_start)


def finish(own, other, own_start, other_start, sums, column, guess):
    return pl.pallas_call(
        finish_kernel,
        out_shape=[
            jax.ShapeDtypeStruct(guess.shape, F32),
            jax.ShapeDtypeStruct(guess.shape, F32),
            jax.ShapeDtypeStruct((3,), F32),
        ],
        in_specs=[VMEM] * 7,
        out_specs=[VMEM, VMEM, pl.BlockSpec(memory_space=pltpu.SMEM)],
        scratch_shapes=[pltpu.VMEM((128, 128), F32), pltpu.VMEM((128, 160), F32)],
        compiler_params=limit(24),
        name="finish",
    )(own, other, own_start, other_start, sums, column, guess)


def exchange(x, axis, bits):
    return lax.ppermute(x, axis, [(n, n ^ bits) for n in range(lax.axis_size(axis))])


def gathered_body(rhs, guess, kappa, bc_flags):
    rhs, guess = (jnp.transpose(v, (1, 2, 0, 3)) for v in (rhs, guess))
    mine, theirs = local_part(rhs, guess, kappa, bc_flags)
    got, mine, kappa_piece = lax.optimization_barrier((exchange(theirs, "section", 1), *part(mine)))
    piece = jnp.concatenate([mine + got, kappa_piece])
    pieces = [piece] + [exchange(piece, "gx", bits) for bits in (1, 2, 3)]
    line = plain_call(line_kernel, "line", LINE, [4 * 64], pieces)
    blocks = [line] + [exchange(line, "gy", bits) for bits in (1, 2, 3)]
    halves = plain_call(halves_kernel, "halves", COLS * 16, [], blocks)
    other_halves = exchange(halves, "section", 1)
    start = plain_call(assemble_kernel, "assemble", 128 * 8, [COLS * HALF, COLS * 32, 50 * 8], blocks, 4_000_000)
    start, other_halves = lax.optimization_barrier((start, other_halves))
    coefs = plain_call(setup_kernel, "setup", REGISTERS * 8, [128 * 8], (start, halves, other_halves))
    other_start = exchange(start, "section", 1)
    own, other_start = lax.optimization_barrier((cycle(coefs, start), other_start))
    sums, column = early(own, start, other_start)
    sol, res, arnoldi = finish(own, exchange(own, "section", 1), start, other_start, sums, column, guess)
    sol, res = (jnp.transpose(v, (2, 0, 1, 3)) for v in (sol, res))
    return sol, res, arnoldi


def solution(mesh):
    placed = (
        P("section", "gx", "gy", None),
        P("section", "gx", "gy", None),
        P("gx", "gy", None),
        P(None, "gx", "gy", None),
    )
    sizes = (mesh.shape["section"], mesh.shape["gx"], mesh.shape["gy"])

    def step(rhs, guess, kappa, bc_flags):
        fits = sizes == (2, 4, 4) and rhs.shape == (4, 20, 20, 160)
        return jax.shard_map(
            gathered_body if fits else stepwise,
            mesh=mesh,
            in_specs=placed,
            out_specs=(P("section", "gx", "gy", None), P("section", "gx", "gy", None), P()),
            check_vma=False,
        )(rhs, guess, kappa, bc_flags)

    return step
```

```python
from functools import partial
import math

import jax
import jax.numpy as jnp
import numpy as np
from jax import lax
from jax.experimental import pallas as pl
from jax.experimental.pallas import tpu as pltpu
from jax.sharding import PartitionSpec as P

ADVECT = (1.0, 0.7, 0.5)
DIFFUSE = 0.05
STEP_SIZE = 0.2
JACOBI_SCALE = 0.25
CHEB_LOW = 0.25
CHEB_HIGH = 2.0
LETTERS = "abcdef"


def extended(x, sides, width):
    for axis, dim in sides:
        peers, length = (lax.axis_size(axis), x.shape[dim])
        up = [(i, (i + 1) % peers) for i in range(peers)]
        down = [(j, i) for i, j in up]
        last = lax.slice_in_dim(x, length - width, length, axis=dim)
        leading = lax.slice_in_dim(x, 0, width, axis=dim)
        before = lax.ppermute(last, axis, up)
        after = lax.ppermute(leading, axis, down)
        x = jnp.concatenate([before, x, after], axis=dim)
    return x


def lobatto(count):
    if count == 5:
        inner = math.sqrt(3.0 / 7.0)
        return (
            np.array([-1.0, -inner, 0.0, inner, 1.0]),
            np.array([0.1, 49.0 / 90.0, 32.0 / 45.0, 49.0 / 90.0, 0.1]),
        )
    if count == 3:
        return (np.array([-1.0, 0.0, 1.0]), np.array([1.0 / 3.0, 4.0 / 3.0, 1.0 / 3.0]))
    return (np.array([-1.0, 1.0]), np.array([1.0, 1.0]))


def lagrange_table(nodes, points):
    table = np.ones((len(points), len(nodes)))
    for column in range(len(nodes)):
        for other in range(len(nodes)):
            if other != column:
                table[:, column] *= (points - nodes[other]) / (nodes[column] - nodes[other])
    return table


def slope_table(nodes):
    total = len(nodes)
    factor = np.array(
        [np.prod([nodes[i] - nodes[k] for k in range(total) if k != i]) for i in range(total)]
    )
    table = np.zeros((total, total))
    for row in range(total):
        for column in range(total):
            if row != column:
                table[row, column] = factor[row] / factor[column] / (nodes[row] - nodes[column])
        table[row, row] = -np.sum(table[row])
    return table


def element_matrix(count, direction):
    nodes, weights = lobatto(count)
    slopes = slope_table(nodes)
    stiffness = (1.0 / weights)[:, None] * (slopes.T @ (weights[:, None] * slopes))
    return ADVECT[direction] * slopes + DIFFUSE * stiffness


def legendre_pair(point, order):
    values = [1.0, point]
    slopes = [0.0, 1.0]
    for index in range(1, order):
        values.append(
            ((2 * index + 1) * point * values[index] - index * values[index - 1]) / (index + 1)
        )
        slopes.append(slopes[index - 1] + (2 * index + 1) * values[index])
    return (values, slopes)


def radau_nodes():
    starts = [0.0885879595127039, 0.4094668644407347, 0.7876594617608471]
    found = []
    for start in starts:
        point = start
        for sweep in range(30):
            values, slopes = legendre_pair(2.0 * point - 1.0, 4)
            change = (values[4] - values[3]) / (2.0 * (slopes[4] - slopes[3]))
            point = point - change
        found.append(point)
    found.append(1.0)
    return found


def poly_times(coefs, root):
    result = [0.0] * (len(coefs) + 1)
    for index in range(len(coefs)):
        result[index + 1] += coefs[index]
        result[index] -= root * coefs[index]
    return result


def radau_matrix():
    order = 4
    nodes = radau_nodes()
    matrix = np.zeros((order, order))
    for column in range(order):
        coefs = [1.0]
        denominator = 1.0
        for other in range(order):
            if other != column:
                coefs = poly_times(coefs, nodes[other])
                denominator *= nodes[column] - nodes[other]
        for row in range(order):
            upper_end = nodes[row]
            integral = 0.0
            for index in range(len(coefs)):
                integral += coefs[index] * upper_end ** (index + 1) / (index + 1)
            matrix[row, column] = integral / denominator
    return matrix


def node_einsum(table, field, axis):
    labels = LETTERS[: field.ndim]
    source = labels[: axis + 1] + "j" + labels[axis + 2 :]
    target = labels[: axis + 1] + "i" + labels[axis + 2 :]
    return jnp.einsum(
        "ij," + source + "->" + target,
        jnp.asarray(table, jnp.float32),
        field,
        precision=lax.Precision.HIGHEST,
    )


def apply_along(field, axis, count, table):
    shape = field.shape
    split = shape[:axis] + (shape[axis] // count, count) + shape[axis + 1 :]
    mapped = node_einsum(table, field.reshape(split), axis)
    return mapped.reshape(
        shape[:axis] + (mapped.shape[axis] * mapped.shape[axis + 1],) + shape[axis + 1 :]
    )


def line_part(field, axis, count, table, left_gain, right_gain, left_edge, right_edge):
    shape = field.shape
    elements = shape[axis] // count
    split = field.reshape(shape[:axis] + (elements, count) + shape[axis + 1 :])
    linear = node_einsum(table, split, axis)
    first = lax.index_in_dim(split, 0, axis + 1, keepdims=False)
    last = lax.index_in_dim(split, count - 1, axis + 1, keepdims=False)
    before = jnp.concatenate(
        [jnp.expand_dims(left_edge, axis), lax.slice_in_dim(last, 0, elements - 1, axis=axis)], axis
    )
    after = jnp.concatenate(
        [lax.slice_in_dim(first, 1, elements, axis=axis), jnp.expand_dims(right_edge, axis)], axis
    )
    front = jnp.expand_dims(left_gain * (first - before), axis + 1)
    back = jnp.expand_dims(right_gain * (last - after), axis + 1)
    if count > 2:
        middle_shape = list(front.shape)
        middle_shape[axis + 1] = count - 2
        pieces = [front, jnp.zeros(middle_shape, jnp.float32), back]
    else:
        pieces = [front, back]
    return (linear + jnp.concatenate(pieces, axis + 1)).reshape(shape)


def diag_along(shape, axis, count, table, left_gain, right_gain):
    elements = shape[axis] // count
    split = shape[:axis] + (elements, count) + shape[axis + 1 :]
    profile = [1] * len(split)
    profile[axis + 1] = count
    diagonal_entries = np.array([table[index, index] for index in range(count)])
    base = jnp.broadcast_to(jnp.asarray(diagonal_entries, jnp.float32).reshape(profile), split)
    front = jnp.expand_dims(left_gain, axis + 1)
    back = jnp.expand_dims(right_gain, axis + 1)
    if count > 2:
        middle_shape = list(front.shape)
        middle_shape[axis + 1] = count - 2
        pieces = [front, jnp.zeros(middle_shape, jnp.float32), back]
    else:
        pieces = [front, back]
    return (base + jnp.concatenate(pieces, axis + 1)).reshape(shape)


def level_kappa(kappa, count):
    if count == 5:
        return kappa
    picks = np.array([0, 2, 4]) if count == 3 else np.array([0, 4])
    extents = [extent // 5 for extent in kappa.shape]
    grouped = kappa.reshape(extents[0], 5, extents[1], 5, extents[2], 5)
    for axis in (1, 3, 5):
        grouped = jnp.take(grouped, picks, axis=axis)
    return grouped.reshape(extents[0] * count, extents[1] * count, extents[2] * count)


def face_plane(face, direction, count):
    plane = face.astype(jnp.float32)
    for axis in range(3):
        if axis != direction:
            plane = jnp.repeat(plane, count, axis=axis)
    return plane


def build_level(kappa, flags, count):
    nodes, weights = lobatto(count)
    kappa_level = level_kappa(kappa, count)
    tables, lefts, rights = ([], [], [])
    diagonal = kappa_level
    for direction in range(3):
        table = element_matrix(count, direction)
        lower = face_plane(flags[2 * direction], direction, count)
        upper = face_plane(flags[2 * direction + 1], direction, count)
        left_gain = (ADVECT[direction] * (1.0 + lower) / 2.0 + DIFFUSE * count * count) / float(
            weights[0]
        )
        right_gain = (DIFFUSE * count * count - ADVECT[direction] * (1.0 - upper) / 2.0) / float(
            weights[-1]
        )
        tables.append(table)
        lefts.append(left_gain)
        rights.append(right_gain)
        diagonal = diagonal + diag_along(
            kappa_level.shape, direction, count, table, left_gain, right_gain
        )
    scale = 1.0 / (1.0 + STEP_SIZE * JACOBI_SCALE * diagonal)
    return (count, tables, lefts, rights, kappa_level, scale)


def restrict(field, fine_count, coarse_count):
    fine_nodes, fine_weights = lobatto(fine_count)
    coarse_nodes, coarse_weights = lobatto(coarse_count)
    table = (
        (1.0 / coarse_weights)[:, None]
        * lagrange_table(coarse_nodes, fine_nodes).T
        * fine_weights[None, :]
    )
    for axis in range(field.ndim - 3, field.ndim):
        field = apply_along(field, axis, fine_count, table)
    return field


def prolong(field, coarse_count, fine_count):
    fine_nodes, fine_weights = lobatto(fine_count)
    coarse_nodes, coarse_weights = lobatto(coarse_count)
    table = lagrange_table(coarse_nodes, fine_nodes)
    for axis in range(field.ndim - 3, field.ndim):
        field = apply_along(field, axis, coarse_count, table)
    return field


def chebyshev(rhs, start, level, operator):
    centre = (CHEB_HIGH + CHEB_LOW) / 2.0
    radius = (CHEB_HIGH - CHEB_LOW) / 2.0
    ratio = centre / radius
    first_rho = 1.0 / ratio
    second_rho = 1.0 / (2.0 * ratio - first_rho)
    scale = level[5]
    if start is None:
        remain = rhs
    else:
        remain = rhs - operator(start, level)
    step = scale * remain / centre
    guess = step if start is None else start + step
    remain = remain - operator(step, level)
    step = second_rho * first_rho * step + 2.0 * second_rho / radius * scale * remain
    return guess + step


def vcycle(rhs, levels, operator):
    fine, middle, coarse = levels
    fine_x = chebyshev(rhs, None, fine, operator)
    middle_rhs = restrict(rhs - operator(fine_x, fine), 5, 3)
    middle_x = chebyshev(middle_rhs, None, middle, operator)
    coarse_rhs = restrict(middle_rhs - operator(middle_x, middle), 3, 2)
    coarse_x = chebyshev(coarse_rhs, None, coarse, operator)
    middle_x = chebyshev(middle_rhs, middle_x + prolong(coarse_x, 2, 3), middle, operator)
    return chebyshev(rhs, fine_x + prolong(middle_x, 3, 5), fine, operator)


def spatial(field, level):
    count, tables, lefts, rights, kappa_level, scale = level
    padded = extended(field, (("gx", 1), ("gy", 2)), 1)
    total = kappa_level * field
    total = total + line_part(
        field,
        1,
        count,
        tables[0],
        lefts[0],
        rights[0],
        padded[:, 0, 1:-1, :],
        padded[:, -1, 1:-1, :],
    )
    total = total + line_part(
        field,
        2,
        count,
        tables[1],
        lefts[1],
        rights[1],
        padded[:, 1:-1, 0, :],
        padded[:, 1:-1, -1, :],
    )
    total = total + line_part(
        field, 3, count, tables[2], lefts[2], rights[2], field[:, :, :, -1], field[:, :, :, 0]
    )
    return total


def apply_system(field, level, coupling):
    image = spatial(field, level)
    everyone = lax.all_gather(image, "section", axis=0, tiled=True)
    butcher = jnp.asarray(radau_matrix(), jnp.float32)
    rows = lax.dynamic_slice_in_dim(
        butcher, lax.axis_index("section") * field.shape[0], field.shape[0], 0
    )
    mixed = jnp.einsum("ij,jabc->iabc", rows, everyone, precision=lax.Precision.HIGHEST)
    return field + STEP_SIZE * mixed


def global_total(values):
    return lax.psum(values, ("section", "gx", "gy"))


def stepwise(rhs, guess, kappa, bc_flags):
    levels = [build_level(kappa, bc_flags, count) for count in (5, 3, 2)]
    section_operator = partial(apply_system, coupling=None)
    start_residual = rhs - section_operator(guess, levels[0])
    dofs = float(rhs.size * lax.axis_size("section") * lax.axis_size("gx") * lax.axis_size("gy"))
    beta = jnp.sqrt(global_total(jnp.sum(start_residual * start_residual).reshape(1))[0])
    basis = start_residual / beta
    precond = vcycle(basis, levels, section_operator)
    image = section_operator(precond, levels[0])
    upper = global_total(jnp.sum(image * basis).reshape(1))[0]
    remainder = image - upper * basis
    lower = jnp.sqrt(global_total(jnp.sum(remainder * remainder).reshape(1))[0])
    weight = beta * upper / (upper * upper + lower * lower)
    solution = guess + weight * precond
    residual = start_residual - weight * image
    arnoldi = jnp.stack([beta / math.sqrt(dofs), upper, lower]).astype(jnp.float32)
    return (solution, residual, arnoldi)


EZ = 32
COLS = 16
HALF = 64
FACE_X = HALF + 25
KAPPA = FACE_X + 15
PIECE = KAPPA + 16
LINE_KAPPA = 4 * HALF
LINE_Y = LINE_KAPPA + 4 * 16
LINE = LINE_Y + 104
FIELD = 1000
F32 = jnp.float32


def split_sections():
    matrix = radau_matrix()
    values, vectors = np.linalg.eig(matrix)
    order = [n for n in np.argsort(np.abs(values.imag), kind="stable") if values[n].imag > 0]
    bases = []
    for n in order:
        plane = np.stack([vectors[:, n].real, vectors[:, n].imag], axis=1)
        bases.append(np.linalg.qr(plane)[0])
    left, cross, right = np.linalg.svd(bases[0].T @ bases[1])
    bases = [bases[0] @ left, bases[1] @ right.T]
    for c in range(2):
        sign = np.sign(bases[0][np.argmax(np.abs(bases[0][:, c])), c])
        bases = [np.concatenate([b[:, :c], sign * b[:, c : c + 1], b[:, c + 1 :]], axis=1) for b in bases]
    whole = np.concatenate(bases, axis=1)
    back = np.linalg.inv(whole)
    return whole, back, back @ matrix, back @ matrix @ whole, cross


def iota(shape, dim):
    return lax.broadcasted_iota(jnp.int32, shape, dim)


def exact_dot(a, b):
    return lax.dot_general(
        a, b, (((1,), (0,)), ((), ())), precision=lax.Precision.HIGHEST, preferred_element_type=F32
    )


def split_dot(a, b):
    high = a.astype(jnp.bfloat16)
    rest = a - high.astype(F32)
    middle = rest.astype(jnp.bfloat16)
    low = (rest - middle.astype(F32)).astype(jnp.bfloat16)
    b = b.astype(jnp.bfloat16)
    return sum(
        lax.dot_general(part, b, (((1,), (0,)), ((), ())), preferred_element_type=F32)
        for part in (low, middle, high)
    )


def choose(index, values):
    out = values[-1]
    for place in range(len(values) - 2, -1, -1):
        out = jnp.where(index == place, values[place], out)
    return out


def face_gains(flag, direction, side, count):
    nodes, weights = lobatto(count)
    c, nu = ADVECT[direction], DIFFUSE * count * count
    if side == 0:
        return (c * (1.0 + flag) / 2.0 + nu) * (1.0 / float(weights[0]))
    return (nu - c * (1.0 - flag) / 2.0) * (1.0 / float(weights[-1]))


def row_table():
    kx, ky = (element_matrix(5, d) for d in range(2))
    rows = np.zeros((64, 64))
    for s in range(2):
        for i in range(5):
            for j in range(5):
                r = s * 32 + i * 5 + j
                for m in range(5):
                    rows[r, s * 32 + m * 5 + j] += kx[i, m]
                    rows[r, s * 32 + i * 5 + m] += ky[j, m]
    return rows.astype(np.float32)


def pick_lines(k):
    lane = iota((160, 256), 1)
    return (iota((160, 256), 0) == 5 * (lane % EZ) + k + lane // 128).astype(F32)


def pair_factors(sec, table, own, s):
    upper = iota((32, 128), 1) < 64
    first = jnp.where(upper, float(table[0, s]), float(table[1, s]))
    second = jnp.where(upper, float(table[2, 2 + s]), float(table[3, 2 + s]))
    if not own:
        first = jnp.where(upper, float(table[2, s]), float(table[3, s]))
        second = jnp.where(upper, float(table[0, 2 + s]), float(table[1, 2 + s]))
    return jnp.where(sec == 0, first, second)


def pack_nodes(nodes):
    half = nodes.shape[0] // 2
    odd = iota((half, 128), 1) // EZ % 2 == 1
    return jnp.where(odd, nodes[half:, :], nodes[:half, :])


def fetch(pairs, sems):
    copies = [pltpu.make_async_copy(src, dst, sems.at[n]) for n, (src, dst) in enumerate(pairs)]
    for copy in copies:
        copy.start()
    for copy in copies:
        copy.wait()


def local_kernel(
    rhs_in, guess_in, kappa_in, flags_in, rows_in, mine, theirs,
    rhs, guess, kappa, flags, rows_t, sems, stack, lines, nodes, y_faces, x_faces,
):
    sec = lax.axis_index("section")
    fetch([(rhs_in, rhs), (guess_in, guess), (kappa_in, kappa), (flags_in, flags), (rows_in, rows_t)], sems)
    stack[...] = jnp.zeros_like(stack)
    for i in range(5):
        stack[192 + 5 * i : 197 + 5 * i, :] = kappa[i]
        for j in range(5):
            r = 5 * i + j
            value = guess[i, j]
            left = rhs[i, j] - value
            for s in range(2):
                stack[s * 32 + r : s * 32 + r + 1, :] = left[s : s + 1]
                stack[128 + s * 32 + r : 128 + s * 32 + r + 1, :] = value[s : s + 1]
    stack[64:128, :] = exact_dot(rows_t[...], stack[128:192, :])
    source = stack[...]
    for k in (0, 2, 4):
        shown = split_dot(source, pick_lines(k))
        lines[224 * k : 224 * k + 224, :] = shown[:, :128]
        if k < 4:
            lines[224 * k + 224 : 224 * k + 448, :] = shown[:, 128:]

    def part(k, first):
        return lines[224 * k + first : 224 * k + first + 32, :]

    repeat = (iota((EZ, 128), 1) % EZ == iota((EZ, 128), 0)).astype(F32)
    shown = split_dot(flags[:, 0, 0, :].astype(F32), repeat)
    gains = [face_gains(shown[d : d + 1, :], d // 2, d % 2, 5) for d in range(6)]
    row = iota((32, 128), 0)
    none = jnp.zeros((32, 128), F32)
    own = jnp.where(row < 5, gains[0], jnp.where((row >= 20) & (row < 25), gains[1], none))
    own = own + jnp.where(row % 5 == 0, gains[2], jnp.where(row % 5 == 4, gains[3], none))
    kz = element_matrix(5, 2)
    back, back_matrix = split_sections()[1:3]
    for ref in (nodes, y_faces, x_faces):
        ref[...] = jnp.zeros_like(ref)
    for k in range(5):
        diagonal = part(k, 192) + own
        if k == 0:
            diagonal = diagonal + gains[4]
        if k == 4:
            diagonal = diagonal + gains[5]
        images = []
        for s in range(2):
            first = 128 + 32 * s
            image = diagonal * part(k, first) + part(k, 64 + 32 * s)
            for m in range(5):
                image = image + float(kz[k, m]) * part(m, first)
            if k == 0:
                image = image - gains[4] * pltpu.roll(part(4, first), 1, 1)
            if k == 4:
                image = image - gains[5] * pltpu.roll(part(0, first), 127, 1)
            images.append(image)
        for p, mark in enumerate((True, False)):
            total = jnp.zeros((32, 128), F32)
            trace = jnp.zeros((32, 128), F32)
            for s in range(2):
                total = total + pair_factors(sec, back, mark, s) * part(k, 32 * s)
                factor = pair_factors(sec, STEP_SIZE * back_matrix, mark, s)
                total = total - factor * images[s]
                trace = trace + factor * part(k, 128 + 32 * s)
            nodes[128 * p + 25 * k : 128 * p + 25 * k + 25, :] = total[:25]
            for i in range(5):
                for f in range(2):
                    r = 64 * p + 32 * f + 5 * k + i
                    y_faces[r : r + 1, :] = trace[5 * i + 4 * f : 5 * i + 4 * f + 1]
            for f in range(2):
                r = 32 * p + 16 * f + 3 * k
                x_faces[r : r + 3, :] = trace[20 * f + 1 : 20 * f + 4]
    upper = iota((1, 128), 1) < 64
    for r in range(3):
        nodes[125 + r : 126 + r, :] = jnp.where(upper, shown[2 * r : 2 * r + 1], shown[2 * r + 1 : 2 * r + 2])
    for p, out in enumerate((mine, theirs)):
        out[:HALF, :] = pack_nodes(nodes[128 * p : 128 * p + 128, :])
        out[HALF:FACE_X, :] = pack_nodes(y_faces[64 * p : 64 * p + 64, :])[:25]
        out[FACE_X:KAPPA, :] = pack_nodes(x_faces[32 * p : 32 * p + 32, :])[:15]
    for k in range(5):
        nodes[25 * k : 25 * k + 25, :] = part(k, 192)[:25]
    kappas = choose(iota((32, 128), 1) // EZ, [nodes[32 * q : 32 * q + 32, :] for q in range(4)])
    mine[KAPPA:, :] = jnp.where(sec == 0, kappas[:16], kappas[16:])


def part_kernel(source, piece, kappa):
    piece[...] = source[:KAPPA, :]
    kappa[...] = source[KAPPA:, :]


VMEM = pl.BlockSpec(memory_space=pltpu.VMEM)
HBM = pl.BlockSpec(memory_space=pltpu.HBM)


def limit(mib):
    return pltpu.CompilerParams(vmem_limit_bytes=mib * 2**20)


def local_part(rhs, guess, kappa, flags):
    operands = (rhs, guess, kappa, flags, jnp.asarray(row_table()))
    return pl.pallas_call(
        local_kernel,
        out_shape=[jax.ShapeDtypeStruct((rows, 128), F32) for rows in (PIECE, KAPPA)],
        in_specs=[HBM] * 5,
        out_specs=[VMEM] * 2,
        scratch_shapes=[pltpu.VMEM(o.shape, o.dtype) for o in operands]
        + [
            pltpu.SemaphoreType.DMA((5,)),
            pltpu.VMEM((224, 160), F32),
            pltpu.VMEM((5 * 224, 128), F32),
            pltpu.VMEM((256, 128), F32),
            pltpu.VMEM((128, 128), F32),
            pltpu.VMEM((64, 128), F32),
        ],
        compiler_params=limit(60),
        cost_estimate=pl.CostEstimate(flops=20_000_000, bytes_accessed=8_000_000, transcendentals=0),
        name="local_part",
    )(*operands)


def part(x):
    return pl.pallas_call(
        part_kernel,
        out_shape=[jax.ShapeDtypeStruct((rows, 128), F32) for rows in (KAPPA, 16)],
        in_specs=[VMEM],
        out_specs=[VMEM] * 2,
        compiler_params=limit(16),
        name="part",
    )(x)


class Level:
    def __init__(self, count, refs):
        self.count = count
        self.x, self.dir, self.res, self.f = refs
        self.tables = [element_matrix(count, d) for d in range(3)]
        self.gains = self.diag = self.jac = None


def tile(index):
    return pl.ds(index * 8, 8)


def rows_of(pieces, size, r, h):
    return pieces[pl.ds(8 * h * size + r, 8, stride=size), :]


def place_pieces(blocks, pieces, first, size, room):
    my_gx, my_gy = lax.axis_index("gx"), lax.axis_index("gy")
    for b, block in enumerate(blocks):
        for a in range(4):
            column = (my_gx ^ a) * 4 + (my_gy ^ b)
            start = pl.multiple_of(column * room, 8)
            pieces[pl.ds(start, size), :] = block[first + a * size : first + a * size + size, :]


class Lanes:
    def __init__(self):
        self.lane = iota((8, 128), 1)
        sub = iota((8, 128), 0)
        self.group = self.lane // EZ
        self.odd = self.group % 2 == 1
        self.element = self.lane % EZ
        self.place = sub % 4
        self.low_half = sub < 4

    def around(self, u):
        turned = pltpu.roll(u, 4, u.ndim - 2)
        far = jnp.where(self.odd, pltpu.roll(turned, 32, u.ndim - 1), pltpu.roll(turned, 96, u.ndim - 1))
        return turned, far

    def x_before(self, u):
        turned, far = self.around(u)
        return jnp.where(self.low_half, far, turned)

    def x_after(self, u):
        turned, far = self.around(u)
        return jnp.where(self.low_half, turned, far)

    def y_before(self, u):
        return jnp.where(self.place == 0, pltpu.roll(u, 5, 0), pltpu.roll(u, 1, 0))

    def y_after(self, u):
        return jnp.where(self.place == 3, pltpu.roll(u, 3, 0), pltpu.roll(u, 7, 0))

    def z_before(self, u):
        return jnp.where(self.element == 0, pltpu.roll(u, 97, u.ndim - 1), pltpu.roll(u, 1, u.ndim - 1))

    def z_after(self, u):
        last = self.element == EZ - 1
        return jnp.where(last, pltpu.roll(u, 31, u.ndim - 1), pltpu.roll(u, 127, u.ndim - 1))


def load(ref, first, count):
    return ref[pl.ds(first * 8, count * 8), :].reshape(count, 8, 128)


def store(ref, first, value):
    ref[pl.ds(first * 8, value.shape[0] * 8), :] = value.reshape(value.shape[0] * 8, 128)


DIAGS = (0, 250, 304)
GAINS = (320, 326, 332)
REGISTERS = 338
CENTRE = (CHEB_HIGH + CHEB_LOW) / 2.0
RADIUS = (CHEB_HIGH - CHEB_LOW) / 2.0


def flag_lanes(row, slot):
    turned = [row] + [pltpu.roll(row, 32 * m, 1) for m in range(1, 4)]
    return choose(iota(row.shape, 1) // EZ, [turned[(g - 2 * slot - 1) % 4] for g in range(4)])


def line_kernel(piece3, piece2, piece1, piece0, line, faces):
    pieces = (piece0, piece1, piece2, piece3)
    even = lax.axis_index("gx") % 2 == 0
    odd = iota((8, 128), 1) // EZ % 2 == 1
    faces[...] = jnp.zeros_like(faces)

    def both(rows, f):
        side = odd[:1] if f else jnp.logical_not(odd[:1])
        return jnp.where(side, rows, pltpu.roll(rows, 96 if f else 32, 1))

    for a, piece in enumerate(pieces):
        for f in range(2):
            base = 64 * a + 32 * f
            inner = both(piece[FACE_X:KAPPA, :], f)
            ends = [both(piece[HALF:FACE_X, :], g) for g in range(2)]
            for k in range(5):
                r = base + 5 * k
                node = 5 * k + 4 * f
                faces[r : r + 1, :] = ends[0][node : node + 1]
                faces[r + 1 : r + 4, :] = inner[3 * k : 3 * k + 3]
                faces[r + 4 : r + 5, :] = ends[1][node : node + 1]
    for a, piece in enumerate(pieces):
        line[HALF * a : HALF * a + HALF, :] = piece[:HALF, :]
        line[LINE_KAPPA + 16 * a : LINE_KAPPA + 16 * a + 16, :] = piece[KAPPA:, :]
        line[LINE_Y + 25 * a : LINE_Y + 25 * a + 25, :] = piece[HALF:FACE_X, :]
        flags = [flag_lanes(piece[61:62, :], slot) for slot in range(2)]
        gains = [face_gains(flags[d], 0, d, 5) for d in range(2)]
        next_first = even if a % 2 == 0 else jnp.logical_not(even)
        for f in range(2):
            one = faces[64 * (a ^ 1) + 32 * (1 - f) : 64 * (a ^ 1) + 32 * (1 - f) + 32, :]
            three = faces[64 * (a ^ 3) + 32 * (1 - f) : 64 * (a ^ 3) + 32 * (1 - f) + 32, :]
            near = jnp.where(next_first, one, three) if f else jnp.where(next_first, three, one)
            term = gains[f] * near
            for k in range(5):
                node = 25 * k + 20 * f
                side = odd[:5] if node >= HALF else jnp.logical_not(odd[:5])
                r = HALF * a + node % HALF
                line[r : r + 5, :] = line[r : r + 5, :] + jnp.where(side, term[5 * k : 5 * k + 5], 0.0)
    line[LINE_Y + 100 :, :] = jnp.zeros((4, 128), F32)


def halves_kernel(block0, block1, block2, block3, out):
    place_pieces((block0, block1, block2, block3), out, LINE_KAPPA, 16, 16)


def widen(low, high, odd):
    return jnp.where(odd, pltpu.roll(high, 32, 1), low), jnp.where(odd, high, pltpu.roll(low, 96, 1))


def assemble_kernel(block0, block1, block2, block3, field, pieces, edges, traces):
    blocks = (block0, block1, block2, block3)
    place_pieces(blocks, pieces, 0, HALF, HALF)
    place_pieces(blocks, edges, LINE_Y, 25, 32)
    lanes = Lanes()
    for source, size, rows, target, apart in ((edges, 32, 25, traces, 25), (pieces, HALF, HALF, field, HALF)):
        for r in range(rows):
            first, second = widen(rows_of(source, size, r, 0), rows_of(source, size, r, 1), lanes.odd)
            target[tile(r), :] = first
            target[tile(apart + r), :] = second
    got = field[tile(126), :]
    across = pltpu.roll(got, 64, 1)
    gains = [
        face_gains(jnp.where(lanes.lane < 64, got, across), 1, 0, 5),
        face_gains(jnp.where(lanes.lane < 64, across, got), 1, 1, 5),
    ]
    for k in range(5):
        for i in range(5):
            lower, upper = traces[tile(5 * k + i), :], traces[tile(25 + 5 * k + i), :]
            node = 25 * k + 5 * i
            field[tile(node), :] = field[tile(node), :] + gains[0] * lanes.y_before(upper)
            field[tile(node + 4), :] = field[tile(node + 4), :] + gains[1] * lanes.y_after(lower)


def setup_kernel(field, own_halves, other_halves, coefs, kap):
    sec = lax.axis_index("section")
    lanes = Lanes()
    group, lane = lanes.group, lanes.lane
    flags = []
    for r in range(3):
        got = field[tile(125 + r), :]
        across = pltpu.roll(got, 64, 1)
        flags += [jnp.where(lane < 64, got, across), jnp.where(lane < 64, across, got)]
    for r in range(16):
        pairs = [[rows_of(ref, 16, r, h) for h in range(2)] for ref in (own_halves, other_halves)]
        for half in range(2):
            turned = []
            for h in range(2):
                got = jnp.where(sec == half, pairs[0][h], pairs[1][h])
                turned.append([pltpu.roll(got, 32 * m, 1) if m else got for m in range(4)])
            for q in range(4):
                value = choose(group, [turned[g % 2][(g - q) % 4] for g in range(4)])
                kap[tile(q * 32 + half * 16 + r), :] = value
    for p, n in enumerate((5, 3, 2)):
        stride = 4 // (n - 1)
        gains = [face_gains(flags[d], d // 2, d % 2, n) for d in range(6)]
        rows = []
        for d in range(3):
            coefs[tile(GAINS[p] + 2 * d), :] = gains[2 * d]
            coefs[tile(GAINS[p] + 2 * d + 1), :] = gains[2 * d + 1]
            table = element_matrix(n, d)
            row = [jnp.full((8, 128), float(table[m, m]), F32) for m in range(n)]
            row[0] = row[0] + gains[2 * d]
            row[n - 1] = row[n - 1] + gains[2 * d + 1]
            rows.append(row)
        along = jnp.stack(rows[1])
        for k in range(n):
            for i in range(n):
                line = load(kap, k * 25 * stride + i * stride * 5, 5)
                line = jnp.stack([line[j * stride] for j in range(n)])
                value = line + (along + (rows[2][k] + rows[0][i]))
                scale = 1.0 / (1.0 + STEP_SIZE * JACOBI_SCALE * value)
                store(coefs, DIAGS[p] + (k * n + i) * n, value)
                store(coefs, DIAGS[p] + n**3 + (k * n + i) * n, scale * (1.0 / CENTRE))


def cycle_kernel(coefs, assembled, fields, *scratch):
    sec = lax.axis_index("section")
    my_gx, my_gy = lax.axis_index("gx"), lax.axis_index("gy")
    levels = [Level(n, scratch[4 * p : 4 * p + 4]) for p, n in enumerate((5, 3, 2))]
    half = scratch[12]
    lanes = Lanes()
    lane = lanes.lane
    blocks = split_sections()[3]

    def lanes_of(upper, lower):
        return jnp.where(lane < 64, jnp.where(sec == 0, upper[0], upper[1]), jnp.where(sec == 0, lower[0], lower[1]))

    entry = [[[float(STEP_SIZE * blocks[2 * p + a, 2 * p + b]) for p in range(2)] for b in range(2)] for a in range(2)]
    same = lanes_of(entry[0][0], entry[1][1])
    swap = lanes_of(entry[0][1], entry[1][0])
    first_rho = RADIUS / CENTRE
    second_rho = 1.0 / (2.0 * CENTRE / RADIUS - first_rho)
    keep = 1.0 + second_rho * first_rho
    push = 2.0 * second_rho / RADIUS * CENTRE
    for p, level in enumerate(levels):
        size = level.count**3
        level.gains = [coefs[tile(GAINS[p] + d), :] for d in range(6)]
        level.diag = lambda first, count, p=p: load(coefs, DIAGS[p] + first, count)
        level.jac = lambda first, count, p=p, size=size: load(coefs, DIAGS[p] + size + first, count)

    def begin(level, source):
        n = level.count
        for first in range(0, n**3, n):
            f = load(source, first, n)
            store(level.dir, first, level.jac(first, n) * f)
            store(level.res, first, f)
            store(level.x, first, jnp.zeros_like(f))

    def apply(level, smooth, always):
        n = level.count
        kx, ky, kz = level.tables
        gains = level.gains
        source = level.dir if smooth else level.x
        def plane(k):
            def line_at(i):
                return load(source, (k * n + i) * n, n)

            for i in range(n):
                first = (k * n + i) * n
                v = line_at(i)
                total = level.diag(first, n) * v
                for m in range(n):
                    if m != i:
                        total = total + float(kx[i, m]) * line_at(m)
                for m in range(n):
                    if m != k:
                        total = total + float(kz[k, m]) * load(source, (m * n + i) * n, n)
                lines = []
                for j in range(n):
                    line = None
                    for m in range(n):
                        if m != j:
                            term = float(ky[j, m]) * v[m]
                            line = term if line is None else line + term
                    if j == 0:
                        line = line - gains[2] * lanes.y_before(v[n - 1])
                    if j == n - 1:
                        line = line - gains[3] * lanes.y_after(v[0])
                    lines.append(line)
                total = total + jnp.stack(lines)
                if i == 0:
                    total = total - gains[0] * lanes.x_before(line_at(n - 1))
                if i == n - 1:
                    total = total - gains[1] * lanes.x_after(line_at(0))
                if k == 0:
                    total = total - gains[4] * lanes.z_before(load(source, ((n - 1) * n + i) * n, n))
                if k == n - 1:
                    total = total - gains[5] * lanes.z_after(load(source, i * n, n))
                image = v + (same * total + swap * pltpu.roll(total, 64, 2))
                if smooth:
                    scaled = level.jac(first, n) * (load(level.res, first, n) - image)
                    store(level.x, first, load(level.x, first, n) + keep * v + push * scaled)
                else:
                    rest = load(level.f, first, n) - image
                    store(level.res, first, rest)
                    store(level.dir, first, level.jac(first, n) * rest)

        for k in range(n):
            @pl.when(always)
            def _(k=k):
                plane(k)

    def combine(weights, parts):
        total = None
        for weight, part in zip(weights, parts):
            if abs(weight) > 1e-14:
                term = part if abs(weight - 1.0) < 1e-14 else float(weight) * part
                total = term if total is None else total + term
        return total

    def change(table, source, target, add):
        m, n = table.shape
        for i in range(n):
            parts = [load(source, i * n + k * n * n, n) for k in range(n)]
            for k in range(m):
                store(half, i * n + k * n * n, combine(table[k], parts))
        for k in range(m):
            parts = [load(half, k * n * n + i * n, n) for i in range(n)]
            for i in range(m):
                line = combine(table[i], parts)
                value = jnp.stack([combine(table[j], [line[a] for a in range(n)]) for j in range(m)])
                first = k * m * m + i * m
                store(target, first, load(target, first, m) + value if add else value)

    def down(n, m):
        fine_nodes, fine_weights = lobatto(n)
        coarse_nodes, coarse_weights = lobatto(m)
        table = lagrange_table(coarse_nodes, fine_nodes)
        return (1.0 / coarse_weights)[:, None] * table.T * fine_weights[None, :]

    def up(m, n):
        return lagrange_table(lobatto(m)[0], lobatto(n)[0])

    def solve(p, always=None):
        level = levels[p]
        if p == 2:
            apply(level, True, always)
            return
        below = levels[p + 1]

        def step(t, carry):
            @pl.when(t != 1)
            def _():
                apply(level, True, t >= 0)

            @pl.when((t != 2) | (p == 0))
            def _():
                apply(level, False, t >= 0)

            @pl.when(t == 0)
            def _():
                n, m = level.count, below.count
                change(down(n, m), level.res, below.f, False)
                begin(below, below.f)
                solve(p + 1, t >= 0)
                change(up(m, n), below.x, level.x, True)
            return carry
        lax.fori_loop(0, 3, step, 0)

    fine = levels[0]
    fine.f = assembled
    begin(fine, assembled)
    solve(0)

    for first in range(0, 125, 5):
        store(fields, first, load(fine.res, first, 5))
    column = (my_gx % 2) * 4 + my_gy
    fields[FIELD : FIELD + 125, :] = fine.x[pl.ds(column, 125, stride=8), :]
    fields[FIELD + 125 : FIELD + 128, :] = jnp.zeros((3, 128), F32)


def pair_weights():
    cross = split_sections()[4]
    return jnp.where(iota((8, 128), 1) < 64, float(cross[0]), float(cross[1]))


def column_factors(p):
    sec = lax.axis_index("section")
    whole = split_sections()[0]
    lane = iota((25, 128), 1)
    here = lane // EZ % 2 == lax.axis_index("gx") // 2
    factors = []
    for s in range(2):
        parts = []
        for mine in range(2):
            t = whole[2 * mine + s]
            q = mine if p == 0 else 1 - mine
            parts.append(jnp.where(lane < 64, float(t[2 * q]), float(t[2 * q + 1])))
        factors.append(jnp.where(here, jnp.where(sec == 0, parts[0], parts[1]), 0.0))
    return factors


def column_rows(k):
    column = (lax.axis_index("gx") % 2) * 4 + lax.axis_index("gy")
    return pl.ds(k * 200 + column, 25, stride=8)


def raw_order(k):
    lane = iota((256, 160), 0)
    return (iota((256, 160), 1) == 5 * (lane % EZ) + k + lane // 128).astype(F32)


def early_kernel(own, own_start, other_start, sums, column_out, cols):
    weights = pair_weights()
    cols[...] = jnp.zeros_like(cols)
    total = jnp.zeros((192, 160), F32)
    own_factors, other_factors = column_factors(0), column_factors(1)
    for k in range(5):
        where = column_rows(k)
        z = own[FIELD + k * 25 : FIELD + k * 25 + 25, :]
        start, other = own_start[where, :], other_start[where, :]
        w = start - own[where, :]
        side = slice(0, 128) if k % 2 == 0 else slice(128, 256)
        for s in range(2):
            cols[s * 32 : s * 32 + 25, side] = own_factors[s] * z
            cols[64 + s * 32 : 64 + s * 32 + 25, side] = own_factors[s] * start + other_factors[s] * other
            cols[128 + s * 32 : 128 + s * 32 + 25, side] = own_factors[s] * w
        if k % 2 == 1:
            total = total + split_dot(cols[...], raw_order(k - 1))
    cols[:, 128:] = jnp.zeros((192, 128), F32)
    total = total + split_dot(cols[...], raw_order(4))
    column_out[...] = total
    nothing = jnp.zeros((8, 128), F32)
    uppers, sizes = [nothing] * 5, [nothing] * 5
    for r in range(125):
        c, d = own_start[tile(r), :], other_start[tile(r), :]
        a = c - own[tile(r), :]
        uppers[r % 5] = uppers[r % 5] + a * (c + weights * d)
        sizes[r % 5] = sizes[r % 5] + ((c * c + d * d) + 2.0 * (weights * (c * d)))
    sums[0:8, :] = sum(uppers)
    sums[8:16, :] = sum(sizes)


def finish_kernel(own, other, own_start, other_start, sums, column, guess, sol, res_out, arnoldi, cols, outs):
    sec = lax.axis_index("section")
    weights = pair_weights()
    cols[...] = jnp.zeros_like(cols)
    total = jnp.zeros((128, 160), F32)
    factors = column_factors(1)
    for k in range(5):
        where = column_rows(k)
        z = other[FIELD + k * 25 : FIELD + k * 25 + 25, :]
        w = other_start[where, :] - other[where, :]
        side = slice(0, 128) if k % 2 == 0 else slice(128, 256)
        for s in range(2):
            cols[s * 32 : s * 32 + 25, side] = factors[s] * z
            cols[64 + s * 32 : 64 + s * 32 + 25, side] = factors[s] * w
        if k % 2 == 1:
            total = total + split_dot(cols[...], raw_order(k - 1))
    cols[:, 128:] = jnp.zeros((128, 128), F32)
    total = total + split_dot(cols[...], raw_order(4))
    nothing = jnp.zeros((8, 128), F32)
    uppers = [nothing] * 5
    for r in range(125):
        c, d = own_start[tile(r), :], other_start[tile(r), :]
        b = d - other[tile(r), :]
        uppers[r % 5] = uppers[r % 5] + b * (d + weights * c)

    mine, theirs = sums[0:8, :], sum(uppers)
    size = jnp.sum(sums[8:16, :], keepdims=True)
    upper = jnp.sum(mine + theirs, keepdims=True) / size
    rests = [nothing] * 5
    for r in range(125):
        c, d = own_start[tile(r), :], other_start[tile(r), :]
        a = (c - own[tile(r), :]) - upper * c
        b = (d - other[tile(r), :]) - upper * d
        rests[r % 5] = rests[r % 5] + ((a * a + b * b) + 2.0 * (weights * (a * b)))
    rest = jnp.sum(sum(rests), keepdims=True)
    beta = jnp.sqrt(size)
    lower = jnp.sqrt(rest) / beta
    weight = upper / (upper * upper + lower * lower)
    entries = float(125 * EZ * COLS * 4)
    for place_out, value in enumerate((beta * (1.0 / math.sqrt(entries)), upper, lower)):
        arnoldi[place_out] = value[0, 0]
    outs[:64, :] = weight * (column[:64, :] + total[:64])
    outs[64:, :] = column[64:128, :] - weight * (column[128:, :] + total[64:])
    for i in range(5):
        for j in range(5):
            r = 5 * i + j
            for s in range(2):
                sol[i, j, s : s + 1, :] = guess[i, j, s : s + 1, :] + outs[s * 32 + r : s * 32 + r + 1, :]
                res_out[i, j, s : s + 1, :] = outs[64 + s * 32 + r : 64 + s * 32 + r + 1, :]


def plain_call(kernel, name, rows, scratch, operands, cost=1_000_000):
    return pl.pallas_call(
        kernel,
        out_shape=jax.ShapeDtypeStruct((rows, 128), F32),
        in_specs=[VMEM] * len(operands),
        out_specs=VMEM,
        scratch_shapes=[pltpu.VMEM((r, 128), F32) for r in scratch],
        compiler_params=limit(16),
        cost_estimate=pl.CostEstimate(flops=cost, bytes_accessed=cost, transcendentals=0),
        name=name,
    )(*operands)


def cycle(coefs, assembled):
    scratch = []
    for n in (5, 3, 2):
        scratch += [pltpu.VMEM((n**3 * 8, 128), F32)] * 4
    scratch += [pltpu.VMEM((FIELD, 128), F32)]
    return pl.pallas_call(
        cycle_kernel,
        out_shape=jax.ShapeDtypeStruct((FIELD + 128, 128), F32),
        in_specs=[VMEM] * 2,
        out_specs=VMEM,
        scratch_shapes=scratch,
        compiler_params=limit(24),
        cost_estimate=pl.CostEstimate(flops=40_000_000, bytes_accessed=30_000_000, transcendentals=0),
        name="cycle",
    )(coefs, assembled)


def early(own, own_start, other_start):
    return pl.pallas_call(
        early_kernel,
        out_shape=[jax.ShapeDtypeStruct((16, 128), F32), jax.ShapeDtypeStruct((192, 160), F32)],
        in_specs=[VMEM] * 3,
        out_specs=[VMEM] * 2,
        scratch_shapes=[pltpu.VMEM((192, 256), F32)],
        compiler_params=limit(16),
        cost_estimate=pl.CostEstimate(flops=4_000_000, bytes_accessed=4_000_000, transcendentals=0),
        name="early",
    )(own, own_start, other_start)


def finish(own, other, own_start, other_start, sums, column, guess):
    return pl.pallas_call(
        finish_kernel,
        out_shape=[
            jax.ShapeDtypeStruct(guess.shape, F32),
            jax.ShapeDtypeStruct(guess.shape, F32),
            jax.ShapeDtypeStruct((3,), F32),
        ],
        in_specs=[VMEM] * 7,
        out_specs=[VMEM, VMEM, pl.BlockSpec(memory_space=pltpu.SMEM)],
        scratch_shapes=[pltpu.VMEM((128, 256), F32), pltpu.VMEM((128, 160), F32)],
        compiler_params=limit(24),
        name="finish",
    )(own, other, own_start, other_start, sums, column, guess)


def exchange(x, axis, bits):
    return lax.ppermute(x, axis, [(n, n ^ bits) for n in range(lax.axis_size(axis))])


def gathered_body(rhs, guess, kappa, bc_flags):
    rhs, guess = (jnp.transpose(v, (1, 2, 0, 3)) for v in (rhs, guess))
    mine, theirs = local_part(rhs, guess, kappa, bc_flags)
    got, mine, kappa_piece = lax.optimization_barrier((exchange(theirs, "section", 1), *part(mine)))
    piece = jnp.concatenate([mine + got, kappa_piece])
    pieces = [piece] + [exchange(piece, "gx", bits) for bits in (1, 2, 3)]
    line = plain_call(line_kernel, "line", LINE, [4 * 64], pieces[::-1])
    blocks = [line] + [exchange(line, "gy", bits) for bits in (1, 2, 3)]
    halves = plain_call(halves_kernel, "halves", COLS * 16, [], blocks)
    other_halves = exchange(halves, "section", 1)
    start = plain_call(assemble_kernel, "assemble", 128 * 8, [COLS * HALF, COLS * 32, 50 * 8], blocks, 4_000_000)
    start, other_halves = lax.optimization_barrier((start, other_halves))
    coefs = plain_call(setup_kernel, "setup", REGISTERS * 8, [128 * 8], (start, halves, other_halves))
    other_start = exchange(start, "section", 1)
    own, other_start = lax.optimization_barrier((cycle(coefs, start), other_start))
    sums, column = early(own, start, other_start)
    sol, res, arnoldi = finish(own, exchange(own, "section", 1), start, other_start, sums, column, guess)
    sol, res = (jnp.transpose(v, (2, 0, 1, 3)) for v in (sol, res))
    return sol, res, arnoldi


def solution(mesh):
    placed = (
        P("section", "gx", "gy", None),
        P("section", "gx", "gy", None),
        P("gx", "gy", None),
        P(None, "gx", "gy", None),
    )
    sizes = (mesh.shape["section"], mesh.shape["gx"], mesh.shape["gy"])

    def step(rhs, guess, kappa, bc_flags):
        fits = sizes == (2, 4, 4) and rhs.shape == (4, 20, 20, 160)
        return jax.shard_map(
            gathered_body if fits else stepwise,
            mesh=mesh,
            in_specs=placed,
            out_specs=(P("section", "gx", "gy", None), P("section", "gx", "gy", None), P()),
            check_vma=False,
        )(rhs, guess, kappa, bc_flags)

    return step
```

```python
from functools import partial
import math

import jax
import jax.numpy as jnp
import numpy as np
from jax import lax
from jax.experimental import pallas as pl
from jax.experimental.pallas import tpu as pltpu
from jax.sharding import PartitionSpec as P

ADVECT = (1.0, 0.7, 0.5)
DIFFUSE = 0.05
STEP_SIZE = 0.2
JACOBI_SCALE = 0.25
CHEB_LOW = 0.25
CHEB_HIGH = 2.0
LETTERS = "abcdef"


def extended(x, sides, width):
    for axis, dim in sides:
        peers, length = (lax.axis_size(axis), x.shape[dim])
        up = [(i, (i + 1) % peers) for i in range(peers)]
        down = [(j, i) for i, j in up]
        last = lax.slice_in_dim(x, length - width, length, axis=dim)
        leading = lax.slice_in_dim(x, 0, width, axis=dim)
        before = lax.ppermute(last, axis, up)
        after = lax.ppermute(leading, axis, down)
        x = jnp.concatenate([before, x, after], axis=dim)
    return x


def lobatto(count):
    if count == 5:
        inner = math.sqrt(3.0 / 7.0)
        return (
            np.array([-1.0, -inner, 0.0, inner, 1.0]),
            np.array([0.1, 49.0 / 90.0, 32.0 / 45.0, 49.0 / 90.0, 0.1]),
        )
    if count == 3:
        return (np.array([-1.0, 0.0, 1.0]), np.array([1.0 / 3.0, 4.0 / 3.0, 1.0 / 3.0]))
    return (np.array([-1.0, 1.0]), np.array([1.0, 1.0]))


def lagrange_table(nodes, points):
    table = np.ones((len(points), len(nodes)))
    for column in range(len(nodes)):
        for other in range(len(nodes)):
            if other != column:
                table[:, column] *= (points - nodes[other]) / (nodes[column] - nodes[other])
    return table


def slope_table(nodes):
    total = len(nodes)
    factor = np.array(
        [np.prod([nodes[i] - nodes[k] for k in range(total) if k != i]) for i in range(total)]
    )
    table = np.zeros((total, total))
    for row in range(total):
        for column in range(total):
            if row != column:
                table[row, column] = factor[row] / factor[column] / (nodes[row] - nodes[column])
        table[row, row] = -np.sum(table[row])
    return table


def element_matrix(count, direction):
    nodes, weights = lobatto(count)
    slopes = slope_table(nodes)
    stiffness = (1.0 / weights)[:, None] * (slopes.T @ (weights[:, None] * slopes))
    return ADVECT[direction] * slopes + DIFFUSE * stiffness


def legendre_pair(point, order):
    values = [1.0, point]
    slopes = [0.0, 1.0]
    for index in range(1, order):
        values.append(
            ((2 * index + 1) * point * values[index] - index * values[index - 1]) / (index + 1)
        )
        slopes.append(slopes[index - 1] + (2 * index + 1) * values[index])
    return (values, slopes)


def radau_nodes():
    starts = [0.0885879595127039, 0.4094668644407347, 0.7876594617608471]
    found = []
    for start in starts:
        point = start
        for sweep in range(30):
            values, slopes = legendre_pair(2.0 * point - 1.0, 4)
            change = (values[4] - values[3]) / (2.0 * (slopes[4] - slopes[3]))
            point = point - change
        found.append(point)
    found.append(1.0)
    return found


def poly_times(coefs, root):
    result = [0.0] * (len(coefs) + 1)
    for index in range(len(coefs)):
        result[index + 1] += coefs[index]
        result[index] -= root * coefs[index]
    return result


def radau_matrix():
    order = 4
    nodes = radau_nodes()
    matrix = np.zeros((order, order))
    for column in range(order):
        coefs = [1.0]
        denominator = 1.0
        for other in range(order):
            if other != column:
                coefs = poly_times(coefs, nodes[other])
                denominator *= nodes[column] - nodes[other]
        for row in range(order):
            upper_end = nodes[row]
            integral = 0.0
            for index in range(len(coefs)):
                integral += coefs[index] * upper_end ** (index + 1) / (index + 1)
            matrix[row, column] = integral / denominator
    return matrix


def node_einsum(table, field, axis):
    labels = LETTERS[: field.ndim]
    source = labels[: axis + 1] + "j" + labels[axis + 2 :]
    target = labels[: axis + 1] + "i" + labels[axis + 2 :]
    return jnp.einsum(
        "ij," + source + "->" + target,
        jnp.asarray(table, jnp.float32),
        field,
        precision=lax.Precision.HIGHEST,
    )


def apply_along(field, axis, count, table):
    shape = field.shape
    split = shape[:axis] + (shape[axis] // count, count) + shape[axis + 1 :]
    mapped = node_einsum(table, field.reshape(split), axis)
    return mapped.reshape(
        shape[:axis] + (mapped.shape[axis] * mapped.shape[axis + 1],) + shape[axis + 1 :]
    )


def line_part(field, axis, count, table, left_gain, right_gain, left_edge, right_edge):
    shape = field.shape
    elements = shape[axis] // count
    split = field.reshape(shape[:axis] + (elements, count) + shape[axis + 1 :])
    linear = node_einsum(table, split, axis)
    first = lax.index_in_dim(split, 0, axis + 1, keepdims=False)
    last = lax.index_in_dim(split, count - 1, axis + 1, keepdims=False)
    before = jnp.concatenate(
        [jnp.expand_dims(left_edge, axis), lax.slice_in_dim(last, 0, elements - 1, axis=axis)], axis
    )
    after = jnp.concatenate(
        [lax.slice_in_dim(first, 1, elements, axis=axis), jnp.expand_dims(right_edge, axis)], axis
    )
    front = jnp.expand_dims(left_gain * (first - before), axis + 1)
    back = jnp.expand_dims(right_gain * (last - after), axis + 1)
    if count > 2:
        middle_shape = list(front.shape)
        middle_shape[axis + 1] = count - 2
        pieces = [front, jnp.zeros(middle_shape, jnp.float32), back]
    else:
        pieces = [front, back]
    return (linear + jnp.concatenate(pieces, axis + 1)).reshape(shape)


def diag_along(shape, axis, count, table, left_gain, right_gain):
    elements = shape[axis] // count
    split = shape[:axis] + (elements, count) + shape[axis + 1 :]
    profile = [1] * len(split)
    profile[axis + 1] = count
    diagonal_entries = np.array([table[index, index] for index in range(count)])
    base = jnp.broadcast_to(jnp.asarray(diagonal_entries, jnp.float32).reshape(profile), split)
    front = jnp.expand_dims(left_gain, axis + 1)
    back = jnp.expand_dims(right_gain, axis + 1)
    if count > 2:
        middle_shape = list(front.shape)
        middle_shape[axis + 1] = count - 2
        pieces = [front, jnp.zeros(middle_shape, jnp.float32), back]
    else:
        pieces = [front, back]
    return (base + jnp.concatenate(pieces, axis + 1)).reshape(shape)


def level_kappa(kappa, count):
    if count == 5:
        return kappa
    picks = np.array([0, 2, 4]) if count == 3 else np.array([0, 4])
    extents = [extent // 5 for extent in kappa.shape]
    grouped = kappa.reshape(extents[0], 5, extents[1], 5, extents[2], 5)
    for axis in (1, 3, 5):
        grouped = jnp.take(grouped, picks, axis=axis)
    return grouped.reshape(extents[0] * count, extents[1] * count, extents[2] * count)


def face_plane(face, direction, count):
    plane = face.astype(jnp.float32)
    for axis in range(3):
        if axis != direction:
            plane = jnp.repeat(plane, count, axis=axis)
    return plane


def build_level(kappa, flags, count):
    nodes, weights = lobatto(count)
    kappa_level = level_kappa(kappa, count)
    tables, lefts, rights = ([], [], [])
    diagonal = kappa_level
    for direction in range(3):
        table = element_matrix(count, direction)
        lower = face_plane(flags[2 * direction], direction, count)
        upper = face_plane(flags[2 * direction + 1], direction, count)
        left_gain = (ADVECT[direction] * (1.0 + lower) / 2.0 + DIFFUSE * count * count) / float(
            weights[0]
        )
        right_gain = (DIFFUSE * count * count - ADVECT[direction] * (1.0 - upper) / 2.0) / float(
            weights[-1]
        )
        tables.append(table)
        lefts.append(left_gain)
        rights.append(right_gain)
        diagonal = diagonal + diag_along(
            kappa_level.shape, direction, count, table, left_gain, right_gain
        )
    scale = 1.0 / (1.0 + STEP_SIZE * JACOBI_SCALE * diagonal)
    return (count, tables, lefts, rights, kappa_level, scale)


def restrict(field, fine_count, coarse_count):
    fine_nodes, fine_weights = lobatto(fine_count)
    coarse_nodes, coarse_weights = lobatto(coarse_count)
    table = (
        (1.0 / coarse_weights)[:, None]
        * lagrange_table(coarse_nodes, fine_nodes).T
        * fine_weights[None, :]
    )
    for axis in range(field.ndim - 3, field.ndim):
        field = apply_along(field, axis, fine_count, table)
    return field


def prolong(field, coarse_count, fine_count):
    fine_nodes, fine_weights = lobatto(fine_count)
    coarse_nodes, coarse_weights = lobatto(coarse_count)
    table = lagrange_table(coarse_nodes, fine_nodes)
    for axis in range(field.ndim - 3, field.ndim):
        field = apply_along(field, axis, coarse_count, table)
    return field


def chebyshev(rhs, start, level, operator):
    centre = (CHEB_HIGH + CHEB_LOW) / 2.0
    radius = (CHEB_HIGH - CHEB_LOW) / 2.0
    ratio = centre / radius
    first_rho = 1.0 / ratio
    second_rho = 1.0 / (2.0 * ratio - first_rho)
    scale = level[5]
    if start is None:
        remain = rhs
    else:
        remain = rhs - operator(start, level)
    step = scale * remain / centre
    guess = step if start is None else start + step
    remain = remain - operator(step, level)
    step = second_rho * first_rho * step + 2.0 * second_rho / radius * scale * remain
    return guess + step


def vcycle(rhs, levels, operator):
    fine, middle, coarse = levels
    fine_x = chebyshev(rhs, None, fine, operator)
    middle_rhs = restrict(rhs - operator(fine_x, fine), 5, 3)
    middle_x = chebyshev(middle_rhs, None, middle, operator)
    coarse_rhs = restrict(middle_rhs - operator(middle_x, middle), 3, 2)
    coarse_x = chebyshev(coarse_rhs, None, coarse, operator)
    middle_x = chebyshev(middle_rhs, middle_x + prolong(coarse_x, 2, 3), middle, operator)
    return chebyshev(rhs, fine_x + prolong(middle_x, 3, 5), fine, operator)


def spatial(field, level):
    count, tables, lefts, rights, kappa_level, scale = level
    padded = extended(field, (("gx", 1), ("gy", 2)), 1)
    total = kappa_level * field
    total = total + line_part(
        field,
        1,
        count,
        tables[0],
        lefts[0],
        rights[0],
        padded[:, 0, 1:-1, :],
        padded[:, -1, 1:-1, :],
    )
    total = total + line_part(
        field,
        2,
        count,
        tables[1],
        lefts[1],
        rights[1],
        padded[:, 1:-1, 0, :],
        padded[:, 1:-1, -1, :],
    )
    total = total + line_part(
        field, 3, count, tables[2], lefts[2], rights[2], field[:, :, :, -1], field[:, :, :, 0]
    )
    return total


def apply_system(field, level, coupling):
    image = spatial(field, level)
    everyone = lax.all_gather(image, "section", axis=0, tiled=True)
    butcher = jnp.asarray(radau_matrix(), jnp.float32)
    rows = lax.dynamic_slice_in_dim(
        butcher, lax.axis_index("section") * field.shape[0], field.shape[0], 0
    )
    mixed = jnp.einsum("ij,jabc->iabc", rows, everyone, precision=lax.Precision.HIGHEST)
    return field + STEP_SIZE * mixed


def global_total(values):
    return lax.psum(values, ("section", "gx", "gy"))


def stepwise(rhs, guess, kappa, bc_flags):
    levels = [build_level(kappa, bc_flags, count) for count in (5, 3, 2)]
    section_operator = partial(apply_system, coupling=None)
    start_residual = rhs - section_operator(guess, levels[0])
    dofs = float(rhs.size * lax.axis_size("section") * lax.axis_size("gx") * lax.axis_size("gy"))
    beta = jnp.sqrt(global_total(jnp.sum(start_residual * start_residual).reshape(1))[0])
    basis = start_residual / beta
    precond = vcycle(basis, levels, section_operator)
    image = section_operator(precond, levels[0])
    upper = global_total(jnp.sum(image * basis).reshape(1))[0]
    remainder = image - upper * basis
    lower = jnp.sqrt(global_total(jnp.sum(remainder * remainder).reshape(1))[0])
    weight = beta * upper / (upper * upper + lower * lower)
    solution = guess + weight * precond
    residual = start_residual - weight * image
    arnoldi = jnp.stack([beta / math.sqrt(dofs), upper, lower]).astype(jnp.float32)
    return (solution, residual, arnoldi)


EZ = 32
COLS = 16
HALF = 64
FACE_X = HALF + 25
KAPPA = FACE_X + 15
PIECE = KAPPA + 16
LINE_KAPPA = 4 * HALF
LINE_Y = LINE_KAPPA + 4 * 16
LINE = LINE_Y + 104
FIELD = 1000
F32 = jnp.float32


def split_sections():
    matrix = radau_matrix()
    values, vectors = np.linalg.eig(matrix)
    order = [n for n in np.argsort(np.abs(values.imag), kind="stable") if values[n].imag > 0]
    bases = []
    for n in order:
        plane = np.stack([vectors[:, n].real, vectors[:, n].imag], axis=1)
        bases.append(np.linalg.qr(plane)[0])
    left, cross, right = np.linalg.svd(bases[0].T @ bases[1])
    bases = [bases[0] @ left, bases[1] @ right.T]
    for c in range(2):
        sign = np.sign(bases[0][np.argmax(np.abs(bases[0][:, c])), c])
        bases = [np.concatenate([b[:, :c], sign * b[:, c : c + 1], b[:, c + 1 :]], axis=1) for b in bases]
    whole = np.concatenate(bases, axis=1)
    back = np.linalg.inv(whole)
    return whole, back, back @ matrix, back @ matrix @ whole, cross


def iota(shape, dim):
    return lax.broadcasted_iota(jnp.int32, shape, dim)


def exact_dot(a, b):
    return lax.dot_general(
        a, b, (((1,), (0,)), ((), ())), precision=lax.Precision.HIGHEST, preferred_element_type=F32
    )


def split_dot(a, b):
    high = a.astype(jnp.bfloat16)
    rest = a - high.astype(F32)
    middle = rest.astype(jnp.bfloat16)
    low = (rest - middle.astype(F32)).astype(jnp.bfloat16)
    b = b.astype(jnp.bfloat16)
    return sum(
        lax.dot_general(part, b, (((1,), (0,)), ((), ())), preferred_element_type=F32)
        for part in (low, middle, high)
    )


def choose(index, values):
    out = values[-1]
    for place in range(len(values) - 2, -1, -1):
        out = jnp.where(index == place, values[place], out)
    return out


def face_gains(flag, direction, side, count):
    nodes, weights = lobatto(count)
    c, nu = ADVECT[direction], DIFFUSE * count * count
    if side == 0:
        return (c * (1.0 + flag) / 2.0 + nu) * (1.0 / float(weights[0]))
    return (nu - c * (1.0 - flag) / 2.0) * (1.0 / float(weights[-1]))


def row_table():
    kx, ky = (element_matrix(5, d) for d in range(2))
    rows = np.zeros((64, 64))
    for s in range(2):
        for i in range(5):
            for j in range(5):
                r = s * 32 + i * 5 + j
                for m in range(5):
                    rows[r, s * 32 + m * 5 + j] += kx[i, m]
                    rows[r, s * 32 + i * 5 + m] += ky[j, m]
    return rows.astype(np.float32)


def pick_lines(k):
    lane = iota((160, 256), 1)
    return (iota((160, 256), 0) == 5 * (lane % EZ) + k + lane // 128).astype(F32)


def pair_factors(sec, table, own, s):
    upper = iota((32, 128), 1) < 64
    first = jnp.where(upper, float(table[0, s]), float(table[1, s]))
    second = jnp.where(upper, float(table[2, 2 + s]), float(table[3, 2 + s]))
    if not own:
        first = jnp.where(upper, float(table[2, s]), float(table[3, s]))
        second = jnp.where(upper, float(table[0, 2 + s]), float(table[1, 2 + s]))
    return jnp.where(sec == 0, first, second)


def pack_nodes(nodes):
    half = nodes.shape[0] // 2
    odd = iota((half, 128), 1) // EZ % 2 == 1
    return jnp.where(odd, nodes[half:, :], nodes[:half, :])


def fetch(pairs, sems):
    copies = [pltpu.make_async_copy(src, dst, sems.at[n]) for n, (src, dst) in enumerate(pairs)]
    for copy in copies:
        copy.start()
    for copy in copies:
        copy.wait()


def local_kernel(
    rhs_in, guess_in, kappa_in, flags_in, rows_in, mine, theirs,
    rhs, guess, kappa, flags, rows_t, sems, stack, lines, nodes, y_faces, x_faces,
):
    sec = lax.axis_index("section")
    fetch([(rhs_in, rhs), (guess_in, guess), (kappa_in, kappa), (flags_in, flags), (rows_in, rows_t)], sems)
    stack[...] = jnp.zeros_like(stack)
    for i in range(5):
        stack[192 + 5 * i : 197 + 5 * i, :] = kappa[i]
        for j in range(5):
            r = 5 * i + j
            value = guess[i, j]
            left = rhs[i, j] - value
            for s in range(2):
                stack[s * 32 + r : s * 32 + r + 1, :] = left[s : s + 1]
                stack[128 + s * 32 + r : 128 + s * 32 + r + 1, :] = value[s : s + 1]
    stack[64:128, :] = exact_dot(rows_t[...], stack[128:192, :])
    source = stack[...]
    for k in (0, 2, 4):
        shown = split_dot(source, pick_lines(k))
        lines[224 * k : 224 * k + 224, :] = shown[:, :128]
        if k < 4:
            lines[224 * k + 224 : 224 * k + 448, :] = shown[:, 128:]

    def part(k, first):
        return lines[224 * k + first : 224 * k + first + 32, :]

    repeat = (iota((EZ, 128), 1) % EZ == iota((EZ, 128), 0)).astype(F32)
    shown = split_dot(flags[:, 0, 0, :].astype(F32), repeat)
    gains = [face_gains(shown[d : d + 1, :], d // 2, d % 2, 5) for d in range(6)]
    row = iota((32, 128), 0)
    none = jnp.zeros((32, 128), F32)
    own = jnp.where(row < 5, gains[0], jnp.where((row >= 20) & (row < 25), gains[1], none))
    own = own + jnp.where(row % 5 == 0, gains[2], jnp.where(row % 5 == 4, gains[3], none))
    kz = element_matrix(5, 2)
    back, back_matrix = split_sections()[1:3]
    for ref in (nodes, y_faces, x_faces):
        ref[...] = jnp.zeros_like(ref)
    for k in range(5):
        diagonal = part(k, 192) + own
        if k == 0:
            diagonal = diagonal + gains[4]
        if k == 4:
            diagonal = diagonal + gains[5]
        images = []
        for s in range(2):
            first = 128 + 32 * s
            image = diagonal * part(k, first) + part(k, 64 + 32 * s)
            for m in range(5):
                image = image + float(kz[k, m]) * part(m, first)
            if k == 0:
                image = image - gains[4] * pltpu.roll(part(4, first), 1, 1)
            if k == 4:
                image = image - gains[5] * pltpu.roll(part(0, first), 127, 1)
            images.append(image)
        for p, mark in enumerate((True, False)):
            total = jnp.zeros((32, 128), F32)
            trace = jnp.zeros((32, 128), F32)
            for s in range(2):
                total = total + pair_factors(sec, back, mark, s) * part(k, 32 * s)
                factor = pair_factors(sec, STEP_SIZE * back_matrix, mark, s)
                total = total - factor * images[s]
                trace = trace + factor * part(k, 128 + 32 * s)
            nodes[128 * p + 25 * k : 128 * p + 25 * k + 25, :] = total[:25]
            for i in range(5):
                for f in range(2):
                    r = 64 * p + 32 * f + 5 * k + i
                    y_faces[r : r + 1, :] = trace[5 * i + 4 * f : 5 * i + 4 * f + 1]
            for f in range(2):
                r = 32 * p + 16 * f + 3 * k
                x_faces[r : r + 3, :] = trace[20 * f + 1 : 20 * f + 4]
    upper = iota((1, 128), 1) < 64
    for r in range(3):
        nodes[125 + r : 126 + r, :] = jnp.where(upper, shown[2 * r : 2 * r + 1], shown[2 * r + 1 : 2 * r + 2])
    for p, out in enumerate((mine, theirs)):
        out[:HALF, :] = pack_nodes(nodes[128 * p : 128 * p + 128, :])
        out[HALF:FACE_X, :] = pack_nodes(y_faces[64 * p : 64 * p + 64, :])[:25]
        out[FACE_X:KAPPA, :] = pack_nodes(x_faces[32 * p : 32 * p + 32, :])[:15]
    for k in range(5):
        nodes[25 * k : 25 * k + 25, :] = part(k, 192)[:25]
    kappas = choose(iota((32, 128), 1) // EZ, [nodes[32 * q : 32 * q + 32, :] for q in range(4)])
    mine[KAPPA:, :] = jnp.where(sec == 0, kappas[:16], kappas[16:])


def part_kernel(source, piece, kappa):
    piece[...] = source[:KAPPA, :]
    kappa[...] = source[KAPPA:, :]


VMEM = pl.BlockSpec(memory_space=pltpu.VMEM)
HBM = pl.BlockSpec(memory_space=pltpu.HBM)


def limit(mib):
    return pltpu.CompilerParams(vmem_limit_bytes=mib * 2**20)


def local_part(rhs, guess, kappa, flags):
    operands = (rhs, guess, kappa, flags, jnp.asarray(row_table()))
    return pl.pallas_call(
        local_kernel,
        out_shape=[jax.ShapeDtypeStruct((rows, 128), F32) for rows in (PIECE, KAPPA)],
        in_specs=[HBM] * 5,
        out_specs=[VMEM] * 2,
        scratch_shapes=[pltpu.VMEM(o.shape, o.dtype) for o in operands]
        + [
            pltpu.SemaphoreType.DMA((5,)),
            pltpu.VMEM((224, 160), F32),
            pltpu.VMEM((5 * 224, 128), F32),
            pltpu.VMEM((256, 128), F32),
            pltpu.VMEM((128, 128), F32),
            pltpu.VMEM((64, 128), F32),
        ],
        compiler_params=limit(60),
        cost_estimate=pl.CostEstimate(flops=20_000_000, bytes_accessed=8_000_000, transcendentals=0),
        name="local_part",
    )(*operands)


def part(x):
    return pl.pallas_call(
        part_kernel,
        out_shape=[jax.ShapeDtypeStruct((rows, 128), F32) for rows in (KAPPA, 16)],
        in_specs=[VMEM],
        out_specs=[VMEM] * 2,
        compiler_params=limit(16),
        name="part",
    )(x)


class Level:
    def __init__(self, count, refs):
        self.count = count
        self.x, self.dir, self.res, self.f = refs
        self.tables = [element_matrix(count, d) for d in range(3)]
        self.gains = self.diag = self.jac = None


def tile(index):
    return pl.ds(index * 8, 8)


def rows_of(pieces, size, r, h):
    return pieces[pl.ds(8 * h * size + r, 8, stride=size), :]


def place_pieces(blocks, pieces, first, size, room):
    my_gx, my_gy = lax.axis_index("gx"), lax.axis_index("gy")
    for b, block in enumerate(blocks):
        for a in range(4):
            column = (my_gx ^ a) * 4 + (my_gy ^ b)
            start = pl.multiple_of(column * room, 8)
            pieces[pl.ds(start, size), :] = block[first + a * size : first + a * size + size, :]


class Lanes:
    def __init__(self):
        self.lane = iota((8, 128), 1)
        sub = iota((8, 128), 0)
        self.group = self.lane // EZ
        self.odd = self.group % 2 == 1
        self.element = self.lane % EZ
        self.place = sub % 4
        self.low_half = sub < 4

    def around(self, u):
        turned = pltpu.roll(u, 4, u.ndim - 2)
        far = jnp.where(self.odd, pltpu.roll(turned, 32, u.ndim - 1), pltpu.roll(turned, 96, u.ndim - 1))
        return turned, far

    def x_before(self, u):
        turned, far = self.around(u)
        return jnp.where(self.low_half, far, turned)

    def x_after(self, u):
        turned, far = self.around(u)
        return jnp.where(self.low_half, turned, far)

    def y_before(self, u):
        return jnp.where(self.place == 0, pltpu.roll(u, 5, 0), pltpu.roll(u, 1, 0))

    def y_after(self, u):
        return jnp.where(self.place == 3, pltpu.roll(u, 3, 0), pltpu.roll(u, 7, 0))

    def z_before(self, u):
        return jnp.where(self.element == 0, pltpu.roll(u, 97, u.ndim - 1), pltpu.roll(u, 1, u.ndim - 1))

    def z_after(self, u):
        last = self.element == EZ - 1
        return jnp.where(last, pltpu.roll(u, 31, u.ndim - 1), pltpu.roll(u, 127, u.ndim - 1))


def load(ref, first, count):
    return ref[pl.ds(first * 8, count * 8), :].reshape(count, 8, 128)


def store(ref, first, value):
    ref[pl.ds(first * 8, value.shape[0] * 8), :] = value.reshape(value.shape[0] * 8, 128)


DIAGS = (0, 250, 304)
GAINS = (320, 326, 332)
REGISTERS = 338
CENTRE = (CHEB_HIGH + CHEB_LOW) / 2.0
RADIUS = (CHEB_HIGH - CHEB_LOW) / 2.0


def flag_lanes(row, slot):
    turned = [row] + [pltpu.roll(row, 32 * m, 1) for m in range(1, 4)]
    return choose(iota(row.shape, 1) // EZ, [turned[(g - 2 * slot - 1) % 4] for g in range(4)])


def line_kernel(piece3, piece2, piece1, piece0, line, faces):
    pieces = (piece0, piece1, piece2, piece3)
    even = lax.axis_index("gx") % 2 == 0
    odd = iota((8, 128), 1) // EZ % 2 == 1
    faces[...] = jnp.zeros_like(faces)

    def both(rows, f):
        side = odd[:1] if f else jnp.logical_not(odd[:1])
        return jnp.where(side, rows, pltpu.roll(rows, 96 if f else 32, 1))

    for a, piece in enumerate(pieces):
        for f in range(2):
            base = 64 * a + 32 * f
            inner = both(piece[FACE_X:KAPPA, :], f)
            ends = [both(piece[HALF:FACE_X, :], g) for g in range(2)]
            for k in range(5):
                r = base + 5 * k
                node = 5 * k + 4 * f
                faces[r : r + 1, :] = ends[0][node : node + 1]
                faces[r + 1 : r + 4, :] = inner[3 * k : 3 * k + 3]
                faces[r + 4 : r + 5, :] = ends[1][node : node + 1]
    for a, piece in enumerate(pieces):
        line[HALF * a : HALF * a + HALF, :] = piece[:HALF, :]
        line[LINE_KAPPA + 16 * a : LINE_KAPPA + 16 * a + 16, :] = piece[KAPPA:, :]
        line[LINE_Y + 25 * a : LINE_Y + 25 * a + 25, :] = piece[HALF:FACE_X, :]
        flags = [flag_lanes(piece[61:62, :], slot) for slot in range(2)]
        gains = [face_gains(flags[d], 0, d, 5) for d in range(2)]
        next_first = even if a % 2 == 0 else jnp.logical_not(even)
        for f in range(2):
            one = faces[64 * (a ^ 1) + 32 * (1 - f) : 64 * (a ^ 1) + 32 * (1 - f) + 32, :]
            three = faces[64 * (a ^ 3) + 32 * (1 - f) : 64 * (a ^ 3) + 32 * (1 - f) + 32, :]
            near = jnp.where(next_first, one, three) if f else jnp.where(next_first, three, one)
            term = gains[f] * near
            for k in range(5):
                node = 25 * k + 20 * f
                side = odd[:5] if node >= HALF else jnp.logical_not(odd[:5])
                r = HALF * a + node % HALF
                line[r : r + 5, :] = line[r : r + 5, :] + jnp.where(side, term[5 * k : 5 * k + 5], 0.0)
    line[LINE_Y + 100 :, :] = jnp.zeros((4, 128), F32)


def halves_kernel(block0, block1, block2, block3, out):
    place_pieces((block0, block1, block2, block3), out, LINE_KAPPA, 16, 16)


def widen(low, high, odd):
    return jnp.where(odd, pltpu.roll(high, 32, 1), low), jnp.where(odd, high, pltpu.roll(low, 96, 1))


def assemble_kernel(block0, block1, block2, block3, field, pieces, edges, traces):
    blocks = (block0, block1, block2, block3)
    place_pieces(blocks, pieces, 0, HALF, HALF)
    place_pieces(blocks, edges, LINE_Y, 25, 32)
    lanes = Lanes()
    for source, size, rows, target, apart in ((edges, 32, 25, traces, 25), (pieces, HALF, HALF, field, HALF)):
        for r in range(rows):
            first, second = widen(rows_of(source, size, r, 0), rows_of(source, size, r, 1), lanes.odd)
            target[tile(r), :] = first
            target[tile(apart + r), :] = second
    got = field[tile(126), :]
    across = pltpu.roll(got, 64, 1)
    gains = [
        face_gains(jnp.where(lanes.lane < 64, got, across), 1, 0, 5),
        face_gains(jnp.where(lanes.lane < 64, across, got), 1, 1, 5),
    ]
    for k in range(5):
        for i in range(5):
            lower, upper = traces[tile(5 * k + i), :], traces[tile(25 + 5 * k + i), :]
            node = 25 * k + 5 * i
            field[tile(node), :] = field[tile(node), :] + gains[0] * lanes.y_before(upper)
            field[tile(node + 4), :] = field[tile(node + 4), :] + gains[1] * lanes.y_after(lower)


def setup_kernel(field, own_halves, other_halves, coefs, kap):
    sec = lax.axis_index("section")
    lanes = Lanes()
    group, lane = lanes.group, lanes.lane
    flags = []
    for r in range(3):
        got = field[tile(125 + r), :]
        across = pltpu.roll(got, 64, 1)
        flags += [jnp.where(lane < 64, got, across), jnp.where(lane < 64, across, got)]
    for r in range(16):
        pairs = [[rows_of(ref, 16, r, h) for h in range(2)] for ref in (own_halves, other_halves)]
        for half in range(2):
            turned = []
            for h in range(2):
                got = jnp.where(sec == half, pairs[0][h], pairs[1][h])
                turned.append([pltpu.roll(got, 32 * m, 1) if m else got for m in range(4)])
            for q in range(4):
                value = choose(group, [turned[g % 2][(g - q) % 4] for g in range(4)])
                kap[tile(q * 32 + half * 16 + r), :] = value
    for p, n in enumerate((5, 3, 2)):
        stride = 4 // (n - 1)
        gains = [face_gains(flags[d], d // 2, d % 2, n) for d in range(6)]
        rows = []
        for d in range(3):
            coefs[tile(GAINS[p] + 2 * d), :] = gains[2 * d]
            coefs[tile(GAINS[p] + 2 * d + 1), :] = gains[2 * d + 1]
            table = element_matrix(n, d)
            row = [jnp.full((8, 128), float(table[m, m]), F32) for m in range(n)]
            row[0] = row[0] + gains[2 * d]
            row[n - 1] = row[n - 1] + gains[2 * d + 1]
            rows.append(row)
        along = jnp.stack(rows[1])
        for k in range(n):
            for i in range(n):
                line = load(kap, k * 25 * stride + i * stride * 5, 5)
                line = jnp.stack([line[j * stride] for j in range(n)])
                value = line + (along + (rows[2][k] + rows[0][i]))
                scale = 1.0 / (1.0 + STEP_SIZE * JACOBI_SCALE * value)
                store(coefs, DIAGS[p] + (k * n + i) * n, value)
                store(coefs, DIAGS[p] + n**3 + (k * n + i) * n, scale * (1.0 / CENTRE))


def cycle_kernel(coefs, assembled, fields, *scratch):
    sec = lax.axis_index("section")
    my_gx, my_gy = lax.axis_index("gx"), lax.axis_index("gy")
    levels = [Level(n, scratch[4 * p : 4 * p + 4]) for p, n in enumerate((5, 3, 2))]
    half = scratch[12]
    lanes = Lanes()
    lane = lanes.lane
    blocks = split_sections()[3]

    def lanes_of(upper, lower):
        return jnp.where(lane < 64, jnp.where(sec == 0, upper[0], upper[1]), jnp.where(sec == 0, lower[0], lower[1]))

    entry = [[[float(STEP_SIZE * blocks[2 * p + a, 2 * p + b]) for p in range(2)] for b in range(2)] for a in range(2)]
    same = lanes_of(entry[0][0], entry[1][1])
    swap = lanes_of(entry[0][1], entry[1][0])
    first_rho = RADIUS / CENTRE
    second_rho = 1.0 / (2.0 * CENTRE / RADIUS - first_rho)
    keep = 1.0 + second_rho * first_rho
    push = 2.0 * second_rho / RADIUS * CENTRE
    for p, level in enumerate(levels):
        size = level.count**3
        level.gains = [-coefs[tile(GAINS[p] + d), :] for d in range(6)]
        level.diag = lambda first, count, p=p: load(coefs, DIAGS[p] + first, count)
        level.jac = lambda first, count, p=p, size=size: load(coefs, DIAGS[p] + size + first, count)

    def begin(level, source):
        n = level.count
        for first in range(0, n**3, n):
            f = load(source, first, n)
            store(level.dir, first, level.jac(first, n) * f)
            store(level.res, first, f)
            store(level.x, first, jnp.zeros_like(f))

    def apply(level, smooth, always):
        n = level.count
        kx, ky, kz = level.tables
        gains = level.gains
        source = level.dir if smooth else level.x
        def tree(terms):
            while len(terms) > 1:
                pairs = [a + b for a, b in zip(terms[::2], terms[1::2])]
                terms = pairs + terms[len(terms) // 2 * 2 :]
            return terms[0]

        def plane(k):
            def line_at(i):
                return load(source, (k * n + i) * n, n)

            lines, totals = [], []
            for i in range(n):
                first = (k * n + i) * n
                v = line_at(i)
                along_x = [float(kx[i, m]) * line_at(m) for m in range(n) if m != i]
                if i == 0:
                    along_x.append(gains[0] * lanes.x_before(line_at(n - 1)))
                if i == n - 1:
                    along_x.append(gains[1] * lanes.x_after(line_at(0)))
                along_z = [float(kz[k, m]) * load(source, (m * n + i) * n, n) for m in range(n) if m != k]
                if k == 0:
                    along_z.append(gains[4] * lanes.z_before(load(source, ((n - 1) * n + i) * n, n)))
                if k == n - 1:
                    along_z.append(gains[5] * lanes.z_after(load(source, i * n, n)))
                along_y = []
                for j in range(n):
                    terms = [float(ky[j, m]) * v[m] for m in range(n) if m != j]
                    if j == 0:
                        terms.append(gains[2] * lanes.y_before(v[n - 1]))
                    if j == n - 1:
                        terms.append(gains[3] * lanes.y_after(v[0]))
                    along_y.append(tree(terms))
                lines.append(v)
                totals.append(tree([level.diag(first, n) * v, tree(along_x), tree(along_z), jnp.stack(along_y)]))
            moved = [pltpu.roll(total, 64, 2) for total in totals]
            for i in range(n):
                first = (k * n + i) * n
                v = lines[i]
                image = v + (same * totals[i] + swap * moved[i])
                if smooth:
                    scaled = level.jac(first, n) * (load(level.res, first, n) - image)
                    store(level.x, first, (load(level.x, first, n) + keep * v) + push * scaled)
                else:
                    rest = load(level.f, first, n) - image
                    store(level.res, first, rest)
                    store(level.dir, first, level.jac(first, n) * rest)

        for k in range(n):
            @pl.when(always)
            def _(k=k):
                plane(k)

    def combine(weights, parts):
        total = None
        for weight, part in zip(weights, parts):
            if abs(weight) > 1e-14:
                term = part if abs(weight - 1.0) < 1e-14 else float(weight) * part
                total = term if total is None else total + term
        return total

    def change(table, source, target, add):
        m, n = table.shape
        for i in range(n):
            parts = [load(source, i * n + k * n * n, n) for k in range(n)]
            for k in range(m):
                store(half, i * n + k * n * n, combine(table[k], parts))
        for k in range(m):
            parts = [load(half, k * n * n + i * n, n) for i in range(n)]
            for i in range(m):
                line = combine(table[i], parts)
                value = jnp.stack([combine(table[j], [line[a] for a in range(n)]) for j in range(m)])
                first = k * m * m + i * m
                store(target, first, load(target, first, m) + value if add else value)

    def down(n, m):
        fine_nodes, fine_weights = lobatto(n)
        coarse_nodes, coarse_weights = lobatto(m)
        table = lagrange_table(coarse_nodes, fine_nodes)
        return (1.0 / coarse_weights)[:, None] * table.T * fine_weights[None, :]

    def up(m, n):
        return lagrange_table(lobatto(m)[0], lobatto(n)[0])

    def solve(p, always=None):
        level = levels[p]
        if p == 2:
            apply(level, True, always)
            return
        below = levels[p + 1]

        def step(t, carry):
            @pl.when(t != 1)
            def _():
                apply(level, True, t >= 0)

            @pl.when((t != 2) | (p == 0))
            def _():
                apply(level, False, t >= 0)

            @pl.when(t == 0)
            def _():
                n, m = level.count, below.count
                change(down(n, m), level.res, below.f, False)
                begin(below, below.f)
                solve(p + 1, t >= 0)
                change(up(m, n), below.x, level.x, True)
            return carry
        lax.fori_loop(0, 3, step, 0)

    fine = levels[0]
    fine.f = assembled
    begin(fine, assembled)
    solve(0)

    for first in range(0, 125, 5):
        store(fields, first, load(fine.res, first, 5))
    column = (my_gx % 2) * 4 + my_gy
    fields[FIELD : FIELD + 125, :] = fine.x[pl.ds(column, 125, stride=8), :]
    fields[FIELD + 125 : FIELD + 128, :] = jnp.zeros((3, 128), F32)


def pair_weights():
    cross = split_sections()[4]
    return jnp.where(iota((8, 128), 1) < 64, float(cross[0]), float(cross[1]))


def column_factors(p):
    sec = lax.axis_index("section")
    whole = split_sections()[0]
    lane = iota((25, 128), 1)
    here = lane // EZ % 2 == lax.axis_index("gx") // 2
    factors = []
    for s in range(2):
        parts = []
        for mine in range(2):
            t = whole[2 * mine + s]
            q = mine if p == 0 else 1 - mine
            parts.append(jnp.where(lane < 64, float(t[2 * q]), float(t[2 * q + 1])))
        factors.append(jnp.where(here, jnp.where(sec == 0, parts[0], parts[1]), 0.0))
    return factors


def column_rows(k):
    column = (lax.axis_index("gx") % 2) * 4 + lax.axis_index("gy")
    return pl.ds(k * 200 + column, 25, stride=8)


def raw_order(k):
    lane = iota((256, 160), 0)
    return (iota((256, 160), 1) == 5 * (lane % EZ) + k + lane // 128).astype(F32)


def early_kernel(own, own_start, other_start, sums, column_out, cols):
    weights = pair_weights()
    cols[...] = jnp.zeros_like(cols)
    total = jnp.zeros((192, 160), F32)
    own_factors, other_factors = column_factors(0), column_factors(1)
    for k in range(5):
        where = column_rows(k)
        z = own[FIELD + k * 25 : FIELD + k * 25 + 25, :]
        start, other = own_start[where, :], other_start[where, :]
        w = start - own[where, :]
        side = slice(0, 128) if k % 2 == 0 else slice(128, 256)
        for s in range(2):
            cols[s * 32 : s * 32 + 25, side] = own_factors[s] * z
            cols[64 + s * 32 : 64 + s * 32 + 25, side] = own_factors[s] * start + other_factors[s] * other
            cols[128 + s * 32 : 128 + s * 32 + 25, side] = own_factors[s] * w
        if k % 2 == 1:
            total = total + split_dot(cols[...], raw_order(k - 1))
    cols[:, 128:] = jnp.zeros((192, 128), F32)
    total = total + split_dot(cols[...], raw_order(4))
    column_out[...] = total
    nothing = jnp.zeros((8, 128), F32)
    uppers, sizes = [nothing] * 5, [nothing] * 5
    for r in range(125):
        c, d = own_start[tile(r), :], other_start[tile(r), :]
        a = c - own[tile(r), :]
        uppers[r % 5] = uppers[r % 5] + a * (c + weights * d)
        sizes[r % 5] = sizes[r % 5] + ((c * c + d * d) + 2.0 * (weights * (c * d)))
    sums[0:8, :] = sum(uppers)
    sums[8:16, :] = sum(sizes)


def finish_kernel(own, other, own_start, other_start, sums, column, guess, sol, res_out, arnoldi, cols, outs):
    sec = lax.axis_index("section")
    weights = pair_weights()
    cols[...] = jnp.zeros_like(cols)
    total = jnp.zeros((128, 160), F32)
    factors = column_factors(1)
    for k in range(5):
        where = column_rows(k)
        z = other[FIELD + k * 25 : FIELD + k * 25 + 25, :]
        w = other_start[where, :] - other[where, :]
        side = slice(0, 128) if k % 2 == 0 else slice(128, 256)
        for s in range(2):
            cols[s * 32 : s * 32 + 25, side] = factors[s] * z
            cols[64 + s * 32 : 64 + s * 32 + 25, side] = factors[s] * w
        if k % 2 == 1:
            total = total + split_dot(cols[...], raw_order(k - 1))
    cols[:, 128:] = jnp.zeros((128, 128), F32)
    total = total + split_dot(cols[...], raw_order(4))
    nothing = jnp.zeros((8, 128), F32)
    uppers = [nothing] * 5
    for r in range(125):
        c, d = own_start[tile(r), :], other_start[tile(r), :]
        b = d - other[tile(r), :]
        uppers[r % 5] = uppers[r % 5] + b * (d + weights * c)

    mine, theirs = sums[0:8, :], sum(uppers)
    size = jnp.sum(sums[8:16, :], keepdims=True)
    upper = jnp.sum(mine + theirs, keepdims=True) / size
    rests = [nothing] * 5
    for r in range(125):
        c, d = own_start[tile(r), :], other_start[tile(r), :]
        a = (c - own[tile(r), :]) - upper * c
        b = (d - other[tile(r), :]) - upper * d
        rests[r % 5] = rests[r % 5] + ((a * a + b * b) + 2.0 * (weights * (a * b)))
    rest = jnp.sum(sum(rests), keepdims=True)
    beta = jnp.sqrt(size)
    lower = jnp.sqrt(rest) / beta
    weight = upper / (upper * upper + lower * lower)
    entries = float(125 * EZ * COLS * 4)
    for place_out, value in enumerate((beta * (1.0 / math.sqrt(entries)), upper, lower)):
        arnoldi[place_out] = value[0, 0]
    outs[:64, :] = weight * (column[:64, :] + total[:64])
    outs[64:, :] = column[64:128, :] - weight * (column[128:, :] + total[64:])
    for i in range(5):
        for j in range(5):
            r = 5 * i + j
            for s in range(2):
                sol[i, j, s : s + 1, :] = guess[i, j, s : s + 1, :] + outs[s * 32 + r : s * 32 + r + 1, :]
                res_out[i, j, s : s + 1, :] = outs[64 + s * 32 + r : 64 + s * 32 + r + 1, :]


def plain_call(kernel, name, rows, scratch, operands, cost=1_000_000):
    return pl.pallas_call(
        kernel,
        out_shape=jax.ShapeDtypeStruct((rows, 128), F32),
        in_specs=[VMEM] * len(operands),
        out_specs=VMEM,
        scratch_shapes=[pltpu.VMEM((r, 128), F32) for r in scratch],
        compiler_params=limit(16),
        cost_estimate=pl.CostEstimate(flops=cost, bytes_accessed=cost, transcendentals=0),
        name=name,
    )(*operands)


def cycle(coefs, assembled):
    scratch = []
    for n in (5, 3, 2):
        scratch += [pltpu.VMEM((n**3 * 8, 128), F32)] * 4
    scratch += [pltpu.VMEM((FIELD, 128), F32)]
    return pl.pallas_call(
        cycle_kernel,
        out_shape=jax.ShapeDtypeStruct((FIELD + 128, 128), F32),
        in_specs=[VMEM] * 2,
        out_specs=VMEM,
        scratch_shapes=scratch,
        compiler_params=limit(24),
        cost_estimate=pl.CostEstimate(flops=40_000_000, bytes_accessed=30_000_000, transcendentals=0),
        name="cycle",
    )(coefs, assembled)


def early(own, own_start, other_start):
    return pl.pallas_call(
        early_kernel,
        out_shape=[jax.ShapeDtypeStruct((16, 128), F32), jax.ShapeDtypeStruct((192, 160), F32)],
        in_specs=[VMEM] * 3,
        out_specs=[VMEM] * 2,
        scratch_shapes=[pltpu.VMEM((192, 256), F32)],
        compiler_params=limit(16),
        cost_estimate=pl.CostEstimate(flops=4_000_000, bytes_accessed=4_000_000, transcendentals=0),
        name="early",
    )(own, own_start, other_start)


def finish(own, other, own_start, other_start, sums, column, guess):
    return pl.pallas_call(
        finish_kernel,
        out_shape=[
            jax.ShapeDtypeStruct(guess.shape, F32),
            jax.ShapeDtypeStruct(guess.shape, F32),
            jax.ShapeDtypeStruct((3,), F32),
        ],
        in_specs=[VMEM] * 7,
        out_specs=[VMEM, VMEM, pl.BlockSpec(memory_space=pltpu.SMEM)],
        scratch_shapes=[pltpu.VMEM((128, 256), F32), pltpu.VMEM((128, 160), F32)],
        compiler_params=limit(24),
        name="finish",
    )(own, other, own_start, other_start, sums, column, guess)


def exchange(x, axis, bits):
    return lax.ppermute(x, axis, [(n, n ^ bits) for n in range(lax.axis_size(axis))])


def gathered_body(rhs, guess, kappa, bc_flags):
    rhs, guess = (jnp.transpose(v, (1, 2, 0, 3)) for v in (rhs, guess))
    mine, theirs = local_part(rhs, guess, kappa, bc_flags)
    got, mine, kappa_piece = lax.optimization_barrier((exchange(theirs, "section", 1), *part(mine)))
    piece = jnp.concatenate([mine + got, kappa_piece])
    pieces = [piece] + [exchange(piece, "gx", bits) for bits in (1, 2, 3)]
    line = plain_call(line_kernel, "line", LINE, [4 * 64], pieces[::-1])
    blocks = [line] + [exchange(line, "gy", bits) for bits in (1, 2, 3)]
    halves = plain_call(halves_kernel, "halves", COLS * 16, [], blocks)
    other_halves = exchange(halves, "section", 1)
    start = plain_call(assemble_kernel, "assemble", 128 * 8, [COLS * HALF, COLS * 32, 50 * 8], blocks, 4_000_000)
    start, other_halves = lax.optimization_barrier((start, other_halves))
    coefs = plain_call(setup_kernel, "setup", REGISTERS * 8, [128 * 8], (start, halves, other_halves))
    other_start = exchange(start, "section", 1)
    own, other_start = lax.optimization_barrier((cycle(coefs, start), other_start))
    sums, column = early(own, start, other_start)
    sol, res, arnoldi = finish(own, exchange(own, "section", 1), start, other_start, sums, column, guess)
    sol, res = (jnp.transpose(v, (2, 0, 1, 3)) for v in (sol, res))
    return sol, res, arnoldi


def solution(mesh):
    placed = (
        P("section", "gx", "gy", None),
        P("section", "gx", "gy", None),
        P("gx", "gy", None),
        P(None, "gx", "gy", None),
    )
    sizes = (mesh.shape["section"], mesh.shape["gx"], mesh.shape["gy"])

    def step(rhs, guess, kappa, bc_flags):
        fits = sizes == (2, 4, 4) and rhs.shape == (4, 20, 20, 160)
        return jax.shard_map(
            gathered_body if fits else stepwise,
            mesh=mesh,
            in_specs=placed,
            out_specs=(P("section", "gx", "gy", None), P("section", "gx", "gy", None), P()),
            check_vma=False,
        )(rhs, guess, kappa, bc_flags)

    return step
```

```python
from functools import partial
import math

import jax
import jax.numpy as jnp
import numpy as np
from jax import lax
from jax.experimental import pallas as pl
from jax.experimental.pallas import tpu as pltpu
from jax.sharding import PartitionSpec as P

ADVECT = (1.0, 0.7, 0.5)
DIFFUSE = 0.05
STEP_SIZE = 0.2
JACOBI_SCALE = 0.25
CHEB_LOW = 0.25
CHEB_HIGH = 2.0
LETTERS = "abcdef"


def extended(x, sides, width):
    for axis, dim in sides:
        peers, length = (lax.axis_size(axis), x.shape[dim])
        up = [(i, (i + 1) % peers) for i in range(peers)]
        down = [(j, i) for i, j in up]
        last = lax.slice_in_dim(x, length - width, length, axis=dim)
        leading = lax.slice_in_dim(x, 0, width, axis=dim)
        before = lax.ppermute(last, axis, up)
        after = lax.ppermute(leading, axis, down)
        x = jnp.concatenate([before, x, after], axis=dim)
    return x


def lobatto(count):
    if count == 5:
        inner = math.sqrt(3.0 / 7.0)
        return (
            np.array([-1.0, -inner, 0.0, inner, 1.0]),
            np.array([0.1, 49.0 / 90.0, 32.0 / 45.0, 49.0 / 90.0, 0.1]),
        )
    if count == 3:
        return (np.array([-1.0, 0.0, 1.0]), np.array([1.0 / 3.0, 4.0 / 3.0, 1.0 / 3.0]))
    return (np.array([-1.0, 1.0]), np.array([1.0, 1.0]))


def lagrange_table(nodes, points):
    table = np.ones((len(points), len(nodes)))
    for column in range(len(nodes)):
        for other in range(len(nodes)):
            if other != column:
                table[:, column] *= (points - nodes[other]) / (nodes[column] - nodes[other])
    return table


def slope_table(nodes):
    total = len(nodes)
    factor = np.array(
        [np.prod([nodes[i] - nodes[k] for k in range(total) if k != i]) for i in range(total)]
    )
    table = np.zeros((total, total))
    for row in range(total):
        for column in range(total):
            if row != column:
                table[row, column] = factor[row] / factor[column] / (nodes[row] - nodes[column])
        table[row, row] = -np.sum(table[row])
    return table


def element_matrix(count, direction):
    nodes, weights = lobatto(count)
    slopes = slope_table(nodes)
    stiffness = (1.0 / weights)[:, None] * (slopes.T @ (weights[:, None] * slopes))
    return ADVECT[direction] * slopes + DIFFUSE * stiffness


def legendre_pair(point, order):
    values = [1.0, point]
    slopes = [0.0, 1.0]
    for index in range(1, order):
        values.append(
            ((2 * index + 1) * point * values[index] - index * values[index - 1]) / (index + 1)
        )
        slopes.append(slopes[index - 1] + (2 * index + 1) * values[index])
    return (values, slopes)


def radau_nodes():
    starts = [0.0885879595127039, 0.4094668644407347, 0.7876594617608471]
    found = []
    for start in starts:
        point = start
        for sweep in range(30):
            values, slopes = legendre_pair(2.0 * point - 1.0, 4)
            change = (values[4] - values[3]) / (2.0 * (slopes[4] - slopes[3]))
            point = point - change
        found.append(point)
    found.append(1.0)
    return found


def poly_times(coefs, root):
    result = [0.0] * (len(coefs) + 1)
    for index in range(len(coefs)):
        result[index + 1] += coefs[index]
        result[index] -= root * coefs[index]
    return result


def radau_matrix():
    order = 4
    nodes = radau_nodes()
    matrix = np.zeros((order, order))
    for column in range(order):
        coefs = [1.0]
        denominator = 1.0
        for other in range(order):
            if other != column:
                coefs = poly_times(coefs, nodes[other])
                denominator *= nodes[column] - nodes[other]
        for row in range(order):
            upper_end = nodes[row]
            integral = 0.0
            for index in range(len(coefs)):
                integral += coefs[index] * upper_end ** (index + 1) / (index + 1)
            matrix[row, column] = integral / denominator
    return matrix


def node_einsum(table, field, axis):
    labels = LETTERS[: field.ndim]
    source = labels[: axis + 1] + "j" + labels[axis + 2 :]
    target = labels[: axis + 1] + "i" + labels[axis + 2 :]
    return jnp.einsum(
        "ij," + source + "->" + target,
        jnp.asarray(table, jnp.float32),
        field,
        precision=lax.Precision.HIGHEST,
    )


def apply_along(field, axis, count, table):
    shape = field.shape
    split = shape[:axis] + (shape[axis] // count, count) + shape[axis + 1 :]
    mapped = node_einsum(table, field.reshape(split), axis)
    return mapped.reshape(
        shape[:axis] + (mapped.shape[axis] * mapped.shape[axis + 1],) + shape[axis + 1 :]
    )


def line_part(field, axis, count, table, left_gain, right_gain, left_edge, right_edge):
    shape = field.shape
    elements = shape[axis] // count
    split = field.reshape(shape[:axis] + (elements, count) + shape[axis + 1 :])
    linear = node_einsum(table, split, axis)
    first = lax.index_in_dim(split, 0, axis + 1, keepdims=False)
    last = lax.index_in_dim(split, count - 1, axis + 1, keepdims=False)
    before = jnp.concatenate(
        [jnp.expand_dims(left_edge, axis), lax.slice_in_dim(last, 0, elements - 1, axis=axis)], axis
    )
    after = jnp.concatenate(
        [lax.slice_in_dim(first, 1, elements, axis=axis), jnp.expand_dims(right_edge, axis)], axis
    )
    front = jnp.expand_dims(left_gain * (first - before), axis + 1)
    back = jnp.expand_dims(right_gain * (last - after), axis + 1)
    if count > 2:
        middle_shape = list(front.shape)
        middle_shape[axis + 1] = count - 2
        pieces = [front, jnp.zeros(middle_shape, jnp.float32), back]
    else:
        pieces = [front, back]
    return (linear + jnp.concatenate(pieces, axis + 1)).reshape(shape)


def diag_along(shape, axis, count, table, left_gain, right_gain):
    elements = shape[axis] // count
    split = shape[:axis] + (elements, count) + shape[axis + 1 :]
    profile = [1] * len(split)
    profile[axis + 1] = count
    diagonal_entries = np.array([table[index, index] for index in range(count)])
    base = jnp.broadcast_to(jnp.asarray(diagonal_entries, jnp.float32).reshape(profile), split)
    front = jnp.expand_dims(left_gain, axis + 1)
    back = jnp.expand_dims(right_gain, axis + 1)
    if count > 2:
        middle_shape = list(front.shape)
        middle_shape[axis + 1] = count - 2
        pieces = [front, jnp.zeros(middle_shape, jnp.float32), back]
    else:
        pieces = [front, back]
    return (base + jnp.concatenate(pieces, axis + 1)).reshape(shape)


def level_kappa(kappa, count):
    if count == 5:
        return kappa
    picks = np.array([0, 2, 4]) if count == 3 else np.array([0, 4])
    extents = [extent // 5 for extent in kappa.shape]
    grouped = kappa.reshape(extents[0], 5, extents[1], 5, extents[2], 5)
    for axis in (1, 3, 5):
        grouped = jnp.take(grouped, picks, axis=axis)
    return grouped.reshape(extents[0] * count, extents[1] * count, extents[2] * count)


def face_plane(face, direction, count):
    plane = face.astype(jnp.float32)
    for axis in range(3):
        if axis != direction:
            plane = jnp.repeat(plane, count, axis=axis)
    return plane


def build_level(kappa, flags, count):
    nodes, weights = lobatto(count)
    kappa_level = level_kappa(kappa, count)
    tables, lefts, rights = ([], [], [])
    diagonal = kappa_level
    for direction in range(3):
        table = element_matrix(count, direction)
        lower = face_plane(flags[2 * direction], direction, count)
        upper = face_plane(flags[2 * direction + 1], direction, count)
        left_gain = (ADVECT[direction] * (1.0 + lower) / 2.0 + DIFFUSE * count * count) / float(
            weights[0]
        )
        right_gain = (DIFFUSE * count * count - ADVECT[direction] * (1.0 - upper) / 2.0) / float(
            weights[-1]
        )
        tables.append(table)
        lefts.append(left_gain)
        rights.append(right_gain)
        diagonal = diagonal + diag_along(
            kappa_level.shape, direction, count, table, left_gain, right_gain
        )
    scale = 1.0 / (1.0 + STEP_SIZE * JACOBI_SCALE * diagonal)
    return (count, tables, lefts, rights, kappa_level, scale)


def restrict(field, fine_count, coarse_count):
    fine_nodes, fine_weights = lobatto(fine_count)
    coarse_nodes, coarse_weights = lobatto(coarse_count)
    table = (
        (1.0 / coarse_weights)[:, None]
        * lagrange_table(coarse_nodes, fine_nodes).T
        * fine_weights[None, :]
    )
    for axis in range(field.ndim - 3, field.ndim):
        field = apply_along(field, axis, fine_count, table)
    return field


def prolong(field, coarse_count, fine_count):
    fine_nodes, fine_weights = lobatto(fine_count)
    coarse_nodes, coarse_weights = lobatto(coarse_count)
    table = lagrange_table(coarse_nodes, fine_nodes)
    for axis in range(field.ndim - 3, field.ndim):
        field = apply_along(field, axis, coarse_count, table)
    return field


def chebyshev(rhs, start, level, operator):
    centre = (CHEB_HIGH + CHEB_LOW) / 2.0
    radius = (CHEB_HIGH - CHEB_LOW) / 2.0
    ratio = centre / radius
    first_rho = 1.0 / ratio
    second_rho = 1.0 / (2.0 * ratio - first_rho)
    scale = level[5]
    if start is None:
        remain = rhs
    else:
        remain = rhs - operator(start, level)
    step = scale * remain / centre
    guess = step if start is None else start + step
    remain = remain - operator(step, level)
    step = second_rho * first_rho * step + 2.0 * second_rho / radius * scale * remain
    return guess + step


def vcycle(rhs, levels, operator):
    fine, middle, coarse = levels
    fine_x = chebyshev(rhs, None, fine, operator)
    middle_rhs = restrict(rhs - operator(fine_x, fine), 5, 3)
    middle_x = chebyshev(middle_rhs, None, middle, operator)
    coarse_rhs = restrict(middle_rhs - operator(middle_x, middle), 3, 2)
    coarse_x = chebyshev(coarse_rhs, None, coarse, operator)
    middle_x = chebyshev(middle_rhs, middle_x + prolong(coarse_x, 2, 3), middle, operator)
    return chebyshev(rhs, fine_x + prolong(middle_x, 3, 5), fine, operator)


def spatial(field, level):
    count, tables, lefts, rights, kappa_level, scale = level
    padded = extended(field, (("gx", 1), ("gy", 2)), 1)
    total = kappa_level * field
    total = total + line_part(
        field,
        1,
        count,
        tables[0],
        lefts[0],
        rights[0],
        padded[:, 0, 1:-1, :],
        padded[:, -1, 1:-1, :],
    )
    total = total + line_part(
        field,
        2,
        count,
        tables[1],
        lefts[1],
        rights[1],
        padded[:, 1:-1, 0, :],
        padded[:, 1:-1, -1, :],
    )
    total = total + line_part(
        field, 3, count, tables[2], lefts[2], rights[2], field[:, :, :, -1], field[:, :, :, 0]
    )
    return total


def apply_system(field, level, coupling):
    image = spatial(field, level)
    everyone = lax.all_gather(image, "section", axis=0, tiled=True)
    butcher = jnp.asarray(radau_matrix(), jnp.float32)
    rows = lax.dynamic_slice_in_dim(
        butcher, lax.axis_index("section") * field.shape[0], field.shape[0], 0
    )
    mixed = jnp.einsum("ij,jabc->iabc", rows, everyone, precision=lax.Precision.HIGHEST)
    return field + STEP_SIZE * mixed


def global_total(values):
    return lax.psum(values, ("section", "gx", "gy"))


def stepwise(rhs, guess, kappa, bc_flags):
    levels = [build_level(kappa, bc_flags, count) for count in (5, 3, 2)]
    section_operator = partial(apply_system, coupling=None)
    start_residual = rhs - section_operator(guess, levels[0])
    dofs = float(rhs.size * lax.axis_size("section") * lax.axis_size("gx") * lax.axis_size("gy"))
    beta = jnp.sqrt(global_total(jnp.sum(start_residual * start_residual).reshape(1))[0])
    basis = start_residual / beta
    precond = vcycle(basis, levels, section_operator)
    image = section_operator(precond, levels[0])
    upper = global_total(jnp.sum(image * basis).reshape(1))[0]
    remainder = image - upper * basis
    lower = jnp.sqrt(global_total(jnp.sum(remainder * remainder).reshape(1))[0])
    weight = beta * upper / (upper * upper + lower * lower)
    solution = guess + weight * precond
    residual = start_residual - weight * image
    arnoldi = jnp.stack([beta / math.sqrt(dofs), upper, lower]).astype(jnp.float32)
    return (solution, residual, arnoldi)


EZ = 32
COLS = 16
HALF = 64
FACE_X = HALF + 25
KAPPA = FACE_X + 15
PIECE = KAPPA + 16
LINE_KAPPA = 4 * HALF
LINE_Y = LINE_KAPPA + 4 * 16
LINE = LINE_Y + 104
FIELD = 1000
F32 = jnp.float32


def split_sections():
    matrix = radau_matrix()
    values, vectors = np.linalg.eig(matrix)
    order = [n for n in np.argsort(np.abs(values.imag), kind="stable") if values[n].imag > 0]
    bases = []
    for n in order:
        plane = np.stack([vectors[:, n].real, vectors[:, n].imag], axis=1)
        bases.append(np.linalg.qr(plane)[0])
    left, cross, right = np.linalg.svd(bases[0].T @ bases[1])
    bases = [bases[0] @ left, bases[1] @ right.T]
    for c in range(2):
        sign = np.sign(bases[0][np.argmax(np.abs(bases[0][:, c])), c])
        bases = [np.concatenate([b[:, :c], sign * b[:, c : c + 1], b[:, c + 1 :]], axis=1) for b in bases]
    whole = np.concatenate(bases, axis=1)
    back = np.linalg.inv(whole)
    return whole, back, back @ matrix, back @ matrix @ whole, cross


def iota(shape, dim):
    return lax.broadcasted_iota(jnp.int32, shape, dim)


def exact_dot(a, b):
    return lax.dot_general(
        a, b, (((1,), (0,)), ((), ())), precision=lax.Precision.HIGHEST, preferred_element_type=F32
    )


def split_dot(a, b):
    high = a.astype(jnp.bfloat16)
    rest = a - high.astype(F32)
    middle = rest.astype(jnp.bfloat16)
    low = (rest - middle.astype(F32)).astype(jnp.bfloat16)
    b = b.astype(jnp.bfloat16)
    return sum(
        lax.dot_general(part, b, (((1,), (0,)), ((), ())), preferred_element_type=F32)
        for part in (low, middle, high)
    )


def choose(index, values):
    out = values[-1]
    for place in range(len(values) - 2, -1, -1):
        out = jnp.where(index == place, values[place], out)
    return out


def face_gains(flag, direction, side, count):
    nodes, weights = lobatto(count)
    c, nu = ADVECT[direction], DIFFUSE * count * count
    if side == 0:
        return (c * (1.0 + flag) / 2.0 + nu) * (1.0 / float(weights[0]))
    return (nu - c * (1.0 - flag) / 2.0) * (1.0 / float(weights[-1]))


def row_table():
    kx, ky = (element_matrix(5, d) for d in range(2))
    rows = np.zeros((64, 64))
    for s in range(2):
        for i in range(5):
            for j in range(5):
                r = s * 32 + i * 5 + j
                for m in range(5):
                    rows[r, s * 32 + m * 5 + j] += kx[i, m]
                    rows[r, s * 32 + i * 5 + m] += ky[j, m]
    return rows.astype(np.float32)


def pick_lines(k):
    lane = iota((160, 256), 1)
    return (iota((160, 256), 0) == 5 * (lane % EZ) + k + lane // 128).astype(F32)


def pair_factors(sec, table, own, s):
    upper = iota((32, 128), 1) < 64
    first = jnp.where(upper, float(table[0, s]), float(table[1, s]))
    second = jnp.where(upper, float(table[2, 2 + s]), float(table[3, 2 + s]))
    if not own:
        first = jnp.where(upper, float(table[2, s]), float(table[3, s]))
        second = jnp.where(upper, float(table[0, 2 + s]), float(table[1, 2 + s]))
    return jnp.where(sec == 0, first, second)


def pack_nodes(nodes):
    half = nodes.shape[0] // 2
    odd = iota((half, 128), 1) // EZ % 2 == 1
    return jnp.where(odd, nodes[half:, :], nodes[:half, :])


def fetch(pairs, sems):
    copies = [pltpu.make_async_copy(src, dst, sems.at[n]) for n, (src, dst) in enumerate(pairs)]
    for copy in copies:
        copy.start()
    for copy in copies:
        copy.wait()


def local_kernel(
    rhs_in, guess_in, kappa_in, flags_in, rows_in, mine, theirs,
    rhs, guess, kappa, flags, rows_t, sems, stack, lines, nodes, y_faces, x_faces,
):
    sec = lax.axis_index("section")
    fetch([(rhs_in, rhs), (guess_in, guess), (kappa_in, kappa), (flags_in, flags), (rows_in, rows_t)], sems)
    stack[...] = jnp.zeros_like(stack)
    for i in range(5):
        stack[192 + 5 * i : 197 + 5 * i, :] = kappa[i]
        for j in range(5):
            r = 5 * i + j
            value = guess[i, j]
            left = rhs[i, j] - value
            for s in range(2):
                stack[s * 32 + r : s * 32 + r + 1, :] = left[s : s + 1]
                stack[128 + s * 32 + r : 128 + s * 32 + r + 1, :] = value[s : s + 1]
    stack[64:128, :] = exact_dot(rows_t[...], stack[128:192, :])
    source = stack[...]
    for k in (0, 2, 4):
        shown = split_dot(source, pick_lines(k))
        lines[224 * k : 224 * k + 224, :] = shown[:, :128]
        if k < 4:
            lines[224 * k + 224 : 224 * k + 448, :] = shown[:, 128:]

    def part(k, first):
        return lines[224 * k + first : 224 * k + first + 32, :]

    repeat = (iota((EZ, 128), 1) % EZ == iota((EZ, 128), 0)).astype(F32)
    shown = split_dot(flags[:, 0, 0, :].astype(F32), repeat)
    gains = [face_gains(shown[d : d + 1, :], d // 2, d % 2, 5) for d in range(6)]
    row = iota((32, 128), 0)
    none = jnp.zeros((32, 128), F32)
    own = jnp.where(row < 5, gains[0], jnp.where((row >= 20) & (row < 25), gains[1], none))
    own = own + jnp.where(row % 5 == 0, gains[2], jnp.where(row % 5 == 4, gains[3], none))
    kz = element_matrix(5, 2)
    back, back_matrix = split_sections()[1:3]
    for ref in (nodes, y_faces, x_faces):
        ref[...] = jnp.zeros_like(ref)
    for k in range(5):
        diagonal = part(k, 192) + own
        if k == 0:
            diagonal = diagonal + gains[4]
        if k == 4:
            diagonal = diagonal + gains[5]
        images = []
        for s in range(2):
            first = 128 + 32 * s
            image = diagonal * part(k, first) + part(k, 64 + 32 * s)
            for m in range(5):
                image = image + float(kz[k, m]) * part(m, first)
            if k == 0:
                image = image - gains[4] * pltpu.roll(part(4, first), 1, 1)
            if k == 4:
                image = image - gains[5] * pltpu.roll(part(0, first), 127, 1)
            images.append(image)
        for p, mark in enumerate((True, False)):
            total = jnp.zeros((32, 128), F32)
            trace = jnp.zeros((32, 128), F32)
            for s in range(2):
                total = total + pair_factors(sec, back, mark, s) * part(k, 32 * s)
                factor = pair_factors(sec, STEP_SIZE * back_matrix, mark, s)
                total = total - factor * images[s]
                trace = trace + factor * part(k, 128 + 32 * s)
            nodes[128 * p + 25 * k : 128 * p + 25 * k + 25, :] = total[:25]
            for i in range(5):
                for f in range(2):
                    r = 64 * p + 32 * f + 5 * k + i
                    y_faces[r : r + 1, :] = trace[5 * i + 4 * f : 5 * i + 4 * f + 1]
            for f in range(2):
                r = 32 * p + 16 * f + 3 * k
                x_faces[r : r + 3, :] = trace[20 * f + 1 : 20 * f + 4]
    upper = iota((1, 128), 1) < 64
    for r in range(3):
        nodes[125 + r : 126 + r, :] = jnp.where(upper, shown[2 * r : 2 * r + 1], shown[2 * r + 1 : 2 * r + 2])
    for p, out in enumerate((mine, theirs)):
        out[:HALF, :] = pack_nodes(nodes[128 * p : 128 * p + 128, :])
        out[HALF:FACE_X, :] = pack_nodes(y_faces[64 * p : 64 * p + 64, :])[:25]
        out[FACE_X:KAPPA, :] = pack_nodes(x_faces[32 * p : 32 * p + 32, :])[:15]
    for k in range(5):
        nodes[25 * k : 25 * k + 25, :] = part(k, 192)[:25]
    kappas = choose(iota((32, 128), 1) // EZ, [nodes[32 * q : 32 * q + 32, :] for q in range(4)])
    mine[KAPPA:, :] = jnp.where(sec == 0, kappas[:16], kappas[16:])


def part_kernel(source, piece, kappa):
    piece[...] = source[:KAPPA, :]
    kappa[...] = source[KAPPA:, :]


VMEM = pl.BlockSpec(memory_space=pltpu.VMEM)
HBM = pl.BlockSpec(memory_space=pltpu.HBM)


def limit(mib):
    return pltpu.CompilerParams(vmem_limit_bytes=mib * 2**20)


def local_part(rhs, guess, kappa, flags):
    operands = (rhs, guess, kappa, flags, jnp.asarray(row_table()))
    return pl.pallas_call(
        local_kernel,
        out_shape=[jax.ShapeDtypeStruct((rows, 128), F32) for rows in (PIECE, KAPPA)],
        in_specs=[HBM] * 5,
        out_specs=[VMEM] * 2,
        scratch_shapes=[pltpu.VMEM(o.shape, o.dtype) for o in operands]
        + [
            pltpu.SemaphoreType.DMA((5,)),
            pltpu.VMEM((224, 160), F32),
            pltpu.VMEM((5 * 224, 128), F32),
            pltpu.VMEM((256, 128), F32),
            pltpu.VMEM((128, 128), F32),
            pltpu.VMEM((64, 128), F32),
        ],
        compiler_params=limit(60),
        cost_estimate=pl.CostEstimate(flops=20_000_000, bytes_accessed=8_000_000, transcendentals=0),
        name="local_part",
    )(*operands)


def part(x):
    return pl.pallas_call(
        part_kernel,
        out_shape=[jax.ShapeDtypeStruct((rows, 128), F32) for rows in (KAPPA, 16)],
        in_specs=[VMEM],
        out_specs=[VMEM] * 2,
        compiler_params=limit(16),
        name="part",
    )(x)


class Level:
    def __init__(self, count, refs):
        self.count = count
        self.x, self.dir, self.res, self.f = refs
        self.tables = [element_matrix(count, d) for d in range(3)]
        self.gains = self.diag = self.jac = None


def tile(index):
    return pl.ds(index * 8, 8)


def rows_of(pieces, size, r, h):
    return pieces[pl.ds(8 * h * size + r, 8, stride=size), :]


def place_pieces(blocks, pieces, first, size, room):
    my_gx, my_gy = lax.axis_index("gx"), lax.axis_index("gy")
    for b, block in enumerate(blocks):
        for a in range(4):
            column = (my_gx ^ a) * 4 + (my_gy ^ b)
            start = pl.multiple_of(column * room, 8)
            pieces[pl.ds(start, size), :] = block[first + a * size : first + a * size + size, :]


class Lanes:
    def __init__(self):
        self.lane = iota((8, 128), 1)
        sub = iota((8, 128), 0)
        self.group = self.lane // EZ
        self.odd = self.group % 2 == 1
        self.element = self.lane % EZ
        self.place = sub % 4
        self.low_half = sub < 4

    def around(self, u):
        turned = pltpu.roll(u, 4, u.ndim - 2)
        far = jnp.where(self.odd, pltpu.roll(turned, 32, u.ndim - 1), pltpu.roll(turned, 96, u.ndim - 1))
        return turned, far

    def x_before(self, u):
        turned, far = self.around(u)
        return jnp.where(self.low_half, far, turned)

    def x_after(self, u):
        turned, far = self.around(u)
        return jnp.where(self.low_half, turned, far)

    def y_before(self, u):
        return jnp.where(self.place == 0, pltpu.roll(u, 5, 0), pltpu.roll(u, 1, 0))

    def y_after(self, u):
        return jnp.where(self.place == 3, pltpu.roll(u, 3, 0), pltpu.roll(u, 7, 0))

    def z_before(self, u):
        return jnp.where(self.element == 0, pltpu.roll(u, 97, u.ndim - 1), pltpu.roll(u, 1, u.ndim - 1))

    def z_after(self, u):
        last = self.element == EZ - 1
        return jnp.where(last, pltpu.roll(u, 31, u.ndim - 1), pltpu.roll(u, 127, u.ndim - 1))


def load(ref, first, count):
    return ref[pl.ds(first * 8, count * 8), :].reshape(count, 8, 128)


def store(ref, first, value):
    ref[pl.ds(first * 8, value.shape[0] * 8), :] = value.reshape(value.shape[0] * 8, 128)


DIAGS = (0, 250, 304)
GAINS = (320, 326, 332)
REGISTERS = 338
CENTRE = (CHEB_HIGH + CHEB_LOW) / 2.0
RADIUS = (CHEB_HIGH - CHEB_LOW) / 2.0


def flag_lanes(row, slot):
    turned = [row] + [pltpu.roll(row, 32 * m, 1) for m in range(1, 4)]
    return choose(iota(row.shape, 1) // EZ, [turned[(g - 2 * slot - 1) % 4] for g in range(4)])


def line_kernel(piece3, piece2, piece1, piece0, line, faces):
    pieces = (piece0, piece1, piece2, piece3)
    even = lax.axis_index("gx") % 2 == 0
    odd = iota((8, 128), 1) // EZ % 2 == 1
    faces[...] = jnp.zeros_like(faces)

    def both(rows, f):
        side = odd[:1] if f else jnp.logical_not(odd[:1])
        return jnp.where(side, rows, pltpu.roll(rows, 96 if f else 32, 1))

    for a, piece in enumerate(pieces):
        for f in range(2):
            base = 64 * a + 32 * f
            inner = both(piece[FACE_X:KAPPA, :], f)
            ends = [both(piece[HALF:FACE_X, :], g) for g in range(2)]
            for k in range(5):
                r = base + 5 * k
                node = 5 * k + 4 * f
                faces[r : r + 1, :] = ends[0][node : node + 1]
                faces[r + 1 : r + 4, :] = inner[3 * k : 3 * k + 3]
                faces[r + 4 : r + 5, :] = ends[1][node : node + 1]
    for a, piece in enumerate(pieces):
        line[HALF * a : HALF * a + HALF, :] = piece[:HALF, :]
        line[LINE_KAPPA + 16 * a : LINE_KAPPA + 16 * a + 16, :] = piece[KAPPA:, :]
        line[LINE_Y + 25 * a : LINE_Y + 25 * a + 25, :] = piece[HALF:FACE_X, :]
        flags = [flag_lanes(piece[61:62, :], slot) for slot in range(2)]
        gains = [face_gains(flags[d], 0, d, 5) for d in range(2)]
        next_first = even if a % 2 == 0 else jnp.logical_not(even)
        for f in range(2):
            one = faces[64 * (a ^ 1) + 32 * (1 - f) : 64 * (a ^ 1) + 32 * (1 - f) + 32, :]
            three = faces[64 * (a ^ 3) + 32 * (1 - f) : 64 * (a ^ 3) + 32 * (1 - f) + 32, :]
            near = jnp.where(next_first, one, three) if f else jnp.where(next_first, three, one)
            term = gains[f] * near
            for k in range(5):
                node = 25 * k + 20 * f
                side = odd[:5] if node >= HALF else jnp.logical_not(odd[:5])
                r = HALF * a + node % HALF
                line[r : r + 5, :] = line[r : r + 5, :] + jnp.where(side, term[5 * k : 5 * k + 5], 0.0)
    line[LINE_Y + 100 :, :] = jnp.zeros((4, 128), F32)


def halves_kernel(block0, block1, block2, block3, out):
    place_pieces((block0, block1, block2, block3), out, LINE_KAPPA, 16, 16)


def widen(low, high, odd):
    return jnp.where(odd, pltpu.roll(high, 32, 1), low), jnp.where(odd, high, pltpu.roll(low, 96, 1))


def assemble_kernel(block0, block1, block2, block3, field, pieces, edges, traces):
    blocks = (block0, block1, block2, block3)
    place_pieces(blocks, pieces, 0, HALF, HALF)
    place_pieces(blocks, edges, LINE_Y, 25, 32)
    lanes = Lanes()
    for source, size, rows, target, apart in ((edges, 32, 25, traces, 25), (pieces, HALF, HALF, field, HALF)):
        for r in range(rows):
            first, second = widen(rows_of(source, size, r, 0), rows_of(source, size, r, 1), lanes.odd)
            target[tile(r), :] = first
            target[tile(apart + r), :] = second
    got = field[tile(126), :]
    across = pltpu.roll(got, 64, 1)
    gains = [
        face_gains(jnp.where(lanes.lane < 64, got, across), 1, 0, 5),
        face_gains(jnp.where(lanes.lane < 64, across, got), 1, 1, 5),
    ]
    for k in range(5):
        for i in range(5):
            lower, upper = traces[tile(5 * k + i), :], traces[tile(25 + 5 * k + i), :]
            node = 25 * k + 5 * i
            field[tile(node), :] = field[tile(node), :] + gains[0] * lanes.y_before(upper)
            field[tile(node + 4), :] = field[tile(node + 4), :] + gains[1] * lanes.y_after(lower)


def setup_kernel(field, own_halves, other_halves, coefs, kap):
    sec = lax.axis_index("section")
    lanes = Lanes()
    group, lane = lanes.group, lanes.lane
    flags = []
    for r in range(3):
        got = field[tile(125 + r), :]
        across = pltpu.roll(got, 64, 1)
        flags += [jnp.where(lane < 64, got, across), jnp.where(lane < 64, across, got)]
    for r in range(16):
        pairs = [[rows_of(ref, 16, r, h) for h in range(2)] for ref in (own_halves, other_halves)]
        for half in range(2):
            turned = []
            for h in range(2):
                got = jnp.where(sec == half, pairs[0][h], pairs[1][h])
                turned.append([pltpu.roll(got, 32 * m, 1) if m else got for m in range(4)])
            for q in range(4):
                value = choose(group, [turned[g % 2][(g - q) % 4] for g in range(4)])
                kap[tile(q * 32 + half * 16 + r), :] = value
    for p, n in enumerate((5, 3, 2)):
        stride = 4 // (n - 1)
        gains = [face_gains(flags[d], d // 2, d % 2, n) for d in range(6)]
        rows = []
        for d in range(3):
            coefs[tile(GAINS[p] + 2 * d), :] = gains[2 * d]
            coefs[tile(GAINS[p] + 2 * d + 1), :] = gains[2 * d + 1]
            table = element_matrix(n, d)
            row = [jnp.full((8, 128), float(table[m, m]), F32) for m in range(n)]
            row[0] = row[0] + gains[2 * d]
            row[n - 1] = row[n - 1] + gains[2 * d + 1]
            rows.append(row)
        along = jnp.stack(rows[1])
        for k in range(n):
            for i in range(n):
                line = load(kap, k * 25 * stride + i * stride * 5, 5)
                line = jnp.stack([line[j * stride] for j in range(n)])
                value = line + (along + (rows[2][k] + rows[0][i]))
                scale = 1.0 / (1.0 + STEP_SIZE * JACOBI_SCALE * value)
                store(coefs, DIAGS[p] + (k * n + i) * n, value)
                store(coefs, DIAGS[p] + n**3 + (k * n + i) * n, scale * (1.0 / CENTRE))


def cycle_kernel(coefs, assembled, fields, *scratch):
    sec = lax.axis_index("section")
    my_gx, my_gy = lax.axis_index("gx"), lax.axis_index("gy")
    levels = [Level(n, scratch[4 * p : 4 * p + 4]) for p, n in enumerate((5, 3, 2))]
    half = scratch[12]
    lanes = Lanes()
    lane = lanes.lane
    blocks = split_sections()[3]

    def lanes_of(upper, lower):
        return jnp.where(lane < 64, jnp.where(sec == 0, upper[0], upper[1]), jnp.where(sec == 0, lower[0], lower[1]))

    entry = [[[float(STEP_SIZE * blocks[2 * p + a, 2 * p + b]) for p in range(2)] for b in range(2)] for a in range(2)]
    same = lanes_of(entry[0][0], entry[1][1])
    swap = lanes_of(entry[0][1], entry[1][0])
    first_rho = RADIUS / CENTRE
    second_rho = 1.0 / (2.0 * CENTRE / RADIUS - first_rho)
    keep = 1.0 + second_rho * first_rho
    push = 2.0 * second_rho / RADIUS * CENTRE
    for p, level in enumerate(levels):
        size = level.count**3
        level.gains = [-coefs[tile(GAINS[p] + d), :] for d in range(6)]
        level.diag = lambda first, count, p=p: load(coefs, DIAGS[p] + first, count)
        level.jac = lambda first, count, p=p, size=size: load(coefs, DIAGS[p] + size + first, count)

    def begin(level, source):
        n = level.count
        for first in range(0, n**3, n):
            f = load(source, first, n)
            store(level.dir, first, level.jac(first, n) * f)
            store(level.res, first, f)
            store(level.x, first, jnp.zeros_like(f))

    def apply(level, smooth):
        n = level.count
        kx, ky, kz = level.tables
        gains = level.gains
        source = level.dir if smooth else level.x
        def tree(terms):
            while len(terms) > 1:
                pairs = [a + b for a, b in zip(terms[::2], terms[1::2])]
                terms = pairs + terms[len(terms) // 2 * 2 :]
            return terms[0]

        def sums(k):
            def line_at(i):
                return load(source, (k * n + i) * n, n)

            totals = []
            for i in range(n):
                first = (k * n + i) * n
                v = line_at(i)
                along_x = [float(kx[i, m]) * line_at(m) for m in range(n) if m != i]
                if i == 0:
                    along_x.append(gains[0] * lanes.x_before(line_at(n - 1)))
                if i == n - 1:
                    along_x.append(gains[1] * lanes.x_after(line_at(0)))
                along_z = [float(kz[k, m]) * load(source, (m * n + i) * n, n) for m in range(n) if m != k]
                if k == 0:
                    along_z.append(gains[4] * lanes.z_before(load(source, ((n - 1) * n + i) * n, n)))
                if k == n - 1:
                    along_z.append(gains[5] * lanes.z_after(load(source, i * n, n)))
                along_y = []
                for j in range(n):
                    terms = [float(ky[j, m]) * v[m] for m in range(n) if m != j]
                    if j == 0:
                        terms.append(gains[2] * lanes.y_before(v[n - 1]))
                    if j == n - 1:
                        terms.append(gains[3] * lanes.y_after(v[0]))
                    along_y.append(tree(terms))
                totals.append(tree([level.diag(first, n) * v, tree(along_x), tree(along_z), jnp.stack(along_y)]))
            return totals

        def update(k, totals):
            moved = [pltpu.roll(total, 64, 2) for total in totals]
            for i in range(n):
                first = (k * n + i) * n
                v = load(source, first, n)
                image = v + (same * totals[i] + swap * moved[i])
                if smooth:
                    scaled = level.jac(first, n) * (load(level.res, first, n) - image)
                    store(level.x, first, (load(level.x, first, n) + keep * v) + push * scaled)
                else:
                    rest = load(level.f, first, n) - image
                    store(level.res, first, rest)
                    store(level.dir, first, level.jac(first, n) * rest)

        if n == 5:
            for k in range(n):
                update(k, sums(k))
        else:
            for k, totals in enumerate([sums(k) for k in range(n)]):
                update(k, totals)

    def combine(weights, parts):
        total = None
        for weight, part in zip(weights, parts):
            if abs(weight) > 1e-14:
                term = part if abs(weight - 1.0) < 1e-14 else float(weight) * part
                total = term if total is None else total + term
        return total

    def change(table, source, target, add):
        m, n = table.shape
        for i in range(n):
            parts = [load(source, i * n + k * n * n, n) for k in range(n)]
            for k in range(m):
                store(half, i * n + k * n * n, combine(table[k], parts))
        for k in range(m):
            parts = [load(half, k * n * n + i * n, n) for i in range(n)]
            for i in range(m):
                line = combine(table[i], parts)
                value = jnp.stack([combine(table[j], [line[a] for a in range(n)]) for j in range(m)])
                first = k * m * m + i * m
                store(target, first, load(target, first, m) + value if add else value)

    def down(n, m):
        fine_nodes, fine_weights = lobatto(n)
        coarse_nodes, coarse_weights = lobatto(m)
        table = lagrange_table(coarse_nodes, fine_nodes)
        return (1.0 / coarse_weights)[:, None] * table.T * fine_weights[None, :]

    def up(m, n):
        return lagrange_table(lobatto(m)[0], lobatto(n)[0])

    def solve(p):
        level = levels[p]
        if p == 2:
            apply(level, True)
            return
        below = levels[p + 1]

        def step(t, carry):
            @pl.when(t != 1)
            def _():
                apply(level, True)

            @pl.when((t != 2) | (p == 0))
            def _():
                apply(level, False)

            @pl.when(t == 0)
            def _():
                n, m = level.count, below.count
                change(down(n, m), level.res, below.f, False)
                begin(below, below.f)
                solve(p + 1)
                change(up(m, n), below.x, level.x, True)
            return carry
        lax.fori_loop(0, 3, step, 0)

    fine = levels[0]
    fine.f = assembled
    begin(fine, assembled)
    solve(0)

    for first in range(0, 125, 5):
        store(fields, first, load(fine.res, first, 5))
    column = (my_gx % 2) * 4 + my_gy
    fields[FIELD : FIELD + 125, :] = fine.x[pl.ds(column, 125, stride=8), :]
    fields[FIELD + 125 : FIELD + 128, :] = jnp.zeros((3, 128), F32)


def pair_weights():
    cross = split_sections()[4]
    return jnp.where(iota((8, 128), 1) < 64, float(cross[0]), float(cross[1]))


def column_factors(p):
    sec = lax.axis_index("section")
    whole = split_sections()[0]
    lane = iota((25, 128), 1)
    here = lane // EZ % 2 == lax.axis_index("gx") // 2
    factors = []
    for s in range(2):
        parts = []
        for mine in range(2):
            t = whole[2 * mine + s]
            q = mine if p == 0 else 1 - mine
            parts.append(jnp.where(lane < 64, float(t[2 * q]), float(t[2 * q + 1])))
        factors.append(jnp.where(here, jnp.where(sec == 0, parts[0], parts[1]), 0.0))
    return factors


def column_rows(k):
    column = (lax.axis_index("gx") % 2) * 4 + lax.axis_index("gy")
    return pl.ds(k * 200 + column, 25, stride=8)


def raw_order(k):
    lane = iota((256, 160), 0)
    return (iota((256, 160), 1) == 5 * (lane % EZ) + k + lane // 128).astype(F32)


def early_kernel(own, own_start, other_start, sums, column_out, cols):
    weights = pair_weights()
    cols[...] = jnp.zeros_like(cols)
    total = jnp.zeros((192, 160), F32)
    own_factors, other_factors = column_factors(0), column_factors(1)
    for k in range(5):
        where = column_rows(k)
        z = own[FIELD + k * 25 : FIELD + k * 25 + 25, :]
        start, other = own_start[where, :], other_start[where, :]
        w = start - own[where, :]
        side = slice(0, 128) if k % 2 == 0 else slice(128, 256)
        for s in range(2):
            cols[s * 32 : s * 32 + 25, side] = own_factors[s] * z
            cols[64 + s * 32 : 64 + s * 32 + 25, side] = own_factors[s] * start + other_factors[s] * other
            cols[128 + s * 32 : 128 + s * 32 + 25, side] = own_factors[s] * w
        if k % 2 == 1:
            total = total + split_dot(cols[...], raw_order(k - 1))
    cols[:, 128:] = jnp.zeros((192, 128), F32)
    total = total + split_dot(cols[...], raw_order(4))
    column_out[...] = total
    nothing = jnp.zeros((8, 128), F32)
    uppers, sizes = [nothing] * 5, [nothing] * 5
    for r in range(125):
        c, d = own_start[tile(r), :], other_start[tile(r), :]
        a = c - own[tile(r), :]
        uppers[r % 5] = uppers[r % 5] + a * (c + weights * d)
        sizes[r % 5] = sizes[r % 5] + ((c * c + d * d) + 2.0 * (weights * (c * d)))
    sums[0:8, :] = sum(uppers)
    sums[8:16, :] = sum(sizes)


def finish_kernel(own, other, own_start, other_start, sums, column, guess, sol, res_out, arnoldi, cols, outs):
    sec = lax.axis_index("section")
    weights = pair_weights()
    cols[...] = jnp.zeros_like(cols)
    total = jnp.zeros((128, 160), F32)
    factors = column_factors(1)
    for k in range(5):
        where = column_rows(k)
        z = other[FIELD + k * 25 : FIELD + k * 25 + 25, :]
        w = other_start[where, :] - other[where, :]
        side = slice(0, 128) if k % 2 == 0 else slice(128, 256)
        for s in range(2):
            cols[s * 32 : s * 32 + 25, side] = factors[s] * z
            cols[64 + s * 32 : 64 + s * 32 + 25, side] = factors[s] * w
        if k % 2 == 1:
            total = total + split_dot(cols[...], raw_order(k - 1))
    cols[:, 128:] = jnp.zeros((128, 128), F32)
    total = total + split_dot(cols[...], raw_order(4))
    nothing = jnp.zeros((8, 128), F32)
    uppers = [nothing] * 5
    for r in range(125):
        c, d = own_start[tile(r), :], other_start[tile(r), :]
        b = d - other[tile(r), :]
        uppers[r % 5] = uppers[r % 5] + b * (d + weights * c)

    mine, theirs = sums[0:8, :], sum(uppers)
    size = jnp.sum(sums[8:16, :], keepdims=True)
    upper = jnp.sum(mine + theirs, keepdims=True) / size
    rests = [nothing] * 5
    for r in range(125):
        c, d = own_start[tile(r), :], other_start[tile(r), :]
        a = (c - own[tile(r), :]) - upper * c
        b = (d - other[tile(r), :]) - upper * d
        rests[r % 5] = rests[r % 5] + ((a * a + b * b) + 2.0 * (weights * (a * b)))
    rest = jnp.sum(sum(rests), keepdims=True)
    beta = jnp.sqrt(size)
    lower = jnp.sqrt(rest) / beta
    weight = upper / (upper * upper + lower * lower)
    entries = float(125 * EZ * COLS * 4)
    for place_out, value in enumerate((beta * (1.0 / math.sqrt(entries)), upper, lower)):
        arnoldi[place_out] = value[0, 0]
    outs[:64, :] = weight * (column[:64, :] + total[:64])
    outs[64:, :] = column[64:128, :] - weight * (column[128:, :] + total[64:])
    for i in range(5):
        for j in range(5):
            r = 5 * i + j
            for s in range(2):
                sol[i, j, s : s + 1, :] = guess[i, j, s : s + 1, :] + outs[s * 32 + r : s * 32 + r + 1, :]
                res_out[i, j, s : s + 1, :] = outs[64 + s * 32 + r : 64 + s * 32 + r + 1, :]


def plain_call(kernel, name, rows, scratch, operands, cost=1_000_000):
    return pl.pallas_call(
        kernel,
        out_shape=jax.ShapeDtypeStruct((rows, 128), F32),
        in_specs=[VMEM] * len(operands),
        out_specs=VMEM,
        scratch_shapes=[pltpu.VMEM((r, 128), F32) for r in scratch],
        compiler_params=limit(16),
        cost_estimate=pl.CostEstimate(flops=cost, bytes_accessed=cost, transcendentals=0),
        name=name,
    )(*operands)


def cycle(coefs, assembled):
    scratch = []
    for n in (5, 3, 2):
        scratch += [pltpu.VMEM((n**3 * 8, 128), F32)] * 4
    scratch += [pltpu.VMEM((FIELD, 128), F32)]
    return pl.pallas_call(
        cycle_kernel,
        out_shape=jax.ShapeDtypeStruct((FIELD + 128, 128), F32),
        in_specs=[VMEM] * 2,
        out_specs=VMEM,
        scratch_shapes=scratch,
        compiler_params=limit(24),
        cost_estimate=pl.CostEstimate(flops=40_000_000, bytes_accessed=30_000_000, transcendentals=0),
        name="cycle",
    )(coefs, assembled)


def early(own, own_start, other_start):
    return pl.pallas_call(
        early_kernel,
        out_shape=[jax.ShapeDtypeStruct((16, 128), F32), jax.ShapeDtypeStruct((192, 160), F32)],
        in_specs=[VMEM] * 3,
        out_specs=[VMEM] * 2,
        scratch_shapes=[pltpu.VMEM((192, 256), F32)],
        compiler_params=limit(16),
        cost_estimate=pl.CostEstimate(flops=4_000_000, bytes_accessed=4_000_000, transcendentals=0),
        name="early",
    )(own, own_start, other_start)


def finish(own, other, own_start, other_start, sums, column, guess):
    return pl.pallas_call(
        finish_kernel,
        out_shape=[
            jax.ShapeDtypeStruct(guess.shape, F32),
            jax.ShapeDtypeStruct(guess.shape, F32),
            jax.ShapeDtypeStruct((3,), F32),
        ],
        in_specs=[VMEM] * 7,
        out_specs=[VMEM, VMEM, pl.BlockSpec(memory_space=pltpu.SMEM)],
        scratch_shapes=[pltpu.VMEM((128, 256), F32), pltpu.VMEM((128, 160), F32)],
        compiler_params=limit(24),
        name="finish",
    )(own, other, own_start, other_start, sums, column, guess)


def exchange(x, axis, bits):
    return lax.ppermute(x, axis, [(n, n ^ bits) for n in range(lax.axis_size(axis))])


def gathered_body(rhs, guess, kappa, bc_flags):
    rhs, guess = (jnp.transpose(v, (1, 2, 0, 3)) for v in (rhs, guess))
    mine, theirs = local_part(rhs, guess, kappa, bc_flags)
    got, mine, kappa_piece = lax.optimization_barrier((exchange(theirs, "section", 1), *part(mine)))
    piece = jnp.concatenate([mine + got, kappa_piece])
    pieces = [piece] + [exchange(piece, "gx", bits) for bits in (1, 2, 3)]
    line = plain_call(line_kernel, "line", LINE, [4 * 64], pieces[::-1])
    blocks = [line] + [exchange(line, "gy", bits) for bits in (1, 2, 3)]
    halves = plain_call(halves_kernel, "halves", COLS * 16, [], blocks)
    other_halves = exchange(halves, "section", 1)
    start = plain_call(assemble_kernel, "assemble", 128 * 8, [COLS * HALF, COLS * 32, 50 * 8], blocks, 4_000_000)
    start, other_halves = lax.optimization_barrier((start, other_halves))
    coefs = plain_call(setup_kernel, "setup", REGISTERS * 8, [128 * 8], (start, halves, other_halves))
    other_start = exchange(start, "section", 1)
    own, other_start = lax.optimization_barrier((cycle(coefs, start), other_start))
    sums, column = early(own, start, other_start)
    sol, res, arnoldi = finish(own, exchange(own, "section", 1), start, other_start, sums, column, guess)
    sol, res = (jnp.transpose(v, (2, 0, 1, 3)) for v in (sol, res))
    return sol, res, arnoldi


def solution(mesh):
    placed = (
        P("section", "gx", "gy", None),
        P("section", "gx", "gy", None),
        P("gx", "gy", None),
        P(None, "gx", "gy", None),
    )
    sizes = (mesh.shape["section"], mesh.shape["gx"], mesh.shape["gy"])

    def step(rhs, guess, kappa, bc_flags):
        fits = sizes == (2, 4, 4) and rhs.shape == (4, 20, 20, 160)
        return jax.shard_map(
            gathered_body if fits else stepwise,
            mesh=mesh,
            in_specs=placed,
            out_specs=(P("section", "gx", "gy", None), P("section", "gx", "gy", None), P()),
            check_vma=False,
        )(rhs, guess, kappa, bc_flags)

    return step
```

```python
from functools import partial
import math

import jax
import jax.numpy as jnp
import numpy as np
from jax import lax
from jax.experimental import pallas as pl
from jax.experimental.pallas import tpu as pltpu
from jax.sharding import PartitionSpec as P

ADVECT = (1.0, 0.7, 0.5)
DIFFUSE = 0.05
STEP_SIZE = 0.2
JACOBI_SCALE = 0.25
CHEB_LOW = 0.25
CHEB_HIGH = 2.0
LETTERS = "abcdef"


def extended(x, sides, width):
    for axis, dim in sides:
        peers, length = (lax.axis_size(axis), x.shape[dim])
        up = [(i, (i + 1) % peers) for i in range(peers)]
        down = [(j, i) for i, j in up]
        last = lax.slice_in_dim(x, length - width, length, axis=dim)
        leading = lax.slice_in_dim(x, 0, width, axis=dim)
        before = lax.ppermute(last, axis, up)
        after = lax.ppermute(leading, axis, down)
        x = jnp.concatenate([before, x, after], axis=dim)
    return x


def lobatto(count):
    if count == 5:
        inner = math.sqrt(3.0 / 7.0)
        return (
            np.array([-1.0, -inner, 0.0, inner, 1.0]),
            np.array([0.1, 49.0 / 90.0, 32.0 / 45.0, 49.0 / 90.0, 0.1]),
        )
    if count == 3:
        return (np.array([-1.0, 0.0, 1.0]), np.array([1.0 / 3.0, 4.0 / 3.0, 1.0 / 3.0]))
    return (np.array([-1.0, 1.0]), np.array([1.0, 1.0]))


def lagrange_table(nodes, points):
    table = np.ones((len(points), len(nodes)))
    for column in range(len(nodes)):
        for other in range(len(nodes)):
            if other != column:
                table[:, column] *= (points - nodes[other]) / (nodes[column] - nodes[other])
    return table


def slope_table(nodes):
    total = len(nodes)
    factor = np.array(
        [np.prod([nodes[i] - nodes[k] for k in range(total) if k != i]) for i in range(total)]
    )
    table = np.zeros((total, total))
    for row in range(total):
        for column in range(total):
            if row != column:
                table[row, column] = factor[row] / factor[column] / (nodes[row] - nodes[column])
        table[row, row] = -np.sum(table[row])
    return table


def element_matrix(count, direction):
    nodes, weights = lobatto(count)
    slopes = slope_table(nodes)
    stiffness = (1.0 / weights)[:, None] * (slopes.T @ (weights[:, None] * slopes))
    return ADVECT[direction] * slopes + DIFFUSE * stiffness


def legendre_pair(point, order):
    values = [1.0, point]
    slopes = [0.0, 1.0]
    for index in range(1, order):
        values.append(
            ((2 * index + 1) * point * values[index] - index * values[index - 1]) / (index + 1)
        )
        slopes.append(slopes[index - 1] + (2 * index + 1) * values[index])
    return (values, slopes)


def radau_nodes():
    starts = [0.0885879595127039, 0.4094668644407347, 0.7876594617608471]
    found = []
    for start in starts:
        point = start
        for sweep in range(30):
            values, slopes = legendre_pair(2.0 * point - 1.0, 4)
            change = (values[4] - values[3]) / (2.0 * (slopes[4] - slopes[3]))
            point = point - change
        found.append(point)
    found.append(1.0)
    return found


def poly_times(coefs, root):
    result = [0.0] * (len(coefs) + 1)
    for index in range(len(coefs)):
        result[index + 1] += coefs[index]
        result[index] -= root * coefs[index]
    return result


def radau_matrix():
    order = 4
    nodes = radau_nodes()
    matrix = np.zeros((order, order))
    for column in range(order):
        coefs = [1.0]
        denominator = 1.0
        for other in range(order):
            if other != column:
                coefs = poly_times(coefs, nodes[other])
                denominator *= nodes[column] - nodes[other]
        for row in range(order):
            upper_end = nodes[row]
            integral = 0.0
            for index in range(len(coefs)):
                integral += coefs[index] * upper_end ** (index + 1) / (index + 1)
            matrix[row, column] = integral / denominator
    return matrix


def node_einsum(table, field, axis):
    labels = LETTERS[: field.ndim]
    source = labels[: axis + 1] + "j" + labels[axis + 2 :]
    target = labels[: axis + 1] + "i" + labels[axis + 2 :]
    return jnp.einsum(
        "ij," + source + "->" + target,
        jnp.asarray(table, jnp.float32),
        field,
        precision=lax.Precision.HIGHEST,
    )


def apply_along(field, axis, count, table):
    shape = field.shape
    split = shape[:axis] + (shape[axis] // count, count) + shape[axis + 1 :]
    mapped = node_einsum(table, field.reshape(split), axis)
    return mapped.reshape(
        shape[:axis] + (mapped.shape[axis] * mapped.shape[axis + 1],) + shape[axis + 1 :]
    )


def line_part(field, axis, count, table, left_gain, right_gain, left_edge, right_edge):
    shape = field.shape
    elements = shape[axis] // count
    split = field.reshape(shape[:axis] + (elements, count) + shape[axis + 1 :])
    linear = node_einsum(table, split, axis)
    first = lax.index_in_dim(split, 0, axis + 1, keepdims=False)
    last = lax.index_in_dim(split, count - 1, axis + 1, keepdims=False)
    before = jnp.concatenate(
        [jnp.expand_dims(left_edge, axis), lax.slice_in_dim(last, 0, elements - 1, axis=axis)], axis
    )
    after = jnp.concatenate(
        [lax.slice_in_dim(first, 1, elements, axis=axis), jnp.expand_dims(right_edge, axis)], axis
    )
    front = jnp.expand_dims(left_gain * (first - before), axis + 1)
    back = jnp.expand_dims(right_gain * (last - after), axis + 1)
    if count > 2:
        middle_shape = list(front.shape)
        middle_shape[axis + 1] = count - 2
        pieces = [front, jnp.zeros(middle_shape, jnp.float32), back]
    else:
        pieces = [front, back]
    return (linear + jnp.concatenate(pieces, axis + 1)).reshape(shape)


def diag_along(shape, axis, count, table, left_gain, right_gain):
    elements = shape[axis] // count
    split = shape[:axis] + (elements, count) + shape[axis + 1 :]
    profile = [1] * len(split)
    profile[axis + 1] = count
    diagonal_entries = np.array([table[index, index] for index in range(count)])
    base = jnp.broadcast_to(jnp.asarray(diagonal_entries, jnp.float32).reshape(profile), split)
    front = jnp.expand_dims(left_gain, axis + 1)
    back = jnp.expand_dims(right_gain, axis + 1)
    if count > 2:
        middle_shape = list(front.shape)
        middle_shape[axis + 1] = count - 2
        pieces = [front, jnp.zeros(middle_shape, jnp.float32), back]
    else:
        pieces = [front, back]
    return (base + jnp.concatenate(pieces, axis + 1)).reshape(shape)


def level_kappa(kappa, count):
    if count == 5:
        return kappa
    picks = np.array([0, 2, 4]) if count == 3 else np.array([0, 4])
    extents = [extent // 5 for extent in kappa.shape]
    grouped = kappa.reshape(extents[0], 5, extents[1], 5, extents[2], 5)
    for axis in (1, 3, 5):
        grouped = jnp.take(grouped, picks, axis=axis)
    return grouped.reshape(extents[0] * count, extents[1] * count, extents[2] * count)


def face_plane(face, direction, count):
    plane = face.astype(jnp.float32)
    for axis in range(3):
        if axis != direction:
            plane = jnp.repeat(plane, count, axis=axis)
    return plane


def build_level(kappa, flags, count):
    nodes, weights = lobatto(count)
    kappa_level = level_kappa(kappa, count)
    tables, lefts, rights = ([], [], [])
    diagonal = kappa_level
    for direction in range(3):
        table = element_matrix(count, direction)
        lower = face_plane(flags[2 * direction], direction, count)
        upper = face_plane(flags[2 * direction + 1], direction, count)
        left_gain = (ADVECT[direction] * (1.0 + lower) / 2.0 + DIFFUSE * count * count) / float(
            weights[0]
        )
        right_gain = (DIFFUSE * count * count - ADVECT[direction] * (1.0 - upper) / 2.0) / float(
            weights[-1]
        )
        tables.append(table)
        lefts.append(left_gain)
        rights.append(right_gain)
        diagonal = diagonal + diag_along(
            kappa_level.shape, direction, count, table, left_gain, right_gain
        )
    scale = 1.0 / (1.0 + STEP_SIZE * JACOBI_SCALE * diagonal)
    return (count, tables, lefts, rights, kappa_level, scale)


def restrict(field, fine_count, coarse_count):
    fine_nodes, fine_weights = lobatto(fine_count)
    coarse_nodes, coarse_weights = lobatto(coarse_count)
    table = (
        (1.0 / coarse_weights)[:, None]
        * lagrange_table(coarse_nodes, fine_nodes).T
        * fine_weights[None, :]
    )
    for axis in range(field.ndim - 3, field.ndim):
        field = apply_along(field, axis, fine_count, table)
    return field


def prolong(field, coarse_count, fine_count):
    fine_nodes, fine_weights = lobatto(fine_count)
    coarse_nodes, coarse_weights = lobatto(coarse_count)
    table = lagrange_table(coarse_nodes, fine_nodes)
    for axis in range(field.ndim - 3, field.ndim):
        field = apply_along(field, axis, coarse_count, table)
    return field


def chebyshev(rhs, start, level, operator):
    centre = (CHEB_HIGH + CHEB_LOW) / 2.0
    radius = (CHEB_HIGH - CHEB_LOW) / 2.0
    ratio = centre / radius
    first_rho = 1.0 / ratio
    second_rho = 1.0 / (2.0 * ratio - first_rho)
    scale = level[5]
    if start is None:
        remain = rhs
    else:
        remain = rhs - operator(start, level)
    step = scale * remain / centre
    guess = step if start is None else start + step
    remain = remain - operator(step, level)
    step = second_rho * first_rho * step + 2.0 * second_rho / radius * scale * remain
    return guess + step


def vcycle(rhs, levels, operator):
    fine, middle, coarse = levels
    fine_x = chebyshev(rhs, None, fine, operator)
    middle_rhs = restrict(rhs - operator(fine_x, fine), 5, 3)
    middle_x = chebyshev(middle_rhs, None, middle, operator)
    coarse_rhs = restrict(middle_rhs - operator(middle_x, middle), 3, 2)
    coarse_x = chebyshev(coarse_rhs, None, coarse, operator)
    middle_x = chebyshev(middle_rhs, middle_x + prolong(coarse_x, 2, 3), middle, operator)
    return chebyshev(rhs, fine_x + prolong(middle_x, 3, 5), fine, operator)


def spatial(field, level):
    count, tables, lefts, rights, kappa_level, scale = level
    padded = extended(field, (("gx", 1), ("gy", 2)), 1)
    total = kappa_level * field
    total = total + line_part(
        field,
        1,
        count,
        tables[0],
        lefts[0],
        rights[0],
        padded[:, 0, 1:-1, :],
        padded[:, -1, 1:-1, :],
    )
    total = total + line_part(
        field,
        2,
        count,
        tables[1],
        lefts[1],
        rights[1],
        padded[:, 1:-1, 0, :],
        padded[:, 1:-1, -1, :],
    )
    total = total + line_part(
        field, 3, count, tables[2], lefts[2], rights[2], field[:, :, :, -1], field[:, :, :, 0]
    )
    return total


def apply_system(field, level, coupling):
    image = spatial(field, level)
    everyone = lax.all_gather(image, "section", axis=0, tiled=True)
    butcher = jnp.asarray(radau_matrix(), jnp.float32)
    rows = lax.dynamic_slice_in_dim(
        butcher, lax.axis_index("section") * field.shape[0], field.shape[0], 0
    )
    mixed = jnp.einsum("ij,jabc->iabc", rows, everyone, precision=lax.Precision.HIGHEST)
    return field + STEP_SIZE * mixed


def global_total(values):
    return lax.psum(values, ("section", "gx", "gy"))


def stepwise(rhs, guess, kappa, bc_flags):
    levels = [build_level(kappa, bc_flags, count) for count in (5, 3, 2)]
    section_operator = partial(apply_system, coupling=None)
    start_residual = rhs - section_operator(guess, levels[0])
    dofs = float(rhs.size * lax.axis_size("section") * lax.axis_size("gx") * lax.axis_size("gy"))
    beta = jnp.sqrt(global_total(jnp.sum(start_residual * start_residual).reshape(1))[0])
    basis = start_residual / beta
    precond = vcycle(basis, levels, section_operator)
    image = section_operator(precond, levels[0])
    upper = global_total(jnp.sum(image * basis).reshape(1))[0]
    remainder = image - upper * basis
    lower = jnp.sqrt(global_total(jnp.sum(remainder * remainder).reshape(1))[0])
    weight = beta * upper / (upper * upper + lower * lower)
    solution = guess + weight * precond
    residual = start_residual - weight * image
    arnoldi = jnp.stack([beta / math.sqrt(dofs), upper, lower]).astype(jnp.float32)
    return (solution, residual, arnoldi)


EZ = 32
COLS = 16
HALF = 64
FACE_X = HALF + 25
KAPPA = FACE_X + 15
PIECE = KAPPA + 16
LINE_KAPPA = 4 * HALF
LINE_Y = LINE_KAPPA + 4 * 16
LINE = LINE_Y + 104
FIELD = 1000
F32 = jnp.float32


def split_sections():
    matrix = radau_matrix()
    values, vectors = np.linalg.eig(matrix)
    order = [n for n in np.argsort(np.abs(values.imag), kind="stable") if values[n].imag > 0]
    bases = []
    for n in order:
        plane = np.stack([vectors[:, n].real, vectors[:, n].imag], axis=1)
        bases.append(np.linalg.qr(plane)[0])
    left, cross, right = np.linalg.svd(bases[0].T @ bases[1])
    bases = [bases[0] @ left, bases[1] @ right.T]
    for c in range(2):
        sign = np.sign(bases[0][np.argmax(np.abs(bases[0][:, c])), c])
        bases = [np.concatenate([b[:, :c], sign * b[:, c : c + 1], b[:, c + 1 :]], axis=1) for b in bases]
    whole = np.concatenate(bases, axis=1)
    back = np.linalg.inv(whole)
    return whole, back, back @ matrix, back @ matrix @ whole, cross


def iota(shape, dim):
    return lax.broadcasted_iota(jnp.int32, shape, dim)


def exact_dot(a, b):
    return lax.dot_general(
        a, b, (((1,), (0,)), ((), ())), precision=lax.Precision.HIGHEST, preferred_element_type=F32
    )


def split_dot(a, b):
    high = a.astype(jnp.bfloat16)
    rest = a - high.astype(F32)
    middle = rest.astype(jnp.bfloat16)
    low = (rest - middle.astype(F32)).astype(jnp.bfloat16)
    b = b.astype(jnp.bfloat16)
    return sum(
        lax.dot_general(part, b, (((1,), (0,)), ((), ())), preferred_element_type=F32)
        for part in (low, middle, high)
    )


def choose(index, values):
    out = values[-1]
    for place in range(len(values) - 2, -1, -1):
        out = jnp.where(index == place, values[place], out)
    return out


def face_gains(flag, direction, side, count):
    nodes, weights = lobatto(count)
    c, nu = ADVECT[direction], DIFFUSE * count * count
    if side == 0:
        return (c * (1.0 + flag) / 2.0 + nu) * (1.0 / float(weights[0]))
    return (nu - c * (1.0 - flag) / 2.0) * (1.0 / float(weights[-1]))


def row_table():
    kx, ky = (element_matrix(5, d) for d in range(2))
    rows = np.zeros((64, 64))
    for s in range(2):
        for i in range(5):
            for j in range(5):
                r = s * 32 + i * 5 + j
                for m in range(5):
                    rows[r, s * 32 + m * 5 + j] += kx[i, m]
                    rows[r, s * 32 + i * 5 + m] += ky[j, m]
    return rows.astype(np.float32)


def pick_lines(k):
    lane = iota((160, 256), 1)
    return (iota((160, 256), 0) == 5 * (lane % EZ) + k + lane // 128).astype(F32)


def pair_factors(sec, table, own, s):
    upper = iota((32, 128), 1) < 64
    first = jnp.where(upper, float(table[0, s]), float(table[1, s]))
    second = jnp.where(upper, float(table[2, 2 + s]), float(table[3, 2 + s]))
    if not own:
        first = jnp.where(upper, float(table[2, s]), float(table[3, s]))
        second = jnp.where(upper, float(table[0, 2 + s]), float(table[1, 2 + s]))
    return jnp.where(sec == 0, first, second)


def pack_nodes(nodes):
    half = nodes.shape[0] // 2
    odd = iota((half, 128), 1) // EZ % 2 == 1
    return jnp.where(odd, nodes[half:, :], nodes[:half, :])


def fetch(pairs, sems):
    copies = [pltpu.make_async_copy(src, dst, sems.at[n]) for n, (src, dst) in enumerate(pairs)]
    for copy in copies:
        copy.start()
    for copy in copies:
        copy.wait()


def local_kernel(
    rhs_in, guess_in, kappa_in, flags_in, rows_in, mine, theirs,
    rhs, guess, kappa, flags, rows_t, sems, stack, lines, nodes, y_faces, x_faces,
):
    sec = lax.axis_index("section")
    fetch([(rhs_in, rhs), (guess_in, guess), (kappa_in, kappa), (flags_in, flags), (rows_in, rows_t)], sems)
    stack[...] = jnp.zeros_like(stack)
    for i in range(5):
        stack[192 + 5 * i : 197 + 5 * i, :] = kappa[i]
        for j in range(5):
            r = 5 * i + j
            value = guess[i, j]
            left = rhs[i, j] - value
            for s in range(2):
                stack[s * 32 + r : s * 32 + r + 1, :] = left[s : s + 1]
                stack[128 + s * 32 + r : 128 + s * 32 + r + 1, :] = value[s : s + 1]
    stack[64:128, :] = exact_dot(rows_t[...], stack[128:192, :])
    source = stack[...]
    for k in (0, 2, 4):
        shown = split_dot(source, pick_lines(k))
        lines[224 * k : 224 * k + 224, :] = shown[:, :128]
        if k < 4:
            lines[224 * k + 224 : 224 * k + 448, :] = shown[:, 128:]

    def part(k, first):
        return lines[224 * k + first : 224 * k + first + 32, :]

    repeat = (iota((EZ, 128), 1) % EZ == iota((EZ, 128), 0)).astype(F32)
    shown = split_dot(flags[:, 0, 0, :].astype(F32), repeat)
    gains = [face_gains(shown[d : d + 1, :], d // 2, d % 2, 5) for d in range(6)]
    row = iota((32, 128), 0)
    none = jnp.zeros((32, 128), F32)
    own = jnp.where(row < 5, gains[0], jnp.where((row >= 20) & (row < 25), gains[1], none))
    own = own + jnp.where(row % 5 == 0, gains[2], jnp.where(row % 5 == 4, gains[3], none))
    kz = element_matrix(5, 2)
    back, back_matrix = split_sections()[1:3]
    for ref in (nodes, y_faces, x_faces):
        ref[...] = jnp.zeros_like(ref)
    for k in range(5):
        diagonal = part(k, 192) + own
        if k == 0:
            diagonal = diagonal + gains[4]
        if k == 4:
            diagonal = diagonal + gains[5]
        images = []
        for s in range(2):
            first = 128 + 32 * s
            image = diagonal * part(k, first) + part(k, 64 + 32 * s)
            for m in range(5):
                image = image + float(kz[k, m]) * part(m, first)
            if k == 0:
                image = image - gains[4] * pltpu.roll(part(4, first), 1, 1)
            if k == 4:
                image = image - gains[5] * pltpu.roll(part(0, first), 127, 1)
            images.append(image)
        for p, mark in enumerate((True, False)):
            total = jnp.zeros((32, 128), F32)
            trace = jnp.zeros((32, 128), F32)
            for s in range(2):
                total = total + pair_factors(sec, back, mark, s) * part(k, 32 * s)
                factor = pair_factors(sec, STEP_SIZE * back_matrix, mark, s)
                total = total - factor * images[s]
                trace = trace + factor * part(k, 128 + 32 * s)
            nodes[128 * p + 25 * k : 128 * p + 25 * k + 25, :] = total[:25]
            for i in range(5):
                for f in range(2):
                    r = 64 * p + 32 * f + 5 * k + i
                    y_faces[r : r + 1, :] = trace[5 * i + 4 * f : 5 * i + 4 * f + 1]
            for f in range(2):
                r = 32 * p + 16 * f + 3 * k
                x_faces[r : r + 3, :] = trace[20 * f + 1 : 20 * f + 4]
    upper = iota((1, 128), 1) < 64
    for r in range(3):
        nodes[125 + r : 126 + r, :] = jnp.where(upper, shown[2 * r : 2 * r + 1], shown[2 * r + 1 : 2 * r + 2])
    for p, out in enumerate((mine, theirs)):
        out[:HALF, :] = pack_nodes(nodes[128 * p : 128 * p + 128, :])
        out[HALF:FACE_X, :] = pack_nodes(y_faces[64 * p : 64 * p + 64, :])[:25]
        out[FACE_X:KAPPA, :] = pack_nodes(x_faces[32 * p : 32 * p + 32, :])[:15]
    for k in range(5):
        nodes[25 * k : 25 * k + 25, :] = part(k, 192)[:25]
    kappas = choose(iota((32, 128), 1) // EZ, [nodes[32 * q : 32 * q + 32, :] for q in range(4)])
    mine[KAPPA:, :] = jnp.where(sec == 0, kappas[:16], kappas[16:])


def part_kernel(source, piece, kappa):
    piece[...] = source[:KAPPA, :]
    kappa[...] = source[KAPPA:, :]


VMEM = pl.BlockSpec(memory_space=pltpu.VMEM)
HBM = pl.BlockSpec(memory_space=pltpu.HBM)


def limit(mib):
    return pltpu.CompilerParams(vmem_limit_bytes=mib * 2**20)


def local_part(rhs, guess, kappa, flags):
    operands = (rhs, guess, kappa, flags, jnp.asarray(row_table()))
    return pl.pallas_call(
        local_kernel,
        out_shape=[jax.ShapeDtypeStruct((rows, 128), F32) for rows in (PIECE, KAPPA)],
        in_specs=[HBM] * 5,
        out_specs=[VMEM] * 2,
        scratch_shapes=[pltpu.VMEM(o.shape, o.dtype) for o in operands]
        + [
            pltpu.SemaphoreType.DMA((5,)),
            pltpu.VMEM((224, 160), F32),
            pltpu.VMEM((5 * 224, 128), F32),
            pltpu.VMEM((256, 128), F32),
            pltpu.VMEM((128, 128), F32),
            pltpu.VMEM((64, 128), F32),
        ],
        compiler_params=limit(60),
        cost_estimate=pl.CostEstimate(flops=20_000_000, bytes_accessed=8_000_000, transcendentals=0),
        name="local_part",
    )(*operands)


def part(x):
    return pl.pallas_call(
        part_kernel,
        out_shape=[jax.ShapeDtypeStruct((rows, 128), F32) for rows in (KAPPA, 16)],
        in_specs=[VMEM],
        out_specs=[VMEM] * 2,
        compiler_params=limit(16),
        name="part",
    )(x)


class Level:
    def __init__(self, count, refs):
        self.count = count
        self.x, self.dir, self.res, self.f = refs
        self.tables = [element_matrix(count, d) for d in range(3)]
        self.gains = self.diag = self.jac = None


def tile(index):
    return pl.ds(index * 8, 8)


def rows_of(pieces, size, r, h):
    return pieces[pl.ds(8 * h * size + r, 8, stride=size), :]


ORDER_X = ((3, 2), (2, 3), (1, 1))
ORDER_Y = ((1, 2), (2, 1), (3, 3))


def partner(bits):
    return jnp.where(lax.axis_index("section") == 0, bits[0], bits[1])


def place_pieces(blocks, pieces, first, size, room):
    my_gx, my_gy = lax.axis_index("gx"), lax.axis_index("gy")
    for b, block in enumerate(blocks):
        gy = my_gy ^ partner(ORDER_Y[b - 1]) if b else my_gy
        for a in range(4):
            column = (my_gx ^ a) * 4 + gy
            start = pl.multiple_of(column * room, 8)
            pieces[pl.ds(start, size), :] = block[first + a * size : first + a * size + size, :]


class Lanes:
    def __init__(self):
        self.lane = iota((8, 128), 1)
        sub = iota((8, 128), 0)
        self.group = self.lane // EZ
        self.odd = self.group % 2 == 1
        self.element = self.lane % EZ
        self.place = sub % 4
        self.low_half = sub < 4

    def around(self, u):
        turned = pltpu.roll(u, 4, u.ndim - 2)
        far = jnp.where(self.odd, pltpu.roll(turned, 32, u.ndim - 1), pltpu.roll(turned, 96, u.ndim - 1))
        return turned, far

    def x_before(self, u):
        turned, far = self.around(u)
        return jnp.where(self.low_half, far, turned)

    def x_after(self, u):
        turned, far = self.around(u)
        return jnp.where(self.low_half, turned, far)

    def y_before(self, u):
        return jnp.where(self.place == 0, pltpu.roll(u, 5, 0), pltpu.roll(u, 1, 0))

    def y_after(self, u):
        return jnp.where(self.place == 3, pltpu.roll(u, 3, 0), pltpu.roll(u, 7, 0))

    def z_before(self, u):
        return jnp.where(self.element == 0, pltpu.roll(u, 97, u.ndim - 1), pltpu.roll(u, 1, u.ndim - 1))

    def z_after(self, u):
        last = self.element == EZ - 1
        return jnp.where(last, pltpu.roll(u, 31, u.ndim - 1), pltpu.roll(u, 127, u.ndim - 1))


def load(ref, first, count):
    return ref[pl.ds(first * 8, count * 8), :].reshape(count, 8, 128)


def store(ref, first, value):
    ref[pl.ds(first * 8, value.shape[0] * 8), :] = value.reshape(value.shape[0] * 8, 128)


DIAGS = (0, 250, 304)
GAINS = (320, 326, 332)
REGISTERS = 338
CENTRE = (CHEB_HIGH + CHEB_LOW) / 2.0
RADIUS = (CHEB_HIGH - CHEB_LOW) / 2.0


def flag_lanes(row, slot):
    turned = [row] + [pltpu.roll(row, 32 * m, 1) for m in range(1, 4)]
    return choose(iota(row.shape, 1) // EZ, [turned[(g - 2 * slot - 1) % 4] for g in range(4)])


def line_kernel(first, second, third, own, line, faces, sorted_pieces):
    sorted_pieces[:PIECE, :] = own[...]
    for bits, piece in zip(ORDER_X, (first, second, third)):
        sorted_pieces[pl.ds(pl.multiple_of(partner(bits) * PIECE, 8), PIECE), :] = piece[...]
    pieces = [sorted_pieces.at[PIECE * a : PIECE * a + PIECE, :] for a in range(4)]
    even = lax.axis_index("gx") % 2 == 0
    odd = iota((8, 128), 1) // EZ % 2 == 1
    faces[...] = jnp.zeros_like(faces)

    def both(rows, f):
        side = odd[:1] if f else jnp.logical_not(odd[:1])
        return jnp.where(side, rows, pltpu.roll(rows, 96 if f else 32, 1))

    for a, piece in enumerate(pieces):
        for f in range(2):
            base = 64 * a + 32 * f
            inner = both(piece[FACE_X:KAPPA, :], f)
            ends = [both(piece[HALF:FACE_X, :], g) for g in range(2)]
            for k in range(5):
                r = base + 5 * k
                node = 5 * k + 4 * f
                faces[r : r + 1, :] = ends[0][node : node + 1]
                faces[r + 1 : r + 4, :] = inner[3 * k : 3 * k + 3]
                faces[r + 4 : r + 5, :] = ends[1][node : node + 1]
    for a, piece in enumerate(pieces):
        line[HALF * a : HALF * a + HALF, :] = piece[:HALF, :]
        line[LINE_KAPPA + 16 * a : LINE_KAPPA + 16 * a + 16, :] = piece[KAPPA:, :]
        line[LINE_Y + 25 * a : LINE_Y + 25 * a + 25, :] = piece[HALF:FACE_X, :]
        flags = [flag_lanes(piece[61:62, :], slot) for slot in range(2)]
        gains = [face_gains(flags[d], 0, d, 5) for d in range(2)]
        next_first = even if a % 2 == 0 else jnp.logical_not(even)
        for f in range(2):
            one = faces[64 * (a ^ 1) + 32 * (1 - f) : 64 * (a ^ 1) + 32 * (1 - f) + 32, :]
            three = faces[64 * (a ^ 3) + 32 * (1 - f) : 64 * (a ^ 3) + 32 * (1 - f) + 32, :]
            near = jnp.where(next_first, one, three) if f else jnp.where(next_first, three, one)
            term = gains[f] * near
            for k in range(5):
                node = 25 * k + 20 * f
                side = odd[:5] if node >= HALF else jnp.logical_not(odd[:5])
                r = HALF * a + node % HALF
                line[r : r + 5, :] = line[r : r + 5, :] + jnp.where(side, term[5 * k : 5 * k + 5], 0.0)
    line[LINE_Y + 100 :, :] = jnp.zeros((4, 128), F32)


def halves_kernel(block0, block1, block2, block3, out):
    place_pieces((block0, block1, block2, block3), out, LINE_KAPPA, 16, 16)


def widen(low, high, odd):
    return jnp.where(odd, pltpu.roll(high, 32, 1), low), jnp.where(odd, high, pltpu.roll(low, 96, 1))


def assemble_kernel(block0, block1, block2, block3, field, pieces, edges, traces):
    blocks = (block0, block1, block2, block3)
    place_pieces(blocks, pieces, 0, HALF, HALF)
    place_pieces(blocks, edges, LINE_Y, 25, 32)
    lanes = Lanes()
    for source, size, rows, target, apart in ((edges, 32, 25, traces, 25), (pieces, HALF, HALF, field, HALF)):
        for r in range(rows):
            first, second = widen(rows_of(source, size, r, 0), rows_of(source, size, r, 1), lanes.odd)
            target[tile(r), :] = first
            target[tile(apart + r), :] = second
    got = field[tile(126), :]
    across = pltpu.roll(got, 64, 1)
    gains = [
        face_gains(jnp.where(lanes.lane < 64, got, across), 1, 0, 5),
        face_gains(jnp.where(lanes.lane < 64, across, got), 1, 1, 5),
    ]
    for k in range(5):
        for i in range(5):
            lower, upper = traces[tile(5 * k + i), :], traces[tile(25 + 5 * k + i), :]
            node = 25 * k + 5 * i
            field[tile(node), :] = field[tile(node), :] + gains[0] * lanes.y_before(upper)
            field[tile(node + 4), :] = field[tile(node + 4), :] + gains[1] * lanes.y_after(lower)


def setup_kernel(field, own_halves, other_halves, coefs, kap):
    sec = lax.axis_index("section")
    lanes = Lanes()
    group, lane = lanes.group, lanes.lane
    flags = []
    for r in range(3):
        got = field[tile(125 + r), :]
        across = pltpu.roll(got, 64, 1)
        flags += [jnp.where(lane < 64, got, across), jnp.where(lane < 64, across, got)]
    for r in range(16):
        pairs = [[rows_of(ref, 16, r, h) for h in range(2)] for ref in (own_halves, other_halves)]
        for half in range(2):
            turned = []
            for h in range(2):
                got = jnp.where(sec == half, pairs[0][h], pairs[1][h])
                turned.append([pltpu.roll(got, 32 * m, 1) if m else got for m in range(4)])
            for q in range(4):
                value = choose(group, [turned[g % 2][(g - q) % 4] for g in range(4)])
                kap[tile(q * 32 + half * 16 + r), :] = value
    for p, n in enumerate((5, 3, 2)):
        stride = 4 // (n - 1)
        gains = [face_gains(flags[d], d // 2, d % 2, n) for d in range(6)]
        rows = []
        for d in range(3):
            coefs[tile(GAINS[p] + 2 * d), :] = gains[2 * d]
            coefs[tile(GAINS[p] + 2 * d + 1), :] = gains[2 * d + 1]
            table = element_matrix(n, d)
            row = [jnp.full((8, 128), float(table[m, m]), F32) for m in range(n)]
            row[0] = row[0] + gains[2 * d]
            row[n - 1] = row[n - 1] + gains[2 * d + 1]
            rows.append(row)
        along = jnp.stack(rows[1])
        for k in range(n):
            for i in range(n):
                line = load(kap, k * 25 * stride + i * stride * 5, 5)
                line = jnp.stack([line[j * stride] for j in range(n)])
                value = line + (along + (rows[2][k] + rows[0][i]))
                scale = 1.0 / (1.0 + STEP_SIZE * JACOBI_SCALE * value)
                store(coefs, DIAGS[p] + (k * n + i) * n, value)
                store(coefs, DIAGS[p] + n**3 + (k * n + i) * n, scale * (1.0 / CENTRE))


def cycle_kernel(coefs, assembled, fields, *scratch):
    sec = lax.axis_index("section")
    my_gx, my_gy = lax.axis_index("gx"), lax.axis_index("gy")
    levels = [Level(n, scratch[4 * p : 4 * p + 4]) for p, n in enumerate((5, 3, 2))]
    half = scratch[12]
    lanes = Lanes()
    lane = lanes.lane
    blocks = split_sections()[3]

    def lanes_of(upper, lower):
        return jnp.where(lane < 64, jnp.where(sec == 0, upper[0], upper[1]), jnp.where(sec == 0, lower[0], lower[1]))

    entry = [[[float(STEP_SIZE * blocks[2 * p + a, 2 * p + b]) for p in range(2)] for b in range(2)] for a in range(2)]
    same = lanes_of(entry[0][0], entry[1][1])
    swap = lanes_of(entry[0][1], entry[1][0])
    first_rho = RADIUS / CENTRE
    second_rho = 1.0 / (2.0 * CENTRE / RADIUS - first_rho)
    keep = 1.0 + second_rho * first_rho
    push = 2.0 * second_rho / RADIUS * CENTRE
    for p, level in enumerate(levels):
        size = level.count**3
        level.gains = [-coefs[tile(GAINS[p] + d), :] for d in range(6)]
        level.diag = lambda first, count, p=p: load(coefs, DIAGS[p] + first, count)
        level.jac = lambda first, count, p=p, size=size: load(coefs, DIAGS[p] + size + first, count)

    def begin(level, source):
        n = level.count
        for first in range(0, n**3, n):
            f = load(source, first, n)
            store(level.dir, first, level.jac(first, n) * f)
            store(level.res, first, f)
            store(level.x, first, jnp.zeros_like(f))

    def apply(level, smooth):
        n = level.count
        kx, ky, kz = level.tables
        gains = level.gains
        source = level.dir if smooth else level.x
        def tree(terms):
            while len(terms) > 1:
                pairs = [a + b for a, b in zip(terms[::2], terms[1::2])]
                terms = pairs + terms[len(terms) // 2 * 2 :]
            return terms[0]

        def sums(k):
            def line_at(i):
                return load(source, (k * n + i) * n, n)

            totals = []
            for i in range(n):
                first = (k * n + i) * n
                v = line_at(i)
                along_x = [float(kx[i, m]) * line_at(m) for m in range(n) if m != i]
                if i == 0:
                    along_x.append(gains[0] * lanes.x_before(line_at(n - 1)))
                if i == n - 1:
                    along_x.append(gains[1] * lanes.x_after(line_at(0)))
                along_z = [float(kz[k, m]) * load(source, (m * n + i) * n, n) for m in range(n) if m != k]
                if k == 0:
                    along_z.append(gains[4] * lanes.z_before(load(source, ((n - 1) * n + i) * n, n)))
                if k == n - 1:
                    along_z.append(gains[5] * lanes.z_after(load(source, i * n, n)))
                along_y = []
                for j in range(n):
                    terms = [float(ky[j, m]) * v[m] for m in range(n) if m != j]
                    if j == 0:
                        terms.append(gains[2] * lanes.y_before(v[n - 1]))
                    if j == n - 1:
                        terms.append(gains[3] * lanes.y_after(v[0]))
                    along_y.append(tree(terms))
                totals.append(tree([level.diag(first, n) * v, tree(along_x), tree(along_z), jnp.stack(along_y)]))
            return totals

        def update(k, totals):
            moved = [pltpu.roll(total, 64, 2) for total in totals]
            for i in range(n):
                first = (k * n + i) * n
                v = load(source, first, n)
                image = v + (same * totals[i] + swap * moved[i])
                if smooth:
                    scaled = level.jac(first, n) * (load(level.res, first, n) - image)
                    store(level.x, first, (load(level.x, first, n) + keep * v) + push * scaled)
                else:
                    rest = load(level.f, first, n) - image
                    store(level.res, first, rest)
                    store(level.dir, first, level.jac(first, n) * rest)

        if n == 5:
            for k in range(n):
                update(k, sums(k))
        else:
            for k, totals in enumerate([sums(k) for k in range(n)]):
                update(k, totals)

    def combine(weights, parts):
        total = None
        for weight, part in zip(weights, parts):
            if abs(weight) > 1e-14:
                term = part if abs(weight - 1.0) < 1e-14 else float(weight) * part
                total = term if total is None else total + term
        return total

    def change(table, source, target, add):
        m, n = table.shape
        for i in range(n):
            parts = [load(source, i * n + k * n * n, n) for k in range(n)]
            for k in range(m):
                store(half, i * n + k * n * n, combine(table[k], parts))
        for k in range(m):
            parts = [load(half, k * n * n + i * n, n) for i in range(n)]
            for i in range(m):
                line = combine(table[i], parts)
                value = jnp.stack([combine(table[j], [line[a] for a in range(n)]) for j in range(m)])
                first = k * m * m + i * m
                store(target, first, load(target, first, m) + value if add else value)

    def down(n, m):
        fine_nodes, fine_weights = lobatto(n)
        coarse_nodes, coarse_weights = lobatto(m)
        table = lagrange_table(coarse_nodes, fine_nodes)
        return (1.0 / coarse_weights)[:, None] * table.T * fine_weights[None, :]

    def up(m, n):
        return lagrange_table(lobatto(m)[0], lobatto(n)[0])

    def solve(p):
        level = levels[p]
        if p == 2:
            apply(level, True)
            return
        below = levels[p + 1]

        def step(t, carry):
            @pl.when(t != 1)
            def _():
                apply(level, True)

            @pl.when((t != 2) | (p == 0))
            def _():
                apply(level, False)

            @pl.when(t == 0)
            def _():
                n, m = level.count, below.count
                change(down(n, m), level.res, below.f, False)
                begin(below, below.f)
                solve(p + 1)
                change(up(m, n), below.x, level.x, True)
            return carry
        lax.fori_loop(0, 3, step, 0)

    fine = levels[0]
    fine.f = assembled
    begin(fine, assembled)
    solve(0)

    for first in range(0, 125, 5):
        store(fields, first, load(fine.res, first, 5))
    column = (my_gx % 2) * 4 + my_gy
    fields[FIELD : FIELD + 125, :] = fine.x[pl.ds(column, 125, stride=8), :]
    fields[FIELD + 125 : FIELD + 128, :] = jnp.zeros((3, 128), F32)


def pair_weights():
    cross = split_sections()[4]
    return jnp.where(iota((8, 128), 1) < 64, float(cross[0]), float(cross[1]))


def column_factors(p):
    sec = lax.axis_index("section")
    whole = split_sections()[0]
    lane = iota((25, 128), 1)
    here = lane // EZ % 2 == lax.axis_index("gx") // 2
    factors = []
    for s in range(2):
        parts = []
        for mine in range(2):
            t = whole[2 * mine + s]
            q = mine if p == 0 else 1 - mine
            parts.append(jnp.where(lane < 64, float(t[2 * q]), float(t[2 * q + 1])))
        factors.append(jnp.where(here, jnp.where(sec == 0, parts[0], parts[1]), 0.0))
    return factors


def column_rows(k):
    column = (lax.axis_index("gx") % 2) * 4 + lax.axis_index("gy")
    return pl.ds(k * 200 + column, 25, stride=8)


def raw_order(k):
    lane = iota((256, 160), 0)
    return (iota((256, 160), 1) == 5 * (lane % EZ) + k + lane // 128).astype(F32)


def early_kernel(own, own_start, other_start, sums, column_out, cols):
    weights = pair_weights()
    cols[...] = jnp.zeros_like(cols)
    total = jnp.zeros((192, 160), F32)
    own_factors, other_factors = column_factors(0), column_factors(1)
    for k in range(5):
        where = column_rows(k)
        z = own[FIELD + k * 25 : FIELD + k * 25 + 25, :]
        start, other = own_start[where, :], other_start[where, :]
        w = start - own[where, :]
        side = slice(0, 128) if k % 2 == 0 else slice(128, 256)
        for s in range(2):
            cols[s * 32 : s * 32 + 25, side] = own_factors[s] * z
            cols[64 + s * 32 : 64 + s * 32 + 25, side] = own_factors[s] * start + other_factors[s] * other
            cols[128 + s * 32 : 128 + s * 32 + 25, side] = own_factors[s] * w
        if k % 2 == 1:
            total = total + split_dot(cols[...], raw_order(k - 1))
    cols[:, 128:] = jnp.zeros((192, 128), F32)
    total = total + split_dot(cols[...], raw_order(4))
    column_out[...] = total
    nothing = jnp.zeros((8, 128), F32)
    uppers, sizes = [nothing] * 5, [nothing] * 5
    for r in range(125):
        c, d = own_start[tile(r), :], other_start[tile(r), :]
        a = c - own[tile(r), :]
        uppers[r % 5] = uppers[r % 5] + a * (c + weights * d)
        sizes[r % 5] = sizes[r % 5] + ((c * c + d * d) + 2.0 * (weights * (c * d)))
    sums[0:8, :] = sum(uppers)
    sums[8:16, :] = sum(sizes)


def finish_kernel(own, other, own_start, other_start, sums, column, guess, sol, res_out, arnoldi, cols, outs):
    sec = lax.axis_index("section")
    weights = pair_weights()
    cols[...] = jnp.zeros_like(cols)
    total = jnp.zeros((128, 160), F32)
    factors = column_factors(1)
    for k in range(5):
        where = column_rows(k)
        z = other[FIELD + k * 25 : FIELD + k * 25 + 25, :]
        w = other_start[where, :] - other[where, :]
        side = slice(0, 128) if k % 2 == 0 else slice(128, 256)
        for s in range(2):
            cols[s * 32 : s * 32 + 25, side] = factors[s] * z
            cols[64 + s * 32 : 64 + s * 32 + 25, side] = factors[s] * w
        if k % 2 == 1:
            total = total + split_dot(cols[...], raw_order(k - 1))
    cols[:, 128:] = jnp.zeros((128, 128), F32)
    total = total + split_dot(cols[...], raw_order(4))
    nothing = jnp.zeros((8, 128), F32)
    uppers = [nothing] * 5
    for r in range(125):
        c, d = own_start[tile(r), :], other_start[tile(r), :]
        b = d - other[tile(r), :]
        uppers[r % 5] = uppers[r % 5] + b * (d + weights * c)

    mine, theirs = sums[0:8, :], sum(uppers)
    size = jnp.sum(sums[8:16, :], keepdims=True)
    upper = jnp.sum(mine + theirs, keepdims=True) / size
    rests = [nothing] * 5
    for r in range(125):
        c, d = own_start[tile(r), :], other_start[tile(r), :]
        a = (c - own[tile(r), :]) - upper * c
        b = (d - other[tile(r), :]) - upper * d
        rests[r % 5] = rests[r % 5] + ((a * a + b * b) + 2.0 * (weights * (a * b)))
    rest = jnp.sum(sum(rests), keepdims=True)
    beta = jnp.sqrt(size)
    lower = jnp.sqrt(rest) / beta
    weight = upper / (upper * upper + lower * lower)
    entries = float(125 * EZ * COLS * 4)
    for place_out, value in enumerate((beta * (1.0 / math.sqrt(entries)), upper, lower)):
        arnoldi[place_out] = value[0, 0]
    outs[:64, :] = weight * (column[:64, :] + total[:64])
    outs[64:, :] = column[64:128, :] - weight * (column[128:, :] + total[64:])
    for i in range(5):
        for j in range(5):
            r = 5 * i + j
            for s in range(2):
                sol[i, j, s : s + 1, :] = guess[i, j, s : s + 1, :] + outs[s * 32 + r : s * 32 + r + 1, :]
                res_out[i, j, s : s + 1, :] = outs[64 + s * 32 + r : 64 + s * 32 + r + 1, :]


def plain_call(kernel, name, rows, scratch, operands, cost=1_000_000):
    return pl.pallas_call(
        kernel,
        out_shape=jax.ShapeDtypeStruct((rows, 128), F32),
        in_specs=[VMEM] * len(operands),
        out_specs=VMEM,
        scratch_shapes=[pltpu.VMEM((r, 128), F32) for r in scratch],
        compiler_params=limit(16),
        cost_estimate=pl.CostEstimate(flops=cost, bytes_accessed=cost, transcendentals=0),
        name=name,
    )(*operands)


def cycle(coefs, assembled):
    scratch = []
    for n in (5, 3, 2):
        scratch += [pltpu.VMEM((n**3 * 8, 128), F32)] * 4
    scratch += [pltpu.VMEM((FIELD, 128), F32)]
    return pl.pallas_call(
        cycle_kernel,
        out_shape=jax.ShapeDtypeStruct((FIELD + 128, 128), F32),
        in_specs=[VMEM] * 2,
        out_specs=VMEM,
        scratch_shapes=scratch,
        compiler_params=limit(24),
        cost_estimate=pl.CostEstimate(flops=40_000_000, bytes_accessed=30_000_000, transcendentals=0),
        name="cycle",
    )(coefs, assembled)


def early(own, own_start, other_start):
    return pl.pallas_call(
        early_kernel,
        out_shape=[jax.ShapeDtypeStruct((16, 128), F32), jax.ShapeDtypeStruct((192, 160), F32)],
        in_specs=[VMEM] * 3,
        out_specs=[VMEM] * 2,
        scratch_shapes=[pltpu.VMEM((192, 256), F32)],
        compiler_params=limit(16),
        cost_estimate=pl.CostEstimate(flops=4_000_000, bytes_accessed=4_000_000, transcendentals=0),
        name="early",
    )(own, own_start, other_start)


def finish(own, other, own_start, other_start, sums, column, guess):
    return pl.pallas_call(
        finish_kernel,
        out_shape=[
            jax.ShapeDtypeStruct(guess.shape, F32),
            jax.ShapeDtypeStruct(guess.shape, F32),
            jax.ShapeDtypeStruct((3,), F32),
        ],
        in_specs=[VMEM] * 7,
        out_specs=[VMEM, VMEM, pl.BlockSpec(memory_space=pltpu.SMEM)],
        scratch_shapes=[pltpu.VMEM((128, 256), F32), pltpu.VMEM((128, 160), F32)],
        compiler_params=limit(24),
        name="finish",
    )(own, other, own_start, other_start, sums, column, guess)


def exchange(x, axis, bits):
    return lax.ppermute(x, axis, [(n, n ^ bits) for n in range(lax.axis_size(axis))])


def exchange_by_core(x, axis, bits):
    count = lax.axis_size(axis)
    pairs = [(s * count + n, s * count + (n ^ bits[s])) for s in range(2) for n in range(count)]
    return lax.ppermute(x, ("section", axis), pairs)


def gathered_body(rhs, guess, kappa, bc_flags):
    rhs, guess = (jnp.transpose(v, (1, 2, 0, 3)) for v in (rhs, guess))
    mine, theirs = local_part(rhs, guess, kappa, bc_flags)
    got, mine, kappa_piece = lax.optimization_barrier((exchange(theirs, "section", 1), *part(mine)))
    piece = jnp.concatenate([mine + got, kappa_piece])
    pieces = [exchange_by_core(piece, "gx", bits) for bits in ORDER_X] + [piece]
    line = plain_call(line_kernel, "line", LINE, [4 * 64, 4 * PIECE], pieces)
    blocks = [line] + [exchange_by_core(line, "gy", bits) for bits in ORDER_Y]
    halves = plain_call(halves_kernel, "halves", COLS * 16, [], blocks)
    other_halves = exchange(halves, "section", 1)
    start = plain_call(assemble_kernel, "assemble", 128 * 8, [COLS * HALF, COLS * 32, 50 * 8], blocks, 4_000_000)
    start, other_halves = lax.optimization_barrier((start, other_halves))
    coefs = plain_call(setup_kernel, "setup", REGISTERS * 8, [128 * 8], (start, halves, other_halves))
    other_start = exchange(start, "section", 1)
    own, other_start = lax.optimization_barrier((cycle(coefs, start), other_start))
    sums, column = early(own, start, other_start)
    sol, res, arnoldi = finish(own, exchange(own, "section", 1), start, other_start, sums, column, guess)
    sol, res = (jnp.transpose(v, (2, 0, 1, 3)) for v in (sol, res))
    return sol, res, arnoldi


def solution(mesh):
    placed = (
        P("section", "gx", "gy", None),
        P("section", "gx", "gy", None),
        P("gx", "gy", None),
        P(None, "gx", "gy", None),
    )
    sizes = (mesh.shape["section"], mesh.shape["gx"], mesh.shape["gy"])

    def step(rhs, guess, kappa, bc_flags):
        fits = sizes == (2, 4, 4) and rhs.shape == (4, 20, 20, 160)
        return jax.shard_map(
            gathered_body if fits else stepwise,
            mesh=mesh,
            in_specs=placed,
            out_specs=(P("section", "gx", "gy", None), P("section", "gx", "gy", None), P()),
            check_vma=False,
        )(rhs, guess, kappa, bc_flags)

    return step
```

```python
from functools import partial
import math

import jax
import jax.numpy as jnp
import numpy as np
from jax import lax
from jax.experimental import pallas as pl
from jax.experimental.pallas import tpu as pltpu
from jax.sharding import PartitionSpec as P

ADVECT = (1.0, 0.7, 0.5)
DIFFUSE = 0.05
STEP_SIZE = 0.2
JACOBI_SCALE = 0.25
CHEB_LOW = 0.25
CHEB_HIGH = 2.0
LETTERS = "abcdef"


def extended(x, sides, width):
    for axis, dim in sides:
        peers, length = (lax.axis_size(axis), x.shape[dim])
        up = [(i, (i + 1) % peers) for i in range(peers)]
        down = [(j, i) for i, j in up]
        last = lax.slice_in_dim(x, length - width, length, axis=dim)
        leading = lax.slice_in_dim(x, 0, width, axis=dim)
        before = lax.ppermute(last, axis, up)
        after = lax.ppermute(leading, axis, down)
        x = jnp.concatenate([before, x, after], axis=dim)
    return x


def lobatto(count):
    if count == 5:
        inner = math.sqrt(3.0 / 7.0)
        return (
            np.array([-1.0, -inner, 0.0, inner, 1.0]),
            np.array([0.1, 49.0 / 90.0, 32.0 / 45.0, 49.0 / 90.0, 0.1]),
        )
    if count == 3:
        return (np.array([-1.0, 0.0, 1.0]), np.array([1.0 / 3.0, 4.0 / 3.0, 1.0 / 3.0]))
    return (np.array([-1.0, 1.0]), np.array([1.0, 1.0]))


def lagrange_table(nodes, points):
    table = np.ones((len(points), len(nodes)))
    for column in range(len(nodes)):
        for other in range(len(nodes)):
            if other != column:
                table[:, column] *= (points - nodes[other]) / (nodes[column] - nodes[other])
    return table


def slope_table(nodes):
    total = len(nodes)
    factor = np.array(
        [np.prod([nodes[i] - nodes[k] for k in range(total) if k != i]) for i in range(total)]
    )
    table = np.zeros((total, total))
    for row in range(total):
        for column in range(total):
            if row != column:
                table[row, column] = factor[row] / factor[column] / (nodes[row] - nodes[column])
        table[row, row] = -np.sum(table[row])
    return table


def element_matrix(count, direction):
    nodes, weights = lobatto(count)
    slopes = slope_table(nodes)
    stiffness = (1.0 / weights)[:, None] * (slopes.T @ (weights[:, None] * slopes))
    return ADVECT[direction] * slopes + DIFFUSE * stiffness


def legendre_pair(point, order):
    values = [1.0, point]
    slopes = [0.0, 1.0]
    for index in range(1, order):
        values.append(
            ((2 * index + 1) * point * values[index] - index * values[index - 1]) / (index + 1)
        )
        slopes.append(slopes[index - 1] + (2 * index + 1) * values[index])
    return (values, slopes)


def radau_nodes():
    starts = [0.0885879595127039, 0.4094668644407347, 0.7876594617608471]
    found = []
    for start in starts:
        point = start
        for sweep in range(30):
            values, slopes = legendre_pair(2.0 * point - 1.0, 4)
            change = (values[4] - values[3]) / (2.0 * (slopes[4] - slopes[3]))
            point = point - change
        found.append(point)
    found.append(1.0)
    return found


def poly_times(coefs, root):
    result = [0.0] * (len(coefs) + 1)
    for index in range(len(coefs)):
        result[index + 1] += coefs[index]
        result[index] -= root * coefs[index]
    return result


def radau_matrix():
    order = 4
    nodes = radau_nodes()
    matrix = np.zeros((order, order))
    for column in range(order):
        coefs = [1.0]
        denominator = 1.0
        for other in range(order):
            if other != column:
                coefs = poly_times(coefs, nodes[other])
                denominator *= nodes[column] - nodes[other]
        for row in range(order):
            upper_end = nodes[row]
            integral = 0.0
            for index in range(len(coefs)):
                integral += coefs[index] * upper_end ** (index + 1) / (index + 1)
            matrix[row, column] = integral / denominator
    return matrix


def node_einsum(table, field, axis):
    labels = LETTERS[: field.ndim]
    source = labels[: axis + 1] + "j" + labels[axis + 2 :]
    target = labels[: axis + 1] + "i" + labels[axis + 2 :]
    return jnp.einsum(
        "ij," + source + "->" + target,
        jnp.asarray(table, jnp.float32),
        field,
        precision=lax.Precision.HIGHEST,
    )


def apply_along(field, axis, count, table):
    shape = field.shape
    split = shape[:axis] + (shape[axis] // count, count) + shape[axis + 1 :]
    mapped = node_einsum(table, field.reshape(split), axis)
    return mapped.reshape(
        shape[:axis] + (mapped.shape[axis] * mapped.shape[axis + 1],) + shape[axis + 1 :]
    )


def line_part(field, axis, count, table, left_gain, right_gain, left_edge, right_edge):
    shape = field.shape
    elements = shape[axis] // count
    split = field.reshape(shape[:axis] + (elements, count) + shape[axis + 1 :])
    linear = node_einsum(table, split, axis)
    first = lax.index_in_dim(split, 0, axis + 1, keepdims=False)
    last = lax.index_in_dim(split, count - 1, axis + 1, keepdims=False)
    before = jnp.concatenate(
        [jnp.expand_dims(left_edge, axis), lax.slice_in_dim(last, 0, elements - 1, axis=axis)], axis
    )
    after = jnp.concatenate(
        [lax.slice_in_dim(first, 1, elements, axis=axis), jnp.expand_dims(right_edge, axis)], axis
    )
    front = jnp.expand_dims(left_gain * (first - before), axis + 1)
    back = jnp.expand_dims(right_gain * (last - after), axis + 1)
    if count > 2:
        middle_shape = list(front.shape)
        middle_shape[axis + 1] = count - 2
        pieces = [front, jnp.zeros(middle_shape, jnp.float32), back]
    else:
        pieces = [front, back]
    return (linear + jnp.concatenate(pieces, axis + 1)).reshape(shape)


def diag_along(shape, axis, count, table, left_gain, right_gain):
    elements = shape[axis] // count
    split = shape[:axis] + (elements, count) + shape[axis + 1 :]
    profile = [1] * len(split)
    profile[axis + 1] = count
    diagonal_entries = np.array([table[index, index] for index in range(count)])
    base = jnp.broadcast_to(jnp.asarray(diagonal_entries, jnp.float32).reshape(profile), split)
    front = jnp.expand_dims(left_gain, axis + 1)
    back = jnp.expand_dims(right_gain, axis + 1)
    if count > 2:
        middle_shape = list(front.shape)
        middle_shape[axis + 1] = count - 2
        pieces = [front, jnp.zeros(middle_shape, jnp.float32), back]
    else:
        pieces = [front, back]
    return (base + jnp.concatenate(pieces, axis + 1)).reshape(shape)


def level_kappa(kappa, count):
    if count == 5:
        return kappa
    picks = np.array([0, 2, 4]) if count == 3 else np.array([0, 4])
    extents = [extent // 5 for extent in kappa.shape]
    grouped = kappa.reshape(extents[0], 5, extents[1], 5, extents[2], 5)
    for axis in (1, 3, 5):
        grouped = jnp.take(grouped, picks, axis=axis)
    return grouped.reshape(extents[0] * count, extents[1] * count, extents[2] * count)


def face_plane(face, direction, count):
    plane = face.astype(jnp.float32)
    for axis in range(3):
        if axis != direction:
            plane = jnp.repeat(plane, count, axis=axis)
    return plane


def build_level(kappa, flags, count):
    nodes, weights = lobatto(count)
    kappa_level = level_kappa(kappa, count)
    tables, lefts, rights = ([], [], [])
    diagonal = kappa_level
    for direction in range(3):
        table = element_matrix(count, direction)
        lower = face_plane(flags[2 * direction], direction, count)
        upper = face_plane(flags[2 * direction + 1], direction, count)
        left_gain = (ADVECT[direction] * (1.0 + lower) / 2.0 + DIFFUSE * count * count) / float(
            weights[0]
        )
        right_gain = (DIFFUSE * count * count - ADVECT[direction] * (1.0 - upper) / 2.0) / float(
            weights[-1]
        )
        tables.append(table)
        lefts.append(left_gain)
        rights.append(right_gain)
        diagonal = diagonal + diag_along(
            kappa_level.shape, direction, count, table, left_gain, right_gain
        )
    scale = 1.0 / (1.0 + STEP_SIZE * JACOBI_SCALE * diagonal)
    return (count, tables, lefts, rights, kappa_level, scale)


def restrict(field, fine_count, coarse_count):
    fine_nodes, fine_weights = lobatto(fine_count)
    coarse_nodes, coarse_weights = lobatto(coarse_count)
    table = (
        (1.0 / coarse_weights)[:, None]
        * lagrange_table(coarse_nodes, fine_nodes).T
        * fine_weights[None, :]
    )
    for axis in range(field.ndim - 3, field.ndim):
        field = apply_along(field, axis, fine_count, table)
    return field


def prolong(field, coarse_count, fine_count):
    fine_nodes, fine_weights = lobatto(fine_count)
    coarse_nodes, coarse_weights = lobatto(coarse_count)
    table = lagrange_table(coarse_nodes, fine_nodes)
    for axis in range(field.ndim - 3, field.ndim):
        field = apply_along(field, axis, coarse_count, table)
    return field


def chebyshev(rhs, start, level, operator):
    centre = (CHEB_HIGH + CHEB_LOW) / 2.0
    radius = (CHEB_HIGH - CHEB_LOW) / 2.0
    ratio = centre / radius
    first_rho = 1.0 / ratio
    second_rho = 1.0 / (2.0 * ratio - first_rho)
    scale = level[5]
    if start is None:
        remain = rhs
    else:
        remain = rhs - operator(start, level)
    step = scale * remain / centre
    guess = step if start is None else start + step
    remain = remain - operator(step, level)
    step = second_rho * first_rho * step + 2.0 * second_rho / radius * scale * remain
    return guess + step


def vcycle(rhs, levels, operator):
    fine, middle, coarse = levels
    fine_x = chebyshev(rhs, None, fine, operator)
    middle_rhs = restrict(rhs - operator(fine_x, fine), 5, 3)
    middle_x = chebyshev(middle_rhs, None, middle, operator)
    coarse_rhs = restrict(middle_rhs - operator(middle_x, middle), 3, 2)
    coarse_x = chebyshev(coarse_rhs, None, coarse, operator)
    middle_x = chebyshev(middle_rhs, middle_x + prolong(coarse_x, 2, 3), middle, operator)
    return chebyshev(rhs, fine_x + prolong(middle_x, 3, 5), fine, operator)


def spatial(field, level):
    count, tables, lefts, rights, kappa_level, scale = level
    padded = extended(field, (("gx", 1), ("gy", 2)), 1)
    total = kappa_level * field
    total = total + line_part(
        field,
        1,
        count,
        tables[0],
        lefts[0],
        rights[0],
        padded[:, 0, 1:-1, :],
        padded[:, -1, 1:-1, :],
    )
    total = total + line_part(
        field,
        2,
        count,
        tables[1],
        lefts[1],
        rights[1],
        padded[:, 1:-1, 0, :],
        padded[:, 1:-1, -1, :],
    )
    total = total + line_part(
        field, 3, count, tables[2], lefts[2], rights[2], field[:, :, :, -1], field[:, :, :, 0]
    )
    return total


def apply_system(field, level, coupling):
    image = spatial(field, level)
    everyone = lax.all_gather(image, "section", axis=0, tiled=True)
    butcher = jnp.asarray(radau_matrix(), jnp.float32)
    rows = lax.dynamic_slice_in_dim(
        butcher, lax.axis_index("section") * field.shape[0], field.shape[0], 0
    )
    mixed = jnp.einsum("ij,jabc->iabc", rows, everyone, precision=lax.Precision.HIGHEST)
    return field + STEP_SIZE * mixed


def global_total(values):
    return lax.psum(values, ("section", "gx", "gy"))


def stepwise(rhs, guess, kappa, bc_flags):
    levels = [build_level(kappa, bc_flags, count) for count in (5, 3, 2)]
    section_operator = partial(apply_system, coupling=None)
    start_residual = rhs - section_operator(guess, levels[0])
    dofs = float(rhs.size * lax.axis_size("section") * lax.axis_size("gx") * lax.axis_size("gy"))
    beta = jnp.sqrt(global_total(jnp.sum(start_residual * start_residual).reshape(1))[0])
    basis = start_residual / beta
    precond = vcycle(basis, levels, section_operator)
    image = section_operator(precond, levels[0])
    upper = global_total(jnp.sum(image * basis).reshape(1))[0]
    remainder = image - upper * basis
    lower = jnp.sqrt(global_total(jnp.sum(remainder * remainder).reshape(1))[0])
    weight = beta * upper / (upper * upper + lower * lower)
    solution = guess + weight * precond
    residual = start_residual - weight * image
    arnoldi = jnp.stack([beta / math.sqrt(dofs), upper, lower]).astype(jnp.float32)
    return (solution, residual, arnoldi)


EZ = 32
COLS = 16
HALF = 64
FACE_X = HALF + 25
KAPPA = FACE_X + 15
PIECE = KAPPA + 16
LINE_KAPPA = 4 * HALF
LINE_Y = LINE_KAPPA + 4 * 16
LINE = LINE_Y + 104
FIELD = 1000
F32 = jnp.float32


def split_sections():
    matrix = radau_matrix()
    values, vectors = np.linalg.eig(matrix)
    order = [n for n in np.argsort(np.abs(values.imag), kind="stable") if values[n].imag > 0]
    bases = []
    for n in order:
        plane = np.stack([vectors[:, n].real, vectors[:, n].imag], axis=1)
        bases.append(np.linalg.qr(plane)[0])
    left, cross, right = np.linalg.svd(bases[0].T @ bases[1])
    bases = [bases[0] @ left, bases[1] @ right.T]
    for c in range(2):
        sign = np.sign(bases[0][np.argmax(np.abs(bases[0][:, c])), c])
        bases = [np.concatenate([b[:, :c], sign * b[:, c : c + 1], b[:, c + 1 :]], axis=1) for b in bases]
    whole = np.concatenate(bases, axis=1)
    back = np.linalg.inv(whole)
    return whole, back, back @ matrix, back @ matrix @ whole, cross


def iota(shape, dim):
    return lax.broadcasted_iota(jnp.int32, shape, dim)


def exact_dot(a, b):
    return lax.dot_general(
        a, b, (((1,), (0,)), ((), ())), precision=lax.Precision.HIGHEST, preferred_element_type=F32
    )


def split_dot(a, b):
    high = a.astype(jnp.bfloat16)
    rest = a - high.astype(F32)
    middle = rest.astype(jnp.bfloat16)
    low = (rest - middle.astype(F32)).astype(jnp.bfloat16)
    b = b.astype(jnp.bfloat16)
    return sum(
        lax.dot_general(part, b, (((1,), (0,)), ((), ())), preferred_element_type=F32)
        for part in (low, middle, high)
    )


def choose(index, values):
    out = values[-1]
    for place in range(len(values) - 2, -1, -1):
        out = jnp.where(index == place, values[place], out)
    return out


def face_gains(flag, direction, side, count):
    nodes, weights = lobatto(count)
    c, nu = ADVECT[direction], DIFFUSE * count * count
    if side == 0:
        return (c * (1.0 + flag) / 2.0 + nu) * (1.0 / float(weights[0]))
    return (nu - c * (1.0 - flag) / 2.0) * (1.0 / float(weights[-1]))


def row_table():
    kx, ky = (element_matrix(5, d) for d in range(2))
    rows = np.zeros((64, 64))
    for s in range(2):
        for i in range(5):
            for j in range(5):
                r = s * 32 + i * 5 + j
                for m in range(5):
                    rows[r, s * 32 + m * 5 + j] += kx[i, m]
                    rows[r, s * 32 + i * 5 + m] += ky[j, m]
    return rows.astype(np.float32)


def pick_lines(k):
    lane = iota((160, 256), 1)
    return (iota((160, 256), 0) == 5 * (lane % EZ) + k + lane // 128).astype(F32)


def pair_factors(sec, table, own, s):
    upper = iota((32, 128), 1) < 64
    first = jnp.where(upper, float(table[0, s]), float(table[1, s]))
    second = jnp.where(upper, float(table[2, 2 + s]), float(table[3, 2 + s]))
    if not own:
        first = jnp.where(upper, float(table[2, s]), float(table[3, s]))
        second = jnp.where(upper, float(table[0, 2 + s]), float(table[1, 2 + s]))
    return jnp.where(sec == 0, first, second)


def pack_nodes(nodes):
    half = nodes.shape[0] // 2
    odd = iota((half, 128), 1) // EZ % 2 == 1
    return jnp.where(odd, nodes[half:, :], nodes[:half, :])


def fetch(pairs, sems):
    copies = [pltpu.make_async_copy(src, dst, sems.at[n]) for n, (src, dst) in enumerate(pairs)]
    for copy in copies:
        copy.start()
    for copy in copies:
        copy.wait()


def local_kernel(
    rhs_in, guess_in, kappa_in, flags_in, rows_in, mine, theirs,
    rhs, guess, kappa, flags, rows_t, sems, stack, lines, nodes, y_faces, x_faces,
):
    sec = lax.axis_index("section")
    fetch([(rhs_in, rhs), (guess_in, guess), (kappa_in, kappa), (flags_in, flags), (rows_in, rows_t)], sems)
    stack[...] = jnp.zeros_like(stack)
    for i in range(5):
        stack[192 + 5 * i : 197 + 5 * i, :] = kappa[i]
        for j in range(5):
            r = 5 * i + j
            value = guess[i, j]
            left = rhs[i, j] - value
            for s in range(2):
                stack[s * 32 + r : s * 32 + r + 1, :] = left[s : s + 1]
                stack[128 + s * 32 + r : 128 + s * 32 + r + 1, :] = value[s : s + 1]
    stack[64:128, :] = exact_dot(rows_t[...], stack[128:192, :])
    source = stack[...]
    for k in (0, 2, 4):
        shown = split_dot(source, pick_lines(k))
        lines[224 * k : 224 * k + 224, :] = shown[:, :128]
        if k < 4:
            lines[224 * k + 224 : 224 * k + 448, :] = shown[:, 128:]

    def part(k, first):
        return lines[224 * k + first : 224 * k + first + 32, :]

    repeat = (iota((EZ, 128), 1) % EZ == iota((EZ, 128), 0)).astype(F32)
    shown = split_dot(flags[:, 0, 0, :].astype(F32), repeat)
    gains = [face_gains(shown[d : d + 1, :], d // 2, d % 2, 5) for d in range(6)]
    row = iota((32, 128), 0)
    none = jnp.zeros((32, 128), F32)
    own = jnp.where(row < 5, gains[0], jnp.where((row >= 20) & (row < 25), gains[1], none))
    own = own + jnp.where(row % 5 == 0, gains[2], jnp.where(row % 5 == 4, gains[3], none))
    kz = element_matrix(5, 2)
    back, back_matrix = split_sections()[1:3]
    for ref in (nodes, y_faces, x_faces):
        ref[...] = jnp.zeros_like(ref)
    for k in range(5):
        diagonal = part(k, 192) + own
        if k == 0:
            diagonal = diagonal + gains[4]
        if k == 4:
            diagonal = diagonal + gains[5]
        images = []
        for s in range(2):
            first = 128 + 32 * s
            image = diagonal * part(k, first) + part(k, 64 + 32 * s)
            for m in range(5):
                image = image + float(kz[k, m]) * part(m, first)
            if k == 0:
                image = image - gains[4] * pltpu.roll(part(4, first), 1, 1)
            if k == 4:
                image = image - gains[5] * pltpu.roll(part(0, first), 127, 1)
            images.append(image)
        for p, mark in enumerate((True, False)):
            total = jnp.zeros((32, 128), F32)
            trace = jnp.zeros((32, 128), F32)
            for s in range(2):
                total = total + pair_factors(sec, back, mark, s) * part(k, 32 * s)
                factor = pair_factors(sec, STEP_SIZE * back_matrix, mark, s)
                total = total - factor * images[s]
                trace = trace + factor * part(k, 128 + 32 * s)
            nodes[128 * p + 25 * k : 128 * p + 25 * k + 25, :] = total[:25]
            for i in range(5):
                for f in range(2):
                    r = 64 * p + 32 * f + 5 * k + i
                    y_faces[r : r + 1, :] = trace[5 * i + 4 * f : 5 * i + 4 * f + 1]
            for f in range(2):
                r = 32 * p + 16 * f + 3 * k
                x_faces[r : r + 3, :] = trace[20 * f + 1 : 20 * f + 4]
    upper = iota((1, 128), 1) < 64
    for r in range(3):
        nodes[125 + r : 126 + r, :] = jnp.where(upper, shown[2 * r : 2 * r + 1], shown[2 * r + 1 : 2 * r + 2])
    for p, out in enumerate((mine, theirs)):
        out[:HALF, :] = pack_nodes(nodes[128 * p : 128 * p + 128, :])
        out[HALF:FACE_X, :] = pack_nodes(y_faces[64 * p : 64 * p + 64, :])[:25]
        out[FACE_X:KAPPA, :] = pack_nodes(x_faces[32 * p : 32 * p + 32, :])[:15]
    for k in range(5):
        nodes[25 * k : 25 * k + 25, :] = part(k, 192)[:25]
    kappas = choose(iota((32, 128), 1) // EZ, [nodes[32 * q : 32 * q + 32, :] for q in range(4)])
    mine[KAPPA:, :] = jnp.where(sec == 0, kappas[:16], kappas[16:])


def part_kernel(source, piece, kappa):
    piece[...] = source[:KAPPA, :]
    kappa[...] = source[KAPPA:, :]


VMEM = pl.BlockSpec(memory_space=pltpu.VMEM)
HBM = pl.BlockSpec(memory_space=pltpu.HBM)


def limit(mib):
    return pltpu.CompilerParams(vmem_limit_bytes=mib * 2**20)


def local_part(rhs, guess, kappa, flags):
    operands = (rhs, guess, kappa, flags, jnp.asarray(row_table()))
    return pl.pallas_call(
        local_kernel,
        out_shape=[jax.ShapeDtypeStruct((rows, 128), F32) for rows in (PIECE, KAPPA)],
        in_specs=[HBM] * 5,
        out_specs=[VMEM] * 2,
        scratch_shapes=[pltpu.VMEM(o.shape, o.dtype) for o in operands]
        + [
            pltpu.SemaphoreType.DMA((5,)),
            pltpu.VMEM((224, 160), F32),
            pltpu.VMEM((5 * 224, 128), F32),
            pltpu.VMEM((256, 128), F32),
            pltpu.VMEM((128, 128), F32),
            pltpu.VMEM((64, 128), F32),
        ],
        compiler_params=limit(60),
        cost_estimate=pl.CostEstimate(flops=20_000_000, bytes_accessed=8_000_000, transcendentals=0),
        name="local_part",
    )(*operands)


def part(x):
    return pl.pallas_call(
        part_kernel,
        out_shape=[jax.ShapeDtypeStruct((rows, 128), F32) for rows in (KAPPA, 16)],
        in_specs=[VMEM],
        out_specs=[VMEM] * 2,
        compiler_params=limit(16),
        name="part",
    )(x)


class Level:
    def __init__(self, count, refs):
        self.count = count
        self.x, self.dir, self.res, self.f = refs
        self.tables = [element_matrix(count, d) for d in range(3)]
        self.gains = self.diag = self.jac = None


def tile(index):
    return pl.ds(index * 8, 8)


def rows_of(pieces, size, r, h):
    return pieces[pl.ds(8 * h * size + r, 8, stride=size), :]


ORDER_X = ((3, 2), (2, 3), (1, 1))
ORDER_Y = ((1, 2), (2, 1), (3, 3))


def partner(bits):
    return jnp.where(lax.axis_index("section") == 0, bits[0], bits[1])


def place_pieces(blocks, pieces, first, size, room):
    my_gx, my_gy = lax.axis_index("gx"), lax.axis_index("gy")
    for b, block in enumerate(blocks):
        gy = my_gy ^ partner(ORDER_Y[b - 1]) if b else my_gy
        for a in range(4):
            column = (my_gx ^ a) * 4 + gy
            start = pl.multiple_of(column * room, 8)
            pieces[pl.ds(start, size), :] = block[first + a * size : first + a * size + size, :]


class Lanes:
    def __init__(self):
        self.lane = iota((8, 128), 1)
        sub = iota((8, 128), 0)
        self.group = self.lane // EZ
        self.odd = self.group % 2 == 1
        self.element = self.lane % EZ
        self.place = sub % 4
        self.low_half = sub < 4

    def around(self, u):
        turned = pltpu.roll(u, 4, u.ndim - 2)
        far = jnp.where(self.odd, pltpu.roll(turned, 32, u.ndim - 1), pltpu.roll(turned, 96, u.ndim - 1))
        return turned, far

    def x_before(self, u):
        turned, far = self.around(u)
        return jnp.where(self.low_half, far, turned)

    def x_after(self, u):
        turned, far = self.around(u)
        return jnp.where(self.low_half, turned, far)

    def y_before(self, u):
        return jnp.where(self.place == 0, pltpu.roll(u, 5, 0), pltpu.roll(u, 1, 0))

    def y_after(self, u):
        return jnp.where(self.place == 3, pltpu.roll(u, 3, 0), pltpu.roll(u, 7, 0))

    def z_before(self, u):
        return jnp.where(self.element == 0, pltpu.roll(u, 97, u.ndim - 1), pltpu.roll(u, 1, u.ndim - 1))

    def z_after(self, u):
        last = self.element == EZ - 1
        return jnp.where(last, pltpu.roll(u, 31, u.ndim - 1), pltpu.roll(u, 127, u.ndim - 1))


def load(ref, first, count):
    return ref[pl.ds(first * 8, count * 8), :].reshape(count, 8, 128)


def store(ref, first, value):
    ref[pl.ds(first * 8, value.shape[0] * 8), :] = value.reshape(value.shape[0] * 8, 128)


DIAGS = (0, 250, 304)
GAINS = (320, 326, 332)
REGISTERS = 338
CENTRE = (CHEB_HIGH + CHEB_LOW) / 2.0
RADIUS = (CHEB_HIGH - CHEB_LOW) / 2.0


def flag_lanes(row, slot):
    turned = [row] + [pltpu.roll(row, 32 * m, 1) for m in range(1, 4)]
    return choose(iota(row.shape, 1) // EZ, [turned[(g - 2 * slot - 1) % 4] for g in range(4)])


def line_kernel(first, second, third, own, line, faces, sorted_pieces):
    sorted_pieces[:PIECE, :] = own[...]
    for bits, piece in zip(ORDER_X, (first, second, third)):
        sorted_pieces[pl.ds(pl.multiple_of(partner(bits) * PIECE, 8), PIECE), :] = piece[...]
    pieces = [sorted_pieces.at[PIECE * a : PIECE * a + PIECE, :] for a in range(4)]
    even = lax.axis_index("gx") % 2 == 0
    odd = iota((8, 128), 1) // EZ % 2 == 1
    faces[...] = jnp.zeros_like(faces)

    def both(rows, f):
        side = odd[:1] if f else jnp.logical_not(odd[:1])
        return jnp.where(side, rows, pltpu.roll(rows, 96 if f else 32, 1))

    for a, piece in enumerate(pieces):
        for f in range(2):
            base = 64 * a + 32 * f
            inner = both(piece[FACE_X:KAPPA, :], f)
            ends = [both(piece[HALF:FACE_X, :], g) for g in range(2)]
            for k in range(5):
                r = base + 5 * k
                node = 5 * k + 4 * f
                faces[r : r + 1, :] = ends[0][node : node + 1]
                faces[r + 1 : r + 4, :] = inner[3 * k : 3 * k + 3]
                faces[r + 4 : r + 5, :] = ends[1][node : node + 1]
    for a, piece in enumerate(pieces):
        line[HALF * a : HALF * a + HALF, :] = piece[:HALF, :]
        line[LINE_KAPPA + 16 * a : LINE_KAPPA + 16 * a + 16, :] = piece[KAPPA:, :]
        line[LINE_Y + 25 * a : LINE_Y + 25 * a + 25, :] = piece[HALF:FACE_X, :]
        flags = [flag_lanes(piece[61:62, :], slot) for slot in range(2)]
        gains = [face_gains(flags[d], 0, d, 5) for d in range(2)]
        next_first = even if a % 2 == 0 else jnp.logical_not(even)
        for f in range(2):
            one = faces[64 * (a ^ 1) + 32 * (1 - f) : 64 * (a ^ 1) + 32 * (1 - f) + 32, :]
            three = faces[64 * (a ^ 3) + 32 * (1 - f) : 64 * (a ^ 3) + 32 * (1 - f) + 32, :]
            near = jnp.where(next_first, one, three) if f else jnp.where(next_first, three, one)
            term = gains[f] * near
            for k in range(5):
                node = 25 * k + 20 * f
                side = odd[:5] if node >= HALF else jnp.logical_not(odd[:5])
                r = HALF * a + node % HALF
                line[r : r + 5, :] = line[r : r + 5, :] + jnp.where(side, term[5 * k : 5 * k + 5], 0.0)
    line[LINE_Y + 100 :, :] = jnp.zeros((4, 128), F32)


def halves_kernel(block0, block1, block2, block3, out):
    place_pieces((block0, block1, block2, block3), out, LINE_KAPPA, 16, 16)


def widen(low, high, odd):
    return jnp.where(odd, pltpu.roll(high, 32, 1), low), jnp.where(odd, high, pltpu.roll(low, 96, 1))


def assemble_kernel(block0, block1, block2, block3, field, pieces, edges, traces):
    blocks = (block0, block1, block2, block3)
    place_pieces(blocks, pieces, 0, HALF, HALF)
    place_pieces(blocks, edges, LINE_Y, 25, 32)
    lanes = Lanes()
    for source, size, rows, target, apart in ((edges, 32, 25, traces, 25), (pieces, HALF, HALF, field, HALF)):
        for r in range(rows):
            first, second = widen(rows_of(source, size, r, 0), rows_of(source, size, r, 1), lanes.odd)
            target[tile(r), :] = first
            target[tile(apart + r), :] = second
    got = field[tile(126), :]
    across = pltpu.roll(got, 64, 1)
    gains = [
        face_gains(jnp.where(lanes.lane < 64, got, across), 1, 0, 5),
        face_gains(jnp.where(lanes.lane < 64, across, got), 1, 1, 5),
    ]
    for k in range(5):
        for i in range(5):
            lower, upper = traces[tile(5 * k + i), :], traces[tile(25 + 5 * k + i), :]
            node = 25 * k + 5 * i
            field[tile(node), :] = field[tile(node), :] + gains[0] * lanes.y_before(upper)
            field[tile(node + 4), :] = field[tile(node + 4), :] + gains[1] * lanes.y_after(lower)


def setup_kernel(field, own_halves, other_halves, coefs, kap):
    sec = lax.axis_index("section")
    lanes = Lanes()
    group, lane = lanes.group, lanes.lane
    flags = []
    for r in range(3):
        got = field[tile(125 + r), :]
        across = pltpu.roll(got, 64, 1)
        flags += [jnp.where(lane < 64, got, across), jnp.where(lane < 64, across, got)]
    for r in range(16):
        pairs = [[rows_of(ref, 16, r, h) for h in range(2)] for ref in (own_halves, other_halves)]
        for half in range(2):
            turned = []
            for h in range(2):
                got = jnp.where(sec == half, pairs[0][h], pairs[1][h])
                turned.append([pltpu.roll(got, 32 * m, 1) if m else got for m in range(4)])
            for q in range(4):
                value = choose(group, [turned[g % 2][(g - q) % 4] for g in range(4)])
                kap[tile(q * 32 + half * 16 + r), :] = value
    for p, n in enumerate((5, 3, 2)):
        stride = 4 // (n - 1)
        gains = [face_gains(flags[d], d // 2, d % 2, n) for d in range(6)]
        rows = []
        for d in range(3):
            coefs[tile(GAINS[p] + 2 * d), :] = gains[2 * d]
            coefs[tile(GAINS[p] + 2 * d + 1), :] = gains[2 * d + 1]
            table = element_matrix(n, d)
            row = [jnp.full((8, 128), float(table[m, m]), F32) for m in range(n)]
            row[0] = row[0] + gains[2 * d]
            row[n - 1] = row[n - 1] + gains[2 * d + 1]
            rows.append(row)
        along = jnp.stack(rows[1])
        for k in range(n):
            for i in range(n):
                line = load(kap, k * 25 * stride + i * stride * 5, 5)
                line = jnp.stack([line[j * stride] for j in range(n)])
                value = line + (along + (rows[2][k] + rows[0][i]))
                scale = 1.0 / (1.0 + STEP_SIZE * JACOBI_SCALE * value)
                store(coefs, DIAGS[p] + (k * n + i) * n, value)
                store(coefs, DIAGS[p] + n**3 + (k * n + i) * n, scale * (1.0 / CENTRE))


def cycle_kernel(coefs, assembled, fields, *scratch):
    sec = lax.axis_index("section")
    my_gx, my_gy = lax.axis_index("gx"), lax.axis_index("gy")
    levels = [Level(n, scratch[4 * p : 4 * p + 4]) for p, n in enumerate((5, 3, 2))]
    half = scratch[12]
    lanes = Lanes()
    lane = lanes.lane
    blocks = split_sections()[3]

    def lanes_of(upper, lower):
        return jnp.where(lane < 64, jnp.where(sec == 0, upper[0], upper[1]), jnp.where(sec == 0, lower[0], lower[1]))

    entry = [[[float(STEP_SIZE * blocks[2 * p + a, 2 * p + b]) for p in range(2)] for b in range(2)] for a in range(2)]
    same = lanes_of(entry[0][0], entry[1][1])
    swap = lanes_of(entry[0][1], entry[1][0])
    first_rho = RADIUS / CENTRE
    second_rho = 1.0 / (2.0 * CENTRE / RADIUS - first_rho)
    keep = 1.0 + second_rho * first_rho
    push = 2.0 * second_rho / RADIUS * CENTRE
    for p, level in enumerate(levels):
        size = level.count**3
        level.gains = [-coefs[tile(GAINS[p] + d), :] for d in range(6)]
        level.diag = lambda first, count, p=p: load(coefs, DIAGS[p] + first, count)
        level.jac = lambda first, count, p=p, size=size: load(coefs, DIAGS[p] + size + first, count)

    def begin(level, source):
        n = level.count
        for first in range(0, n**3, n):
            f = load(source, first, n)
            store(level.dir, first, level.jac(first, n) * f)
            store(level.res, first, f)
            store(level.x, first, jnp.zeros_like(f))

    def apply(level, smooth):
        n = level.count
        kx, ky, kz = level.tables
        gains = level.gains
        source = level.dir if smooth else level.x
        def tree(terms):
            while len(terms) > 1:
                pairs = [a + b for a, b in zip(terms[::2], terms[1::2])]
                terms = pairs + terms[len(terms) // 2 * 2 :]
            return terms[0]

        def sums(k):
            def line_at(i):
                return load(source, (k * n + i) * n, n)

            totals = []
            for i in range(n):
                first = (k * n + i) * n
                v = line_at(i)
                along_x = [float(kx[i, m]) * line_at(m) for m in range(n) if m != i]
                if i == 0:
                    along_x.append(gains[0] * lanes.x_before(line_at(n - 1)))
                if i == n - 1:
                    along_x.append(gains[1] * lanes.x_after(line_at(0)))
                along_z = [float(kz[k, m]) * load(source, (m * n + i) * n, n) for m in range(n) if m != k]
                if k == 0:
                    along_z.append(gains[4] * lanes.z_before(load(source, ((n - 1) * n + i) * n, n)))
                if k == n - 1:
                    along_z.append(gains[5] * lanes.z_after(load(source, i * n, n)))
                along_y = []
                for j in range(n):
                    terms = [float(ky[j, m]) * v[m] for m in range(n) if m != j]
                    if j == 0:
                        terms.append(gains[2] * lanes.y_before(v[n - 1]))
                    if j == n - 1:
                        terms.append(gains[3] * lanes.y_after(v[0]))
                    along_y.append(tree(terms))
                totals.append(tree([level.diag(first, n) * v, tree(along_x), tree(along_z), jnp.stack(along_y)]))
            return totals

        def update(k, totals):
            moved = [pltpu.roll(total, 64, 2) for total in totals]
            for i in range(n):
                first = (k * n + i) * n
                v = load(source, first, n)
                image = v + (same * totals[i] + swap * moved[i])
                if smooth:
                    scaled = level.jac(first, n) * (load(level.res, first, n) - image)
                    store(level.x, first, (load(level.x, first, n) + keep * v) + push * scaled)
                else:
                    rest = load(level.f, first, n) - image
                    store(level.res, first, rest)
                    store(level.dir, first, level.jac(first, n) * rest)

        if n == 5:
            for k in range(n):
                update(k, sums(k))
        else:
            for k, totals in enumerate([sums(k) for k in range(n)]):
                update(k, totals)

    def combine(weights, parts):
        total = None
        for weight, part in zip(weights, parts):
            if abs(weight) > 1e-14:
                term = part if abs(weight - 1.0) < 1e-14 else float(weight) * part
                total = term if total is None else total + term
        return total

    def change(table, source, target, add):
        m, n = table.shape
        for i in range(n):
            parts = [load(source, i * n + k * n * n, n) for k in range(n)]
            for k in range(m):
                store(half, i * n + k * n * n, combine(table[k], parts))
        for k in range(m):
            parts = [load(half, k * n * n + i * n, n) for i in range(n)]
            for i in range(m):
                line = combine(table[i], parts)
                value = jnp.stack([combine(table[j], [line[a] for a in range(n)]) for j in range(m)])
                first = k * m * m + i * m
                store(target, first, load(target, first, m) + value if add else value)

    def down(n, m):
        fine_nodes, fine_weights = lobatto(n)
        coarse_nodes, coarse_weights = lobatto(m)
        table = lagrange_table(coarse_nodes, fine_nodes)
        return (1.0 / coarse_weights)[:, None] * table.T * fine_weights[None, :]

    def up(m, n):
        return lagrange_table(lobatto(m)[0], lobatto(n)[0])

    def solve(p):
        level = levels[p]
        if p == 2:
            apply(level, True)
            return
        below = levels[p + 1]

        def step(t, carry):
            @pl.when(t != 1)
            def _():
                apply(level, True)

            @pl.when((t != 2) | (p == 0))
            def _():
                apply(level, False)

            @pl.when(t == 0)
            def _():
                n, m = level.count, below.count
                change(down(n, m), level.res, below.f, False)
                begin(below, below.f)
                solve(p + 1)
                change(up(m, n), below.x, level.x, True)
            return carry
        lax.fori_loop(0, 3, step, 0)

    fine = levels[0]
    fine.f = assembled
    begin(fine, assembled)
    solve(0)

    for first in range(0, 125, 5):
        store(fields, first, load(fine.res, first, 5))
    column = (my_gx % 2) * 4 + my_gy
    fields[FIELD : FIELD + 125, :] = fine.x[pl.ds(column, 125, stride=8), :]
    fields[FIELD + 125 : FIELD + 128, :] = jnp.zeros((3, 128), F32)


def pair_weights():
    cross = split_sections()[4]
    return jnp.where(iota((8, 128), 1) < 64, float(cross[0]), float(cross[1]))


def column_factors(p):
    sec = lax.axis_index("section")
    whole = split_sections()[0]
    lane = iota((25, 128), 1)
    here = lane // EZ % 2 == lax.axis_index("gx") // 2
    factors = []
    for s in range(2):
        parts = []
        for mine in range(2):
            t = whole[2 * mine + s]
            q = mine if p == 0 else 1 - mine
            parts.append(jnp.where(lane < 64, float(t[2 * q]), float(t[2 * q + 1])))
        factors.append(jnp.where(here, jnp.where(sec == 0, parts[0], parts[1]), 0.0))
    return factors


def column_rows(k):
    column = (lax.axis_index("gx") % 2) * 4 + lax.axis_index("gy")
    return pl.ds(k * 200 + column, 25, stride=8)


def raw_order(k):
    lane = iota((256, 160), 0)
    return (iota((256, 160), 1) == 5 * (lane % EZ) + k + lane // 128).astype(F32)


def early_kernel(own, own_start, other_start, sums, column_out, cols):
    weights = pair_weights()
    cols[...] = jnp.zeros_like(cols)
    total = jnp.zeros((192, 160), F32)
    own_factors, other_factors = column_factors(0), column_factors(1)
    for k in range(5):
        where = column_rows(k)
        z = own[FIELD + k * 25 : FIELD + k * 25 + 25, :]
        start, other = own_start[where, :], other_start[where, :]
        w = start - own[where, :]
        side = slice(0, 128) if k % 2 == 0 else slice(128, 256)
        for s in range(2):
            cols[s * 32 : s * 32 + 25, side] = own_factors[s] * z
            cols[64 + s * 32 : 64 + s * 32 + 25, side] = own_factors[s] * start + other_factors[s] * other
            cols[128 + s * 32 : 128 + s * 32 + 25, side] = own_factors[s] * w
        if k % 2 == 1:
            total = total + split_dot(cols[...], raw_order(k - 1))
    cols[:, 128:] = jnp.zeros((192, 128), F32)
    total = total + split_dot(cols[...], raw_order(4))
    column_out[...] = total
    nothing = jnp.zeros((8, 128), F32)
    uppers, sizes = [nothing] * 5, [nothing] * 5
    for r in range(125):
        c, d = own_start[tile(r), :], other_start[tile(r), :]
        a = c - own[tile(r), :]
        uppers[r % 5] = uppers[r % 5] + a * (c + weights * d)
        sizes[r % 5] = sizes[r % 5] + ((c * c + d * d) + 2.0 * (weights * (c * d)))
    sums[0:8, :] = sum(uppers)
    sums[8:16, :] = sum(sizes)


def finish_kernel(own, other, own_start, other_start, sums, column, guess, sol, res_out, arnoldi, cols, outs):
    sec = lax.axis_index("section")
    weights = pair_weights()
    cols[...] = jnp.zeros_like(cols)
    total = jnp.zeros((128, 160), F32)
    factors = column_factors(1)
    for k in range(5):
        where = column_rows(k)
        z = other[FIELD + k * 25 : FIELD + k * 25 + 25, :]
        w = other_start[where, :] - other[where, :]
        side = slice(0, 128) if k % 2 == 0 else slice(128, 256)
        for s in range(2):
            cols[s * 32 : s * 32 + 25, side] = factors[s] * z
            cols[64 + s * 32 : 64 + s * 32 + 25, side] = factors[s] * w
        if k % 2 == 1:
            total = total + split_dot(cols[...], raw_order(k - 1))
    cols[:, 128:] = jnp.zeros((128, 128), F32)
    total = total + split_dot(cols[...], raw_order(4))
    nothing = jnp.zeros((8, 128), F32)
    uppers = [nothing] * 5
    for r in range(125):
        c, d = own_start[tile(r), :], other_start[tile(r), :]
        b = d - other[tile(r), :]
        uppers[r % 5] = uppers[r % 5] + b * (d + weights * c)

    mine, theirs = sums[0:8, :], sum(uppers)
    size = jnp.sum(sums[8:16, :], keepdims=True)
    upper = jnp.sum(mine + theirs, keepdims=True) / size
    rests = [nothing] * 5
    for r in range(125):
        c, d = own_start[tile(r), :], other_start[tile(r), :]
        a = (c - own[tile(r), :]) - upper * c
        b = (d - other[tile(r), :]) - upper * d
        rests[r % 5] = rests[r % 5] + ((a * a + b * b) + 2.0 * (weights * (a * b)))
    rest = jnp.sum(sum(rests), keepdims=True)
    beta = jnp.sqrt(size)
    lower = jnp.sqrt(rest) / beta
    weight = upper / (upper * upper + lower * lower)
    entries = float(125 * EZ * COLS * 4)
    for place_out, value in enumerate((beta * (1.0 / math.sqrt(entries)), upper, lower)):
        arnoldi[place_out] = value[0, 0]
    outs[:64, :] = weight * (column[:64, :] + total[:64])
    outs[64:, :] = column[64:128, :] - weight * (column[128:, :] + total[64:])
    for i in range(5):
        for j in range(5):
            r = 5 * i + j
            for s in range(2):
                sol[i, j, s : s + 1, :] = guess[i, j, s : s + 1, :] + outs[s * 32 + r : s * 32 + r + 1, :]
                res_out[i, j, s : s + 1, :] = outs[64 + s * 32 + r : 64 + s * 32 + r + 1, :]


def plain_call(kernel, name, rows, scratch, operands, cost=1_000_000):
    return pl.pallas_call(
        kernel,
        out_shape=jax.ShapeDtypeStruct((rows, 128), F32),
        in_specs=[VMEM] * len(operands),
        out_specs=VMEM,
        scratch_shapes=[pltpu.VMEM((r, 128), F32) for r in scratch],
        compiler_params=limit(16),
        cost_estimate=pl.CostEstimate(flops=cost, bytes_accessed=cost, transcendentals=0),
        name=name,
    )(*operands)


def cycle(coefs, assembled):
    scratch = []
    for n in (5, 3, 2):
        scratch += [pltpu.VMEM((n**3 * 8, 128), F32)] * 4
    scratch += [pltpu.VMEM((FIELD, 128), F32)]
    return pl.pallas_call(
        cycle_kernel,
        out_shape=jax.ShapeDtypeStruct((FIELD + 128, 128), F32),
        in_specs=[VMEM] * 2,
        out_specs=VMEM,
        scratch_shapes=scratch,
        compiler_params=limit(24),
        cost_estimate=pl.CostEstimate(flops=40_000_000, bytes_accessed=30_000_000, transcendentals=0),
        name="cycle",
    )(coefs, assembled)


def early(own, own_start, other_start):
    return pl.pallas_call(
        early_kernel,
        out_shape=[jax.ShapeDtypeStruct((16, 128), F32), jax.ShapeDtypeStruct((192, 160), F32)],
        in_specs=[VMEM] * 3,
        out_specs=[VMEM] * 2,
        scratch_shapes=[pltpu.VMEM((192, 256), F32)],
        compiler_params=limit(16),
        cost_estimate=pl.CostEstimate(flops=4_000_000, bytes_accessed=4_000_000, transcendentals=0),
        name="early",
    )(own, own_start, other_start)


def finish(own, other, own_start, other_start, sums, column, guess):
    return pl.pallas_call(
        finish_kernel,
        out_shape=[
            jax.ShapeDtypeStruct(guess.shape, F32),
            jax.ShapeDtypeStruct(guess.shape, F32),
            jax.ShapeDtypeStruct((3,), F32),
        ],
        in_specs=[VMEM] * 7,
        out_specs=[VMEM, VMEM, pl.BlockSpec(memory_space=pltpu.SMEM)],
        scratch_shapes=[pltpu.VMEM((128, 256), F32), pltpu.VMEM((128, 160), F32)],
        compiler_params=limit(24),
        name="finish",
    )(own, other, own_start, other_start, sums, column, guess)


def exchange(x, axis, bits):
    return lax.ppermute(x, axis, [(n, n ^ bits) for n in range(lax.axis_size(axis))])


def exchange_by_core(x, axis, bits):
    count = lax.axis_size(axis)
    pairs = [(s * count + n, s * count + (n ^ bits[s])) for s in range(2) for n in range(count)]
    return lax.ppermute(x, ("section", axis), pairs)


def gathered_body(rhs, guess, kappa, bc_flags):
    rhs, guess = (jnp.transpose(v, (1, 2, 0, 3)) for v in (rhs, guess))
    mine, theirs = local_part(rhs, guess, kappa, bc_flags)
    got, mine, kappa_piece = lax.optimization_barrier((exchange(theirs, "section", 1), *part(mine)))
    piece = jnp.concatenate([mine + got, kappa_piece])
    pieces = [exchange_by_core(piece, "gx", bits) for bits in ORDER_X] + [piece]
    line = plain_call(line_kernel, "line", LINE, [4 * 64, 4 * PIECE], pieces)
    first = exchange_by_core(line, "gy", ORDER_Y[0])
    second = exchange_by_core(line, "gy", ORDER_Y[1])
    blocks = [line, first, second, exchange_by_core(first, "gy", ORDER_Y[1])]
    halves = plain_call(halves_kernel, "halves", COLS * 16, [], blocks)
    other_halves = exchange(halves, "section", 1)
    start = plain_call(assemble_kernel, "assemble", 128 * 8, [COLS * HALF, COLS * 32, 50 * 8], blocks, 4_000_000)
    start, other_halves = lax.optimization_barrier((start, other_halves))
    coefs = plain_call(setup_kernel, "setup", REGISTERS * 8, [128 * 8], (start, halves, other_halves))
    other_start = exchange(start, "section", 1)
    own, other_start = lax.optimization_barrier((cycle(coefs, start), other_start))
    sums, column = early(own, start, other_start)
    sol, res, arnoldi = finish(own, exchange(own, "section", 1), start, other_start, sums, column, guess)
    sol, res = (jnp.transpose(v, (2, 0, 1, 3)) for v in (sol, res))
    return sol, res, arnoldi


def solution(mesh):
    placed = (
        P("section", "gx", "gy", None),
        P("section", "gx", "gy", None),
        P("gx", "gy", None),
        P(None, "gx", "gy", None),
    )
    sizes = (mesh.shape["section"], mesh.shape["gx"], mesh.shape["gy"])

    def step(rhs, guess, kappa, bc_flags):
        fits = sizes == (2, 4, 4) and rhs.shape == (4, 20, 20, 160)
        return jax.shard_map(
            gathered_body if fits else stepwise,
            mesh=mesh,
            in_specs=placed,
            out_specs=(P("section", "gx", "gy", None), P("section", "gx", "gy", None), P()),
            check_vma=False,
        )(rhs, guess, kappa, bc_flags)

    return step
```

```python
from functools import partial
import math

import jax
import jax.numpy as jnp
import numpy as np
from jax import lax
from jax.experimental import pallas as pl
from jax.experimental.pallas import tpu as pltpu
from jax.sharding import PartitionSpec as P

ADVECT = (1.0, 0.7, 0.5)
DIFFUSE = 0.05
STEP_SIZE = 0.2
JACOBI_SCALE = 0.25
CHEB_LOW = 0.25
CHEB_HIGH = 2.0
LETTERS = "abcdef"


def extended(x, sides, width):
    for axis, dim in sides:
        peers, length = (lax.axis_size(axis), x.shape[dim])
        up = [(i, (i + 1) % peers) for i in range(peers)]
        down = [(j, i) for i, j in up]
        last = lax.slice_in_dim(x, length - width, length, axis=dim)
        leading = lax.slice_in_dim(x, 0, width, axis=dim)
        before = lax.ppermute(last, axis, up)
        after = lax.ppermute(leading, axis, down)
        x = jnp.concatenate([before, x, after], axis=dim)
    return x


def lobatto(count):
    if count == 5:
        inner = math.sqrt(3.0 / 7.0)
        return (
            np.array([-1.0, -inner, 0.0, inner, 1.0]),
            np.array([0.1, 49.0 / 90.0, 32.0 / 45.0, 49.0 / 90.0, 0.1]),
        )
    if count == 3:
        return (np.array([-1.0, 0.0, 1.0]), np.array([1.0 / 3.0, 4.0 / 3.0, 1.0 / 3.0]))
    return (np.array([-1.0, 1.0]), np.array([1.0, 1.0]))


def lagrange_table(nodes, points):
    table = np.ones((len(points), len(nodes)))
    for column in range(len(nodes)):
        for other in range(len(nodes)):
            if other != column:
                table[:, column] *= (points - nodes[other]) / (nodes[column] - nodes[other])
    return table


def slope_table(nodes):
    total = len(nodes)
    factor = np.array(
        [np.prod([nodes[i] - nodes[k] for k in range(total) if k != i]) for i in range(total)]
    )
    table = np.zeros((total, total))
    for row in range(total):
        for column in range(total):
            if row != column:
                table[row, column] = factor[row] / factor[column] / (nodes[row] - nodes[column])
        table[row, row] = -np.sum(table[row])
    return table


def element_matrix(count, direction):
    nodes, weights = lobatto(count)
    slopes = slope_table(nodes)
    stiffness = (1.0 / weights)[:, None] * (slopes.T @ (weights[:, None] * slopes))
    return ADVECT[direction] * slopes + DIFFUSE * stiffness


def legendre_pair(point, order):
    values = [1.0, point]
    slopes = [0.0, 1.0]
    for index in range(1, order):
        values.append(
            ((2 * index + 1) * point * values[index] - index * values[index - 1]) / (index + 1)
        )
        slopes.append(slopes[index - 1] + (2 * index + 1) * values[index])
    return (values, slopes)


def radau_nodes():
    starts = [0.0885879595127039, 0.4094668644407347, 0.7876594617608471]
    found = []
    for start in starts:
        point = start
        for sweep in range(30):
            values, slopes = legendre_pair(2.0 * point - 1.0, 4)
            change = (values[4] - values[3]) / (2.0 * (slopes[4] - slopes[3]))
            point = point - change
        found.append(point)
    found.append(1.0)
    return found


def poly_times(coefs, root):
    result = [0.0] * (len(coefs) + 1)
    for index in range(len(coefs)):
        result[index + 1] += coefs[index]
        result[index] -= root * coefs[index]
    return result


def radau_matrix():
    order = 4
    nodes = radau_nodes()
    matrix = np.zeros((order, order))
    for column in range(order):
        coefs = [1.0]
        denominator = 1.0
        for other in range(order):
            if other != column:
                coefs = poly_times(coefs, nodes[other])
                denominator *= nodes[column] - nodes[other]
        for row in range(order):
            upper_end = nodes[row]
            integral = 0.0
            for index in range(len(coefs)):
                integral += coefs[index] * upper_end ** (index + 1) / (index + 1)
            matrix[row, column] = integral / denominator
    return matrix


def node_einsum(table, field, axis):
    labels = LETTERS[: field.ndim]
    source = labels[: axis + 1] + "j" + labels[axis + 2 :]
    target = labels[: axis + 1] + "i" + labels[axis + 2 :]
    return jnp.einsum(
        "ij," + source + "->" + target,
        jnp.asarray(table, jnp.float32),
        field,
        precision=lax.Precision.HIGHEST,
    )


def apply_along(field, axis, count, table):
    shape = field.shape
    split = shape[:axis] + (shape[axis] // count, count) + shape[axis + 1 :]
    mapped = node_einsum(table, field.reshape(split), axis)
    return mapped.reshape(
        shape[:axis] + (mapped.shape[axis] * mapped.shape[axis + 1],) + shape[axis + 1 :]
    )


def line_part(field, axis, count, table, left_gain, right_gain, left_edge, right_edge):
    shape = field.shape
    elements = shape[axis] // count
    split = field.reshape(shape[:axis] + (elements, count) + shape[axis + 1 :])
    linear = node_einsum(table, split, axis)
    first = lax.index_in_dim(split, 0, axis + 1, keepdims=False)
    last = lax.index_in_dim(split, count - 1, axis + 1, keepdims=False)
    before = jnp.concatenate(
        [jnp.expand_dims(left_edge, axis), lax.slice_in_dim(last, 0, elements - 1, axis=axis)], axis
    )
    after = jnp.concatenate(
        [lax.slice_in_dim(first, 1, elements, axis=axis), jnp.expand_dims(right_edge, axis)], axis
    )
    front = jnp.expand_dims(left_gain * (first - before), axis + 1)
    back = jnp.expand_dims(right_gain * (last - after), axis + 1)
    if count > 2:
        middle_shape = list(front.shape)
        middle_shape[axis + 1] = count - 2
        pieces = [front, jnp.zeros(middle_shape, jnp.float32), back]
    else:
        pieces = [front, back]
    return (linear + jnp.concatenate(pieces, axis + 1)).reshape(shape)


def diag_along(shape, axis, count, table, left_gain, right_gain):
    elements = shape[axis] // count
    split = shape[:axis] + (elements, count) + shape[axis + 1 :]
    profile = [1] * len(split)
    profile[axis + 1] = count
    diagonal_entries = np.array([table[index, index] for index in range(count)])
    base = jnp.broadcast_to(jnp.asarray(diagonal_entries, jnp.float32).reshape(profile), split)
    front = jnp.expand_dims(left_gain, axis + 1)
    back = jnp.expand_dims(right_gain, axis + 1)
    if count > 2:
        middle_shape = list(front.shape)
        middle_shape[axis + 1] = count - 2
        pieces = [front, jnp.zeros(middle_shape, jnp.float32), back]
    else:
        pieces = [front, back]
    return (base + jnp.concatenate(pieces, axis + 1)).reshape(shape)


def level_kappa(kappa, count):
    if count == 5:
        return kappa
    picks = np.array([0, 2, 4]) if count == 3 else np.array([0, 4])
    extents = [extent // 5 for extent in kappa.shape]
    grouped = kappa.reshape(extents[0], 5, extents[1], 5, extents[2], 5)
    for axis in (1, 3, 5):
        grouped = jnp.take(grouped, picks, axis=axis)
    return grouped.reshape(extents[0] * count, extents[1] * count, extents[2] * count)


def face_plane(face, direction, count):
    plane = face.astype(jnp.float32)
    for axis in range(3):
        if axis != direction:
            plane = jnp.repeat(plane, count, axis=axis)
    return plane


def build_level(kappa, flags, count):
    nodes, weights = lobatto(count)
    kappa_level = level_kappa(kappa, count)
    tables, lefts, rights = ([], [], [])
    diagonal = kappa_level
    for direction in range(3):
        table = element_matrix(count, direction)
        lower = face_plane(flags[2 * direction], direction, count)
        upper = face_plane(flags[2 * direction + 1], direction, count)
        left_gain = (ADVECT[direction] * (1.0 + lower) / 2.0 + DIFFUSE * count * count) / float(
            weights[0]
        )
        right_gain = (DIFFUSE * count * count - ADVECT[direction] * (1.0 - upper) / 2.0) / float(
            weights[-1]
        )
        tables.append(table)
        lefts.append(left_gain)
        rights.append(right_gain)
        diagonal = diagonal + diag_along(
            kappa_level.shape, direction, count, table, left_gain, right_gain
        )
    scale = 1.0 / (1.0 + STEP_SIZE * JACOBI_SCALE * diagonal)
    return (count, tables, lefts, rights, kappa_level, scale)


def restrict(field, fine_count, coarse_count):
    fine_nodes, fine_weights = lobatto(fine_count)
    coarse_nodes, coarse_weights = lobatto(coarse_count)
    table = (
        (1.0 / coarse_weights)[:, None]
        * lagrange_table(coarse_nodes, fine_nodes).T
        * fine_weights[None, :]
    )
    for axis in range(field.ndim - 3, field.ndim):
        field = apply_along(field, axis, fine_count, table)
    return field


def prolong(field, coarse_count, fine_count):
    fine_nodes, fine_weights = lobatto(fine_count)
    coarse_nodes, coarse_weights = lobatto(coarse_count)
    table = lagrange_table(coarse_nodes, fine_nodes)
    for axis in range(field.ndim - 3, field.ndim):
        field = apply_along(field, axis, coarse_count, table)
    return field


def chebyshev(rhs, start, level, operator):
    centre = (CHEB_HIGH + CHEB_LOW) / 2.0
    radius = (CHEB_HIGH - CHEB_LOW) / 2.0
    ratio = centre / radius
    first_rho = 1.0 / ratio
    second_rho = 1.0 / (2.0 * ratio - first_rho)
    scale = level[5]
    if start is None:
        remain = rhs
    else:
        remain = rhs - operator(start, level)
    step = scale * remain / centre
    guess = step if start is None else start + step
    remain = remain - operator(step, level)
    step = second_rho * first_rho * step + 2.0 * second_rho / radius * scale * remain
    return guess + step


def vcycle(rhs, levels, operator):
    fine, middle, coarse = levels
    fine_x = chebyshev(rhs, None, fine, operator)
    middle_rhs = restrict(rhs - operator(fine_x, fine), 5, 3)
    middle_x = chebyshev(middle_rhs, None, middle, operator)
    coarse_rhs = restrict(middle_rhs - operator(middle_x, middle), 3, 2)
    coarse_x = chebyshev(coarse_rhs, None, coarse, operator)
    middle_x = chebyshev(middle_rhs, middle_x + prolong(coarse_x, 2, 3), middle, operator)
    return chebyshev(rhs, fine_x + prolong(middle_x, 3, 5), fine, operator)


def spatial(field, level):
    count, tables, lefts, rights, kappa_level, scale = level
    padded = extended(field, (("gx", 1), ("gy", 2)), 1)
    total = kappa_level * field
    total = total + line_part(
        field,
        1,
        count,
        tables[0],
        lefts[0],
        rights[0],
        padded[:, 0, 1:-1, :],
        padded[:, -1, 1:-1, :],
    )
    total = total + line_part(
        field,
        2,
        count,
        tables[1],
        lefts[1],
        rights[1],
        padded[:, 1:-1, 0, :],
        padded[:, 1:-1, -1, :],
    )
    total = total + line_part(
        field, 3, count, tables[2], lefts[2], rights[2], field[:, :, :, -1], field[:, :, :, 0]
    )
    return total


def apply_system(field, level, coupling):
    image = spatial(field, level)
    everyone = lax.all_gather(image, "section", axis=0, tiled=True)
    butcher = jnp.asarray(radau_matrix(), jnp.float32)
    rows = lax.dynamic_slice_in_dim(
        butcher, lax.axis_index("section") * field.shape[0], field.shape[0], 0
    )
    mixed = jnp.einsum("ij,jabc->iabc", rows, everyone, precision=lax.Precision.HIGHEST)
    return field + STEP_SIZE * mixed


def global_total(values):
    return lax.psum(values, ("section", "gx", "gy"))


def stepwise(rhs, guess, kappa, bc_flags):
    levels = [build_level(kappa, bc_flags, count) for count in (5, 3, 2)]
    section_operator = partial(apply_system, coupling=None)
    start_residual = rhs - section_operator(guess, levels[0])
    dofs = float(rhs.size * lax.axis_size("section") * lax.axis_size("gx") * lax.axis_size("gy"))
    beta = jnp.sqrt(global_total(jnp.sum(start_residual * start_residual).reshape(1))[0])
    basis = start_residual / beta
    precond = vcycle(basis, levels, section_operator)
    image = section_operator(precond, levels[0])
    upper = global_total(jnp.sum(image * basis).reshape(1))[0]
    remainder = image - upper * basis
    lower = jnp.sqrt(global_total(jnp.sum(remainder * remainder).reshape(1))[0])
    weight = beta * upper / (upper * upper + lower * lower)
    solution = guess + weight * precond
    residual = start_residual - weight * image
    arnoldi = jnp.stack([beta / math.sqrt(dofs), upper, lower]).astype(jnp.float32)
    return (solution, residual, arnoldi)


EZ = 32
COLS = 16
HALF = 64
FACE_X = HALF + 25
KAPPA = FACE_X + 15
PIECE = KAPPA + 16
LINE_KAPPA = 4 * HALF
LINE_Y = LINE_KAPPA + 4 * 16
LINE = LINE_Y + 104
FIELD = 1000
F32 = jnp.float32


def split_sections():
    matrix = radau_matrix()
    values, vectors = np.linalg.eig(matrix)
    order = [n for n in np.argsort(np.abs(values.imag), kind="stable") if values[n].imag > 0]
    bases = []
    for n in order:
        plane = np.stack([vectors[:, n].real, vectors[:, n].imag], axis=1)
        bases.append(np.linalg.qr(plane)[0])
    left, cross, right = np.linalg.svd(bases[0].T @ bases[1])
    bases = [bases[0] @ left, bases[1] @ right.T]
    for c in range(2):
        sign = np.sign(bases[0][np.argmax(np.abs(bases[0][:, c])), c])
        bases = [np.concatenate([b[:, :c], sign * b[:, c : c + 1], b[:, c + 1 :]], axis=1) for b in bases]
    whole = np.concatenate(bases, axis=1)
    back = np.linalg.inv(whole)
    return whole, back, back @ matrix, back @ matrix @ whole, cross


def iota(shape, dim):
    return lax.broadcasted_iota(jnp.int32, shape, dim)


def exact_dot(a, b):
    return lax.dot_general(
        a, b, (((1,), (0,)), ((), ())), precision=lax.Precision.HIGHEST, preferred_element_type=F32
    )


def split_dot(a, b):
    high = a.astype(jnp.bfloat16)
    rest = a - high.astype(F32)
    middle = rest.astype(jnp.bfloat16)
    low = (rest - middle.astype(F32)).astype(jnp.bfloat16)
    b = b.astype(jnp.bfloat16)
    return sum(
        lax.dot_general(part, b, (((1,), (0,)), ((), ())), preferred_element_type=F32)
        for part in (low, middle, high)
    )


def choose(index, values):
    out = values[-1]
    for place in range(len(values) - 2, -1, -1):
        out = jnp.where(index == place, values[place], out)
    return out


def face_gains(flag, direction, side, count):
    nodes, weights = lobatto(count)
    c, nu = ADVECT[direction], DIFFUSE * count * count
    if side == 0:
        return (c * (1.0 + flag) / 2.0 + nu) * (1.0 / float(weights[0]))
    return (nu - c * (1.0 - flag) / 2.0) * (1.0 / float(weights[-1]))


def row_table():
    kx, ky = (element_matrix(5, d) for d in range(2))
    rows = np.zeros((64, 64))
    for s in range(2):
        for i in range(5):
            for j in range(5):
                r = s * 32 + i * 5 + j
                for m in range(5):
                    rows[r, s * 32 + m * 5 + j] += kx[i, m]
                    rows[r, s * 32 + i * 5 + m] += ky[j, m]
    return rows.astype(np.float32)


def pick_lines(k):
    lane = iota((160, 256), 1)
    return (iota((160, 256), 0) == 5 * (lane % EZ) + k + lane // 128).astype(F32)


def pair_factors(sec, table, own, s):
    upper = iota((32, 128), 1) < 64
    first = jnp.where(upper, float(table[0, s]), float(table[1, s]))
    second = jnp.where(upper, float(table[2, 2 + s]), float(table[3, 2 + s]))
    if not own:
        first = jnp.where(upper, float(table[2, s]), float(table[3, s]))
        second = jnp.where(upper, float(table[0, 2 + s]), float(table[1, 2 + s]))
    return jnp.where(sec == 0, first, second)


def pack_nodes(nodes):
    half = nodes.shape[0] // 2
    odd = iota((half, 128), 1) // EZ % 2 == 1
    return jnp.where(odd, nodes[half:, :], nodes[:half, :])


def fetch(pairs, sems):
    copies = [pltpu.make_async_copy(src, dst, sems.at[n]) for n, (src, dst) in enumerate(pairs)]
    for copy in copies:
        copy.start()
    for copy in copies:
        copy.wait()


def local_kernel(
    rhs_in, guess_in, kappa_in, flags_in, rows_in, mine, theirs,
    rhs, guess, kappa, flags, rows_t, sems, stack, lines, nodes, y_faces, x_faces,
):
    sec = lax.axis_index("section")
    fetch([(rhs_in, rhs), (guess_in, guess), (kappa_in, kappa), (flags_in, flags), (rows_in, rows_t)], sems)
    stack[...] = jnp.zeros_like(stack)
    for i in range(5):
        stack[192 + 5 * i : 197 + 5 * i, :] = kappa[i]
        for j in range(5):
            r = 5 * i + j
            value = guess[i, j]
            left = rhs[i, j] - value
            for s in range(2):
                stack[s * 32 + r : s * 32 + r + 1, :] = left[s : s + 1]
                stack[128 + s * 32 + r : 128 + s * 32 + r + 1, :] = value[s : s + 1]
    stack[64:128, :] = exact_dot(rows_t[...], stack[128:192, :])
    source = stack[...]
    for k in (0, 2, 4):
        shown = split_dot(source, pick_lines(k))
        lines[224 * k : 224 * k + 224, :] = shown[:, :128]
        if k < 4:
            lines[224 * k + 224 : 224 * k + 448, :] = shown[:, 128:]

    def part(k, first):
        return lines[224 * k + first : 224 * k + first + 32, :]

    repeat = (iota((EZ, 128), 1) % EZ == iota((EZ, 128), 0)).astype(F32)
    shown = split_dot(flags[:, 0, 0, :].astype(F32), repeat)
    gains = [face_gains(shown[d : d + 1, :], d // 2, d % 2, 5) for d in range(6)]
    row = iota((32, 128), 0)
    none = jnp.zeros((32, 128), F32)
    own = jnp.where(row < 5, gains[0], jnp.where((row >= 20) & (row < 25), gains[1], none))
    own = own + jnp.where(row % 5 == 0, gains[2], jnp.where(row % 5 == 4, gains[3], none))
    kz = element_matrix(5, 2)
    back, back_matrix = split_sections()[1:3]
    for ref in (nodes, y_faces, x_faces):
        ref[...] = jnp.zeros_like(ref)
    for k in range(5):
        diagonal = part(k, 192) + own
        if k == 0:
            diagonal = diagonal + gains[4]
        if k == 4:
            diagonal = diagonal + gains[5]
        images = []
        for s in range(2):
            first = 128 + 32 * s
            image = diagonal * part(k, first) + part(k, 64 + 32 * s)
            for m in range(5):
                image = image + float(kz[k, m]) * part(m, first)
            if k == 0:
                image = image - gains[4] * pltpu.roll(part(4, first), 1, 1)
            if k == 4:
                image = image - gains[5] * pltpu.roll(part(0, first), 127, 1)
            images.append(image)
        for p, mark in enumerate((True, False)):
            total = jnp.zeros((32, 128), F32)
            trace = jnp.zeros((32, 128), F32)
            for s in range(2):
                total = total + pair_factors(sec, back, mark, s) * part(k, 32 * s)
                factor = pair_factors(sec, STEP_SIZE * back_matrix, mark, s)
                total = total - factor * images[s]
                trace = trace + factor * part(k, 128 + 32 * s)
            nodes[128 * p + 25 * k : 128 * p + 25 * k + 25, :] = total[:25]
            for i in range(5):
                for f in range(2):
                    r = 64 * p + 32 * f + 5 * k + i
                    y_faces[r : r + 1, :] = trace[5 * i + 4 * f : 5 * i + 4 * f + 1]
            for f in range(2):
                r = 32 * p + 16 * f + 3 * k
                x_faces[r : r + 3, :] = trace[20 * f + 1 : 20 * f + 4]
    upper = iota((1, 128), 1) < 64
    for r in range(3):
        nodes[125 + r : 126 + r, :] = jnp.where(upper, shown[2 * r : 2 * r + 1], shown[2 * r + 1 : 2 * r + 2])
    for p, out in enumerate((mine, theirs)):
        out[:HALF, :] = pack_nodes(nodes[128 * p : 128 * p + 128, :])
        out[HALF:FACE_X, :] = pack_nodes(y_faces[64 * p : 64 * p + 64, :])[:25]
        out[FACE_X:KAPPA, :] = pack_nodes(x_faces[32 * p : 32 * p + 32, :])[:15]
    for k in range(5):
        nodes[25 * k : 25 * k + 25, :] = part(k, 192)[:25]
    kappas = choose(iota((32, 128), 1) // EZ, [nodes[32 * q : 32 * q + 32, :] for q in range(4)])
    mine[KAPPA:, :] = jnp.where(sec == 0, kappas[:16], kappas[16:])


def part_kernel(source, piece, kappa):
    piece[...] = source[:KAPPA, :]
    kappa[...] = source[KAPPA:, :]


VMEM = pl.BlockSpec(memory_space=pltpu.VMEM)
HBM = pl.BlockSpec(memory_space=pltpu.HBM)


def limit(mib):
    return pltpu.CompilerParams(vmem_limit_bytes=mib * 2**20)


def local_part(rhs, guess, kappa, flags):
    operands = (rhs, guess, kappa, flags, jnp.asarray(row_table()))
    return pl.pallas_call(
        local_kernel,
        out_shape=[jax.ShapeDtypeStruct((rows, 128), F32) for rows in (PIECE, KAPPA)],
        in_specs=[HBM] * 5,
        out_specs=[VMEM] * 2,
        scratch_shapes=[pltpu.VMEM(o.shape, o.dtype) for o in operands]
        + [
            pltpu.SemaphoreType.DMA((5,)),
            pltpu.VMEM((224, 160), F32),
            pltpu.VMEM((5 * 224, 128), F32),
            pltpu.VMEM((256, 128), F32),
            pltpu.VMEM((128, 128), F32),
            pltpu.VMEM((64, 128), F32),
        ],
        compiler_params=limit(60),
        cost_estimate=pl.CostEstimate(flops=20_000_000, bytes_accessed=8_000_000, transcendentals=0),
        name="local_part",
    )(*operands)


def part(x):
    return pl.pallas_call(
        part_kernel,
        out_shape=[jax.ShapeDtypeStruct((rows, 128), F32) for rows in (KAPPA, 16)],
        in_specs=[VMEM],
        out_specs=[VMEM] * 2,
        compiler_params=limit(16),
        name="part",
    )(x)


class Level:
    def __init__(self, count, refs):
        self.count = count
        self.x, self.dir, self.res, self.f = refs
        self.tables = [element_matrix(count, d) for d in range(3)]
        self.gains = self.diag = self.jac = None


def tile(index):
    return pl.ds(index * 8, 8)


def rows_of(pieces, size, r, h):
    return pieces[pl.ds(8 * h * size + r, 8, stride=size), :]


ORDER_X = ((3, 2), (2, 3), (1, 1))
ORDER_Y = ((1, 2), (2, 1), (3, 3))


def partner(bits):
    return jnp.where(lax.axis_index("section") == 0, bits[0], bits[1])


def place_pieces(blocks, pieces, first, size, room):
    my_gx, my_gy = lax.axis_index("gx"), lax.axis_index("gy")
    for b, block in enumerate(blocks):
        gy = my_gy ^ partner(ORDER_Y[b - 1]) if b else my_gy
        for a in range(4):
            column = (my_gx ^ a) * 4 + gy
            start = pl.multiple_of(column * room, 8)
            pieces[pl.ds(start, size), :] = block[first + a * size : first + a * size + size, :]


class Lanes:
    def __init__(self):
        self.lane = iota((8, 128), 1)
        sub = iota((8, 128), 0)
        self.group = self.lane // EZ
        self.odd = self.group % 2 == 1
        self.element = self.lane % EZ
        self.place = sub % 4
        self.low_half = sub < 4

    def around(self, u):
        turned = pltpu.roll(u, 4, u.ndim - 2)
        far = jnp.where(self.odd, pltpu.roll(turned, 32, u.ndim - 1), pltpu.roll(turned, 96, u.ndim - 1))
        return turned, far

    def x_before(self, u):
        turned, far = self.around(u)
        return jnp.where(self.low_half, far, turned)

    def x_after(self, u):
        turned, far = self.around(u)
        return jnp.where(self.low_half, turned, far)

    def y_before(self, u):
        return jnp.where(self.place == 0, pltpu.roll(u, 5, 0), pltpu.roll(u, 1, 0))

    def y_after(self, u):
        return jnp.where(self.place == 3, pltpu.roll(u, 3, 0), pltpu.roll(u, 7, 0))

    def z_before(self, u):
        return jnp.where(self.element == 0, pltpu.roll(u, 97, u.ndim - 1), pltpu.roll(u, 1, u.ndim - 1))

    def z_after(self, u):
        last = self.element == EZ - 1
        return jnp.where(last, pltpu.roll(u, 31, u.ndim - 1), pltpu.roll(u, 127, u.ndim - 1))


def load(ref, first, count):
    return ref[pl.ds(first * 8, count * 8), :].reshape(count, 8, 128)


def store(ref, first, value):
    ref[pl.ds(first * 8, value.shape[0] * 8), :] = value.reshape(value.shape[0] * 8, 128)


DIAGS = (0, 250, 304)
GAINS = (320, 326, 332)
REGISTERS = 338
CENTRE = (CHEB_HIGH + CHEB_LOW) / 2.0
RADIUS = (CHEB_HIGH - CHEB_LOW) / 2.0


def flag_lanes(row, slot):
    turned = [row] + [pltpu.roll(row, 32 * m, 1) for m in range(1, 4)]
    return choose(iota(row.shape, 1) // EZ, [turned[(g - 2 * slot - 1) % 4] for g in range(4)])


def line_kernel(first, second, third, own, line, faces, sorted_pieces):
    sorted_pieces[:PIECE, :] = own[...]
    for bits, piece in zip(ORDER_X, (first, second, third)):
        sorted_pieces[pl.ds(pl.multiple_of(partner(bits) * PIECE, 8), PIECE), :] = piece[...]
    pieces = [sorted_pieces.at[PIECE * a : PIECE * a + PIECE, :] for a in range(4)]
    even = lax.axis_index("gx") % 2 == 0
    odd = iota((8, 128), 1) // EZ % 2 == 1
    faces[...] = jnp.zeros_like(faces)

    def both(rows, f):
        side = odd[:1] if f else jnp.logical_not(odd[:1])
        return jnp.where(side, rows, pltpu.roll(rows, 96 if f else 32, 1))

    for a, piece in enumerate(pieces):
        for f in range(2):
            base = 64 * a + 32 * f
            inner = both(piece[FACE_X:KAPPA, :], f)
            ends = [both(piece[HALF:FACE_X, :], g) for g in range(2)]
            for k in range(5):
                r = base + 5 * k
                node = 5 * k + 4 * f
                faces[r : r + 1, :] = ends[0][node : node + 1]
                faces[r + 1 : r + 4, :] = inner[3 * k : 3 * k + 3]
                faces[r + 4 : r + 5, :] = ends[1][node : node + 1]
    for a, piece in enumerate(pieces):
        line[HALF * a : HALF * a + HALF, :] = piece[:HALF, :]
        line[LINE_KAPPA + 16 * a : LINE_KAPPA + 16 * a + 16, :] = piece[KAPPA:, :]
        line[LINE_Y + 25 * a : LINE_Y + 25 * a + 25, :] = piece[HALF:FACE_X, :]
        flags = [flag_lanes(piece[61:62, :], slot) for slot in range(2)]
        gains = [face_gains(flags[d], 0, d, 5) for d in range(2)]
        next_first = even if a % 2 == 0 else jnp.logical_not(even)
        for f in range(2):
            one = faces[64 * (a ^ 1) + 32 * (1 - f) : 64 * (a ^ 1) + 32 * (1 - f) + 32, :]
            three = faces[64 * (a ^ 3) + 32 * (1 - f) : 64 * (a ^ 3) + 32 * (1 - f) + 32, :]
            near = jnp.where(next_first, one, three) if f else jnp.where(next_first, three, one)
            term = gains[f] * near
            for k in range(5):
                node = 25 * k + 20 * f
                side = odd[:5] if node >= HALF else jnp.logical_not(odd[:5])
                r = HALF * a + node % HALF
                line[r : r + 5, :] = line[r : r + 5, :] + jnp.where(side, term[5 * k : 5 * k + 5], 0.0)
    line[LINE_Y + 100 :, :] = jnp.zeros((4, 128), F32)


def halves_kernel(block0, block1, block2, block3, out):
    place_pieces((block0, block1, block2, block3), out, LINE_KAPPA, 16, 16)


def widen(low, high, odd):
    return jnp.where(odd, pltpu.roll(high, 32, 1), low), jnp.where(odd, high, pltpu.roll(low, 96, 1))


def assemble_kernel(block0, block1, block2, block3, field, pieces, edges, traces):
    blocks = (block0, block1, block2, block3)
    place_pieces(blocks, pieces, 0, HALF, HALF)
    place_pieces(blocks, edges, LINE_Y, 25, 32)
    lanes = Lanes()
    for source, size, rows, target, apart in ((edges, 32, 25, traces, 25), (pieces, HALF, HALF, field, HALF)):
        for r in range(rows):
            first, second = widen(rows_of(source, size, r, 0), rows_of(source, size, r, 1), lanes.odd)
            target[tile(r), :] = first
            target[tile(apart + r), :] = second
    got = field[tile(126), :]
    across = pltpu.roll(got, 64, 1)
    gains = [
        face_gains(jnp.where(lanes.lane < 64, got, across), 1, 0, 5),
        face_gains(jnp.where(lanes.lane < 64, across, got), 1, 1, 5),
    ]
    for k in range(5):
        for i in range(5):
            lower, upper = traces[tile(5 * k + i), :], traces[tile(25 + 5 * k + i), :]
            node = 25 * k + 5 * i
            field[tile(node), :] = field[tile(node), :] + gains[0] * lanes.y_before(upper)
            field[tile(node + 4), :] = field[tile(node + 4), :] + gains[1] * lanes.y_after(lower)


def setup_kernel(field, own_halves, other_halves, coefs, kap):
    sec = lax.axis_index("section")
    lanes = Lanes()
    group, lane = lanes.group, lanes.lane
    flags = []
    for r in range(3):
        got = field[tile(125 + r), :]
        across = pltpu.roll(got, 64, 1)
        flags += [jnp.where(lane < 64, got, across), jnp.where(lane < 64, across, got)]
    for r in range(16):
        pairs = [[rows_of(ref, 16, r, h) for h in range(2)] for ref in (own_halves, other_halves)]
        for half in range(2):
            turned = []
            for h in range(2):
                got = jnp.where(sec == half, pairs[0][h], pairs[1][h])
                turned.append([pltpu.roll(got, 32 * m, 1) if m else got for m in range(4)])
            for q in range(4):
                value = choose(group, [turned[g % 2][(g - q) % 4] for g in range(4)])
                kap[tile(q * 32 + half * 16 + r), :] = value
    for p, n in enumerate((5, 3, 2)):
        stride = 4 // (n - 1)
        gains = [face_gains(flags[d], d // 2, d % 2, n) for d in range(6)]
        rows = []
        for d in range(3):
            coefs[tile(GAINS[p] + 2 * d), :] = gains[2 * d]
            coefs[tile(GAINS[p] + 2 * d + 1), :] = gains[2 * d + 1]
            table = element_matrix(n, d)
            row = [jnp.full((8, 128), float(table[m, m]), F32) for m in range(n)]
            row[0] = row[0] + gains[2 * d]
            row[n - 1] = row[n - 1] + gains[2 * d + 1]
            rows.append(row)
        along = jnp.stack(rows[1])
        for k in range(n):
            for i in range(n):
                line = load(kap, k * 25 * stride + i * stride * 5, 5)
                line = jnp.stack([line[j * stride] for j in range(n)])
                value = line + (along + (rows[2][k] + rows[0][i]))
                scale = 1.0 / (1.0 + STEP_SIZE * JACOBI_SCALE * value)
                store(coefs, DIAGS[p] + (k * n + i) * n, value)
                store(coefs, DIAGS[p] + n**3 + (k * n + i) * n, scale * (1.0 / CENTRE))


def cycle_kernel(coefs, assembled, fields, *scratch):
    sec = lax.axis_index("section")
    my_gx, my_gy = lax.axis_index("gx"), lax.axis_index("gy")
    levels = [Level(n, scratch[4 * p : 4 * p + 4]) for p, n in enumerate((5, 3, 2))]
    half = scratch[12]
    lanes = Lanes()
    lane = lanes.lane
    blocks = split_sections()[3]

    def lanes_of(upper, lower):
        return jnp.where(lane < 64, jnp.where(sec == 0, upper[0], upper[1]), jnp.where(sec == 0, lower[0], lower[1]))

    entry = [[[float(STEP_SIZE * blocks[2 * p + a, 2 * p + b]) for p in range(2)] for b in range(2)] for a in range(2)]
    same = lanes_of(entry[0][0], entry[1][1])
    swap = lanes_of(entry[0][1], entry[1][0])
    first_rho = RADIUS / CENTRE
    second_rho = 1.0 / (2.0 * CENTRE / RADIUS - first_rho)
    keep = 1.0 + second_rho * first_rho
    push = 2.0 * second_rho / RADIUS * CENTRE
    for p, level in enumerate(levels):
        size = level.count**3
        level.gains = [-coefs[tile(GAINS[p] + d), :] for d in range(6)]
        level.diag = lambda first, count, p=p: load(coefs, DIAGS[p] + first, count)
        level.jac = lambda first, count, p=p, size=size: load(coefs, DIAGS[p] + size + first, count)

    def begin(level, source):
        n = level.count
        for first in range(0, n**3, n):
            f = load(source, first, n)
            store(level.dir, first, level.jac(first, n) * f)
            store(level.res, first, f)
            store(level.x, first, jnp.zeros_like(f))

    def apply(level, smooth):
        n = level.count
        kx, ky, kz = level.tables
        gains = level.gains
        source = level.dir if smooth else level.x
        def tree(terms):
            while len(terms) > 1:
                pairs = [a + b for a, b in zip(terms[::2], terms[1::2])]
                terms = pairs + terms[len(terms) // 2 * 2 :]
            return terms[0]

        def sums(k):
            def line_at(i):
                return load(source, (k * n + i) * n, n)

            x_left = gains[0] * lanes.x_before(line_at(n - 1))
            x_right = gains[1] * lanes.x_after(line_at(0))
            z_low, z_high, y_low, y_high = [], [], [], []
            for i in range(n):
                if k == 0:
                    z_low.append(gains[4] * lanes.z_before(load(source, ((n - 1) * n + i) * n, n)))
                if k == n - 1:
                    z_high.append(gains[5] * lanes.z_after(load(source, i * n, n)))
                v = line_at(i)
                y_low.append(gains[2] * lanes.y_before(v[n - 1]))
                y_high.append(gains[3] * lanes.y_after(v[0]))
            totals = []
            for i in range(n):
                first = (k * n + i) * n
                v = line_at(i)
                along_x = [float(kx[i, m]) * line_at(m) for m in range(n) if m != i]
                along_z = [float(kz[k, m]) * load(source, (m * n + i) * n, n) for m in range(n) if m != k]
                along_y = []
                for j in range(n):
                    terms = [float(ky[j, m]) * v[m] for m in range(n) if m != j]
                    if j == 0:
                        terms.append(y_low[i])
                    if j == n - 1:
                        terms.append(y_high[i])
                    along_y.append(tree(terms))
                if i == 0:
                    along_x.append(x_left)
                if i == n - 1:
                    along_x.append(x_right)
                if k == 0:
                    along_z.append(z_low[i])
                if k == n - 1:
                    along_z.append(z_high[i])
                totals.append(tree([level.diag(first, n) * v, tree(along_x), tree(along_z), jnp.stack(along_y)]))
            return totals

        def update(k, totals):
            moved = [pltpu.roll(total, 64, 2) for total in totals]
            for i in range(n):
                first = (k * n + i) * n
                v = load(source, first, n)
                image = v + (same * totals[i] + swap * moved[i])
                if smooth:
                    scaled = level.jac(first, n) * (load(level.res, first, n) - image)
                    store(level.x, first, (load(level.x, first, n) + keep * v) + push * scaled)
                else:
                    rest = load(level.f, first, n) - image
                    store(level.res, first, rest)
                    store(level.dir, first, level.jac(first, n) * rest)

        if n == 5:
            ready = sums(0)
            for k in range(n):
                following = sums(k + 1) if k + 1 < n else None
                update(k, ready)
                ready = following
        else:
            for k, totals in enumerate([sums(k) for k in range(n)]):
                update(k, totals)

    def combine(weights, parts):
        total = None
        for weight, part in zip(weights, parts):
            if abs(weight) > 1e-14:
                term = part if abs(weight - 1.0) < 1e-14 else float(weight) * part
                total = term if total is None else total + term
        return total

    def change(table, source, target, add):
        m, n = table.shape
        for i in range(n):
            parts = [load(source, i * n + k * n * n, n) for k in range(n)]
            for k in range(m):
                store(half, i * n + k * n * n, combine(table[k], parts))
        for k in range(m):
            parts = [load(half, k * n * n + i * n, n) for i in range(n)]
            for i in range(m):
                line = combine(table[i], parts)
                value = jnp.stack([combine(table[j], [line[a] for a in range(n)]) for j in range(m)])
                first = k * m * m + i * m
                store(target, first, load(target, first, m) + value if add else value)

    def down(n, m):
        fine_nodes, fine_weights = lobatto(n)
        coarse_nodes, coarse_weights = lobatto(m)
        table = lagrange_table(coarse_nodes, fine_nodes)
        return (1.0 / coarse_weights)[:, None] * table.T * fine_weights[None, :]

    def up(m, n):
        return lagrange_table(lobatto(m)[0], lobatto(n)[0])

    def solve(p):
        level = levels[p]
        if p == 2:
            apply(level, True)
            return
        below = levels[p + 1]

        def step(t, carry):
            @pl.when(t != 1)
            def _():
                apply(level, True)

            @pl.when((t != 2) | (p == 0))
            def _():
                apply(level, False)

            @pl.when(t == 0)
            def _():
                n, m = level.count, below.count
                change(down(n, m), level.res, below.f, False)
                begin(below, below.f)
                solve(p + 1)
                change(up(m, n), below.x, level.x, True)
            return carry
        lax.fori_loop(0, 3, step, 0)

    fine = levels[0]
    fine.f = assembled
    begin(fine, assembled)
    solve(0)

    for first in range(0, 125, 5):
        store(fields, first, load(fine.res, first, 5))
    column = (my_gx % 2) * 4 + my_gy
    fields[FIELD : FIELD + 125, :] = fine.x[pl.ds(column, 125, stride=8), :]
    fields[FIELD + 125 : FIELD + 128, :] = jnp.zeros((3, 128), F32)


def pair_weights():
    cross = split_sections()[4]
    return jnp.where(iota((8, 128), 1) < 64, float(cross[0]), float(cross[1]))


def column_factors(p):
    sec = lax.axis_index("section")
    whole = split_sections()[0]
    lane = iota((25, 128), 1)
    here = lane // EZ % 2 == lax.axis_index("gx") // 2
    factors = []
    for s in range(2):
        parts = []
        for mine in range(2):
            t = whole[2 * mine + s]
            q = mine if p == 0 else 1 - mine
            parts.append(jnp.where(lane < 64, float(t[2 * q]), float(t[2 * q + 1])))
        factors.append(jnp.where(here, jnp.where(sec == 0, parts[0], parts[1]), 0.0))
    return factors


def column_rows(k):
    column = (lax.axis_index("gx") % 2) * 4 + lax.axis_index("gy")
    return pl.ds(k * 200 + column, 25, stride=8)


def raw_order(k):
    lane = iota((256, 160), 0)
    return (iota((256, 160), 1) == 5 * (lane % EZ) + k + lane // 128).astype(F32)


def early_kernel(own, own_start, other_start, sums, column_out, cols):
    weights = pair_weights()
    cols[...] = jnp.zeros_like(cols)
    total = jnp.zeros((192, 160), F32)
    own_factors, other_factors = column_factors(0), column_factors(1)
    for k in range(5):
        where = column_rows(k)
        z = own[FIELD + k * 25 : FIELD + k * 25 + 25, :]
        start, other = own_start[where, :], other_start[where, :]
        w = start - own[where, :]
        side = slice(0, 128) if k % 2 == 0 else slice(128, 256)
        for s in range(2):
            cols[s * 32 : s * 32 + 25, side] = own_factors[s] * z
            cols[64 + s * 32 : 64 + s * 32 + 25, side] = own_factors[s] * start + other_factors[s] * other
            cols[128 + s * 32 : 128 + s * 32 + 25, side] = own_factors[s] * w
        if k % 2 == 1:
            total = total + split_dot(cols[...], raw_order(k - 1))
    cols[:, 128:] = jnp.zeros((192, 128), F32)
    total = total + split_dot(cols[...], raw_order(4))
    column_out[...] = total
    nothing = jnp.zeros((8, 128), F32)
    uppers, sizes = [nothing] * 5, [nothing] * 5
    for r in range(125):
        c, d = own_start[tile(r), :], other_start[tile(r), :]
        a = c - own[tile(r), :]
        uppers[r % 5] = uppers[r % 5] + a * (c + weights * d)
        sizes[r % 5] = sizes[r % 5] + ((c * c + d * d) + 2.0 * (weights * (c * d)))
    sums[0:8, :] = sum(uppers)
    sums[8:16, :] = jnp.broadcast_to(jnp.sum(sum(sizes), keepdims=True), (8, 128))


def finish_kernel(own, other, own_start, other_start, sums, column, guess, sol, res_out, arnoldi, cols, outs):
    weights = pair_weights()
    nothing = jnp.zeros((8, 128), F32)
    uppers = [nothing] * 5
    for r in range(125):
        c, d = own_start[tile(r), :], other_start[tile(r), :]
        b = d - other[tile(r), :]
        uppers[r % 5] = uppers[r % 5] + b * (d + weights * c)

    mine, theirs = sums[0:8, :], sum(uppers)
    size = sums[8:9, 0:1]
    upper = jnp.sum(mine + theirs, keepdims=True) / size
    cols[...] = jnp.zeros_like(cols)
    total = jnp.zeros((128, 160), F32)
    factors = column_factors(1)
    for k in range(5):
        where = column_rows(k)
        z = other[FIELD + k * 25 : FIELD + k * 25 + 25, :]
        w = other_start[where, :] - other[where, :]
        side = slice(0, 128) if k % 2 == 0 else slice(128, 256)
        for s in range(2):
            cols[s * 32 : s * 32 + 25, side] = factors[s] * z
            cols[64 + s * 32 : 64 + s * 32 + 25, side] = factors[s] * w
        if k % 2 == 1:
            total = total + split_dot(cols[...], raw_order(k - 1))
    cols[:, 128:] = jnp.zeros((128, 128), F32)
    total = total + split_dot(cols[...], raw_order(4))
    rests = [nothing] * 5
    for r in range(125):
        c, d = own_start[tile(r), :], other_start[tile(r), :]
        a = (c - own[tile(r), :]) - upper * c
        b = (d - other[tile(r), :]) - upper * d
        rests[r % 5] = rests[r % 5] + ((a * a + b * b) + 2.0 * (weights * (a * b)))
    rest = jnp.sum(sum(rests), keepdims=True)
    beta = jnp.sqrt(size)
    lower = jnp.sqrt(rest) / beta
    weight = upper / (upper * upper + lower * lower)
    entries = float(125 * EZ * COLS * 4)
    for place_out, value in enumerate((beta * (1.0 / math.sqrt(entries)), upper, lower)):
        arnoldi[place_out] = value[0, 0]
    outs[:64, :] = weight * (column[:64, :] + total[:64])
    outs[64:, :] = column[64:128, :] - weight * (column[128:, :] + total[64:])
    for i in range(5):
        for j in range(5):
            r = 5 * i + j
            for s in range(2):
                sol[i, j, s : s + 1, :] = guess[i, j, s : s + 1, :] + outs[s * 32 + r : s * 32 + r + 1, :]
                res_out[i, j, s : s + 1, :] = outs[64 + s * 32 + r : 64 + s * 32 + r + 1, :]


def plain_call(kernel, name, rows, scratch, operands, cost=1_000_000):
    return pl.pallas_call(
        kernel,
        out_shape=jax.ShapeDtypeStruct((rows, 128), F32),
        in_specs=[VMEM] * len(operands),
        out_specs=VMEM,
        scratch_shapes=[pltpu.VMEM((r, 128), F32) for r in scratch],
        compiler_params=limit(16),
        cost_estimate=pl.CostEstimate(flops=cost, bytes_accessed=cost, transcendentals=0),
        name=name,
    )(*operands)


def cycle(coefs, assembled):
    scratch = []
    for n in (5, 3, 2):
        scratch += [pltpu.VMEM((n**3 * 8, 128), F32)] * 4
    scratch += [pltpu.VMEM((FIELD, 128), F32)]
    return pl.pallas_call(
        cycle_kernel,
        out_shape=jax.ShapeDtypeStruct((FIELD + 128, 128), F32),
        in_specs=[VMEM] * 2,
        out_specs=VMEM,
        scratch_shapes=scratch,
        compiler_params=limit(24),
        cost_estimate=pl.CostEstimate(flops=40_000_000, bytes_accessed=30_000_000, transcendentals=0),
        name="cycle",
    )(coefs, assembled)


def early(own, own_start, other_start):
    return pl.pallas_call(
        early_kernel,
        out_shape=[jax.ShapeDtypeStruct((16, 128), F32), jax.ShapeDtypeStruct((192, 160), F32)],
        in_specs=[VMEM] * 3,
        out_specs=[VMEM] * 2,
        scratch_shapes=[pltpu.VMEM((192, 256), F32)],
        compiler_params=limit(16),
        cost_estimate=pl.CostEstimate(flops=4_000_000, bytes_accessed=4_000_000, transcendentals=0),
        name="early",
    )(own, own_start, other_start)


def finish(own, other, own_start, other_start, sums, column, guess):
    return pl.pallas_call(
        finish_kernel,
        out_shape=[
            jax.ShapeDtypeStruct(guess.shape, F32),
            jax.ShapeDtypeStruct(guess.shape, F32),
            jax.ShapeDtypeStruct((3,), F32),
        ],
        in_specs=[VMEM] * 7,
        out_specs=[VMEM, VMEM, pl.BlockSpec(memory_space=pltpu.SMEM)],
        scratch_shapes=[pltpu.VMEM((128, 256), F32), pltpu.VMEM((128, 160), F32)],
        compiler_params=limit(24),
        name="finish",
    )(own, other, own_start, other_start, sums, column, guess)


def exchange(x, axis, bits):
    return lax.ppermute(x, axis, [(n, n ^ bits) for n in range(lax.axis_size(axis))])


def exchange_by_core(x, axis, bits):
    count = lax.axis_size(axis)
    pairs = [(s * count + n, s * count + (n ^ bits[s])) for s in range(2) for n in range(count)]
    return lax.ppermute(x, ("section", axis), pairs)


def gathered_body(rhs, guess, kappa, bc_flags):
    rhs, guess = (jnp.transpose(v, (1, 2, 0, 3)) for v in (rhs, guess))
    mine, theirs = local_part(rhs, guess, kappa, bc_flags)
    got, mine, kappa_piece = lax.optimization_barrier((exchange(theirs, "section", 1), *part(mine)))
    piece = jnp.concatenate([mine + got, kappa_piece])
    pieces = [exchange_by_core(piece, "gx", bits) for bits in ORDER_X] + [piece]
    line = plain_call(line_kernel, "line", LINE, [4 * 64, 4 * PIECE], pieces)
    blocks = [line] + [exchange_by_core(line, "gy", bits) for bits in ORDER_Y]
    halves = plain_call(halves_kernel, "halves", COLS * 16, [], blocks)
    other_halves = exchange(halves, "section", 1)
    start = plain_call(assemble_kernel, "assemble", 128 * 8, [COLS * HALF, COLS * 32, 50 * 8], blocks, 4_000_000)
    start, other_halves = lax.optimization_barrier((start, other_halves))
    coefs = plain_call(setup_kernel, "setup", REGISTERS * 8, [128 * 8], (start, halves, other_halves))
    other_start = exchange(start, "section", 1)
    own, other_start = lax.optimization_barrier((cycle(coefs, start), other_start))
    sums, column = early(own, start, other_start)
    sol, res, arnoldi = finish(own, exchange(own, "section", 1), start, other_start, sums, column, guess)
    sol, res = (jnp.transpose(v, (2, 0, 1, 3)) for v in (sol, res))
    return sol, res, arnoldi


def solution(mesh):
    placed = (
        P("section", "gx", "gy", None),
        P("section", "gx", "gy", None),
        P("gx", "gy", None),
        P(None, "gx", "gy", None),
    )
    sizes = (mesh.shape["section"], mesh.shape["gx"], mesh.shape["gy"])

    def step(rhs, guess, kappa, bc_flags):
        fits = sizes == (2, 4, 4) and rhs.shape == (4, 20, 20, 160)
        return jax.shard_map(
            gathered_body if fits else stepwise,
            mesh=mesh,
            in_specs=placed,
            out_specs=(P("section", "gx", "gy", None), P("section", "gx", "gy", None), P()),
            check_vma=False,
        )(rhs, guess, kappa, bc_flags)

    return step
```

```python
from functools import partial
import math

import jax
import jax.numpy as jnp
import numpy as np
from jax import lax
from jax.experimental import pallas as pl
from jax.experimental.pallas import tpu as pltpu
from jax.sharding import PartitionSpec as P

ADVECT = (1.0, 0.7, 0.5)
DIFFUSE = 0.05
STEP_SIZE = 0.2
JACOBI_SCALE = 0.25
CHEB_LOW = 0.25
CHEB_HIGH = 2.0
LETTERS = "abcdef"


def extended(x, sides, width):
    for axis, dim in sides:
        peers, length = (lax.axis_size(axis), x.shape[dim])
        up = [(i, (i + 1) % peers) for i in range(peers)]
        down = [(j, i) for i, j in up]
        last = lax.slice_in_dim(x, length - width, length, axis=dim)
        leading = lax.slice_in_dim(x, 0, width, axis=dim)
        before = lax.ppermute(last, axis, up)
        after = lax.ppermute(leading, axis, down)
        x = jnp.concatenate([before, x, after], axis=dim)
    return x


def lobatto(count):
    if count == 5:
        inner = math.sqrt(3.0 / 7.0)
        return (
            np.array([-1.0, -inner, 0.0, inner, 1.0]),
            np.array([0.1, 49.0 / 90.0, 32.0 / 45.0, 49.0 / 90.0, 0.1]),
        )
    if count == 3:
        return (np.array([-1.0, 0.0, 1.0]), np.array([1.0 / 3.0, 4.0 / 3.0, 1.0 / 3.0]))
    return (np.array([-1.0, 1.0]), np.array([1.0, 1.0]))


def lagrange_table(nodes, points):
    table = np.ones((len(points), len(nodes)))
    for column in range(len(nodes)):
        for other in range(len(nodes)):
            if other != column:
                table[:, column] *= (points - nodes[other]) / (nodes[column] - nodes[other])
    return table


def slope_table(nodes):
    total = len(nodes)
    factor = np.array(
        [np.prod([nodes[i] - nodes[k] for k in range(total) if k != i]) for i in range(total)]
    )
    table = np.zeros((total, total))
    for row in range(total):
        for column in range(total):
            if row != column:
                table[row, column] = factor[row] / factor[column] / (nodes[row] - nodes[column])
        table[row, row] = -np.sum(table[row])
    return table


def element_matrix(count, direction):
    nodes, weights = lobatto(count)
    slopes = slope_table(nodes)
    stiffness = (1.0 / weights)[:, None] * (slopes.T @ (weights[:, None] * slopes))
    return ADVECT[direction] * slopes + DIFFUSE * stiffness


def legendre_pair(point, order):
    values = [1.0, point]
    slopes = [0.0, 1.0]
    for index in range(1, order):
        values.append(
            ((2 * index + 1) * point * values[index] - index * values[index - 1]) / (index + 1)
        )
        slopes.append(slopes[index - 1] + (2 * index + 1) * values[index])
    return (values, slopes)


def radau_nodes():
    starts = [0.0885879595127039, 0.4094668644407347, 0.7876594617608471]
    found = []
    for start in starts:
        point = start
        for sweep in range(30):
            values, slopes = legendre_pair(2.0 * point - 1.0, 4)
            change = (values[4] - values[3]) / (2.0 * (slopes[4] - slopes[3]))
            point = point - change
        found.append(point)
    found.append(1.0)
    return found


def poly_times(coefs, root):
    result = [0.0] * (len(coefs) + 1)
    for index in range(len(coefs)):
        result[index + 1] += coefs[index]
        result[index] -= root * coefs[index]
    return result


def radau_matrix():
    order = 4
    nodes = radau_nodes()
    matrix = np.zeros((order, order))
    for column in range(order):
        coefs = [1.0]
        denominator = 1.0
        for other in range(order):
            if other != column:
                coefs = poly_times(coefs, nodes[other])
                denominator *= nodes[column] - nodes[other]
        for row in range(order):
            upper_end = nodes[row]
            integral = 0.0
            for index in range(len(coefs)):
                integral += coefs[index] * upper_end ** (index + 1) / (index + 1)
            matrix[row, column] = integral / denominator
    return matrix


def node_einsum(table, field, axis):
    labels = LETTERS[: field.ndim]
    source = labels[: axis + 1] + "j" + labels[axis + 2 :]
    target = labels[: axis + 1] + "i" + labels[axis + 2 :]
    return jnp.einsum(
        "ij," + source + "->" + target,
        jnp.asarray(table, jnp.float32),
        field,
        precision=lax.Precision.HIGHEST,
    )


def apply_along(field, axis, count, table):
    shape = field.shape
    split = shape[:axis] + (shape[axis] // count, count) + shape[axis + 1 :]
    mapped = node_einsum(table, field.reshape(split), axis)
    return mapped.reshape(
        shape[:axis] + (mapped.shape[axis] * mapped.shape[axis + 1],) + shape[axis + 1 :]
    )


def line_part(field, axis, count, table, left_gain, right_gain, left_edge, right_edge):
    shape = field.shape
    elements = shape[axis] // count
    split = field.reshape(shape[:axis] + (elements, count) + shape[axis + 1 :])
    linear = node_einsum(table, split, axis)
    first = lax.index_in_dim(split, 0, axis + 1, keepdims=False)
    last = lax.index_in_dim(split, count - 1, axis + 1, keepdims=False)
    before = jnp.concatenate(
        [jnp.expand_dims(left_edge, axis), lax.slice_in_dim(last, 0, elements - 1, axis=axis)], axis
    )
    after = jnp.concatenate(
        [lax.slice_in_dim(first, 1, elements, axis=axis), jnp.expand_dims(right_edge, axis)], axis
    )
    front = jnp.expand_dims(left_gain * (first - before), axis + 1)
    back = jnp.expand_dims(right_gain * (last - after), axis + 1)
    if count > 2:
        middle_shape = list(front.shape)
        middle_shape[axis + 1] = count - 2
        pieces = [front, jnp.zeros(middle_shape, jnp.float32), back]
    else:
        pieces = [front, back]
    return (linear + jnp.concatenate(pieces, axis + 1)).reshape(shape)


def diag_along(shape, axis, count, table, left_gain, right_gain):
    elements = shape[axis] // count
    split = shape[:axis] + (elements, count) + shape[axis + 1 :]
    profile = [1] * len(split)
    profile[axis + 1] = count
    diagonal_entries = np.array([table[index, index] for index in range(count)])
    base = jnp.broadcast_to(jnp.asarray(diagonal_entries, jnp.float32).reshape(profile), split)
    front = jnp.expand_dims(left_gain, axis + 1)
    back = jnp.expand_dims(right_gain, axis + 1)
    if count > 2:
        middle_shape = list(front.shape)
        middle_shape[axis + 1] = count - 2
        pieces = [front, jnp.zeros(middle_shape, jnp.float32), back]
    else:
        pieces = [front, back]
    return (base + jnp.concatenate(pieces, axis + 1)).reshape(shape)


def level_kappa(kappa, count):
    if count == 5:
        return kappa
    picks = np.array([0, 2, 4]) if count == 3 else np.array([0, 4])
    extents = [extent // 5 for extent in kappa.shape]
    grouped = kappa.reshape(extents[0], 5, extents[1], 5, extents[2], 5)
    for axis in (1, 3, 5):
        grouped = jnp.take(grouped, picks, axis=axis)
    return grouped.reshape(extents[0] * count, extents[1] * count, extents[2] * count)


def face_plane(face, direction, count):
    plane = face.astype(jnp.float32)
    for axis in range(3):
        if axis != direction:
            plane = jnp.repeat(plane, count, axis=axis)
    return plane


def build_level(kappa, flags, count):
    nodes, weights = lobatto(count)
    kappa_level = level_kappa(kappa, count)
    tables, lefts, rights = ([], [], [])
    diagonal = kappa_level
    for direction in range(3):
        table = element_matrix(count, direction)
        lower = face_plane(flags[2 * direction], direction, count)
        upper = face_plane(flags[2 * direction + 1], direction, count)
        left_gain = (ADVECT[direction] * (1.0 + lower) / 2.0 + DIFFUSE * count * count) / float(
            weights[0]
        )
        right_gain = (DIFFUSE * count * count - ADVECT[direction] * (1.0 - upper) / 2.0) / float(
            weights[-1]
        )
        tables.append(table)
        lefts.append(left_gain)
        rights.append(right_gain)
        diagonal = diagonal + diag_along(
            kappa_level.shape, direction, count, table, left_gain, right_gain
        )
    scale = 1.0 / (1.0 + STEP_SIZE * JACOBI_SCALE * diagonal)
    return (count, tables, lefts, rights, kappa_level, scale)


def restrict(field, fine_count, coarse_count):
    fine_nodes, fine_weights = lobatto(fine_count)
    coarse_nodes, coarse_weights = lobatto(coarse_count)
    table = (
        (1.0 / coarse_weights)[:, None]
        * lagrange_table(coarse_nodes, fine_nodes).T
        * fine_weights[None, :]
    )
    for axis in range(field.ndim - 3, field.ndim):
        field = apply_along(field, axis, fine_count, table)
    return field


def prolong(field, coarse_count, fine_count):
    fine_nodes, fine_weights = lobatto(fine_count)
    coarse_nodes, coarse_weights = lobatto(coarse_count)
    table = lagrange_table(coarse_nodes, fine_nodes)
    for axis in range(field.ndim - 3, field.ndim):
        field = apply_along(field, axis, coarse_count, table)
    return field


def chebyshev(rhs, start, level, operator):
    centre = (CHEB_HIGH + CHEB_LOW) / 2.0
    radius = (CHEB_HIGH - CHEB_LOW) / 2.0
    ratio = centre / radius
    first_rho = 1.0 / ratio
    second_rho = 1.0 / (2.0 * ratio - first_rho)
    scale = level[5]
    if start is None:
        remain = rhs
    else:
        remain = rhs - operator(start, level)
    step = scale * remain / centre
    guess = step if start is None else start + step
    remain = remain - operator(step, level)
    step = second_rho * first_rho * step + 2.0 * second_rho / radius * scale * remain
    return guess + step


def vcycle(rhs, levels, operator):
    fine, middle, coarse = levels
    fine_x = chebyshev(rhs, None, fine, operator)
    middle_rhs = restrict(rhs - operator(fine_x, fine), 5, 3)
    middle_x = chebyshev(middle_rhs, None, middle, operator)
    coarse_rhs = restrict(middle_rhs - operator(middle_x, middle), 3, 2)
    coarse_x = chebyshev(coarse_rhs, None, coarse, operator)
    middle_x = chebyshev(middle_rhs, middle_x + prolong(coarse_x, 2, 3), middle, operator)
    return chebyshev(rhs, fine_x + prolong(middle_x, 3, 5), fine, operator)


def spatial(field, level):
    count, tables, lefts, rights, kappa_level, scale = level
    padded = extended(field, (("gx", 1), ("gy", 2)), 1)
    total = kappa_level * field
    total = total + line_part(
        field,
        1,
        count,
        tables[0],
        lefts[0],
        rights[0],
        padded[:, 0, 1:-1, :],
        padded[:, -1, 1:-1, :],
    )
    total = total + line_part(
        field,
        2,
        count,
        tables[1],
        lefts[1],
        rights[1],
        padded[:, 1:-1, 0, :],
        padded[:, 1:-1, -1, :],
    )
    total = total + line_part(
        field, 3, count, tables[2], lefts[2], rights[2], field[:, :, :, -1], field[:, :, :, 0]
    )
    return total


def apply_system(field, level, coupling):
    image = spatial(field, level)
    everyone = lax.all_gather(image, "section", axis=0, tiled=True)
    butcher = jnp.asarray(radau_matrix(), jnp.float32)
    rows = lax.dynamic_slice_in_dim(
        butcher, lax.axis_index("section") * field.shape[0], field.shape[0], 0
    )
    mixed = jnp.einsum("ij,jabc->iabc", rows, everyone, precision=lax.Precision.HIGHEST)
    return field + STEP_SIZE * mixed


def global_total(values):
    return lax.psum(values, ("section", "gx", "gy"))


def stepwise(rhs, guess, kappa, bc_flags):
    levels = [build_level(kappa, bc_flags, count) for count in (5, 3, 2)]
    section_operator = partial(apply_system, coupling=None)
    start_residual = rhs - section_operator(guess, levels[0])
    dofs = float(rhs.size * lax.axis_size("section") * lax.axis_size("gx") * lax.axis_size("gy"))
    beta = jnp.sqrt(global_total(jnp.sum(start_residual * start_residual).reshape(1))[0])
    basis = start_residual / beta
    precond = vcycle(basis, levels, section_operator)
    image = section_operator(precond, levels[0])
    upper = global_total(jnp.sum(image * basis).reshape(1))[0]
    remainder = image - upper * basis
    lower = jnp.sqrt(global_total(jnp.sum(remainder * remainder).reshape(1))[0])
    weight = beta * upper / (upper * upper + lower * lower)
    solution = guess + weight * precond
    residual = start_residual - weight * image
    arnoldi = jnp.stack([beta / math.sqrt(dofs), upper, lower]).astype(jnp.float32)
    return (solution, residual, arnoldi)


EZ = 32
COLS = 16
HALF = 64
FACE_X = HALF + 25
KAPPA = FACE_X + 15
PIECE = KAPPA + 16
LINE_KAPPA = 4 * HALF
LINE_Y = LINE_KAPPA + 4 * 16
LINE = LINE_Y + 104
FIELD = 1000
F32 = jnp.float32


def split_sections():
    matrix = radau_matrix()
    values, vectors = np.linalg.eig(matrix)
    order = [n for n in np.argsort(np.abs(values.imag), kind="stable") if values[n].imag > 0]
    bases = []
    for n in order:
        plane = np.stack([vectors[:, n].real, vectors[:, n].imag], axis=1)
        bases.append(np.linalg.qr(plane)[0])
    left, cross, right = np.linalg.svd(bases[0].T @ bases[1])
    bases = [bases[0] @ left, bases[1] @ right.T]
    for c in range(2):
        sign = np.sign(bases[0][np.argmax(np.abs(bases[0][:, c])), c])
        bases = [np.concatenate([b[:, :c], sign * b[:, c : c + 1], b[:, c + 1 :]], axis=1) for b in bases]
    whole = np.concatenate(bases, axis=1)
    back = np.linalg.inv(whole)
    return whole, back, back @ matrix, back @ matrix @ whole, cross


def iota(shape, dim):
    return lax.broadcasted_iota(jnp.int32, shape, dim)


def exact_dot(a, b):
    return lax.dot_general(
        a, b, (((1,), (0,)), ((), ())), precision=lax.Precision.HIGHEST, preferred_element_type=F32
    )


def split_dot(a, b):
    high = a.astype(jnp.bfloat16)
    rest = a - high.astype(F32)
    middle = rest.astype(jnp.bfloat16)
    low = (rest - middle.astype(F32)).astype(jnp.bfloat16)
    b = b.astype(jnp.bfloat16)
    return sum(
        lax.dot_general(part, b, (((1,), (0,)), ((), ())), preferred_element_type=F32)
        for part in (low, middle, high)
    )


def choose(index, values):
    out = values[-1]
    for place in range(len(values) - 2, -1, -1):
        out = jnp.where(index == place, values[place], out)
    return out


def face_gains(flag, direction, side, count):
    nodes, weights = lobatto(count)
    c, nu = ADVECT[direction], DIFFUSE * count * count
    if side == 0:
        return (c * (1.0 + flag) / 2.0 + nu) * (1.0 / float(weights[0]))
    return (nu - c * (1.0 - flag) / 2.0) * (1.0 / float(weights[-1]))


def row_table():
    kx, ky = (element_matrix(5, d) for d in range(2))
    rows = np.zeros((64, 64))
    for s in range(2):
        for i in range(5):
            for j in range(5):
                r = 2 * (i * 5 + j) + s
                for m in range(5):
                    rows[r, 2 * (m * 5 + j) + s] += kx[i, m]
                    rows[r, 2 * (i * 5 + m) + s] += ky[j, m]
    return rows.astype(np.float32)


def pick_lines(k):
    lane = iota((160, 256), 1)
    return (iota((160, 256), 0) == 5 * (lane % EZ) + k + lane // 128).astype(F32)


def pair_factors(sec, table, own, s):
    upper = iota((32, 128), 1) < 64
    first = jnp.where(upper, float(table[0, s]), float(table[1, s]))
    second = jnp.where(upper, float(table[2, 2 + s]), float(table[3, 2 + s]))
    if not own:
        first = jnp.where(upper, float(table[2, s]), float(table[3, s]))
        second = jnp.where(upper, float(table[0, 2 + s]), float(table[1, 2 + s]))
    return jnp.where(sec == 0, first, second)


def pack_nodes(nodes):
    half = nodes.shape[0] // 2
    odd = iota((half, 128), 1) // EZ % 2 == 1
    return jnp.where(odd, nodes[half:, :], nodes[:half, :])


def local_kernel(
    rhs_in, guess_in, kappa_in, flags_in, rows_in, mine, theirs,
    rhs, guess, kappa, flags, rows_t, sems, stack, lines, nodes, y_faces, x_faces,
):
    sec = lax.axis_index("section")
    pairs = [(guess_in, guess), (rhs_in, rhs), (rows_in, rows_t), (kappa_in, kappa), (flags_in, flags)]
    copies = [pltpu.make_async_copy(source, target, sems.at[n]) for n, (source, target) in enumerate(pairs)]
    for copy in copies:
        copy.start()
    for ref in (stack, nodes, y_faces, x_faces):
        ref[...] = jnp.zeros_like(ref)
    for copy in copies:
        copy.wait()
    for i in range(5):
        stack[192 + 5 * i : 197 + 5 * i, :] = kappa[i]
        for j in range(5):
            r = 2 * (5 * i + j)
            value = guess[i, j]
            stack[128 + r : 130 + r, :] = value
            stack[r : r + 2, :] = rhs[i, j] - value
    stack[64:128, :] = exact_dot(rows_t[...], stack[128:192, :])
    source = stack[...]
    for k in (0, 2, 4):
        shown = split_dot(source, pick_lines(k))
        lines[224 * k : 224 * k + 224, :] = shown[:, :128]
        if k < 4:
            lines[224 * k + 224 : 224 * k + 448, :] = shown[:, 128:]

    def part(k, first, s):
        return lines[pl.ds(224 * k + first + s, 32, stride=2), :]

    def kappa_part(k):
        return lines[224 * k + 192 : 224 * k + 224, :]

    repeat = (iota((EZ, 128), 1) % EZ == iota((EZ, 128), 0)).astype(F32)
    shown = split_dot(flags[:, 0, 0, :].astype(F32), repeat)
    gains = [face_gains(shown[d : d + 1, :], d // 2, d % 2, 5) for d in range(6)]
    row = iota((32, 128), 0)
    none = jnp.zeros((32, 128), F32)
    own = jnp.where(row < 5, gains[0], jnp.where((row >= 20) & (row < 25), gains[1], none))
    own = own + jnp.where(row % 5 == 0, gains[2], jnp.where(row % 5 == 4, gains[3], none))
    kz = element_matrix(5, 2)
    back, back_matrix = split_sections()[1:3]
    fields = [[part(k, 128, s) for k in range(5)] for s in range(2)]
    for k in range(5):
        diagonal = kappa_part(k) + own
        if k == 0:
            diagonal = diagonal + gains[4]
        if k == 4:
            diagonal = diagonal + gains[5]
        images = []
        for s in range(2):
            image = diagonal * fields[s][k] + part(k, 64, s)
            for m in range(5):
                image = image + float(kz[k, m]) * fields[s][m]
            if k == 0:
                image = image - gains[4] * pltpu.roll(fields[s][4], 1, 1)
            if k == 4:
                image = image - gains[5] * pltpu.roll(fields[s][0], 127, 1)
            images.append(image)
        for p, mark in enumerate((True, False)):
            total = jnp.zeros((32, 128), F32)
            trace = jnp.zeros((32, 128), F32)
            for s in range(2):
                total = total + pair_factors(sec, back, mark, s) * part(k, 0, s)
                factor = pair_factors(sec, STEP_SIZE * back_matrix, mark, s)
                total = total - factor * images[s]
                trace = trace + factor * fields[s][k]
            nodes[128 * p + 25 * k : 128 * p + 25 * k + 25, :] = total[:25]
            for i in range(5):
                for f in range(2):
                    r = 64 * p + 32 * f + 5 * k + i
                    y_faces[r : r + 1, :] = trace[5 * i + 4 * f : 5 * i + 4 * f + 1]
            for f in range(2):
                r = 32 * p + 16 * f + 3 * k
                x_faces[r : r + 3, :] = trace[20 * f + 1 : 20 * f + 4]
    upper = iota((1, 128), 1) < 64
    for r in range(3):
        nodes[125 + r : 126 + r, :] = jnp.where(upper, shown[2 * r : 2 * r + 1], shown[2 * r + 1 : 2 * r + 2])
    for p, out in enumerate((mine, theirs)):
        out[:HALF, :] = pack_nodes(nodes[128 * p : 128 * p + 128, :])
        out[HALF:FACE_X, :] = pack_nodes(y_faces[64 * p : 64 * p + 64, :])[:25]
        out[FACE_X:KAPPA, :] = pack_nodes(x_faces[32 * p : 32 * p + 32, :])[:15]
    for k in range(5):
        nodes[25 * k : 25 * k + 25, :] = kappa_part(k)[:25]
    kappas = choose(iota((32, 128), 1) // EZ, [nodes[32 * q : 32 * q + 32, :] for q in range(4)])
    mine[KAPPA:, :] = jnp.where(sec == 0, kappas[:16], kappas[16:])


def part_kernel(source, piece, kappa):
    piece[...] = source[:KAPPA, :]
    kappa[...] = source[KAPPA:, :]


VMEM = pl.BlockSpec(memory_space=pltpu.VMEM)
HBM = pl.BlockSpec(memory_space=pltpu.HBM)


def limit(mib):
    return pltpu.CompilerParams(vmem_limit_bytes=mib * 2**20)


def local_part(rhs, guess, kappa, flags):
    operands = (rhs, guess, kappa, flags, jnp.asarray(row_table()))
    return pl.pallas_call(
        local_kernel,
        out_shape=[jax.ShapeDtypeStruct((rows, 128), F32) for rows in (PIECE, KAPPA)],
        in_specs=[HBM] * 5,
        out_specs=[VMEM] * 2,
        scratch_shapes=[pltpu.VMEM(o.shape, o.dtype) for o in operands]
        + [
            pltpu.SemaphoreType.DMA((5,)),
            pltpu.VMEM((224, 160), F32),
            pltpu.VMEM((5 * 224, 128), F32),
            pltpu.VMEM((256, 128), F32),
            pltpu.VMEM((128, 128), F32),
            pltpu.VMEM((64, 128), F32),
        ],
        compiler_params=limit(60),
        cost_estimate=pl.CostEstimate(flops=20_000_000, bytes_accessed=8_000_000, transcendentals=0),
        name="local_part",
    )(*operands)


def part(x):
    return pl.pallas_call(
        part_kernel,
        out_shape=[jax.ShapeDtypeStruct((rows, 128), F32) for rows in (KAPPA, 16)],
        in_specs=[VMEM],
        out_specs=[VMEM] * 2,
        compiler_params=limit(16),
        name="part",
    )(x)


class Level:
    def __init__(self, count, refs):
        self.count = count
        self.x, self.dir, self.res, self.f = refs
        self.tables = [element_matrix(count, d) for d in range(3)]
        self.gains = self.diag = self.jac = None


def tile(index):
    return pl.ds(index * 8, 8)


def rows_of(pieces, size, r, h):
    return pieces[pl.ds(8 * h * size + r, 8, stride=size), :]


ORDER_X = ((3, 2), (2, 3), (1, 1))
ORDER_Y = ((1, 2), (2, 1), (3, 3))


def partner(bits):
    return jnp.where(lax.axis_index("section") == 0, bits[0], bits[1])


def place_pieces(blocks, pieces, first, size, room):
    my_gx, my_gy = lax.axis_index("gx"), lax.axis_index("gy")
    for b, block in enumerate(blocks):
        gy = my_gy ^ partner(ORDER_Y[b - 1]) if b else my_gy
        for a in range(4):
            column = (my_gx ^ a) * 4 + gy
            start = pl.multiple_of(column * room, 8)
            pieces[pl.ds(start, size), :] = block[first + a * size : first + a * size + size, :]


class Lanes:
    def __init__(self):
        self.lane = iota((8, 128), 1)
        sub = iota((8, 128), 0)
        self.group = self.lane // EZ
        self.odd = self.group % 2 == 1
        self.element = self.lane % EZ
        self.place = sub % 4
        self.low_half = sub < 4

    def around(self, u):
        turned = pltpu.roll(u, 4, u.ndim - 2)
        far = jnp.where(self.odd, pltpu.roll(turned, 32, u.ndim - 1), pltpu.roll(turned, 96, u.ndim - 1))
        return turned, far

    def x_before(self, u):
        turned, far = self.around(u)
        return jnp.where(self.low_half, far, turned)

    def x_after(self, u):
        turned, far = self.around(u)
        return jnp.where(self.low_half, turned, far)

    def y_before(self, u):
        return jnp.where(self.place == 0, pltpu.roll(u, 5, 0), pltpu.roll(u, 1, 0))

    def y_after(self, u):
        return jnp.where(self.place == 3, pltpu.roll(u, 3, 0), pltpu.roll(u, 7, 0))

    def z_before(self, u):
        return jnp.where(self.element == 0, pltpu.roll(u, 97, u.ndim - 1), pltpu.roll(u, 1, u.ndim - 1))

    def z_after(self, u):
        last = self.element == EZ - 1
        return jnp.where(last, pltpu.roll(u, 31, u.ndim - 1), pltpu.roll(u, 127, u.ndim - 1))


def load(ref, first, count):
    return ref[pl.ds(first * 8, count * 8), :].reshape(count, 8, 128)


def store(ref, first, value):
    ref[pl.ds(first * 8, value.shape[0] * 8), :] = value.reshape(value.shape[0] * 8, 128)


DIAGS = (0, 250, 304)
GAINS = (320, 326, 332)
REGISTERS = 338
CENTRE = (CHEB_HIGH + CHEB_LOW) / 2.0
RADIUS = (CHEB_HIGH - CHEB_LOW) / 2.0


def flag_lanes(row, slot):
    turned = [row] + [pltpu.roll(row, 32 * m, 1) for m in range(1, 4)]
    return choose(iota(row.shape, 1) // EZ, [turned[(g - 2 * slot - 1) % 4] for g in range(4)])


def line_kernel(first, second, third, own, line, faces, sorted_pieces):
    sorted_pieces[:PIECE, :] = own[...]
    for bits, piece in zip(ORDER_X, (first, second, third)):
        sorted_pieces[pl.ds(pl.multiple_of(partner(bits) * PIECE, 8), PIECE), :] = piece[...]
    pieces = [sorted_pieces.at[PIECE * a : PIECE * a + PIECE, :] for a in range(4)]
    even = lax.axis_index("gx") % 2 == 0
    odd = iota((8, 128), 1) // EZ % 2 == 1
    faces[...] = jnp.zeros_like(faces)

    def both(rows, f):
        side = odd[:1] if f else jnp.logical_not(odd[:1])
        return jnp.where(side, rows, pltpu.roll(rows, 96 if f else 32, 1))

    for a, piece in enumerate(pieces):
        for f in range(2):
            base = 64 * a + 32 * f
            inner = both(piece[FACE_X:KAPPA, :], f)
            ends = [both(piece[HALF:FACE_X, :], g) for g in range(2)]
            for k in range(5):
                r = base + 5 * k
                node = 5 * k + 4 * f
                faces[r : r + 1, :] = ends[0][node : node + 1]
                faces[r + 1 : r + 4, :] = inner[3 * k : 3 * k + 3]
                faces[r + 4 : r + 5, :] = ends[1][node : node + 1]
    for a, piece in enumerate(pieces):
        line[HALF * a : HALF * a + HALF, :] = piece[:HALF, :]
        line[LINE_KAPPA + 16 * a : LINE_KAPPA + 16 * a + 16, :] = piece[KAPPA:, :]
        line[LINE_Y + 25 * a : LINE_Y + 25 * a + 25, :] = piece[HALF:FACE_X, :]
        flags = [flag_lanes(piece[61:62, :], slot) for slot in range(2)]
        gains = [face_gains(flags[d], 0, d, 5) for d in range(2)]
        next_first = even if a % 2 == 0 else jnp.logical_not(even)
        for f in range(2):
            one = faces[64 * (a ^ 1) + 32 * (1 - f) : 64 * (a ^ 1) + 32 * (1 - f) + 32, :]
            three = faces[64 * (a ^ 3) + 32 * (1 - f) : 64 * (a ^ 3) + 32 * (1 - f) + 32, :]
            near = jnp.where(next_first, one, three) if f else jnp.where(next_first, three, one)
            term = gains[f] * near
            for k in range(5):
                node = 25 * k + 20 * f
                side = odd[:5] if node >= HALF else jnp.logical_not(odd[:5])
                r = HALF * a + node % HALF
                line[r : r + 5, :] = line[r : r + 5, :] + jnp.where(side, term[5 * k : 5 * k + 5], 0.0)
    line[LINE_Y + 100 :, :] = jnp.zeros((4, 128), F32)


def halves_kernel(block0, block1, block2, block3, out):
    place_pieces((block0, block1, block2, block3), out, LINE_KAPPA, 16, 16)


def widen(low, high, odd):
    return jnp.where(odd, pltpu.roll(high, 32, 1), low), jnp.where(odd, high, pltpu.roll(low, 96, 1))


def assemble_kernel(block0, block1, block2, block3, field, pieces, edges, traces):
    blocks = (block0, block1, block2, block3)
    place_pieces(blocks, pieces, 0, HALF, HALF)
    place_pieces(blocks, edges, LINE_Y, 25, 32)
    lanes = Lanes()
    for source, size, rows, target, apart in ((edges, 32, 25, traces, 25), (pieces, HALF, HALF, field, HALF)):
        for r in range(rows):
            first, second = widen(rows_of(source, size, r, 0), rows_of(source, size, r, 1), lanes.odd)
            target[tile(r), :] = first
            target[tile(apart + r), :] = second
    got = field[tile(126), :]
    across = pltpu.roll(got, 64, 1)
    gains = [
        face_gains(jnp.where(lanes.lane < 64, got, across), 1, 0, 5),
        face_gains(jnp.where(lanes.lane < 64, across, got), 1, 1, 5),
    ]
    for k in range(5):
        for i in range(5):
            lower, upper = traces[tile(5 * k + i), :], traces[tile(25 + 5 * k + i), :]
            node = 25 * k + 5 * i
            field[tile(node), :] = field[tile(node), :] + gains[0] * lanes.y_before(upper)
            field[tile(node + 4), :] = field[tile(node + 4), :] + gains[1] * lanes.y_after(lower)


def setup_kernel(field, own_halves, other_halves, coefs, kap):
    sec = lax.axis_index("section")
    lanes = Lanes()
    group, lane = lanes.group, lanes.lane
    flags = []
    for r in range(3):
        got = field[tile(125 + r), :]
        across = pltpu.roll(got, 64, 1)
        flags += [jnp.where(lane < 64, got, across), jnp.where(lane < 64, across, got)]
    for r in range(16):
        pairs = [[rows_of(ref, 16, r, h) for h in range(2)] for ref in (own_halves, other_halves)]
        for half in range(2):
            turned = []
            for h in range(2):
                got = jnp.where(sec == half, pairs[0][h], pairs[1][h])
                turned.append([pltpu.roll(got, 32 * m, 1) if m else got for m in range(4)])
            for q in range(4):
                value = choose(group, [turned[g % 2][(g - q) % 4] for g in range(4)])
                kap[tile(q * 32 + half * 16 + r), :] = value
    for p, n in enumerate((5, 3, 2)):
        stride = 4 // (n - 1)
        gains = [face_gains(flags[d], d // 2, d % 2, n) for d in range(6)]
        rows = []
        for d in range(3):
            coefs[tile(GAINS[p] + 2 * d), :] = gains[2 * d]
            coefs[tile(GAINS[p] + 2 * d + 1), :] = gains[2 * d + 1]
            table = element_matrix(n, d)
            row = [jnp.full((8, 128), float(table[m, m]), F32) for m in range(n)]
            row[0] = row[0] + gains[2 * d]
            row[n - 1] = row[n - 1] + gains[2 * d + 1]
            rows.append(row)
        along = jnp.stack(rows[1])
        for k in range(n):
            for i in range(n):
                line = load(kap, k * 25 * stride + i * stride * 5, 5)
                line = jnp.stack([line[j * stride] for j in range(n)])
                value = line + (along + (rows[2][k] + rows[0][i]))
                scale = 1.0 / (1.0 + STEP_SIZE * JACOBI_SCALE * value)
                store(coefs, DIAGS[p] + (k * n + i) * n, value)
                store(coefs, DIAGS[p] + n**3 + (k * n + i) * n, scale * (1.0 / CENTRE))


def cycle_kernel(coefs, assembled, fields, *scratch):
    sec = lax.axis_index("section")
    my_gx, my_gy = lax.axis_index("gx"), lax.axis_index("gy")
    levels = [Level(n, scratch[4 * p : 4 * p + 4]) for p, n in enumerate((5, 3, 2))]
    half = scratch[12]
    lanes = Lanes()
    lane = lanes.lane
    blocks = split_sections()[3]

    def lanes_of(upper, lower):
        return jnp.where(lane < 64, jnp.where(sec == 0, upper[0], upper[1]), jnp.where(sec == 0, lower[0], lower[1]))

    entry = [[[float(STEP_SIZE * blocks[2 * p + a, 2 * p + b]) for p in range(2)] for b in range(2)] for a in range(2)]
    same = lanes_of(entry[0][0], entry[1][1])
    swap = lanes_of(entry[0][1], entry[1][0])
    first_rho = RADIUS / CENTRE
    second_rho = 1.0 / (2.0 * CENTRE / RADIUS - first_rho)
    keep = 1.0 + second_rho * first_rho
    push = 2.0 * second_rho / RADIUS * CENTRE
    for p, level in enumerate(levels):
        size = level.count**3
        level.gains = [-coefs[tile(GAINS[p] + d), :] for d in range(6)]
        level.diag = lambda first, count, p=p: load(coefs, DIAGS[p] + first, count)
        level.jac = lambda first, count, p=p, size=size: load(coefs, DIAGS[p] + size + first, count)

    def begin(level, source):
        n = level.count
        for first in range(0, n**3, n):
            f = load(source, first, n)
            store(level.dir, first, level.jac(first, n) * f)
            store(level.res, first, f)
            store(level.x, first, jnp.zeros_like(f))

    def apply(level, smooth):
        n = level.count
        kx, ky, kz = level.tables
        gains = level.gains
        source = level.dir if smooth else level.x
        def tree(terms):
            while len(terms) > 1:
                pairs = [a + b for a, b in zip(terms[::2], terms[1::2])]
                terms = pairs + terms[len(terms) // 2 * 2 :]
            return terms[0]

        def sums(k):
            def line_at(i):
                return load(source, (k * n + i) * n, n)

            x_left = gains[0] * lanes.x_before(line_at(n - 1))
            x_right = gains[1] * lanes.x_after(line_at(0))
            z_low, z_high, y_low, y_high = [], [], [], []
            for i in range(n):
                if k == 0:
                    z_low.append(gains[4] * lanes.z_before(load(source, ((n - 1) * n + i) * n, n)))
                if k == n - 1:
                    z_high.append(gains[5] * lanes.z_after(load(source, i * n, n)))
                v = line_at(i)
                y_low.append(gains[2] * lanes.y_before(v[n - 1]))
                y_high.append(gains[3] * lanes.y_after(v[0]))
            totals = []
            for i in range(n):
                first = (k * n + i) * n
                v = line_at(i)
                along_x = [float(kx[i, m]) * line_at(m) for m in range(n) if m != i]
                along_z = [float(kz[k, m]) * load(source, (m * n + i) * n, n) for m in range(n) if m != k]
                along_y = []
                for j in range(n):
                    terms = [float(ky[j, m]) * v[m] for m in range(n) if m != j]
                    if j == 0:
                        terms.append(y_low[i])
                    if j == n - 1:
                        terms.append(y_high[i])
                    along_y.append(tree(terms))
                if i == 0:
                    along_x.append(x_left)
                if i == n - 1:
                    along_x.append(x_right)
                if k == 0:
                    along_z.append(z_low[i])
                if k == n - 1:
                    along_z.append(z_high[i])
                totals.append(tree([level.diag(first, n) * v, tree(along_x), tree(along_z), jnp.stack(along_y)]))
            return totals

        def update(k, totals):
            moved = [pltpu.roll(total, 64, 2) for total in totals]
            for i in range(n):
                first = (k * n + i) * n
                v = load(source, first, n)
                image = v + (same * totals[i] + swap * moved[i])
                if smooth:
                    scaled = level.jac(first, n) * (load(level.res, first, n) - image)
                    store(level.x, first, (load(level.x, first, n) + keep * v) + push * scaled)
                else:
                    rest = load(level.f, first, n) - image
                    store(level.res, first, rest)
                    store(level.dir, first, level.jac(first, n) * rest)

        if n == 5:
            ready = sums(0)
            for k in range(n):
                following = sums(k + 1) if k + 1 < n else None
                update(k, ready)
                ready = following
        else:
            for k, totals in enumerate([sums(k) for k in range(n)]):
                update(k, totals)

    def combine(weights, parts):
        total = None
        for weight, part in zip(weights, parts):
            if abs(weight) > 1e-14:
                term = part if abs(weight - 1.0) < 1e-14 else float(weight) * part
                total = term if total is None else total + term
        return total

    def change(table, source, target, add):
        m, n = table.shape
        for i in range(n):
            parts = [load(source, i * n + k * n * n, n) for k in range(n)]
            for k in range(m):
                store(half, i * n + k * n * n, combine(table[k], parts))
        for k in range(m):
            parts = [load(half, k * n * n + i * n, n) for i in range(n)]
            for i in range(m):
                line = combine(table[i], parts)
                value = jnp.stack([combine(table[j], [line[a] for a in range(n)]) for j in range(m)])
                first = k * m * m + i * m
                store(target, first, load(target, first, m) + value if add else value)

    def down(n, m):
        fine_nodes, fine_weights = lobatto(n)
        coarse_nodes, coarse_weights = lobatto(m)
        table = lagrange_table(coarse_nodes, fine_nodes)
        return (1.0 / coarse_weights)[:, None] * table.T * fine_weights[None, :]

    def up(m, n):
        return lagrange_table(lobatto(m)[0], lobatto(n)[0])

    def solve(p):
        level = levels[p]
        if p == 2:
            apply(level, True)
            return
        below = levels[p + 1]

        def step(t, carry):
            @pl.when(t != 1)
            def _():
                apply(level, True)

            @pl.when((t != 2) | (p == 0))
            def _():
                apply(level, False)

            @pl.when(t == 0)
            def _():
                n, m = level.count, below.count
                change(down(n, m), level.res, below.f, False)
                begin(below, below.f)
                solve(p + 1)
                change(up(m, n), below.x, level.x, True)
            return carry
        lax.fori_loop(0, 3, step, 0)

    fine = levels[0]
    fine.f = assembled
    begin(fine, assembled)
    solve(0)

    for first in range(0, 125, 5):
        store(fields, first, load(fine.res, first, 5))
    column = (my_gx % 2) * 4 + my_gy
    fields[FIELD : FIELD + 125, :] = fine.x[pl.ds(column, 125, stride=8), :]
    fields[FIELD + 125 : FIELD + 128, :] = jnp.zeros((3, 128), F32)


def pair_weights():
    cross = split_sections()[4]
    return jnp.where(iota((8, 128), 1) < 64, float(cross[0]), float(cross[1]))


def column_factors(p):
    sec = lax.axis_index("section")
    whole = split_sections()[0]
    lane = iota((25, 128), 1)
    here = lane // EZ % 2 == lax.axis_index("gx") // 2
    factors = []
    for s in range(2):
        parts = []
        for mine in range(2):
            t = whole[2 * mine + s]
            q = mine if p == 0 else 1 - mine
            parts.append(jnp.where(lane < 64, float(t[2 * q]), float(t[2 * q + 1])))
        factors.append(jnp.where(here, jnp.where(sec == 0, parts[0], parts[1]), 0.0))
    return factors


def column_rows(k):
    column = (lax.axis_index("gx") % 2) * 4 + lax.axis_index("gy")
    return pl.ds(k * 200 + column, 25, stride=8)


def raw_order(k):
    lane = iota((256, 160), 0)
    return (iota((256, 160), 1) == 5 * (lane % EZ) + k + lane // 128).astype(F32)


def side_by_side(cols):
    half = cols.shape[0] // 2
    return jnp.concatenate([cols[:half, :], cols[half:, :]], axis=1)


def early_kernel(own, own_start, other_start, sums, column_out, cols):
    weights = pair_weights()
    cols[...] = jnp.zeros_like(cols)
    total = jnp.zeros((192, 160), F32)
    own_factors, other_factors = column_factors(0), column_factors(1)
    for k in range(5):
        where = column_rows(k)
        z = own[FIELD + k * 25 : FIELD + k * 25 + 25, :]
        start, other = own_start[where, :], other_start[where, :]
        w = start - own[where, :]
        side = 192 * (k % 2)
        for s in range(2):
            cols[pl.ds(side + s, 25, stride=2), :] = own_factors[s] * z
            cols[pl.ds(side + 64 + s, 25, stride=2), :] = own_factors[s] * start + other_factors[s] * other
            cols[pl.ds(side + 128 + s, 25, stride=2), :] = own_factors[s] * w
        if k % 2 == 1:
            total = total + split_dot(side_by_side(cols), raw_order(k - 1))
    cols[192:, :] = jnp.zeros((192, 128), F32)
    total = total + split_dot(side_by_side(cols), raw_order(4))
    column_out[...] = total
    nothing = jnp.zeros((8, 128), F32)
    uppers, sizes = [nothing] * 5, [nothing] * 5
    for r in range(125):
        c, d = own_start[tile(r), :], other_start[tile(r), :]
        a = c - own[tile(r), :]
        uppers[r % 5] = uppers[r % 5] + a * (c + weights * d)
        sizes[r % 5] = sizes[r % 5] + ((c * c + d * d) + 2.0 * (weights * (c * d)))
    sums[0:8, :] = sum(uppers)
    sums[8:16, :] = jnp.broadcast_to(jnp.sum(sum(sizes), keepdims=True), (8, 128))


def finish_kernel(own, other, own_start, other_start, sums, column, guess, sol, res_out, arnoldi, cols, outs):
    cols[...] = jnp.zeros_like(cols)
    total = jnp.zeros((128, 160), F32)
    factors = column_factors(1)
    for k in range(5):
        where = column_rows(k)
        z = other[FIELD + k * 25 : FIELD + k * 25 + 25, :]
        w = other_start[where, :] - other[where, :]
        side = 128 * (k % 2)
        for s in range(2):
            cols[pl.ds(side + s, 25, stride=2), :] = factors[s] * z
            cols[pl.ds(side + 64 + s, 25, stride=2), :] = factors[s] * w
        if k % 2 == 1:
            total = total + split_dot(side_by_side(cols), raw_order(k - 1))
    cols[128:, :] = jnp.zeros((128, 128), F32)
    total = total + split_dot(side_by_side(cols), raw_order(4))
    weights = pair_weights()
    nothing = jnp.zeros((8, 128), F32)
    uppers = [nothing] * 5
    for r in range(125):
        c, d = own_start[tile(r), :], other_start[tile(r), :]
        b = d - other[tile(r), :]
        uppers[r % 5] = uppers[r % 5] + b * (d + weights * c)

    mine, theirs = sums[0:8, :], sum(uppers)
    size = sums[8:9, 0:1]
    upper = jnp.sum(mine + theirs, keepdims=True) / size
    rests = [nothing] * 5
    for r in range(125):
        c, d = own_start[tile(r), :], other_start[tile(r), :]
        a = (c - own[tile(r), :]) - upper * c
        b = (d - other[tile(r), :]) - upper * d
        rests[r % 5] = rests[r % 5] + ((a * a + b * b) + 2.0 * (weights * (a * b)))
    rest = jnp.sum(sum(rests), keepdims=True)
    beta = jnp.sqrt(size)
    lower = jnp.sqrt(rest) / beta
    weight = upper / (upper * upper + lower * lower)
    entries = float(125 * EZ * COLS * 4)
    for place_out, value in enumerate((beta * (1.0 / math.sqrt(entries)), upper, lower)):
        arnoldi[place_out] = value[0, 0]
    outs[:64, :] = weight * (column[:64, :] + total[:64])
    outs[64:, :] = column[64:128, :] - weight * (column[128:, :] + total[64:])
    for i in range(5):
        for j in range(5):
            r = 2 * (5 * i + j)
            sol[i, j] = guess[i, j] + outs[r : r + 2, :]
            res_out[i, j] = outs[64 + r : 66 + r, :]


def plain_call(kernel, name, rows, scratch, operands, cost=1_000_000):
    return pl.pallas_call(
        kernel,
        out_shape=jax.ShapeDtypeStruct((rows, 128), F32),
        in_specs=[VMEM] * len(operands),
        out_specs=VMEM,
        scratch_shapes=[pltpu.VMEM((r, 128), F32) for r in scratch],
        compiler_params=limit(16),
        cost_estimate=pl.CostEstimate(flops=cost, bytes_accessed=cost, transcendentals=0),
        name=name,
    )(*operands)


def cycle(coefs, assembled):
    scratch = []
    for n in (5, 3, 2):
        scratch += [pltpu.VMEM((n**3 * 8, 128), F32)] * 4
    scratch += [pltpu.VMEM((FIELD, 128), F32)]
    return pl.pallas_call(
        cycle_kernel,
        out_shape=jax.ShapeDtypeStruct((FIELD + 128, 128), F32),
        in_specs=[VMEM] * 2,
        out_specs=VMEM,
        scratch_shapes=scratch,
        compiler_params=limit(24),
        cost_estimate=pl.CostEstimate(flops=40_000_000, bytes_accessed=30_000_000, transcendentals=0),
        name="cycle",
    )(coefs, assembled)


def early(own, own_start, other_start):
    return pl.pallas_call(
        early_kernel,
        out_shape=[jax.ShapeDtypeStruct((16, 128), F32), jax.ShapeDtypeStruct((192, 160), F32)],
        in_specs=[VMEM] * 3,
        out_specs=[VMEM] * 2,
        scratch_shapes=[pltpu.VMEM((384, 128), F32)],
        compiler_params=limit(16),
        cost_estimate=pl.CostEstimate(flops=4_000_000, bytes_accessed=4_000_000, transcendentals=0),
        name="early",
    )(own, own_start, other_start)


def finish(own, other, own_start, other_start, sums, column, guess):
    return pl.pallas_call(
        finish_kernel,
        out_shape=[
            jax.ShapeDtypeStruct(guess.shape, F32),
            jax.ShapeDtypeStruct(guess.shape, F32),
            jax.ShapeDtypeStruct((3,), F32),
        ],
        in_specs=[VMEM] * 7,
        out_specs=[VMEM, VMEM, pl.BlockSpec(memory_space=pltpu.SMEM)],
        scratch_shapes=[pltpu.VMEM((256, 128), F32), pltpu.VMEM((128, 160), F32)],
        compiler_params=limit(24),
        name="finish",
    )(own, other, own_start, other_start, sums, column, guess)


def exchange(x, axis, bits):
    return lax.ppermute(x, axis, [(n, n ^ bits) for n in range(lax.axis_size(axis))])


def exchange_by_core(x, axis, bits):
    count = lax.axis_size(axis)
    pairs = [(s * count + n, s * count + (n ^ bits[s])) for s in range(2) for n in range(count)]
    return lax.ppermute(x, ("section", axis), pairs)


def gathered_body(rhs, guess, kappa, bc_flags):
    rhs, guess = (jnp.transpose(v, (1, 2, 0, 3)) for v in (rhs, guess))
    mine, theirs = local_part(rhs, guess, kappa, bc_flags)
    got, mine, kappa_piece = lax.optimization_barrier((exchange(theirs, "section", 1), *part(mine)))
    piece = jnp.concatenate([mine + got, kappa_piece])
    pieces = [exchange_by_core(piece, "gx", bits) for bits in ORDER_X] + [piece]
    line = plain_call(line_kernel, "line", LINE, [4 * 64, 4 * PIECE], pieces)
    blocks = [line] + [exchange_by_core(line, "gy", bits) for bits in ORDER_Y]
    halves = plain_call(halves_kernel, "halves", COLS * 16, [], blocks)
    other_halves = exchange(halves, "section", 1)
    start = plain_call(assemble_kernel, "assemble", 128 * 8, [COLS * HALF, COLS * 32, 50 * 8], blocks, 4_000_000)
    start, other_halves = lax.optimization_barrier((start, other_halves))
    coefs = plain_call(setup_kernel, "setup", REGISTERS * 8, [128 * 8], (start, halves, other_halves))
    other_start = exchange(start, "section", 1)
    own, other_start = lax.optimization_barrier((cycle(coefs, start), other_start))
    sums, column = early(own, start, other_start)
    sol, res, arnoldi = finish(own, exchange(own, "section", 1), start, other_start, sums, column, guess)
    sol, res = (jnp.transpose(v, (2, 0, 1, 3)) for v in (sol, res))
    return sol, res, arnoldi


def solution(mesh):
    placed = (
        P("section", "gx", "gy", None),
        P("section", "gx", "gy", None),
        P("gx", "gy", None),
        P(None, "gx", "gy", None),
    )
    sizes = (mesh.shape["section"], mesh.shape["gx"], mesh.shape["gy"])

    def step(rhs, guess, kappa, bc_flags):
        fits = sizes == (2, 4, 4) and rhs.shape == (4, 20, 20, 160)
        return jax.shard_map(
            gathered_body if fits else stepwise,
            mesh=mesh,
            in_specs=placed,
            out_specs=(P("section", "gx", "gy", None), P("section", "gx", "gy", None), P()),
            check_vma=False,
        )(rhs, guess, kappa, bc_flags)

    return step
```

```python
from functools import partial
import math

import jax
import jax.numpy as jnp
import numpy as np
from jax import lax
from jax.experimental import pallas as pl
from jax.experimental.pallas import tpu as pltpu
from jax.sharding import PartitionSpec as P

ADVECT = (1.0, 0.7, 0.5)
DIFFUSE = 0.05
STEP_SIZE = 0.2
JACOBI_SCALE = 0.25
CHEB_LOW = 0.25
CHEB_HIGH = 2.0
LETTERS = "abcdef"


def extended(x, sides, width):
    for axis, dim in sides:
        peers, length = (lax.axis_size(axis), x.shape[dim])
        up = [(i, (i + 1) % peers) for i in range(peers)]
        down = [(j, i) for i, j in up]
        last = lax.slice_in_dim(x, length - width, length, axis=dim)
        leading = lax.slice_in_dim(x, 0, width, axis=dim)
        before = lax.ppermute(last, axis, up)
        after = lax.ppermute(leading, axis, down)
        x = jnp.concatenate([before, x, after], axis=dim)
    return x


def lobatto(count):
    if count == 5:
        inner = math.sqrt(3.0 / 7.0)
        return (
            np.array([-1.0, -inner, 0.0, inner, 1.0]),
            np.array([0.1, 49.0 / 90.0, 32.0 / 45.0, 49.0 / 90.0, 0.1]),
        )
    if count == 3:
        return (np.array([-1.0, 0.0, 1.0]), np.array([1.0 / 3.0, 4.0 / 3.0, 1.0 / 3.0]))
    return (np.array([-1.0, 1.0]), np.array([1.0, 1.0]))


def lagrange_table(nodes, points):
    table = np.ones((len(points), len(nodes)))
    for column in range(len(nodes)):
        for other in range(len(nodes)):
            if other != column:
                table[:, column] *= (points - nodes[other]) / (nodes[column] - nodes[other])
    return table


def slope_table(nodes):
    total = len(nodes)
    factor = np.array(
        [np.prod([nodes[i] - nodes[k] for k in range(total) if k != i]) for i in range(total)]
    )
    table = np.zeros((total, total))
    for row in range(total):
        for column in range(total):
            if row != column:
                table[row, column] = factor[row] / factor[column] / (nodes[row] - nodes[column])
        table[row, row] = -np.sum(table[row])
    return table


def element_matrix(count, direction):
    nodes, weights = lobatto(count)
    slopes = slope_table(nodes)
    stiffness = (1.0 / weights)[:, None] * (slopes.T @ (weights[:, None] * slopes))
    return ADVECT[direction] * slopes + DIFFUSE * stiffness


def legendre_pair(point, order):
    values = [1.0, point]
    slopes = [0.0, 1.0]
    for index in range(1, order):
        values.append(
            ((2 * index + 1) * point * values[index] - index * values[index - 1]) / (index + 1)
        )
        slopes.append(slopes[index - 1] + (2 * index + 1) * values[index])
    return (values, slopes)


def radau_nodes():
    starts = [0.0885879595127039, 0.4094668644407347, 0.7876594617608471]
    found = []
    for start in starts:
        point = start
        for sweep in range(30):
            values, slopes = legendre_pair(2.0 * point - 1.0, 4)
            change = (values[4] - values[3]) / (2.0 * (slopes[4] - slopes[3]))
            point = point - change
        found.append(point)
    found.append(1.0)
    return found


def poly_times(coefs, root):
    result = [0.0] * (len(coefs) + 1)
    for index in range(len(coefs)):
        result[index + 1] += coefs[index]
        result[index] -= root * coefs[index]
    return result


def radau_matrix():
    order = 4
    nodes = radau_nodes()
    matrix = np.zeros((order, order))
    for column in range(order):
        coefs = [1.0]
        denominator = 1.0
        for other in range(order):
            if other != column:
                coefs = poly_times(coefs, nodes[other])
                denominator *= nodes[column] - nodes[other]
        for row in range(order):
            upper_end = nodes[row]
            integral = 0.0
            for index in range(len(coefs)):
                integral += coefs[index] * upper_end ** (index + 1) / (index + 1)
            matrix[row, column] = integral / denominator
    return matrix


def node_einsum(table, field, axis):
    labels = LETTERS[: field.ndim]
    source = labels[: axis + 1] + "j" + labels[axis + 2 :]
    target = labels[: axis + 1] + "i" + labels[axis + 2 :]
    return jnp.einsum(
        "ij," + source + "->" + target,
        jnp.asarray(table, jnp.float32),
        field,
        precision=lax.Precision.HIGHEST,
    )


def apply_along(field, axis, count, table):
    shape = field.shape
    split = shape[:axis] + (shape[axis] // count, count) + shape[axis + 1 :]
    mapped = node_einsum(table, field.reshape(split), axis)
    return mapped.reshape(
        shape[:axis] + (mapped.shape[axis] * mapped.shape[axis + 1],) + shape[axis + 1 :]
    )


def line_part(field, axis, count, table, left_gain, right_gain, left_edge, right_edge):
    shape = field.shape
    elements = shape[axis] // count
    split = field.reshape(shape[:axis] + (elements, count) + shape[axis + 1 :])
    linear = node_einsum(table, split, axis)
    first = lax.index_in_dim(split, 0, axis + 1, keepdims=False)
    last = lax.index_in_dim(split, count - 1, axis + 1, keepdims=False)
    before = jnp.concatenate(
        [jnp.expand_dims(left_edge, axis), lax.slice_in_dim(last, 0, elements - 1, axis=axis)], axis
    )
    after = jnp.concatenate(
        [lax.slice_in_dim(first, 1, elements, axis=axis), jnp.expand_dims(right_edge, axis)], axis
    )
    front = jnp.expand_dims(left_gain * (first - before), axis + 1)
    back = jnp.expand_dims(right_gain * (last - after), axis + 1)
    if count > 2:
        middle_shape = list(front.shape)
        middle_shape[axis + 1] = count - 2
        pieces = [front, jnp.zeros(middle_shape, jnp.float32), back]
    else:
        pieces = [front, back]
    return (linear + jnp.concatenate(pieces, axis + 1)).reshape(shape)


def diag_along(shape, axis, count, table, left_gain, right_gain):
    elements = shape[axis] // count
    split = shape[:axis] + (elements, count) + shape[axis + 1 :]
    profile = [1] * len(split)
    profile[axis + 1] = count
    diagonal_entries = np.array([table[index, index] for index in range(count)])
    base = jnp.broadcast_to(jnp.asarray(diagonal_entries, jnp.float32).reshape(profile), split)
    front = jnp.expand_dims(left_gain, axis + 1)
    back = jnp.expand_dims(right_gain, axis + 1)
    if count > 2:
        middle_shape = list(front.shape)
        middle_shape[axis + 1] = count - 2
        pieces = [front, jnp.zeros(middle_shape, jnp.float32), back]
    else:
        pieces = [front, back]
    return (base + jnp.concatenate(pieces, axis + 1)).reshape(shape)


def level_kappa(kappa, count):
    if count == 5:
        return kappa
    picks = np.array([0, 2, 4]) if count == 3 else np.array([0, 4])
    extents = [extent // 5 for extent in kappa.shape]
    grouped = kappa.reshape(extents[0], 5, extents[1], 5, extents[2], 5)
    for axis in (1, 3, 5):
        grouped = jnp.take(grouped, picks, axis=axis)
    return grouped.reshape(extents[0] * count, extents[1] * count, extents[2] * count)


def face_plane(face, direction, count):
    plane = face.astype(jnp.float32)
    for axis in range(3):
        if axis != direction:
            plane = jnp.repeat(plane, count, axis=axis)
    return plane


def build_level(kappa, flags, count):
    nodes, weights = lobatto(count)
    kappa_level = level_kappa(kappa, count)
    tables, lefts, rights = ([], [], [])
    diagonal = kappa_level
    for direction in range(3):
        table = element_matrix(count, direction)
        lower = face_plane(flags[2 * direction], direction, count)
        upper = face_plane(flags[2 * direction + 1], direction, count)
        left_gain = (ADVECT[direction] * (1.0 + lower) / 2.0 + DIFFUSE * count * count) / float(
            weights[0]
        )
        right_gain = (DIFFUSE * count * count - ADVECT[direction] * (1.0 - upper) / 2.0) / float(
            weights[-1]
        )
        tables.append(table)
        lefts.append(left_gain)
        rights.append(right_gain)
        diagonal = diagonal + diag_along(
            kappa_level.shape, direction, count, table, left_gain, right_gain
        )
    scale = 1.0 / (1.0 + STEP_SIZE * JACOBI_SCALE * diagonal)
    return (count, tables, lefts, rights, kappa_level, scale)


def restrict(field, fine_count, coarse_count):
    fine_nodes, fine_weights = lobatto(fine_count)
    coarse_nodes, coarse_weights = lobatto(coarse_count)
    table = (
        (1.0 / coarse_weights)[:, None]
        * lagrange_table(coarse_nodes, fine_nodes).T
        * fine_weights[None, :]
    )
    for axis in range(field.ndim - 3, field.ndim):
        field = apply_along(field, axis, fine_count, table)
    return field


def prolong(field, coarse_count, fine_count):
    fine_nodes, fine_weights = lobatto(fine_count)
    coarse_nodes, coarse_weights = lobatto(coarse_count)
    table = lagrange_table(coarse_nodes, fine_nodes)
    for axis in range(field.ndim - 3, field.ndim):
        field = apply_along(field, axis, coarse_count, table)
    return field


def chebyshev(rhs, start, level, operator):
    centre = (CHEB_HIGH + CHEB_LOW) / 2.0
    radius = (CHEB_HIGH - CHEB_LOW) / 2.0
    ratio = centre / radius
    first_rho = 1.0 / ratio
    second_rho = 1.0 / (2.0 * ratio - first_rho)
    scale = level[5]
    if start is None:
        remain = rhs
    else:
        remain = rhs - operator(start, level)
    step = scale * remain / centre
    guess = step if start is None else start + step
    remain = remain - operator(step, level)
    step = second_rho * first_rho * step + 2.0 * second_rho / radius * scale * remain
    return guess + step


def vcycle(rhs, levels, operator):
    fine, middle, coarse = levels
    fine_x = chebyshev(rhs, None, fine, operator)
    middle_rhs = restrict(rhs - operator(fine_x, fine), 5, 3)
    middle_x = chebyshev(middle_rhs, None, middle, operator)
    coarse_rhs = restrict(middle_rhs - operator(middle_x, middle), 3, 2)
    coarse_x = chebyshev(coarse_rhs, None, coarse, operator)
    middle_x = chebyshev(middle_rhs, middle_x + prolong(coarse_x, 2, 3), middle, operator)
    return chebyshev(rhs, fine_x + prolong(middle_x, 3, 5), fine, operator)


def spatial(field, level):
    count, tables, lefts, rights, kappa_level, scale = level
    padded = extended(field, (("gx", 1), ("gy", 2)), 1)
    total = kappa_level * field
    total = total + line_part(
        field,
        1,
        count,
        tables[0],
        lefts[0],
        rights[0],
        padded[:, 0, 1:-1, :],
        padded[:, -1, 1:-1, :],
    )
    total = total + line_part(
        field,
        2,
        count,
        tables[1],
        lefts[1],
        rights[1],
        padded[:, 1:-1, 0, :],
        padded[:, 1:-1, -1, :],
    )
    total = total + line_part(
        field, 3, count, tables[2], lefts[2], rights[2], field[:, :, :, -1], field[:, :, :, 0]
    )
    return total


def apply_system(field, level, coupling):
    image = spatial(field, level)
    everyone = lax.all_gather(image, "section", axis=0, tiled=True)
    butcher = jnp.asarray(radau_matrix(), jnp.float32)
    rows = lax.dynamic_slice_in_dim(
        butcher, lax.axis_index("section") * field.shape[0], field.shape[0], 0
    )
    mixed = jnp.einsum("ij,jabc->iabc", rows, everyone, precision=lax.Precision.HIGHEST)
    return field + STEP_SIZE * mixed


def global_total(values):
    return lax.psum(values, ("section", "gx", "gy"))


def stepwise(rhs, guess, kappa, bc_flags):
    levels = [build_level(kappa, bc_flags, count) for count in (5, 3, 2)]
    section_operator = partial(apply_system, coupling=None)
    start_residual = rhs - section_operator(guess, levels[0])
    dofs = float(rhs.size * lax.axis_size("section") * lax.axis_size("gx") * lax.axis_size("gy"))
    beta = jnp.sqrt(global_total(jnp.sum(start_residual * start_residual).reshape(1))[0])
    basis = start_residual / beta
    precond = vcycle(basis, levels, section_operator)
    image = section_operator(precond, levels[0])
    upper = global_total(jnp.sum(image * basis).reshape(1))[0]
    remainder = image - upper * basis
    lower = jnp.sqrt(global_total(jnp.sum(remainder * remainder).reshape(1))[0])
    weight = beta * upper / (upper * upper + lower * lower)
    solution = guess + weight * precond
    residual = start_residual - weight * image
    arnoldi = jnp.stack([beta / math.sqrt(dofs), upper, lower]).astype(jnp.float32)
    return (solution, residual, arnoldi)


EZ = 32
COLS = 16
HALF = 64
FACE_X = HALF + 25
KAPPA = FACE_X + 15
PIECE = KAPPA + 16
LINE_KAPPA = 4 * HALF
LINE_Y = LINE_KAPPA + 4 * 16
LINE = LINE_Y + 104
FIELD = 1000
F32 = jnp.float32


def split_sections():
    matrix = radau_matrix()
    values, vectors = np.linalg.eig(matrix)
    order = [n for n in np.argsort(np.abs(values.imag), kind="stable") if values[n].imag > 0]
    bases = []
    for n in order:
        plane = np.stack([vectors[:, n].real, vectors[:, n].imag], axis=1)
        bases.append(np.linalg.qr(plane)[0])
    left, cross, right = np.linalg.svd(bases[0].T @ bases[1])
    bases = [bases[0] @ left, bases[1] @ right.T]
    for c in range(2):
        sign = np.sign(bases[0][np.argmax(np.abs(bases[0][:, c])), c])
        bases = [np.concatenate([b[:, :c], sign * b[:, c : c + 1], b[:, c + 1 :]], axis=1) for b in bases]
    whole = np.concatenate(bases, axis=1)
    back = np.linalg.inv(whole)
    return whole, back, back @ matrix, back @ matrix @ whole, cross


def iota(shape, dim):
    return lax.broadcasted_iota(jnp.int32, shape, dim)


def exact_dot(a, b):
    return lax.dot_general(
        a, b, (((1,), (0,)), ((), ())), precision=lax.Precision.HIGHEST, preferred_element_type=F32
    )


def split_dot(a, b):
    high = a.astype(jnp.bfloat16)
    rest = a - high.astype(F32)
    middle = rest.astype(jnp.bfloat16)
    low = (rest - middle.astype(F32)).astype(jnp.bfloat16)
    b = b.astype(jnp.bfloat16)
    return sum(
        lax.dot_general(part, b, (((1,), (0,)), ((), ())), preferred_element_type=F32)
        for part in (low, middle, high)
    )


def choose(index, values):
    out = values[-1]
    for place in range(len(values) - 2, -1, -1):
        out = jnp.where(index == place, values[place], out)
    return out


def face_gains(flag, direction, side, count):
    nodes, weights = lobatto(count)
    c, nu = ADVECT[direction], DIFFUSE * count * count
    if side == 0:
        return (c * (1.0 + flag) / 2.0 + nu) * (1.0 / float(weights[0]))
    return (nu - c * (1.0 - flag) / 2.0) * (1.0 / float(weights[-1]))


def row_table():
    kx, ky = (element_matrix(5, d) for d in range(2))
    rows = np.zeros((64, 64))
    for s in range(2):
        for i in range(5):
            for j in range(5):
                r = 2 * (i * 5 + j) + s
                for m in range(5):
                    rows[r, 2 * (m * 5 + j) + s] += kx[i, m]
                    rows[r, 2 * (i * 5 + m) + s] += ky[j, m]
    return rows.astype(np.float32)


def pick_lines(k):
    lane = iota((160, 256), 1)
    return (iota((160, 256), 0) == 5 * (lane % EZ) + k + lane // 128).astype(F32)


def pair_factors(sec, table, own, s):
    upper = iota((32, 128), 1) < 64
    first = jnp.where(upper, float(table[0, s]), float(table[1, s]))
    second = jnp.where(upper, float(table[2, 2 + s]), float(table[3, 2 + s]))
    if not own:
        first = jnp.where(upper, float(table[2, s]), float(table[3, s]))
        second = jnp.where(upper, float(table[0, 2 + s]), float(table[1, 2 + s]))
    return jnp.where(sec == 0, first, second)


def pack_nodes(nodes):
    half = nodes.shape[0] // 2
    odd = iota((half, 128), 1) // EZ % 2 == 1
    return jnp.where(odd, nodes[half:, :], nodes[:half, :])


def local_kernel(
    rhs_in, guess_in, kappa_in, flags_in, rows_in, mine, theirs,
    rhs, guess, kappa, flags, rows_t, sems, stack, lines, nodes, y_faces, x_faces,
):
    sec = lax.axis_index("section")
    pairs = [(guess_in, guess), (rhs_in, rhs), (rows_in, rows_t), (kappa_in, kappa), (flags_in, flags)]
    copies = [pltpu.make_async_copy(source, target, sems.at[n]) for n, (source, target) in enumerate(pairs)]
    for copy in copies:
        copy.start()
    for ref in (stack, nodes, y_faces, x_faces):
        ref[...] = jnp.zeros_like(ref)
    for copy in copies:
        copy.wait()
    for i in range(5):
        stack[192 + 5 * i : 197 + 5 * i, :] = kappa[i]
        for j in range(5):
            r = 2 * (5 * i + j)
            value = guess[i, j]
            stack[128 + r : 130 + r, :] = value
            stack[r : r + 2, :] = rhs[i, j] - value
    stack[64:128, :] = exact_dot(rows_t[...], stack[128:192, :])
    source = stack[...]
    for k in (0, 2, 4):
        shown = split_dot(source, pick_lines(k))
        lines[224 * k : 224 * k + 224, :] = shown[:, :128]
        if k < 4:
            lines[224 * k + 224 : 224 * k + 448, :] = shown[:, 128:]

    def part(k, first, s):
        return lines[pl.ds(224 * k + first + s, 32, stride=2), :]

    def kappa_part(k):
        return lines[224 * k + 192 : 224 * k + 224, :]

    repeat = (iota((EZ, 128), 1) % EZ == iota((EZ, 128), 0)).astype(F32)
    shown = split_dot(flags[:, 0, 0, :].astype(F32), repeat)
    gains = [face_gains(shown[d : d + 1, :], d // 2, d % 2, 5) for d in range(6)]
    row = iota((32, 128), 0)
    none = jnp.zeros((32, 128), F32)
    own = jnp.where(row < 5, gains[0], jnp.where((row >= 20) & (row < 25), gains[1], none))
    own = own + jnp.where(row % 5 == 0, gains[2], jnp.where(row % 5 == 4, gains[3], none))
    kz = element_matrix(5, 2)
    back, back_matrix = split_sections()[1:3]
    fields = [[part(k, 128, s) for k in range(5)] for s in range(2)]
    for k in range(5):
        diagonal = kappa_part(k) + own
        if k == 0:
            diagonal = diagonal + gains[4]
        if k == 4:
            diagonal = diagonal + gains[5]
        images = []
        for s in range(2):
            image = diagonal * fields[s][k] + part(k, 64, s)
            for m in range(5):
                image = image + float(kz[k, m]) * fields[s][m]
            if k == 0:
                image = image - gains[4] * pltpu.roll(fields[s][4], 1, 1)
            if k == 4:
                image = image - gains[5] * pltpu.roll(fields[s][0], 127, 1)
            images.append(image)
        for p, mark in enumerate((True, False)):
            total = jnp.zeros((32, 128), F32)
            trace = jnp.zeros((32, 128), F32)
            for s in range(2):
                total = total + pair_factors(sec, back, mark, s) * part(k, 0, s)
                factor = pair_factors(sec, STEP_SIZE * back_matrix, mark, s)
                total = total - factor * images[s]
                trace = trace + factor * fields[s][k]
            nodes[128 * p + 25 * k : 128 * p + 25 * k + 25, :] = total[:25]
            for i in range(5):
                for f in range(2):
                    r = 64 * p + 32 * f + 5 * k + i
                    y_faces[r : r + 1, :] = trace[5 * i + 4 * f : 5 * i + 4 * f + 1]
            for f in range(2):
                r = 32 * p + 16 * f + 3 * k
                x_faces[r : r + 3, :] = trace[20 * f + 1 : 20 * f + 4]
    upper = iota((1, 128), 1) < 64
    for r in range(3):
        nodes[125 + r : 126 + r, :] = jnp.where(upper, shown[2 * r : 2 * r + 1], shown[2 * r + 1 : 2 * r + 2])
    for p, out in enumerate((mine, theirs)):
        out[:HALF, :] = pack_nodes(nodes[128 * p : 128 * p + 128, :])
        out[HALF:FACE_X, :] = pack_nodes(y_faces[64 * p : 64 * p + 64, :])[:25]
        out[FACE_X:KAPPA, :] = pack_nodes(x_faces[32 * p : 32 * p + 32, :])[:15]
    for k in range(5):
        nodes[25 * k : 25 * k + 25, :] = kappa_part(k)[:25]
    kappas = choose(iota((32, 128), 1) // EZ, [nodes[32 * q : 32 * q + 32, :] for q in range(4)])
    mine[KAPPA:, :] = jnp.where(sec == 0, kappas[:16], kappas[16:])


def part_kernel(source, piece, kappa):
    piece[...] = source[:KAPPA, :]
    kappa[...] = source[KAPPA:, :]


VMEM = pl.BlockSpec(memory_space=pltpu.VMEM)
HBM = pl.BlockSpec(memory_space=pltpu.HBM)


def limit(mib):
    return pltpu.CompilerParams(vmem_limit_bytes=mib * 2**20)


def local_part(rhs, guess, kappa, flags):
    operands = (rhs, guess, kappa, flags, jnp.asarray(row_table()))
    return pl.pallas_call(
        local_kernel,
        out_shape=[jax.ShapeDtypeStruct((rows, 128), F32) for rows in (PIECE, KAPPA)],
        in_specs=[HBM] * 5,
        out_specs=[VMEM] * 2,
        scratch_shapes=[pltpu.VMEM(o.shape, o.dtype) for o in operands]
        + [
            pltpu.SemaphoreType.DMA((5,)),
            pltpu.VMEM((224, 160), F32),
            pltpu.VMEM((5 * 224, 128), F32),
            pltpu.VMEM((256, 128), F32),
            pltpu.VMEM((128, 128), F32),
            pltpu.VMEM((64, 128), F32),
        ],
        compiler_params=limit(60),
        cost_estimate=pl.CostEstimate(flops=20_000_000, bytes_accessed=8_000_000, transcendentals=0),
        name="local_part",
    )(*operands)


def part(x):
    return pl.pallas_call(
        part_kernel,
        out_shape=[jax.ShapeDtypeStruct((rows, 128), F32) for rows in (KAPPA, 16)],
        in_specs=[VMEM],
        out_specs=[VMEM] * 2,
        compiler_params=limit(16),
        name="part",
    )(x)


class Level:
    def __init__(self, count, refs):
        self.count = count
        self.x, self.dir, self.res, self.f = refs
        self.tables = [element_matrix(count, d) for d in range(3)]
        self.gains = self.diag = self.jac = None


def tile(index):
    return pl.ds(index * 8, 8)


def rows_of(pieces, size, r, h):
    return pieces[pl.ds(8 * h * size + r, 8, stride=size), :]


ORDER_X = ((3, 2), (2, 3), (1, 1))
ORDER_Y = ((1, 2), (2, 1), (3, 3))


def partner(bits):
    return jnp.where(lax.axis_index("section") == 0, bits[0], bits[1])


def place_pieces(blocks, pieces, first, size, room):
    my_gx, my_gy = lax.axis_index("gx"), lax.axis_index("gy")
    for b, block in enumerate(blocks):
        gy = my_gy ^ partner(ORDER_Y[b - 1]) if b else my_gy
        for a in range(4):
            column = (my_gx ^ a) * 4 + gy
            start = pl.multiple_of(column * room, 8)
            pieces[pl.ds(start, size), :] = block[first + a * size : first + a * size + size, :]


class Lanes:
    def __init__(self):
        self.lane = iota((8, 128), 1)
        sub = iota((8, 128), 0)
        self.group = self.lane // EZ
        self.odd = self.group % 2 == 1
        self.element = self.lane % EZ
        self.place = sub % 4
        self.low_half = sub < 4

    def around(self, u):
        turned = pltpu.roll(u, 4, u.ndim - 2)
        far = jnp.where(self.odd, pltpu.roll(turned, 32, u.ndim - 1), pltpu.roll(turned, 96, u.ndim - 1))
        return turned, far

    def x_before(self, u):
        turned, far = self.around(u)
        return jnp.where(self.low_half, far, turned)

    def x_after(self, u):
        turned, far = self.around(u)
        return jnp.where(self.low_half, turned, far)

    def y_before(self, u):
        return jnp.where(self.place == 0, pltpu.roll(u, 5, 0), pltpu.roll(u, 1, 0))

    def y_after(self, u):
        return jnp.where(self.place == 3, pltpu.roll(u, 3, 0), pltpu.roll(u, 7, 0))

    def z_before(self, u):
        return jnp.where(self.element == 0, pltpu.roll(u, 97, u.ndim - 1), pltpu.roll(u, 1, u.ndim - 1))

    def z_after(self, u):
        last = self.element == EZ - 1
        return jnp.where(last, pltpu.roll(u, 31, u.ndim - 1), pltpu.roll(u, 127, u.ndim - 1))


def load(ref, first, count):
    return ref[pl.ds(first * 8, count * 8), :].reshape(count, 8, 128)


def store(ref, first, value):
    ref[pl.ds(first * 8, value.shape[0] * 8), :] = value.reshape(value.shape[0] * 8, 128)


DIAGS = (0, 250, 304)
GAINS = (320, 326, 332)
REGISTERS = 338
CENTRE = (CHEB_HIGH + CHEB_LOW) / 2.0
RADIUS = (CHEB_HIGH - CHEB_LOW) / 2.0


def flag_lanes(row, slot):
    turned = [row] + [pltpu.roll(row, 32 * m, 1) for m in range(1, 4)]
    return choose(iota(row.shape, 1) // EZ, [turned[(g - 2 * slot - 1) % 4] for g in range(4)])


def line_kernel(first, second, third, own, line, faces, sorted_pieces):
    sorted_pieces[:PIECE, :] = own[...]
    for bits, piece in zip(ORDER_X, (first, second, third)):
        sorted_pieces[pl.ds(pl.multiple_of(partner(bits) * PIECE, 8), PIECE), :] = piece[...]
    pieces = [sorted_pieces.at[PIECE * a : PIECE * a + PIECE, :] for a in range(4)]
    even = lax.axis_index("gx") % 2 == 0
    odd = iota((8, 128), 1) // EZ % 2 == 1
    faces[...] = jnp.zeros_like(faces)

    def both(rows, f):
        side = odd[:1] if f else jnp.logical_not(odd[:1])
        return jnp.where(side, rows, pltpu.roll(rows, 96 if f else 32, 1))

    for a, piece in enumerate(pieces):
        for f in range(2):
            base = 64 * a + 32 * f
            inner = both(piece[FACE_X:KAPPA, :], f)
            ends = [both(piece[HALF:FACE_X, :], g) for g in range(2)]
            for k in range(5):
                r = base + 5 * k
                node = 5 * k + 4 * f
                faces[r : r + 1, :] = ends[0][node : node + 1]
                faces[r + 1 : r + 4, :] = inner[3 * k : 3 * k + 3]
                faces[r + 4 : r + 5, :] = ends[1][node : node + 1]
    for a, piece in enumerate(pieces):
        line[HALF * a : HALF * a + HALF, :] = piece[:HALF, :]
        line[LINE_KAPPA + 16 * a : LINE_KAPPA + 16 * a + 16, :] = piece[KAPPA:, :]
        line[LINE_Y + 25 * a : LINE_Y + 25 * a + 25, :] = piece[HALF:FACE_X, :]
        flags = [flag_lanes(piece[61:62, :], slot) for slot in range(2)]
        gains = [face_gains(flags[d], 0, d, 5) for d in range(2)]
        next_first = even if a % 2 == 0 else jnp.logical_not(even)
        for f in range(2):
            one = faces[64 * (a ^ 1) + 32 * (1 - f) : 64 * (a ^ 1) + 32 * (1 - f) + 32, :]
            three = faces[64 * (a ^ 3) + 32 * (1 - f) : 64 * (a ^ 3) + 32 * (1 - f) + 32, :]
            near = jnp.where(next_first, one, three) if f else jnp.where(next_first, three, one)
            term = gains[f] * near
            for k in range(5):
                node = 25 * k + 20 * f
                side = odd[:5] if node >= HALF else jnp.logical_not(odd[:5])
                r = HALF * a + node % HALF
                line[r : r + 5, :] = line[r : r + 5, :] + jnp.where(side, term[5 * k : 5 * k + 5], 0.0)
    line[LINE_Y + 100 :, :] = jnp.zeros((4, 128), F32)


def halves_kernel(block0, block1, block2, block3, out):
    place_pieces((block0, block1, block2, block3), out, LINE_KAPPA, 16, 16)


def widen(low, high, odd):
    return jnp.where(odd, pltpu.roll(high, 32, 1), low), jnp.where(odd, high, pltpu.roll(low, 96, 1))


def assemble_kernel(block0, block1, block2, block3, field, pieces, edges, traces):
    blocks = (block0, block1, block2, block3)
    place_pieces(blocks, pieces, 0, HALF, HALF)
    place_pieces(blocks, edges, LINE_Y, 25, 32)
    lanes = Lanes()
    for source, size, rows, target, apart in ((edges, 32, 25, traces, 25), (pieces, HALF, HALF, field, HALF)):
        for r in range(rows):
            first, second = widen(rows_of(source, size, r, 0), rows_of(source, size, r, 1), lanes.odd)
            target[tile(r), :] = first
            target[tile(apart + r), :] = second
    got = field[tile(126), :]
    across = pltpu.roll(got, 64, 1)
    gains = [
        face_gains(jnp.where(lanes.lane < 64, got, across), 1, 0, 5),
        face_gains(jnp.where(lanes.lane < 64, across, got), 1, 1, 5),
    ]
    for k in range(5):
        for i in range(5):
            lower, upper = traces[tile(5 * k + i), :], traces[tile(25 + 5 * k + i), :]
            node = 25 * k + 5 * i
            field[tile(node), :] = field[tile(node), :] + gains[0] * lanes.y_before(upper)
            field[tile(node + 4), :] = field[tile(node + 4), :] + gains[1] * lanes.y_after(lower)


def setup_kernel(field, own_halves, other_halves, coefs, kap):
    sec = lax.axis_index("section")
    lanes = Lanes()
    group, lane = lanes.group, lanes.lane
    flags = []
    for r in range(3):
        got = field[tile(125 + r), :]
        across = pltpu.roll(got, 64, 1)
        flags += [jnp.where(lane < 64, got, across), jnp.where(lane < 64, across, got)]
    for r in range(16):
        pairs = [[rows_of(ref, 16, r, h) for h in range(2)] for ref in (own_halves, other_halves)]
        for half in range(2):
            turned = []
            for h in range(2):
                got = jnp.where(sec == half, pairs[0][h], pairs[1][h])
                turned.append([pltpu.roll(got, 32 * m, 1) if m else got for m in range(4)])
            for q in range(4):
                value = choose(group, [turned[g % 2][(g - q) % 4] for g in range(4)])
                kap[tile(q * 32 + half * 16 + r), :] = value
    for p, n in enumerate((5, 3, 2)):
        stride = 4 // (n - 1)
        gains = [face_gains(flags[d], d // 2, d % 2, n) for d in range(6)]
        rows = []
        for d in range(3):
            coefs[tile(GAINS[p] + 2 * d), :] = gains[2 * d]
            coefs[tile(GAINS[p] + 2 * d + 1), :] = gains[2 * d + 1]
            table = element_matrix(n, d)
            row = [jnp.full((8, 128), float(table[m, m]), F32) for m in range(n)]
            row[0] = row[0] + gains[2 * d]
            row[n - 1] = row[n - 1] + gains[2 * d + 1]
            rows.append(row)
        along = jnp.stack(rows[1])
        for k in range(n):
            for i in range(n):
                line = load(kap, k * 25 * stride + i * stride * 5, 5)
                line = jnp.stack([line[j * stride] for j in range(n)])
                value = line + (along + (rows[2][k] + rows[0][i]))
                scale = 1.0 / (1.0 + STEP_SIZE * JACOBI_SCALE * value)
                store(coefs, DIAGS[p] + (k * n + i) * n, value)
                store(coefs, DIAGS[p] + n**3 + (k * n + i) * n, scale * (1.0 / CENTRE))


def cycle_kernel(coefs, assembled, fields, more, *scratch):
    sec = lax.axis_index("section")
    my_gx, my_gy = lax.axis_index("gx"), lax.axis_index("gy")
    levels = [Level(n, scratch[4 * p : 4 * p + 4]) for p, n in enumerate((5, 3, 2))]
    half = scratch[12]
    lanes = Lanes()
    lane = lanes.lane
    blocks = split_sections()[3]

    def lanes_of(upper, lower):
        return jnp.where(lane < 64, jnp.where(sec == 0, upper[0], upper[1]), jnp.where(sec == 0, lower[0], lower[1]))

    entry = [[[float(STEP_SIZE * blocks[2 * p + a, 2 * p + b]) for p in range(2)] for b in range(2)] for a in range(2)]
    same = lanes_of(entry[0][0], entry[1][1])
    swap = lanes_of(entry[0][1], entry[1][0])
    first_rho = RADIUS / CENTRE
    second_rho = 1.0 / (2.0 * CENTRE / RADIUS - first_rho)
    keep = 1.0 + second_rho * first_rho
    push = 2.0 * second_rho / RADIUS * CENTRE
    for p, level in enumerate(levels):
        size = level.count**3
        level.gains = [-coefs[tile(GAINS[p] + d), :] for d in range(6)]
        level.diag = lambda first, count, p=p: load(coefs, DIAGS[p] + first, count)
        level.jac = lambda first, count, p=p, size=size: load(coefs, DIAGS[p] + size + first, count)

    def begin(level, source):
        n = level.count
        for first in range(0, n**3, n):
            f = load(source, first, n)
            store(level.dir, first, level.jac(first, n) * f)
            store(level.res, first, f)
            store(level.x, first, jnp.zeros_like(f))

    def apply(level, smooth):
        n = level.count
        kx, ky, kz = level.tables
        gains = level.gains
        source = level.dir if smooth else level.x
        def tree(terms):
            while len(terms) > 1:
                pairs = [a + b for a, b in zip(terms[::2], terms[1::2])]
                terms = pairs + terms[len(terms) // 2 * 2 :]
            return terms[0]

        def sums(k):
            def line_at(i):
                return load(source, (k * n + i) * n, n)

            x_left = gains[0] * lanes.x_before(line_at(n - 1))
            x_right = gains[1] * lanes.x_after(line_at(0))
            z_low, z_high, y_low, y_high = [], [], [], []
            for i in range(n):
                if k == 0:
                    z_low.append(gains[4] * lanes.z_before(load(source, ((n - 1) * n + i) * n, n)))
                if k == n - 1:
                    z_high.append(gains[5] * lanes.z_after(load(source, i * n, n)))
                v = line_at(i)
                y_low.append(gains[2] * lanes.y_before(v[n - 1]))
                y_high.append(gains[3] * lanes.y_after(v[0]))
            totals = []
            for i in range(n):
                first = (k * n + i) * n
                v = line_at(i)
                along_x = [float(kx[i, m]) * line_at(m) for m in range(n) if m != i]
                along_z = [float(kz[k, m]) * load(source, (m * n + i) * n, n) for m in range(n) if m != k]
                along_y = []
                for j in range(n):
                    terms = [float(ky[j, m]) * v[m] for m in range(n) if m != j]
                    if j == 0:
                        terms.append(y_low[i])
                    if j == n - 1:
                        terms.append(y_high[i])
                    along_y.append(tree(terms))
                if i == 0:
                    along_x.append(x_left)
                if i == n - 1:
                    along_x.append(x_right)
                if k == 0:
                    along_z.append(z_low[i])
                if k == n - 1:
                    along_z.append(z_high[i])
                totals.append(tree([level.diag(first, n) * v, tree(along_x), tree(along_z), jnp.stack(along_y)]))
            return totals

        def update(k, totals):
            moved = [pltpu.roll(total, 64, 2) for total in totals]
            for i in range(n):
                first = (k * n + i) * n
                v = load(source, first, n)
                image = v + (same * totals[i] + swap * moved[i])
                if smooth:
                    scaled = level.jac(first, n) * (load(level.res, first, n) - image)
                    store(level.x, first, (load(level.x, first, n) + keep * v) + push * scaled)
                else:
                    rest = load(level.f, first, n) - image
                    store(level.res, first, rest)
                    store(level.dir, first, level.jac(first, n) * rest)

        if n == 5:
            ready = sums(0)
            for k in range(n):
                following = sums(k + 1) if k + 1 < n else None
                update(k, ready)
                ready = following
        else:
            for k, totals in enumerate([sums(k) for k in range(n)]):
                update(k, totals)

    def combine(weights, parts):
        total = None
        for weight, part in zip(weights, parts):
            if abs(weight) > 1e-14:
                term = part if abs(weight - 1.0) < 1e-14 else float(weight) * part
                total = term if total is None else total + term
        return total

    def change(table, source, target, add):
        m, n = table.shape
        for i in range(n):
            parts = [load(source, i * n + k * n * n, n) for k in range(n)]
            for k in range(m):
                store(half, i * n + k * n * n, combine(table[k], parts))
        for k in range(m):
            parts = [load(half, k * n * n + i * n, n) for i in range(n)]
            for i in range(m):
                line = combine(table[i], parts)
                value = jnp.stack([combine(table[j], [line[a] for a in range(n)]) for j in range(m)])
                first = k * m * m + i * m
                store(target, first, load(target, first, m) + value if add else value)

    def down(n, m):
        fine_nodes, fine_weights = lobatto(n)
        coarse_nodes, coarse_weights = lobatto(m)
        table = lagrange_table(coarse_nodes, fine_nodes)
        return (1.0 / coarse_weights)[:, None] * table.T * fine_weights[None, :]

    def up(m, n):
        return lagrange_table(lobatto(m)[0], lobatto(n)[0])

    def solve(p):
        level = levels[p]
        if p == 2:
            apply(level, True)
            return
        below = levels[p + 1]

        def correct():
            n, m = level.count, below.count
            change(down(n, m), level.res, below.f, False)
            begin(below, below.f)
            solve(p + 1)
            change(up(m, n), below.x, level.x, True)

        if p == 1:
            apply(level, True)
            apply(level, False)
            correct()
            apply(level, False)
            apply(level, True)
            return

        def step(t, carry):
            @pl.when(t != 1)
            def _():
                apply(level, True)

            apply(level, False)

            @pl.when(t == 0)
            def _():
                correct()
            return carry
        lax.fori_loop(0, 3, step, 0)

    fine = levels[0]
    fine.f = assembled
    begin(fine, assembled)
    solve(0)

    for first in range(0, 125, 5):
        part, place = (fields, first) if first < SPLIT else (more, first - SPLIT)
        store(part, place, load(fine.res, first, 5))
    column = (my_gx % 2) * 4 + my_gy
    more[AFTER : AFTER + 125, :] = fine.x[pl.ds(column, 125, stride=8), :]
    more[AFTER + 125 :, :] = jnp.zeros((3, 128), F32)


SPLIT = 75
AFTER = 8 * (125 - SPLIT)


def register(parts, r):
    return parts[0][tile(r), :] if r < SPLIT else parts[1][tile(r - SPLIT), :]


def column_of(parts, k):
    first = 3 * (k // 3)
    return parts[k // 3][column_rows(k - first), :]


def column_z(parts, k):
    return parts[1][AFTER + 25 * k : AFTER + 25 * k + 25, :]


def pair_weights():
    cross = split_sections()[4]
    return jnp.where(iota((8, 128), 1) < 64, float(cross[0]), float(cross[1]))


def column_factors(p):
    sec = lax.axis_index("section")
    whole = split_sections()[0]
    lane = iota((25, 128), 1)
    here = lane // EZ % 2 == lax.axis_index("gx") // 2
    factors = []
    for s in range(2):
        parts = []
        for mine in range(2):
            t = whole[2 * mine + s]
            q = mine if p == 0 else 1 - mine
            parts.append(jnp.where(lane < 64, float(t[2 * q]), float(t[2 * q + 1])))
        factors.append(jnp.where(here, jnp.where(sec == 0, parts[0], parts[1]), 0.0))
    return factors


def column_rows(k):
    column = (lax.axis_index("gx") % 2) * 4 + lax.axis_index("gy")
    return pl.ds(k * 200 + column, 25, stride=8)


def raw_order(k):
    lane = iota((256, 160), 0)
    return (iota((256, 160), 1) == 5 * (lane % EZ) + k + lane // 128).astype(F32)


def side_by_side(cols):
    half = cols.shape[0] // 2
    return jnp.concatenate([cols[:half, :], cols[half:, :]], axis=1)


def early_kernel(own0, own1, own_start, other_start, sums, column_out, cols):
    own = (own0, own1)
    weights = pair_weights()
    cols[...] = jnp.zeros_like(cols)
    total = jnp.zeros((192, 160), F32)
    own_factors, other_factors = column_factors(0), column_factors(1)
    for k in range(5):
        where = column_rows(k)
        z = column_z(own, k)
        start, other = own_start[where, :], other_start[where, :]
        w = start - column_of(own, k)
        side = 192 * (k % 2)
        for s in range(2):
            cols[pl.ds(side + s, 25, stride=2), :] = own_factors[s] * z
            cols[pl.ds(side + 64 + s, 25, stride=2), :] = own_factors[s] * start + other_factors[s] * other
            cols[pl.ds(side + 128 + s, 25, stride=2), :] = own_factors[s] * w
        if k % 2 == 1:
            total = total + split_dot(side_by_side(cols), raw_order(k - 1))
    cols[192:, :] = jnp.zeros((192, 128), F32)
    total = total + split_dot(side_by_side(cols), raw_order(4))
    column_out[...] = total
    nothing = jnp.zeros((8, 128), F32)
    uppers, sizes = [nothing] * 5, [nothing] * 5
    for r in range(125):
        c, d = own_start[tile(r), :], other_start[tile(r), :]
        a = c - register(own, r)
        uppers[r % 5] = uppers[r % 5] + a * (c + weights * d)
        sizes[r % 5] = sizes[r % 5] + ((c * c + d * d) + 2.0 * (weights * (c * d)))
    sums[0:8, :] = sum(uppers)
    sums[8:16, :] = jnp.broadcast_to(jnp.sum(sum(sizes), keepdims=True), (8, 128))


def finish_kernel(own0, own1, other0, other1, own_start, other_start, sums, column, guess, sol, res_out, arnoldi, cols, outs):
    own, other = (own0, own1), (other0, other1)
    cols[...] = jnp.zeros_like(cols)
    total = jnp.zeros((128, 160), F32)
    factors = column_factors(1)
    for k in range(5):
        where = column_rows(k)
        z = column_z(other, k)
        w = other_start[where, :] - column_of(other, k)
        side = 128 * (k % 2)
        for s in range(2):
            cols[pl.ds(side + s, 25, stride=2), :] = factors[s] * z
            cols[pl.ds(side + 64 + s, 25, stride=2), :] = factors[s] * w
        if k % 2 == 1:
            total = total + split_dot(side_by_side(cols), raw_order(k - 1))
    cols[128:, :] = jnp.zeros((128, 128), F32)
    total = total + split_dot(side_by_side(cols), raw_order(4))
    weights = pair_weights()
    nothing = jnp.zeros((8, 128), F32)
    uppers = [nothing] * 5
    for r in range(125):
        c, d = own_start[tile(r), :], other_start[tile(r), :]
        b = d - register(other, r)
        uppers[r % 5] = uppers[r % 5] + b * (d + weights * c)

    mine, theirs = sums[0:8, :], sum(uppers)
    size = sums[8:9, 0:1]
    upper = jnp.sum(mine + theirs, keepdims=True) / size
    rests = [nothing] * 5
    for r in range(125):
        c, d = own_start[tile(r), :], other_start[tile(r), :]
        a = (c - register(own, r)) - upper * c
        b = (d - register(other, r)) - upper * d
        rests[r % 5] = rests[r % 5] + ((a * a + b * b) + 2.0 * (weights * (a * b)))
    rest = jnp.sum(sum(rests), keepdims=True)
    beta = jnp.sqrt(size)
    lower = jnp.sqrt(rest) / beta
    weight = upper / (upper * upper + lower * lower)
    entries = float(125 * EZ * COLS * 4)
    for place_out, value in enumerate((beta * (1.0 / math.sqrt(entries)), upper, lower)):
        arnoldi[place_out] = value[0, 0]
    outs[:64, :] = weight * (column[:64, :] + total[:64])
    outs[64:, :] = column[64:128, :] - weight * (column[128:, :] + total[64:])
    for i in range(5):
        for j in range(5):
            r = 2 * (5 * i + j)
            sol[i, j] = guess[i, j] + outs[r : r + 2, :]
            res_out[i, j] = outs[64 + r : 66 + r, :]


def plain_call(kernel, name, rows, scratch, operands, cost=1_000_000):
    return pl.pallas_call(
        kernel,
        out_shape=jax.ShapeDtypeStruct((rows, 128), F32),
        in_specs=[VMEM] * len(operands),
        out_specs=VMEM,
        scratch_shapes=[pltpu.VMEM((r, 128), F32) for r in scratch],
        compiler_params=limit(16),
        cost_estimate=pl.CostEstimate(flops=cost, bytes_accessed=cost, transcendentals=0),
        name=name,
    )(*operands)


def cycle(coefs, assembled):
    scratch = []
    for n in (5, 3, 2):
        scratch += [pltpu.VMEM((n**3 * 8, 128), F32)] * 4
    scratch += [pltpu.VMEM((FIELD, 128), F32)]
    return pl.pallas_call(
        cycle_kernel,
        out_shape=[jax.ShapeDtypeStruct((rows, 128), F32) for rows in (SPLIT * 8, AFTER + 128)],
        in_specs=[VMEM] * 2,
        out_specs=[VMEM] * 2,
        scratch_shapes=scratch,
        compiler_params=limit(24),
        cost_estimate=pl.CostEstimate(flops=40_000_000, bytes_accessed=30_000_000, transcendentals=0),
        name="cycle",
    )(coefs, assembled)


def early(own, own_start, other_start):
    return pl.pallas_call(
        early_kernel,
        out_shape=[jax.ShapeDtypeStruct((16, 128), F32), jax.ShapeDtypeStruct((192, 160), F32)],
        in_specs=[VMEM] * 4,
        out_specs=[VMEM] * 2,
        scratch_shapes=[pltpu.VMEM((384, 128), F32)],
        compiler_params=limit(16),
        cost_estimate=pl.CostEstimate(flops=4_000_000, bytes_accessed=4_000_000, transcendentals=0),
        name="early",
    )(*own, own_start, other_start)


def finish(own, other, own_start, other_start, sums, column, guess):
    return pl.pallas_call(
        finish_kernel,
        out_shape=[
            jax.ShapeDtypeStruct(guess.shape, F32),
            jax.ShapeDtypeStruct(guess.shape, F32),
            jax.ShapeDtypeStruct((3,), F32),
        ],
        in_specs=[VMEM] * 9,
        out_specs=[VMEM, VMEM, pl.BlockSpec(memory_space=pltpu.SMEM)],
        scratch_shapes=[pltpu.VMEM((256, 128), F32), pltpu.VMEM((128, 160), F32)],
        compiler_params=limit(24),
        name="finish",
    )(*own, *other, own_start, other_start, sums, column, guess)


def exchange(x, axis, bits):
    return lax.ppermute(x, axis, [(n, n ^ bits) for n in range(lax.axis_size(axis))])


def exchange_by_core(x, axis, bits):
    count = lax.axis_size(axis)
    pairs = [(s * count + n, s * count + (n ^ bits[s])) for s in range(2) for n in range(count)]
    return lax.ppermute(x, ("section", axis), pairs)


def gathered_body(rhs, guess, kappa, bc_flags):
    rhs, guess = (jnp.transpose(v, (1, 2, 0, 3)) for v in (rhs, guess))
    mine, theirs = local_part(rhs, guess, kappa, bc_flags)
    got, mine, kappa_piece = lax.optimization_barrier((exchange(theirs, "section", 1), *part(mine)))
    piece = jnp.concatenate([mine + got, kappa_piece])
    pieces = [exchange_by_core(piece, "gx", bits) for bits in ORDER_X] + [piece]
    line = plain_call(line_kernel, "line", LINE, [4 * 64, 4 * PIECE], pieces)
    blocks = [line] + [exchange_by_core(line, "gy", bits) for bits in ORDER_Y]
    halves = plain_call(halves_kernel, "halves", COLS * 16, [], blocks)
    other_halves = exchange(halves, "section", 1)
    start = plain_call(assemble_kernel, "assemble", 128 * 8, [COLS * HALF, COLS * 32, 50 * 8], blocks, 4_000_000)
    start, other_halves = lax.optimization_barrier((start, other_halves))
    coefs = plain_call(setup_kernel, "setup", REGISTERS * 8, [128 * 8], (start, halves, other_halves))
    other_start = exchange(start, "section", 1)
    own, other_start = lax.optimization_barrier((cycle(coefs, start), other_start))
    other = [exchange(part, "section", 1) for part in own]
    sums, column = early(own, start, other_start)
    sol, res, arnoldi = finish(own, other, start, other_start, sums, column, guess)
    sol, res = (jnp.transpose(v, (2, 0, 1, 3)) for v in (sol, res))
    return sol, res, arnoldi


def solution(mesh):
    placed = (
        P("section", "gx", "gy", None),
        P("section", "gx", "gy", None),
        P("gx", "gy", None),
        P(None, "gx", "gy", None),
    )
    sizes = (mesh.shape["section"], mesh.shape["gx"], mesh.shape["gy"])

    def step(rhs, guess, kappa, bc_flags):
        fits = sizes == (2, 4, 4) and rhs.shape == (4, 20, 20, 160)
        return jax.shard_map(
            gathered_body if fits else stepwise,
            mesh=mesh,
            in_specs=placed,
            out_specs=(P("section", "gx", "gy", None), P("section", "gx", "gy", None), P()),
            check_vma=False,
        )(rhs, guess, kappa, bc_flags)

    return step
```

```python
from functools import partial
import math

import jax
import jax.numpy as jnp
import numpy as np
from jax import lax
from jax.experimental import pallas as pl
from jax.experimental.pallas import tpu as pltpu
from jax.sharding import PartitionSpec as P

ADVECT = (1.0, 0.7, 0.5)
DIFFUSE = 0.05
STEP_SIZE = 0.2
JACOBI_SCALE = 0.25
CHEB_LOW = 0.25
CHEB_HIGH = 2.0
LETTERS = "abcdef"


def extended(x, sides, width):
    for axis, dim in sides:
        peers, length = (lax.axis_size(axis), x.shape[dim])
        up = [(i, (i + 1) % peers) for i in range(peers)]
        down = [(j, i) for i, j in up]
        last = lax.slice_in_dim(x, length - width, length, axis=dim)
        leading = lax.slice_in_dim(x, 0, width, axis=dim)
        before = lax.ppermute(last, axis, up)
        after = lax.ppermute(leading, axis, down)
        x = jnp.concatenate([before, x, after], axis=dim)
    return x


def lobatto(count):
    if count == 5:
        inner = math.sqrt(3.0 / 7.0)
        return (
            np.array([-1.0, -inner, 0.0, inner, 1.0]),
            np.array([0.1, 49.0 / 90.0, 32.0 / 45.0, 49.0 / 90.0, 0.1]),
        )
    if count == 3:
        return (np.array([-1.0, 0.0, 1.0]), np.array([1.0 / 3.0, 4.0 / 3.0, 1.0 / 3.0]))
    return (np.array([-1.0, 1.0]), np.array([1.0, 1.0]))


def lagrange_table(nodes, points):
    table = np.ones((len(points), len(nodes)))
    for column in range(len(nodes)):
        for other in range(len(nodes)):
            if other != column:
                table[:, column] *= (points - nodes[other]) / (nodes[column] - nodes[other])
    return table


def slope_table(nodes):
    total = len(nodes)
    factor = np.array(
        [np.prod([nodes[i] - nodes[k] for k in range(total) if k != i]) for i in range(total)]
    )
    table = np.zeros((total, total))
    for row in range(total):
        for column in range(total):
            if row != column:
                table[row, column] = factor[row] / factor[column] / (nodes[row] - nodes[column])
        table[row, row] = -np.sum(table[row])
    return table


def element_matrix(count, direction):
    nodes, weights = lobatto(count)
    slopes = slope_table(nodes)
    stiffness = (1.0 / weights)[:, None] * (slopes.T @ (weights[:, None] * slopes))
    return ADVECT[direction] * slopes + DIFFUSE * stiffness


def legendre_pair(point, order):
    values = [1.0, point]
    slopes = [0.0, 1.0]
    for index in range(1, order):
        values.append(
            ((2 * index + 1) * point * values[index] - index * values[index - 1]) / (index + 1)
        )
        slopes.append(slopes[index - 1] + (2 * index + 1) * values[index])
    return (values, slopes)


def radau_nodes():
    starts = [0.0885879595127039, 0.4094668644407347, 0.7876594617608471]
    found = []
    for start in starts:
        point = start
        for sweep in range(30):
            values, slopes = legendre_pair(2.0 * point - 1.0, 4)
            change = (values[4] - values[3]) / (2.0 * (slopes[4] - slopes[3]))
            point = point - change
        found.append(point)
    found.append(1.0)
    return found


def poly_times(coefs, root):
    result = [0.0] * (len(coefs) + 1)
    for index in range(len(coefs)):
        result[index + 1] += coefs[index]
        result[index] -= root * coefs[index]
    return result


def radau_matrix():
    order = 4
    nodes = radau_nodes()
    matrix = np.zeros((order, order))
    for column in range(order):
        coefs = [1.0]
        denominator = 1.0
        for other in range(order):
            if other != column:
                coefs = poly_times(coefs, nodes[other])
                denominator *= nodes[column] - nodes[other]
        for row in range(order):
            upper_end = nodes[row]
            integral = 0.0
            for index in range(len(coefs)):
                integral += coefs[index] * upper_end ** (index + 1) / (index + 1)
            matrix[row, column] = integral / denominator
    return matrix


def node_einsum(table, field, axis):
    labels = LETTERS[: field.ndim]
    source = labels[: axis + 1] + "j" + labels[axis + 2 :]
    target = labels[: axis + 1] + "i" + labels[axis + 2 :]
    return jnp.einsum(
        "ij," + source + "->" + target,
        jnp.asarray(table, jnp.float32),
        field,
        precision=lax.Precision.HIGHEST,
    )


def apply_along(field, axis, count, table):
    shape = field.shape
    split = shape[:axis] + (shape[axis] // count, count) + shape[axis + 1 :]
    mapped = node_einsum(table, field.reshape(split), axis)
    return mapped.reshape(
        shape[:axis] + (mapped.shape[axis] * mapped.shape[axis + 1],) + shape[axis + 1 :]
    )


def line_part(field, axis, count, table, left_gain, right_gain, left_edge, right_edge):
    shape = field.shape
    elements = shape[axis] // count
    split = field.reshape(shape[:axis] + (elements, count) + shape[axis + 1 :])
    linear = node_einsum(table, split, axis)
    first = lax.index_in_dim(split, 0, axis + 1, keepdims=False)
    last = lax.index_in_dim(split, count - 1, axis + 1, keepdims=False)
    before = jnp.concatenate(
        [jnp.expand_dims(left_edge, axis), lax.slice_in_dim(last, 0, elements - 1, axis=axis)], axis
    )
    after = jnp.concatenate(
        [lax.slice_in_dim(first, 1, elements, axis=axis), jnp.expand_dims(right_edge, axis)], axis
    )
    front = jnp.expand_dims(left_gain * (first - before), axis + 1)
    back = jnp.expand_dims(right_gain * (last - after), axis + 1)
    if count > 2:
        middle_shape = list(front.shape)
        middle_shape[axis + 1] = count - 2
        pieces = [front, jnp.zeros(middle_shape, jnp.float32), back]
    else:
        pieces = [front, back]
    return (linear + jnp.concatenate(pieces, axis + 1)).reshape(shape)


def diag_along(shape, axis, count, table, left_gain, right_gain):
    elements = shape[axis] // count
    split = shape[:axis] + (elements, count) + shape[axis + 1 :]
    profile = [1] * len(split)
    profile[axis + 1] = count
    diagonal_entries = np.array([table[index, index] for index in range(count)])
    base = jnp.broadcast_to(jnp.asarray(diagonal_entries, jnp.float32).reshape(profile), split)
    front = jnp.expand_dims(left_gain, axis + 1)
    back = jnp.expand_dims(right_gain, axis + 1)
    if count > 2:
        middle_shape = list(front.shape)
        middle_shape[axis + 1] = count - 2
        pieces = [front, jnp.zeros(middle_shape, jnp.float32), back]
    else:
        pieces = [front, back]
    return (base + jnp.concatenate(pieces, axis + 1)).reshape(shape)


def level_kappa(kappa, count):
    if count == 5:
        return kappa
    picks = np.array([0, 2, 4]) if count == 3 else np.array([0, 4])
    extents = [extent // 5 for extent in kappa.shape]
    grouped = kappa.reshape(extents[0], 5, extents[1], 5, extents[2], 5)
    for axis in (1, 3, 5):
        grouped = jnp.take(grouped, picks, axis=axis)
    return grouped.reshape(extents[0] * count, extents[1] * count, extents[2] * count)


def face_plane(face, direction, count):
    plane = face.astype(jnp.float32)
    for axis in range(3):
        if axis != direction:
            plane = jnp.repeat(plane, count, axis=axis)
    return plane


def build_level(kappa, flags, count):
    nodes, weights = lobatto(count)
    kappa_level = level_kappa(kappa, count)
    tables, lefts, rights = ([], [], [])
    diagonal = kappa_level
    for direction in range(3):
        table = element_matrix(count, direction)
        lower = face_plane(flags[2 * direction], direction, count)
        upper = face_plane(flags[2 * direction + 1], direction, count)
        left_gain = (ADVECT[direction] * (1.0 + lower) / 2.0 + DIFFUSE * count * count) / float(
            weights[0]
        )
        right_gain = (DIFFUSE * count * count - ADVECT[direction] * (1.0 - upper) / 2.0) / float(
            weights[-1]
        )
        tables.append(table)
        lefts.append(left_gain)
        rights.append(right_gain)
        diagonal = diagonal + diag_along(
            kappa_level.shape, direction, count, table, left_gain, right_gain
        )
    scale = 1.0 / (1.0 + STEP_SIZE * JACOBI_SCALE * diagonal)
    return (count, tables, lefts, rights, kappa_level, scale)


def restrict(field, fine_count, coarse_count):
    fine_nodes, fine_weights = lobatto(fine_count)
    coarse_nodes, coarse_weights = lobatto(coarse_count)
    table = (
        (1.0 / coarse_weights)[:, None]
        * lagrange_table(coarse_nodes, fine_nodes).T
        * fine_weights[None, :]
    )
    for axis in range(field.ndim - 3, field.ndim):
        field = apply_along(field, axis, fine_count, table)
    return field


def prolong(field, coarse_count, fine_count):
    fine_nodes, fine_weights = lobatto(fine_count)
    coarse_nodes, coarse_weights = lobatto(coarse_count)
    table = lagrange_table(coarse_nodes, fine_nodes)
    for axis in range(field.ndim - 3, field.ndim):
        field = apply_along(field, axis, coarse_count, table)
    return field


def chebyshev(rhs, start, level, operator):
    centre = (CHEB_HIGH + CHEB_LOW) / 2.0
    radius = (CHEB_HIGH - CHEB_LOW) / 2.0
    ratio = centre / radius
    first_rho = 1.0 / ratio
    second_rho = 1.0 / (2.0 * ratio - first_rho)
    scale = level[5]
    if start is None:
        remain = rhs
    else:
        remain = rhs - operator(start, level)
    step = scale * remain / centre
    guess = step if start is None else start + step
    remain = remain - operator(step, level)
    step = second_rho * first_rho * step + 2.0 * second_rho / radius * scale * remain
    return guess + step


def vcycle(rhs, levels, operator):
    fine, middle, coarse = levels
    fine_x = chebyshev(rhs, None, fine, operator)
    middle_rhs = restrict(rhs - operator(fine_x, fine), 5, 3)
    middle_x = chebyshev(middle_rhs, None, middle, operator)
    coarse_rhs = restrict(middle_rhs - operator(middle_x, middle), 3, 2)
    coarse_x = chebyshev(coarse_rhs, None, coarse, operator)
    middle_x = chebyshev(middle_rhs, middle_x + prolong(coarse_x, 2, 3), middle, operator)
    return chebyshev(rhs, fine_x + prolong(middle_x, 3, 5), fine, operator)


def spatial(field, level):
    count, tables, lefts, rights, kappa_level, scale = level
    padded = extended(field, (("gx", 1), ("gy", 2)), 1)
    total = kappa_level * field
    total = total + line_part(
        field,
        1,
        count,
        tables[0],
        lefts[0],
        rights[0],
        padded[:, 0, 1:-1, :],
        padded[:, -1, 1:-1, :],
    )
    total = total + line_part(
        field,
        2,
        count,
        tables[1],
        lefts[1],
        rights[1],
        padded[:, 1:-1, 0, :],
        padded[:, 1:-1, -1, :],
    )
    total = total + line_part(
        field, 3, count, tables[2], lefts[2], rights[2], field[:, :, :, -1], field[:, :, :, 0]
    )
    return total


def apply_system(field, level, coupling):
    image = spatial(field, level)
    everyone = lax.all_gather(image, "section", axis=0, tiled=True)
    butcher = jnp.asarray(radau_matrix(), jnp.float32)
    rows = lax.dynamic_slice_in_dim(
        butcher, lax.axis_index("section") * field.shape[0], field.shape[0], 0
    )
    mixed = jnp.einsum("ij,jabc->iabc", rows, everyone, precision=lax.Precision.HIGHEST)
    return field + STEP_SIZE * mixed


def global_total(values):
    return lax.psum(values, ("section", "gx", "gy"))


def stepwise(rhs, guess, kappa, bc_flags):
    levels = [build_level(kappa, bc_flags, count) for count in (5, 3, 2)]
    section_operator = partial(apply_system, coupling=None)
    start_residual = rhs - section_operator(guess, levels[0])
    dofs = float(rhs.size * lax.axis_size("section") * lax.axis_size("gx") * lax.axis_size("gy"))
    beta = jnp.sqrt(global_total(jnp.sum(start_residual * start_residual).reshape(1))[0])
    basis = start_residual / beta
    precond = vcycle(basis, levels, section_operator)
    image = section_operator(precond, levels[0])
    upper = global_total(jnp.sum(image * basis).reshape(1))[0]
    remainder = image - upper * basis
    lower = jnp.sqrt(global_total(jnp.sum(remainder * remainder).reshape(1))[0])
    weight = beta * upper / (upper * upper + lower * lower)
    solution = guess + weight * precond
    residual = start_residual - weight * image
    arnoldi = jnp.stack([beta / math.sqrt(dofs), upper, lower]).astype(jnp.float32)
    return (solution, residual, arnoldi)


EZ = 32
COLS = 16
HALF = 64
FACE_X = HALF + 25
KAPPA = FACE_X + 15
PIECE = KAPPA + 16
LINE_KAPPA = 4 * HALF
LINE_Y = LINE_KAPPA + 4 * 16
LINE = LINE_Y + 104
FIELD = 1000
F32 = jnp.float32


def split_sections():
    matrix = radau_matrix()
    values, vectors = np.linalg.eig(matrix)
    order = [n for n in np.argsort(np.abs(values.imag), kind="stable") if values[n].imag > 0]
    bases = []
    for n in order:
        plane = np.stack([vectors[:, n].real, vectors[:, n].imag], axis=1)
        bases.append(np.linalg.qr(plane)[0])
    left, cross, right = np.linalg.svd(bases[0].T @ bases[1])
    bases = [bases[0] @ left, bases[1] @ right.T]
    for c in range(2):
        sign = np.sign(bases[0][np.argmax(np.abs(bases[0][:, c])), c])
        bases = [np.concatenate([b[:, :c], sign * b[:, c : c + 1], b[:, c + 1 :]], axis=1) for b in bases]
    whole = np.concatenate(bases, axis=1)
    back = np.linalg.inv(whole)
    return whole, back, back @ matrix, back @ matrix @ whole, cross


def iota(shape, dim):
    return lax.broadcasted_iota(jnp.int32, shape, dim)


def exact_dot(a, b):
    return lax.dot_general(
        a, b, (((1,), (0,)), ((), ())), precision=lax.Precision.HIGHEST, preferred_element_type=F32
    )


def split_dot(a, b):
    high = a.astype(jnp.bfloat16)
    rest = a - high.astype(F32)
    middle = rest.astype(jnp.bfloat16)
    low = (rest - middle.astype(F32)).astype(jnp.bfloat16)
    b = b.astype(jnp.bfloat16)
    return sum(
        lax.dot_general(part, b, (((1,), (0,)), ((), ())), preferred_element_type=F32)
        for part in (low, middle, high)
    )


def choose(index, values):
    out = values[-1]
    for place in range(len(values) - 2, -1, -1):
        out = jnp.where(index == place, values[place], out)
    return out


def face_gains(flag, direction, side, count):
    nodes, weights = lobatto(count)
    c, nu = ADVECT[direction], DIFFUSE * count * count
    if side == 0:
        return (c * (1.0 + flag) / 2.0 + nu) * (1.0 / float(weights[0]))
    return (nu - c * (1.0 - flag) / 2.0) * (1.0 / float(weights[-1]))


def row_table():
    kx, ky = (element_matrix(5, d) for d in range(2))
    rows = np.zeros((64, 64))
    for s in range(2):
        for i in range(5):
            for j in range(5):
                r = 2 * (i * 5 + j) + s
                for m in range(5):
                    rows[r, 2 * (m * 5 + j) + s] += kx[i, m]
                    rows[r, 2 * (i * 5 + m) + s] += ky[j, m]
    return rows.astype(np.float32)


def pick_lines(k):
    lane = iota((160, 256), 1)
    return (iota((160, 256), 0) == 5 * (lane % EZ) + k + lane // 128).astype(F32)


def pair_factors(sec, table, own, s):
    upper = iota((32, 128), 1) < 64
    first = jnp.where(upper, float(table[0, s]), float(table[1, s]))
    second = jnp.where(upper, float(table[2, 2 + s]), float(table[3, 2 + s]))
    if not own:
        first = jnp.where(upper, float(table[2, s]), float(table[3, s]))
        second = jnp.where(upper, float(table[0, 2 + s]), float(table[1, 2 + s]))
    return jnp.where(sec == 0, first, second)


def pack_nodes(nodes):
    half = nodes.shape[0] // 2
    odd = iota((half, 128), 1) // EZ % 2 == 1
    return jnp.where(odd, nodes[half:, :], nodes[:half, :])


def local_kernel(
    rhs_in, guess_in, kappa_in, flags_in, rows_in, mine, theirs,
    rhs, guess, kappa, flags, rows_t, sems, stack, lines, nodes, y_faces, x_faces,
):
    sec = lax.axis_index("section")
    pairs = [(guess_in, guess), (rhs_in, rhs), (rows_in, rows_t), (kappa_in, kappa), (flags_in, flags)]
    copies = [pltpu.make_async_copy(source, target, sems.at[n]) for n, (source, target) in enumerate(pairs)]
    for copy in copies:
        copy.start()
    for ref in (stack, nodes, y_faces, x_faces):
        ref[...] = jnp.zeros_like(ref)
    for copy in copies:
        copy.wait()
    for i in range(5):
        stack[192 + 5 * i : 197 + 5 * i, :] = kappa[i]
        for j in range(5):
            r = 2 * (5 * i + j)
            value = guess[i, j]
            stack[128 + r : 130 + r, :] = value
            stack[r : r + 2, :] = rhs[i, j] - value
    stack[64:128, :] = exact_dot(rows_t[...], stack[128:192, :])
    source = stack[...]
    for k in (0, 2, 4):
        shown = split_dot(source, pick_lines(k))
        lines[224 * k : 224 * k + 224, :] = shown[:, :128]
        if k < 4:
            lines[224 * k + 224 : 224 * k + 448, :] = shown[:, 128:]

    def part(k, first, s):
        return lines[pl.ds(224 * k + first + s, 32, stride=2), :]

    def kappa_part(k):
        return lines[224 * k + 192 : 224 * k + 224, :]

    repeat = (iota((EZ, 128), 1) % EZ == iota((EZ, 128), 0)).astype(F32)
    shown = split_dot(flags[:, 0, 0, :].astype(F32), repeat)
    gains = [face_gains(shown[d : d + 1, :], d // 2, d % 2, 5) for d in range(6)]
    row = iota((32, 128), 0)
    none = jnp.zeros((32, 128), F32)
    own = jnp.where(row < 5, gains[0], jnp.where((row >= 20) & (row < 25), gains[1], none))
    own = own + jnp.where(row % 5 == 0, gains[2], jnp.where(row % 5 == 4, gains[3], none))
    kz = element_matrix(5, 2)
    back, back_matrix = split_sections()[1:3]
    fields = [[part(k, 128, s) for k in range(5)] for s in range(2)]
    for k in range(5):
        diagonal = kappa_part(k) + own
        if k == 0:
            diagonal = diagonal + gains[4]
        if k == 4:
            diagonal = diagonal + gains[5]
        images = []
        for s in range(2):
            image = diagonal * fields[s][k] + part(k, 64, s)
            for m in range(5):
                image = image + float(kz[k, m]) * fields[s][m]
            if k == 0:
                image = image - gains[4] * pltpu.roll(fields[s][4], 1, 1)
            if k == 4:
                image = image - gains[5] * pltpu.roll(fields[s][0], 127, 1)
            images.append(image)
        for p, mark in enumerate((True, False)):
            total = jnp.zeros((32, 128), F32)
            trace = jnp.zeros((32, 128), F32)
            for s in range(2):
                total = total + pair_factors(sec, back, mark, s) * part(k, 0, s)
                factor = pair_factors(sec, STEP_SIZE * back_matrix, mark, s)
                total = total - factor * images[s]
                trace = trace + factor * fields[s][k]
            nodes[128 * p + 25 * k : 128 * p + 25 * k + 25, :] = total[:25]
            for i in range(5):
                for f in range(2):
                    r = 64 * p + 32 * f + 5 * k + i
                    y_faces[r : r + 1, :] = trace[5 * i + 4 * f : 5 * i + 4 * f + 1]
            for f in range(2):
                r = 32 * p + 16 * f + 3 * k
                x_faces[r : r + 3, :] = trace[20 * f + 1 : 20 * f + 4]
    upper = iota((1, 128), 1) < 64
    for r in range(3):
        nodes[125 + r : 126 + r, :] = jnp.where(upper, shown[2 * r : 2 * r + 1], shown[2 * r + 1 : 2 * r + 2])
    for p, out in enumerate((mine, theirs)):
        out[:HALF, :] = pack_nodes(nodes[128 * p : 128 * p + 128, :])
        out[HALF:FACE_X, :] = pack_nodes(y_faces[64 * p : 64 * p + 64, :])[:25]
        out[FACE_X:KAPPA, :] = pack_nodes(x_faces[32 * p : 32 * p + 32, :])[:15]
    for k in range(5):
        nodes[25 * k : 25 * k + 25, :] = kappa_part(k)[:25]
    kappas = choose(iota((32, 128), 1) // EZ, [nodes[32 * q : 32 * q + 32, :] for q in range(4)])
    mine[KAPPA:, :] = jnp.where(sec == 0, kappas[:16], kappas[16:])


def part_kernel(source, piece, kappa):
    piece[...] = source[:KAPPA, :]
    kappa[...] = source[KAPPA:, :]


VMEM = pl.BlockSpec(memory_space=pltpu.VMEM)
HBM = pl.BlockSpec(memory_space=pltpu.HBM)


def limit(mib):
    return pltpu.CompilerParams(vmem_limit_bytes=mib * 2**20)


def local_part(rhs, guess, kappa, flags):
    operands = (rhs, guess, kappa, flags, jnp.asarray(row_table()))
    return pl.pallas_call(
        local_kernel,
        out_shape=[jax.ShapeDtypeStruct((rows, 128), F32) for rows in (PIECE, KAPPA)],
        in_specs=[HBM] * 5,
        out_specs=[VMEM] * 2,
        scratch_shapes=[pltpu.VMEM(o.shape, o.dtype) for o in operands]
        + [
            pltpu.SemaphoreType.DMA((5,)),
            pltpu.VMEM((224, 160), F32),
            pltpu.VMEM((5 * 224, 128), F32),
            pltpu.VMEM((256, 128), F32),
            pltpu.VMEM((128, 128), F32),
            pltpu.VMEM((64, 128), F32),
        ],
        compiler_params=limit(60),
        cost_estimate=pl.CostEstimate(flops=20_000_000, bytes_accessed=8_000_000, transcendentals=0),
        name="local_part",
    )(*operands)


def part(x):
    return pl.pallas_call(
        part_kernel,
        out_shape=[jax.ShapeDtypeStruct((rows, 128), F32) for rows in (KAPPA, 16)],
        in_specs=[VMEM],
        out_specs=[VMEM] * 2,
        compiler_params=limit(16),
        name="part",
    )(x)


class Level:
    def __init__(self, count, refs):
        self.count = count
        self.x, self.dir, self.res, self.f = refs
        self.tables = [element_matrix(count, d) for d in range(3)]
        self.gains = self.diag = self.jac = None


def tile(index):
    return pl.ds(index * 8, 8)


def rows_of(pieces, size, r, h):
    return pieces[pl.ds(8 * h * size + r, 8, stride=size), :]


ORDER_X = ((3, 2), (2, 3), (1, 1))
ORDER_Y = ((3, 3), (1, 2), (2, 1))


def partner(bits):
    return jnp.where(lax.axis_index("section") == 0, bits[0], bits[1])


def place_pieces(blocks, pieces, first, size, room):
    my_gx, my_gy = lax.axis_index("gx"), lax.axis_index("gy")
    for b, block in enumerate(blocks):
        gy = my_gy ^ partner(ORDER_Y[b - 1]) if b else my_gy
        for a in range(4):
            column = (my_gx ^ a) * 4 + gy
            start = pl.multiple_of(column * room, 8)
            pieces[pl.ds(start, size), :] = block[first + a * size : first + a * size + size, :]


class Lanes:
    def __init__(self):
        self.lane = iota((8, 128), 1)
        sub = iota((8, 128), 0)
        self.group = self.lane // EZ
        self.odd = self.group % 2 == 1
        self.element = self.lane % EZ
        self.place = sub % 4
        self.low_half = sub < 4

    def around(self, u):
        turned = pltpu.roll(u, 4, u.ndim - 2)
        far = jnp.where(self.odd, pltpu.roll(turned, 32, u.ndim - 1), pltpu.roll(turned, 96, u.ndim - 1))
        return turned, far

    def x_before(self, u):
        turned, far = self.around(u)
        return jnp.where(self.low_half, far, turned)

    def x_after(self, u):
        turned, far = self.around(u)
        return jnp.where(self.low_half, turned, far)

    def y_before(self, u):
        return jnp.where(self.place == 0, pltpu.roll(u, 5, 0), pltpu.roll(u, 1, 0))

    def y_after(self, u):
        return jnp.where(self.place == 3, pltpu.roll(u, 3, 0), pltpu.roll(u, 7, 0))

    def z_before(self, u):
        return jnp.where(self.element == 0, pltpu.roll(u, 97, u.ndim - 1), pltpu.roll(u, 1, u.ndim - 1))

    def z_after(self, u):
        last = self.element == EZ - 1
        return jnp.where(last, pltpu.roll(u, 31, u.ndim - 1), pltpu.roll(u, 127, u.ndim - 1))


def load(ref, first, count):
    return ref[pl.ds(first * 8, count * 8), :].reshape(count, 8, 128)


def store(ref, first, value):
    ref[pl.ds(first * 8, value.shape[0] * 8), :] = value.reshape(value.shape[0] * 8, 128)


DIAGS = (0, 250, 304)
GAINS = (320, 326, 332)
REGISTERS = 338
CENTRE = (CHEB_HIGH + CHEB_LOW) / 2.0
RADIUS = (CHEB_HIGH - CHEB_LOW) / 2.0


def flag_lanes(row, slot):
    turned = [row] + [pltpu.roll(row, 32 * m, 1) for m in range(1, 4)]
    return choose(iota(row.shape, 1) // EZ, [turned[(g - 2 * slot - 1) % 4] for g in range(4)])


def line_kernel(first, second, third, own, line, faces, sorted_pieces):
    sorted_pieces[:PIECE, :] = own[...]
    for bits, piece in zip(ORDER_X, (first, second, third)):
        sorted_pieces[pl.ds(pl.multiple_of(partner(bits) * PIECE, 8), PIECE), :] = piece[...]
    pieces = [sorted_pieces.at[PIECE * a : PIECE * a + PIECE, :] for a in range(4)]
    even = lax.axis_index("gx") % 2 == 0
    odd = iota((8, 128), 1) // EZ % 2 == 1
    faces[...] = jnp.zeros_like(faces)

    def both(rows, f):
        side = odd[:1] if f else jnp.logical_not(odd[:1])
        return jnp.where(side, rows, pltpu.roll(rows, 96 if f else 32, 1))

    for a, piece in enumerate(pieces):
        for f in range(2):
            base = 64 * a + 32 * f
            inner = both(piece[FACE_X:KAPPA, :], f)
            ends = [both(piece[HALF:FACE_X, :], g) for g in range(2)]
            for k in range(5):
                r = base + 5 * k
                node = 5 * k + 4 * f
                faces[r : r + 1, :] = ends[0][node : node + 1]
                faces[r + 1 : r + 4, :] = inner[3 * k : 3 * k + 3]
                faces[r + 4 : r + 5, :] = ends[1][node : node + 1]
    for a, piece in enumerate(pieces):
        line[HALF * a : HALF * a + HALF, :] = piece[:HALF, :]
        line[LINE_KAPPA + 16 * a : LINE_KAPPA + 16 * a + 16, :] = piece[KAPPA:, :]
        line[LINE_Y + 25 * a : LINE_Y + 25 * a + 25, :] = piece[HALF:FACE_X, :]
        flags = [flag_lanes(piece[61:62, :], slot) for slot in range(2)]
        gains = [face_gains(flags[d], 0, d, 5) for d in range(2)]
        next_first = even if a % 2 == 0 else jnp.logical_not(even)
        for f in range(2):
            one = faces[64 * (a ^ 1) + 32 * (1 - f) : 64 * (a ^ 1) + 32 * (1 - f) + 32, :]
            three = faces[64 * (a ^ 3) + 32 * (1 - f) : 64 * (a ^ 3) + 32 * (1 - f) + 32, :]
            near = jnp.where(next_first, one, three) if f else jnp.where(next_first, three, one)
            term = gains[f] * near
            for k in range(5):
                node = 25 * k + 20 * f
                side = odd[:5] if node >= HALF else jnp.logical_not(odd[:5])
                r = HALF * a + node % HALF
                line[r : r + 5, :] = line[r : r + 5, :] + jnp.where(side, term[5 * k : 5 * k + 5], 0.0)
    line[LINE_Y + 100 :, :] = jnp.zeros((4, 128), F32)


def halves_kernel(block0, block1, block2, block3, out):
    place_pieces((block0, block1, block2, block3), out, LINE_KAPPA, 16, 16)


def widen(low, high, odd):
    return jnp.where(odd, pltpu.roll(high, 32, 1), low), jnp.where(odd, high, pltpu.roll(low, 96, 1))


def assemble_kernel(block0, block1, block2, block3, field, pieces, edges, traces):
    blocks = (block0, block1, block2, block3)
    place_pieces(blocks, pieces, 0, HALF, HALF)
    place_pieces(blocks, edges, LINE_Y, 25, 32)
    lanes = Lanes()
    for source, size, rows, target, apart in ((edges, 32, 25, traces, 25), (pieces, HALF, HALF, field, HALF)):
        for r in range(rows):
            first, second = widen(rows_of(source, size, r, 0), rows_of(source, size, r, 1), lanes.odd)
            target[tile(r), :] = first
            target[tile(apart + r), :] = second
    got = field[tile(126), :]
    across = pltpu.roll(got, 64, 1)
    gains = [
        face_gains(jnp.where(lanes.lane < 64, got, across), 1, 0, 5),
        face_gains(jnp.where(lanes.lane < 64, across, got), 1, 1, 5),
    ]
    for k in range(5):
        for i in range(5):
            lower, upper = traces[tile(5 * k + i), :], traces[tile(25 + 5 * k + i), :]
            node = 25 * k + 5 * i
            field[tile(node), :] = field[tile(node), :] + gains[0] * lanes.y_before(upper)
            field[tile(node + 4), :] = field[tile(node + 4), :] + gains[1] * lanes.y_after(lower)


def setup_kernel(field, own_halves, other_halves, coefs, kap):
    sec = lax.axis_index("section")
    lanes = Lanes()
    group, lane = lanes.group, lanes.lane
    flags = []
    for r in range(3):
        got = field[tile(125 + r), :]
        across = pltpu.roll(got, 64, 1)
        flags += [jnp.where(lane < 64, got, across), jnp.where(lane < 64, across, got)]
    for r in range(16):
        pairs = [[rows_of(ref, 16, r, h) for h in range(2)] for ref in (own_halves, other_halves)]
        for half in range(2):
            turned = []
            for h in range(2):
                got = jnp.where(sec == half, pairs[0][h], pairs[1][h])
                turned.append([pltpu.roll(got, 32 * m, 1) if m else got for m in range(4)])
            for q in range(4):
                value = choose(group, [turned[g % 2][(g - q) % 4] for g in range(4)])
                kap[tile(q * 32 + half * 16 + r), :] = value
    for p, n in enumerate((5, 3, 2)):
        stride = 4 // (n - 1)
        gains = [face_gains(flags[d], d // 2, d % 2, n) for d in range(6)]
        rows = []
        for d in range(3):
            coefs[tile(GAINS[p] + 2 * d), :] = gains[2 * d]
            coefs[tile(GAINS[p] + 2 * d + 1), :] = gains[2 * d + 1]
            table = element_matrix(n, d)
            row = [jnp.full((8, 128), float(table[m, m]), F32) for m in range(n)]
            row[0] = row[0] + gains[2 * d]
            row[n - 1] = row[n - 1] + gains[2 * d + 1]
            rows.append(row)
        along = jnp.stack(rows[1])
        for k in range(n):
            for i in range(n):
                line = load(kap, k * 25 * stride + i * stride * 5, 5)
                line = jnp.stack([line[j * stride] for j in range(n)])
                value = line + (along + (rows[2][k] + rows[0][i]))
                scale = 1.0 / (1.0 + STEP_SIZE * JACOBI_SCALE * value)
                store(coefs, DIAGS[p] + (k * n + i) * n, value)
                store(coefs, DIAGS[p] + n**3 + (k * n + i) * n, scale * (1.0 / CENTRE))


def cycle_kernel(coefs, assembled, fields, more, *scratch):
    sec = lax.axis_index("section")
    my_gx, my_gy = lax.axis_index("gx"), lax.axis_index("gy")
    levels = [Level(n, scratch[4 * p : 4 * p + 4]) for p, n in enumerate((5, 3, 2))]
    half = scratch[12]
    lanes = Lanes()
    lane = lanes.lane
    blocks = split_sections()[3]

    def lanes_of(upper, lower):
        return jnp.where(lane < 64, jnp.where(sec == 0, upper[0], upper[1]), jnp.where(sec == 0, lower[0], lower[1]))

    entry = [[[float(STEP_SIZE * blocks[2 * p + a, 2 * p + b]) for p in range(2)] for b in range(2)] for a in range(2)]
    same = lanes_of(entry[0][0], entry[1][1])
    swap = lanes_of(entry[0][1], entry[1][0])
    first_rho = RADIUS / CENTRE
    second_rho = 1.0 / (2.0 * CENTRE / RADIUS - first_rho)
    keep = 1.0 + second_rho * first_rho
    push = 2.0 * second_rho / RADIUS * CENTRE
    for p, level in enumerate(levels):
        size = level.count**3
        level.gains = [-coefs[tile(GAINS[p] + d), :] for d in range(6)]
        level.diag = lambda first, count, p=p: load(coefs, DIAGS[p] + first, count)
        level.jac = lambda first, count, p=p, size=size: load(coefs, DIAGS[p] + size + first, count)

    def begin(level, source):
        n = level.count
        for first in range(0, n**3, n):
            f = load(source, first, n)
            store(level.dir, first, level.jac(first, n) * f)
            store(level.res, first, f)
            store(level.x, first, jnp.zeros_like(f))

    def apply(level, smooth):
        n = level.count
        kx, ky, kz = level.tables
        gains = level.gains
        source = level.dir if smooth else level.x
        def tree(terms):
            while len(terms) > 1:
                pairs = [a + b for a, b in zip(terms[::2], terms[1::2])]
                terms = pairs + terms[len(terms) // 2 * 2 :]
            return terms[0]

        def sums(k):
            def line_at(i):
                return load(source, (k * n + i) * n, n)

            x_left = gains[0] * lanes.x_before(line_at(n - 1))
            x_right = gains[1] * lanes.x_after(line_at(0))
            z_low, z_high, y_low, y_high = [], [], [], []
            for i in range(n):
                if k == 0:
                    z_low.append(gains[4] * lanes.z_before(load(source, ((n - 1) * n + i) * n, n)))
                if k == n - 1:
                    z_high.append(gains[5] * lanes.z_after(load(source, i * n, n)))
                v = line_at(i)
                y_low.append(gains[2] * lanes.y_before(v[n - 1]))
                y_high.append(gains[3] * lanes.y_after(v[0]))
            totals = []
            for i in range(n):
                first = (k * n + i) * n
                v = line_at(i)
                along_x = [float(kx[i, m]) * line_at(m) for m in range(n) if m != i]
                along_z = [float(kz[k, m]) * load(source, (m * n + i) * n, n) for m in range(n) if m != k]
                along_y = []
                for j in range(n):
                    terms = [float(ky[j, m]) * v[m] for m in range(n) if m != j]
                    if j == 0:
                        terms.append(y_low[i])
                    if j == n - 1:
                        terms.append(y_high[i])
                    along_y.append(tree(terms))
                if i == 0:
                    along_x.append(x_left)
                if i == n - 1:
                    along_x.append(x_right)
                if k == 0:
                    along_z.append(z_low[i])
                if k == n - 1:
                    along_z.append(z_high[i])
                totals.append(tree([level.diag(first, n) * v, tree(along_x), tree(along_z), jnp.stack(along_y)]))
            return totals

        def update(k, totals):
            moved = [pltpu.roll(total, 64, 2) for total in totals]
            for i in range(n):
                first = (k * n + i) * n
                v = load(source, first, n)
                image = v + (same * totals[i] + swap * moved[i])
                if smooth:
                    scaled = level.jac(first, n) * (load(level.res, first, n) - image)
                    store(level.x, first, (load(level.x, first, n) + keep * v) + push * scaled)
                else:
                    rest = load(level.f, first, n) - image
                    store(level.res, first, rest)
                    store(level.dir, first, level.jac(first, n) * rest)

        if n == 5:
            ready = sums(0)
            for k in range(n):
                following = sums(k + 1) if k + 1 < n else None
                update(k, ready)
                ready = following
        else:
            for k, totals in enumerate([sums(k) for k in range(n)]):
                update(k, totals)

    def combine(weights, parts):
        total = None
        for weight, part in zip(weights, parts):
            if abs(weight) > 1e-14:
                term = part if abs(weight - 1.0) < 1e-14 else float(weight) * part
                total = term if total is None else total + term
        return total

    def change(table, source, target, add):
        m, n = table.shape
        for i in range(n):
            parts = [load(source, i * n + k * n * n, n) for k in range(n)]
            for k in range(m):
                store(half, i * n + k * n * n, combine(table[k], parts))
        for k in range(m):
            parts = [load(half, k * n * n + i * n, n) for i in range(n)]
            for i in range(m):
                line = combine(table[i], parts)
                value = jnp.stack([combine(table[j], [line[a] for a in range(n)]) for j in range(m)])
                first = k * m * m + i * m
                store(target, first, load(target, first, m) + value if add else value)

    def down(n, m):
        fine_nodes, fine_weights = lobatto(n)
        coarse_nodes, coarse_weights = lobatto(m)
        table = lagrange_table(coarse_nodes, fine_nodes)
        return (1.0 / coarse_weights)[:, None] * table.T * fine_weights[None, :]

    def up(m, n):
        return lagrange_table(lobatto(m)[0], lobatto(n)[0])

    def solve(p):
        level = levels[p]
        if p == 2:
            apply(level, True)
            return
        below = levels[p + 1]

        def correct():
            n, m = level.count, below.count
            change(down(n, m), level.res, below.f, False)
            begin(below, below.f)
            solve(p + 1)
            change(up(m, n), below.x, level.x, True)

        if p == 1:
            apply(level, True)
            apply(level, False)
            correct()
            apply(level, False)
            apply(level, True)
            return

        def step(t, carry):
            @pl.when(t != 1)
            def _():
                apply(level, True)

            apply(level, False)

            @pl.when(t == 0)
            def _():
                correct()
            return carry
        lax.fori_loop(0, 3, step, 0)

    fine = levels[0]
    fine.f = assembled
    begin(fine, assembled)
    solve(0)

    for first in range(0, 125, 5):
        part, place = (fields, first) if first < SPLIT else (more, first - SPLIT)
        store(part, place, load(fine.res, first, 5))
    column = (my_gx % 2) * 4 + my_gy
    more[AFTER : AFTER + 125, :] = fine.x[pl.ds(column, 125, stride=8), :]
    more[AFTER + 125 :, :] = jnp.zeros((3, 128), F32)


SPLIT = 75
AFTER = 8 * (125 - SPLIT)


def register(parts, r):
    return parts[0][tile(r), :] if r < SPLIT else parts[1][tile(r - SPLIT), :]


def column_of(parts, k):
    first = 3 * (k // 3)
    return parts[k // 3][column_rows(k - first), :]


def column_z(parts, k):
    return parts[1][AFTER + 25 * k : AFTER + 25 * k + 25, :]


def pair_weights():
    cross = split_sections()[4]
    return jnp.where(iota((8, 128), 1) < 64, float(cross[0]), float(cross[1]))


def column_factors(p):
    sec = lax.axis_index("section")
    whole = split_sections()[0]
    lane = iota((25, 128), 1)
    here = lane // EZ % 2 == lax.axis_index("gx") // 2
    factors = []
    for s in range(2):
        parts = []
        for mine in range(2):
            t = whole[2 * mine + s]
            q = mine if p == 0 else 1 - mine
            parts.append(jnp.where(lane < 64, float(t[2 * q]), float(t[2 * q + 1])))
        factors.append(jnp.where(here, jnp.where(sec == 0, parts[0], parts[1]), 0.0))
    return factors


def column_rows(k):
    column = (lax.axis_index("gx") % 2) * 4 + lax.axis_index("gy")
    return pl.ds(k * 200 + column, 25, stride=8)


def raw_order(k):
    lane = iota((256, 160), 0)
    return (iota((256, 160), 1) == 5 * (lane % EZ) + k + lane // 128).astype(F32)


def side_by_side(cols):
    half = cols.shape[0] // 2
    return jnp.concatenate([cols[:half, :], cols[half:, :]], axis=1)


def early_kernel(own0, own1, own_start, other_start, sums, column_out, cols):
    own = (own0, own1)
    weights = pair_weights()
    cols[...] = jnp.zeros_like(cols)
    total = jnp.zeros((192, 160), F32)
    own_factors, other_factors = column_factors(0), column_factors(1)
    for k in range(5):
        where = column_rows(k)
        z = column_z(own, k)
        start, other = own_start[where, :], other_start[where, :]
        w = start - column_of(own, k)
        side = 192 * (k % 2)
        for s in range(2):
            cols[pl.ds(side + s, 25, stride=2), :] = own_factors[s] * z
            cols[pl.ds(side + 64 + s, 25, stride=2), :] = own_factors[s] * start + other_factors[s] * other
            cols[pl.ds(side + 128 + s, 25, stride=2), :] = own_factors[s] * w
        if k % 2 == 1:
            total = total + split_dot(side_by_side(cols), raw_order(k - 1))
    cols[192:, :] = jnp.zeros((192, 128), F32)
    total = total + split_dot(side_by_side(cols), raw_order(4))
    column_out[...] = total
    nothing = jnp.zeros((8, 128), F32)
    uppers, sizes = [nothing] * 5, [nothing] * 5
    for r in range(125):
        c, d = own_start[tile(r), :], other_start[tile(r), :]
        a = c - register(own, r)
        uppers[r % 5] = uppers[r % 5] + a * (c + weights * d)
        sizes[r % 5] = sizes[r % 5] + ((c * c + d * d) + 2.0 * (weights * (c * d)))
    sums[0:8, :] = sum(uppers)
    sums[8:16, :] = jnp.broadcast_to(jnp.sum(sum(sizes), keepdims=True), (8, 128))


def finish_kernel(own0, own1, other0, other1, own_start, other_start, sums, column, guess, sol, res_out, arnoldi, cols, outs):
    own, other = (own0, own1), (other0, other1)
    cols[...] = jnp.zeros_like(cols)
    total = jnp.zeros((128, 160), F32)
    factors = column_factors(1)
    for k in range(5):
        where = column_rows(k)
        z = column_z(other, k)
        w = other_start[where, :] - column_of(other, k)
        side = 128 * (k % 2)
        for s in range(2):
            cols[pl.ds(side + s, 25, stride=2), :] = factors[s] * z
            cols[pl.ds(side + 64 + s, 25, stride=2), :] = factors[s] * w
        if k % 2 == 1:
            total = total + split_dot(side_by_side(cols), raw_order(k - 1))
    cols[128:, :] = jnp.zeros((128, 128), F32)
    total = total + split_dot(side_by_side(cols), raw_order(4))
    weights = pair_weights()
    nothing = jnp.zeros((8, 128), F32)
    uppers = [nothing] * 5
    for r in range(125):
        c, d = own_start[tile(r), :], other_start[tile(r), :]
        b = d - register(other, r)
        uppers[r % 5] = uppers[r % 5] + b * (d + weights * c)

    mine, theirs = sums[0:8, :], sum(uppers)
    size = sums[8:9, 0:1]
    upper = jnp.sum(mine + theirs, keepdims=True) / size
    rests = [nothing] * 5
    for r in range(125):
        c, d = own_start[tile(r), :], other_start[tile(r), :]
        a = (c - register(own, r)) - upper * c
        b = (d - register(other, r)) - upper * d
        rests[r % 5] = rests[r % 5] + ((a * a + b * b) + 2.0 * (weights * (a * b)))
    rest = jnp.sum(sum(rests), keepdims=True)
    beta = jnp.sqrt(size)
    lower = jnp.sqrt(rest) / beta
    weight = upper / (upper * upper + lower * lower)
    entries = float(125 * EZ * COLS * 4)
    for place_out, value in enumerate((beta * (1.0 / math.sqrt(entries)), upper, lower)):
        arnoldi[place_out] = value[0, 0]
    outs[:64, :] = weight * (column[:64, :] + total[:64])
    outs[64:, :] = column[64:128, :] - weight * (column[128:, :] + total[64:])
    for i in range(5):
        for j in range(5):
            r = 2 * (5 * i + j)
            sol[i, j] = guess[i, j] + outs[r : r + 2, :]
            res_out[i, j] = outs[64 + r : 66 + r, :]


def plain_call(kernel, name, rows, scratch, operands, cost=1_000_000):
    return pl.pallas_call(
        kernel,
        out_shape=jax.ShapeDtypeStruct((rows, 128), F32),
        in_specs=[VMEM] * len(operands),
        out_specs=VMEM,
        scratch_shapes=[pltpu.VMEM((r, 128), F32) for r in scratch],
        compiler_params=limit(16),
        cost_estimate=pl.CostEstimate(flops=cost, bytes_accessed=cost, transcendentals=0),
        name=name,
    )(*operands)


def cycle(coefs, assembled):
    scratch = []
    for n in (5, 3, 2):
        scratch += [pltpu.VMEM((n**3 * 8, 128), F32)] * 4
    scratch += [pltpu.VMEM((FIELD, 128), F32)]
    return pl.pallas_call(
        cycle_kernel,
        out_shape=[jax.ShapeDtypeStruct((rows, 128), F32) for rows in (SPLIT * 8, AFTER + 128)],
        in_specs=[VMEM] * 2,
        out_specs=[VMEM] * 2,
        scratch_shapes=scratch,
        compiler_params=limit(24),
        cost_estimate=pl.CostEstimate(flops=40_000_000, bytes_accessed=30_000_000, transcendentals=0),
        name="cycle",
    )(coefs, assembled)


def early(own, own_start, other_start):
    return pl.pallas_call(
        early_kernel,
        out_shape=[jax.ShapeDtypeStruct((16, 128), F32), jax.ShapeDtypeStruct((192, 160), F32)],
        in_specs=[VMEM] * 4,
        out_specs=[VMEM] * 2,
        scratch_shapes=[pltpu.VMEM((384, 128), F32)],
        compiler_params=limit(16),
        cost_estimate=pl.CostEstimate(flops=4_000_000, bytes_accessed=4_000_000, transcendentals=0),
        name="early",
    )(*own, own_start, other_start)


def finish(own, other, own_start, other_start, sums, column, guess):
    return pl.pallas_call(
        finish_kernel,
        out_shape=[
            jax.ShapeDtypeStruct(guess.shape, F32),
            jax.ShapeDtypeStruct(guess.shape, F32),
            jax.ShapeDtypeStruct((3,), F32),
        ],
        in_specs=[VMEM] * 9,
        out_specs=[VMEM, VMEM, pl.BlockSpec(memory_space=pltpu.SMEM)],
        scratch_shapes=[pltpu.VMEM((256, 128), F32), pltpu.VMEM((128, 160), F32)],
        compiler_params=limit(24),
        name="finish",
    )(*own, *other, own_start, other_start, sums, column, guess)


def exchange(x, axis, bits):
    return lax.ppermute(x, axis, [(n, n ^ bits) for n in range(lax.axis_size(axis))])


def exchange_by_core(x, axis, bits):
    count = lax.axis_size(axis)
    pairs = [(s * count + n, s * count + (n ^ bits[s])) for s in range(2) for n in range(count)]
    return lax.ppermute(x, ("section", axis), pairs)


def gathered_body(rhs, guess, kappa, bc_flags):
    rhs, guess = (jnp.transpose(v, (1, 2, 0, 3)) for v in (rhs, guess))
    mine, theirs = local_part(rhs, guess, kappa, bc_flags)
    got, mine, kappa_piece = lax.optimization_barrier((exchange(theirs, "section", 1), *part(mine)))
    piece = jnp.concatenate([mine + got, kappa_piece])
    pieces = [exchange_by_core(piece, "gx", bits) for bits in ORDER_X] + [piece]
    line = plain_call(line_kernel, "line", LINE, [4 * 64, 4 * PIECE], pieces)
    blocks = [line] + [exchange_by_core(line, "gy", bits) for bits in ORDER_Y]
    halves = plain_call(halves_kernel, "halves", COLS * 16, [], blocks)
    other_halves = exchange(halves, "section", 1)
    start = plain_call(assemble_kernel, "assemble", 128 * 8, [COLS * HALF, COLS * 32, 50 * 8], blocks, 4_000_000)
    start, other_halves = lax.optimization_barrier((start, other_halves))
    coefs = plain_call(setup_kernel, "setup", REGISTERS * 8, [128 * 8], (start, halves, other_halves))
    other_start = exchange(start, "section", 1)
    own, other_start = lax.optimization_barrier((cycle(coefs, start), other_start))
    other = [exchange(part, "section", 1) for part in own]
    sums, column = early(own, start, other_start)
    sol, res, arnoldi = finish(own, other, start, other_start, sums, column, guess)
    sol, res = (jnp.transpose(v, (2, 0, 1, 3)) for v in (sol, res))
    return sol, res, arnoldi


def solution(mesh):
    placed = (
        P("section", "gx", "gy", None),
        P("section", "gx", "gy", None),
        P("gx", "gy", None),
        P(None, "gx", "gy", None),
    )
    sizes = (mesh.shape["section"], mesh.shape["gx"], mesh.shape["gy"])

    def step(rhs, guess, kappa, bc_flags):
        fits = sizes == (2, 4, 4) and rhs.shape == (4, 20, 20, 160)
        return jax.shard_map(
            gathered_body if fits else stepwise,
            mesh=mesh,
            in_specs=placed,
            out_specs=(P("section", "gx", "gy", None), P("section", "gx", "gy", None), P()),
            check_vma=False,
        )(rhs, guess, kappa, bc_flags)

    return step
```

```python
from functools import partial
import math

import jax
import jax.numpy as jnp
import numpy as np
from jax import lax
from jax.experimental import pallas as pl
from jax.experimental.pallas import tpu as pltpu
from jax.sharding import PartitionSpec as P

ADVECT = (1.0, 0.7, 0.5)
DIFFUSE = 0.05
STEP_SIZE = 0.2
JACOBI_SCALE = 0.25
CHEB_LOW = 0.25
CHEB_HIGH = 2.0
LETTERS = "abcdef"


def extended(x, sides, width):
    for axis, dim in sides:
        peers, length = (lax.axis_size(axis), x.shape[dim])
        up = [(i, (i + 1) % peers) for i in range(peers)]
        down = [(j, i) for i, j in up]
        last = lax.slice_in_dim(x, length - width, length, axis=dim)
        leading = lax.slice_in_dim(x, 0, width, axis=dim)
        before = lax.ppermute(last, axis, up)
        after = lax.ppermute(leading, axis, down)
        x = jnp.concatenate([before, x, after], axis=dim)
    return x


def lobatto(count):
    if count == 5:
        inner = math.sqrt(3.0 / 7.0)
        return (
            np.array([-1.0, -inner, 0.0, inner, 1.0]),
            np.array([0.1, 49.0 / 90.0, 32.0 / 45.0, 49.0 / 90.0, 0.1]),
        )
    if count == 3:
        return (np.array([-1.0, 0.0, 1.0]), np.array([1.0 / 3.0, 4.0 / 3.0, 1.0 / 3.0]))
    return (np.array([-1.0, 1.0]), np.array([1.0, 1.0]))


def lagrange_table(nodes, points):
    table = np.ones((len(points), len(nodes)))
    for column in range(len(nodes)):
        for other in range(len(nodes)):
            if other != column:
                table[:, column] *= (points - nodes[other]) / (nodes[column] - nodes[other])
    return table


def slope_table(nodes):
    total = len(nodes)
    factor = np.array(
        [np.prod([nodes[i] - nodes[k] for k in range(total) if k != i]) for i in range(total)]
    )
    table = np.zeros((total, total))
    for row in range(total):
        for column in range(total):
            if row != column:
                table[row, column] = factor[row] / factor[column] / (nodes[row] - nodes[column])
        table[row, row] = -np.sum(table[row])
    return table


def element_matrix(count, direction):
    nodes, weights = lobatto(count)
    slopes = slope_table(nodes)
    stiffness = (1.0 / weights)[:, None] * (slopes.T @ (weights[:, None] * slopes))
    return ADVECT[direction] * slopes + DIFFUSE * stiffness


def legendre_pair(point, order):
    values = [1.0, point]
    slopes = [0.0, 1.0]
    for index in range(1, order):
        values.append(
            ((2 * index + 1) * point * values[index] - index * values[index - 1]) / (index + 1)
        )
        slopes.append(slopes[index - 1] + (2 * index + 1) * values[index])
    return (values, slopes)


def radau_nodes():
    starts = [0.0885879595127039, 0.4094668644407347, 0.7876594617608471]
    found = []
    for start in starts:
        point = start
        for sweep in range(30):
            values, slopes = legendre_pair(2.0 * point - 1.0, 4)
            change = (values[4] - values[3]) / (2.0 * (slopes[4] - slopes[3]))
            point = point - change
        found.append(point)
    found.append(1.0)
    return found


def poly_times(coefs, root):
    result = [0.0] * (len(coefs) + 1)
    for index in range(len(coefs)):
        result[index + 1] += coefs[index]
        result[index] -= root * coefs[index]
    return result


def radau_matrix():
    order = 4
    nodes = radau_nodes()
    matrix = np.zeros((order, order))
    for column in range(order):
        coefs = [1.0]
        denominator = 1.0
        for other in range(order):
            if other != column:
                coefs = poly_times(coefs, nodes[other])
                denominator *= nodes[column] - nodes[other]
        for row in range(order):
            upper_end = nodes[row]
            integral = 0.0
            for index in range(len(coefs)):
                integral += coefs[index] * upper_end ** (index + 1) / (index + 1)
            matrix[row, column] = integral / denominator
    return matrix


def node_einsum(table, field, axis):
    labels = LETTERS[: field.ndim]
    source = labels[: axis + 1] + "j" + labels[axis + 2 :]
    target = labels[: axis + 1] + "i" + labels[axis + 2 :]
    return jnp.einsum(
        "ij," + source + "->" + target,
        jnp.asarray(table, jnp.float32),
        field,
        precision=lax.Precision.HIGHEST,
    )


def apply_along(field, axis, count, table):
    shape = field.shape
    split = shape[:axis] + (shape[axis] // count, count) + shape[axis + 1 :]
    mapped = node_einsum(table, field.reshape(split), axis)
    return mapped.reshape(
        shape[:axis] + (mapped.shape[axis] * mapped.shape[axis + 1],) + shape[axis + 1 :]
    )


def line_part(field, axis, count, table, left_gain, right_gain, left_edge, right_edge):
    shape = field.shape
    elements = shape[axis] // count
    split = field.reshape(shape[:axis] + (elements, count) + shape[axis + 1 :])
    linear = node_einsum(table, split, axis)
    first = lax.index_in_dim(split, 0, axis + 1, keepdims=False)
    last = lax.index_in_dim(split, count - 1, axis + 1, keepdims=False)
    before = jnp.concatenate(
        [jnp.expand_dims(left_edge, axis), lax.slice_in_dim(last, 0, elements - 1, axis=axis)], axis
    )
    after = jnp.concatenate(
        [lax.slice_in_dim(first, 1, elements, axis=axis), jnp.expand_dims(right_edge, axis)], axis
    )
    front = jnp.expand_dims(left_gain * (first - before), axis + 1)
    back = jnp.expand_dims(right_gain * (last - after), axis + 1)
    if count > 2:
        middle_shape = list(front.shape)
        middle_shape[axis + 1] = count - 2
        pieces = [front, jnp.zeros(middle_shape, jnp.float32), back]
    else:
        pieces = [front, back]
    return (linear + jnp.concatenate(pieces, axis + 1)).reshape(shape)


def diag_along(shape, axis, count, table, left_gain, right_gain):
    elements = shape[axis] // count
    split = shape[:axis] + (elements, count) + shape[axis + 1 :]
    profile = [1] * len(split)
    profile[axis + 1] = count
    diagonal_entries = np.array([table[index, index] for index in range(count)])
    base = jnp.broadcast_to(jnp.asarray(diagonal_entries, jnp.float32).reshape(profile), split)
    front = jnp.expand_dims(left_gain, axis + 1)
    back = jnp.expand_dims(right_gain, axis + 1)
    if count > 2:
        middle_shape = list(front.shape)
        middle_shape[axis + 1] = count - 2
        pieces = [front, jnp.zeros(middle_shape, jnp.float32), back]
    else:
        pieces = [front, back]
    return (base + jnp.concatenate(pieces, axis + 1)).reshape(shape)


def level_kappa(kappa, count):
    if count == 5:
        return kappa
    picks = np.array([0, 2, 4]) if count == 3 else np.array([0, 4])
    extents = [extent // 5 for extent in kappa.shape]
    grouped = kappa.reshape(extents[0], 5, extents[1], 5, extents[2], 5)
    for axis in (1, 3, 5):
        grouped = jnp.take(grouped, picks, axis=axis)
    return grouped.reshape(extents[0] * count, extents[1] * count, extents[2] * count)


def face_plane(face, direction, count):
    plane = face.astype(jnp.float32)
    for axis in range(3):
        if axis != direction:
            plane = jnp.repeat(plane, count, axis=axis)
    return plane


def build_level(kappa, flags, count):
    nodes, weights = lobatto(count)
    kappa_level = level_kappa(kappa, count)
    tables, lefts, rights = ([], [], [])
    diagonal = kappa_level
    for direction in range(3):
        table = element_matrix(count, direction)
        lower = face_plane(flags[2 * direction], direction, count)
        upper = face_plane(flags[2 * direction + 1], direction, count)
        left_gain = (ADVECT[direction] * (1.0 + lower) / 2.0 + DIFFUSE * count * count) / float(
            weights[0]
        )
        right_gain = (DIFFUSE * count * count - ADVECT[direction] * (1.0 - upper) / 2.0) / float(
            weights[-1]
        )
        tables.append(table)
        lefts.append(left_gain)
        rights.append(right_gain)
        diagonal = diagonal + diag_along(
            kappa_level.shape, direction, count, table, left_gain, right_gain
        )
    scale = 1.0 / (1.0 + STEP_SIZE * JACOBI_SCALE * diagonal)
    return (count, tables, lefts, rights, kappa_level, scale)


def restrict(field, fine_count, coarse_count):
    fine_nodes, fine_weights = lobatto(fine_count)
    coarse_nodes, coarse_weights = lobatto(coarse_count)
    table = (
        (1.0 / coarse_weights)[:, None]
        * lagrange_table(coarse_nodes, fine_nodes).T
        * fine_weights[None, :]
    )
    for axis in range(field.ndim - 3, field.ndim):
        field = apply_along(field, axis, fine_count, table)
    return field


def prolong(field, coarse_count, fine_count):
    fine_nodes, fine_weights = lobatto(fine_count)
    coarse_nodes, coarse_weights = lobatto(coarse_count)
    table = lagrange_table(coarse_nodes, fine_nodes)
    for axis in range(field.ndim - 3, field.ndim):
        field = apply_along(field, axis, coarse_count, table)
    return field


def chebyshev(rhs, start, level, operator):
    centre = (CHEB_HIGH + CHEB_LOW) / 2.0
    radius = (CHEB_HIGH - CHEB_LOW) / 2.0
    ratio = centre / radius
    first_rho = 1.0 / ratio
    second_rho = 1.0 / (2.0 * ratio - first_rho)
    scale = level[5]
    if start is None:
        remain = rhs
    else:
        remain = rhs - operator(start, level)
    step = scale * remain / centre
    guess = step if start is None else start + step
    remain = remain - operator(step, level)
    step = second_rho * first_rho * step + 2.0 * second_rho / radius * scale * remain
    return guess + step


def vcycle(rhs, levels, operator):
    fine, middle, coarse = levels
    fine_x = chebyshev(rhs, None, fine, operator)
    middle_rhs = restrict(rhs - operator(fine_x, fine), 5, 3)
    middle_x = chebyshev(middle_rhs, None, middle, operator)
    coarse_rhs = restrict(middle_rhs - operator(middle_x, middle), 3, 2)
    coarse_x = chebyshev(coarse_rhs, None, coarse, operator)
    middle_x = chebyshev(middle_rhs, middle_x + prolong(coarse_x, 2, 3), middle, operator)
    return chebyshev(rhs, fine_x + prolong(middle_x, 3, 5), fine, operator)


def spatial(field, level):
    count, tables, lefts, rights, kappa_level, scale = level
    padded = extended(field, (("gx", 1), ("gy", 2)), 1)
    total = kappa_level * field
    total = total + line_part(
        field,
        1,
        count,
        tables[0],
        lefts[0],
        rights[0],
        padded[:, 0, 1:-1, :],
        padded[:, -1, 1:-1, :],
    )
    total = total + line_part(
        field,
        2,
        count,
        tables[1],
        lefts[1],
        rights[1],
        padded[:, 1:-1, 0, :],
        padded[:, 1:-1, -1, :],
    )
    total = total + line_part(
        field, 3, count, tables[2], lefts[2], rights[2], field[:, :, :, -1], field[:, :, :, 0]
    )
    return total


def apply_system(field, level, coupling):
    image = spatial(field, level)
    everyone = lax.all_gather(image, "section", axis=0, tiled=True)
    butcher = jnp.asarray(radau_matrix(), jnp.float32)
    rows = lax.dynamic_slice_in_dim(
        butcher, lax.axis_index("section") * field.shape[0], field.shape[0], 0
    )
    mixed = jnp.einsum("ij,jabc->iabc", rows, everyone, precision=lax.Precision.HIGHEST)
    return field + STEP_SIZE * mixed


def global_total(values):
    return lax.psum(values, ("section", "gx", "gy"))


def stepwise(rhs, guess, kappa, bc_flags):
    levels = [build_level(kappa, bc_flags, count) for count in (5, 3, 2)]
    section_operator = partial(apply_system, coupling=None)
    start_residual = rhs - section_operator(guess, levels[0])
    dofs = float(rhs.size * lax.axis_size("section") * lax.axis_size("gx") * lax.axis_size("gy"))
    beta = jnp.sqrt(global_total(jnp.sum(start_residual * start_residual).reshape(1))[0])
    basis = start_residual / beta
    precond = vcycle(basis, levels, section_operator)
    image = section_operator(precond, levels[0])
    upper = global_total(jnp.sum(image * basis).reshape(1))[0]
    remainder = image - upper * basis
    lower = jnp.sqrt(global_total(jnp.sum(remainder * remainder).reshape(1))[0])
    weight = beta * upper / (upper * upper + lower * lower)
    solution = guess + weight * precond
    residual = start_residual - weight * image
    arnoldi = jnp.stack([beta / math.sqrt(dofs), upper, lower]).astype(jnp.float32)
    return (solution, residual, arnoldi)


EZ = 32
COLS = 16
HALF = 64
FACE_X = HALF + 25
KAPPA = FACE_X + 15
PIECE = KAPPA + 16
LINE_KAPPA = 4 * HALF
LINE_Y = LINE_KAPPA + 4 * 16
LINE = LINE_Y + 104
FIELD = 1000
F32 = jnp.float32


def split_sections():
    matrix = radau_matrix()
    values, vectors = np.linalg.eig(matrix)
    order = [n for n in np.argsort(np.abs(values.imag), kind="stable") if values[n].imag > 0]
    bases = []
    for n in order:
        plane = np.stack([vectors[:, n].real, vectors[:, n].imag], axis=1)
        bases.append(np.linalg.qr(plane)[0])
    left, cross, right = np.linalg.svd(bases[0].T @ bases[1])
    bases = [bases[0] @ left, bases[1] @ right.T]
    for c in range(2):
        sign = np.sign(bases[0][np.argmax(np.abs(bases[0][:, c])), c])
        bases = [np.concatenate([b[:, :c], sign * b[:, c : c + 1], b[:, c + 1 :]], axis=1) for b in bases]
    whole = np.concatenate(bases, axis=1)
    back = np.linalg.inv(whole)
    return whole, back, back @ matrix, back @ matrix @ whole, cross


def iota(shape, dim):
    return lax.broadcasted_iota(jnp.int32, shape, dim)


def exact_dot(a, b):
    return lax.dot_general(
        a, b, (((1,), (0,)), ((), ())), precision=lax.Precision.HIGHEST, preferred_element_type=F32
    )


def split_dot(a, b):
    high = a.astype(jnp.bfloat16)
    rest = a - high.astype(F32)
    middle = rest.astype(jnp.bfloat16)
    low = (rest - middle.astype(F32)).astype(jnp.bfloat16)
    b = b.astype(jnp.bfloat16)
    return sum(
        lax.dot_general(part, b, (((1,), (0,)), ((), ())), preferred_element_type=F32)
        for part in (low, middle, high)
    )


def choose(index, values):
    out = values[-1]
    for place in range(len(values) - 2, -1, -1):
        out = jnp.where(index == place, values[place], out)
    return out


def face_gains(flag, direction, side, count):
    nodes, weights = lobatto(count)
    c, nu = ADVECT[direction], DIFFUSE * count * count
    if side == 0:
        return (c * (1.0 + flag) / 2.0 + nu) * (1.0 / float(weights[0]))
    return (nu - c * (1.0 - flag) / 2.0) * (1.0 / float(weights[-1]))


def row_table():
    kx, ky = (element_matrix(5, d) for d in range(2))
    rows = np.zeros((64, 64))
    for s in range(2):
        for i in range(5):
            for j in range(5):
                r = 2 * (i * 5 + j) + s
                for m in range(5):
                    rows[r, 2 * (m * 5 + j) + s] += kx[i, m]
                    rows[r, 2 * (i * 5 + m) + s] += ky[j, m]
    return rows.astype(np.float32)


def pick_lines(k):
    lane = iota((160, 256), 1)
    return (iota((160, 256), 0) == 5 * (lane % EZ) + k + lane // 128).astype(F32)


def pair_factors(sec, table, own, s):
    upper = iota((32, 128), 1) < 64
    first = jnp.where(upper, float(table[0, s]), float(table[1, s]))
    second = jnp.where(upper, float(table[2, 2 + s]), float(table[3, 2 + s]))
    if not own:
        first = jnp.where(upper, float(table[2, s]), float(table[3, s]))
        second = jnp.where(upper, float(table[0, 2 + s]), float(table[1, 2 + s]))
    return jnp.where(sec == 0, first, second)


def pack_nodes(nodes):
    half = nodes.shape[0] // 2
    odd = iota((half, 128), 1) // EZ % 2 == 1
    return jnp.where(odd, nodes[half:, :], nodes[:half, :])


def local_kernel(
    rhs_in, guess_in, kappa_in, flags_in, rows_in, mine, theirs,
    rhs, guess, kappa, flags, rows_t, sems, stack, lines, nodes, y_faces, x_faces,
):
    sec = lax.axis_index("section")
    pairs = [(guess_in, guess), (rhs_in, rhs), (rows_in, rows_t), (kappa_in, kappa), (flags_in, flags)]
    copies = [pltpu.make_async_copy(source, target, sems.at[n]) for n, (source, target) in enumerate(pairs)]
    for copy in copies:
        copy.start()
    for ref in (stack, nodes, y_faces, x_faces):
        ref[...] = jnp.zeros_like(ref)
    for copy in copies:
        copy.wait()
    for i in range(5):
        stack[192 + 5 * i : 197 + 5 * i, :] = kappa[i]
        for j in range(5):
            r = 2 * (5 * i + j)
            value = guess[i, j]
            stack[128 + r : 130 + r, :] = value
            stack[r : r + 2, :] = rhs[i, j] - value
    stack[64:128, :] = exact_dot(rows_t[...], stack[128:192, :])
    source = stack[...]
    for k in (0, 2, 4):
        shown = split_dot(source, pick_lines(k))
        lines[224 * k : 224 * k + 224, :] = shown[:, :128]
        if k < 4:
            lines[224 * k + 224 : 224 * k + 448, :] = shown[:, 128:]

    def part(k, first, s):
        return lines[pl.ds(224 * k + first + s, 32, stride=2), :]

    def kappa_part(k):
        return lines[224 * k + 192 : 224 * k + 224, :]

    repeat = (iota((EZ, 128), 1) % EZ == iota((EZ, 128), 0)).astype(F32)
    shown = split_dot(flags[:, 0, 0, :].astype(F32), repeat)
    gains = [face_gains(shown[d : d + 1, :], d // 2, d % 2, 5) for d in range(6)]
    row = iota((32, 128), 0)
    none = jnp.zeros((32, 128), F32)
    own = jnp.where(row < 5, gains[0], jnp.where((row >= 20) & (row < 25), gains[1], none))
    own = own + jnp.where(row % 5 == 0, gains[2], jnp.where(row % 5 == 4, gains[3], none))
    kz = element_matrix(5, 2)
    back, back_matrix = split_sections()[1:3]
    fields = [[part(k, 128, s) for k in range(5)] for s in range(2)]
    for k in range(5):
        diagonal = kappa_part(k) + own
        if k == 0:
            diagonal = diagonal + gains[4]
        if k == 4:
            diagonal = diagonal + gains[5]
        images = []
        for s in range(2):
            image = diagonal * fields[s][k] + part(k, 64, s)
            for m in range(5):
                image = image + float(kz[k, m]) * fields[s][m]
            if k == 0:
                image = image - gains[4] * pltpu.roll(fields[s][4], 1, 1)
            if k == 4:
                image = image - gains[5] * pltpu.roll(fields[s][0], 127, 1)
            images.append(image)
        for p, mark in enumerate((True, False)):
            total = jnp.zeros((32, 128), F32)
            trace = jnp.zeros((32, 128), F32)
            for s in range(2):
                total = total + pair_factors(sec, back, mark, s) * part(k, 0, s)
                factor = pair_factors(sec, STEP_SIZE * back_matrix, mark, s)
                total = total - factor * images[s]
                trace = trace + factor * fields[s][k]
            nodes[128 * p + 25 * k : 128 * p + 25 * k + 25, :] = total[:25]
            for i in range(5):
                for f in range(2):
                    r = 64 * p + 32 * f + 5 * k + i
                    y_faces[r : r + 1, :] = trace[5 * i + 4 * f : 5 * i + 4 * f + 1]
            for f in range(2):
                r = 32 * p + 16 * f + 3 * k
                x_faces[r : r + 3, :] = trace[20 * f + 1 : 20 * f + 4]
    upper = iota((1, 128), 1) < 64
    for r in range(3):
        nodes[125 + r : 126 + r, :] = jnp.where(upper, shown[2 * r : 2 * r + 1], shown[2 * r + 1 : 2 * r + 2])
    for p, out in enumerate((mine, theirs)):
        out[:HALF, :] = pack_nodes(nodes[128 * p : 128 * p + 128, :])
        out[HALF:FACE_X, :] = pack_nodes(y_faces[64 * p : 64 * p + 64, :])[:25]
        out[FACE_X:KAPPA, :] = pack_nodes(x_faces[32 * p : 32 * p + 32, :])[:15]
    for k in range(5):
        nodes[25 * k : 25 * k + 25, :] = kappa_part(k)[:25]
    kappas = choose(iota((32, 128), 1) // EZ, [nodes[32 * q : 32 * q + 32, :] for q in range(4)])
    mine[KAPPA:, :] = jnp.where(sec == 0, kappas[:16], kappas[16:])


def part_kernel(source, piece, kappa):
    piece[...] = source[:KAPPA, :]
    kappa[...] = source[KAPPA:, :]


VMEM = pl.BlockSpec(memory_space=pltpu.VMEM)
HBM = pl.BlockSpec(memory_space=pltpu.HBM)


def limit(mib):
    return pltpu.CompilerParams(vmem_limit_bytes=mib * 2**20)


def local_part(rhs, guess, kappa, flags):
    operands = (rhs, guess, kappa, flags, jnp.asarray(row_table()))
    return pl.pallas_call(
        local_kernel,
        out_shape=[jax.ShapeDtypeStruct((rows, 128), F32) for rows in (PIECE, KAPPA)],
        in_specs=[HBM] * 5,
        out_specs=[VMEM] * 2,
        scratch_shapes=[pltpu.VMEM(o.shape, o.dtype) for o in operands]
        + [
            pltpu.SemaphoreType.DMA((5,)),
            pltpu.VMEM((224, 160), F32),
            pltpu.VMEM((5 * 224, 128), F32),
            pltpu.VMEM((256, 128), F32),
            pltpu.VMEM((128, 128), F32),
            pltpu.VMEM((64, 128), F32),
        ],
        compiler_params=limit(60),
        cost_estimate=pl.CostEstimate(flops=20_000_000, bytes_accessed=8_000_000, transcendentals=0),
        name="local_part",
    )(*operands)


def part(x):
    return pl.pallas_call(
        part_kernel,
        out_shape=[jax.ShapeDtypeStruct((rows, 128), F32) for rows in (KAPPA, 16)],
        in_specs=[VMEM],
        out_specs=[VMEM] * 2,
        compiler_params=limit(16),
        name="part",
    )(x)


class Level:
    def __init__(self, count, refs):
        self.count = count
        self.x, self.dir, self.res, self.f = refs
        self.tables = [element_matrix(count, d) for d in range(3)]
        self.gains = self.diag = self.jac = None


def tile(index):
    return pl.ds(index * 8, 8)


def rows_of(pieces, size, r, h):
    return pieces[pl.ds(8 * h * size + r, 8, stride=size), :]


ORDER_X = ((2, 3), (3, 2), (1, 1))
ORDER_Y = ((3, 3), (1, 2), (2, 1))


def partner(bits):
    return jnp.where(lax.axis_index("section") == 0, bits[0], bits[1])


def place_pieces(blocks, pieces, first, size, room):
    my_gx, my_gy = lax.axis_index("gx"), lax.axis_index("gy")
    for b, block in enumerate(blocks):
        gy = my_gy ^ partner(ORDER_Y[b - 1]) if b else my_gy
        for a in range(4):
            column = (my_gx ^ a) * 4 + gy
            start = pl.multiple_of(column * room, 8)
            pieces[pl.ds(start, size), :] = block[first + a * size : first + a * size + size, :]


class Lanes:
    def __init__(self):
        self.lane = iota((8, 128), 1)
        sub = iota((8, 128), 0)
        self.group = self.lane // EZ
        self.odd = self.group % 2 == 1
        self.element = self.lane % EZ
        self.place = sub % 4
        self.low_half = sub < 4

    def around(self, u):
        turned = pltpu.roll(u, 4, u.ndim - 2)
        far = jnp.where(self.odd, pltpu.roll(turned, 32, u.ndim - 1), pltpu.roll(turned, 96, u.ndim - 1))
        return turned, far

    def x_before(self, u):
        turned, far = self.around(u)
        return jnp.where(self.low_half, far, turned)

    def x_after(self, u):
        turned, far = self.around(u)
        return jnp.where(self.low_half, turned, far)

    def y_before(self, u):
        return jnp.where(self.place == 0, pltpu.roll(u, 5, 0), pltpu.roll(u, 1, 0))

    def y_after(self, u):
        return jnp.where(self.place == 3, pltpu.roll(u, 3, 0), pltpu.roll(u, 7, 0))

    def z_before(self, u):
        return jnp.where(self.element == 0, pltpu.roll(u, 97, u.ndim - 1), pltpu.roll(u, 1, u.ndim - 1))

    def z_after(self, u):
        last = self.element == EZ - 1
        return jnp.where(last, pltpu.roll(u, 31, u.ndim - 1), pltpu.roll(u, 127, u.ndim - 1))


def load(ref, first, count):
    return ref[pl.ds(first * 8, count * 8), :].reshape(count, 8, 128)


def store(ref, first, value):
    ref[pl.ds(first * 8, value.shape[0] * 8), :] = value.reshape(value.shape[0] * 8, 128)


DIAGS = (0, 250, 304)
GAINS = (320, 326, 332)
REGISTERS = 338
CENTRE = (CHEB_HIGH + CHEB_LOW) / 2.0
RADIUS = (CHEB_HIGH - CHEB_LOW) / 2.0


def flag_lanes(row, slot):
    turned = [row] + [pltpu.roll(row, 32 * m, 1) for m in range(1, 4)]
    return choose(iota(row.shape, 1) // EZ, [turned[(g - 2 * slot - 1) % 4] for g in range(4)])


def line_kernel(first, second, third, own, line, faces, sorted_pieces):
    sorted_pieces[:PIECE, :] = own[...]
    for bits, piece in zip(ORDER_X, (first, second, third)):
        sorted_pieces[pl.ds(pl.multiple_of(partner(bits) * PIECE, 8), PIECE), :] = piece[...]
    pieces = [sorted_pieces.at[PIECE * a : PIECE * a + PIECE, :] for a in range(4)]
    even = lax.axis_index("gx") % 2 == 0
    odd = iota((8, 128), 1) // EZ % 2 == 1
    faces[...] = jnp.zeros_like(faces)

    def both(rows, f):
        side = odd[:1] if f else jnp.logical_not(odd[:1])
        return jnp.where(side, rows, pltpu.roll(rows, 96 if f else 32, 1))

    for a, piece in enumerate(pieces):
        for f in range(2):
            base = 64 * a + 32 * f
            inner = both(piece[FACE_X:KAPPA, :], f)
            ends = [both(piece[HALF:FACE_X, :], g) for g in range(2)]
            for k in range(5):
                r = base + 5 * k
                node = 5 * k + 4 * f
                faces[r : r + 1, :] = ends[0][node : node + 1]
                faces[r + 1 : r + 4, :] = inner[3 * k : 3 * k + 3]
                faces[r + 4 : r + 5, :] = ends[1][node : node + 1]
    for a, piece in enumerate(pieces):
        line[HALF * a : HALF * a + HALF, :] = piece[:HALF, :]
        line[LINE_KAPPA + 16 * a : LINE_KAPPA + 16 * a + 16, :] = piece[KAPPA:, :]
        line[LINE_Y + 25 * a : LINE_Y + 25 * a + 25, :] = piece[HALF:FACE_X, :]
        flags = [flag_lanes(piece[61:62, :], slot) for slot in range(2)]
        gains = [face_gains(flags[d], 0, d, 5) for d in range(2)]
        next_first = even if a % 2 == 0 else jnp.logical_not(even)
        for f in range(2):
            one = faces[64 * (a ^ 1) + 32 * (1 - f) : 64 * (a ^ 1) + 32 * (1 - f) + 32, :]
            three = faces[64 * (a ^ 3) + 32 * (1 - f) : 64 * (a ^ 3) + 32 * (1 - f) + 32, :]
            near = jnp.where(next_first, one, three) if f else jnp.where(next_first, three, one)
            term = gains[f] * near
            for k in range(5):
                node = 25 * k + 20 * f
                side = odd[:5] if node >= HALF else jnp.logical_not(odd[:5])
                r = HALF * a + node % HALF
                line[r : r + 5, :] = line[r : r + 5, :] + jnp.where(side, term[5 * k : 5 * k + 5], 0.0)
    line[LINE_Y + 100 :, :] = jnp.zeros((4, 128), F32)


def halves_kernel(block0, block1, block2, block3, out):
    place_pieces((block0, block1, block2, block3), out, LINE_KAPPA, 16, 16)


def widen(low, high, odd):
    return jnp.where(odd, pltpu.roll(high, 32, 1), low), jnp.where(odd, high, pltpu.roll(low, 96, 1))


def assemble_kernel(block0, block1, block2, block3, field, pieces, edges, traces):
    blocks = (block0, block1, block2, block3)
    place_pieces(blocks, pieces, 0, HALF, HALF)
    place_pieces(blocks, edges, LINE_Y, 25, 32)
    lanes = Lanes()
    for source, size, rows, target, apart in ((edges, 32, 25, traces, 25), (pieces, HALF, HALF, field, HALF)):
        for r in range(rows):
            first, second = widen(rows_of(source, size, r, 0), rows_of(source, size, r, 1), lanes.odd)
            target[tile(r), :] = first
            target[tile(apart + r), :] = second
    got = field[tile(126), :]
    across = pltpu.roll(got, 64, 1)
    gains = [
        face_gains(jnp.where(lanes.lane < 64, got, across), 1, 0, 5),
        face_gains(jnp.where(lanes.lane < 64, across, got), 1, 1, 5),
    ]
    for k in range(5):
        for i in range(5):
            lower, upper = traces[tile(5 * k + i), :], traces[tile(25 + 5 * k + i), :]
            node = 25 * k + 5 * i
            field[tile(node), :] = field[tile(node), :] + gains[0] * lanes.y_before(upper)
            field[tile(node + 4), :] = field[tile(node + 4), :] + gains[1] * lanes.y_after(lower)


def setup_kernel(field, own_halves, other_halves, coefs, kap):
    sec = lax.axis_index("section")
    lanes = Lanes()
    group, lane = lanes.group, lanes.lane
    flags = []
    for r in range(3):
        got = field[tile(125 + r), :]
        across = pltpu.roll(got, 64, 1)
        flags += [jnp.where(lane < 64, got, across), jnp.where(lane < 64, across, got)]
    for r in range(16):
        pairs = [[rows_of(ref, 16, r, h) for h in range(2)] for ref in (own_halves, other_halves)]
        for half in range(2):
            turned = []
            for h in range(2):
                got = jnp.where(sec == half, pairs[0][h], pairs[1][h])
                turned.append([pltpu.roll(got, 32 * m, 1) if m else got for m in range(4)])
            for q in range(4):
                value = choose(group, [turned[g % 2][(g - q) % 4] for g in range(4)])
                kap[tile(q * 32 + half * 16 + r), :] = value
    for p, n in enumerate((5, 3, 2)):
        stride = 4 // (n - 1)
        gains = [face_gains(flags[d], d // 2, d % 2, n) for d in range(6)]
        rows = []
        for d in range(3):
            coefs[tile(GAINS[p] + 2 * d), :] = gains[2 * d]
            coefs[tile(GAINS[p] + 2 * d + 1), :] = gains[2 * d + 1]
            table = element_matrix(n, d)
            row = [jnp.full((8, 128), float(table[m, m]), F32) for m in range(n)]
            row[0] = row[0] + gains[2 * d]
            row[n - 1] = row[n - 1] + gains[2 * d + 1]
            rows.append(row)
        along = jnp.stack(rows[1])
        for k in range(n):
            for i in range(n):
                line = load(kap, k * 25 * stride + i * stride * 5, 5)
                line = jnp.stack([line[j * stride] for j in range(n)])
                value = line + (along + (rows[2][k] + rows[0][i]))
                scale = 1.0 / (1.0 + STEP_SIZE * JACOBI_SCALE * value)
                store(coefs, DIAGS[p] + (k * n + i) * n, value)
                store(coefs, DIAGS[p] + n**3 + (k * n + i) * n, scale * (1.0 / CENTRE))


def cycle_kernel(coefs, assembled, fields, more, *scratch):
    sec = lax.axis_index("section")
    my_gx, my_gy = lax.axis_index("gx"), lax.axis_index("gy")
    levels = [Level(n, scratch[4 * p : 4 * p + 4]) for p, n in enumerate((5, 3, 2))]
    half = scratch[12]
    lanes = Lanes()
    lane = lanes.lane
    blocks = split_sections()[3]

    def lanes_of(upper, lower):
        return jnp.where(lane < 64, jnp.where(sec == 0, upper[0], upper[1]), jnp.where(sec == 0, lower[0], lower[1]))

    entry = [[[float(STEP_SIZE * blocks[2 * p + a, 2 * p + b]) for p in range(2)] for b in range(2)] for a in range(2)]
    same = lanes_of(entry[0][0], entry[1][1])
    swap = lanes_of(entry[0][1], entry[1][0])
    first_rho = RADIUS / CENTRE
    second_rho = 1.0 / (2.0 * CENTRE / RADIUS - first_rho)
    keep = 1.0 + second_rho * first_rho
    push = 2.0 * second_rho / RADIUS * CENTRE
    for p, level in enumerate(levels):
        size = level.count**3
        level.gains = [-coefs[tile(GAINS[p] + d), :] for d in range(6)]
        level.diag = lambda first, count, p=p: load(coefs, DIAGS[p] + first, count)
        level.jac = lambda first, count, p=p, size=size: load(coefs, DIAGS[p] + size + first, count)

    def begin(level, source):
        n = level.count
        for first in range(0, n**3, n):
            f = load(source, first, n)
            store(level.dir, first, level.jac(first, n) * f)
            store(level.res, first, f)
            store(level.x, first, jnp.zeros_like(f))

    def apply(level, smooth):
        n = level.count
        kx, ky, kz = level.tables
        gains = level.gains
        source = level.dir if smooth else level.x
        def tree(terms):
            while len(terms) > 1:
                pairs = [a + b for a, b in zip(terms[::2], terms[1::2])]
                terms = pairs + terms[len(terms) // 2 * 2 :]
            return terms[0]

        def sums(k):
            def line_at(i):
                return load(source, (k * n + i) * n, n)

            x_left = gains[0] * lanes.x_before(line_at(n - 1))
            x_right = gains[1] * lanes.x_after(line_at(0))
            z_low, z_high, y_low, y_high = [], [], [], []
            for i in range(n):
                if k == 0:
                    z_low.append(gains[4] * lanes.z_before(load(source, ((n - 1) * n + i) * n, n)))
                if k == n - 1:
                    z_high.append(gains[5] * lanes.z_after(load(source, i * n, n)))
                v = line_at(i)
                y_low.append(gains[2] * lanes.y_before(v[n - 1]))
                y_high.append(gains[3] * lanes.y_after(v[0]))
            totals = []
            for i in range(n):
                first = (k * n + i) * n
                v = line_at(i)
                along_x = [float(kx[i, m]) * line_at(m) for m in range(n) if m != i]
                along_z = [float(kz[k, m]) * load(source, (m * n + i) * n, n) for m in range(n) if m != k]
                along_y = []
                for j in range(n):
                    terms = [float(ky[j, m]) * v[m] for m in range(n) if m != j]
                    if j == 0:
                        terms.append(y_low[i])
                    if j == n - 1:
                        terms.append(y_high[i])
                    along_y.append(tree(terms))
                if i == 0:
                    along_x.append(x_left)
                if i == n - 1:
                    along_x.append(x_right)
                if k == 0:
                    along_z.append(z_low[i])
                if k == n - 1:
                    along_z.append(z_high[i])
                totals.append(tree([level.diag(first, n) * v, tree(along_x), tree(along_z), jnp.stack(along_y)]))
            return totals

        def update(k, totals):
            moved = [pltpu.roll(total, 64, 2) for total in totals]
            for i in range(n):
                first = (k * n + i) * n
                v = load(source, first, n)
                image = v + (same * totals[i] + swap * moved[i])
                if smooth:
                    scaled = level.jac(first, n) * (load(level.res, first, n) - image)
                    store(level.x, first, (load(level.x, first, n) + keep * v) + push * scaled)
                else:
                    rest = load(level.f, first, n) - image
                    store(level.res, first, rest)
                    store(level.dir, first, level.jac(first, n) * rest)

        if n == 5:
            ready = sums(0)
            for k in range(n):
                following = sums(k + 1) if k + 1 < n else None
                update(k, ready)
                ready = following
        else:
            for k, totals in enumerate([sums(k) for k in range(n)]):
                update(k, totals)

    def combine(weights, parts):
        total = None
        for weight, part in zip(weights, parts):
            if abs(weight) > 1e-14:
                term = part if abs(weight - 1.0) < 1e-14 else float(weight) * part
                total = term if total is None else total + term
        return total

    def change(table, source, target, add):
        m, n = table.shape
        for i in range(n):
            parts = [load(source, i * n + k * n * n, n) for k in range(n)]
            for k in range(m):
                store(half, i * n + k * n * n, combine(table[k], parts))
        for k in range(m):
            parts = [load(half, k * n * n + i * n, n) for i in range(n)]
            for i in range(m):
                line = combine(table[i], parts)
                value = jnp.stack([combine(table[j], [line[a] for a in range(n)]) for j in range(m)])
                first = k * m * m + i * m
                store(target, first, load(target, first, m) + value if add else value)

    def down(n, m):
        fine_nodes, fine_weights = lobatto(n)
        coarse_nodes, coarse_weights = lobatto(m)
        table = lagrange_table(coarse_nodes, fine_nodes)
        return (1.0 / coarse_weights)[:, None] * table.T * fine_weights[None, :]

    def up(m, n):
        return lagrange_table(lobatto(m)[0], lobatto(n)[0])

    def solve(p):
        level = levels[p]
        if p == 2:
            apply(level, True)
            return
        below = levels[p + 1]

        def correct():
            n, m = level.count, below.count
            change(down(n, m), level.res, below.f, False)
            begin(below, below.f)
            solve(p + 1)
            change(up(m, n), below.x, level.x, True)

        if p == 1:
            apply(level, True)
            apply(level, False)
            correct()
            apply(level, False)
            apply(level, True)
            return

        def step(t, carry):
            @pl.when(t != 1)
            def _():
                apply(level, True)

            apply(level, False)

            @pl.when(t == 0)
            def _():
                correct()
            return carry
        lax.fori_loop(0, 3, step, 0)

    fine = levels[0]
    fine.f = assembled
    begin(fine, assembled)
    solve(0)

    for first in range(0, 125, 5):
        part, place = (fields, first) if first < SPLIT else (more, first - SPLIT)
        store(part, place, load(fine.res, first, 5))
    column = (my_gx % 2) * 4 + my_gy
    more[AFTER : AFTER + 125, :] = fine.x[pl.ds(column, 125, stride=8), :]
    more[AFTER + 125 :, :] = jnp.zeros((3, 128), F32)


SPLIT = 75
AFTER = 8 * (125 - SPLIT)


def register(parts, r):
    return parts[0][tile(r), :] if r < SPLIT else parts[1][tile(r - SPLIT), :]


def column_of(parts, k):
    first = 3 * (k // 3)
    return parts[k // 3][column_rows(k - first), :]


def column_z(parts, k):
    return parts[1][AFTER + 25 * k : AFTER + 25 * k + 25, :]


def pair_weights():
    cross = split_sections()[4]
    return jnp.where(iota((8, 128), 1) < 64, float(cross[0]), float(cross[1]))


def column_factors(p):
    sec = lax.axis_index("section")
    whole = split_sections()[0]
    lane = iota((25, 128), 1)
    here = lane // EZ % 2 == lax.axis_index("gx") // 2
    factors = []
    for s in range(2):
        parts = []
        for mine in range(2):
            t = whole[2 * mine + s]
            q = mine if p == 0 else 1 - mine
            parts.append(jnp.where(lane < 64, float(t[2 * q]), float(t[2 * q + 1])))
        factors.append(jnp.where(here, jnp.where(sec == 0, parts[0], parts[1]), 0.0))
    return factors


def column_rows(k):
    column = (lax.axis_index("gx") % 2) * 4 + lax.axis_index("gy")
    return pl.ds(k * 200 + column, 25, stride=8)


def raw_order(k):
    lane = iota((256, 160), 0)
    return (iota((256, 160), 1) == 5 * (lane % EZ) + k + lane // 128).astype(F32)


def side_by_side(cols):
    half = cols.shape[0] // 2
    return jnp.concatenate([cols[:half, :], cols[half:, :]], axis=1)


def early_kernel(own0, own1, own_start, other_start, sums, column_out, cols):
    own = (own0, own1)
    weights = pair_weights()
    cols[...] = jnp.zeros_like(cols)
    total = jnp.zeros((192, 160), F32)
    own_factors, other_factors = column_factors(0), column_factors(1)
    for k in range(5):
        where = column_rows(k)
        z = column_z(own, k)
        start, other = own_start[where, :], other_start[where, :]
        w = start - column_of(own, k)
        side = 192 * (k % 2)
        for s in range(2):
            cols[pl.ds(side + s, 25, stride=2), :] = own_factors[s] * z
            cols[pl.ds(side + 64 + s, 25, stride=2), :] = own_factors[s] * start + other_factors[s] * other
            cols[pl.ds(side + 128 + s, 25, stride=2), :] = own_factors[s] * w
        if k % 2 == 1:
            total = total + split_dot(side_by_side(cols), raw_order(k - 1))
    cols[192:, :] = jnp.zeros((192, 128), F32)
    total = total + split_dot(side_by_side(cols), raw_order(4))
    column_out[...] = total
    nothing = jnp.zeros((8, 128), F32)
    uppers, sizes = [nothing] * 5, [nothing] * 5
    for r in range(125):
        c, d = own_start[tile(r), :], other_start[tile(r), :]
        a = c - register(own, r)
        uppers[r % 5] = uppers[r % 5] + a * (c + weights * d)
        sizes[r % 5] = sizes[r % 5] + ((c * c + d * d) + 2.0 * (weights * (c * d)))
    sums[0:8, :] = sum(uppers)
    sums[8:16, :] = jnp.broadcast_to(jnp.sum(sum(sizes), keepdims=True), (8, 128))


def finish_kernel(own0, own1, other0, other1, own_start, other_start, sums, column, guess, sol, res_out, arnoldi, cols, outs):
    own, other = (own0, own1), (other0, other1)
    cols[...] = jnp.zeros_like(cols)
    total = jnp.zeros((128, 160), F32)
    factors = column_factors(1)
    for k in range(5):
        where = column_rows(k)
        z = column_z(other, k)
        w = other_start[where, :] - column_of(other, k)
        side = 128 * (k % 2)
        for s in range(2):
            cols[pl.ds(side + s, 25, stride=2), :] = factors[s] * z
            cols[pl.ds(side + 64 + s, 25, stride=2), :] = factors[s] * w
        if k % 2 == 1:
            total = total + split_dot(side_by_side(cols), raw_order(k - 1))
    cols[128:, :] = jnp.zeros((128, 128), F32)
    total = total + split_dot(side_by_side(cols), raw_order(4))
    weights = pair_weights()
    nothing = jnp.zeros((8, 128), F32)
    uppers = [nothing] * 5
    for r in range(125):
        c, d = own_start[tile(r), :], other_start[tile(r), :]
        b = d - register(other, r)
        uppers[r % 5] = uppers[r % 5] + b * (d + weights * c)

    mine, theirs = sums[0:8, :], sum(uppers)
    size = sums[8:9, 0:1]
    upper = jnp.sum(mine + theirs, keepdims=True) / size
    rests = [nothing] * 5
    for r in range(125):
        c, d = own_start[tile(r), :], other_start[tile(r), :]
        a = (c - register(own, r)) - upper * c
        b = (d - register(other, r)) - upper * d
        rests[r % 5] = rests[r % 5] + ((a * a + b * b) + 2.0 * (weights * (a * b)))
    rest = jnp.sum(sum(rests), keepdims=True)
    beta = jnp.sqrt(size)
    lower = jnp.sqrt(rest) / beta
    weight = upper / (upper * upper + lower * lower)
    entries = float(125 * EZ * COLS * 4)
    for place_out, value in enumerate((beta * (1.0 / math.sqrt(entries)), upper, lower)):
        arnoldi[place_out] = value[0, 0]
    outs[:64, :] = weight * (column[:64, :] + total[:64])
    outs[64:, :] = column[64:128, :] - weight * (column[128:, :] + total[64:])
    for i in range(5):
        for j in range(5):
            r = 2 * (5 * i + j)
            sol[i, j] = guess[i, j] + outs[r : r + 2, :]
            res_out[i, j] = outs[64 + r : 66 + r, :]


def plain_call(kernel, name, rows, scratch, operands, cost=1_000_000):
    return pl.pallas_call(
        kernel,
        out_shape=jax.ShapeDtypeStruct((rows, 128), F32),
        in_specs=[VMEM] * len(operands),
        out_specs=VMEM,
        scratch_shapes=[pltpu.VMEM((r, 128), F32) for r in scratch],
        compiler_params=limit(16),
        cost_estimate=pl.CostEstimate(flops=cost, bytes_accessed=cost, transcendentals=0),
        name=name,
    )(*operands)


def cycle(coefs, assembled):
    scratch = []
    for n in (5, 3, 2):
        scratch += [pltpu.VMEM((n**3 * 8, 128), F32)] * 4
    scratch += [pltpu.VMEM((FIELD, 128), F32)]
    return pl.pallas_call(
        cycle_kernel,
        out_shape=[jax.ShapeDtypeStruct((rows, 128), F32) for rows in (SPLIT * 8, AFTER + 128)],
        in_specs=[VMEM] * 2,
        out_specs=[VMEM] * 2,
        scratch_shapes=scratch,
        compiler_params=limit(24),
        cost_estimate=pl.CostEstimate(flops=40_000_000, bytes_accessed=30_000_000, transcendentals=0),
        name="cycle",
    )(coefs, assembled)


def early(own, own_start, other_start):
    return pl.pallas_call(
        early_kernel,
        out_shape=[jax.ShapeDtypeStruct((16, 128), F32), jax.ShapeDtypeStruct((192, 160), F32)],
        in_specs=[VMEM] * 4,
        out_specs=[VMEM] * 2,
        scratch_shapes=[pltpu.VMEM((384, 128), F32)],
        compiler_params=limit(16),
        cost_estimate=pl.CostEstimate(flops=4_000_000, bytes_accessed=4_000_000, transcendentals=0),
        name="early",
    )(*own, own_start, other_start)


def finish(own, other, own_start, other_start, sums, column, guess):
    return pl.pallas_call(
        finish_kernel,
        out_shape=[
            jax.ShapeDtypeStruct(guess.shape, F32),
            jax.ShapeDtypeStruct(guess.shape, F32),
            jax.ShapeDtypeStruct((3,), F32),
        ],
        in_specs=[VMEM] * 9,
        out_specs=[VMEM, VMEM, pl.BlockSpec(memory_space=pltpu.SMEM)],
        scratch_shapes=[pltpu.VMEM((256, 128), F32), pltpu.VMEM((128, 160), F32)],
        compiler_params=limit(24),
        name="finish",
    )(*own, *other, own_start, other_start, sums, column, guess)


def exchange(x, axis, bits):
    return lax.ppermute(x, axis, [(n, n ^ bits) for n in range(lax.axis_size(axis))])


def exchange_by_core(x, axis, bits):
    count = lax.axis_size(axis)
    pairs = [(s * count + n, s * count + (n ^ bits[s])) for s in range(2) for n in range(count)]
    return lax.ppermute(x, ("section", axis), pairs)


def gathered_body(rhs, guess, kappa, bc_flags):
    rhs, guess = (jnp.transpose(v, (1, 2, 0, 3)) for v in (rhs, guess))
    mine, theirs = local_part(rhs, guess, kappa, bc_flags)
    got, mine, kappa_piece = lax.optimization_barrier((exchange(theirs, "section", 1), *part(mine)))
    piece = jnp.concatenate([mine + got, kappa_piece])
    pieces = [exchange_by_core(piece, "gx", bits) for bits in ORDER_X] + [piece]
    line = plain_call(line_kernel, "line", LINE, [4 * 64, 4 * PIECE], pieces)
    blocks = [line] + [exchange_by_core(line, "gy", bits) for bits in ORDER_Y]
    halves = plain_call(halves_kernel, "halves", COLS * 16, [], blocks)
    other_halves = exchange(halves, "section", 1)
    start = plain_call(assemble_kernel, "assemble", 128 * 8, [COLS * HALF, COLS * 32, 50 * 8], blocks, 4_000_000)
    start, other_halves = lax.optimization_barrier((start, other_halves))
    coefs = plain_call(setup_kernel, "setup", REGISTERS * 8, [128 * 8], (start, halves, other_halves))
    other_start = exchange(start, "section", 1)
    own, other_start = lax.optimization_barrier((cycle(coefs, start), other_start))
    other = [exchange(part, "section", 1) for part in own]
    sums, column = early(own, start, other_start)
    sol, res, arnoldi = finish(own, other, start, other_start, sums, column, guess)
    sol, res = (jnp.transpose(v, (2, 0, 1, 3)) for v in (sol, res))
    return sol, res, arnoldi


def solution(mesh):
    placed = (
        P("section", "gx", "gy", None),
        P("section", "gx", "gy", None),
        P("gx", "gy", None),
        P(None, "gx", "gy", None),
    )
    sizes = (mesh.shape["section"], mesh.shape["gx"], mesh.shape["gy"])

    def step(rhs, guess, kappa, bc_flags):
        fits = sizes == (2, 4, 4) and rhs.shape == (4, 20, 20, 160)
        return jax.shard_map(
            gathered_body if fits else stepwise,
            mesh=mesh,
            in_specs=placed,
            out_specs=(P("section", "gx", "gy", None), P("section", "gx", "gy", None), P()),
            check_vma=False,
        )(rhs, guess, kappa, bc_flags)

    return step
```

```python
from functools import partial
import math

import jax
import jax.numpy as jnp
import numpy as np
from jax import lax
from jax.experimental import pallas as pl
from jax.experimental.pallas import tpu as pltpu
from jax.sharding import PartitionSpec as P

ADVECT = (1.0, 0.7, 0.5)
DIFFUSE = 0.05
STEP_SIZE = 0.2
JACOBI_SCALE = 0.25
CHEB_LOW = 0.25
CHEB_HIGH = 2.0
LETTERS = "abcdef"


def extended(x, sides, width):
    for axis, dim in sides:
        peers, length = (lax.axis_size(axis), x.shape[dim])
        up = [(i, (i + 1) % peers) for i in range(peers)]
        down = [(j, i) for i, j in up]
        last = lax.slice_in_dim(x, length - width, length, axis=dim)
        leading = lax.slice_in_dim(x, 0, width, axis=dim)
        before = lax.ppermute(last, axis, up)
        after = lax.ppermute(leading, axis, down)
        x = jnp.concatenate([before, x, after], axis=dim)
    return x


def lobatto(count):
    if count == 5:
        inner = math.sqrt(3.0 / 7.0)
        return (
            np.array([-1.0, -inner, 0.0, inner, 1.0]),
            np.array([0.1, 49.0 / 90.0, 32.0 / 45.0, 49.0 / 90.0, 0.1]),
        )
    if count == 3:
        return (np.array([-1.0, 0.0, 1.0]), np.array([1.0 / 3.0, 4.0 / 3.0, 1.0 / 3.0]))
    return (np.array([-1.0, 1.0]), np.array([1.0, 1.0]))


def lagrange_table(nodes, points):
    table = np.ones((len(points), len(nodes)))
    for column in range(len(nodes)):
        for other in range(len(nodes)):
            if other != column:
                table[:, column] *= (points - nodes[other]) / (nodes[column] - nodes[other])
    return table


def slope_table(nodes):
    total = len(nodes)
    factor = np.array(
        [np.prod([nodes[i] - nodes[k] for k in range(total) if k != i]) for i in range(total)]
    )
    table = np.zeros((total, total))
    for row in range(total):
        for column in range(total):
            if row != column:
                table[row, column] = factor[row] / factor[column] / (nodes[row] - nodes[column])
        table[row, row] = -np.sum(table[row])
    return table


def element_matrix(count, direction):
    nodes, weights = lobatto(count)
    slopes = slope_table(nodes)
    stiffness = (1.0 / weights)[:, None] * (slopes.T @ (weights[:, None] * slopes))
    return ADVECT[direction] * slopes + DIFFUSE * stiffness


def legendre_pair(point, order):
    values = [1.0, point]
    slopes = [0.0, 1.0]
    for index in range(1, order):
        values.append(
            ((2 * index + 1) * point * values[index] - index * values[index - 1]) / (index + 1)
        )
        slopes.append(slopes[index - 1] + (2 * index + 1) * values[index])
    return (values, slopes)


def radau_nodes():
    starts = [0.0885879595127039, 0.4094668644407347, 0.7876594617608471]
    found = []
    for start in starts:
        point = start
        for sweep in range(30):
            values, slopes = legendre_pair(2.0 * point - 1.0, 4)
            change = (values[4] - values[3]) / (2.0 * (slopes[4] - slopes[3]))
            point = point - change
        found.append(point)
    found.append(1.0)
    return found


def poly_times(coefs, root):
    result = [0.0] * (len(coefs) + 1)
    for index in range(len(coefs)):
        result[index + 1] += coefs[index]
        result[index] -= root * coefs[index]
    return result


def radau_matrix():
    order = 4
    nodes = radau_nodes()
    matrix = np.zeros((order, order))
    for column in range(order):
        coefs = [1.0]
        denominator = 1.0
        for other in range(order):
            if other != column:
                coefs = poly_times(coefs, nodes[other])
                denominator *= nodes[column] - nodes[other]
        for row in range(order):
            upper_end = nodes[row]
            integral = 0.0
            for index in range(len(coefs)):
                integral += coefs[index] * upper_end ** (index + 1) / (index + 1)
            matrix[row, column] = integral / denominator
    return matrix


def node_einsum(table, field, axis):
    labels = LETTERS[: field.ndim]
    source = labels[: axis + 1] + "j" + labels[axis + 2 :]
    target = labels[: axis + 1] + "i" + labels[axis + 2 :]
    return jnp.einsum(
        "ij," + source + "->" + target,
        jnp.asarray(table, jnp.float32),
        field,
        precision=lax.Precision.HIGHEST,
    )


def apply_along(field, axis, count, table):
    shape = field.shape
    split = shape[:axis] + (shape[axis] // count, count) + shape[axis + 1 :]
    mapped = node_einsum(table, field.reshape(split), axis)
    return mapped.reshape(
        shape[:axis] + (mapped.shape[axis] * mapped.shape[axis + 1],) + shape[axis + 1 :]
    )


def line_part(field, axis, count, table, left_gain, right_gain, left_edge, right_edge):
    shape = field.shape
    elements = shape[axis] // count
    split = field.reshape(shape[:axis] + (elements, count) + shape[axis + 1 :])
    linear = node_einsum(table, split, axis)
    first = lax.index_in_dim(split, 0, axis + 1, keepdims=False)
    last = lax.index_in_dim(split, count - 1, axis + 1, keepdims=False)
    before = jnp.concatenate(
        [jnp.expand_dims(left_edge, axis), lax.slice_in_dim(last, 0, elements - 1, axis=axis)], axis
    )
    after = jnp.concatenate(
        [lax.slice_in_dim(first, 1, elements, axis=axis), jnp.expand_dims(right_edge, axis)], axis
    )
    front = jnp.expand_dims(left_gain * (first - before), axis + 1)
    back = jnp.expand_dims(right_gain * (last - after), axis + 1)
    if count > 2:
        middle_shape = list(front.shape)
        middle_shape[axis + 1] = count - 2
        pieces = [front, jnp.zeros(middle_shape, jnp.float32), back]
    else:
        pieces = [front, back]
    return (linear + jnp.concatenate(pieces, axis + 1)).reshape(shape)


def diag_along(shape, axis, count, table, left_gain, right_gain):
    elements = shape[axis] // count
    split = shape[:axis] + (elements, count) + shape[axis + 1 :]
    profile = [1] * len(split)
    profile[axis + 1] = count
    diagonal_entries = np.array([table[index, index] for index in range(count)])
    base = jnp.broadcast_to(jnp.asarray(diagonal_entries, jnp.float32).reshape(profile), split)
    front = jnp.expand_dims(left_gain, axis + 1)
    back = jnp.expand_dims(right_gain, axis + 1)
    if count > 2:
        middle_shape = list(front.shape)
        middle_shape[axis + 1] = count - 2
        pieces = [front, jnp.zeros(middle_shape, jnp.float32), back]
    else:
        pieces = [front, back]
    return (base + jnp.concatenate(pieces, axis + 1)).reshape(shape)


def level_kappa(kappa, count):
    if count == 5:
        return kappa
    picks = np.array([0, 2, 4]) if count == 3 else np.array([0, 4])
    extents = [extent // 5 for extent in kappa.shape]
    grouped = kappa.reshape(extents[0], 5, extents[1], 5, extents[2], 5)
    for axis in (1, 3, 5):
        grouped = jnp.take(grouped, picks, axis=axis)
    return grouped.reshape(extents[0] * count, extents[1] * count, extents[2] * count)


def face_plane(face, direction, count):
    plane = face.astype(jnp.float32)
    for axis in range(3):
        if axis != direction:
            plane = jnp.repeat(plane, count, axis=axis)
    return plane


def build_level(kappa, flags, count):
    nodes, weights = lobatto(count)
    kappa_level = level_kappa(kappa, count)
    tables, lefts, rights = ([], [], [])
    diagonal = kappa_level
    for direction in range(3):
        table = element_matrix(count, direction)
        lower = face_plane(flags[2 * direction], direction, count)
        upper = face_plane(flags[2 * direction + 1], direction, count)
        left_gain = (ADVECT[direction] * (1.0 + lower) / 2.0 + DIFFUSE * count * count) / float(
            weights[0]
        )
        right_gain = (DIFFUSE * count * count - ADVECT[direction] * (1.0 - upper) / 2.0) / float(
            weights[-1]
        )
        tables.append(table)
        lefts.append(left_gain)
        rights.append(right_gain)
        diagonal = diagonal + diag_along(
            kappa_level.shape, direction, count, table, left_gain, right_gain
        )
    scale = 1.0 / (1.0 + STEP_SIZE * JACOBI_SCALE * diagonal)
    return (count, tables, lefts, rights, kappa_level, scale)


def restrict(field, fine_count, coarse_count):
    fine_nodes, fine_weights = lobatto(fine_count)
    coarse_nodes, coarse_weights = lobatto(coarse_count)
    table = (
        (1.0 / coarse_weights)[:, None]
        * lagrange_table(coarse_nodes, fine_nodes).T
        * fine_weights[None, :]
    )
    for axis in range(field.ndim - 3, field.ndim):
        field = apply_along(field, axis, fine_count, table)
    return field


def prolong(field, coarse_count, fine_count):
    fine_nodes, fine_weights = lobatto(fine_count)
    coarse_nodes, coarse_weights = lobatto(coarse_count)
    table = lagrange_table(coarse_nodes, fine_nodes)
    for axis in range(field.ndim - 3, field.ndim):
        field = apply_along(field, axis, coarse_count, table)
    return field


def chebyshev(rhs, start, level, operator):
    centre = (CHEB_HIGH + CHEB_LOW) / 2.0
    radius = (CHEB_HIGH - CHEB_LOW) / 2.0
    ratio = centre / radius
    first_rho = 1.0 / ratio
    second_rho = 1.0 / (2.0 * ratio - first_rho)
    scale = level[5]
    if start is None:
        remain = rhs
    else:
        remain = rhs - operator(start, level)
    step = scale * remain / centre
    guess = step if start is None else start + step
    remain = remain - operator(step, level)
    step = second_rho * first_rho * step + 2.0 * second_rho / radius * scale * remain
    return guess + step


def vcycle(rhs, levels, operator):
    fine, middle, coarse = levels
    fine_x = chebyshev(rhs, None, fine, operator)
    middle_rhs = restrict(rhs - operator(fine_x, fine), 5, 3)
    middle_x = chebyshev(middle_rhs, None, middle, operator)
    coarse_rhs = restrict(middle_rhs - operator(middle_x, middle), 3, 2)
    coarse_x = chebyshev(coarse_rhs, None, coarse, operator)
    middle_x = chebyshev(middle_rhs, middle_x + prolong(coarse_x, 2, 3), middle, operator)
    return chebyshev(rhs, fine_x + prolong(middle_x, 3, 5), fine, operator)


def spatial(field, level):
    count, tables, lefts, rights, kappa_level, scale = level
    padded = extended(field, (("gx", 1), ("gy", 2)), 1)
    total = kappa_level * field
    total = total + line_part(
        field,
        1,
        count,
        tables[0],
        lefts[0],
        rights[0],
        padded[:, 0, 1:-1, :],
        padded[:, -1, 1:-1, :],
    )
    total = total + line_part(
        field,
        2,
        count,
        tables[1],
        lefts[1],
        rights[1],
        padded[:, 1:-1, 0, :],
        padded[:, 1:-1, -1, :],
    )
    total = total + line_part(
        field, 3, count, tables[2], lefts[2], rights[2], field[:, :, :, -1], field[:, :, :, 0]
    )
    return total


def apply_system(field, level, coupling):
    image = spatial(field, level)
    everyone = lax.all_gather(image, "section", axis=0, tiled=True)
    butcher = jnp.asarray(radau_matrix(), jnp.float32)
    rows = lax.dynamic_slice_in_dim(
        butcher, lax.axis_index("section") * field.shape[0], field.shape[0], 0
    )
    mixed = jnp.einsum("ij,jabc->iabc", rows, everyone, precision=lax.Precision.HIGHEST)
    return field + STEP_SIZE * mixed


def global_total(values):
    return lax.psum(values, ("section", "gx", "gy"))


def stepwise(rhs, guess, kappa, bc_flags):
    levels = [build_level(kappa, bc_flags, count) for count in (5, 3, 2)]
    section_operator = partial(apply_system, coupling=None)
    start_residual = rhs - section_operator(guess, levels[0])
    dofs = float(rhs.size * lax.axis_size("section") * lax.axis_size("gx") * lax.axis_size("gy"))
    beta = jnp.sqrt(global_total(jnp.sum(start_residual * start_residual).reshape(1))[0])
    basis = start_residual / beta
    precond = vcycle(basis, levels, section_operator)
    image = section_operator(precond, levels[0])
    upper = global_total(jnp.sum(image * basis).reshape(1))[0]
    remainder = image - upper * basis
    lower = jnp.sqrt(global_total(jnp.sum(remainder * remainder).reshape(1))[0])
    weight = beta * upper / (upper * upper + lower * lower)
    solution = guess + weight * precond
    residual = start_residual - weight * image
    arnoldi = jnp.stack([beta / math.sqrt(dofs), upper, lower]).astype(jnp.float32)
    return (solution, residual, arnoldi)


EZ = 32
COLS = 16
HALF = 64
FACE_X = HALF + 25
KAPPA = FACE_X + 15
PIECE = KAPPA + 16
LINE = 4 * HALF
REST_Y = 4 * 16
REST = REST_Y + 104
FIELD = 1000
F32 = jnp.float32


def split_sections():
    matrix = radau_matrix()
    values, vectors = np.linalg.eig(matrix)
    order = [n for n in np.argsort(np.abs(values.imag), kind="stable") if values[n].imag > 0]
    bases = []
    for n in order:
        plane = np.stack([vectors[:, n].real, vectors[:, n].imag], axis=1)
        bases.append(np.linalg.qr(plane)[0])
    left, cross, right = np.linalg.svd(bases[0].T @ bases[1])
    bases = [bases[0] @ left, bases[1] @ right.T]
    for c in range(2):
        sign = np.sign(bases[0][np.argmax(np.abs(bases[0][:, c])), c])
        bases = [np.concatenate([b[:, :c], sign * b[:, c : c + 1], b[:, c + 1 :]], axis=1) for b in bases]
    whole = np.concatenate(bases, axis=1)
    back = np.linalg.inv(whole)
    return whole, back, back @ matrix, back @ matrix @ whole, cross


def iota(shape, dim):
    return lax.broadcasted_iota(jnp.int32, shape, dim)


def exact_dot(a, b):
    return lax.dot_general(
        a, b, (((1,), (0,)), ((), ())), precision=lax.Precision.HIGHEST, preferred_element_type=F32
    )


def split_dot(a, b):
    high = a.astype(jnp.bfloat16)
    rest = a - high.astype(F32)
    middle = rest.astype(jnp.bfloat16)
    low = (rest - middle.astype(F32)).astype(jnp.bfloat16)
    b = b.astype(jnp.bfloat16)
    return sum(
        lax.dot_general(part, b, (((1,), (0,)), ((), ())), preferred_element_type=F32)
        for part in (low, middle, high)
    )


def choose(index, values):
    out = values[-1]
    for place in range(len(values) - 2, -1, -1):
        out = jnp.where(index == place, values[place], out)
    return out


def face_gains(flag, direction, side, count):
    nodes, weights = lobatto(count)
    c, nu = ADVECT[direction], DIFFUSE * count * count
    if side == 0:
        return (c * (1.0 + flag) / 2.0 + nu) * (1.0 / float(weights[0]))
    return (nu - c * (1.0 - flag) / 2.0) * (1.0 / float(weights[-1]))


def row_table():
    kx, ky = (element_matrix(5, d) for d in range(2))
    rows = np.zeros((64, 64))
    for s in range(2):
        for i in range(5):
            for j in range(5):
                r = 2 * (i * 5 + j) + s
                for m in range(5):
                    rows[r, 2 * (m * 5 + j) + s] += kx[i, m]
                    rows[r, 2 * (i * 5 + m) + s] += ky[j, m]
    return rows.astype(np.float32)


def pick_lines(k):
    lane = iota((160, 256), 1)
    return (iota((160, 256), 0) == 5 * (lane % EZ) + k + lane // 128).astype(F32)


def pair_factors(sec, table, own, s):
    upper = iota((32, 128), 1) < 64
    first = jnp.where(upper, float(table[0, s]), float(table[1, s]))
    second = jnp.where(upper, float(table[2, 2 + s]), float(table[3, 2 + s]))
    if not own:
        first = jnp.where(upper, float(table[2, s]), float(table[3, s]))
        second = jnp.where(upper, float(table[0, 2 + s]), float(table[1, 2 + s]))
    return jnp.where(sec == 0, first, second)


def pack_nodes(nodes):
    half = nodes.shape[0] // 2
    odd = iota((half, 128), 1) // EZ % 2 == 1
    return jnp.where(odd, nodes[half:, :], nodes[:half, :])


def local_kernel(
    rhs_in, guess_in, kappa_in, flags_in, rows_in, mine, theirs,
    rhs, guess, kappa, flags, rows_t, sems, stack, lines, nodes, y_faces, x_faces,
):
    sec = lax.axis_index("section")
    pairs = [(guess_in, guess), (rhs_in, rhs), (rows_in, rows_t), (kappa_in, kappa), (flags_in, flags)]
    copies = [pltpu.make_async_copy(source, target, sems.at[n]) for n, (source, target) in enumerate(pairs)]
    for copy in copies:
        copy.start()
    for ref in (stack, nodes, y_faces, x_faces):
        ref[...] = jnp.zeros_like(ref)
    for copy in copies:
        copy.wait()
    for i in range(5):
        stack[192 + 5 * i : 197 + 5 * i, :] = kappa[i]
        for j in range(5):
            r = 2 * (5 * i + j)
            value = guess[i, j]
            stack[128 + r : 130 + r, :] = value
            stack[r : r + 2, :] = rhs[i, j] - value
    stack[64:128, :] = exact_dot(rows_t[...], stack[128:192, :])
    source = stack[...]
    for k in (0, 2, 4):
        shown = split_dot(source, pick_lines(k))
        lines[224 * k : 224 * k + 224, :] = shown[:, :128]
        if k < 4:
            lines[224 * k + 224 : 224 * k + 448, :] = shown[:, 128:]

    def part(k, first, s):
        return lines[pl.ds(224 * k + first + s, 32, stride=2), :]

    def kappa_part(k):
        return lines[224 * k + 192 : 224 * k + 224, :]

    repeat = (iota((EZ, 128), 1) % EZ == iota((EZ, 128), 0)).astype(F32)
    shown = split_dot(flags[:, 0, 0, :].astype(F32), repeat)
    gains = [face_gains(shown[d : d + 1, :], d // 2, d % 2, 5) for d in range(6)]
    row = iota((32, 128), 0)
    none = jnp.zeros((32, 128), F32)
    own = jnp.where(row < 5, gains[0], jnp.where((row >= 20) & (row < 25), gains[1], none))
    own = own + jnp.where(row % 5 == 0, gains[2], jnp.where(row % 5 == 4, gains[3], none))
    kz = element_matrix(5, 2)
    back, back_matrix = split_sections()[1:3]
    fields = [[part(k, 128, s) for k in range(5)] for s in range(2)]
    for k in range(5):
        diagonal = kappa_part(k) + own
        if k == 0:
            diagonal = diagonal + gains[4]
        if k == 4:
            diagonal = diagonal + gains[5]
        images = []
        for s in range(2):
            image = diagonal * fields[s][k] + part(k, 64, s)
            for m in range(5):
                image = image + float(kz[k, m]) * fields[s][m]
            if k == 0:
                image = image - gains[4] * pltpu.roll(fields[s][4], 1, 1)
            if k == 4:
                image = image - gains[5] * pltpu.roll(fields[s][0], 127, 1)
            images.append(image)
        for p, mark in enumerate((True, False)):
            total = jnp.zeros((32, 128), F32)
            trace = jnp.zeros((32, 128), F32)
            for s in range(2):
                total = total + pair_factors(sec, back, mark, s) * part(k, 0, s)
                factor = pair_factors(sec, STEP_SIZE * back_matrix, mark, s)
                total = total - factor * images[s]
                trace = trace + factor * fields[s][k]
            nodes[128 * p + 25 * k : 128 * p + 25 * k + 25, :] = total[:25]
            for i in range(5):
                for f in range(2):
                    r = 64 * p + 32 * f + 5 * k + i
                    y_faces[r : r + 1, :] = trace[5 * i + 4 * f : 5 * i + 4 * f + 1]
            for f in range(2):
                r = 32 * p + 16 * f + 3 * k
                x_faces[r : r + 3, :] = trace[20 * f + 1 : 20 * f + 4]
    upper = iota((1, 128), 1) < 64
    for r in range(3):
        nodes[125 + r : 126 + r, :] = jnp.where(upper, shown[2 * r : 2 * r + 1], shown[2 * r + 1 : 2 * r + 2])
    for p, out in enumerate((mine, theirs)):
        out[:HALF, :] = pack_nodes(nodes[128 * p : 128 * p + 128, :])
        out[HALF:FACE_X, :] = pack_nodes(y_faces[64 * p : 64 * p + 64, :])[:25]
        out[FACE_X:KAPPA, :] = pack_nodes(x_faces[32 * p : 32 * p + 32, :])[:15]
    for k in range(5):
        nodes[25 * k : 25 * k + 25, :] = kappa_part(k)[:25]
    kappas = choose(iota((32, 128), 1) // EZ, [nodes[32 * q : 32 * q + 32, :] for q in range(4)])
    mine[KAPPA:, :] = jnp.where(sec == 0, kappas[:16], kappas[16:])


def part_kernel(source, piece, kappa):
    piece[...] = source[:KAPPA, :]
    kappa[...] = source[KAPPA:, :]


VMEM = pl.BlockSpec(memory_space=pltpu.VMEM)
HBM = pl.BlockSpec(memory_space=pltpu.HBM)


def limit(mib):
    return pltpu.CompilerParams(vmem_limit_bytes=mib * 2**20)


def local_part(rhs, guess, kappa, flags):
    operands = (rhs, guess, kappa, flags, jnp.asarray(row_table()))
    return pl.pallas_call(
        local_kernel,
        out_shape=[jax.ShapeDtypeStruct((rows, 128), F32) for rows in (PIECE, KAPPA)],
        in_specs=[HBM] * 5,
        out_specs=[VMEM] * 2,
        scratch_shapes=[pltpu.VMEM(o.shape, o.dtype) for o in operands]
        + [
            pltpu.SemaphoreType.DMA((5,)),
            pltpu.VMEM((224, 160), F32),
            pltpu.VMEM((5 * 224, 128), F32),
            pltpu.VMEM((256, 128), F32),
            pltpu.VMEM((128, 128), F32),
            pltpu.VMEM((64, 128), F32),
        ],
        compiler_params=limit(60),
        cost_estimate=pl.CostEstimate(flops=20_000_000, bytes_accessed=8_000_000, transcendentals=0),
        name="local_part",
    )(*operands)


def part(x):
    return pl.pallas_call(
        part_kernel,
        out_shape=[jax.ShapeDtypeStruct((rows, 128), F32) for rows in (KAPPA, 16)],
        in_specs=[VMEM],
        out_specs=[VMEM] * 2,
        compiler_params=limit(16),
        name="part",
    )(x)


class Level:
    def __init__(self, count, refs):
        self.count = count
        self.x, self.dir, self.res, self.f = refs
        self.tables = [element_matrix(count, d) for d in range(3)]
        self.gains = self.diag = self.jac = None


def tile(index):
    return pl.ds(index * 8, 8)


def rows_of(pieces, size, r, h):
    return pieces[pl.ds(8 * h * size + r, 8, stride=size), :]


ORDER_X = ((3, 2), (2, 3), (1, 1))
ORDER_Y = ((3, 3), (1, 2), (2, 1))


def partner(bits):
    return jnp.where(lax.axis_index("section") == 0, bits[0], bits[1])


def place_pieces(blocks, pieces, first, size, room):
    my_gx, my_gy = lax.axis_index("gx"), lax.axis_index("gy")
    for b, block in enumerate(blocks):
        gy = my_gy ^ partner(ORDER_Y[b - 1]) if b else my_gy
        for a in range(4):
            column = (my_gx ^ a) * 4 + gy
            start = pl.multiple_of(column * room, 8)
            pieces[pl.ds(start, size), :] = block[first + a * size : first + a * size + size, :]


class Lanes:
    def __init__(self):
        self.lane = iota((8, 128), 1)
        sub = iota((8, 128), 0)
        self.group = self.lane // EZ
        self.odd = self.group % 2 == 1
        self.element = self.lane % EZ
        self.place = sub % 4
        self.low_half = sub < 4

    def around(self, u):
        turned = pltpu.roll(u, 4, u.ndim - 2)
        far = jnp.where(self.odd, pltpu.roll(turned, 32, u.ndim - 1), pltpu.roll(turned, 96, u.ndim - 1))
        return turned, far

    def x_before(self, u):
        turned, far = self.around(u)
        return jnp.where(self.low_half, far, turned)

    def x_after(self, u):
        turned, far = self.around(u)
        return jnp.where(self.low_half, turned, far)

    def y_before(self, u):
        return jnp.where(self.place == 0, pltpu.roll(u, 5, 0), pltpu.roll(u, 1, 0))

    def y_after(self, u):
        return jnp.where(self.place == 3, pltpu.roll(u, 3, 0), pltpu.roll(u, 7, 0))

    def z_before(self, u):
        return jnp.where(self.element == 0, pltpu.roll(u, 97, u.ndim - 1), pltpu.roll(u, 1, u.ndim - 1))

    def z_after(self, u):
        last = self.element == EZ - 1
        return jnp.where(last, pltpu.roll(u, 31, u.ndim - 1), pltpu.roll(u, 127, u.ndim - 1))


def load(ref, first, count):
    return ref[pl.ds(first * 8, count * 8), :].reshape(count, 8, 128)


def store(ref, first, value):
    ref[pl.ds(first * 8, value.shape[0] * 8), :] = value.reshape(value.shape[0] * 8, 128)


DIAGS = (0, 250, 304)
GAINS = (320, 326, 332)
REGISTERS = 338
CENTRE = (CHEB_HIGH + CHEB_LOW) / 2.0
RADIUS = (CHEB_HIGH - CHEB_LOW) / 2.0


def flag_lanes(row, slot):
    turned = [row] + [pltpu.roll(row, 32 * m, 1) for m in range(1, 4)]
    return choose(iota(row.shape, 1) // EZ, [turned[(g - 2 * slot - 1) % 4] for g in range(4)])


def line_kernel(first, second, third, own, line, rest, faces, sorted_pieces):
    sorted_pieces[:PIECE, :] = own[...]
    for bits, piece in zip(ORDER_X, (first, second, third)):
        sorted_pieces[pl.ds(pl.multiple_of(partner(bits) * PIECE, 8), PIECE), :] = piece[...]
    pieces = [sorted_pieces.at[PIECE * a : PIECE * a + PIECE, :] for a in range(4)]
    even = lax.axis_index("gx") % 2 == 0
    odd = iota((8, 128), 1) // EZ % 2 == 1
    faces[...] = jnp.zeros_like(faces)

    def both(rows, f):
        side = odd[:1] if f else jnp.logical_not(odd[:1])
        return jnp.where(side, rows, pltpu.roll(rows, 96 if f else 32, 1))

    for a, piece in enumerate(pieces):
        for f in range(2):
            base = 64 * a + 32 * f
            inner = both(piece[FACE_X:KAPPA, :], f)
            ends = [both(piece[HALF:FACE_X, :], g) for g in range(2)]
            for k in range(5):
                r = base + 5 * k
                node = 5 * k + 4 * f
                faces[r : r + 1, :] = ends[0][node : node + 1]
                faces[r + 1 : r + 4, :] = inner[3 * k : 3 * k + 3]
                faces[r + 4 : r + 5, :] = ends[1][node : node + 1]
    for a, piece in enumerate(pieces):
        line[HALF * a : HALF * a + HALF, :] = piece[:HALF, :]
        rest[16 * a : 16 * a + 16, :] = piece[KAPPA:, :]
        rest[REST_Y + 25 * a : REST_Y + 25 * a + 25, :] = piece[HALF:FACE_X, :]
        flags = [flag_lanes(piece[61:62, :], slot) for slot in range(2)]
        gains = [face_gains(flags[d], 0, d, 5) for d in range(2)]
        next_first = even if a % 2 == 0 else jnp.logical_not(even)
        for f in range(2):
            one = faces[64 * (a ^ 1) + 32 * (1 - f) : 64 * (a ^ 1) + 32 * (1 - f) + 32, :]
            three = faces[64 * (a ^ 3) + 32 * (1 - f) : 64 * (a ^ 3) + 32 * (1 - f) + 32, :]
            near = jnp.where(next_first, one, three) if f else jnp.where(next_first, three, one)
            term = gains[f] * near
            for k in range(5):
                node = 25 * k + 20 * f
                side = odd[:5] if node >= HALF else jnp.logical_not(odd[:5])
                r = HALF * a + node % HALF
                line[r : r + 5, :] = line[r : r + 5, :] + jnp.where(side, term[5 * k : 5 * k + 5], 0.0)
    rest[REST_Y + 100 :, :] = jnp.zeros((4, 128), F32)


def halves_kernel(block0, block1, block2, block3, out):
    place_pieces((block0, block1, block2, block3), out, 0, 16, 16)


def widen(low, high, odd):
    return jnp.where(odd, pltpu.roll(high, 32, 1), low), jnp.where(odd, high, pltpu.roll(low, 96, 1))


def assemble_kernel(block0, block1, block2, block3, rest0, rest1, rest2, rest3, field, pieces, edges, traces):
    place_pieces((block0, block1, block2, block3), pieces, 0, HALF, HALF)
    place_pieces((rest0, rest1, rest2, rest3), edges, REST_Y, 25, 32)
    lanes = Lanes()
    for source, size, rows, target, apart in ((edges, 32, 25, traces, 25), (pieces, HALF, HALF, field, HALF)):
        for r in range(rows):
            first, second = widen(rows_of(source, size, r, 0), rows_of(source, size, r, 1), lanes.odd)
            target[tile(r), :] = first
            target[tile(apart + r), :] = second
    got = field[tile(126), :]
    across = pltpu.roll(got, 64, 1)
    gains = [
        face_gains(jnp.where(lanes.lane < 64, got, across), 1, 0, 5),
        face_gains(jnp.where(lanes.lane < 64, across, got), 1, 1, 5),
    ]
    for k in range(5):
        for i in range(5):
            lower, upper = traces[tile(5 * k + i), :], traces[tile(25 + 5 * k + i), :]
            node = 25 * k + 5 * i
            field[tile(node), :] = field[tile(node), :] + gains[0] * lanes.y_before(upper)
            field[tile(node + 4), :] = field[tile(node + 4), :] + gains[1] * lanes.y_after(lower)


def setup_kernel(field, own_halves, other_halves, coefs, kap):
    sec = lax.axis_index("section")
    lanes = Lanes()
    group, lane = lanes.group, lanes.lane
    flags = []
    for r in range(3):
        got = field[tile(125 + r), :]
        across = pltpu.roll(got, 64, 1)
        flags += [jnp.where(lane < 64, got, across), jnp.where(lane < 64, across, got)]
    for r in range(16):
        pairs = [[rows_of(ref, 16, r, h) for h in range(2)] for ref in (own_halves, other_halves)]
        for half in range(2):
            turned = []
            for h in range(2):
                got = jnp.where(sec == half, pairs[0][h], pairs[1][h])
                turned.append([pltpu.roll(got, 32 * m, 1) if m else got for m in range(4)])
            for q in range(4):
                value = choose(group, [turned[g % 2][(g - q) % 4] for g in range(4)])
                kap[tile(q * 32 + half * 16 + r), :] = value
    for p, n in enumerate((5, 3, 2)):
        stride = 4 // (n - 1)
        gains = [face_gains(flags[d], d // 2, d % 2, n) for d in range(6)]
        rows = []
        for d in range(3):
            coefs[tile(GAINS[p] + 2 * d), :] = gains[2 * d]
            coefs[tile(GAINS[p] + 2 * d + 1), :] = gains[2 * d + 1]
            table = element_matrix(n, d)
            row = [jnp.full((8, 128), float(table[m, m]), F32) for m in range(n)]
            row[0] = row[0] + gains[2 * d]
            row[n - 1] = row[n - 1] + gains[2 * d + 1]
            rows.append(row)
        along = jnp.stack(rows[1])
        for k in range(n):
            for i in range(n):
                line = load(kap, k * 25 * stride + i * stride * 5, 5)
                line = jnp.stack([line[j * stride] for j in range(n)])
                value = line + (along + (rows[2][k] + rows[0][i]))
                scale = 1.0 / (1.0 + STEP_SIZE * JACOBI_SCALE * value)
                store(coefs, DIAGS[p] + (k * n + i) * n, value)
                store(coefs, DIAGS[p] + n**3 + (k * n + i) * n, scale * (1.0 / CENTRE))


def cycle_kernel(coefs, assembled, fields, more, *scratch):
    sec = lax.axis_index("section")
    my_gx, my_gy = lax.axis_index("gx"), lax.axis_index("gy")
    levels = [Level(n, scratch[4 * p : 4 * p + 4]) for p, n in enumerate((5, 3, 2))]
    half = scratch[12]
    lanes = Lanes()
    lane = lanes.lane
    blocks = split_sections()[3]

    def lanes_of(upper, lower):
        return jnp.where(lane < 64, jnp.where(sec == 0, upper[0], upper[1]), jnp.where(sec == 0, lower[0], lower[1]))

    entry = [[[float(STEP_SIZE * blocks[2 * p + a, 2 * p + b]) for p in range(2)] for b in range(2)] for a in range(2)]
    same = lanes_of(entry[0][0], entry[1][1])
    swap = lanes_of(entry[0][1], entry[1][0])
    first_rho = RADIUS / CENTRE
    second_rho = 1.0 / (2.0 * CENTRE / RADIUS - first_rho)
    keep = 1.0 + second_rho * first_rho
    push = 2.0 * second_rho / RADIUS * CENTRE
    for p, level in enumerate(levels):
        size = level.count**3
        level.gains = [-coefs[tile(GAINS[p] + d), :] for d in range(6)]
        level.diag = lambda first, count, p=p: load(coefs, DIAGS[p] + first, count)
        level.jac = lambda first, count, p=p, size=size: load(coefs, DIAGS[p] + size + first, count)

    def begin(level, source):
        n = level.count
        for first in range(0, n**3, n):
            f = load(source, first, n)
            store(level.dir, first, level.jac(first, n) * f)
            store(level.res, first, f)
            store(level.x, first, jnp.zeros_like(f))

    def apply(level, smooth):
        n = level.count
        kx, ky, kz = level.tables
        gains = level.gains
        source = level.dir if smooth else level.x
        def tree(terms):
            while len(terms) > 1:
                pairs = [a + b for a, b in zip(terms[::2], terms[1::2])]
                terms = pairs + terms[len(terms) // 2 * 2 :]
            return terms[0]

        def sums(k):
            def line_at(i):
                return load(source, (k * n + i) * n, n)

            x_left = gains[0] * lanes.x_before(line_at(n - 1))
            x_right = gains[1] * lanes.x_after(line_at(0))
            z_low, z_high, y_low, y_high = [], [], [], []
            for i in range(n):
                if k == 0:
                    z_low.append(gains[4] * lanes.z_before(load(source, ((n - 1) * n + i) * n, n)))
                if k == n - 1:
                    z_high.append(gains[5] * lanes.z_after(load(source, i * n, n)))
                v = line_at(i)
                y_low.append(gains[2] * lanes.y_before(v[n - 1]))
                y_high.append(gains[3] * lanes.y_after(v[0]))
            totals = []
            for i in range(n):
                first = (k * n + i) * n
                v = line_at(i)
                along_x = [float(kx[i, m]) * line_at(m) for m in range(n) if m != i]
                along_z = [float(kz[k, m]) * load(source, (m * n + i) * n, n) for m in range(n) if m != k]
                along_y = []
                for j in range(n):
                    terms = [float(ky[j, m]) * v[m] for m in range(n) if m != j]
                    if j == 0:
                        terms.append(y_low[i])
                    if j == n - 1:
                        terms.append(y_high[i])
                    along_y.append(tree(terms))
                if i == 0:
                    along_x.append(x_left)
                if i == n - 1:
                    along_x.append(x_right)
                if k == 0:
                    along_z.append(z_low[i])
                if k == n - 1:
                    along_z.append(z_high[i])
                totals.append(tree([level.diag(first, n) * v, tree(along_x), tree(along_z), jnp.stack(along_y)]))
            return totals

        def update(k, totals):
            moved = [pltpu.roll(total, 64, 2) for total in totals]
            for i in range(n):
                first = (k * n + i) * n
                v = load(source, first, n)
                image = v + (same * totals[i] + swap * moved[i])
                if smooth:
                    scaled = level.jac(first, n) * (load(level.res, first, n) - image)
                    store(level.x, first, (load(level.x, first, n) + keep * v) + push * scaled)
                else:
                    rest = load(level.f, first, n) - image
                    store(level.res, first, rest)
                    store(level.dir, first, level.jac(first, n) * rest)

        if n == 5:
            ready = sums(0)
            for k in range(n):
                following = sums(k + 1) if k + 1 < n else None
                update(k, ready)
                ready = following
        else:
            for k, totals in enumerate([sums(k) for k in range(n)]):
                update(k, totals)

    def combine(weights, parts):
        total = None
        for weight, part in zip(weights, parts):
            if abs(weight) > 1e-14:
                term = part if abs(weight - 1.0) < 1e-14 else float(weight) * part
                total = term if total is None else total + term
        return total

    def change(table, source, target, add):
        m, n = table.shape
        for i in range(n):
            parts = [load(source, i * n + k * n * n, n) for k in range(n)]
            for k in range(m):
                store(half, i * n + k * n * n, combine(table[k], parts))
        for k in range(m):
            parts = [load(half, k * n * n + i * n, n) for i in range(n)]
            for i in range(m):
                line = combine(table[i], parts)
                value = jnp.stack([combine(table[j], [line[a] for a in range(n)]) for j in range(m)])
                first = k * m * m + i * m
                store(target, first, load(target, first, m) + value if add else value)

    def down(n, m):
        fine_nodes, fine_weights = lobatto(n)
        coarse_nodes, coarse_weights = lobatto(m)
        table = lagrange_table(coarse_nodes, fine_nodes)
        return (1.0 / coarse_weights)[:, None] * table.T * fine_weights[None, :]

    def up(m, n):
        return lagrange_table(lobatto(m)[0], lobatto(n)[0])

    def solve(p):
        level = levels[p]
        if p == 2:
            apply(level, True)
            return
        below = levels[p + 1]

        def correct():
            n, m = level.count, below.count
            change(down(n, m), level.res, below.f, False)
            begin(below, below.f)
            solve(p + 1)
            change(up(m, n), below.x, level.x, True)

        if p == 1:
            apply(level, True)
            apply(level, False)
            correct()
            apply(level, False)
            apply(level, True)
            return

        def step(t, carry):
            @pl.when(t != 1)
            def _():
                apply(level, True)

            apply(level, False)

            @pl.when(t == 0)
            def _():
                correct()
            return carry
        lax.fori_loop(0, 3, step, 0)

    fine = levels[0]
    fine.f = assembled
    begin(fine, assembled)
    solve(0)

    for first in range(0, 125, 5):
        part, place = (fields, first) if first < SPLIT else (more, first - SPLIT)
        store(part, place, load(fine.res, first, 5))
    column = (my_gx % 2) * 4 + my_gy
    more[AFTER : AFTER + 125, :] = fine.x[pl.ds(column, 125, stride=8), :]
    more[AFTER + 125 :, :] = jnp.zeros((3, 128), F32)


SPLIT = 75
AFTER = 8 * (125 - SPLIT)


def register(parts, r):
    return parts[0][tile(r), :] if r < SPLIT else parts[1][tile(r - SPLIT), :]


def column_of(parts, k):
    first = 3 * (k // 3)
    return parts[k // 3][column_rows(k - first), :]


def column_z(parts, k):
    return parts[1][AFTER + 25 * k : AFTER + 25 * k + 25, :]


def pair_weights():
    cross = split_sections()[4]
    return jnp.where(iota((8, 128), 1) < 64, float(cross[0]), float(cross[1]))


def column_factors(p):
    sec = lax.axis_index("section")
    whole = split_sections()[0]
    lane = iota((25, 128), 1)
    here = lane // EZ % 2 == lax.axis_index("gx") // 2
    factors = []
    for s in range(2):
        parts = []
        for mine in range(2):
            t = whole[2 * mine + s]
            q = mine if p == 0 else 1 - mine
            parts.append(jnp.where(lane < 64, float(t[2 * q]), float(t[2 * q + 1])))
        factors.append(jnp.where(here, jnp.where(sec == 0, parts[0], parts[1]), 0.0))
    return factors


def column_rows(k):
    column = (lax.axis_index("gx") % 2) * 4 + lax.axis_index("gy")
    return pl.ds(k * 200 + column, 25, stride=8)


def raw_order(k):
    lane = iota((256, 160), 0)
    return (iota((256, 160), 1) == 5 * (lane % EZ) + k + lane // 128).astype(F32)


def side_by_side(cols):
    half = cols.shape[0] // 2
    return jnp.concatenate([cols[:half, :], cols[half:, :]], axis=1)


def early_kernel(own0, own1, own_start, other_start, sums, column_out, cols):
    own = (own0, own1)
    weights = pair_weights()
    cols[...] = jnp.zeros_like(cols)
    total = jnp.zeros((192, 160), F32)
    own_factors, other_factors = column_factors(0), column_factors(1)
    for k in range(5):
        where = column_rows(k)
        z = column_z(own, k)
        start, other = own_start[where, :], other_start[where, :]
        w = start - column_of(own, k)
        side = 192 * (k % 2)
        for s in range(2):
            cols[pl.ds(side + s, 25, stride=2), :] = own_factors[s] * z
            cols[pl.ds(side + 64 + s, 25, stride=2), :] = own_factors[s] * start + other_factors[s] * other
            cols[pl.ds(side + 128 + s, 25, stride=2), :] = own_factors[s] * w
        if k % 2 == 1:
            total = total + split_dot(side_by_side(cols), raw_order(k - 1))
    cols[192:, :] = jnp.zeros((192, 128), F32)
    total = total + split_dot(side_by_side(cols), raw_order(4))
    column_out[...] = total
    nothing = jnp.zeros((8, 128), F32)
    uppers, sizes = [nothing] * 5, [nothing] * 5
    for r in range(125):
        c, d = own_start[tile(r), :], other_start[tile(r), :]
        a = c - register(own, r)
        uppers[r % 5] = uppers[r % 5] + a * (c + weights * d)
        sizes[r % 5] = sizes[r % 5] + ((c * c + d * d) + 2.0 * (weights * (c * d)))
    sums[0:8, :] = sum(uppers)
    sums[8:16, :] = jnp.broadcast_to(jnp.sum(sum(sizes), keepdims=True), (8, 128))


def finish_kernel(own0, own1, other0, other1, own_start, other_start, sums, column, guess, sol, res_out, arnoldi, cols, outs):
    own, other = (own0, own1), (other0, other1)
    cols[...] = jnp.zeros_like(cols)
    total = jnp.zeros((128, 160), F32)
    factors = column_factors(1)
    for k in range(5):
        where = column_rows(k)
        z = column_z(other, k)
        w = other_start[where, :] - column_of(other, k)
        side = 128 * (k % 2)
        for s in range(2):
            cols[pl.ds(side + s, 25, stride=2), :] = factors[s] * z
            cols[pl.ds(side + 64 + s, 25, stride=2), :] = factors[s] * w
        if k % 2 == 1:
            total = total + split_dot(side_by_side(cols), raw_order(k - 1))
    cols[128:, :] = jnp.zeros((128, 128), F32)
    total = total + split_dot(side_by_side(cols), raw_order(4))
    weights = pair_weights()
    nothing = jnp.zeros((8, 128), F32)
    uppers = [nothing] * 5
    for r in range(125):
        c, d = own_start[tile(r), :], other_start[tile(r), :]
        b = d - register(other, r)
        uppers[r % 5] = uppers[r % 5] + b * (d + weights * c)

    mine, theirs = sums[0:8, :], sum(uppers)
    size = sums[8:9, 0:1]
    upper = jnp.sum(mine + theirs, keepdims=True) / size
    rests = [nothing] * 5
    for r in range(125):
        c, d = own_start[tile(r), :], other_start[tile(r), :]
        a = (c - register(own, r)) - upper * c
        b = (d - register(other, r)) - upper * d
        rests[r % 5] = rests[r % 5] + ((a * a + b * b) + 2.0 * (weights * (a * b)))
    rest = jnp.sum(sum(rests), keepdims=True)
    beta = jnp.sqrt(size)
    lower = jnp.sqrt(rest) / beta
    weight = upper / (upper * upper + lower * lower)
    entries = float(125 * EZ * COLS * 4)
    for place_out, value in enumerate((beta * (1.0 / math.sqrt(entries)), upper, lower)):
        arnoldi[place_out] = value[0, 0]
    outs[:64, :] = weight * (column[:64, :] + total[:64])
    outs[64:, :] = column[64:128, :] - weight * (column[128:, :] + total[64:])
    for i in range(5):
        for j in range(5):
            r = 2 * (5 * i + j)
            sol[i, j] = guess[i, j] + outs[r : r + 2, :]
            res_out[i, j] = outs[64 + r : 66 + r, :]


def plain_call(kernel, name, rows, scratch, operands, cost=1_000_000):
    many = isinstance(rows, tuple)
    shapes = [jax.ShapeDtypeStruct((r, 128), F32) for r in (rows if many else (rows,))]
    return pl.pallas_call(
        kernel,
        out_shape=shapes if many else shapes[0],
        in_specs=[VMEM] * len(operands),
        out_specs=[VMEM] * len(shapes) if many else VMEM,
        scratch_shapes=[pltpu.VMEM((r, 128), F32) for r in scratch],
        compiler_params=limit(16),
        cost_estimate=pl.CostEstimate(flops=cost, bytes_accessed=cost, transcendentals=0),
        name=name,
    )(*operands)


def cycle(coefs, assembled):
    scratch = []
    for n in (5, 3, 2):
        scratch += [pltpu.VMEM((n**3 * 8, 128), F32)] * 4
    scratch += [pltpu.VMEM((FIELD, 128), F32)]
    return pl.pallas_call(
        cycle_kernel,
        out_shape=[jax.ShapeDtypeStruct((rows, 128), F32) for rows in (SPLIT * 8, AFTER + 128)],
        in_specs=[VMEM] * 2,
        out_specs=[VMEM] * 2,
        scratch_shapes=scratch,
        compiler_params=limit(24),
        cost_estimate=pl.CostEstimate(flops=40_000_000, bytes_accessed=30_000_000, transcendentals=0),
        name="cycle",
    )(coefs, assembled)


def early(own, own_start, other_start):
    return pl.pallas_call(
        early_kernel,
        out_shape=[jax.ShapeDtypeStruct((16, 128), F32), jax.ShapeDtypeStruct((192, 160), F32)],
        in_specs=[VMEM] * 4,
        out_specs=[VMEM] * 2,
        scratch_shapes=[pltpu.VMEM((384, 128), F32)],
        compiler_params=limit(16),
        cost_estimate=pl.CostEstimate(flops=4_000_000, bytes_accessed=4_000_000, transcendentals=0),
        name="early",
    )(*own, own_start, other_start)


def finish(own, other, own_start, other_start, sums, column, guess):
    return pl.pallas_call(
        finish_kernel,
        out_shape=[
            jax.ShapeDtypeStruct(guess.shape, F32),
            jax.ShapeDtypeStruct(guess.shape, F32),
            jax.ShapeDtypeStruct((3,), F32),
        ],
        in_specs=[VMEM] * 9,
        out_specs=[VMEM, VMEM, pl.BlockSpec(memory_space=pltpu.SMEM)],
        scratch_shapes=[pltpu.VMEM((256, 128), F32), pltpu.VMEM((128, 160), F32)],
        compiler_params=limit(24),
        name="finish",
    )(*own, *other, own_start, other_start, sums, column, guess)


def exchange(x, axis, bits):
    return lax.ppermute(x, axis, [(n, n ^ bits) for n in range(lax.axis_size(axis))])


def exchange_by_core(x, axis, bits):
    count = lax.axis_size(axis)
    pairs = [(s * count + n, s * count + (n ^ bits[s])) for s in range(2) for n in range(count)]
    return lax.ppermute(x, ("section", axis), pairs)


def gathered_body(rhs, guess, kappa, bc_flags):
    rhs, guess = (jnp.transpose(v, (1, 2, 0, 3)) for v in (rhs, guess))
    mine, theirs = local_part(rhs, guess, kappa, bc_flags)
    got, mine, kappa_piece = lax.optimization_barrier((exchange(theirs, "section", 1), *part(mine)))
    piece = jnp.concatenate([mine + got, kappa_piece])
    pieces = [exchange_by_core(piece, "gx", bits) for bits in ORDER_X] + [piece]
    line, rest = plain_call(line_kernel, "line", (LINE, REST), [4 * 64, 4 * PIECE], pieces)
    rests = [rest] + [exchange_by_core(rest, "gy", bits) for bits in ORDER_Y]
    halves = plain_call(halves_kernel, "halves", COLS * 16, [], rests)
    other_halves = exchange(halves, "section", 1)
    blocks = [line] + [exchange_by_core(line, "gy", bits) for bits in ORDER_Y]
    blocks, other_halves = lax.optimization_barrier((blocks, other_halves))
    start = plain_call(
        assemble_kernel, "assemble", 128 * 8, [COLS * HALF, COLS * 32, 50 * 8], blocks + rests, 4_000_000
    )
    coefs = plain_call(setup_kernel, "setup", REGISTERS * 8, [128 * 8], (start, halves, other_halves))
    other_start = exchange(start, "section", 1)
    own, other_start = lax.optimization_barrier((cycle(coefs, start), other_start))
    other = [exchange(part, "section", 1) for part in own]
    sums, column = early(own, start, other_start)
    sol, res, arnoldi = finish(own, other, start, other_start, sums, column, guess)
    sol, res = (jnp.transpose(v, (2, 0, 1, 3)) for v in (sol, res))
    return sol, res, arnoldi


def solution(mesh):
    placed = (
        P("section", "gx", "gy", None),
        P("section", "gx", "gy", None),
        P("gx", "gy", None),
        P(None, "gx", "gy", None),
    )
    sizes = (mesh.shape["section"], mesh.shape["gx"], mesh.shape["gy"])

    def step(rhs, guess, kappa, bc_flags):
        fits = sizes == (2, 4, 4) and rhs.shape == (4, 20, 20, 160)
        return jax.shard_map(
            gathered_body if fits else stepwise,
            mesh=mesh,
            in_specs=placed,
            out_specs=(P("section", "gx", "gy", None), P("section", "gx", "gy", None), P()),
            check_vma=False,
        )(rhs, guess, kappa, bc_flags)

    return step
```

```python
from functools import partial
import math

import jax
import jax.numpy as jnp
import numpy as np
from jax import lax
from jax.experimental import pallas as pl
from jax.experimental.pallas import tpu as pltpu
from jax.sharding import PartitionSpec as P

ADVECT = (1.0, 0.7, 0.5)
DIFFUSE = 0.05
STEP_SIZE = 0.2
JACOBI_SCALE = 0.25
CHEB_LOW = 0.25
CHEB_HIGH = 2.0
LETTERS = "abcdef"


def extended(x, sides, width):
    for axis, dim in sides:
        peers, length = (lax.axis_size(axis), x.shape[dim])
        up = [(i, (i + 1) % peers) for i in range(peers)]
        down = [(j, i) for i, j in up]
        last = lax.slice_in_dim(x, length - width, length, axis=dim)
        leading = lax.slice_in_dim(x, 0, width, axis=dim)
        before = lax.ppermute(last, axis, up)
        after = lax.ppermute(leading, axis, down)
        x = jnp.concatenate([before, x, after], axis=dim)
    return x


def lobatto(count):
    if count == 5:
        inner = math.sqrt(3.0 / 7.0)
        return (
            np.array([-1.0, -inner, 0.0, inner, 1.0]),
            np.array([0.1, 49.0 / 90.0, 32.0 / 45.0, 49.0 / 90.0, 0.1]),
        )
    if count == 3:
        return (np.array([-1.0, 0.0, 1.0]), np.array([1.0 / 3.0, 4.0 / 3.0, 1.0 / 3.0]))
    return (np.array([-1.0, 1.0]), np.array([1.0, 1.0]))


def lagrange_table(nodes, points):
    table = np.ones((len(points), len(nodes)))
    for column in range(len(nodes)):
        for other in range(len(nodes)):
            if other != column:
                table[:, column] *= (points - nodes[other]) / (nodes[column] - nodes[other])
    return table


def slope_table(nodes):
    total = len(nodes)
    factor = np.array(
        [np.prod([nodes[i] - nodes[k] for k in range(total) if k != i]) for i in range(total)]
    )
    table = np.zeros((total, total))
    for row in range(total):
        for column in range(total):
            if row != column:
                table[row, column] = factor[row] / factor[column] / (nodes[row] - nodes[column])
        table[row, row] = -np.sum(table[row])
    return table


def element_matrix(count, direction):
    nodes, weights = lobatto(count)
    slopes = slope_table(nodes)
    stiffness = (1.0 / weights)[:, None] * (slopes.T @ (weights[:, None] * slopes))
    return ADVECT[direction] * slopes + DIFFUSE * stiffness


def legendre_pair(point, order):
    values = [1.0, point]
    slopes = [0.0, 1.0]
    for index in range(1, order):
        values.append(
            ((2 * index + 1) * point * values[index] - index * values[index - 1]) / (index + 1)
        )
        slopes.append(slopes[index - 1] + (2 * index + 1) * values[index])
    return (values, slopes)


def radau_nodes():
    starts = [0.0885879595127039, 0.4094668644407347, 0.7876594617608471]
    found = []
    for start in starts:
        point = start
        for sweep in range(30):
            values, slopes = legendre_pair(2.0 * point - 1.0, 4)
            change = (values[4] - values[3]) / (2.0 * (slopes[4] - slopes[3]))
            point = point - change
        found.append(point)
    found.append(1.0)
    return found


def poly_times(coefs, root):
    result = [0.0] * (len(coefs) + 1)
    for index in range(len(coefs)):
        result[index + 1] += coefs[index]
        result[index] -= root * coefs[index]
    return result


def radau_matrix():
    order = 4
    nodes = radau_nodes()
    matrix = np.zeros((order, order))
    for column in range(order):
        coefs = [1.0]
        denominator = 1.0
        for other in range(order):
            if other != column:
                coefs = poly_times(coefs, nodes[other])
                denominator *= nodes[column] - nodes[other]
        for row in range(order):
            upper_end = nodes[row]
            integral = 0.0
            for index in range(len(coefs)):
                integral += coefs[index] * upper_end ** (index + 1) / (index + 1)
            matrix[row, column] = integral / denominator
    return matrix


def node_einsum(table, field, axis):
    labels = LETTERS[: field.ndim]
    source = labels[: axis + 1] + "j" + labels[axis + 2 :]
    target = labels[: axis + 1] + "i" + labels[axis + 2 :]
    return jnp.einsum(
        "ij," + source + "->" + target,
        jnp.asarray(table, jnp.float32),
        field,
        precision=lax.Precision.HIGHEST,
    )


def apply_along(field, axis, count, table):
    shape = field.shape
    split = shape[:axis] + (shape[axis] // count, count) + shape[axis + 1 :]
    mapped = node_einsum(table, field.reshape(split), axis)
    return mapped.reshape(
        shape[:axis] + (mapped.shape[axis] * mapped.shape[axis + 1],) + shape[axis + 1 :]
    )


def line_part(field, axis, count, table, left_gain, right_gain, left_edge, right_edge):
    shape = field.shape
    elements = shape[axis] // count
    split = field.reshape(shape[:axis] + (elements, count) + shape[axis + 1 :])
    linear = node_einsum(table, split, axis)
    first = lax.index_in_dim(split, 0, axis + 1, keepdims=False)
    last = lax.index_in_dim(split, count - 1, axis + 1, keepdims=False)
    before = jnp.concatenate(
        [jnp.expand_dims(left_edge, axis), lax.slice_in_dim(last, 0, elements - 1, axis=axis)], axis
    )
    after = jnp.concatenate(
        [lax.slice_in_dim(first, 1, elements, axis=axis), jnp.expand_dims(right_edge, axis)], axis
    )
    front = jnp.expand_dims(left_gain * (first - before), axis + 1)
    back = jnp.expand_dims(right_gain * (last - after), axis + 1)
    if count > 2:
        middle_shape = list(front.shape)
        middle_shape[axis + 1] = count - 2
        pieces = [front, jnp.zeros(middle_shape, jnp.float32), back]
    else:
        pieces = [front, back]
    return (linear + jnp.concatenate(pieces, axis + 1)).reshape(shape)


def diag_along(shape, axis, count, table, left_gain, right_gain):
    elements = shape[axis] // count
    split = shape[:axis] + (elements, count) + shape[axis + 1 :]
    profile = [1] * len(split)
    profile[axis + 1] = count
    diagonal_entries = np.array([table[index, index] for index in range(count)])
    base = jnp.broadcast_to(jnp.asarray(diagonal_entries, jnp.float32).reshape(profile), split)
    front = jnp.expand_dims(left_gain, axis + 1)
    back = jnp.expand_dims(right_gain, axis + 1)
    if count > 2:
        middle_shape = list(front.shape)
        middle_shape[axis + 1] = count - 2
        pieces = [front, jnp.zeros(middle_shape, jnp.float32), back]
    else:
        pieces = [front, back]
    return (base + jnp.concatenate(pieces, axis + 1)).reshape(shape)


def level_kappa(kappa, count):
    if count == 5:
        return kappa
    picks = np.array([0, 2, 4]) if count == 3 else np.array([0, 4])
    extents = [extent // 5 for extent in kappa.shape]
    grouped = kappa.reshape(extents[0], 5, extents[1], 5, extents[2], 5)
    for axis in (1, 3, 5):
        grouped = jnp.take(grouped, picks, axis=axis)
    return grouped.reshape(extents[0] * count, extents[1] * count, extents[2] * count)


def face_plane(face, direction, count):
    plane = face.astype(jnp.float32)
    for axis in range(3):
        if axis != direction:
            plane = jnp.repeat(plane, count, axis=axis)
    return plane


def build_level(kappa, flags, count):
    nodes, weights = lobatto(count)
    kappa_level = level_kappa(kappa, count)
    tables, lefts, rights = ([], [], [])
    diagonal = kappa_level
    for direction in range(3):
        table = element_matrix(count, direction)
        lower = face_plane(flags[2 * direction], direction, count)
        upper = face_plane(flags[2 * direction + 1], direction, count)
        left_gain = (ADVECT[direction] * (1.0 + lower) / 2.0 + DIFFUSE * count * count) / float(
            weights[0]
        )
        right_gain = (DIFFUSE * count * count - ADVECT[direction] * (1.0 - upper) / 2.0) / float(
            weights[-1]
        )
        tables.append(table)
        lefts.append(left_gain)
        rights.append(right_gain)
        diagonal = diagonal + diag_along(
            kappa_level.shape, direction, count, table, left_gain, right_gain
        )
    scale = 1.0 / (1.0 + STEP_SIZE * JACOBI_SCALE * diagonal)
    return (count, tables, lefts, rights, kappa_level, scale)


def restrict(field, fine_count, coarse_count):
    fine_nodes, fine_weights = lobatto(fine_count)
    coarse_nodes, coarse_weights = lobatto(coarse_count)
    table = (
        (1.0 / coarse_weights)[:, None]
        * lagrange_table(coarse_nodes, fine_nodes).T
        * fine_weights[None, :]
    )
    for axis in range(field.ndim - 3, field.ndim):
        field = apply_along(field, axis, fine_count, table)
    return field


def prolong(field, coarse_count, fine_count):
    fine_nodes, fine_weights = lobatto(fine_count)
    coarse_nodes, coarse_weights = lobatto(coarse_count)
    table = lagrange_table(coarse_nodes, fine_nodes)
    for axis in range(field.ndim - 3, field.ndim):
        field = apply_along(field, axis, coarse_count, table)
    return field


def chebyshev(rhs, start, level, operator):
    centre = (CHEB_HIGH + CHEB_LOW) / 2.0
    radius = (CHEB_HIGH - CHEB_LOW) / 2.0
    ratio = centre / radius
    first_rho = 1.0 / ratio
    second_rho = 1.0 / (2.0 * ratio - first_rho)
    scale = level[5]
    if start is None:
        remain = rhs
    else:
        remain = rhs - operator(start, level)
    step = scale * remain / centre
    guess = step if start is None else start + step
    remain = remain - operator(step, level)
    step = second_rho * first_rho * step + 2.0 * second_rho / radius * scale * remain
    return guess + step


def vcycle(rhs, levels, operator):
    fine, middle, coarse = levels
    fine_x = chebyshev(rhs, None, fine, operator)
    middle_rhs = restrict(rhs - operator(fine_x, fine), 5, 3)
    middle_x = chebyshev(middle_rhs, None, middle, operator)
    coarse_rhs = restrict(middle_rhs - operator(middle_x, middle), 3, 2)
    coarse_x = chebyshev(coarse_rhs, None, coarse, operator)
    middle_x = chebyshev(middle_rhs, middle_x + prolong(coarse_x, 2, 3), middle, operator)
    return chebyshev(rhs, fine_x + prolong(middle_x, 3, 5), fine, operator)


def spatial(field, level):
    count, tables, lefts, rights, kappa_level, scale = level
    padded = extended(field, (("gx", 1), ("gy", 2)), 1)
    total = kappa_level * field
    total = total + line_part(
        field,
        1,
        count,
        tables[0],
        lefts[0],
        rights[0],
        padded[:, 0, 1:-1, :],
        padded[:, -1, 1:-1, :],
    )
    total = total + line_part(
        field,
        2,
        count,
        tables[1],
        lefts[1],
        rights[1],
        padded[:, 1:-1, 0, :],
        padded[:, 1:-1, -1, :],
    )
    total = total + line_part(
        field, 3, count, tables[2], lefts[2], rights[2], field[:, :, :, -1], field[:, :, :, 0]
    )
    return total


def apply_system(field, level, coupling):
    image = spatial(field, level)
    everyone = lax.all_gather(image, "section", axis=0, tiled=True)
    butcher = jnp.asarray(radau_matrix(), jnp.float32)
    rows = lax.dynamic_slice_in_dim(
        butcher, lax.axis_index("section") * field.shape[0], field.shape[0], 0
    )
    mixed = jnp.einsum("ij,jabc->iabc", rows, everyone, precision=lax.Precision.HIGHEST)
    return field + STEP_SIZE * mixed


def global_total(values):
    return lax.psum(values, ("section", "gx", "gy"))


def stepwise(rhs, guess, kappa, bc_flags):
    levels = [build_level(kappa, bc_flags, count) for count in (5, 3, 2)]
    section_operator = partial(apply_system, coupling=None)
    start_residual = rhs - section_operator(guess, levels[0])
    dofs = float(rhs.size * lax.axis_size("section") * lax.axis_size("gx") * lax.axis_size("gy"))
    beta = jnp.sqrt(global_total(jnp.sum(start_residual * start_residual).reshape(1))[0])
    basis = start_residual / beta
    precond = vcycle(basis, levels, section_operator)
    image = section_operator(precond, levels[0])
    upper = global_total(jnp.sum(image * basis).reshape(1))[0]
    remainder = image - upper * basis
    lower = jnp.sqrt(global_total(jnp.sum(remainder * remainder).reshape(1))[0])
    weight = beta * upper / (upper * upper + lower * lower)
    solution = guess + weight * precond
    residual = start_residual - weight * image
    arnoldi = jnp.stack([beta / math.sqrt(dofs), upper, lower]).astype(jnp.float32)
    return (solution, residual, arnoldi)


EZ = 32
COLS = 16
HALF = 64
FACE_X = HALF + 25
KAPPA = FACE_X + 15
PIECE = KAPPA + 16
LINE = 4 * HALF
REST_Y = 4 * 16
REST = REST_Y + 104
FIELD = 1000
F32 = jnp.float32


def split_sections():
    matrix = radau_matrix()
    values, vectors = np.linalg.eig(matrix)
    order = [n for n in np.argsort(np.abs(values.imag), kind="stable") if values[n].imag > 0]
    bases = []
    for n in order:
        plane = np.stack([vectors[:, n].real, vectors[:, n].imag], axis=1)
        bases.append(np.linalg.qr(plane)[0])
    left, cross, right = np.linalg.svd(bases[0].T @ bases[1])
    bases = [bases[0] @ left, bases[1] @ right.T]
    for c in range(2):
        sign = np.sign(bases[0][np.argmax(np.abs(bases[0][:, c])), c])
        bases = [np.concatenate([b[:, :c], sign * b[:, c : c + 1], b[:, c + 1 :]], axis=1) for b in bases]
    whole = np.concatenate(bases, axis=1)
    back = np.linalg.inv(whole)
    return whole, back, back @ matrix, back @ matrix @ whole, cross


def iota(shape, dim):
    return lax.broadcasted_iota(jnp.int32, shape, dim)


def exact_dot(a, b):
    return lax.dot_general(
        a, b, (((1,), (0,)), ((), ())), precision=lax.Precision.HIGHEST, preferred_element_type=F32
    )


def split_dot(a, b):
    high = a.astype(jnp.bfloat16)
    rest = a - high.astype(F32)
    middle = rest.astype(jnp.bfloat16)
    low = (rest - middle.astype(F32)).astype(jnp.bfloat16)
    b = b.astype(jnp.bfloat16)
    return sum(
        lax.dot_general(part, b, (((1,), (0,)), ((), ())), preferred_element_type=F32)
        for part in (low, middle, high)
    )


def choose(index, values):
    out = values[-1]
    for place in range(len(values) - 2, -1, -1):
        out = jnp.where(index == place, values[place], out)
    return out


def face_gains(flag, direction, side, count):
    nodes, weights = lobatto(count)
    c, nu = ADVECT[direction], DIFFUSE * count * count
    if side == 0:
        return (c * (1.0 + flag) / 2.0 + nu) * (1.0 / float(weights[0]))
    return (nu - c * (1.0 - flag) / 2.0) * (1.0 / float(weights[-1]))


def row_table():
    kx, ky = (element_matrix(5, d) for d in range(2))
    rows = np.zeros((64, 64))
    for s in range(2):
        for i in range(5):
            for j in range(5):
                r = 2 * (i * 5 + j) + s
                for m in range(5):
                    rows[r, 2 * (m * 5 + j) + s] += kx[i, m]
                    rows[r, 2 * (i * 5 + m) + s] += ky[j, m]
    return rows.astype(np.float32)


def pick_lines(k):
    lane = iota((160, 256), 1)
    return (iota((160, 256), 0) == 5 * (lane % EZ) + k + lane // 128).astype(F32)


def pair_factors(sec, table, own, s):
    upper = iota((32, 128), 1) < 64
    first = jnp.where(upper, float(table[0, s]), float(table[1, s]))
    second = jnp.where(upper, float(table[2, 2 + s]), float(table[3, 2 + s]))
    if not own:
        first = jnp.where(upper, float(table[2, s]), float(table[3, s]))
        second = jnp.where(upper, float(table[0, 2 + s]), float(table[1, 2 + s]))
    return jnp.where(sec == 0, first, second)


def pack_nodes(nodes):
    half = nodes.shape[0] // 2
    odd = iota((half, 128), 1) // EZ % 2 == 1
    return jnp.where(odd, nodes[half:, :], nodes[:half, :])


def local_kernel(
    rhs_in, guess_in, kappa_in, flags_in, rows_in, mine, theirs,
    rhs, guess, kappa, flags, rows_t, sems, stack, lines, nodes, y_faces, x_faces,
):
    sec = lax.axis_index("section")
    pairs = [(guess_in, guess), (rhs_in, rhs), (rows_in, rows_t), (kappa_in, kappa), (flags_in, flags)]
    copies = [pltpu.make_async_copy(source, target, sems.at[n]) for n, (source, target) in enumerate(pairs)]
    for copy in copies:
        copy.start()
    for ref in (stack, nodes, y_faces, x_faces):
        ref[...] = jnp.zeros_like(ref)
    for copy in copies:
        copy.wait()
    for i in range(5):
        stack[192 + 5 * i : 197 + 5 * i, :] = kappa[i]
        for j in range(5):
            r = 2 * (5 * i + j)
            value = guess[i, j]
            stack[128 + r : 130 + r, :] = value
            stack[r : r + 2, :] = rhs[i, j] - value
    stack[64:128, :] = exact_dot(rows_t[...], stack[128:192, :])
    source = stack[...]
    for k in (0, 2, 4):
        shown = split_dot(source, pick_lines(k))
        lines[224 * k : 224 * k + 224, :] = shown[:, :128]
        if k < 4:
            lines[224 * k + 224 : 224 * k + 448, :] = shown[:, 128:]

    def part(k, first, s):
        return lines[pl.ds(224 * k + first + s, 32, stride=2), :]

    def kappa_part(k):
        return lines[224 * k + 192 : 224 * k + 224, :]

    repeat = (iota((EZ, 128), 1) % EZ == iota((EZ, 128), 0)).astype(F32)
    shown = split_dot(flags[:, 0, 0, :].astype(F32), repeat)
    gains = [face_gains(shown[d : d + 1, :], d // 2, d % 2, 5) for d in range(6)]
    row = iota((32, 128), 0)
    none = jnp.zeros((32, 128), F32)
    own = jnp.where(row < 5, gains[0], jnp.where((row >= 20) & (row < 25), gains[1], none))
    own = own + jnp.where(row % 5 == 0, gains[2], jnp.where(row % 5 == 4, gains[3], none))
    kz = element_matrix(5, 2)
    back, back_matrix = split_sections()[1:3]
    fields = [[part(k, 128, s) for k in range(5)] for s in range(2)]
    for k in range(5):
        diagonal = kappa_part(k) + own
        if k == 0:
            diagonal = diagonal + gains[4]
        if k == 4:
            diagonal = diagonal + gains[5]
        images = []
        for s in range(2):
            image = diagonal * fields[s][k] + part(k, 64, s)
            for m in range(5):
                image = image + float(kz[k, m]) * fields[s][m]
            if k == 0:
                image = image - gains[4] * pltpu.roll(fields[s][4], 1, 1)
            if k == 4:
                image = image - gains[5] * pltpu.roll(fields[s][0], 127, 1)
            images.append(image)
        for p, mark in enumerate((True, False)):
            total = jnp.zeros((32, 128), F32)
            trace = jnp.zeros((32, 128), F32)
            for s in range(2):
                total = total + pair_factors(sec, back, mark, s) * part(k, 0, s)
                factor = pair_factors(sec, STEP_SIZE * back_matrix, mark, s)
                total = total - factor * images[s]
                trace = trace + factor * fields[s][k]
            nodes[128 * p + 25 * k : 128 * p + 25 * k + 25, :] = total[:25]
            for i in range(5):
                for f in range(2):
                    r = 64 * p + 32 * f + 5 * k + i
                    y_faces[r : r + 1, :] = trace[5 * i + 4 * f : 5 * i + 4 * f + 1]
            for f in range(2):
                r = 32 * p + 16 * f + 3 * k
                x_faces[r : r + 3, :] = trace[20 * f + 1 : 20 * f + 4]
    upper = iota((1, 128), 1) < 64
    for r in range(3):
        nodes[125 + r : 126 + r, :] = jnp.where(upper, shown[2 * r : 2 * r + 1], shown[2 * r + 1 : 2 * r + 2])
    for p, out in enumerate((mine, theirs)):
        out[:HALF, :] = pack_nodes(nodes[128 * p : 128 * p + 128, :])
        out[HALF:FACE_X, :] = pack_nodes(y_faces[64 * p : 64 * p + 64, :])[:25]
        out[FACE_X:KAPPA, :] = pack_nodes(x_faces[32 * p : 32 * p + 32, :])[:15]
    for k in range(5):
        nodes[25 * k : 25 * k + 25, :] = kappa_part(k)[:25]
    kappas = choose(iota((32, 128), 1) // EZ, [nodes[32 * q : 32 * q + 32, :] for q in range(4)])
    mine[KAPPA:, :] = jnp.where(sec == 0, kappas[:16], kappas[16:])


def part_kernel(source, piece, kappa):
    piece[...] = source[:KAPPA, :]
    kappa[...] = source[KAPPA:, :]


VMEM = pl.BlockSpec(memory_space=pltpu.VMEM)
HBM = pl.BlockSpec(memory_space=pltpu.HBM)


def limit(mib):
    return pltpu.CompilerParams(vmem_limit_bytes=mib * 2**20)


def local_part(rhs, guess, kappa, flags):
    operands = (rhs, guess, kappa, flags, jnp.asarray(row_table()))
    return pl.pallas_call(
        local_kernel,
        out_shape=[jax.ShapeDtypeStruct((rows, 128), F32) for rows in (PIECE, KAPPA)],
        in_specs=[HBM] * 5,
        out_specs=[VMEM] * 2,
        scratch_shapes=[pltpu.VMEM(o.shape, o.dtype) for o in operands]
        + [
            pltpu.SemaphoreType.DMA((5,)),
            pltpu.VMEM((224, 160), F32),
            pltpu.VMEM((5 * 224, 128), F32),
            pltpu.VMEM((256, 128), F32),
            pltpu.VMEM((128, 128), F32),
            pltpu.VMEM((64, 128), F32),
        ],
        compiler_params=limit(60),
        cost_estimate=pl.CostEstimate(flops=20_000_000, bytes_accessed=8_000_000, transcendentals=0),
        name="local_part",
    )(*operands)


def part(x):
    return pl.pallas_call(
        part_kernel,
        out_shape=[jax.ShapeDtypeStruct((rows, 128), F32) for rows in (KAPPA, 16)],
        in_specs=[VMEM],
        out_specs=[VMEM] * 2,
        compiler_params=limit(16),
        name="part",
    )(x)


class Level:
    def __init__(self, count, refs):
        self.count = count
        self.x, self.dir, self.res, self.f = refs
        self.tables = [element_matrix(count, d) for d in range(3)]
        self.gains = self.diag = self.jac = None


def tile(index):
    return pl.ds(index * 8, 8)


def rows_of(pieces, size, r, h):
    return pieces[pl.ds(8 * h * size + r, 8, stride=size), :]


ORDER_X = ((3, 2), (2, 3), (1, 1))
ORDER_Y = ((1, 2), (2, 1), (3, 3))
ORDER_REST = ((3, 3), (1, 2), (2, 1))


def partner(bits):
    return jnp.where(lax.axis_index("section") == 0, bits[0], bits[1])


def place_pieces(blocks, order, pieces, first, size, room):
    my_gx, my_gy = lax.axis_index("gx"), lax.axis_index("gy")
    for b, block in enumerate(blocks):
        gy = my_gy ^ partner(order[b - 1]) if b else my_gy
        for a in range(4):
            column = (my_gx ^ a) * 4 + gy
            start = pl.multiple_of(column * room, 8)
            pieces[pl.ds(start, size), :] = block[first + a * size : first + a * size + size, :]


class Lanes:
    def __init__(self):
        self.lane = iota((8, 128), 1)
        sub = iota((8, 128), 0)
        self.group = self.lane // EZ
        self.odd = self.group % 2 == 1
        self.element = self.lane % EZ
        self.place = sub % 4
        self.low_half = sub < 4

    def around(self, u):
        turned = pltpu.roll(u, 4, u.ndim - 2)
        far = jnp.where(self.odd, pltpu.roll(turned, 32, u.ndim - 1), pltpu.roll(turned, 96, u.ndim - 1))
        return turned, far

    def x_before(self, u):
        turned, far = self.around(u)
        return jnp.where(self.low_half, far, turned)

    def x_after(self, u):
        turned, far = self.around(u)
        return jnp.where(self.low_half, turned, far)

    def y_before(self, u):
        return jnp.where(self.place == 0, pltpu.roll(u, 5, 0), pltpu.roll(u, 1, 0))

    def y_after(self, u):
        return jnp.where(self.place == 3, pltpu.roll(u, 3, 0), pltpu.roll(u, 7, 0))

    def z_before(self, u):
        return jnp.where(self.element == 0, pltpu.roll(u, 97, u.ndim - 1), pltpu.roll(u, 1, u.ndim - 1))

    def z_after(self, u):
        last = self.element == EZ - 1
        return jnp.where(last, pltpu.roll(u, 31, u.ndim - 1), pltpu.roll(u, 127, u.ndim - 1))


def load(ref, first, count):
    return ref[pl.ds(first * 8, count * 8), :].reshape(count, 8, 128)


def store(ref, first, value):
    ref[pl.ds(first * 8, value.shape[0] * 8), :] = value.reshape(value.shape[0] * 8, 128)


DIAGS = (0, 250, 304)
GAINS = (320, 326, 332)
REGISTERS = 338
CENTRE = (CHEB_HIGH + CHEB_LOW) / 2.0
RADIUS = (CHEB_HIGH - CHEB_LOW) / 2.0


def flag_lanes(row, slot):
    turned = [row] + [pltpu.roll(row, 32 * m, 1) for m in range(1, 4)]
    return choose(iota(row.shape, 1) // EZ, [turned[(g - 2 * slot - 1) % 4] for g in range(4)])


def line_kernel(first, second, third, own, line, rest, faces, sorted_pieces):
    sorted_pieces[:PIECE, :] = own[...]
    for bits, piece in zip(ORDER_X, (first, second, third)):
        sorted_pieces[pl.ds(pl.multiple_of(partner(bits) * PIECE, 8), PIECE), :] = piece[...]
    pieces = [sorted_pieces.at[PIECE * a : PIECE * a + PIECE, :] for a in range(4)]
    even = lax.axis_index("gx") % 2 == 0
    odd = iota((8, 128), 1) // EZ % 2 == 1
    faces[...] = jnp.zeros_like(faces)

    def both(rows, f):
        side = odd[:1] if f else jnp.logical_not(odd[:1])
        return jnp.where(side, rows, pltpu.roll(rows, 96 if f else 32, 1))

    for a, piece in enumerate(pieces):
        for f in range(2):
            base = 64 * a + 32 * f
            inner = both(piece[FACE_X:KAPPA, :], f)
            ends = [both(piece[HALF:FACE_X, :], g) for g in range(2)]
            for k in range(5):
                r = base + 5 * k
                node = 5 * k + 4 * f
                faces[r : r + 1, :] = ends[0][node : node + 1]
                faces[r + 1 : r + 4, :] = inner[3 * k : 3 * k + 3]
                faces[r + 4 : r + 5, :] = ends[1][node : node + 1]
    for a, piece in enumerate(pieces):
        line[HALF * a : HALF * a + HALF, :] = piece[:HALF, :]
        rest[16 * a : 16 * a + 16, :] = piece[KAPPA:, :]
        rest[REST_Y + 25 * a : REST_Y + 25 * a + 25, :] = piece[HALF:FACE_X, :]
        flags = [flag_lanes(piece[61:62, :], slot) for slot in range(2)]
        gains = [face_gains(flags[d], 0, d, 5) for d in range(2)]
        next_first = even if a % 2 == 0 else jnp.logical_not(even)
        for f in range(2):
            one = faces[64 * (a ^ 1) + 32 * (1 - f) : 64 * (a ^ 1) + 32 * (1 - f) + 32, :]
            three = faces[64 * (a ^ 3) + 32 * (1 - f) : 64 * (a ^ 3) + 32 * (1 - f) + 32, :]
            near = jnp.where(next_first, one, three) if f else jnp.where(next_first, three, one)
            term = gains[f] * near
            for k in range(5):
                node = 25 * k + 20 * f
                side = odd[:5] if node >= HALF else jnp.logical_not(odd[:5])
                r = HALF * a + node % HALF
                line[r : r + 5, :] = line[r : r + 5, :] + jnp.where(side, term[5 * k : 5 * k + 5], 0.0)
    rest[REST_Y + 100 :, :] = jnp.zeros((4, 128), F32)


def halves_kernel(block0, block1, block2, block3, out):
    place_pieces((block0, block1, block2, block3), ORDER_REST, out, 0, 16, 16)


def widen(low, high, odd):
    return jnp.where(odd, pltpu.roll(high, 32, 1), low), jnp.where(odd, high, pltpu.roll(low, 96, 1))


def assemble_kernel(block0, block1, block2, block3, rest0, rest1, rest2, rest3, field, pieces, edges, traces):
    place_pieces((block0, block1, block2, block3), ORDER_Y, pieces, 0, HALF, HALF)
    place_pieces((rest0, rest1, rest2, rest3), ORDER_REST, edges, REST_Y, 25, 32)
    lanes = Lanes()
    for source, size, rows, target, apart in ((edges, 32, 25, traces, 25), (pieces, HALF, HALF, field, HALF)):
        for r in range(rows):
            first, second = widen(rows_of(source, size, r, 0), rows_of(source, size, r, 1), lanes.odd)
            target[tile(r), :] = first
            target[tile(apart + r), :] = second
    got = field[tile(126), :]
    across = pltpu.roll(got, 64, 1)
    gains = [
        face_gains(jnp.where(lanes.lane < 64, got, across), 1, 0, 5),
        face_gains(jnp.where(lanes.lane < 64, across, got), 1, 1, 5),
    ]
    for k in range(5):
        for i in range(5):
            lower, upper = traces[tile(5 * k + i), :], traces[tile(25 + 5 * k + i), :]
            node = 25 * k + 5 * i
            field[tile(node), :] = field[tile(node), :] + gains[0] * lanes.y_before(upper)
            field[tile(node + 4), :] = field[tile(node + 4), :] + gains[1] * lanes.y_after(lower)


def setup_kernel(field, own_halves, other_halves, coefs, kap):
    sec = lax.axis_index("section")
    lanes = Lanes()
    group, lane = lanes.group, lanes.lane
    flags = []
    for r in range(3):
        got = field[tile(125 + r), :]
        across = pltpu.roll(got, 64, 1)
        flags += [jnp.where(lane < 64, got, across), jnp.where(lane < 64, across, got)]
    for r in range(16):
        pairs = [[rows_of(ref, 16, r, h) for h in range(2)] for ref in (own_halves, other_halves)]
        for half in range(2):
            turned = []
            for h in range(2):
                got = jnp.where(sec == half, pairs[0][h], pairs[1][h])
                turned.append([pltpu.roll(got, 32 * m, 1) if m else got for m in range(4)])
            for q in range(4):
                value = choose(group, [turned[g % 2][(g - q) % 4] for g in range(4)])
                kap[tile(q * 32 + half * 16 + r), :] = value
    for p, n in enumerate((5, 3, 2)):
        stride = 4 // (n - 1)
        gains = [face_gains(flags[d], d // 2, d % 2, n) for d in range(6)]
        rows = []
        for d in range(3):
            coefs[tile(GAINS[p] + 2 * d), :] = gains[2 * d]
            coefs[tile(GAINS[p] + 2 * d + 1), :] = gains[2 * d + 1]
            table = element_matrix(n, d)
            row = [jnp.full((8, 128), float(table[m, m]), F32) for m in range(n)]
            row[0] = row[0] + gains[2 * d]
            row[n - 1] = row[n - 1] + gains[2 * d + 1]
            rows.append(row)
        along = jnp.stack(rows[1])
        for k in range(n):
            for i in range(n):
                line = load(kap, k * 25 * stride + i * stride * 5, 5)
                line = jnp.stack([line[j * stride] for j in range(n)])
                value = line + (along + (rows[2][k] + rows[0][i]))
                scale = 1.0 / (1.0 + STEP_SIZE * JACOBI_SCALE * value)
                store(coefs, DIAGS[p] + (k * n + i) * n, value)
                store(coefs, DIAGS[p] + n**3 + (k * n + i) * n, scale * (1.0 / CENTRE))


def cycle_kernel(coefs, assembled, fields, more, *scratch):
    sec = lax.axis_index("section")
    my_gx, my_gy = lax.axis_index("gx"), lax.axis_index("gy")
    levels = [Level(n, scratch[4 * p : 4 * p + 4]) for p, n in enumerate((5, 3, 2))]
    half = scratch[12]
    lanes = Lanes()
    lane = lanes.lane
    blocks = split_sections()[3]

    def lanes_of(upper, lower):
        return jnp.where(lane < 64, jnp.where(sec == 0, upper[0], upper[1]), jnp.where(sec == 0, lower[0], lower[1]))

    entry = [[[float(STEP_SIZE * blocks[2 * p + a, 2 * p + b]) for p in range(2)] for b in range(2)] for a in range(2)]
    same = lanes_of(entry[0][0], entry[1][1])
    swap = lanes_of(entry[0][1], entry[1][0])
    first_rho = RADIUS / CENTRE
    second_rho = 1.0 / (2.0 * CENTRE / RADIUS - first_rho)
    keep = 1.0 + second_rho * first_rho
    push = 2.0 * second_rho / RADIUS * CENTRE
    for p, level in enumerate(levels):
        size = level.count**3
        level.gains = [-coefs[tile(GAINS[p] + d), :] for d in range(6)]
        level.diag = lambda first, count, p=p: load(coefs, DIAGS[p] + first, count)
        level.jac = lambda first, count, p=p, size=size: load(coefs, DIAGS[p] + size + first, count)

    def begin(level, source):
        n = level.count
        for first in range(0, n**3, n):
            f = load(source, first, n)
            store(level.dir, first, level.jac(first, n) * f)
            store(level.res, first, f)
            store(level.x, first, jnp.zeros_like(f))

    def apply(level, smooth):
        n = level.count
        kx, ky, kz = level.tables
        gains = level.gains
        source = level.dir if smooth else level.x
        def tree(terms):
            while len(terms) > 1:
                pairs = [a + b for a, b in zip(terms[::2], terms[1::2])]
                terms = pairs + terms[len(terms) // 2 * 2 :]
            return terms[0]

        def sums(k):
            def line_at(i):
                return load(source, (k * n + i) * n, n)

            x_left = gains[0] * lanes.x_before(line_at(n - 1))
            x_right = gains[1] * lanes.x_after(line_at(0))
            z_low, z_high, y_low, y_high = [], [], [], []
            for i in range(n):
                if k == 0:
                    z_low.append(gains[4] * lanes.z_before(load(source, ((n - 1) * n + i) * n, n)))
                if k == n - 1:
                    z_high.append(gains[5] * lanes.z_after(load(source, i * n, n)))
                v = line_at(i)
                y_low.append(gains[2] * lanes.y_before(v[n - 1]))
                y_high.append(gains[3] * lanes.y_after(v[0]))
            totals = []
            for i in range(n):
                first = (k * n + i) * n
                v = line_at(i)
                along_x = [float(kx[i, m]) * line_at(m) for m in range(n) if m != i]
                along_z = [float(kz[k, m]) * load(source, (m * n + i) * n, n) for m in range(n) if m != k]
                along_y = []
                for j in range(n):
                    terms = [float(ky[j, m]) * v[m] for m in range(n) if m != j]
                    if j == 0:
                        terms.append(y_low[i])
                    if j == n - 1:
                        terms.append(y_high[i])
                    along_y.append(tree(terms))
                if i == 0:
                    along_x.append(x_left)
                if i == n - 1:
                    along_x.append(x_right)
                if k == 0:
                    along_z.append(z_low[i])
                if k == n - 1:
                    along_z.append(z_high[i])
                totals.append(tree([level.diag(first, n) * v, tree(along_x), tree(along_z), jnp.stack(along_y)]))
            return totals

        def update(k, totals):
            moved = [pltpu.roll(total, 64, 2) for total in totals]
            for i in range(n):
                first = (k * n + i) * n
                v = load(source, first, n)
                image = v + (same * totals[i] + swap * moved[i])
                if smooth:
                    scaled = level.jac(first, n) * (load(level.res, first, n) - image)
                    store(level.x, first, (load(level.x, first, n) + keep * v) + push * scaled)
                else:
                    rest = load(level.f, first, n) - image
                    store(level.res, first, rest)
                    store(level.dir, first, level.jac(first, n) * rest)

        if n == 5:
            ready = sums(0)
            for k in range(n):
                following = sums(k + 1) if k + 1 < n else None
                update(k, ready)
                ready = following
        else:
            for k, totals in enumerate([sums(k) for k in range(n)]):
                update(k, totals)

    def combine(weights, parts):
        total = None
        for weight, part in zip(weights, parts):
            if abs(weight) > 1e-14:
                term = part if abs(weight - 1.0) < 1e-14 else float(weight) * part
                total = term if total is None else total + term
        return total

    def change(table, source, target, add):
        m, n = table.shape
        for i in range(n):
            parts = [load(source, i * n + k * n * n, n) for k in range(n)]
            for k in range(m):
                store(half, i * n + k * n * n, combine(table[k], parts))
        for k in range(m):
            parts = [load(half, k * n * n + i * n, n) for i in range(n)]
            for i in range(m):
                line = combine(table[i], parts)
                value = jnp.stack([combine(table[j], [line[a] for a in range(n)]) for j in range(m)])
                first = k * m * m + i * m
                store(target, first, load(target, first, m) + value if add else value)

    def down(n, m):
        fine_nodes, fine_weights = lobatto(n)
        coarse_nodes, coarse_weights = lobatto(m)
        table = lagrange_table(coarse_nodes, fine_nodes)
        return (1.0 / coarse_weights)[:, None] * table.T * fine_weights[None, :]

    def up(m, n):
        return lagrange_table(lobatto(m)[0], lobatto(n)[0])

    def solve(p):
        level = levels[p]
        if p == 2:
            apply(level, True)
            return
        below = levels[p + 1]

        def correct():
            n, m = level.count, below.count
            change(down(n, m), level.res, below.f, False)
            begin(below, below.f)
            solve(p + 1)
            change(up(m, n), below.x, level.x, True)

        if p == 1:
            apply(level, True)
            apply(level, False)
            correct()
            apply(level, False)
            apply(level, True)
            return

        def step(t, carry):
            @pl.when(t != 1)
            def _():
                apply(level, True)

            apply(level, False)

            @pl.when(t == 0)
            def _():
                correct()
            return carry
        lax.fori_loop(0, 3, step, 0)

    fine = levels[0]
    fine.f = assembled
    begin(fine, assembled)
    solve(0)

    for first in range(0, 125, 5):
        part, place = (fields, first) if first < SPLIT else (more, first - SPLIT)
        store(part, place, load(fine.res, first, 5))
    column = (my_gx % 2) * 4 + my_gy
    more[AFTER : AFTER + 125, :] = fine.x[pl.ds(column, 125, stride=8), :]
    more[AFTER + 125 :, :] = jnp.zeros((3, 128), F32)


SPLIT = 75
AFTER = 8 * (125 - SPLIT)


def register(parts, r):
    return parts[0][tile(r), :] if r < SPLIT else parts[1][tile(r - SPLIT), :]


def column_of(parts, k):
    first = 3 * (k // 3)
    return parts[k // 3][column_rows(k - first), :]


def column_z(parts, k):
    return parts[1][AFTER + 25 * k : AFTER + 25 * k + 25, :]


def pair_weights():
    cross = split_sections()[4]
    return jnp.where(iota((8, 128), 1) < 64, float(cross[0]), float(cross[1]))


def column_factors(p):
    sec = lax.axis_index("section")
    whole = split_sections()[0]
    lane = iota((25, 128), 1)
    here = lane // EZ % 2 == lax.axis_index("gx") // 2
    factors = []
    for s in range(2):
        parts = []
        for mine in range(2):
            t = whole[2 * mine + s]
            q = mine if p == 0 else 1 - mine
            parts.append(jnp.where(lane < 64, float(t[2 * q]), float(t[2 * q + 1])))
        factors.append(jnp.where(here, jnp.where(sec == 0, parts[0], parts[1]), 0.0))
    return factors


def column_rows(k):
    column = (lax.axis_index("gx") % 2) * 4 + lax.axis_index("gy")
    return pl.ds(k * 200 + column, 25, stride=8)


def raw_order(k):
    lane = iota((256, 160), 0)
    return (iota((256, 160), 1) == 5 * (lane % EZ) + k + lane // 128).astype(F32)


def side_by_side(cols):
    half = cols.shape[0] // 2
    return jnp.concatenate([cols[:half, :], cols[half:, :]], axis=1)


def early_kernel(own0, own1, own_start, other_start, sums, column_out, cols):
    own = (own0, own1)
    weights = pair_weights()
    cols[...] = jnp.zeros_like(cols)
    total = jnp.zeros((192, 160), F32)
    own_factors, other_factors = column_factors(0), column_factors(1)
    for k in range(5):
        where = column_rows(k)
        z = column_z(own, k)
        start, other = own_start[where, :], other_start[where, :]
        w = start - column_of(own, k)
        side = 192 * (k % 2)
        for s in range(2):
            cols[pl.ds(side + s, 25, stride=2), :] = own_factors[s] * z
            cols[pl.ds(side + 64 + s, 25, stride=2), :] = own_factors[s] * start + other_factors[s] * other
            cols[pl.ds(side + 128 + s, 25, stride=2), :] = own_factors[s] * w
        if k % 2 == 1:
            total = total + split_dot(side_by_side(cols), raw_order(k - 1))
    cols[192:, :] = jnp.zeros((192, 128), F32)
    total = total + split_dot(side_by_side(cols), raw_order(4))
    column_out[...] = total
    nothing = jnp.zeros((8, 128), F32)
    uppers, sizes = [nothing] * 5, [nothing] * 5
    for r in range(125):
        c, d = own_start[tile(r), :], other_start[tile(r), :]
        a = c - register(own, r)
        uppers[r % 5] = uppers[r % 5] + a * (c + weights * d)
        sizes[r % 5] = sizes[r % 5] + ((c * c + d * d) + 2.0 * (weights * (c * d)))
    sums[0:8, :] = sum(uppers)
    sums[8:16, :] = jnp.broadcast_to(jnp.sum(sum(sizes), keepdims=True), (8, 128))


def finish_kernel(own0, own1, other0, other1, own_start, other_start, sums, column, guess, sol, res_out, arnoldi, cols, outs):
    own, other = (own0, own1), (other0, other1)
    cols[...] = jnp.zeros_like(cols)
    total = jnp.zeros((128, 160), F32)
    factors = column_factors(1)
    for k in range(5):
        where = column_rows(k)
        z = column_z(other, k)
        w = other_start[where, :] - column_of(other, k)
        side = 128 * (k % 2)
        for s in range(2):
            cols[pl.ds(side + s, 25, stride=2), :] = factors[s] * z
            cols[pl.ds(side + 64 + s, 25, stride=2), :] = factors[s] * w
        if k % 2 == 1:
            total = total + split_dot(side_by_side(cols), raw_order(k - 1))
    cols[128:, :] = jnp.zeros((128, 128), F32)
    total = total + split_dot(side_by_side(cols), raw_order(4))
    weights = pair_weights()
    nothing = jnp.zeros((8, 128), F32)
    uppers = [nothing] * 5
    for r in range(125):
        c, d = own_start[tile(r), :], other_start[tile(r), :]
        b = d - register(other, r)
        uppers[r % 5] = uppers[r % 5] + b * (d + weights * c)

    mine, theirs = sums[0:8, :], sum(uppers)
    size = sums[8:9, 0:1]
    upper = jnp.sum(mine + theirs, keepdims=True) / size
    rests = [nothing] * 5
    for r in range(125):
        c, d = own_start[tile(r), :], other_start[tile(r), :]
        a = (c - register(own, r)) - upper * c
        b = (d - register(other, r)) - upper * d
        rests[r % 5] = rests[r % 5] + ((a * a + b * b) + 2.0 * (weights * (a * b)))
    rest = jnp.sum(sum(rests), keepdims=True)
    beta = jnp.sqrt(size)
    lower = jnp.sqrt(rest) / beta
    weight = upper / (upper * upper + lower * lower)
    entries = float(125 * EZ * COLS * 4)
    for place_out, value in enumerate((beta * (1.0 / math.sqrt(entries)), upper, lower)):
        arnoldi[place_out] = value[0, 0]
    outs[:64, :] = weight * (column[:64, :] + total[:64])
    outs[64:, :] = column[64:128, :] - weight * (column[128:, :] + total[64:])
    for i in range(5):
        for j in range(5):
            r = 2 * (5 * i + j)
            sol[i, j] = guess[i, j] + outs[r : r + 2, :]
            res_out[i, j] = outs[64 + r : 66 + r, :]


def plain_call(kernel, name, rows, scratch, operands, cost=1_000_000):
    many = isinstance(rows, tuple)
    shapes = [jax.ShapeDtypeStruct((r, 128), F32) for r in (rows if many else (rows,))]
    return pl.pallas_call(
        kernel,
        out_shape=shapes if many else shapes[0],
        in_specs=[VMEM] * len(operands),
        out_specs=[VMEM] * len(shapes) if many else VMEM,
        scratch_shapes=[pltpu.VMEM((r, 128), F32) for r in scratch],
        compiler_params=limit(16),
        cost_estimate=pl.CostEstimate(flops=cost, bytes_accessed=cost, transcendentals=0),
        name=name,
    )(*operands)


def cycle(coefs, assembled):
    scratch = []
    for n in (5, 3, 2):
        scratch += [pltpu.VMEM((n**3 * 8, 128), F32)] * 4
    scratch += [pltpu.VMEM((FIELD, 128), F32)]
    return pl.pallas_call(
        cycle_kernel,
        out_shape=[jax.ShapeDtypeStruct((rows, 128), F32) for rows in (SPLIT * 8, AFTER + 128)],
        in_specs=[VMEM] * 2,
        out_specs=[VMEM] * 2,
        scratch_shapes=scratch,
        compiler_params=limit(24),
        cost_estimate=pl.CostEstimate(flops=40_000_000, bytes_accessed=30_000_000, transcendentals=0),
        name="cycle",
    )(coefs, assembled)


def early(own, own_start, other_start):
    return pl.pallas_call(
        early_kernel,
        out_shape=[jax.ShapeDtypeStruct((16, 128), F32), jax.ShapeDtypeStruct((192, 160), F32)],
        in_specs=[VMEM] * 4,
        out_specs=[VMEM] * 2,
        scratch_shapes=[pltpu.VMEM((384, 128), F32)],
        compiler_params=limit(16),
        cost_estimate=pl.CostEstimate(flops=4_000_000, bytes_accessed=4_000_000, transcendentals=0),
        name="early",
    )(*own, own_start, other_start)


def finish(own, other, own_start, other_start, sums, column, guess):
    return pl.pallas_call(
        finish_kernel,
        out_shape=[
            jax.ShapeDtypeStruct(guess.shape, F32),
            jax.ShapeDtypeStruct(guess.shape, F32),
            jax.ShapeDtypeStruct((3,), F32),
        ],
        in_specs=[VMEM] * 9,
        out_specs=[VMEM, VMEM, pl.BlockSpec(memory_space=pltpu.SMEM)],
        scratch_shapes=[pltpu.VMEM((256, 128), F32), pltpu.VMEM((128, 160), F32)],
        compiler_params=limit(24),
        name="finish",
    )(*own, *other, own_start, other_start, sums, column, guess)


def exchange(x, axis, bits):
    return lax.ppermute(x, axis, [(n, n ^ bits) for n in range(lax.axis_size(axis))])


def exchange_by_core(x, axis, bits):
    count = lax.axis_size(axis)
    pairs = [(s * count + n, s * count + (n ^ bits[s])) for s in range(2) for n in range(count)]
    return lax.ppermute(x, ("section", axis), pairs)


def gathered_body(rhs, guess, kappa, bc_flags):
    rhs, guess = (jnp.transpose(v, (1, 2, 0, 3)) for v in (rhs, guess))
    mine, theirs = local_part(rhs, guess, kappa, bc_flags)
    got, mine, kappa_piece = lax.optimization_barrier((exchange(theirs, "section", 1), *part(mine)))
    piece = jnp.concatenate([mine + got, kappa_piece])
    pieces = [exchange_by_core(piece, "gx", bits) for bits in ORDER_X] + [piece]
    line, rest = plain_call(line_kernel, "line", (LINE, REST), [4 * 64, 4 * PIECE], pieces)
    rests = [rest] + [exchange_by_core(rest, "gy", bits) for bits in ORDER_REST]
    halves = plain_call(halves_kernel, "halves", COLS * 16, [], rests)
    other_halves = exchange(halves, "section", 1)
    blocks = [line] + [exchange_by_core(line, "gy", bits) for bits in ORDER_Y]
    blocks, other_halves = lax.optimization_barrier((blocks, other_halves))
    start = plain_call(
        assemble_kernel, "assemble", 128 * 8, [COLS * HALF, COLS * 32, 50 * 8], blocks + rests, 4_000_000
    )
    coefs = plain_call(setup_kernel, "setup", REGISTERS * 8, [128 * 8], (start, halves, other_halves))
    other_start = exchange(start, "section", 1)
    own, other_start = lax.optimization_barrier((cycle(coefs, start), other_start))
    other = [exchange(part, "section", 1) for part in own]
    sums, column = early(own, start, other_start)
    sol, res, arnoldi = finish(own, other, start, other_start, sums, column, guess)
    sol, res = (jnp.transpose(v, (2, 0, 1, 3)) for v in (sol, res))
    return sol, res, arnoldi


def solution(mesh):
    placed = (
        P("section", "gx", "gy", None),
        P("section", "gx", "gy", None),
        P("gx", "gy", None),
        P(None, "gx", "gy", None),
    )
    sizes = (mesh.shape["section"], mesh.shape["gx"], mesh.shape["gy"])

    def step(rhs, guess, kappa, bc_flags):
        fits = sizes == (2, 4, 4) and rhs.shape == (4, 20, 20, 160)
        return jax.shard_map(
            gathered_body if fits else stepwise,
            mesh=mesh,
            in_specs=placed,
            out_specs=(P("section", "gx", "gy", None), P("section", "gx", "gy", None), P()),
            check_vma=False,
        )(rhs, guess, kappa, bc_flags)

    return step
```

```python
from functools import partial
import math

import jax
import jax.numpy as jnp
import numpy as np
from jax import lax
from jax.experimental import pallas as pl
from jax.experimental.pallas import tpu as pltpu
from jax.sharding import PartitionSpec as P

ADVECT = (1.0, 0.7, 0.5)
DIFFUSE = 0.05
STEP_SIZE = 0.2
JACOBI_SCALE = 0.25
CHEB_LOW = 0.25
CHEB_HIGH = 2.0
LETTERS = "abcdef"


def extended(x, sides, width):
    for axis, dim in sides:
        peers, length = (lax.axis_size(axis), x.shape[dim])
        up = [(i, (i + 1) % peers) for i in range(peers)]
        down = [(j, i) for i, j in up]
        last = lax.slice_in_dim(x, length - width, length, axis=dim)
        leading = lax.slice_in_dim(x, 0, width, axis=dim)
        before = lax.ppermute(last, axis, up)
        after = lax.ppermute(leading, axis, down)
        x = jnp.concatenate([before, x, after], axis=dim)
    return x


def lobatto(count):
    if count == 5:
        inner = math.sqrt(3.0 / 7.0)
        return (
            np.array([-1.0, -inner, 0.0, inner, 1.0]),
            np.array([0.1, 49.0 / 90.0, 32.0 / 45.0, 49.0 / 90.0, 0.1]),
        )
    if count == 3:
        return (np.array([-1.0, 0.0, 1.0]), np.array([1.0 / 3.0, 4.0 / 3.0, 1.0 / 3.0]))
    return (np.array([-1.0, 1.0]), np.array([1.0, 1.0]))


def lagrange_table(nodes, points):
    table = np.ones((len(points), len(nodes)))
    for column in range(len(nodes)):
        for other in range(len(nodes)):
            if other != column:
                table[:, column] *= (points - nodes[other]) / (nodes[column] - nodes[other])
    return table


def slope_table(nodes):
    total = len(nodes)
    factor = np.array(
        [np.prod([nodes[i] - nodes[k] for k in range(total) if k != i]) for i in range(total)]
    )
    table = np.zeros((total, total))
    for row in range(total):
        for column in range(total):
            if row != column:
                table[row, column] = factor[row] / factor[column] / (nodes[row] - nodes[column])
        table[row, row] = -np.sum(table[row])
    return table


def element_matrix(count, direction):
    nodes, weights = lobatto(count)
    slopes = slope_table(nodes)
    stiffness = (1.0 / weights)[:, None] * (slopes.T @ (weights[:, None] * slopes))
    return ADVECT[direction] * slopes + DIFFUSE * stiffness


def legendre_pair(point, order):
    values = [1.0, point]
    slopes = [0.0, 1.0]
    for index in range(1, order):
        values.append(
            ((2 * index + 1) * point * values[index] - index * values[index - 1]) / (index + 1)
        )
        slopes.append(slopes[index - 1] + (2 * index + 1) * values[index])
    return (values, slopes)


def radau_nodes():
    starts = [0.0885879595127039, 0.4094668644407347, 0.7876594617608471]
    found = []
    for start in starts:
        point = start
        for sweep in range(30):
            values, slopes = legendre_pair(2.0 * point - 1.0, 4)
            change = (values[4] - values[3]) / (2.0 * (slopes[4] - slopes[3]))
            point = point - change
        found.append(point)
    found.append(1.0)
    return found


def poly_times(coefs, root):
    result = [0.0] * (len(coefs) + 1)
    for index in range(len(coefs)):
        result[index + 1] += coefs[index]
        result[index] -= root * coefs[index]
    return result


def radau_matrix():
    order = 4
    nodes = radau_nodes()
    matrix = np.zeros((order, order))
    for column in range(order):
        coefs = [1.0]
        denominator = 1.0
        for other in range(order):
            if other != column:
                coefs = poly_times(coefs, nodes[other])
                denominator *= nodes[column] - nodes[other]
        for row in range(order):
            upper_end = nodes[row]
            integral = 0.0
            for index in range(len(coefs)):
                integral += coefs[index] * upper_end ** (index + 1) / (index + 1)
            matrix[row, column] = integral / denominator
    return matrix


def node_einsum(table, field, axis):
    labels = LETTERS[: field.ndim]
    source = labels[: axis + 1] + "j" + labels[axis + 2 :]
    target = labels[: axis + 1] + "i" + labels[axis + 2 :]
    return jnp.einsum(
        "ij," + source + "->" + target,
        jnp.asarray(table, jnp.float32),
        field,
        precision=lax.Precision.HIGHEST,
    )


def apply_along(field, axis, count, table):
    shape = field.shape
    split = shape[:axis] + (shape[axis] // count, count) + shape[axis + 1 :]
    mapped = node_einsum(table, field.reshape(split), axis)
    return mapped.reshape(
        shape[:axis] + (mapped.shape[axis] * mapped.shape[axis + 1],) + shape[axis + 1 :]
    )


def line_part(field, axis, count, table, left_gain, right_gain, left_edge, right_edge):
    shape = field.shape
    elements = shape[axis] // count
    split = field.reshape(shape[:axis] + (elements, count) + shape[axis + 1 :])
    linear = node_einsum(table, split, axis)
    first = lax.index_in_dim(split, 0, axis + 1, keepdims=False)
    last = lax.index_in_dim(split, count - 1, axis + 1, keepdims=False)
    before = jnp.concatenate(
        [jnp.expand_dims(left_edge, axis), lax.slice_in_dim(last, 0, elements - 1, axis=axis)], axis
    )
    after = jnp.concatenate(
        [lax.slice_in_dim(first, 1, elements, axis=axis), jnp.expand_dims(right_edge, axis)], axis
    )
    front = jnp.expand_dims(left_gain * (first - before), axis + 1)
    back = jnp.expand_dims(right_gain * (last - after), axis + 1)
    if count > 2:
        middle_shape = list(front.shape)
        middle_shape[axis + 1] = count - 2
        pieces = [front, jnp.zeros(middle_shape, jnp.float32), back]
    else:
        pieces = [front, back]
    return (linear + jnp.concatenate(pieces, axis + 1)).reshape(shape)


def diag_along(shape, axis, count, table, left_gain, right_gain):
    elements = shape[axis] // count
    split = shape[:axis] + (elements, count) + shape[axis + 1 :]
    profile = [1] * len(split)
    profile[axis + 1] = count
    diagonal_entries = np.array([table[index, index] for index in range(count)])
    base = jnp.broadcast_to(jnp.asarray(diagonal_entries, jnp.float32).reshape(profile), split)
    front = jnp.expand_dims(left_gain, axis + 1)
    back = jnp.expand_dims(right_gain, axis + 1)
    if count > 2:
        middle_shape = list(front.shape)
        middle_shape[axis + 1] = count - 2
        pieces = [front, jnp.zeros(middle_shape, jnp.float32), back]
    else:
        pieces = [front, back]
    return (base + jnp.concatenate(pieces, axis + 1)).reshape(shape)


def level_kappa(kappa, count):
    if count == 5:
        return kappa
    picks = np.array([0, 2, 4]) if count == 3 else np.array([0, 4])
    extents = [extent // 5 for extent in kappa.shape]
    grouped = kappa.reshape(extents[0], 5, extents[1], 5, extents[2], 5)
    for axis in (1, 3, 5):
        grouped = jnp.take(grouped, picks, axis=axis)
    return grouped.reshape(extents[0] * count, extents[1] * count, extents[2] * count)


def face_plane(face, direction, count):
    plane = face.astype(jnp.float32)
    for axis in range(3):
        if axis != direction:
            plane = jnp.repeat(plane, count, axis=axis)
    return plane


def build_level(kappa, flags, count):
    nodes, weights = lobatto(count)
    kappa_level = level_kappa(kappa, count)
    tables, lefts, rights = ([], [], [])
    diagonal = kappa_level
    for direction in range(3):
        table = element_matrix(count, direction)
        lower = face_plane(flags[2 * direction], direction, count)
        upper = face_plane(flags[2 * direction + 1], direction, count)
        left_gain = (ADVECT[direction] * (1.0 + lower) / 2.0 + DIFFUSE * count * count) / float(
            weights[0]
        )
        right_gain = (DIFFUSE * count * count - ADVECT[direction] * (1.0 - upper) / 2.0) / float(
            weights[-1]
        )
        tables.append(table)
        lefts.append(left_gain)
        rights.append(right_gain)
        diagonal = diagonal + diag_along(
            kappa_level.shape, direction, count, table, left_gain, right_gain
        )
    scale = 1.0 / (1.0 + STEP_SIZE * JACOBI_SCALE * diagonal)
    return (count, tables, lefts, rights, kappa_level, scale)


def restrict(field, fine_count, coarse_count):
    fine_nodes, fine_weights = lobatto(fine_count)
    coarse_nodes, coarse_weights = lobatto(coarse_count)
    table = (
        (1.0 / coarse_weights)[:, None]
        * lagrange_table(coarse_nodes, fine_nodes).T
        * fine_weights[None, :]
    )
    for axis in range(field.ndim - 3, field.ndim):
        field = apply_along(field, axis, fine_count, table)
    return field


def prolong(field, coarse_count, fine_count):
    fine_nodes, fine_weights = lobatto(fine_count)
    coarse_nodes, coarse_weights = lobatto(coarse_count)
    table = lagrange_table(coarse_nodes, fine_nodes)
    for axis in range(field.ndim - 3, field.ndim):
        field = apply_along(field, axis, coarse_count, table)
    return field


def chebyshev(rhs, start, level, operator):
    centre = (CHEB_HIGH + CHEB_LOW) / 2.0
    radius = (CHEB_HIGH - CHEB_LOW) / 2.0
    ratio = centre / radius
    first_rho = 1.0 / ratio
    second_rho = 1.0 / (2.0 * ratio - first_rho)
    scale = level[5]
    if start is None:
        remain = rhs
    else:
        remain = rhs - operator(start, level)
    step = scale * remain / centre
    guess = step if start is None else start + step
    remain = remain - operator(step, level)
    step = second_rho * first_rho * step + 2.0 * second_rho / radius * scale * remain
    return guess + step


def vcycle(rhs, levels, operator):
    fine, middle, coarse = levels
    fine_x = chebyshev(rhs, None, fine, operator)
    middle_rhs = restrict(rhs - operator(fine_x, fine), 5, 3)
    middle_x = chebyshev(middle_rhs, None, middle, operator)
    coarse_rhs = restrict(middle_rhs - operator(middle_x, middle), 3, 2)
    coarse_x = chebyshev(coarse_rhs, None, coarse, operator)
    middle_x = chebyshev(middle_rhs, middle_x + prolong(coarse_x, 2, 3), middle, operator)
    return chebyshev(rhs, fine_x + prolong(middle_x, 3, 5), fine, operator)


def spatial(field, level):
    count, tables, lefts, rights, kappa_level, scale = level
    padded = extended(field, (("gx", 1), ("gy", 2)), 1)
    total = kappa_level * field
    total = total + line_part(
        field,
        1,
        count,
        tables[0],
        lefts[0],
        rights[0],
        padded[:, 0, 1:-1, :],
        padded[:, -1, 1:-1, :],
    )
    total = total + line_part(
        field,
        2,
        count,
        tables[1],
        lefts[1],
        rights[1],
        padded[:, 1:-1, 0, :],
        padded[:, 1:-1, -1, :],
    )
    total = total + line_part(
        field, 3, count, tables[2], lefts[2], rights[2], field[:, :, :, -1], field[:, :, :, 0]
    )
    return total


def apply_system(field, level, coupling):
    image = spatial(field, level)
    everyone = lax.all_gather(image, "section", axis=0, tiled=True)
    butcher = jnp.asarray(radau_matrix(), jnp.float32)
    rows = lax.dynamic_slice_in_dim(
        butcher, lax.axis_index("section") * field.shape[0], field.shape[0], 0
    )
    mixed = jnp.einsum("ij,jabc->iabc", rows, everyone, precision=lax.Precision.HIGHEST)
    return field + STEP_SIZE * mixed


def global_total(values):
    return lax.psum(values, ("section", "gx", "gy"))


def stepwise(rhs, guess, kappa, bc_flags):
    levels = [build_level(kappa, bc_flags, count) for count in (5, 3, 2)]
    section_operator = partial(apply_system, coupling=None)
    start_residual = rhs - section_operator(guess, levels[0])
    dofs = float(rhs.size * lax.axis_size("section") * lax.axis_size("gx") * lax.axis_size("gy"))
    beta = jnp.sqrt(global_total(jnp.sum(start_residual * start_residual).reshape(1))[0])
    basis = start_residual / beta
    precond = vcycle(basis, levels, section_operator)
    image = section_operator(precond, levels[0])
    upper = global_total(jnp.sum(image * basis).reshape(1))[0]
    remainder = image - upper * basis
    lower = jnp.sqrt(global_total(jnp.sum(remainder * remainder).reshape(1))[0])
    weight = beta * upper / (upper * upper + lower * lower)
    solution = guess + weight * precond
    residual = start_residual - weight * image
    arnoldi = jnp.stack([beta / math.sqrt(dofs), upper, lower]).astype(jnp.float32)
    return (solution, residual, arnoldi)


EZ = 32
COLS = 16
HALF = 64
FACE_X = HALF + 25
KAPPA = FACE_X + 15
PIECE = KAPPA + 16
LINE = 4 * HALF
REST_Y = 4 * 16
REST = REST_Y + 104
FIELD = 1000
F32 = jnp.float32


def split_sections():
    matrix = radau_matrix()
    values, vectors = np.linalg.eig(matrix)
    order = [n for n in np.argsort(np.abs(values.imag), kind="stable") if values[n].imag > 0]
    bases = []
    for n in order:
        plane = np.stack([vectors[:, n].real, vectors[:, n].imag], axis=1)
        bases.append(np.linalg.qr(plane)[0])
    left, cross, right = np.linalg.svd(bases[0].T @ bases[1])
    bases = [bases[0] @ left, bases[1] @ right.T]
    for c in range(2):
        sign = np.sign(bases[0][np.argmax(np.abs(bases[0][:, c])), c])
        bases = [np.concatenate([b[:, :c], sign * b[:, c : c + 1], b[:, c + 1 :]], axis=1) for b in bases]
    whole = np.concatenate(bases, axis=1)
    back = np.linalg.inv(whole)
    return whole, back, back @ matrix, back @ matrix @ whole, cross


def iota(shape, dim):
    return lax.broadcasted_iota(jnp.int32, shape, dim)


def exact_dot(a, b):
    return lax.dot_general(
        a, b, (((1,), (0,)), ((), ())), precision=lax.Precision.HIGHEST, preferred_element_type=F32
    )


def split_dot(a, b):
    high = a.astype(jnp.bfloat16)
    rest = a - high.astype(F32)
    middle = rest.astype(jnp.bfloat16)
    low = (rest - middle.astype(F32)).astype(jnp.bfloat16)
    b = b.astype(jnp.bfloat16)
    return sum(
        lax.dot_general(part, b, (((1,), (0,)), ((), ())), preferred_element_type=F32)
        for part in (low, middle, high)
    )


def choose(index, values):
    out = values[-1]
    for place in range(len(values) - 2, -1, -1):
        out = jnp.where(index == place, values[place], out)
    return out


def face_gains(flag, direction, side, count):
    nodes, weights = lobatto(count)
    c, nu = ADVECT[direction], DIFFUSE * count * count
    if side == 0:
        return (c * (1.0 + flag) / 2.0 + nu) * (1.0 / float(weights[0]))
    return (nu - c * (1.0 - flag) / 2.0) * (1.0 / float(weights[-1]))


def row_table():
    kx, ky = (element_matrix(5, d) for d in range(2))
    rows = np.zeros((64, 64))
    for s in range(2):
        for i in range(5):
            for j in range(5):
                r = 2 * (i * 5 + j) + s
                for m in range(5):
                    rows[r, 2 * (m * 5 + j) + s] += kx[i, m]
                    rows[r, 2 * (i * 5 + m) + s] += ky[j, m]
    return rows.astype(np.float32)


def pick_lines(k):
    lane = iota((160, 256), 1)
    return (iota((160, 256), 0) == 5 * (lane % EZ) + k + lane // 128).astype(F32)


def pair_factors(sec, table, own, s):
    upper = iota((32, 128), 1) < 64
    first = jnp.where(upper, float(table[0, s]), float(table[1, s]))
    second = jnp.where(upper, float(table[2, 2 + s]), float(table[3, 2 + s]))
    if not own:
        first = jnp.where(upper, float(table[2, s]), float(table[3, s]))
        second = jnp.where(upper, float(table[0, 2 + s]), float(table[1, 2 + s]))
    return jnp.where(sec == 0, first, second)


def pack_nodes(nodes):
    half = nodes.shape[0] // 2
    odd = iota((half, 128), 1) // EZ % 2 == 1
    return jnp.where(odd, nodes[half:, :], nodes[:half, :])


def local_kernel(
    rhs_in, guess_in, kappa_in, flags_in, rows_in, mine, theirs,
    rhs, guess, kappa, flags, rows_t, sems, stack, lines, nodes, y_faces, x_faces,
):
    sec = lax.axis_index("section")
    pairs = [(guess_in, guess), (rhs_in, rhs), (rows_in, rows_t), (kappa_in, kappa), (flags_in, flags)]
    copies = [pltpu.make_async_copy(source, target, sems.at[n]) for n, (source, target) in enumerate(pairs)]
    for copy in copies:
        copy.start()
    for ref in (stack, nodes, y_faces, x_faces):
        ref[...] = jnp.zeros_like(ref)
    for copy in copies:
        copy.wait()
    for i in range(5):
        stack[192 + 5 * i : 197 + 5 * i, :] = kappa[i]
        for j in range(5):
            r = 2 * (5 * i + j)
            value = guess[i, j]
            stack[128 + r : 130 + r, :] = value
            stack[r : r + 2, :] = rhs[i, j] - value
    stack[64:128, :] = exact_dot(rows_t[...], stack[128:192, :])
    source = stack[...]
    for k in (0, 2, 4):
        shown = split_dot(source, pick_lines(k))
        lines[224 * k : 224 * k + 224, :] = shown[:, :128]
        if k < 4:
            lines[224 * k + 224 : 224 * k + 448, :] = shown[:, 128:]

    def part(k, first, s):
        return lines[pl.ds(224 * k + first + s, 32, stride=2), :]

    def kappa_part(k):
        return lines[224 * k + 192 : 224 * k + 224, :]

    repeat = (iota((EZ, 128), 1) % EZ == iota((EZ, 128), 0)).astype(F32)
    shown = split_dot(flags[:, 0, 0, :].astype(F32), repeat)
    gains = [face_gains(shown[d : d + 1, :], d // 2, d % 2, 5) for d in range(6)]
    row = iota((32, 128), 0)
    none = jnp.zeros((32, 128), F32)
    own = jnp.where(row < 5, gains[0], jnp.where((row >= 20) & (row < 25), gains[1], none))
    own = own + jnp.where(row % 5 == 0, gains[2], jnp.where(row % 5 == 4, gains[3], none))
    kz = element_matrix(5, 2)
    back, back_matrix = split_sections()[1:3]
    fields = [[part(k, 128, s) for k in range(5)] for s in range(2)]
    for k in range(5):
        diagonal = kappa_part(k) + own
        if k == 0:
            diagonal = diagonal + gains[4]
        if k == 4:
            diagonal = diagonal + gains[5]
        images = []
        for s in range(2):
            image = diagonal * fields[s][k] + part(k, 64, s)
            for m in range(5):
                image = image + float(kz[k, m]) * fields[s][m]
            if k == 0:
                image = image - gains[4] * pltpu.roll(fields[s][4], 1, 1)
            if k == 4:
                image = image - gains[5] * pltpu.roll(fields[s][0], 127, 1)
            images.append(image)
        for p, mark in enumerate((True, False)):
            total = jnp.zeros((32, 128), F32)
            trace = jnp.zeros((32, 128), F32)
            for s in range(2):
                total = total + pair_factors(sec, back, mark, s) * part(k, 0, s)
                factor = pair_factors(sec, STEP_SIZE * back_matrix, mark, s)
                total = total - factor * images[s]
                trace = trace + factor * fields[s][k]
            nodes[128 * p + 25 * k : 128 * p + 25 * k + 25, :] = total[:25]
            for i in range(5):
                for f in range(2):
                    r = 64 * p + 32 * f + 5 * k + i
                    y_faces[r : r + 1, :] = trace[5 * i + 4 * f : 5 * i + 4 * f + 1]
            for f in range(2):
                r = 32 * p + 16 * f + 3 * k
                x_faces[r : r + 3, :] = trace[20 * f + 1 : 20 * f + 4]
    upper = iota((1, 128), 1) < 64
    for r in range(3):
        nodes[125 + r : 126 + r, :] = jnp.where(upper, shown[2 * r : 2 * r + 1], shown[2 * r + 1 : 2 * r + 2])
    for p, out in enumerate((mine, theirs)):
        out[:HALF, :] = pack_nodes(nodes[128 * p : 128 * p + 128, :])
        out[HALF:FACE_X, :] = pack_nodes(y_faces[64 * p : 64 * p + 64, :])[:25]
        out[FACE_X:KAPPA, :] = pack_nodes(x_faces[32 * p : 32 * p + 32, :])[:15]
    for k in range(5):
        nodes[25 * k : 25 * k + 25, :] = kappa_part(k)[:25]
    kappas = choose(iota((32, 128), 1) // EZ, [nodes[32 * q : 32 * q + 32, :] for q in range(4)])
    mine[KAPPA:, :] = jnp.where(sec == 0, kappas[:16], kappas[16:])


def part_kernel(source, piece, kappa):
    piece[...] = source[:KAPPA, :]
    kappa[...] = source[KAPPA:, :]


VMEM = pl.BlockSpec(memory_space=pltpu.VMEM)
HBM = pl.BlockSpec(memory_space=pltpu.HBM)


def limit(mib):
    return pltpu.CompilerParams(vmem_limit_bytes=mib * 2**20)


def local_part(rhs, guess, kappa, flags):
    operands = (rhs, guess, kappa, flags, jnp.asarray(row_table()))
    return pl.pallas_call(
        local_kernel,
        out_shape=[jax.ShapeDtypeStruct((rows, 128), F32) for rows in (PIECE, KAPPA)],
        in_specs=[HBM] * 5,
        out_specs=[VMEM] * 2,
        scratch_shapes=[pltpu.VMEM(o.shape, o.dtype) for o in operands]
        + [
            pltpu.SemaphoreType.DMA((5,)),
            pltpu.VMEM((224, 160), F32),
            pltpu.VMEM((5 * 224, 128), F32),
            pltpu.VMEM((256, 128), F32),
            pltpu.VMEM((128, 128), F32),
            pltpu.VMEM((64, 128), F32),
        ],
        compiler_params=limit(60),
        cost_estimate=pl.CostEstimate(flops=20_000_000, bytes_accessed=8_000_000, transcendentals=0),
        name="local_part",
    )(*operands)


def part(x):
    return pl.pallas_call(
        part_kernel,
        out_shape=[jax.ShapeDtypeStruct((rows, 128), F32) for rows in (KAPPA, 16)],
        in_specs=[VMEM],
        out_specs=[VMEM] * 2,
        compiler_params=limit(16),
        name="part",
    )(x)


class Level:
    def __init__(self, count, refs):
        self.count = count
        self.x, self.dir, self.res, self.f = refs
        self.tables = [element_matrix(count, d) for d in range(3)]
        self.gains = self.diag = self.jac = None


def tile(index):
    return pl.ds(index * 8, 8)


def rows_of(pieces, size, r, h):
    return pieces[pl.ds(8 * h * size + r, 8, stride=size), :]


ORDER_X = ((3, 2), (2, 3), (1, 1))
ORDER_Y = ((3, 3), (1, 2), (2, 1))


def partner(bits):
    return jnp.where(lax.axis_index("section") == 0, bits[0], bits[1])


def place_pieces(blocks, pieces, first, size, room):
    my_gx, my_gy = lax.axis_index("gx"), lax.axis_index("gy")
    for b, block in enumerate(blocks):
        gy = my_gy ^ partner(ORDER_Y[b - 1]) if b else my_gy
        for a in range(4):
            column = (my_gx ^ a) * 4 + gy
            start = pl.multiple_of(column * room, 8)
            pieces[pl.ds(start, size), :] = block[first + a * size : first + a * size + size, :]


class Lanes:
    def __init__(self):
        self.lane = iota((8, 128), 1)
        sub = iota((8, 128), 0)
        self.group = self.lane // EZ
        self.odd = self.group % 2 == 1
        self.element = self.lane % EZ
        self.place = sub % 4
        self.low_half = sub < 4

    def around(self, u):
        turned = pltpu.roll(u, 4, u.ndim - 2)
        far = jnp.where(self.odd, pltpu.roll(turned, 32, u.ndim - 1), pltpu.roll(turned, 96, u.ndim - 1))
        return turned, far

    def x_before(self, u):
        turned, far = self.around(u)
        return jnp.where(self.low_half, far, turned)

    def x_after(self, u):
        turned, far = self.around(u)
        return jnp.where(self.low_half, turned, far)

    def y_before(self, u):
        return jnp.where(self.place == 0, pltpu.roll(u, 5, 0), pltpu.roll(u, 1, 0))

    def y_after(self, u):
        return jnp.where(self.place == 3, pltpu.roll(u, 3, 0), pltpu.roll(u, 7, 0))

    def z_before(self, u):
        return jnp.where(self.element == 0, pltpu.roll(u, 97, u.ndim - 1), pltpu.roll(u, 1, u.ndim - 1))

    def z_after(self, u):
        last = self.element == EZ - 1
        return jnp.where(last, pltpu.roll(u, 31, u.ndim - 1), pltpu.roll(u, 127, u.ndim - 1))


def load(ref, first, count):
    return ref[pl.ds(first * 8, count * 8), :].reshape(count, 8, 128)


def store(ref, first, value):
    ref[pl.ds(first * 8, value.shape[0] * 8), :] = value.reshape(value.shape[0] * 8, 128)


DIAGS = (0, 250, 304)
GAINS = (320, 326, 332)
REGISTERS = 338
CENTRE = (CHEB_HIGH + CHEB_LOW) / 2.0
RADIUS = (CHEB_HIGH - CHEB_LOW) / 2.0


def flag_lanes(row, slot):
    turned = [row] + [pltpu.roll(row, 32 * m, 1) for m in range(1, 4)]
    return choose(iota(row.shape, 1) // EZ, [turned[(g - 2 * slot - 1) % 4] for g in range(4)])


def line_kernel(first, second, third, own, line, rest, faces, sorted_pieces):
    sorted_pieces[:PIECE, :] = own[...]
    for bits, piece in zip(ORDER_X, (first, second, third)):
        sorted_pieces[pl.ds(pl.multiple_of(partner(bits) * PIECE, 8), PIECE), :] = piece[...]
    pieces = [sorted_pieces.at[PIECE * a : PIECE * a + PIECE, :] for a in range(4)]
    even = lax.axis_index("gx") % 2 == 0
    odd = iota((8, 128), 1) // EZ % 2 == 1
    faces[...] = jnp.zeros_like(faces)

    def both(rows, f):
        side = odd[:1] if f else jnp.logical_not(odd[:1])
        return jnp.where(side, rows, pltpu.roll(rows, 96 if f else 32, 1))

    for a, piece in enumerate(pieces):
        for f in range(2):
            base = 64 * a + 32 * f
            inner = both(piece[FACE_X:KAPPA, :], f)
            ends = [both(piece[HALF:FACE_X, :], g) for g in range(2)]
            for k in range(5):
                r = base + 5 * k
                node = 5 * k + 4 * f
                faces[r : r + 1, :] = ends[0][node : node + 1]
                faces[r + 1 : r + 4, :] = inner[3 * k : 3 * k + 3]
                faces[r + 4 : r + 5, :] = ends[1][node : node + 1]
    for a, piece in enumerate(pieces):
        line[HALF * a : HALF * a + HALF, :] = piece[:HALF, :]
        rest[16 * a : 16 * a + 16, :] = piece[KAPPA:, :]
        rest[REST_Y + 25 * a : REST_Y + 25 * a + 25, :] = piece[HALF:FACE_X, :]
        flags = [flag_lanes(piece[61:62, :], slot) for slot in range(2)]
        gains = [face_gains(flags[d], 0, d, 5) for d in range(2)]
        next_first = even if a % 2 == 0 else jnp.logical_not(even)
        for f in range(2):
            one = faces[64 * (a ^ 1) + 32 * (1 - f) : 64 * (a ^ 1) + 32 * (1 - f) + 32, :]
            three = faces[64 * (a ^ 3) + 32 * (1 - f) : 64 * (a ^ 3) + 32 * (1 - f) + 32, :]
            near = jnp.where(next_first, one, three) if f else jnp.where(next_first, three, one)
            term = gains[f] * near
            for k in range(5):
                node = 25 * k + 20 * f
                side = odd[:5] if node >= HALF else jnp.logical_not(odd[:5])
                r = HALF * a + node % HALF
                line[r : r + 5, :] = line[r : r + 5, :] + jnp.where(side, term[5 * k : 5 * k + 5], 0.0)
    rest[REST_Y + 100 :, :] = jnp.zeros((4, 128), F32)


def halves_kernel(block0, block1, block2, block3, out):
    place_pieces((block0, block1, block2, block3), out, 0, 16, 16)


def widen(low, high, odd):
    return jnp.where(odd, pltpu.roll(high, 32, 1), low), jnp.where(odd, high, pltpu.roll(low, 96, 1))


def assemble_kernel(block0, block1, block2, block3, rest0, rest1, rest2, rest3, field, pieces, edges, traces):
    place_pieces((block0, block1, block2, block3), pieces, 0, HALF, HALF)
    place_pieces((rest0, rest1, rest2, rest3), edges, REST_Y, 25, 32)
    lanes = Lanes()
    for source, size, rows, target, apart in ((edges, 32, 25, traces, 25), (pieces, HALF, HALF, field, HALF)):
        for r in range(rows):
            first, second = widen(rows_of(source, size, r, 0), rows_of(source, size, r, 1), lanes.odd)
            target[tile(r), :] = first
            target[tile(apart + r), :] = second
    got = field[tile(126), :]
    across = pltpu.roll(got, 64, 1)
    gains = [
        face_gains(jnp.where(lanes.lane < 64, got, across), 1, 0, 5),
        face_gains(jnp.where(lanes.lane < 64, across, got), 1, 1, 5),
    ]
    for k in range(5):
        for i in range(5):
            lower, upper = traces[tile(5 * k + i), :], traces[tile(25 + 5 * k + i), :]
            node = 25 * k + 5 * i
            field[tile(node), :] = field[tile(node), :] + gains[0] * lanes.y_before(upper)
            field[tile(node + 4), :] = field[tile(node + 4), :] + gains[1] * lanes.y_after(lower)


def setup_kernel(field, own_halves, other_halves, coefs, kap):
    sec = lax.axis_index("section")
    lanes = Lanes()
    group, lane = lanes.group, lanes.lane
    flags = []
    for r in range(3):
        got = field[tile(125 + r), :]
        across = pltpu.roll(got, 64, 1)
        flags += [jnp.where(lane < 64, got, across), jnp.where(lane < 64, across, got)]
    for r in range(16):
        pairs = [[rows_of(ref, 16, r, h) for h in range(2)] for ref in (own_halves, other_halves)]
        for half in range(2):
            turned = []
            for h in range(2):
                got = jnp.where(sec == half, pairs[0][h], pairs[1][h])
                turned.append([pltpu.roll(got, 32 * m, 1) if m else got for m in range(4)])
            for q in range(4):
                value = choose(group, [turned[g % 2][(g - q) % 4] for g in range(4)])
                kap[tile(q * 32 + half * 16 + r), :] = value
    for p, n in enumerate((5, 3, 2)):
        stride = 4 // (n - 1)
        gains = [face_gains(flags[d], d // 2, d % 2, n) for d in range(6)]
        rows = []
        for d in range(3):
            coefs[tile(GAINS[p] + 2 * d), :] = gains[2 * d]
            coefs[tile(GAINS[p] + 2 * d + 1), :] = gains[2 * d + 1]
            table = element_matrix(n, d)
            row = [jnp.full((8, 128), float(table[m, m]), F32) for m in range(n)]
            row[0] = row[0] + gains[2 * d]
            row[n - 1] = row[n - 1] + gains[2 * d + 1]
            rows.append(row)
        along = jnp.stack(rows[1])
        for k in range(n):
            for i in range(n):
                line = load(kap, k * 25 * stride + i * stride * 5, 5)
                line = jnp.stack([line[j * stride] for j in range(n)])
                value = line + (along + (rows[2][k] + rows[0][i]))
                scale = 1.0 / (1.0 + STEP_SIZE * JACOBI_SCALE * value)
                store(coefs, DIAGS[p] + (k * n + i) * n, value)
                store(coefs, DIAGS[p] + n**3 + (k * n + i) * n, scale * (1.0 / CENTRE))


def cycle_kernel(coefs, assembled, fields, more, *scratch):
    sec = lax.axis_index("section")
    my_gx, my_gy = lax.axis_index("gx"), lax.axis_index("gy")
    levels = [Level(n, scratch[4 * p : 4 * p + 4]) for p, n in enumerate((5, 3, 2))]
    half = scratch[12]
    lanes = Lanes()
    lane = lanes.lane
    blocks = split_sections()[3]

    def lanes_of(upper, lower):
        return jnp.where(lane < 64, jnp.where(sec == 0, upper[0], upper[1]), jnp.where(sec == 0, lower[0], lower[1]))

    entry = [[[float(STEP_SIZE * blocks[2 * p + a, 2 * p + b]) for p in range(2)] for b in range(2)] for a in range(2)]
    same = lanes_of(entry[0][0], entry[1][1])
    swap = lanes_of(entry[0][1], entry[1][0])
    first_rho = RADIUS / CENTRE
    second_rho = 1.0 / (2.0 * CENTRE / RADIUS - first_rho)
    keep = 1.0 + second_rho * first_rho
    push = 2.0 * second_rho / RADIUS * CENTRE
    for p, level in enumerate(levels):
        size = level.count**3
        level.gains = [-coefs[tile(GAINS[p] + d), :] for d in range(6)]
        level.diag = lambda first, count, p=p: load(coefs, DIAGS[p] + first, count)
        level.jac = lambda first, count, p=p, size=size: load(coefs, DIAGS[p] + size + first, count)

    def begin(level, source):
        n = level.count
        for first in range(0, n**3, n):
            f = load(source, first, n)
            store(level.dir, first, level.jac(first, n) * f)
            store(level.res, first, f)
            store(level.x, first, jnp.zeros_like(f))

    def apply(level, smooth):
        n = level.count
        kx, ky, kz = level.tables
        gains = level.gains
        source = level.dir if smooth else level.x
        def tree(terms):
            while len(terms) > 1:
                pairs = [a + b for a, b in zip(terms[::2], terms[1::2])]
                terms = pairs + terms[len(terms) // 2 * 2 :]
            return terms[0]

        def sums(k):
            def line_at(i):
                return load(source, (k * n + i) * n, n)

            x_left = gains[0] * lanes.x_before(line_at(n - 1))
            x_right = gains[1] * lanes.x_after(line_at(0))
            z_low, z_high, y_low, y_high = [], [], [], []
            for i in range(n):
                if k == 0:
                    z_low.append(gains[4] * lanes.z_before(load(source, ((n - 1) * n + i) * n, n)))
                if k == n - 1:
                    z_high.append(gains[5] * lanes.z_after(load(source, i * n, n)))
                v = line_at(i)
                y_low.append(gains[2] * lanes.y_before(v[n - 1]))
                y_high.append(gains[3] * lanes.y_after(v[0]))
            totals = []
            for i in range(n):
                first = (k * n + i) * n
                v = line_at(i)
                along_x = [float(kx[i, m]) * line_at(m) for m in range(n) if m != i]
                along_z = [float(kz[k, m]) * load(source, (m * n + i) * n, n) for m in range(n) if m != k]
                along_y = []
                for j in range(n):
                    terms = [float(ky[j, m]) * v[m] for m in range(n) if m != j]
                    if j == 0:
                        terms.append(y_low[i])
                    if j == n - 1:
                        terms.append(y_high[i])
                    along_y.append(tree(terms))
                if i == 0:
                    along_x.append(x_left)
                if i == n - 1:
                    along_x.append(x_right)
                if k == 0:
                    along_z.append(z_low[i])
                if k == n - 1:
                    along_z.append(z_high[i])
                totals.append(tree([level.diag(first, n) * v, tree(along_x), tree(along_z), jnp.stack(along_y)]))
            return totals

        def update(k, totals):
            moved = [pltpu.roll(total, 64, 2) for total in totals]
            for i in range(n):
                first = (k * n + i) * n
                v = load(source, first, n)
                image = v + (same * totals[i] + swap * moved[i])
                if smooth:
                    scaled = level.jac(first, n) * (load(level.res, first, n) - image)
                    store(level.x, first, (load(level.x, first, n) + keep * v) + push * scaled)
                else:
                    rest = load(level.f, first, n) - image
                    store(level.res, first, rest)
                    store(level.dir, first, level.jac(first, n) * rest)

        if n == 5:
            ready = sums(0)
            for k in range(n):
                following = sums(k + 1) if k + 1 < n else None
                update(k, ready)
                ready = following
        else:
            for k, totals in enumerate([sums(k) for k in range(n)]):
                update(k, totals)

    def combine(weights, parts):
        total = None
        for weight, part in zip(weights, parts):
            if abs(weight) > 1e-14:
                term = part if abs(weight - 1.0) < 1e-14 else float(weight) * part
                total = term if total is None else total + term
        return total

    def change(table, source, target, add):
        m, n = table.shape
        for i in range(n):
            parts = [load(source, i * n + k * n * n, n) for k in range(n)]
            for k in range(m):
                store(half, i * n + k * n * n, combine(table[k], parts))
        for k in range(m):
            parts = [load(half, k * n * n + i * n, n) for i in range(n)]
            for i in range(m):
                line = combine(table[i], parts)
                value = jnp.stack([combine(table[j], [line[a] for a in range(n)]) for j in range(m)])
                first = k * m * m + i * m
                store(target, first, load(target, first, m) + value if add else value)

    def down(n, m):
        fine_nodes, fine_weights = lobatto(n)
        coarse_nodes, coarse_weights = lobatto(m)
        table = lagrange_table(coarse_nodes, fine_nodes)
        return (1.0 / coarse_weights)[:, None] * table.T * fine_weights[None, :]

    def up(m, n):
        return lagrange_table(lobatto(m)[0], lobatto(n)[0])

    def solve(p):
        level = levels[p]
        if p == 2:
            apply(level, True)
            return
        below = levels[p + 1]

        def correct():
            n, m = level.count, below.count
            change(down(n, m), level.res, below.f, False)
            begin(below, below.f)
            solve(p + 1)
            change(up(m, n), below.x, level.x, True)

        if p == 1:
            apply(level, True)
            apply(level, False)
            correct()
            apply(level, False)
            apply(level, True)
            return

        def step(t, carry):
            @pl.when(t != 1)
            def _():
                apply(level, True)

            apply(level, False)

            @pl.when(t == 0)
            def _():
                correct()
            return carry
        lax.fori_loop(0, 3, step, 0)

    fine = levels[0]
    fine.f = assembled
    begin(fine, assembled)
    solve(0)

    for first in range(0, 125, 5):
        part, place = (fields, first) if first < SPLIT else (more, first - SPLIT)
        store(part, place, load(fine.res, first, 5))
    column = (my_gx % 2) * 4 + my_gy
    more[AFTER : AFTER + 125, :] = fine.x[pl.ds(column, 125, stride=8), :]
    more[AFTER + 125 :, :] = jnp.zeros((3, 128), F32)


SPLIT = 75
AFTER = 8 * (125 - SPLIT)


def register(parts, r):
    return parts[0][tile(r), :] if r < SPLIT else parts[1][tile(r - SPLIT), :]


def column_of(parts, k):
    first = 3 * (k // 3)
    return parts[k // 3][column_rows(k - first), :]


def column_z(parts, k):
    return parts[1][AFTER + 25 * k : AFTER + 25 * k + 25, :]


def pair_weights():
    cross = split_sections()[4]
    return jnp.where(iota((8, 128), 1) < 64, float(cross[0]), float(cross[1]))


def column_factors(p):
    sec = lax.axis_index("section")
    whole = split_sections()[0]
    lane = iota((25, 128), 1)
    here = lane // EZ % 2 == lax.axis_index("gx") // 2
    factors = []
    for s in range(2):
        parts = []
        for mine in range(2):
            t = whole[2 * mine + s]
            q = mine if p == 0 else 1 - mine
            parts.append(jnp.where(lane < 64, float(t[2 * q]), float(t[2 * q + 1])))
        factors.append(jnp.where(here, jnp.where(sec == 0, parts[0], parts[1]), 0.0))
    return factors


def column_rows(k):
    column = (lax.axis_index("gx") % 2) * 4 + lax.axis_index("gy")
    return pl.ds(k * 200 + column, 25, stride=8)


def raw_order(k):
    lane = iota((256, 160), 0)
    return (iota((256, 160), 1) == 5 * (lane % EZ) + k + lane // 128).astype(F32)


def side_by_side(cols):
    half = cols.shape[0] // 2
    return jnp.concatenate([cols[:half, :], cols[half:, :]], axis=1)


def early_kernel(own0, own1, own_start, other_start, sums, column_out, cols):
    own = (own0, own1)
    weights = pair_weights()
    cols[...] = jnp.zeros_like(cols)
    total = jnp.zeros((192, 160), F32)
    own_factors, other_factors = column_factors(0), column_factors(1)
    for k in range(5):
        where = column_rows(k)
        z = column_z(own, k)
        start, other = own_start[where, :], other_start[where, :]
        w = start - column_of(own, k)
        side = 192 * (k % 2)
        for s in range(2):
            cols[pl.ds(side + s, 25, stride=2), :] = own_factors[s] * z
            cols[pl.ds(side + 64 + s, 25, stride=2), :] = own_factors[s] * start + other_factors[s] * other
            cols[pl.ds(side + 128 + s, 25, stride=2), :] = own_factors[s] * w
        if k % 2 == 1:
            total = total + split_dot(side_by_side(cols), raw_order(k - 1))
    cols[192:, :] = jnp.zeros((192, 128), F32)
    total = total + split_dot(side_by_side(cols), raw_order(4))
    column_out[...] = total
    nothing = jnp.zeros((8, 128), F32)
    uppers, sizes = [nothing] * 5, [nothing] * 5
    for r in range(125):
        c, d = own_start[tile(r), :], other_start[tile(r), :]
        a = c - register(own, r)
        uppers[r % 5] = uppers[r % 5] + a * (c + weights * d)
        sizes[r % 5] = sizes[r % 5] + ((c * c + d * d) + 2.0 * (weights * (c * d)))
    sums[0:8, :] = sum(uppers)
    sums[8:16, :] = jnp.broadcast_to(jnp.sum(sum(sizes), keepdims=True), (8, 128))


def finish_kernel(own0, own1, other0, other1, own_start, other_start, sums, column, guess, sol, res_out, arnoldi, cols, outs):
    own, other = (own0, own1), (other0, other1)
    cols[...] = jnp.zeros_like(cols)
    total = jnp.zeros((128, 160), F32)
    factors = column_factors(1)
    for k in range(5):
        where = column_rows(k)
        z = column_z(other, k)
        w = other_start[where, :] - column_of(other, k)
        side = 128 * (k % 2)
        for s in range(2):
            cols[pl.ds(side + s, 25, stride=2), :] = factors[s] * z
            cols[pl.ds(side + 64 + s, 25, stride=2), :] = factors[s] * w
        if k % 2 == 1:
            total = total + split_dot(side_by_side(cols), raw_order(k - 1))
    cols[128:, :] = jnp.zeros((128, 128), F32)
    total = total + split_dot(side_by_side(cols), raw_order(4))
    weights = pair_weights()
    nothing = jnp.zeros((8, 128), F32)
    uppers = [nothing] * 5
    for r in range(125):
        c, d = own_start[tile(r), :], other_start[tile(r), :]
        b = d - register(other, r)
        uppers[r % 5] = uppers[r % 5] + b * (d + weights * c)

    mine, theirs = sums[0:8, :], sum(uppers)
    size = sums[8:9, 0:1]
    upper = jnp.sum(mine + theirs, keepdims=True) / size
    rests = [nothing] * 5
    for r in range(125):
        c, d = own_start[tile(r), :], other_start[tile(r), :]
        a = (c - register(own, r)) - upper * c
        b = (d - register(other, r)) - upper * d
        rests[r % 5] = rests[r % 5] + ((a * a + b * b) + 2.0 * (weights * (a * b)))
    rest = jnp.sum(sum(rests), keepdims=True)
    beta = jnp.sqrt(size)
    lower = jnp.sqrt(rest) / beta
    weight = upper / (upper * upper + lower * lower)
    entries = float(125 * EZ * COLS * 4)
    for place_out, value in enumerate((beta * (1.0 / math.sqrt(entries)), upper, lower)):
        arnoldi[place_out] = value[0, 0]
    outs[:64, :] = weight * (column[:64, :] + total[:64])
    outs[64:, :] = column[64:128, :] - weight * (column[128:, :] + total[64:])
    for i in range(5):
        for j in range(5):
            r = 2 * (5 * i + j)
            sol[i, j] = guess[i, j] + outs[r : r + 2, :]
            res_out[i, j] = outs[64 + r : 66 + r, :]


def plain_call(kernel, name, rows, scratch, operands, cost=1_000_000):
    many = isinstance(rows, tuple)
    shapes = [jax.ShapeDtypeStruct((r, 128), F32) for r in (rows if many else (rows,))]
    return pl.pallas_call(
        kernel,
        out_shape=shapes if many else shapes[0],
        in_specs=[VMEM] * len(operands),
        out_specs=[VMEM] * len(shapes) if many else VMEM,
        scratch_shapes=[pltpu.VMEM((r, 128), F32) for r in scratch],
        compiler_params=limit(16),
        cost_estimate=pl.CostEstimate(flops=cost, bytes_accessed=cost, transcendentals=0),
        name=name,
    )(*operands)


def cycle(coefs, assembled):
    scratch = []
    for n in (5, 3, 2):
        scratch += [pltpu.VMEM((n**3 * 8, 128), F32)] * 4
    scratch += [pltpu.VMEM((FIELD, 128), F32)]
    return pl.pallas_call(
        cycle_kernel,
        out_shape=[jax.ShapeDtypeStruct((rows, 128), F32) for rows in (SPLIT * 8, AFTER + 128)],
        in_specs=[VMEM] * 2,
        out_specs=[VMEM] * 2,
        scratch_shapes=scratch,
        compiler_params=limit(24),
        cost_estimate=pl.CostEstimate(flops=40_000_000, bytes_accessed=30_000_000, transcendentals=0),
        name="cycle",
    )(coefs, assembled)


def early(own, own_start, other_start):
    return pl.pallas_call(
        early_kernel,
        out_shape=[jax.ShapeDtypeStruct((16, 128), F32), jax.ShapeDtypeStruct((192, 160), F32)],
        in_specs=[VMEM] * 4,
        out_specs=[VMEM] * 2,
        scratch_shapes=[pltpu.VMEM((384, 128), F32)],
        compiler_params=limit(16),
        cost_estimate=pl.CostEstimate(flops=4_000_000, bytes_accessed=4_000_000, transcendentals=0),
        name="early",
    )(*own, own_start, other_start)


def finish(own, other, own_start, other_start, sums, column, guess):
    return pl.pallas_call(
        finish_kernel,
        out_shape=[
            jax.ShapeDtypeStruct(guess.shape, F32),
            jax.ShapeDtypeStruct(guess.shape, F32),
            jax.ShapeDtypeStruct((3,), F32),
        ],
        in_specs=[VMEM] * 9,
        out_specs=[VMEM, VMEM, pl.BlockSpec(memory_space=pltpu.SMEM)],
        scratch_shapes=[pltpu.VMEM((256, 128), F32), pltpu.VMEM((128, 160), F32)],
        compiler_params=limit(24),
        name="finish",
    )(*own, *other, own_start, other_start, sums, column, guess)


def exchange(x, axis, bits):
    return lax.ppermute(x, axis, [(n, n ^ bits) for n in range(lax.axis_size(axis))])


def exchange_by_core(x, axis, bits):
    count = lax.axis_size(axis)
    pairs = [(s * count + n, s * count + (n ^ bits[s])) for s in range(2) for n in range(count)]
    return lax.ppermute(x, ("section", axis), pairs)


def gathered_body(rhs, guess, kappa, bc_flags):
    rhs, guess = (jnp.transpose(v, (1, 2, 0, 3)) for v in (rhs, guess))
    mine, theirs = local_part(rhs, guess, kappa, bc_flags)
    got, mine, kappa_piece = lax.optimization_barrier((exchange(theirs, "section", 1), *part(mine)))
    piece = jnp.concatenate([mine + got, kappa_piece])
    pieces = [exchange_by_core(piece, "gx", bits) for bits in ORDER_X] + [piece]
    line, rest = plain_call(line_kernel, "line", (LINE, REST), [4 * 64, 4 * PIECE], pieces)
    rests = [rest] + [exchange_by_core(rest, "gy", bits) for bits in ORDER_Y]
    halves = plain_call(halves_kernel, "halves", COLS * 16, [], rests)
    other_halves = exchange(halves, "section", 1)
    blocks = [line] + [exchange_by_core(line, "gy", bits) for bits in ORDER_Y]
    blocks, other_halves = lax.optimization_barrier((blocks, other_halves))
    start = plain_call(
        assemble_kernel, "assemble", 128 * 8, [COLS * HALF, COLS * 32, 50 * 8], blocks + rests, 4_000_000
    )
    coefs = plain_call(setup_kernel, "setup", REGISTERS * 8, [128 * 8], (start, halves, other_halves))
    start, coefs = lax.optimization_barrier((start, coefs))
    other_start = exchange(start, "section", 1)
    own, other_start = lax.optimization_barrier((cycle(coefs, start), other_start))
    other = [exchange(part, "section", 1) for part in own]
    sums, column = early(own, start, other_start)
    sol, res, arnoldi = finish(own, other, start, other_start, sums, column, guess)
    sol, res = (jnp.transpose(v, (2, 0, 1, 3)) for v in (sol, res))
    return sol, res, arnoldi


def solution(mesh):
    placed = (
        P("section", "gx", "gy", None),
        P("section", "gx", "gy", None),
        P("gx", "gy", None),
        P(None, "gx", "gy", None),
    )
    sizes = (mesh.shape["section"], mesh.shape["gx"], mesh.shape["gy"])

    def step(rhs, guess, kappa, bc_flags):
        fits = sizes == (2, 4, 4) and rhs.shape == (4, 20, 20, 160)
        return jax.shard_map(
            gathered_body if fits else stepwise,
            mesh=mesh,
            in_specs=placed,
            out_specs=(P("section", "gx", "gy", None), P("section", "gx", "gy", None), P()),
            check_vma=False,
        )(rhs, guess, kappa, bc_flags)

    return step
```
